32 devices in a mesh: groups: 2 (over x), batch: 8 (over z, y), head: 2 (over core).
Axes of the slice: x: 2, y: 2, z: 4, core: 2. Of those that a mesh axis runs over, the one named last changes fastest.
Arguments:
- x_in: bfloat16 [32, 256, 8192], P(('groups', 'batch'), None, 'head'), parts along dimension 0, may hold values from -6 to 6
- b_in: bfloat16 [32, 256, 1024], P(('groups', 'batch'), None, 'head'), parts along dimension 0, may hold values from -6 to 6
- c_in: bfloat16 [32, 256, 1024], P(('groups', 'batch'), None, 'head'), parts along dimension 0, may hold values from -6 to 6
- dt_in: float32 [32, 128, 256], P(('groups', 'batch'), 'head'), parts along dimension 0, may hold values from -6 to 6
- dt_bias: float32 [128], P('head'), may hold values from -6 to -3
- a_log: float32 [128], P('head'), may hold values from -3 to 1.1
- d_skip: float32 [128], P('head'), may hold values from 0.5 to 1.5
- conv_x: float32 [4, 8192], P(None, 'head'), may hold values from -3 to 3
- conv_bc: float32 [2, 4, 1024], P(None, None, 'head'), may hold values from -3 to 3
- par_state: float32 [16, 128, 64, 128], P(('groups', 'batch'), 'head'), parts along dimension 0, may hold values from -1.2 to 1.2
- tail_x: bfloat16 [16, 3, 8192], P(('groups', 'batch'), None, 'head'), parts along dimension 0, may hold values from -6 to 6
- tail_bc: bfloat16 [16, 2, 3, 1024], P(('groups', 'batch'), None, None, 'head'), parts along dimension 0, may hold values from -6 to 6
- counts: int32 [16], P('groups'), parts along dimension 0, may hold values from 1 to 8, 16 in all
- order: int32 [32], P('groups'), parts along dimension 0, may hold values from 0 to 15, as said below
Outputs:
- y_out: bfloat16 [32, 256, 8192], P(('groups', 'batch'), None, 'head'), parts along dimension 0
The draws below stay inside these ranges and needn't reach their ends.
There are 2 independent parts, one for each index of `groups`. The reference program is written for one: setup_inputs(seed, part) draws one part's arguments, and reference() takes and returns one part's arrays. A program takes and returns all parts, laid end to end along the dimension named above; an argument that names none is the same for every part. Nothing has to cross between parts.
Inputs may be any that keep to these rules, and one draw needn't show every extreme that they name: `counts`: every parent has at least one child, 16 in all, and some parent has exactly 8. `order`: a permutation of the 16 slots; the child at position 7 takes the last slot.
All inputs are finite; a program needn't handle non-finite values.
Results may differ from the reference program's by a relative error of at most 0.0041.
Values may be sent and summed in bfloat16 or wider, within the bound.
No kernel may reach another device: no remote copies, remote signals or barrier semaphores. Data moves between devices by JAX's collectives and lax.ppermute only.
A program may use at most 128 MiB of HBM per device.

```python
import math
import jax
import jax.numpy as jnp
import numpy as np
from jax import lax

HEADS = 128
HDIM = 64
STATE = 128
NGROUPS = 8
KCONV = 4
SPAN = 256
MOST_KIDS = 8
PARENTS = 8
CHILDREN = 16


def draw_order(key, part):
    key = jax.random.fold_in(key, 7)
    shuffled = jax.random.permutation(key, jnp.arange(CHILDREN, dtype=jnp.int32)).astype(jnp.int32)
    target = CHILDREN // 2 - 1
    displaced = shuffled[target]
    shuffled = jnp.where(shuffled == CHILDREN - 1, displaced, shuffled)
    shuffled = shuffled.at[target].set(CHILDREN - 1)
    return shuffled.astype(jnp.int32)


def levels(own_key, extent, split, low, top_value):
    def one(axis_at, blocks):
        heights = jax.random.uniform(jax.random.fold_in(jax.random.fold_in(own_key, 6), axis_at), (blocks,), jnp.float32, low / len(split), top_value / len(split))
        return jnp.repeat(jnp.exp(heights), extent[axis_at] // blocks).reshape((-1,) + (1,) * (len(extent) - axis_at - 1))

    gain = one(*split[0])
    for cut in split[1:]:
        gain = gain * one(*cut)
    return gain


def profile(number_of, total, most, slope):
    portions = [(1 << 20) // math.isqrt(grade ** slope) + 1 for grade in range(2, number_of + 1)]
    rest, given = total - most - (number_of - 1), [1] * (number_of - 1)
    while rest > 0:
        free = [i for i in range(number_of - 1) if given[i] < most]
        whole, left = sum([portions[i] for i in free]), rest
        for i in free:
            addition = min(most - given[i], max(1, left * portions[i] // whole), rest)
            given[i] = given[i] + addition
            rest = rest - addition
    return np.array([most] + given)


def ragged_sizes(rng, count, total, reach, skew):
    if count == 2:
        one = jax.random.randint(rng, (), max(1, total - reach), min(reach, total - 1) + 1)
        return jnp.stack([one, total - one])
    lengths = jnp.asarray(profile(count, total, reach, skew), jnp.int32)
    couples = (count - 1) // 2
    source_of, receiver = lengths[1:1 + 2 * couples:2], lengths[2:2 + 2 * couples:2]
    margin = jnp.minimum(source_of - 1, reach - receiver)
    shifted = jax.random.randint(jax.random.fold_in(rng, 1), (couples,), 0, 1 << 20) % (margin + 1)
    lengths = lengths.at[1:1 + 2 * couples:2].set(source_of - shifted).at[2:2 + 2 * couples:2].set(receiver + shifted)
    return lengths[jax.random.permutation(jax.random.fold_in(rng, 2), count)]


def scatter_about(key, dims, scale, bound, shards=(), kind=jnp.bfloat16):
    drawn = jax.random.normal(key, dims, jnp.float32) * scale
    if len(shards) > 0:
        drawn = levels(key, dims, shards, -0.22, 0.18) * drawn
    return jnp.clip(drawn, min=-bound, max=bound).astype(kind)


def setup_inputs(seed: int = 0, part: int = 0) -> dict:
    streams_of = jax.random.split(jax.random.key(seed), 15)
    part_keys = jax.random.split(jax.random.fold_in(streams_of[14], part), 15)
    return {
        "x_in": scatter_about(part_keys[0], (CHILDREN, SPAN, HEADS * HDIM), 1.0, 6.0, ((0, 8), (2, 2))),
        "b_in": scatter_about(part_keys[1], (CHILDREN, SPAN, NGROUPS * STATE), 1.0, 6.0, ((0, 8), (2, 2))),
        "c_in": scatter_about(part_keys[2], (CHILDREN, SPAN, NGROUPS * STATE), 1.0, 6.0, ((0, 8), (2, 2))),
        "dt_in": scatter_about(part_keys[3], (CHILDREN, HEADS, SPAN), 1.0, 6.0, ((0, 8), (1, 2)), jnp.float32),
        "dt_bias": jnp.clip(-6.0 + 3.0 * jax.random.uniform(streams_of[4], (HEADS,), jnp.float32) ** levels(streams_of[4], (HEADS,), ((0, 2),), -0.2, 0.2), -6.0, -3.0),
        "a_log": jnp.clip(-3.0 + 4.1 * jax.random.uniform(streams_of[5], (HEADS,), jnp.float32) ** levels(streams_of[5], (HEADS,), ((0, 2),), -0.2, 0.2), -3.0, 1.1),
        "d_skip": jnp.clip(0.5 + 1.0 * jax.random.uniform(streams_of[6], (HEADS,), jnp.float32) ** levels(streams_of[6], (HEADS,), ((0, 2),), -0.2, 0.2), 0.5, 1.5),
        "conv_x": scatter_about(streams_of[7], (KCONV, HEADS * HDIM), KCONV ** -0.5, 3.0, ((1, 2),), jnp.float32),
        "conv_bc": scatter_about(streams_of[8], (2, KCONV, NGROUPS * STATE), KCONV ** -0.5, 3.0, ((2, 2),), jnp.float32),
        "par_state": scatter_about(part_keys[9], (PARENTS, HEADS, HDIM, STATE), 0.2, 1.2, ((0, 8), (1, 2)), jnp.float32),
        "tail_x": scatter_about(part_keys[10], (PARENTS, KCONV - 1, HEADS * HDIM), 1.0, 6.0, ((0, 8), (2, 2))),
        "tail_bc": scatter_about(part_keys[11], (PARENTS, 2, KCONV - 1, NGROUPS * STATE), 1.0, 6.0, ((0, 8), (3, 2))),
        "counts": ragged_sizes(part_keys[12], PARENTS, CHILDREN, MOST_KIDS, 2).astype(jnp.int32),
        "order": draw_order(jax.random.fold_in(jax.random.fold_in(streams_of[14], part), 71), part),
    }


def parent_rows(counts, order):
    bounds = jnp.cumsum(counts)
    slot_idx = jnp.arange(CHILDREN, dtype=jnp.int32)
    slot_parent = jnp.sum((bounds[None, :] <= slot_idx[:, None]).astype(jnp.int32), axis=1).astype(jnp.int32)
    return slot_parent[order].astype(jnp.int32)


def conv_silu(tail_rows, sequence, weight):
    padded = jnp.concatenate([tail_rows, sequence], axis=1).astype(jnp.float32)
    length = sequence.shape[1]
    summed = padded[:, 0:length, :] * weight[0]
    for offset in range(1, weight.shape[0]):
        summed = summed + padded[:, offset:offset + length, :] * weight[offset]
    return jax.nn.silu(summed).astype(jnp.bfloat16)


def span_mix(x_rows, b_rows, c_rows, dt_step, cumulative):
    scores = jnp.einsum('ctn,csn->cts', c_rows.astype(jnp.float32), b_rows.astype(jnp.float32))
    length = cumulative.shape[2]
    position = jnp.arange(length)
    causal = position[:, None] >= position[None, :]
    decay_gap = cumulative[:, :, :, None] - cumulative[:, :, None, :]
    factor = jnp.exp(jnp.where(causal, decay_gap, -1e30))
    mixing = (scores[:, None] * factor * dt_step[:, :, None, :]).astype(jnp.bfloat16)
    return jnp.einsum('crts,csrp->ctrp', mixing.astype(jnp.float32), x_rows.astype(jnp.float32))


def reference(x_in, b_in, c_in, dt_in, dt_bias, a_log, d_skip, conv_x, conv_bc, par_state, tail_x, tail_bc, counts, order):
    parent = parent_rows(counts, order)
    x_conv = conv_silu(tail_x[parent], x_in, conv_x)
    b_conv = conv_silu(tail_bc[parent, 0], b_in, conv_bc[0])
    c_conv = conv_silu(tail_bc[parent, 1], c_in, conv_bc[1])
    per_group = HEADS // NGROUPS

    def one_child(operands):
        x_rows, b_rows, c_rows, dt_raw, owner = operands
        dt_step = jax.nn.softplus(dt_raw + dt_bias[:, None])
        cumulative = jnp.cumsum(dt_step * (-jnp.exp(a_log))[:, None], axis=1)
        x_groups = x_rows.reshape(SPAN, NGROUPS, per_group, HDIM).transpose(1, 0, 2, 3)
        b_groups = b_rows.reshape(SPAN, NGROUPS, STATE).transpose(1, 0, 2)
        c_groups = c_rows.reshape(SPAN, NGROUPS, STATE).transpose(1, 0, 2)
        within = span_mix(x_groups, b_groups, c_groups, dt_step.reshape(NGROUPS, per_group, SPAN), cumulative.reshape(NGROUPS, per_group, SPAN))
        within = within.transpose(1, 0, 2, 3).reshape(SPAN, HEADS, HDIM)
        c_wide = jnp.repeat(c_rows.reshape(SPAN, NGROUPS, STATE), per_group, axis=1).astype(jnp.float32)
        start_state = par_state[owner]
        contracted = jnp.einsum('thn,hpn->thp', c_wide, start_state, precision=lax.Precision.HIGHEST)
        carried = (contracted * jnp.exp(cumulative).T[:, :, None]).astype(jnp.bfloat16)
        carried = lax.optimization_barrier(carried).astype(jnp.float32)
        result = within + carried + d_skip[None, :, None] * x_rows.reshape(SPAN, HEADS, HDIM).astype(jnp.float32)
        return result.reshape(SPAN, HEADS * HDIM).astype(jnp.bfloat16)

    return lax.map(one_child, (x_conv, b_conv, c_conv, dt_in, parent))
```

```python
import functools

import jax
import jax.numpy as jnp
from jax import lax
from jax.experimental import pallas as pl
from jax.experimental.pallas import tpu as pltpu
from jax.sharding import PartitionSpec as P

VMEM_LIMIT = 48 * 1024 * 1024


def parent_of(counts, order):
    index = jnp.arange(counts.shape[0], dtype=jnp.int32)
    bounds = jnp.sum(jnp.where(index[None, :] <= index[:, None], counts[None, :], 0), axis=1)
    return jnp.sum((bounds[None, :] <= order[:, None]).astype(jnp.int32), axis=1)


def conv_silu(padded, tail, rows, taps):
    length = rows.shape[0]
    reach = taps.shape[0] - 1
    padded[8 - reach : 8, :] = tail.astype(jnp.float32)
    padded[8 : 8 + length, :] = rows.astype(jnp.float32)
    total = padded[8 - reach : 8 - reach + length, :] * taps[0:1, :]
    for k in range(1, reach + 1):
        total = total + padded[8 - reach + k : 8 - reach + k + length, :] * taps[k : k + 1, :]
    return (total / (1.0 + jnp.exp(-total))).astype(jnp.bfloat16)


def within_kernel(
    parent_ref,
    x_ref,
    b_ref,
    c_ref,
    dt_ref,
    bias_ref,
    alog_ref,
    skip_ref,
    taps_x_ref,
    taps_bc_ref,
    tail_x_ref,
    tail_bc_ref,
    mixed_ref,
    c_out_ref,
    grow_ref,
    padded,
):
    length = x_ref.shape[1]
    heads = dt_ref.shape[1]
    width = x_ref.shape[2] // heads
    b_conv = conv_silu(padded, tail_bc_ref[0, 0], b_ref[0], taps_bc_ref[0])
    c_conv = conv_silu(padded, tail_bc_ref[0, 1], c_ref[0], taps_bc_ref[1])
    c_out_ref[0] = c_conv
    scores = lax.dot_general(
        c_conv, b_conv, (((1,), (1,)), ((), ())), preferred_element_type=jnp.float32
    )
    raw = dt_ref[0] + bias_ref[...]
    step = jnp.maximum(raw, 0.0) + jnp.log1p(jnp.exp(-jnp.abs(raw)))
    per_token = step * (-jnp.exp(alog_ref[...]))
    row = lax.broadcasted_iota(jnp.int32, (length, length), 0)
    col = lax.broadcasted_iota(jnp.int32, (length, length), 1)
    upper = (row <= col).astype(jnp.float32)
    total = lax.dot_general(
        per_token,
        upper,
        (((1,), (0,)), ((), ())),
        precision=lax.Precision.HIGHEST,
        preferred_element_type=jnp.float32,
    )
    total_t = total.T
    grow_ref[0, 0] = jnp.exp(total_t)
    causal = row >= col
    low = lax.broadcasted_iota(jnp.int32, (length, 2 * width), 1) < width
    for pair in range(heads // 2):
        lanes = slice(pair * 2 * width, (pair + 1) * 2 * width)
        x_conv = conv_silu(
            padded, tail_x_ref[0, :, lanes], x_ref[0, :, lanes], taps_x_ref[:, lanes]
        )
        parts = []
        for head in (2 * pair, 2 * pair + 1):
            gap = total_t[:, head : head + 1] - total[head : head + 1, :]
            factor = jnp.exp(jnp.where(causal, gap, -1e30))
            mixing = (scores * factor * step[head : head + 1, :]).astype(jnp.bfloat16)
            parts.append(jnp.dot(mixing, x_conv, preferred_element_type=jnp.float32))
        mixed_ref[0, :, lanes] = (
            jnp.where(low, parts[0], parts[1]) + skip_ref[:, lanes] * x_conv.astype(jnp.float32)
        )


def carried_kernel(state_ref, c_ref, grow_ref, mixed_ref, y_ref):
    sources, _, part, width, size = state_ref.shape
    length = c_ref.shape[1]
    low = lax.broadcasted_iota(jnp.int32, (length, 2 * width), 1) < width
    c_conv = c_ref[0]
    for source in range(sources):
        state = state_ref[source, 0].reshape(part * width, size)
        term = lax.dot_general(
            c_conv, state, (((1,), (1,)), ((), ())), preferred_element_type=jnp.float32
        )
        for pair in range(part // 2):
            head = source * part + 2 * pair
            grow = jnp.where(
                low, grow_ref[0, 0, :, head : head + 1], grow_ref[0, 0, :, head + 1 : head + 2]
            )
            here = slice(2 * pair * width, (2 * pair + 2) * width)
            lanes = slice(head * width, (head + 2) * width)
            carried = (term[:, here] * grow).astype(jnp.bfloat16).astype(jnp.float32)
            y_ref[0, :, lanes] = (mixed_ref[0, :, lanes] + carried).astype(jnp.bfloat16)


def pick_kernel(parent_ref, state_ref, out_ref):
    out_ref[...] = state_ref[...]


def local(
    x_in,
    b_in,
    c_in,
    dt_in,
    dt_bias,
    a_log,
    d_skip,
    conv_x,
    conv_bc,
    par_state,
    tail_x,
    tail_bc,
    counts,
    order,
):
    kids, length, columns = x_in.shape
    heads = dt_in.shape[1]
    width, size = par_state.shape[2:]
    ways = lax.axis_size("batch")
    groups = b_in.shape[2] // size
    per_group = heads // groups
    part = heads // ways
    wide = per_group * width
    reach = tail_x.shape[1]
    parents_all = counts.shape[0]
    kids_all = order.shape[0]

    parent = parent_of(counts, order)
    own = lax.dynamic_slice_in_dim(parent, lax.axis_index("batch") * kids, kids)

    sent = par_state.astype(jnp.bfloat16).reshape(ways, part, width, size)
    shares = lax.all_to_all(sent, "batch", split_axis=0, concat_axis=0, tiled=True)

    tails = jnp.concatenate([tail_x.reshape(-1), tail_bc.reshape(-1)])
    tails = jnp.broadcast_to(tails[None], (ways, tails.shape[0]))
    tails = lax.all_to_all(tails, "batch", split_axis=0, concat_axis=0, tiled=True)
    tails_x = tails[:, : reach * columns].reshape(parents_all, reach, columns)
    tails_bc = tails[:, reach * columns :].reshape(parents_all, 2, reach, groups * size)

    picked = pl.pallas_call(
        pick_kernel,
        grid_spec=pltpu.PrefetchScalarGridSpec(
            num_scalar_prefetch=1,
            grid=(kids_all,),
            in_specs=[pl.BlockSpec((1, part, width, size), lambda i, p: (p[i], 0, 0, 0))],
            out_specs=pl.BlockSpec((1, part, width, size), lambda i, p: (i, 0, 0, 0)),
        ),
        out_shape=jax.ShapeDtypeStruct((kids_all, part, width, size), jnp.bfloat16),
        cost_estimate=pl.CostEstimate(
            flops=0, bytes_accessed=4 * kids_all * part * width * size, transcendentals=0
        ),
        name="pick_states",
    )(parent, shares)
    states = lax.all_to_all(
        picked.reshape(ways, kids, part, width, size), "batch", split_axis=0, concat_axis=0, tiled=True
    )

    skip_row = jnp.repeat(d_skip, width)[None, :]
    mixed, c_conv, grow = pl.pallas_call(
        within_kernel,
        grid_spec=pltpu.PrefetchScalarGridSpec(
            num_scalar_prefetch=1,
            grid=(kids, groups),
            in_specs=[
                pl.BlockSpec((1, length, wide), lambda c, q, p: (c, 0, q)),
                pl.BlockSpec((1, length, size), lambda c, q, p: (c, 0, q)),
                pl.BlockSpec((1, length, size), lambda c, q, p: (c, 0, q)),
                pl.BlockSpec((1, per_group, length), lambda c, q, p: (c, q, 0)),
                pl.BlockSpec((per_group, 1), lambda c, q, p: (q, 0)),
                pl.BlockSpec((per_group, 1), lambda c, q, p: (q, 0)),
                pl.BlockSpec((1, wide), lambda c, q, p: (0, q)),
                pl.BlockSpec((reach + 1, wide), lambda c, q, p: (0, q)),
                pl.BlockSpec((2, reach + 1, size), lambda c, q, p: (0, 0, q)),
                pl.BlockSpec((1, reach, wide), lambda c, q, p: (p[c], 0, q)),
                pl.BlockSpec((1, 2, reach, size), lambda c, q, p: (p[c], 0, 0, q)),
            ],
            out_specs=[
                pl.BlockSpec((1, length, wide), lambda c, q, p: (c, 0, q)),
                pl.BlockSpec((1, length, size), lambda c, q, p: (c, 0, q)),
                pl.BlockSpec((1, 1, length, per_group), lambda c, q, p: (c, q, 0, 0)),
            ],
            scratch_shapes=[pltpu.VMEM((8 + length, size), jnp.float32)],
        ),
        out_shape=[
            jax.ShapeDtypeStruct((kids, length, columns), jnp.float32),
            jax.ShapeDtypeStruct((kids, length, groups * size), jnp.bfloat16),
            jax.ShapeDtypeStruct((kids, groups, length, per_group), jnp.float32),
        ],
        compiler_params=pltpu.CompilerParams(vmem_limit_bytes=VMEM_LIMIT),
        cost_estimate=pl.CostEstimate(
            flops=4 * kids * heads * length * length * width,
            bytes_accessed=6 * kids * length * columns,
            transcendentals=kids * heads * length * length,
        ),
        name="within",
    )(
        own,
        x_in,
        b_in,
        c_in,
        dt_in,
        dt_bias[:, None],
        a_log[:, None],
        skip_row,
        conv_x,
        conv_bc,
        tails_x,
        tails_bc,
    )

    sources = per_group // part
    return pl.pallas_call(
        carried_kernel,
        grid=(kids, groups),
        in_specs=[
            pl.BlockSpec((sources, 1, part, width, size), lambda c, q: (q, c, 0, 0, 0)),
            pl.BlockSpec((1, length, size), lambda c, q: (c, 0, q)),
            pl.BlockSpec((1, 1, length, per_group), lambda c, q: (c, q, 0, 0)),
            pl.BlockSpec((1, length, wide), lambda c, q: (c, 0, q)),
        ],
        out_specs=pl.BlockSpec((1, length, wide), lambda c, q: (c, 0, q)),
        out_shape=jax.ShapeDtypeStruct((kids, length, columns), jnp.bfloat16),
        compiler_params=pltpu.CompilerParams(vmem_limit_bytes=VMEM_LIMIT),
        cost_estimate=pl.CostEstimate(
            flops=2 * kids * length * columns * size,
            bytes_accessed=8 * kids * length * columns,
            transcendentals=0,
        ),
        name="carried",
    )(states, c_conv, grow, mixed)


def solution(mesh):
    rows, cols = P(("groups", "batch"), None, "head"), P(("groups", "batch"), "head")
    placed = (
        rows,
        rows,
        rows,
        cols,
        P("head"),
        P("head"),
        P("head"),
        P(None, "head"),
        P(None, None, "head"),
        cols,
        rows,
        P(("groups", "batch"), None, None, "head"),
        P("groups"),
        P("groups"),
    )
    return jax.shard_map(local, mesh=mesh, in_specs=placed, out_specs=rows, check_vma=False)
```

```python
import functools

import jax
import jax.numpy as jnp
from jax import lax
from jax.experimental import pallas as pl
from jax.experimental.pallas import tpu as pltpu
from jax.sharding import PartitionSpec as P

VMEM_LIMIT = 48 * 1024 * 1024
CHUNKS = 4
FIX = 16


def parent_of(counts, order):
    index = jnp.arange(counts.shape[0], dtype=jnp.int32)
    bounds = jnp.sum(jnp.where(index[None, :] <= index[:, None], counts[None, :], 0), axis=1)
    return jnp.sum((bounds[None, :] <= order[:, None]).astype(jnp.int32), axis=1)


def conv_silu(padded, tail, rows, taps):
    length = rows.shape[0]
    reach = taps.shape[0] - 1
    padded[8 - reach : 8, :] = jnp.broadcast_to(tail, (reach, rows.shape[1])).astype(jnp.float32)
    padded[8 : 8 + length, :] = rows.astype(jnp.float32)
    total = padded[8 - reach : 8 - reach + length, :] * taps[0:1, :]
    for k in range(1, reach + 1):
        total = total + padded[8 - reach + k : 8 - reach + k + length, :] * taps[k : k + 1, :]
    half = 0.5 * total
    return (half + half * jnp.tanh(half)).astype(jnp.bfloat16)


def conv_kernel(
    x_ref, b_ref, c_ref, dt_ref, bias_ref, alog_ref, taps_x_ref, taps_bc_ref,
    xc_ref, bc_ref, cc_ref, row_ref, column_ref, padded,
):
    length = x_ref.shape[1]
    lanes_all = x_ref.shape[2]
    bc_ref[0] = conv_silu(padded, 0.0, b_ref[0], taps_bc_ref[0])
    cc_ref[0] = conv_silu(padded, 0.0, c_ref[0], taps_bc_ref[1])
    for start in range(0, lanes_all, 128):
        lanes = slice(start, start + 128)
        xc_ref[0, :, lanes] = conv_silu(padded, 0.0, x_ref[0, :, lanes], taps_x_ref[:, lanes])
    raw = dt_ref[0] + bias_ref[...]
    step = jnp.maximum(raw, 0.0) + jnp.log1p(jnp.exp(-jnp.abs(raw)))
    per_token = step * (-jnp.exp(alog_ref[...]))
    row = lax.broadcasted_iota(jnp.int32, (length, length), 0)
    col = lax.broadcasted_iota(jnp.int32, (length, length), 1)
    total = lax.dot_general(
        per_token,
        (row <= col).astype(jnp.float32),
        (((1,), (0,)), ((), ())),
        precision=lax.Precision.HIGHEST,
        preferred_element_type=jnp.float32,
    )
    row_ref[0] = total - jnp.log(step)
    column_ref[0, 0] = total.T


def out_kernel(offset, group_at, lines, flags_ref, *refs):
    (
        x_ref, xin_ref, b_ref, bin_ref, c_ref, cin_ref, row_ref, column_ref, skip_ref,
        taps_x_ref, taps_bc_ref, tail_own, tail_a, tail_b, tail_c,
        own_ref, a_ref, b2_ref, c2_ref,
    ) = refs[:19]
    y_ref, padded = refs[-2:]
    length = x_ref.shape[1]
    heads, width, size = own_ref.shape[1:]
    half = length // 2
    reach = taps_x_ref.shape[0] - 1
    inner = flags_ref[0] == 1
    same = flags_ref[1] == pl.program_id(1)

    def choose(own, a, b, c):
        return jnp.where(same, jnp.where(inner, own, a), jnp.where(inner, c, b))

    tail = choose(tail_own[0, 0], tail_a[0, 0], tail_b[0, 0], tail_c[0, 0]).astype(jnp.float32)
    state = choose(own_ref[0], a_ref[0], b2_ref[0], c2_ref[0]).reshape(heads * width, size)
    def tail_rows(at):
        return jnp.concatenate([tail[k * lines + at : k * lines + at + 1] for k in range(reach)])

    def fixed(bulk, first, taps, at):
        return jnp.concatenate([conv_silu(padded, tail_rows(at), first, taps), bulk])

    blocks = lines - 4
    b_conv = fixed(b_ref[0, FIX:], bin_ref[0], taps_bc_ref[0], blocks + group_at)
    c_conv = fixed(c_ref[0, FIX:], cin_ref[0], taps_bc_ref[1], blocks + 2 + group_at)
    scores = lax.dot_general(
        c_conv, b_conv, (((1,), (1,)), ((), ())), preferred_element_type=jnp.float32
    )
    term = lax.dot_general(
        c_conv, state, (((1,), (1,)), ((), ())), preferred_element_type=jnp.float32
    )
    causal = lax.broadcasted_iota(jnp.int32, (half, half), 0) >= lax.broadcasted_iota(
        jnp.int32, (half, half), 1
    )
    low = lax.broadcasted_iota(jnp.int32, (length, 2 * width), 1) < width
    for pair in range(heads // 2):
        lanes = slice(pair * 2 * width, (pair + 1) * 2 * width)
        x_conv = fixed(
            x_ref[0, FIX:, lanes],
            xin_ref[0, :, lanes],
            taps_x_ref[:, lanes],
            (offset + pair * 2) * width // 128,
        )
        parts, grow = [], []
        for head in (2 * pair, 2 * pair + 1):
            spot = offset % column_ref.shape[3] + head
            column = jnp.broadcast_to(column_ref[0, 0, :, spot : spot + 1], (length, half))
            rows = row_ref[0, head : head + 1, :]
            near = jnp.exp(jnp.where(causal, column[:half] - rows[:, :half], -1e30))
            far = jnp.exp(column[half:] - rows[:, :half])
            last = jnp.exp(jnp.where(causal, column[half:] - rows[:, half:], -1e30))
            top = (scores[:half, :half] * near).astype(jnp.bfloat16)
            left = (scores[half:, :half] * far).astype(jnp.bfloat16)
            right = (scores[half:, half:] * last).astype(jnp.bfloat16)
            parts.append(
                jnp.concatenate(
                    [
                        jnp.dot(top, x_conv[:half], preferred_element_type=jnp.float32),
                        jnp.dot(
                            jnp.concatenate([left, right], axis=1),
                            x_conv,
                            preferred_element_type=jnp.float32,
                        ),
                    ]
                )
            )
            grow.append(column)
        carried = term[:, lanes] * jnp.exp(jnp.where(low, grow[0], grow[1]))
        carried = carried.astype(jnp.bfloat16).astype(jnp.float32)
        y_ref[0, :, lanes] = (
            jnp.where(low, parts[0], parts[1])
            + carried
            + skip_ref[:, lanes] * x_conv.astype(jnp.float32)
        ).astype(jnp.bfloat16)


def cast_kernel(inputs, flags_ref, *refs):
    mine, other = refs[-2:]
    sources = refs[:inputs]
    part = sources[0].shape[1]
    extra = mine.shape[0] - part
    for at, out in enumerate((mine, other)):
        if extra:
            out[part] = sources[2 + at][0]
        out[:part] = sources[at][0].astype(jnp.bfloat16)


def select_kernel(slots_ref, *refs):
    held, outs, sems = refs[:8], refs[-5:-1], refs[-1]
    kids = outs[0].shape[0]

    def copy(source, kind, kid):
        return pltpu.make_async_copy(
            held[source], outs[kind].at[kid], sems.at[kind, kid]
        )

    for kind in range(4):
        for kid in range(kids):
            for source in range(8):

                @pl.when(slots_ref[kind * kids + kid] == source)
                def _(source=source, kind=kind, kid=kid):
                    copy(source, kind, kid).start()

    for kind in range(4):
        for kid in range(kids):
            copy(0, kind, kid).wait()


def routes():
    at = lambda z, y: z * 2 + y
    both = (0, 1)
    near = [
        [(at(0, y), at(1, y ^ f)) for y in both] + [(at(1, y), at(2, y ^ f)) for y in both]
        for f in both
    ]
    back = [
        [(at(3, y), at(2, y ^ f)) for y in both] + [(at(2, y), at(1, y ^ f)) for y in both]
        for f in both
    ]
    leap = [
        [(at(0, y), at(2, y ^ f)) for y in both] + [(at(3, y), at(1, y ^ f)) for y in both]
        for f in both
    ]
    across = [(at(z, y), at(z, 1 - y)) for z in (1, 2) for y in both]
    out = [
        [(at(1, y), at(0, y ^ f)) for y in both] + [(at(2, y), at(3, y ^ f)) for y in both]
        for f in both
    ]
    return near, back, leap, across, out


def pack_tails(tail_x, tail_bc, width, size):
    reach, columns = tail_x.shape[1:]
    x_lines = tail_x.reshape(reach, 2, columns // 2 // 128, 128).transpose(1, 0, 2, 3)
    bc_lines = tail_bc.reshape(2, reach, 2, -1, 128).transpose(2, 1, 0, 3, 4)
    bc_lines = bc_lines.reshape(2, reach, -1, 128)
    lines = jnp.concatenate([x_lines, bc_lines], axis=2)
    lines = lines.reshape(2, -1, 128)
    return jnp.pad(lines, ((0, 0), (0, width - lines.shape[1]), (0, 0)))


def within_kernel(
    parent_ref,
    x_ref,
    b_ref,
    c_ref,
    dt_ref,
    bias_ref,
    alog_ref,
    skip_ref,
    taps_x_ref,
    taps_bc_ref,
    tail_x_ref,
    tail_bc_ref,
    mixed_ref,
    c_out_ref,
    grow_ref,
    padded,
):
    length = x_ref.shape[1]
    heads = dt_ref.shape[1]
    width = x_ref.shape[2] // heads
    b_conv = conv_silu(padded, tail_bc_ref[0, 0], b_ref[0], taps_bc_ref[0])
    c_conv = conv_silu(padded, tail_bc_ref[0, 1], c_ref[0], taps_bc_ref[1])
    c_out_ref[0] = c_conv
    scores = lax.dot_general(
        c_conv, b_conv, (((1,), (1,)), ((), ())), preferred_element_type=jnp.float32
    )
    raw = dt_ref[0] + bias_ref[...]
    step = jnp.maximum(raw, 0.0) + jnp.log1p(jnp.exp(-jnp.abs(raw)))
    per_token = step * (-jnp.exp(alog_ref[...]))
    row = lax.broadcasted_iota(jnp.int32, (length, length), 0)
    col = lax.broadcasted_iota(jnp.int32, (length, length), 1)
    upper = (row <= col).astype(jnp.float32)
    total = lax.dot_general(
        per_token,
        upper,
        (((1,), (0,)), ((), ())),
        precision=lax.Precision.HIGHEST,
        preferred_element_type=jnp.float32,
    )
    total_t = total.T
    grow_ref[0, 0] = jnp.exp(total_t)
    causal = row >= col
    low = lax.broadcasted_iota(jnp.int32, (length, 2 * width), 1) < width
    for pair in range(heads // 2):
        lanes = slice(pair * 2 * width, (pair + 1) * 2 * width)
        x_conv = conv_silu(
            padded, tail_x_ref[0, :, lanes], x_ref[0, :, lanes], taps_x_ref[:, lanes]
        )
        parts = []
        for head in (2 * pair, 2 * pair + 1):
            gap = total_t[:, head : head + 1] - total[head : head + 1, :]
            factor = jnp.exp(jnp.where(causal, gap, -1e30))
            mixing = (scores * factor * step[head : head + 1, :]).astype(jnp.bfloat16)
            parts.append(jnp.dot(mixing, x_conv, preferred_element_type=jnp.float32))
        mixed_ref[0, :, lanes] = (
            jnp.where(low, parts[0], parts[1]) + skip_ref[:, lanes] * x_conv.astype(jnp.float32)
        )


def carried_kernel(state_ref, c_ref, grow_ref, mixed_ref, y_ref):
    sources, _, part, width, size = state_ref.shape
    length = c_ref.shape[1]
    low = lax.broadcasted_iota(jnp.int32, (length, 2 * width), 1) < width
    c_conv = c_ref[0]
    for source in range(sources):
        state = state_ref[source, 0].reshape(part * width, size)
        term = lax.dot_general(
            c_conv, state, (((1,), (1,)), ((), ())), preferred_element_type=jnp.float32
        )
        for pair in range(part // 2):
            head = source * part + 2 * pair
            grow = jnp.where(
                low, grow_ref[0, 0, :, head : head + 1], grow_ref[0, 0, :, head + 1 : head + 2]
            )
            here = slice(2 * pair * width, (2 * pair + 2) * width)
            lanes = slice(head * width, (head + 2) * width)
            carried = (term[:, here] * grow).astype(jnp.bfloat16).astype(jnp.float32)
            y_ref[0, :, lanes] = (mixed_ref[0, :, lanes] + carried).astype(jnp.bfloat16)


def pick_kernel(parent_ref, state_ref, out_ref):
    out_ref[...] = state_ref[...]


def local_any(
    x_in,
    b_in,
    c_in,
    dt_in,
    dt_bias,
    a_log,
    d_skip,
    conv_x,
    conv_bc,
    par_state,
    tail_x,
    tail_bc,
    counts,
    order,
):
    kids, length, columns = x_in.shape
    heads = dt_in.shape[1]
    width, size = par_state.shape[2:]
    ways = lax.axis_size("batch")
    groups = b_in.shape[2] // size
    per_group = heads // groups
    part = heads // ways
    wide = per_group * width
    reach = tail_x.shape[1]
    parents_all = counts.shape[0]
    kids_all = order.shape[0]

    parent = parent_of(counts, order)
    own = lax.dynamic_slice_in_dim(parent, lax.axis_index("batch") * kids, kids)

    sent = par_state.astype(jnp.bfloat16).reshape(ways, part, width, size)
    shares = lax.all_to_all(sent, "batch", split_axis=0, concat_axis=0, tiled=True)

    tails = jnp.concatenate([tail_x.reshape(-1), tail_bc.reshape(-1)])
    tails = jnp.broadcast_to(tails[None], (ways, tails.shape[0]))
    tails = lax.all_to_all(tails, "batch", split_axis=0, concat_axis=0, tiled=True)
    tails_x = tails[:, : reach * columns].reshape(parents_all, reach, columns)
    tails_bc = tails[:, reach * columns :].reshape(parents_all, 2, reach, groups * size)

    picked = pl.pallas_call(
        pick_kernel,
        grid_spec=pltpu.PrefetchScalarGridSpec(
            num_scalar_prefetch=1,
            grid=(kids_all,),
            in_specs=[pl.BlockSpec((1, part, width, size), lambda i, p: (p[i], 0, 0, 0))],
            out_specs=pl.BlockSpec((1, part, width, size), lambda i, p: (i, 0, 0, 0)),
        ),
        out_shape=jax.ShapeDtypeStruct((kids_all, part, width, size), jnp.bfloat16),
        cost_estimate=pl.CostEstimate(
            flops=0, bytes_accessed=4 * kids_all * part * width * size, transcendentals=0
        ),
        name="pick_states",
    )(parent, shares)
    states = lax.all_to_all(
        picked.reshape(ways, kids, part, width, size), "batch", split_axis=0, concat_axis=0, tiled=True
    )

    skip_row = jnp.repeat(d_skip, width)[None, :]
    mixed, c_conv, grow = pl.pallas_call(
        within_kernel,
        grid_spec=pltpu.PrefetchScalarGridSpec(
            num_scalar_prefetch=1,
            grid=(kids, groups),
            in_specs=[
                pl.BlockSpec((1, length, wide), lambda c, q, p: (c, 0, q)),
                pl.BlockSpec((1, length, size), lambda c, q, p: (c, 0, q)),
                pl.BlockSpec((1, length, size), lambda c, q, p: (c, 0, q)),
                pl.BlockSpec((1, per_group, length), lambda c, q, p: (c, q, 0)),
                pl.BlockSpec((per_group, 1), lambda c, q, p: (q, 0)),
                pl.BlockSpec((per_group, 1), lambda c, q, p: (q, 0)),
                pl.BlockSpec((1, wide), lambda c, q, p: (0, q)),
                pl.BlockSpec((reach + 1, wide), lambda c, q, p: (0, q)),
                pl.BlockSpec((2, reach + 1, size), lambda c, q, p: (0, 0, q)),
                pl.BlockSpec((1, reach, wide), lambda c, q, p: (p[c], 0, q)),
                pl.BlockSpec((1, 2, reach, size), lambda c, q, p: (p[c], 0, 0, q)),
            ],
            out_specs=[
                pl.BlockSpec((1, length, wide), lambda c, q, p: (c, 0, q)),
                pl.BlockSpec((1, length, size), lambda c, q, p: (c, 0, q)),
                pl.BlockSpec((1, 1, length, per_group), lambda c, q, p: (c, q, 0, 0)),
            ],
            scratch_shapes=[pltpu.VMEM((8 + length, size), jnp.float32)],
        ),
        out_shape=[
            jax.ShapeDtypeStruct((kids, length, columns), jnp.float32),
            jax.ShapeDtypeStruct((kids, length, groups * size), jnp.bfloat16),
            jax.ShapeDtypeStruct((kids, groups, length, per_group), jnp.float32),
        ],
        compiler_params=pltpu.CompilerParams(vmem_limit_bytes=VMEM_LIMIT),
        cost_estimate=pl.CostEstimate(
            flops=4 * kids * heads * length * length * width,
            bytes_accessed=6 * kids * length * columns,
            transcendentals=kids * heads * length * length,
        ),
        name="within",
    )(
        own,
        x_in,
        b_in,
        c_in,
        dt_in,
        dt_bias[:, None],
        a_log[:, None],
        skip_row,
        conv_x,
        conv_bc,
        tails_x,
        tails_bc,
    )

    sources = per_group // part
    return pl.pallas_call(
        carried_kernel,
        grid=(kids, groups),
        in_specs=[
            pl.BlockSpec((sources, 1, part, width, size), lambda c, q: (q, c, 0, 0, 0)),
            pl.BlockSpec((1, length, size), lambda c, q: (c, 0, q)),
            pl.BlockSpec((1, 1, length, per_group), lambda c, q: (c, q, 0, 0)),
            pl.BlockSpec((1, length, wide), lambda c, q: (c, 0, q)),
        ],
        out_specs=pl.BlockSpec((1, length, wide), lambda c, q: (c, 0, q)),
        out_shape=jax.ShapeDtypeStruct((kids, length, columns), jnp.bfloat16),
        compiler_params=pltpu.CompilerParams(vmem_limit_bytes=VMEM_LIMIT),
        cost_estimate=pl.CostEstimate(
            flops=2 * kids * length * columns * size,
            bytes_accessed=8 * kids * length * columns,
            transcendentals=0,
        ),
        name="carried",
    )(states, c_conv, grow, mixed)


def local_grid(
    x_in, b_in, c_in, dt_in, dt_bias, a_log, d_skip, conv_x, conv_bc,
    par_state, tail_x, tail_bc, counts, order,
):
    kids, length, columns = x_in.shape
    heads = dt_in.shape[1]
    width, size = par_state.shape[2:]
    groups = b_in.shape[2] // size
    per_group = heads // groups
    wide = per_group * width
    taps = conv_x.shape[0]
    reach = taps - 1
    half_heads = heads // 2
    part = half_heads // CHUNKS

    index = lax.axis_index("batch")
    z, y = index // 2, index % 2
    parent = parent_of(counts, order)
    inner = (z == 1) | (z == 2)
    flags = jnp.stack([inner.astype(jnp.int32), y.astype(jnp.int32)])

    def slot(child):
        owner = parent[child]
        step = owner // 2 - z
        place = jnp.where(step == 0, 0, jnp.where(step == -1, 1, jnp.where(step == 1, 2, 3)))
        return place + 4 * (owner % 2 != y).astype(jnp.int32)

    outer = jnp.where(z <= 1, 0, 3)
    kid = jnp.arange(kids, dtype=jnp.int32)
    wanted = jnp.concatenate(
        [
            (z * 2 + y) * kids + kid,
            (outer * 2 + y) * kids + kid,
            (outer * 2 + 1 - y) * kids + kid,
            (z * 2 + 1 - y) * kids + kid,
        ]
    )
    slots = slot(wanted)

    near, back, leap, across, out = routes()
    send = functools.partial(lax.ppermute, axis_name="batch")
    halves = par_state.reshape(2, half_heads, width, size)
    tails = pack_tails(tail_x, tail_bc, width, size)

    def gather(k, tokens):
        extra = 1 if k == 0 else 0
        specs = [
            pl.BlockSpec((1, part, width, size), lambda i, f: (f[1], k, 0, 0)),
            pl.BlockSpec((1, part, width, size), lambda i, f: (1 - f[1], k, 0, 0)),
        ]
        operands = [halves, halves]
        if extra:
            specs += [
                pl.BlockSpec((1, width, size), lambda i, f: (f[1], 0, 0)),
                pl.BlockSpec((1, width, size), lambda i, f: (1 - f[1], 0, 0)),
            ]
            operands += [tails, tails]
        inputs = len(operands)
        operands += tokens
        specs += [pl.BlockSpec(memory_space=pl.ANY)] * len(tokens)
        block = (extra + part, width, size)
        mine, other = pl.pallas_call(
            functools.partial(cast_kernel, inputs),
            grid_spec=pltpu.PrefetchScalarGridSpec(
                num_scalar_prefetch=1,
                grid=(1,),
                in_specs=specs,
                out_specs=[pl.BlockSpec(block, lambda i, f: (0, 0, 0))] * 2,
            ),
            out_shape=[jax.ShapeDtypeStruct(block, jnp.bfloat16)] * 2,
            compiler_params=pltpu.CompilerParams(vmem_limit_bytes=VMEM_LIMIT),
            cost_estimate=pl.CostEstimate(
                flops=0, bytes_accessed=12 * part * width * size, transcendentals=0
            ),
            name="cast_states",
        )(flags, *operands)
        return (
            mine,
            send(mine, perm=near[0]),
            send(mine, perm=back[0]),
            send(mine, perm=leap[0]),
            send(other, perm=across),
            send(other, perm=near[1]),
            send(other, perm=back[1]),
            send(other, perm=leap[1]),
        )

    x_conv, b_conv, c_conv, row, column = pl.pallas_call(
        conv_kernel,
        grid=(kids, groups),
        in_specs=[
            pl.BlockSpec((1, length, wide), lambda c, q: (c, 0, q)),
            pl.BlockSpec((1, length, size), lambda c, q: (c, 0, q)),
            pl.BlockSpec((1, length, size), lambda c, q: (c, 0, q)),
            pl.BlockSpec((1, per_group, length), lambda c, q: (c, q, 0)),
            pl.BlockSpec((per_group, 1), lambda c, q: (q, 0)),
            pl.BlockSpec((per_group, 1), lambda c, q: (q, 0)),
            pl.BlockSpec((taps, wide), lambda c, q: (0, q)),
            pl.BlockSpec((2, taps, size), lambda c, q: (0, 0, q)),
        ],
        out_specs=[
            pl.BlockSpec((1, length, wide), lambda c, q: (c, 0, q)),
            pl.BlockSpec((1, length, size), lambda c, q: (c, 0, q)),
            pl.BlockSpec((1, length, size), lambda c, q: (c, 0, q)),
            pl.BlockSpec((1, per_group, length), lambda c, q: (c, q, 0)),
            pl.BlockSpec((1, 1, length, per_group), lambda c, q: (c, q, 0, 0)),
        ],
        out_shape=[
            jax.ShapeDtypeStruct(x_in.shape, jnp.bfloat16),
            jax.ShapeDtypeStruct(b_in.shape, jnp.bfloat16),
            jax.ShapeDtypeStruct(c_in.shape, jnp.bfloat16),
            jax.ShapeDtypeStruct(dt_in.shape, jnp.float32),
            jax.ShapeDtypeStruct((kids, groups, length, per_group), jnp.float32),
        ],
        scratch_shapes=[pltpu.VMEM((8 + length, size), jnp.float32)],
        compiler_params=pltpu.CompilerParams(vmem_limit_bytes=VMEM_LIMIT),
        cost_estimate=pl.CostEstimate(
            flops=20 * kids * length * columns,
            bytes_accessed=4 * kids * length * columns,
            transcendentals=kids * length * columns,
        ),
        name="conv",
    )(x_in, b_in, c_in, dt_in, dt_bias[:, None], a_log[:, None], conv_x, conv_bc)

    lines = (columns // 2 + groups * size) // 128
    skip_row = jnp.repeat(d_skip, width)[None, :]
    def select(k, tokens):
        block = gathered[k][0].shape
        own, to_a, to_b, to_c = pl.pallas_call(
            select_kernel,
            grid_spec=pltpu.PrefetchScalarGridSpec(
                num_scalar_prefetch=1,
                grid=(1,),
                in_specs=[pl.BlockSpec(memory_space=pl.ANY)] * (8 + len(tokens)),
                out_specs=[pl.BlockSpec(memory_space=pl.ANY)] * 4,
                scratch_shapes=[pltpu.SemaphoreType.DMA((4, kids))],
            ),
            out_shape=[jax.ShapeDtypeStruct((kids,) + block, jnp.bfloat16)] * 4,
            cost_estimate=pl.CostEstimate(
                flops=0, bytes_accessed=16 * kids * part * width * size, transcendentals=0
            ),
            name="select_states",
        )(slots, *gathered[k], *tokens)
        return own, send(to_a, perm=out[0]), send(to_b, perm=out[1]), send(to_c, perm=across)

    def mix(k, tails_here, states, result, tokens):
        chunk_wide = part * width
        group_at = k * part // per_group
        half_groups = groups // 2
        operands = [
            x_conv, x_in, b_conv, b_in, c_conv, c_in, row, column, skip_row, conv_x, conv_bc,
            *tails_here, *states,
        ]
        x_at = lambda c, h, f: (c, 0, h * CHUNKS + k)
        bc_at = lambda c, h, f: (c, 0, h * half_groups + group_at)
        state_spec = pl.BlockSpec((1, part, width, size), lambda c, h, f: (c, 0, 0, 0))
        specs = [
            pl.BlockSpec((1, length, chunk_wide), x_at),
            pl.BlockSpec((1, FIX, chunk_wide), x_at),
            pl.BlockSpec((1, length, size), bc_at),
            pl.BlockSpec((1, FIX, size), bc_at),
            pl.BlockSpec((1, length, size), bc_at),
            pl.BlockSpec((1, FIX, size), bc_at),
            pl.BlockSpec((1, part, length), lambda c, h, f: (c, h * CHUNKS + k, 0)),
            pl.BlockSpec(
                (1, 1, length, per_group), lambda c, h, f: (c, h * half_groups + group_at, 0, 0)
            ),
            pl.BlockSpec((1, chunk_wide), lambda c, h, f: (0, h * CHUNKS + k)),
            pl.BlockSpec((taps, chunk_wide), lambda c, h, f: (0, h * CHUNKS + k)),
            pl.BlockSpec((2, taps, size), lambda c, h, f: (0, 0, h * half_groups + group_at)),
            *[pl.BlockSpec((1, 1, width, size), lambda c, h, f: (c, part, 0, 0))] * 4,
            *[state_spec] * 4,
        ]
        operands += tokens
        specs += [pl.BlockSpec(memory_space=pl.ANY)] * len(tokens)
        alias = {}
        if result is not None:
            alias = {1 + len(operands): 0}
            operands.append(result)
            specs.append(pl.BlockSpec(memory_space=pl.ANY))
        return pl.pallas_call(
            functools.partial(out_kernel, k * part, group_at, lines),
            grid_spec=pltpu.PrefetchScalarGridSpec(
                num_scalar_prefetch=1,
                grid=(kids, 2),
                in_specs=specs,
                out_specs=pl.BlockSpec((1, length, chunk_wide), x_at),
                scratch_shapes=[pltpu.VMEM((8 + FIX, size), jnp.float32)],
            ),
            out_shape=jax.ShapeDtypeStruct(x_in.shape, jnp.bfloat16),
            input_output_aliases=alias,
            compiler_params=pltpu.CompilerParams(vmem_limit_bytes=VMEM_LIMIT),
            cost_estimate=pl.CostEstimate(
                flops=2 * kids * 2 * part * length * width * (length + size),
                bytes_accessed=8 * kids * length * chunk_wide,
                transcendentals=kids * 2 * part * length * length,
            ),
            name="mix",
        )(flags, *operands)

    gathered = [gather(0, [])]
    gathered.append(gather(1, [gathered[0][0]]))
    result, states = None, []
    for k in range(CHUNKS):
        states.append(select(k, [x_conv] if k == 0 else [] if k == 1 else [result]))
        if k + 2 < CHUNKS:
            gathered.append(gather(k + 2, [states[k][0]]))
        if k > 0:
            result = mix(k - 1, states[0], states[k - 1], result, [states[k][0]])
    return mix(CHUNKS - 1, states[0], states[-1], result, [])


def solution(mesh):
    rows, cols = P(("groups", "batch"), None, "head"), P(("groups", "batch"), "head")
    placed = (
        rows, rows, rows, cols, P("head"), P("head"), P("head"), P(None, "head"),
        P(None, None, "head"), cols, rows, P(("groups", "batch"), None, None, "head"),
        P("groups"), P("groups"),
    )
    grid = mesh.shape["batch"] == 8
    local = local_grid if grid else local_any
    return jax.shard_map(local, mesh=mesh, in_specs=placed, out_specs=rows, check_vma=False)
```

```python
import functools

import jax
import jax.numpy as jnp
from jax import lax
from jax.experimental import pallas as pl
from jax.experimental.pallas import tpu as pltpu
from jax.sharding import PartitionSpec as P

VMEM_LIMIT = 60 * 1024 * 1024
SPLIT = (8, 8)
FIX = 16


def drop_tokens(kernel, keep, tokens, *refs):
    kernel(*refs[:keep], *refs[keep + tokens :])


def parent_of(counts, order):
    index = jnp.arange(counts.shape[0], dtype=jnp.int32)
    bounds = jnp.sum(jnp.where(index[None, :] <= index[:, None], counts[None, :], 0), axis=1)
    return jnp.sum((bounds[None, :] <= order[:, None]).astype(jnp.int32), axis=1)


def conv_silu(padded, tail, rows, taps):
    length = rows.shape[0]
    reach = taps.shape[0] - 1
    padded[8 - reach : 8, :] = jnp.broadcast_to(tail, (reach, rows.shape[1])).astype(jnp.float32)
    padded[8 : 8 + length, :] = rows.astype(jnp.float32)
    total = padded[8 - reach : 8 - reach + length, :] * taps[0:1, :]
    for k in range(1, reach + 1):
        total = total + padded[8 - reach + k : 8 - reach + k + length, :] * taps[k : k + 1, :]
    half = 0.5 * total
    return (half + half * jnp.tanh(half)).astype(jnp.bfloat16)


def conv_kernel(
    x_ref, b_ref, c_ref, dt_ref, bias_ref, alog_ref, taps_x_ref, taps_bc_ref,
    xc_ref, bc_ref, cc_ref, row_ref, column_ref, padded,
):
    length = x_ref.shape[1]
    lanes_all = x_ref.shape[2]
    bc_ref[0] = conv_silu(padded, 0.0, b_ref[0], taps_bc_ref[0])
    cc_ref[0] = conv_silu(padded, 0.0, c_ref[0], taps_bc_ref[1])
    for start in range(0, lanes_all, 128):
        lanes = slice(start, start + 128)
        xc_ref[0, :, lanes] = conv_silu(padded, 0.0, x_ref[0, :, lanes], taps_x_ref[:, lanes])
    raw = dt_ref[0] + bias_ref[...]
    step = jnp.maximum(raw, 0.0) + jnp.log1p(jnp.exp(-jnp.abs(raw)))
    per_token = step * (-jnp.exp(alog_ref[...]))
    row = lax.broadcasted_iota(jnp.int32, (length, length), 0)
    col = lax.broadcasted_iota(jnp.int32, (length, length), 1)
    total = lax.dot_general(
        per_token,
        (row <= col).astype(jnp.float32),
        (((1,), (0,)), ((), ())),
        precision=lax.Precision.HIGHEST,
        preferred_element_type=jnp.float32,
    )
    row_ref[0] = total - jnp.log(step)
    column_ref[0, 0] = total.T


def mix_kernel(
    lines, x_ref, xin_ref, b_ref, bin_ref, c_ref, cin_ref, row_ref, column_ref, skip_ref,
    taps_x_ref, taps_bc_ref, tail_ref, *refs,
):
    mixed_ref, c_out_ref, padded = refs[-3:]
    length = x_ref.shape[1]
    heads = row_ref.shape[1]
    width = x_ref.shape[2] // heads
    half = length // 2
    reach = taps_x_ref.shape[0] - 1
    tail = tail_ref[0, 0].astype(jnp.float32)

    def fixed(bulk_ref, first_ref, lanes, taps, at):
        rows = jnp.concatenate([tail[k * lines + at : k * lines + at + 1] for k in range(reach)])
        first = conv_silu(padded, rows, first_ref[0, :, lanes], taps)
        return jnp.concatenate([first, bulk_ref[0, FIX:, lanes]])

    every = slice(0, b_ref.shape[2])
    b_conv = fixed(b_ref, bin_ref, every, taps_bc_ref[0], lines - 2)
    c_conv = fixed(c_ref, cin_ref, every, taps_bc_ref[1], lines - 1)
    c_out_ref[0] = c_conv
    scores = lax.dot_general(
        c_conv, b_conv, (((1,), (1,)), ((), ())), preferred_element_type=jnp.float32
    )
    causal = lax.broadcasted_iota(jnp.int32, (half, half), 0) >= lax.broadcasted_iota(
        jnp.int32, (half, half), 1
    )
    low = lax.broadcasted_iota(jnp.int32, (length, 2 * width), 1) < width
    for pair in range(heads // 2):
        lanes = slice(pair * 2 * width, (pair + 1) * 2 * width)
        x_conv = fixed(x_ref, xin_ref, lanes, taps_x_ref[:, lanes], pair)
        parts = []
        for head in (2 * pair, 2 * pair + 1):
            column = jnp.broadcast_to(column_ref[0, 0, :, head : head + 1], (length, half))
            rows = row_ref[0, head : head + 1, :]
            near = jnp.exp(jnp.where(causal, column[:half] - rows[:, :half], -1e30))
            far = jnp.exp(column[half:] - rows[:, :half])
            last = jnp.exp(jnp.where(causal, column[half:] - rows[:, half:], -1e30))
            top = (scores[:half, :half] * near).astype(jnp.bfloat16)
            left = (scores[half:, :half] * far).astype(jnp.bfloat16)
            right = (scores[half:, half:] * last).astype(jnp.bfloat16)
            below = jnp.concatenate([left, right], axis=1)
            parts.append(
                jnp.concatenate(
                    [
                        jnp.dot(top, x_conv[:half], preferred_element_type=jnp.float32),
                        jnp.dot(below, x_conv, preferred_element_type=jnp.float32),
                    ]
                )
            )
        mixed_ref[0, :, lanes] = jnp.where(low, parts[0], parts[1]) + skip_ref[
            :, lanes
        ] * x_conv.astype(jnp.float32)


def state_kernel(offset, state_ref, c_ref, column_ref, mixed_ref, *refs):
    y_ref = refs[-1]
    length, wide = y_ref.shape[1:]
    pairs = wide // 128
    width = 64
    low = lax.broadcasted_iota(jnp.int32, (length, 128), 1) < width
    term = lax.dot_general(
        c_ref[0], state_ref[0, 0], (((1,), (1,)), ((), ())), preferred_element_type=jnp.float32
    )
    for pair in range(pairs):
        lanes = slice(pair * 128, pair * 128 + 128)
        head = offset + 2 * pair
        grow = jnp.where(
            low, column_ref[0, 0, :, head : head + 1], column_ref[0, 0, :, head + 1 : head + 2]
        )
        carried = (term[:, lanes] * jnp.exp(grow)).astype(jnp.bfloat16).astype(jnp.float32)
        y_ref[0, :, lanes] = (mixed_ref[0, :, lanes] + carried).astype(jnp.bfloat16)


def cast_kernel(state_ref, *refs):
    out_ref = refs[-1]
    rows = state_ref.shape[1] * state_ref.shape[2]
    value = state_ref[0].reshape(rows, state_ref.shape[3]).astype(jnp.bfloat16)
    for side in range(2):
        out_ref[side, 0, :rows] = value
    if len(refs) > 1:
        x_tail, bc_tail = refs[0][0].astype(jnp.float32), refs[1][0].astype(jnp.float32)
        reach, wide = x_tail.shape
        lines = []
        for k in range(reach):
            lines += [x_tail[k : k + 1, at : at + 128] for at in range(0, wide, 128)]
            lines += [bc_tail[0, k : k + 1], bc_tail[1, k : k + 1]]
        spare = out_ref.shape[2] - rows - len(lines)
        lines = jnp.concatenate(lines + [jnp.zeros((spare, 128), jnp.float32)])
        for side in range(2):
            out_ref[side, 0, rows:] = lines.astype(jnp.bfloat16)


def pick_rows_kernel(slots_ref, held_ref, *refs):
    outs, sems = refs[:-1], refs[-1]
    spots = outs[0].shape[0]
    starts = [0, outs[0].shape[1]]
    copies = []
    for at, out in enumerate(outs):
        rows = pl.ds(starts[at], out.shape[1])
        for i in range(spots):
            copies.append(
                pltpu.make_async_copy(
                    held_ref.at[slots_ref[i], rows], out.at[i], sems.at[at, i]
                )
            )
    for copy in copies:
        copy.start()
    for copy in copies:
        copy.wait()


def within_kernel(
    parent_ref,
    x_ref,
    b_ref,
    c_ref,
    dt_ref,
    bias_ref,
    alog_ref,
    skip_ref,
    taps_x_ref,
    taps_bc_ref,
    tail_x_ref,
    tail_bc_ref,
    mixed_ref,
    c_out_ref,
    grow_ref,
    padded,
):
    length = x_ref.shape[1]
    heads = dt_ref.shape[1]
    width = x_ref.shape[2] // heads
    b_conv = conv_silu(padded, tail_bc_ref[0, 0], b_ref[0], taps_bc_ref[0])
    c_conv = conv_silu(padded, tail_bc_ref[0, 1], c_ref[0], taps_bc_ref[1])
    c_out_ref[0] = c_conv
    scores = lax.dot_general(
        c_conv, b_conv, (((1,), (1,)), ((), ())), preferred_element_type=jnp.float32
    )
    raw = dt_ref[0] + bias_ref[...]
    step = jnp.maximum(raw, 0.0) + jnp.log1p(jnp.exp(-jnp.abs(raw)))
    per_token = step * (-jnp.exp(alog_ref[...]))
    row = lax.broadcasted_iota(jnp.int32, (length, length), 0)
    col = lax.broadcasted_iota(jnp.int32, (length, length), 1)
    upper = (row <= col).astype(jnp.float32)
    total = lax.dot_general(
        per_token,
        upper,
        (((1,), (0,)), ((), ())),
        precision=lax.Precision.HIGHEST,
        preferred_element_type=jnp.float32,
    )
    total_t = total.T
    grow_ref[0, 0] = jnp.exp(total_t)
    causal = row >= col
    low = lax.broadcasted_iota(jnp.int32, (length, 2 * width), 1) < width
    for pair in range(heads // 2):
        lanes = slice(pair * 2 * width, (pair + 1) * 2 * width)
        x_conv = conv_silu(
            padded, tail_x_ref[0, :, lanes], x_ref[0, :, lanes], taps_x_ref[:, lanes]
        )
        parts = []
        for head in (2 * pair, 2 * pair + 1):
            gap = total_t[:, head : head + 1] - total[head : head + 1, :]
            factor = jnp.exp(jnp.where(causal, gap, -1e30))
            mixing = (scores * factor * step[head : head + 1, :]).astype(jnp.bfloat16)
            parts.append(jnp.dot(mixing, x_conv, preferred_element_type=jnp.float32))
        mixed_ref[0, :, lanes] = (
            jnp.where(low, parts[0], parts[1]) + skip_ref[:, lanes] * x_conv.astype(jnp.float32)
        )


def carried_kernel(state_ref, c_ref, grow_ref, mixed_ref, y_ref):
    sources, _, part, width, size = state_ref.shape
    length = c_ref.shape[1]
    low = lax.broadcasted_iota(jnp.int32, (length, 2 * width), 1) < width
    c_conv = c_ref[0]
    for source in range(sources):
        state = state_ref[source, 0].reshape(part * width, size)
        term = lax.dot_general(
            c_conv, state, (((1,), (1,)), ((), ())), preferred_element_type=jnp.float32
        )
        for pair in range(part // 2):
            head = source * part + 2 * pair
            grow = jnp.where(
                low, grow_ref[0, 0, :, head : head + 1], grow_ref[0, 0, :, head + 1 : head + 2]
            )
            here = slice(2 * pair * width, (2 * pair + 2) * width)
            lanes = slice(head * width, (head + 2) * width)
            carried = (term[:, here] * grow).astype(jnp.bfloat16).astype(jnp.float32)
            y_ref[0, :, lanes] = (mixed_ref[0, :, lanes] + carried).astype(jnp.bfloat16)


def pick_kernel(parent_ref, state_ref, out_ref):
    out_ref[...] = state_ref[...]


def local_any(
    x_in,
    b_in,
    c_in,
    dt_in,
    dt_bias,
    a_log,
    d_skip,
    conv_x,
    conv_bc,
    par_state,
    tail_x,
    tail_bc,
    counts,
    order,
):
    kids, length, columns = x_in.shape
    heads = dt_in.shape[1]
    width, size = par_state.shape[2:]
    ways = lax.axis_size("batch")
    groups = b_in.shape[2] // size
    per_group = heads // groups
    part = heads // ways
    wide = per_group * width
    reach = tail_x.shape[1]
    parents_all = counts.shape[0]
    kids_all = order.shape[0]

    parent = parent_of(counts, order)
    own = lax.dynamic_slice_in_dim(parent, lax.axis_index("batch") * kids, kids)

    sent = par_state.astype(jnp.bfloat16).reshape(ways, part, width, size)
    shares = lax.all_to_all(sent, "batch", split_axis=0, concat_axis=0, tiled=True)

    tails = jnp.concatenate([tail_x.reshape(-1), tail_bc.reshape(-1)])
    tails = jnp.broadcast_to(tails[None], (ways, tails.shape[0]))
    tails = lax.all_to_all(tails, "batch", split_axis=0, concat_axis=0, tiled=True)
    tails_x = tails[:, : reach * columns].reshape(parents_all, reach, columns)
    tails_bc = tails[:, reach * columns :].reshape(parents_all, 2, reach, groups * size)

    picked = pl.pallas_call(
        pick_kernel,
        grid_spec=pltpu.PrefetchScalarGridSpec(
            num_scalar_prefetch=1,
            grid=(kids_all,),
            in_specs=[pl.BlockSpec((1, part, width, size), lambda i, p: (p[i], 0, 0, 0))],
            out_specs=pl.BlockSpec((1, part, width, size), lambda i, p: (i, 0, 0, 0)),
        ),
        out_shape=jax.ShapeDtypeStruct((kids_all, part, width, size), jnp.bfloat16),
        cost_estimate=pl.CostEstimate(
            flops=0, bytes_accessed=4 * kids_all * part * width * size, transcendentals=0
        ),
        name="pick_states",
    )(parent, shares)
    states = lax.all_to_all(
        picked.reshape(ways, kids, part, width, size), "batch", split_axis=0, concat_axis=0, tiled=True
    )

    skip_row = jnp.repeat(d_skip, width)[None, :]
    mixed, c_conv, grow = pl.pallas_call(
        within_kernel,
        grid_spec=pltpu.PrefetchScalarGridSpec(
            num_scalar_prefetch=1,
            grid=(kids, groups),
            in_specs=[
                pl.BlockSpec((1, length, wide), lambda c, q, p: (c, 0, q)),
                pl.BlockSpec((1, length, size), lambda c, q, p: (c, 0, q)),
                pl.BlockSpec((1, length, size), lambda c, q, p: (c, 0, q)),
                pl.BlockSpec((1, per_group, length), lambda c, q, p: (c, q, 0)),
                pl.BlockSpec((per_group, 1), lambda c, q, p: (q, 0)),
                pl.BlockSpec((per_group, 1), lambda c, q, p: (q, 0)),
                pl.BlockSpec((1, wide), lambda c, q, p: (0, q)),
                pl.BlockSpec((reach + 1, wide), lambda c, q, p: (0, q)),
                pl.BlockSpec((2, reach + 1, size), lambda c, q, p: (0, 0, q)),
                pl.BlockSpec((1, reach, wide), lambda c, q, p: (p[c], 0, q)),
                pl.BlockSpec((1, 2, reach, size), lambda c, q, p: (p[c], 0, 0, q)),
            ],
            out_specs=[
                pl.BlockSpec((1, length, wide), lambda c, q, p: (c, 0, q)),
                pl.BlockSpec((1, length, size), lambda c, q, p: (c, 0, q)),
                pl.BlockSpec((1, 1, length, per_group), lambda c, q, p: (c, q, 0, 0)),
            ],
            scratch_shapes=[pltpu.VMEM((8 + length, size), jnp.float32)],
        ),
        out_shape=[
            jax.ShapeDtypeStruct((kids, length, columns), jnp.float32),
            jax.ShapeDtypeStruct((kids, length, groups * size), jnp.bfloat16),
            jax.ShapeDtypeStruct((kids, groups, length, per_group), jnp.float32),
        ],
        compiler_params=pltpu.CompilerParams(vmem_limit_bytes=VMEM_LIMIT),
        cost_estimate=pl.CostEstimate(
            flops=4 * kids * heads * length * length * width,
            bytes_accessed=6 * kids * length * columns,
            transcendentals=kids * heads * length * length,
        ),
        name="within",
    )(
        own,
        x_in,
        b_in,
        c_in,
        dt_in,
        dt_bias[:, None],
        a_log[:, None],
        skip_row,
        conv_x,
        conv_bc,
        tails_x,
        tails_bc,
    )

    sources = per_group // part
    return pl.pallas_call(
        carried_kernel,
        grid=(kids, groups),
        in_specs=[
            pl.BlockSpec((sources, 1, part, width, size), lambda c, q: (q, c, 0, 0, 0)),
            pl.BlockSpec((1, length, size), lambda c, q: (c, 0, q)),
            pl.BlockSpec((1, 1, length, per_group), lambda c, q: (c, q, 0, 0)),
            pl.BlockSpec((1, length, wide), lambda c, q: (c, 0, q)),
        ],
        out_specs=pl.BlockSpec((1, length, wide), lambda c, q: (c, 0, q)),
        out_shape=jax.ShapeDtypeStruct((kids, length, columns), jnp.bfloat16),
        compiler_params=pltpu.CompilerParams(vmem_limit_bytes=VMEM_LIMIT),
        cost_estimate=pl.CostEstimate(
            flops=2 * kids * length * columns * size,
            bytes_accessed=8 * kids * length * columns,
            transcendentals=0,
        ),
        name="carried",
    )(states, c_conv, grow, mixed)


def local_halves(
    x_in, b_in, c_in, dt_in, dt_bias, a_log, d_skip, conv_x, conv_bc,
    par_state, tail_x, tail_bc, counts, order,
):
    kids, length, columns = x_in.shape
    heads = dt_in.shape[1]
    width, size = par_state.shape[2:]
    groups = b_in.shape[2] // size
    per_group = heads // groups
    wide = per_group * width
    taps = conv_x.shape[0]
    ways = lax.axis_size("batch")
    side = ways // 2
    halves = [list(range(side)), list(range(side, ways))]
    lines = (wide + 2 * size) // 128
    tail_lines = -(-lines * (taps - 1) // 16) * 16
    exchange = functools.partial(
        lax.all_to_all, axis_name="batch", split_axis=0, concat_axis=0, tiled=True
    )

    parent = parent_of(counts, order)
    slots = lax.dynamic_slice_in_dim(
        parent, lax.axis_index("batch") // side * side * kids, side * kids
    )
    state = par_state.reshape(groups, per_group, width, size)

    offsets = [sum(SPLIT[:k]) for k in range(len(SPLIT))]

    def spread(k, tokens):
        part = SPLIT[k]
        rows = part * width + (tail_lines if k == 0 else 0)
        operands = [state] + ([tail_x, tail_bc] if k == 0 else [])
        specs = [
            pl.BlockSpec((1, part, width, size), lambda q: (q, offsets[k] // part, 0, 0)),
            pl.BlockSpec((1, taps - 1, wide), lambda q: (0, 0, q)),
            pl.BlockSpec((1, 2, taps - 1, size), lambda q: (0, 0, 0, q)),
        ][: len(operands)]
        sent = pl.pallas_call(
            functools.partial(drop_tokens, cast_kernel, len(operands), len(tokens)),
            grid=(groups,),
            in_specs=specs + [pl.BlockSpec(memory_space=pl.ANY)] * len(tokens),
            out_specs=pl.BlockSpec((2, 1, rows, size), lambda q: (0, q, 0, 0)),
            out_shape=jax.ShapeDtypeStruct((2, groups, rows, size), jnp.bfloat16),
            compiler_params=pltpu.CompilerParams(vmem_limit_bytes=VMEM_LIMIT),
            cost_estimate=pl.CostEstimate(
                flops=0, bytes_accessed=8 * groups * rows * size, transcendentals=0
            ),
            name="cast_states",
        )(*operands, *tokens)
        return sent, exchange(sent.reshape(ways, rows, size))

    def pick(k, held, tokens):
        rows = SPLIT[k] * width
        sizes = [rows] + ([tail_lines] if k == 0 else [])
        spots = side * kids
        picked = pl.pallas_call(
            functools.partial(drop_tokens, pick_rows_kernel, 2, len(tokens)),
            grid_spec=pltpu.PrefetchScalarGridSpec(
                num_scalar_prefetch=1,
                grid=(1,),
                in_specs=[pl.BlockSpec(held.shape, lambda i, s: (0, 0, 0))]
                + [pl.BlockSpec(memory_space=pl.ANY)] * len(tokens),
                out_specs=[pl.BlockSpec(memory_space=pl.ANY)] * len(sizes),
                scratch_shapes=[pltpu.SemaphoreType.DMA((len(sizes), spots))],
            ),
            out_shape=[jax.ShapeDtypeStruct((spots, r, size), jnp.bfloat16) for r in sizes],
            compiler_params=pltpu.CompilerParams(vmem_limit_bytes=VMEM_LIMIT),
            cost_estimate=pl.CostEstimate(
                flops=0, bytes_accessed=4 * spots * rows * size, transcendentals=0
            ),
            name="pick_states",
        )(slots, held, *tokens)
        return [exchange(p, axis_index_groups=halves) for p in picked[::-1]][::-1]

    sent, held = [], []
    for k in range(len(SPLIT)):
        buffer, gathered = spread(k, sent[-1:])
        sent.append(buffer)
        held.append(gathered)

    x_conv, b_conv, c_conv, row, column = pl.pallas_call(
        conv_kernel,
        grid=(kids, groups),
        in_specs=[
            pl.BlockSpec((1, length, wide), lambda c, q: (c, 0, q)),
            pl.BlockSpec((1, length, size), lambda c, q: (c, 0, q)),
            pl.BlockSpec((1, length, size), lambda c, q: (c, 0, q)),
            pl.BlockSpec((1, per_group, length), lambda c, q: (c, q, 0)),
            pl.BlockSpec((per_group, 1), lambda c, q: (q, 0)),
            pl.BlockSpec((per_group, 1), lambda c, q: (q, 0)),
            pl.BlockSpec((taps, wide), lambda c, q: (0, q)),
            pl.BlockSpec((2, taps, size), lambda c, q: (0, 0, q)),
        ],
        out_specs=[
            pl.BlockSpec((1, length, wide), lambda c, q: (c, 0, q)),
            pl.BlockSpec((1, length, size), lambda c, q: (c, 0, q)),
            pl.BlockSpec((1, length, size), lambda c, q: (c, 0, q)),
            pl.BlockSpec((1, per_group, length), lambda c, q: (c, q, 0)),
            pl.BlockSpec((1, 1, length, per_group), lambda c, q: (c, q, 0, 0)),
        ],
        out_shape=[
            jax.ShapeDtypeStruct(x_in.shape, jnp.bfloat16),
            jax.ShapeDtypeStruct(b_in.shape, jnp.bfloat16),
            jax.ShapeDtypeStruct(c_in.shape, jnp.bfloat16),
            jax.ShapeDtypeStruct(dt_in.shape, jnp.float32),
            jax.ShapeDtypeStruct((kids, groups, length, per_group), jnp.float32),
        ],
        scratch_shapes=[pltpu.VMEM((8 + length, size), jnp.float32)],
        compiler_params=pltpu.CompilerParams(vmem_limit_bytes=VMEM_LIMIT),
        cost_estimate=pl.CostEstimate(
            flops=20 * kids * length * columns,
            bytes_accessed=4 * kids * length * columns,
            transcendentals=kids * length * columns,
        ),
        name="conv",
    )(x_in, b_in, c_in, dt_in, dt_bias[:, None], a_log[:, None], conv_x, conv_bc)

    skip_row = jnp.repeat(d_skip, width)[None, :]

    def mix(c, tails_here, before, tokens):
        at = lambda q: (c, 0, q)
        operands = [
            x_conv, x_in, b_conv, b_in, c_conv, c_in, row, column, skip_row, conv_x, conv_bc,
            tails_here.reshape(side, kids, tail_lines, size), *tokens, *before,
        ]
        first = len(operands) - len(before)
        return pl.pallas_call(
            functools.partial(mix_kernel, lines),
            grid=(groups,),
            in_specs=[
                pl.BlockSpec((1, length, wide), at),
                pl.BlockSpec((1, FIX, wide), at),
                pl.BlockSpec((1, length, size), at),
                pl.BlockSpec((1, FIX, size), at),
                pl.BlockSpec((1, length, size), at),
                pl.BlockSpec((1, FIX, size), at),
                pl.BlockSpec((1, per_group, length), lambda q: (c, q, 0)),
                pl.BlockSpec((1, 1, length, per_group), lambda q: (c, q, 0, 0)),
                pl.BlockSpec((1, wide), lambda q: (0, q)),
                pl.BlockSpec((taps, wide), lambda q: (0, q)),
                pl.BlockSpec((2, taps, size), lambda q: (0, 0, q)),
                pl.BlockSpec((1, 1, tail_lines, size), lambda q: (q, c, 0, 0)),
                *[pl.BlockSpec(memory_space=pl.ANY)] * (len(tokens) + len(before)),
            ],
            out_specs=[pl.BlockSpec((1, length, wide), at), pl.BlockSpec((1, length, size), at)],
            out_shape=[
                jax.ShapeDtypeStruct(x_in.shape, jnp.float32),
                jax.ShapeDtypeStruct(c_in.shape, jnp.bfloat16),
            ],
            input_output_aliases={first + i: i for i in range(len(before))},
            scratch_shapes=[pltpu.VMEM((8 + FIX, size), jnp.float32)],
            compiler_params=pltpu.CompilerParams(vmem_limit_bytes=VMEM_LIMIT),
            cost_estimate=pl.CostEstimate(
                flops=4 * heads * length * length * width,
                bytes_accessed=6 * length * columns,
                transcendentals=heads * length * length,
            ),
            name="mix",
        )(*operands)

    def finish(k, states, mixed, result):
        part, offset = SPLIT[k], offsets[k]
        chunk = part * width
        blocks = per_group // part
        at = lambda c, q: (c, 0, q * blocks + offset // part)
        operands = [states.reshape(side, kids, chunk, size), mixed[1], column, mixed[0]]
        specs = [
            pl.BlockSpec((1, 1, chunk, size), lambda c, q: (q, c, 0, 0)),
            pl.BlockSpec((1, length, size), lambda c, q: (c, 0, q)),
            pl.BlockSpec((1, 1, length, per_group), lambda c, q: (c, q, 0, 0)),
            pl.BlockSpec((1, length, chunk), at),
        ]
        alias = {}
        if result is not None:
            alias = {len(operands): 0}
            operands.append(result)
            specs.append(pl.BlockSpec(memory_space=pl.ANY))
        return pl.pallas_call(
            functools.partial(state_kernel, offset),
            grid=(kids, groups),
            in_specs=specs,
            out_specs=pl.BlockSpec((1, length, chunk), at),
            out_shape=jax.ShapeDtypeStruct(x_in.shape, jnp.bfloat16),
            input_output_aliases=alias,
            compiler_params=pltpu.CompilerParams(vmem_limit_bytes=VMEM_LIMIT),
            cost_estimate=pl.CostEstimate(
                flops=2 * kids * groups * length * chunk * size,
                bytes_accessed=6 * kids * groups * length * chunk,
                transcendentals=kids * groups * length * chunk,
            ),
            name="add_states",
        )(*operands)

    arrived, tails_here = pick(0, held[0], [x_conv])
    mixed = mix(0, tails_here, [], [])
    states = [arrived] + [pick(k, held[k], [mixed[0]])[0] for k in range(1, len(SPLIT))]
    mixed = mix(1, tails_here, mixed, [])
    result = None
    for k in range(len(SPLIT)):
        result = finish(k, states[k], mixed, result)
    return result


def solution(mesh):
    rows, cols = P(("groups", "batch"), None, "head"), P(("groups", "batch"), "head")
    placed = (
        rows, rows, rows, cols, P("head"), P("head"), P("head"), P(None, "head"),
        P(None, None, "head"), cols, rows, P(("groups", "batch"), None, None, "head"),
        P("groups"), P("groups"),
    )
    local = local_halves if mesh.shape["batch"] == 8 else local_any
    return jax.shard_map(local, mesh=mesh, in_specs=placed, out_specs=rows, check_vma=False)
```

```python
import functools

import jax
import jax.numpy as jnp
from jax import lax
from jax.experimental import pallas as pl
from jax.experimental.pallas import tpu as pltpu
from jax.sharding import PartitionSpec as P

VMEM_LIMIT = 20 * 1024 * 1024
SPLIT = (8, 8)
FIX = 16


def drop_tokens(kernel, keep, tokens, *refs):
    kernel(*refs[:keep], *refs[keep + tokens :])


def parent_of(counts, order):
    index = jnp.arange(counts.shape[0], dtype=jnp.int32)
    bounds = jnp.sum(jnp.where(index[None, :] <= index[:, None], counts[None, :], 0), axis=1)
    return jnp.sum((bounds[None, :] <= order[:, None]).astype(jnp.int32), axis=1)


def conv_silu(padded, tail, rows, taps):
    length = rows.shape[0]
    reach = taps.shape[0] - 1
    padded[8 - reach : 8, :] = jnp.broadcast_to(tail, (reach, rows.shape[1])).astype(jnp.float32)
    padded[8 : 8 + length, :] = rows.astype(jnp.float32)
    total = padded[8 - reach : 8 - reach + length, :] * taps[0:1, :]
    for k in range(1, reach + 1):
        total = total + padded[8 - reach + k : 8 - reach + k + length, :] * taps[k : k + 1, :]
    half = 0.5 * total
    return (half + half * jnp.tanh(half)).astype(jnp.bfloat16)


def conv_kernel(
    x_ref, b_ref, c_ref, dt_ref, bias_ref, alog_ref, taps_x_ref, taps_bc_ref,
    xc_ref, bc_ref, cc_ref, row_ref, column_ref, padded,
):
    length = x_ref.shape[1]
    lanes_all = x_ref.shape[2]
    bc_ref[...] = conv_silu(padded, 0.0, b_ref[0], taps_bc_ref[0])
    cc_ref[...] = conv_silu(padded, 0.0, c_ref[0], taps_bc_ref[1])
    for start in range(0, lanes_all, 128):
        lanes = slice(start, start + 128)
        xc_ref[:, lanes] = conv_silu(padded, 0.0, x_ref[0, :, lanes], taps_x_ref[:, lanes])
    raw = dt_ref[0] + bias_ref[...]
    step = jnp.maximum(raw, 0.0) + jnp.log1p(jnp.exp(-jnp.abs(raw)))
    per_token = step * (-jnp.exp(alog_ref[...]))
    row = lax.broadcasted_iota(jnp.int32, (length, length), 0)
    col = lax.broadcasted_iota(jnp.int32, (length, length), 1)
    total = lax.dot_general(
        per_token,
        (row <= col).astype(jnp.float32),
        (((1,), (0,)), ((), ())),
        precision=lax.Precision.HIGHEST,
        preferred_element_type=jnp.float32,
    )
    row_ref[...] = total - jnp.log(step)
    column_ref[0] = total.T


def choose(refs, place):
    j = place ^ pl.program_id(0)
    near = jnp.where(j == 0, refs[0][0], refs[1][0])
    return jnp.where(j <= 1, near, jnp.where(j == 2, refs[2][0], refs[3][0]))


def mix_kernel(
    lines, x_ref, xin_ref, b_ref, bin_ref, c_ref, cin_ref, row_ref, column_ref, skip_ref,
    taps_x_ref, taps_bc_ref, place_ref, *refs,
):
    mixed_ref, c_out_ref, padded = refs[-3:]
    length, wide = x_ref.shape
    heads = row_ref.shape[0]
    width = wide // heads
    half = length // 2
    reach = taps_x_ref.shape[0] - 1
    tail = choose(refs[:4], place_ref[0]).astype(jnp.float32)

    def fixed(bulk_ref, first_ref, lanes, taps, at):
        rows = jnp.concatenate([tail[k * lines + at : k * lines + at + 1] for k in range(reach)])
        first = conv_silu(padded, rows, first_ref[0, :, lanes], taps)
        return jnp.concatenate([first, bulk_ref[FIX:, lanes]])

    every = slice(0, b_ref.shape[1])
    b_conv = fixed(b_ref, bin_ref, every, taps_bc_ref[0], lines - 2)
    c_conv = fixed(c_ref, cin_ref, every, taps_bc_ref[1], lines - 1)
    c_out_ref[...] = c_conv
    scores = lax.dot_general(
        c_conv, b_conv, (((1,), (1,)), ((), ())), preferred_element_type=jnp.float32
    )
    causal = lax.broadcasted_iota(jnp.int32, (half, half), 0) >= lax.broadcasted_iota(
        jnp.int32, (half, half), 1
    )
    low = lax.broadcasted_iota(jnp.int32, (length, 2 * width), 1) < width
    for pair in range(heads // 2):
        lanes = slice(pair * 2 * width, (pair + 1) * 2 * width)
        x_conv = fixed(x_ref, xin_ref, lanes, taps_x_ref[:, lanes], pair)
        parts = []
        for head in (2 * pair, 2 * pair + 1):
            column = jnp.broadcast_to(column_ref[0, :, head : head + 1], (length, half))
            rows = row_ref[head : head + 1, :]
            near = jnp.exp(jnp.where(causal, column[:half] - rows[:, :half], -1e30))
            far = jnp.exp(column[half:] - rows[:, :half])
            last = jnp.exp(jnp.where(causal, column[half:] - rows[:, half:], -1e30))
            top = (scores[:half, :half] * near).astype(jnp.bfloat16)
            left = (scores[half:, :half] * far).astype(jnp.bfloat16)
            right = (scores[half:, half:] * last).astype(jnp.bfloat16)
            below = jnp.concatenate([left, right], axis=1)
            parts.append(
                jnp.concatenate(
                    [
                        jnp.dot(top, x_conv[:half], preferred_element_type=jnp.float32),
                        jnp.dot(below, x_conv, preferred_element_type=jnp.float32),
                    ]
                )
            )
        mixed_ref[:, lanes] = jnp.where(low, parts[0], parts[1]) + skip_ref[
            :, lanes
        ] * x_conv.astype(jnp.float32)


def state_kernel(offset, place_ref, *refs):
    y_ref = refs[-1]
    kids, length, wide = y_ref.shape
    low = lax.broadcasted_iota(jnp.int32, (length, 128), 1) < 64
    for kid in range(kids):
        c_ref, column_ref, mixed_ref = refs[7 * kid + 4 : 7 * kid + 7]
        state = choose(refs[7 * kid : 7 * kid + 4], place_ref[0])
        term = lax.dot_general(
            c_ref[...], state, (((1,), (1,)), ((), ())), preferred_element_type=jnp.float32
        )
        for pair in range(wide // 128):
            lanes = slice(pair * 128, pair * 128 + 128)
            head = offset + 2 * pair
            grow = jnp.where(
                low, column_ref[0, :, head : head + 1], column_ref[0, :, head + 1 : head + 2]
            )
            carried = (term[:, lanes] * jnp.exp(grow)).astype(jnp.bfloat16).astype(jnp.float32)
            y_ref[kid, :, lanes] = (mixed_ref[:, lanes] + carried).astype(jnp.bfloat16)


def cast_kernel(reach, lines, at_ref, *refs):
    outs = refs[-4:]
    for j, out_ref in enumerate(outs):
        state = refs[j][0]
        rows = state.shape[0] * state.shape[1]
        out_ref[:rows] = state.reshape(rows, state.shape[2]).astype(jnp.bfloat16)
        if lines:
            x_tail = refs[4 + j][0].astype(jnp.float32)
            bc_tail = refs[8 + j][0].astype(jnp.float32)
            parts = []
            for k in range(reach):
                parts += [x_tail[k : k + 1, i * 128 : i * 128 + 128] for i in range(lines - 2)]
                parts.append(bc_tail[k])
            spare = out_ref.shape[0] - rows - lines * reach
            parts.append(jnp.zeros((spare, 128), jnp.float32))
            out_ref[rows:] = jnp.concatenate(parts).astype(jnp.bfloat16)


def pick_rows_kernel(slots_ref, *refs):
    count = 8
    held, outs = refs[:count], refs[count:-3]
    stage, in_sems, out_sems = refs[-3:]
    kids = outs[0].shape[0]
    loads = [
        pltpu.make_async_copy(ref, stage.at[i], in_sems.at[i]) for i, ref in enumerate(held)
    ]
    for load in loads:
        load.start()
    for load in loads:
        load.wait()
    stores = [
        pltpu.make_async_copy(
            stage.at[slots_ref[j * kids + kid]], out.at[kid], out_sems.at[j, kid]
        )
        for j, out in enumerate(outs)
        for kid in range(kids)
    ]
    for store in stores:
        store.start()
    for store in stores:
        store.wait()


def within_kernel(
    parent_ref,
    x_ref,
    b_ref,
    c_ref,
    dt_ref,
    bias_ref,
    alog_ref,
    skip_ref,
    taps_x_ref,
    taps_bc_ref,
    tail_x_ref,
    tail_bc_ref,
    mixed_ref,
    c_out_ref,
    grow_ref,
    padded,
):
    length = x_ref.shape[1]
    heads = dt_ref.shape[1]
    width = x_ref.shape[2] // heads
    b_conv = conv_silu(padded, tail_bc_ref[0, 0], b_ref[0], taps_bc_ref[0])
    c_conv = conv_silu(padded, tail_bc_ref[0, 1], c_ref[0], taps_bc_ref[1])
    c_out_ref[0] = c_conv
    scores = lax.dot_general(
        c_conv, b_conv, (((1,), (1,)), ((), ())), preferred_element_type=jnp.float32
    )
    raw = dt_ref[0] + bias_ref[...]
    step = jnp.maximum(raw, 0.0) + jnp.log1p(jnp.exp(-jnp.abs(raw)))
    per_token = step * (-jnp.exp(alog_ref[...]))
    row = lax.broadcasted_iota(jnp.int32, (length, length), 0)
    col = lax.broadcasted_iota(jnp.int32, (length, length), 1)
    upper = (row <= col).astype(jnp.float32)
    total = lax.dot_general(
        per_token,
        upper,
        (((1,), (0,)), ((), ())),
        precision=lax.Precision.HIGHEST,
        preferred_element_type=jnp.float32,
    )
    total_t = total.T
    grow_ref[0, 0] = jnp.exp(total_t)
    causal = row >= col
    low = lax.broadcasted_iota(jnp.int32, (length, 2 * width), 1) < width
    for pair in range(heads // 2):
        lanes = slice(pair * 2 * width, (pair + 1) * 2 * width)
        x_conv = conv_silu(
            padded, tail_x_ref[0, :, lanes], x_ref[0, :, lanes], taps_x_ref[:, lanes]
        )
        parts = []
        for head in (2 * pair, 2 * pair + 1):
            gap = total_t[:, head : head + 1] - total[head : head + 1, :]
            factor = jnp.exp(jnp.where(causal, gap, -1e30))
            mixing = (scores * factor * step[head : head + 1, :]).astype(jnp.bfloat16)
            parts.append(jnp.dot(mixing, x_conv, preferred_element_type=jnp.float32))
        mixed_ref[0, :, lanes] = (
            jnp.where(low, parts[0], parts[1]) + skip_ref[:, lanes] * x_conv.astype(jnp.float32)
        )


def carried_kernel(state_ref, c_ref, grow_ref, mixed_ref, y_ref):
    sources, _, part, width, size = state_ref.shape
    length = c_ref.shape[1]
    low = lax.broadcasted_iota(jnp.int32, (length, 2 * width), 1) < width
    c_conv = c_ref[0]
    for source in range(sources):
        state = state_ref[source, 0].reshape(part * width, size)
        term = lax.dot_general(
            c_conv, state, (((1,), (1,)), ((), ())), preferred_element_type=jnp.float32
        )
        for pair in range(part // 2):
            head = source * part + 2 * pair
            grow = jnp.where(
                low, grow_ref[0, 0, :, head : head + 1], grow_ref[0, 0, :, head + 1 : head + 2]
            )
            here = slice(2 * pair * width, (2 * pair + 2) * width)
            lanes = slice(head * width, (head + 2) * width)
            carried = (term[:, here] * grow).astype(jnp.bfloat16).astype(jnp.float32)
            y_ref[0, :, lanes] = (mixed_ref[0, :, lanes] + carried).astype(jnp.bfloat16)


def pick_kernel(parent_ref, state_ref, out_ref):
    out_ref[...] = state_ref[...]


def local_any(
    x_in,
    b_in,
    c_in,
    dt_in,
    dt_bias,
    a_log,
    d_skip,
    conv_x,
    conv_bc,
    par_state,
    tail_x,
    tail_bc,
    counts,
    order,
):
    kids, length, columns = x_in.shape
    heads = dt_in.shape[1]
    width, size = par_state.shape[2:]
    ways = lax.axis_size("batch")
    groups = b_in.shape[2] // size
    per_group = heads // groups
    part = heads // ways
    wide = per_group * width
    reach = tail_x.shape[1]
    parents_all = counts.shape[0]
    kids_all = order.shape[0]

    parent = parent_of(counts, order)
    own = lax.dynamic_slice_in_dim(parent, lax.axis_index("batch") * kids, kids)

    sent = par_state.astype(jnp.bfloat16).reshape(ways, part, width, size)
    shares = lax.all_to_all(sent, "batch", split_axis=0, concat_axis=0, tiled=True)

    tails = jnp.concatenate([tail_x.reshape(-1), tail_bc.reshape(-1)])
    tails = jnp.broadcast_to(tails[None], (ways, tails.shape[0]))
    tails = lax.all_to_all(tails, "batch", split_axis=0, concat_axis=0, tiled=True)
    tails_x = tails[:, : reach * columns].reshape(parents_all, reach, columns)
    tails_bc = tails[:, reach * columns :].reshape(parents_all, 2, reach, groups * size)

    picked = pl.pallas_call(
        pick_kernel,
        grid_spec=pltpu.PrefetchScalarGridSpec(
            num_scalar_prefetch=1,
            grid=(kids_all,),
            in_specs=[pl.BlockSpec((1, part, width, size), lambda i, p: (p[i], 0, 0, 0))],
            out_specs=pl.BlockSpec((1, part, width, size), lambda i, p: (i, 0, 0, 0)),
        ),
        out_shape=jax.ShapeDtypeStruct((kids_all, part, width, size), jnp.bfloat16),
        cost_estimate=pl.CostEstimate(
            flops=0, bytes_accessed=4 * kids_all * part * width * size, transcendentals=0
        ),
        name="pick_states",
    )(parent, shares)
    states = lax.all_to_all(
        picked.reshape(ways, kids, part, width, size), "batch", split_axis=0, concat_axis=0, tiled=True
    )

    skip_row = jnp.repeat(d_skip, width)[None, :]
    mixed, c_conv, grow = pl.pallas_call(
        within_kernel,
        grid_spec=pltpu.PrefetchScalarGridSpec(
            num_scalar_prefetch=1,
            grid=(kids, groups),
            in_specs=[
                pl.BlockSpec((1, length, wide), lambda c, q, p: (c, 0, q)),
                pl.BlockSpec((1, length, size), lambda c, q, p: (c, 0, q)),
                pl.BlockSpec((1, length, size), lambda c, q, p: (c, 0, q)),
                pl.BlockSpec((1, per_group, length), lambda c, q, p: (c, q, 0)),
                pl.BlockSpec((per_group, 1), lambda c, q, p: (q, 0)),
                pl.BlockSpec((per_group, 1), lambda c, q, p: (q, 0)),
                pl.BlockSpec((1, wide), lambda c, q, p: (0, q)),
                pl.BlockSpec((reach + 1, wide), lambda c, q, p: (0, q)),
                pl.BlockSpec((2, reach + 1, size), lambda c, q, p: (0, 0, q)),
                pl.BlockSpec((1, reach, wide), lambda c, q, p: (p[c], 0, q)),
                pl.BlockSpec((1, 2, reach, size), lambda c, q, p: (p[c], 0, 0, q)),
            ],
            out_specs=[
                pl.BlockSpec((1, length, wide), lambda c, q, p: (c, 0, q)),
                pl.BlockSpec((1, length, size), lambda c, q, p: (c, 0, q)),
                pl.BlockSpec((1, 1, length, per_group), lambda c, q, p: (c, q, 0, 0)),
            ],
            scratch_shapes=[pltpu.VMEM((8 + length, size), jnp.float32)],
        ),
        out_shape=[
            jax.ShapeDtypeStruct((kids, length, columns), jnp.float32),
            jax.ShapeDtypeStruct((kids, length, groups * size), jnp.bfloat16),
            jax.ShapeDtypeStruct((kids, groups, length, per_group), jnp.float32),
        ],
        compiler_params=pltpu.CompilerParams(vmem_limit_bytes=VMEM_LIMIT),
        cost_estimate=pl.CostEstimate(
            flops=4 * kids * heads * length * length * width,
            bytes_accessed=6 * kids * length * columns,
            transcendentals=kids * heads * length * length,
        ),
        name="within",
    )(
        own,
        x_in,
        b_in,
        c_in,
        dt_in,
        dt_bias[:, None],
        a_log[:, None],
        skip_row,
        conv_x,
        conv_bc,
        tails_x,
        tails_bc,
    )

    sources = per_group // part
    return pl.pallas_call(
        carried_kernel,
        grid=(kids, groups),
        in_specs=[
            pl.BlockSpec((sources, 1, part, width, size), lambda c, q: (q, c, 0, 0, 0)),
            pl.BlockSpec((1, length, size), lambda c, q: (c, 0, q)),
            pl.BlockSpec((1, 1, length, per_group), lambda c, q: (c, q, 0, 0)),
            pl.BlockSpec((1, length, wide), lambda c, q: (c, 0, q)),
        ],
        out_specs=pl.BlockSpec((1, length, wide), lambda c, q: (c, 0, q)),
        out_shape=jax.ShapeDtypeStruct((kids, length, columns), jnp.bfloat16),
        compiler_params=pltpu.CompilerParams(vmem_limit_bytes=VMEM_LIMIT),
        cost_estimate=pl.CostEstimate(
            flops=2 * kids * length * columns * size,
            bytes_accessed=8 * kids * length * columns,
            transcendentals=0,
        ),
        name="carried",
    )(states, c_conv, grow, mixed)


def local_halves(
    x_in, b_in, c_in, dt_in, dt_bias, a_log, d_skip, conv_x, conv_bc,
    par_state, tail_x, tail_bc, counts, order,
):
    kids, length, columns = x_in.shape
    heads = dt_in.shape[1]
    width, size = par_state.shape[2:]
    groups = b_in.shape[2] // size
    per_group = heads // groups
    wide = per_group * width
    taps = conv_x.shape[0]
    reach = taps - 1
    lines = (wide + 2 * size) // 128
    tail_lines = -(-lines * reach // 16) * 16
    params = pltpu.CompilerParams(vmem_limit_bytes=VMEM_LIMIT)
    anywhere = pl.BlockSpec(memory_space=pl.ANY)

    stay = lambda x: pltpu.with_memory_space_constraint(x, pltpu.HBM)
    x_in, b_in, c_in, dt_in, conv_x, conv_bc = map(stay, (x_in, b_in, c_in, dt_in, conv_x, conv_bc))

    me = lax.axis_index("batch")
    parent = parent_of(counts, order)
    near = me ^ jnp.arange(4, dtype=jnp.int32)
    children = (near[:, None] * kids + jnp.arange(kids, dtype=jnp.int32)[None, :]).reshape(-1)
    slots = jnp.take(parent, children) ^ me
    place = (me % 4).astype(jnp.int32)[None]

    state = stay(par_state.reshape(groups, per_group, width, size))
    x_tails, bc_tails = stay(tail_x), stay(tail_bc.transpose(0, 2, 1, 3))
    offsets = [sum(SPLIT[:k]) for k in range(len(SPLIT))]

    def swap(value, r):
        return lax.ppermute(value, "batch", perm=[(i, i ^ r) for i in range(8)])

    def spread(k, tokens):
        part = SPLIT[k]
        rows = part * width + (tail_lines if k == 0 else 0)
        operands = [state] * 4
        specs = [
            pl.BlockSpec((1, part, width, size), lambda i, p, j=j: (p[0] ^ j, offsets[k] // part, 0, 0))
            for j in range(4)
        ]
        if k == 0:
            operands += [x_tails] * 4 + [bc_tails] * 4
            specs += [
                pl.BlockSpec((1, reach, wide), lambda i, p, j=j: (0, 0, p[0] ^ j)) for j in range(4)
            ]
            specs += [
                pl.BlockSpec((1, reach, 2, size), lambda i, p, j=j: (0, 0, 0, p[0] ^ j))
                for j in range(4)
            ]
        sent = pl.pallas_call(
            functools.partial(
                drop_tokens,
                functools.partial(cast_kernel, reach, lines if k == 0 else 0),
                1 + len(operands),
                len(tokens),
            ),
            grid_spec=pltpu.PrefetchScalarGridSpec(
                num_scalar_prefetch=1,
                grid=(1,),
                in_specs=specs + [anywhere] * len(tokens),
                out_specs=[pl.BlockSpec((rows, size), lambda i, p: (0, 0))] * 4,
            ),
            out_shape=[jax.ShapeDtypeStruct((rows, size), jnp.bfloat16)] * 4,
            compiler_params=params,
            cost_estimate=pl.CostEstimate(
                flops=0, bytes_accessed=24 * rows * size, transcendentals=0
            ),
            name="cast_states",
        )(place, *operands, *tokens)
        far = [swap(sent[j], j + 4) for j in range(4)]
        return [sent[0]] + [swap(sent[j], j) for j in range(1, 4)] + far

    def pick(k, held, tokens):
        rows = held[0].shape[0]
        picked = pl.pallas_call(
            functools.partial(drop_tokens, pick_rows_kernel, 9, len(tokens)),
            grid_spec=pltpu.PrefetchScalarGridSpec(
                num_scalar_prefetch=1,
                grid=(1,),
                in_specs=[anywhere] * (8 + len(tokens)),
                out_specs=[anywhere] * 4,
                scratch_shapes=[
                    pltpu.VMEM((8, rows, size), jnp.bfloat16),
                    pltpu.SemaphoreType.DMA((8,)),
                    pltpu.SemaphoreType.DMA((4, kids)),
                ],
            ),
            out_shape=[jax.ShapeDtypeStruct((kids, rows, size), jnp.bfloat16)] * 4,
            compiler_params=params,
            cost_estimate=pl.CostEstimate(
                flops=0, bytes_accessed=32 * kids * rows * size, transcendentals=0
            ),
            name="pick_states",
        )(slots, *held, *tokens)
        return [picked[0]] + [swap(picked[j], j) for j in range(1, 4)]

    def convolve(c, tokens):
        at = lambda q: (c, 0, q)
        operands = [
            x_in, b_in, c_in, dt_in, dt_bias[:, None], a_log[:, None], conv_x, conv_bc
        ]
        return pl.pallas_call(
            functools.partial(drop_tokens, conv_kernel, len(operands), len(tokens)),
            grid=(groups,),
            in_specs=[
                pl.BlockSpec((1, length, wide), at),
                pl.BlockSpec((1, length, size), at),
                pl.BlockSpec((1, length, size), at),
                pl.BlockSpec((1, per_group, length), lambda q: (c, q, 0)),
                pl.BlockSpec((per_group, 1), lambda q: (q, 0)),
                pl.BlockSpec((per_group, 1), lambda q: (q, 0)),
                pl.BlockSpec((taps, wide), lambda q: (0, q)),
                pl.BlockSpec((2, taps, size), lambda q: (0, 0, q)),
                *[anywhere] * len(tokens),
            ],
            out_specs=[
                pl.BlockSpec((length, wide), lambda q: (0, q)),
                pl.BlockSpec((length, size), lambda q: (0, q)),
                pl.BlockSpec((length, size), lambda q: (0, q)),
                pl.BlockSpec((per_group, length), lambda q: (q, 0)),
                pl.BlockSpec((1, length, per_group), lambda q: (q, 0, 0)),
            ],
            out_shape=[
                jax.ShapeDtypeStruct(x_in.shape[1:], jnp.bfloat16),
                jax.ShapeDtypeStruct(b_in.shape[1:], jnp.bfloat16),
                jax.ShapeDtypeStruct(c_in.shape[1:], jnp.bfloat16),
                jax.ShapeDtypeStruct(dt_in.shape[1:], jnp.float32),
                jax.ShapeDtypeStruct((groups, length, per_group), jnp.float32),
            ],
            scratch_shapes=[pltpu.VMEM((8 + length, size), jnp.float32)],
            compiler_params=params,
            cost_estimate=pl.CostEstimate(
                flops=40 * length * columns,
                bytes_accessed=4 * length * columns,
                transcendentals=2 * length * columns,
            ),
            name="conv",
        )(*operands, *tokens)

    def mix(c, early, states, tokens):
        x_conv, b_conv, c_conv, row, column = early
        at = lambda q: (0, q)
        tail_at = SPLIT[0] * width // tail_lines
        operands = [
            x_conv, x_in, b_conv, b_in, c_conv, c_in, row, column, skip_row, conv_x, conv_bc,
            place, *states,
        ]
        return pl.pallas_call(
            functools.partial(drop_tokens, functools.partial(mix_kernel, lines), 16, len(tokens)),
            grid=(groups,),
            in_specs=[
                pl.BlockSpec((length, wide), at),
                pl.BlockSpec((1, FIX, wide), lambda q: (c, 0, q)),
                pl.BlockSpec((length, size), at),
                pl.BlockSpec((1, FIX, size), lambda q: (c, 0, q)),
                pl.BlockSpec((length, size), at),
                pl.BlockSpec((1, FIX, size), lambda q: (c, 0, q)),
                pl.BlockSpec((per_group, length), lambda q: (q, 0)),
                pl.BlockSpec((1, length, per_group), lambda q: (q, 0, 0)),
                pl.BlockSpec((1, wide), at),
                pl.BlockSpec((taps, wide), at),
                pl.BlockSpec((2, taps, size), lambda q: (0, 0, q)),
                pl.BlockSpec(memory_space=pltpu.SMEM),
                *[pl.BlockSpec((1, tail_lines, size), lambda q: (c, tail_at, 0))] * 4,
                *[anywhere] * len(tokens),
            ],
            out_specs=[pl.BlockSpec((length, wide), at), pl.BlockSpec((length, size), at)],
            out_shape=[
                jax.ShapeDtypeStruct((length, columns), jnp.float32),
                jax.ShapeDtypeStruct((length, groups * size), jnp.bfloat16),
            ],
            scratch_shapes=[
                pltpu.VMEM((8 + FIX, size), jnp.float32),
            ],
            compiler_params=params,
            cost_estimate=pl.CostEstimate(
                flops=4 * heads * length * length * width,
                bytes_accessed=6 * length * columns,
                transcendentals=heads * length * length,
            ),
            name="mix",
        )(*operands, *tokens)

    def finish(k, states, early, mixed, result):
        part, offset = SPLIT[k], offsets[k]
        chunk = part * width
        at = lambda q, p: (0, q * (per_group // part) + offset // part)
        operands, specs = [], []
        for c in range(kids):
            operands += [*states, mixed[c][1], early[c][4], mixed[c][0]]
            specs += [
                *[pl.BlockSpec((1, chunk, size), lambda q, p, c=c: (c, 0, 0))] * 4,
                pl.BlockSpec((length, size), lambda q, p: (0, q)),
                pl.BlockSpec((1, length, per_group), lambda q, p: (q, 0, 0)),
                pl.BlockSpec((length, chunk), at),
            ]
        alias = {}
        if result is not None:
            alias = {1 + len(operands): 0}
            operands.append(result)
            specs.append(anywhere)
        return pl.pallas_call(
            functools.partial(state_kernel, offset),
            grid_spec=pltpu.PrefetchScalarGridSpec(
                num_scalar_prefetch=1,
                grid=(groups,),
                in_specs=specs,
                out_specs=pl.BlockSpec((kids, length, chunk), lambda q, p: (0, *at(q, p))),
            ),
            out_shape=jax.ShapeDtypeStruct(x_in.shape, jnp.bfloat16),
            input_output_aliases=alias,
            compiler_params=params,
            cost_estimate=pl.CostEstimate(
                flops=2 * kids * groups * length * chunk * size,
                bytes_accessed=6 * kids * groups * length * chunk,
                transcendentals=kids * groups * length * chunk,
            ),
            name="add_states",
        )(place, *operands)

    skip_row = jnp.repeat(d_skip, width)[None, :]
    held, early = [], []
    for k in range(len(SPLIT)):
        held.append(spread(k, [held[-1][0]] if k else []))
    early.append(convolve(0, [held[1][0]]))
    states = [pick(0, held[0], [early[0][0]])]
    early.append(convolve(1, [states[0][0]]))
    mixed = [mix(0, early[0], states[0], [early[1][0]])]
    states.append(pick(1, held[1], [mixed[0][1]]))
    mixed.append(mix(1, early[1], states[0], [states[1][0]]))
    result = None
    for k in range(len(SPLIT)):
        result = finish(k, states[k], early, mixed, result)
    return result


def solution(mesh):
    rows, cols = P(("groups", "batch"), None, "head"), P(("groups", "batch"), "head")
    placed = (
        rows, rows, rows, cols, P("head"), P("head"), P("head"), P(None, "head"),
        P(None, None, "head"), cols, rows, P(("groups", "batch"), None, None, "head"),
        P("groups"), P("groups"),
    )
    local = local_halves if mesh.shape["batch"] == 8 else local_any
    return jax.shard_map(local, mesh=mesh, in_specs=placed, out_specs=rows, check_vma=False)
```

```python
import functools

import jax
import jax.numpy as jnp
from jax import lax
from jax.experimental import pallas as pl
from jax.experimental.pallas import tpu as pltpu
from jax.sharding import PartitionSpec as P

VMEM_LIMIT = 10 * 1024 * 1024
SPLIT = (8, 8)
FIX = 16


def drop_tokens(kernel, keep, tokens, *refs):
    kernel(*refs[:keep], *refs[keep + tokens :])


def parent_of(counts, order):
    index = jnp.arange(counts.shape[0], dtype=jnp.int32)
    bounds = jnp.sum(jnp.where(index[None, :] <= index[:, None], counts[None, :], 0), axis=1)
    return jnp.sum((bounds[None, :] <= order[:, None]).astype(jnp.int32), axis=1)


def conv_silu(padded, tail, rows, taps):
    length = rows.shape[0]
    reach = taps.shape[0] - 1
    padded[8 - reach : 8, :] = jnp.broadcast_to(tail, (reach, rows.shape[1])).astype(jnp.float32)
    padded[8 : 8 + length, :] = rows.astype(jnp.float32)
    total = padded[8 - reach : 8 - reach + length, :] * taps[0:1, :]
    for k in range(1, reach + 1):
        total = total + padded[8 - reach + k : 8 - reach + k + length, :] * taps[k : k + 1, :]
    half = 0.5 * total
    return (half + half * jnp.tanh(half)).astype(jnp.bfloat16)


def conv_kernel(
    x_ref, b_ref, c_ref, dt_ref, bias_ref, alog_ref, taps_x_ref, taps_bc_ref,
    xc_ref, bc_ref, cc_ref, row_ref, column_ref, padded,
):
    length = x_ref.shape[1]
    lanes_all = x_ref.shape[2]
    bc_ref[...] = conv_silu(padded, 0.0, b_ref[0], taps_bc_ref[0])
    cc_ref[...] = conv_silu(padded, 0.0, c_ref[0], taps_bc_ref[1])
    for start in range(0, lanes_all, 128):
        lanes = slice(start, start + 128)
        xc_ref[:, lanes] = conv_silu(padded, 0.0, x_ref[0, :, lanes], taps_x_ref[:, lanes])
    raw = dt_ref[0] + bias_ref[...]
    step = jnp.maximum(raw, 0.0) + jnp.log1p(jnp.exp(-jnp.abs(raw)))
    per_token = step * (-jnp.exp(alog_ref[...]))
    row = lax.broadcasted_iota(jnp.int32, (length, length), 0)
    col = lax.broadcasted_iota(jnp.int32, (length, length), 1)
    total = lax.dot_general(
        per_token,
        (row <= col).astype(jnp.float32),
        (((1,), (0,)), ((), ())),
        precision=lax.Precision.HIGHEST,
        preferred_element_type=jnp.float32,
    )
    row_ref[...] = total - jnp.log(step)
    column_ref[0] = total.T


def mix_kernel(
    lines, x_ref, xin_ref, b_ref, bin_ref, c_ref, cin_ref, row_ref, column_ref, skip_ref,
    taps_x_ref, taps_bc_ref, tail_ref, *refs,
):
    mixed_ref, c_out_ref, padded = refs[-3:]
    length, wide = x_ref.shape
    heads = row_ref.shape[0]
    width = wide // heads
    half = length // 2
    reach = taps_x_ref.shape[0] - 1
    tail = tail_ref[0, 0].astype(jnp.float32)

    def fixed(bulk_ref, first_ref, lanes, taps, at):
        rows = jnp.concatenate([tail[k * lines + at : k * lines + at + 1] for k in range(reach)])
        first = conv_silu(padded, rows, first_ref[0, :, lanes], taps)
        return jnp.concatenate([first, bulk_ref[FIX:, lanes]])

    every = slice(0, b_ref.shape[1])
    b_conv = fixed(b_ref, bin_ref, every, taps_bc_ref[0], lines - 2)
    c_conv = fixed(c_ref, cin_ref, every, taps_bc_ref[1], lines - 1)
    c_out_ref[...] = c_conv
    scores = lax.dot_general(
        c_conv, b_conv, (((1,), (1,)), ((), ())), preferred_element_type=jnp.float32
    )
    causal = lax.broadcasted_iota(jnp.int32, (half, half), 0) >= lax.broadcasted_iota(
        jnp.int32, (half, half), 1
    )
    low = lax.broadcasted_iota(jnp.int32, (length, 2 * width), 1) < width
    for pair in range(heads // 2):
        lanes = slice(pair * 2 * width, (pair + 1) * 2 * width)
        x_conv = fixed(x_ref, xin_ref, lanes, taps_x_ref[:, lanes], pair)
        parts = []
        for head in (2 * pair, 2 * pair + 1):
            column = jnp.broadcast_to(column_ref[0, :, head : head + 1], (length, half))
            rows = row_ref[head : head + 1, :]
            near = jnp.exp(jnp.where(causal, column[:half] - rows[:, :half], -1e30))
            far = jnp.exp(column[half:] - rows[:, :half])
            last = jnp.exp(jnp.where(causal, column[half:] - rows[:, half:], -1e30))
            top = (scores[:half, :half] * near).astype(jnp.bfloat16)
            left = (scores[half:, :half] * far).astype(jnp.bfloat16)
            right = (scores[half:, half:] * last).astype(jnp.bfloat16)
            below = jnp.concatenate([left, right], axis=1)
            parts.append(
                jnp.concatenate(
                    [
                        jnp.dot(top, x_conv[:half], preferred_element_type=jnp.float32),
                        jnp.dot(below, x_conv, preferred_element_type=jnp.float32),
                    ]
                )
            )
        mixed_ref[:, lanes] = jnp.where(low, parts[0], parts[1]) + skip_ref[
            :, lanes
        ] * x_conv.astype(jnp.float32)


def state_kernel(offset, *refs):
    y_ref = refs[-1]
    kids, length, wide = y_ref.shape
    low = lax.broadcasted_iota(jnp.int32, (length, 128), 1) < 64
    for kid in range(kids):
        state_ref, c_ref, column_ref, mixed_ref = refs[4 * kid : 4 * kid + 4]
        state = state_ref[0, 0]
        term = lax.dot_general(
            c_ref[...], state, (((1,), (1,)), ((), ())), preferred_element_type=jnp.float32
        )
        for pair in range(wide // 128):
            lanes = slice(pair * 128, pair * 128 + 128)
            head = offset + 2 * pair
            grow = jnp.where(
                low, column_ref[0, :, head : head + 1], column_ref[0, :, head + 1 : head + 2]
            )
            carried = (term[:, lanes] * jnp.exp(grow)).astype(jnp.bfloat16).astype(jnp.float32)
            y_ref[kid, :, lanes] = (mixed_ref[:, lanes] + carried).astype(jnp.bfloat16)


def cast_kernel(parts, tailed, reach, lines, *refs):
    count = len(tailed)
    ins, outs = refs[:-count], refs[-count:]
    states, tails = ins[: parts * count], ins[parts * count :]
    for j, out_ref in enumerate(outs):
        start = 0
        for at in range(parts):
            state = states[parts * j + at][0]
            rows = state.shape[0] * state.shape[1]
            out_ref[start : start + rows] = state.reshape(rows, state.shape[2]).astype(jnp.bfloat16)
            start += rows
            if at == 0 and tailed[j]:
                x_tail = tails[2 * j][0].astype(jnp.float32)
                bc_tail = tails[2 * j + 1][0].astype(jnp.float32)
                pieces = []
                for k in range(reach):
                    pieces += [x_tail[k : k + 1, i * 128 : i * 128 + 128] for i in range(lines - 2)]
                    pieces.append(bc_tail[k])
                spare = tailed[j] - lines * reach
                pieces.append(jnp.zeros((spare, 128), jnp.float32))
                out_ref[start : start + tailed[j]] = jnp.concatenate(pieces).astype(jnp.bfloat16)
                start += tailed[j]


def pick_rows_kernel(start, slots_ref, inside_ref, *refs):
    crossed, out, sems = refs[:-2], refs[-2], refs[-1]
    spots, rows = out.shape[:2]
    for i in range(spots):
        for source in range(4 + len(crossed)):
            if source < 4:
                held = inside_ref.at[source, pl.ds(start, rows)]
            else:
                held = crossed[source - 4]

            @pl.when(slots_ref[i] == source)
            def _(held=held, i=i):
                pltpu.make_async_copy(held, out.at[i], sems.at[i]).start()

    for i in range(spots):
        pltpu.make_async_copy(crossed[0], out.at[i], sems.at[i]).wait()


def within_kernel(
    parent_ref,
    x_ref,
    b_ref,
    c_ref,
    dt_ref,
    bias_ref,
    alog_ref,
    skip_ref,
    taps_x_ref,
    taps_bc_ref,
    tail_x_ref,
    tail_bc_ref,
    mixed_ref,
    c_out_ref,
    grow_ref,
    padded,
):
    length = x_ref.shape[1]
    heads = dt_ref.shape[1]
    width = x_ref.shape[2] // heads
    b_conv = conv_silu(padded, tail_bc_ref[0, 0], b_ref[0], taps_bc_ref[0])
    c_conv = conv_silu(padded, tail_bc_ref[0, 1], c_ref[0], taps_bc_ref[1])
    c_out_ref[0] = c_conv
    scores = lax.dot_general(
        c_conv, b_conv, (((1,), (1,)), ((), ())), preferred_element_type=jnp.float32
    )
    raw = dt_ref[0] + bias_ref[...]
    step = jnp.maximum(raw, 0.0) + jnp.log1p(jnp.exp(-jnp.abs(raw)))
    per_token = step * (-jnp.exp(alog_ref[...]))
    row = lax.broadcasted_iota(jnp.int32, (length, length), 0)
    col = lax.broadcasted_iota(jnp.int32, (length, length), 1)
    upper = (row <= col).astype(jnp.float32)
    total = lax.dot_general(
        per_token,
        upper,
        (((1,), (0,)), ((), ())),
        precision=lax.Precision.HIGHEST,
        preferred_element_type=jnp.float32,
    )
    total_t = total.T
    grow_ref[0, 0] = jnp.exp(total_t)
    causal = row >= col
    low = lax.broadcasted_iota(jnp.int32, (length, 2 * width), 1) < width
    for pair in range(heads // 2):
        lanes = slice(pair * 2 * width, (pair + 1) * 2 * width)
        x_conv = conv_silu(
            padded, tail_x_ref[0, :, lanes], x_ref[0, :, lanes], taps_x_ref[:, lanes]
        )
        parts = []
        for head in (2 * pair, 2 * pair + 1):
            gap = total_t[:, head : head + 1] - total[head : head + 1, :]
            factor = jnp.exp(jnp.where(causal, gap, -1e30))
            mixing = (scores * factor * step[head : head + 1, :]).astype(jnp.bfloat16)
            parts.append(jnp.dot(mixing, x_conv, preferred_element_type=jnp.float32))
        mixed_ref[0, :, lanes] = (
            jnp.where(low, parts[0], parts[1]) + skip_ref[:, lanes] * x_conv.astype(jnp.float32)
        )


def carried_kernel(state_ref, c_ref, grow_ref, mixed_ref, y_ref):
    sources, _, part, width, size = state_ref.shape
    length = c_ref.shape[1]
    low = lax.broadcasted_iota(jnp.int32, (length, 2 * width), 1) < width
    c_conv = c_ref[0]
    for source in range(sources):
        state = state_ref[source, 0].reshape(part * width, size)
        term = lax.dot_general(
            c_conv, state, (((1,), (1,)), ((), ())), preferred_element_type=jnp.float32
        )
        for pair in range(part // 2):
            head = source * part + 2 * pair
            grow = jnp.where(
                low, grow_ref[0, 0, :, head : head + 1], grow_ref[0, 0, :, head + 1 : head + 2]
            )
            here = slice(2 * pair * width, (2 * pair + 2) * width)
            lanes = slice(head * width, (head + 2) * width)
            carried = (term[:, here] * grow).astype(jnp.bfloat16).astype(jnp.float32)
            y_ref[0, :, lanes] = (mixed_ref[0, :, lanes] + carried).astype(jnp.bfloat16)


def pick_kernel(parent_ref, state_ref, out_ref):
    out_ref[...] = state_ref[...]


def local_any(
    x_in,
    b_in,
    c_in,
    dt_in,
    dt_bias,
    a_log,
    d_skip,
    conv_x,
    conv_bc,
    par_state,
    tail_x,
    tail_bc,
    counts,
    order,
):
    kids, length, columns = x_in.shape
    heads = dt_in.shape[1]
    width, size = par_state.shape[2:]
    ways = lax.axis_size("batch")
    groups = b_in.shape[2] // size
    per_group = heads // groups
    part = heads // ways
    wide = per_group * width
    reach = tail_x.shape[1]
    parents_all = counts.shape[0]
    kids_all = order.shape[0]

    parent = parent_of(counts, order)
    own = lax.dynamic_slice_in_dim(parent, lax.axis_index("batch") * kids, kids)

    sent = par_state.astype(jnp.bfloat16).reshape(ways, part, width, size)
    shares = lax.all_to_all(sent, "batch", split_axis=0, concat_axis=0, tiled=True)

    tails = jnp.concatenate([tail_x.reshape(-1), tail_bc.reshape(-1)])
    tails = jnp.broadcast_to(tails[None], (ways, tails.shape[0]))
    tails = lax.all_to_all(tails, "batch", split_axis=0, concat_axis=0, tiled=True)
    tails_x = tails[:, : reach * columns].reshape(parents_all, reach, columns)
    tails_bc = tails[:, reach * columns :].reshape(parents_all, 2, reach, groups * size)

    picked = pl.pallas_call(
        pick_kernel,
        grid_spec=pltpu.PrefetchScalarGridSpec(
            num_scalar_prefetch=1,
            grid=(kids_all,),
            in_specs=[pl.BlockSpec((1, part, width, size), lambda i, p: (p[i], 0, 0, 0))],
            out_specs=pl.BlockSpec((1, part, width, size), lambda i, p: (i, 0, 0, 0)),
        ),
        out_shape=jax.ShapeDtypeStruct((kids_all, part, width, size), jnp.bfloat16),
        cost_estimate=pl.CostEstimate(
            flops=0, bytes_accessed=4 * kids_all * part * width * size, transcendentals=0
        ),
        name="pick_states",
    )(parent, shares)
    states = lax.all_to_all(
        picked.reshape(ways, kids, part, width, size), "batch", split_axis=0, concat_axis=0, tiled=True
    )

    skip_row = jnp.repeat(d_skip, width)[None, :]
    mixed, c_conv, grow = pl.pallas_call(
        within_kernel,
        grid_spec=pltpu.PrefetchScalarGridSpec(
            num_scalar_prefetch=1,
            grid=(kids, groups),
            in_specs=[
                pl.BlockSpec((1, length, wide), lambda c, q, p: (c, 0, q)),
                pl.BlockSpec((1, length, size), lambda c, q, p: (c, 0, q)),
                pl.BlockSpec((1, length, size), lambda c, q, p: (c, 0, q)),
                pl.BlockSpec((1, per_group, length), lambda c, q, p: (c, q, 0)),
                pl.BlockSpec((per_group, 1), lambda c, q, p: (q, 0)),
                pl.BlockSpec((per_group, 1), lambda c, q, p: (q, 0)),
                pl.BlockSpec((1, wide), lambda c, q, p: (0, q)),
                pl.BlockSpec((reach + 1, wide), lambda c, q, p: (0, q)),
                pl.BlockSpec((2, reach + 1, size), lambda c, q, p: (0, 0, q)),
                pl.BlockSpec((1, reach, wide), lambda c, q, p: (p[c], 0, q)),
                pl.BlockSpec((1, 2, reach, size), lambda c, q, p: (p[c], 0, 0, q)),
            ],
            out_specs=[
                pl.BlockSpec((1, length, wide), lambda c, q, p: (c, 0, q)),
                pl.BlockSpec((1, length, size), lambda c, q, p: (c, 0, q)),
                pl.BlockSpec((1, 1, length, per_group), lambda c, q, p: (c, q, 0, 0)),
            ],
            scratch_shapes=[pltpu.VMEM((8 + length, size), jnp.float32)],
        ),
        out_shape=[
            jax.ShapeDtypeStruct((kids, length, columns), jnp.float32),
            jax.ShapeDtypeStruct((kids, length, groups * size), jnp.bfloat16),
            jax.ShapeDtypeStruct((kids, groups, length, per_group), jnp.float32),
        ],
        compiler_params=pltpu.CompilerParams(vmem_limit_bytes=4 * VMEM_LIMIT),
        cost_estimate=pl.CostEstimate(
            flops=4 * kids * heads * length * length * width,
            bytes_accessed=6 * kids * length * columns,
            transcendentals=kids * heads * length * length,
        ),
        name="within",
    )(
        own,
        x_in,
        b_in,
        c_in,
        dt_in,
        dt_bias[:, None],
        a_log[:, None],
        skip_row,
        conv_x,
        conv_bc,
        tails_x,
        tails_bc,
    )

    sources = per_group // part
    return pl.pallas_call(
        carried_kernel,
        grid=(kids, groups),
        in_specs=[
            pl.BlockSpec((sources, 1, part, width, size), lambda c, q: (q, c, 0, 0, 0)),
            pl.BlockSpec((1, length, size), lambda c, q: (c, 0, q)),
            pl.BlockSpec((1, 1, length, per_group), lambda c, q: (c, q, 0, 0)),
            pl.BlockSpec((1, length, wide), lambda c, q: (c, 0, q)),
        ],
        out_specs=pl.BlockSpec((1, length, wide), lambda c, q: (c, 0, q)),
        out_shape=jax.ShapeDtypeStruct((kids, length, columns), jnp.bfloat16),
        compiler_params=pltpu.CompilerParams(vmem_limit_bytes=4 * VMEM_LIMIT),
        cost_estimate=pl.CostEstimate(
            flops=2 * kids * length * columns * size,
            bytes_accessed=8 * kids * length * columns,
            transcendentals=0,
        ),
        name="carried",
    )(states, c_conv, grow, mixed)


def local_halves(
    x_in, b_in, c_in, dt_in, dt_bias, a_log, d_skip, conv_x, conv_bc,
    par_state, tail_x, tail_bc, counts, order,
):
    kids, length, columns = x_in.shape
    heads = dt_in.shape[1]
    width, size = par_state.shape[2:]
    groups = b_in.shape[2] // size
    per_group = heads // groups
    wide = per_group * width
    taps = conv_x.shape[0]
    reach = taps - 1
    lines = (wide + 2 * size) // 128
    tail_lines = -(-lines * reach // 16) * 16
    params = pltpu.CompilerParams(vmem_limit_bytes=VMEM_LIMIT)
    anywhere = pl.BlockSpec(memory_space=pl.ANY)

    stay = lambda x: pltpu.with_memory_space_constraint(x, pltpu.HBM)
    x_in, b_in, c_in, dt_in, conv_x, conv_bc = map(stay, (x_in, b_in, c_in, dt_in, conv_x, conv_bc))

    me = lax.axis_index("batch")
    parent = parent_of(counts, order)
    side = me // 4 * 4
    owner = lax.dynamic_slice_in_dim(parent, side * kids, 4 * kids)
    slots = jnp.where(owner // 4 * 4 == side, owner % 4, 4 + ((owner ^ me) % 4))
    place = (me % 4).astype(jnp.int32)[None]

    state = stay(par_state.reshape(groups, per_group, width, size))
    x_tails, bc_tails = stay(tail_x), stay(tail_bc.transpose(0, 2, 1, 3))
    offsets = [sum(SPLIT[:k]) for k in range(len(SPLIT))]

    def swap(value, r):
        return lax.ppermute(value, "batch", perm=[(i, i ^ r) for i in range(8)])

    def cast(quarters, chunks, tokens):
        tailed = [tail_lines if chunks[0] == 0 else 0] * len(quarters)
        rows = sum(SPLIT[k] for k in chunks) * width + tailed[0]
        operands, specs = [], []
        for j in quarters:
            for k in chunks:
                part, at = SPLIT[k], offsets[k] // SPLIT[k]
                operands.append(state)
                specs.append(
                    pl.BlockSpec(
                        (1, part, width, size), lambda i, p, j=j, at=at: (p[0] ^ j, at, 0, 0)
                    )
                )
        if tailed[0]:
            for j in quarters:
                operands += [x_tails, bc_tails]
                specs += [
                    pl.BlockSpec((1, reach, wide), lambda i, p, j=j: (0, 0, p[0] ^ j)),
                    pl.BlockSpec((1, reach, 2, size), lambda i, p, j=j: (0, 0, 0, p[0] ^ j)),
                ]
        kernel = functools.partial(cast_kernel, len(chunks), tailed, reach, lines)
        return pl.pallas_call(
            functools.partial(
                drop_tokens, lambda place_ref, *refs: kernel(*refs), 1 + len(operands), len(tokens)
            ),
            grid_spec=pltpu.PrefetchScalarGridSpec(
                num_scalar_prefetch=1,
                grid=(1,),
                in_specs=specs + [anywhere] * len(tokens),
                out_specs=[pl.BlockSpec((rows, size), lambda i, p: (0, 0))] * len(quarters),
            ),
            out_shape=[jax.ShapeDtypeStruct((rows, size), jnp.bfloat16)] * len(quarters),
            compiler_params=params,
            cost_estimate=pl.CostEstimate(
                flops=0, bytes_accessed=6 * len(quarters) * rows * size, transcendentals=0
            ),
            name="cast_states",
        )(place, *operands, *tokens)

    def cast_whole(tokens):
        rows = per_group * width + tail_lines
        operands = [state, state, x_tails, bc_tails]
        kernel = functools.partial(cast_kernel, 2, [tail_lines], reach, lines)
        return pl.pallas_call(
            functools.partial(
                drop_tokens,
                lambda a, b, c, d, out_ref: kernel(a, b, c, d, out_ref.at[0]),
                4,
                len(tokens),
            ),
            grid=(groups,),
            in_specs=[
                pl.BlockSpec((1, SPLIT[0], width, size), lambda q: (q, 0, 0, 0)),
                pl.BlockSpec((1, SPLIT[1], width, size), lambda q: (q, 1, 0, 0)),
                pl.BlockSpec((1, reach, wide), lambda q: (0, 0, q)),
                pl.BlockSpec((1, reach, 2, size), lambda q: (0, 0, 0, q)),
                *[anywhere] * len(tokens),
            ],
            out_specs=pl.BlockSpec((1, rows, size), lambda q: (q, 0, 0)),
            out_shape=jax.ShapeDtypeStruct((groups, rows, size), jnp.bfloat16),
            compiler_params=params,
            cost_estimate=pl.CostEstimate(
                flops=0, bytes_accessed=6 * groups * rows * size, transcendentals=0
            ),
            name="cast_states",
        )(*operands, *tokens)

    def gather_half(value):
        return lax.all_to_all(
            value,
            "batch",
            split_axis=0,
            concat_axis=0,
            tiled=True,
            axis_index_groups=[[0, 1, 2, 3], [4, 5, 6, 7]],
        )

    def pick(rows, start, inside, crossed, tokens):
        spots = 4 * kids
        picked = pl.pallas_call(
            functools.partial(
                drop_tokens, functools.partial(pick_rows_kernel, start), 6, len(tokens)
            ),
            grid_spec=pltpu.PrefetchScalarGridSpec(
                num_scalar_prefetch=1,
                grid=(1,),
                in_specs=[anywhere] * (5 + len(tokens)),
                out_specs=pl.BlockSpec((spots, rows, size), lambda i, s: (0, 0, 0)),
                scratch_shapes=[pltpu.SemaphoreType.DMA((spots,))],
            ),
            out_shape=jax.ShapeDtypeStruct((spots, rows, size), jnp.bfloat16),
            compiler_params=params,
            cost_estimate=pl.CostEstimate(
                flops=0, bytes_accessed=4 * spots * rows * size, transcendentals=0
            ),
            name="pick_states",
        )(slots, inside, *crossed, *tokens)
        return picked, gather_half(picked).reshape(4, kids, rows, size)

    def convolve(c, tokens):
        at = lambda q: (c, 0, q)
        operands = [
            x_in, b_in, c_in, dt_in, dt_bias[:, None], a_log[:, None], conv_x, conv_bc
        ]
        return pl.pallas_call(
            functools.partial(drop_tokens, conv_kernel, len(operands), len(tokens)),
            grid=(groups,),
            in_specs=[
                pl.BlockSpec((1, length, wide), at),
                pl.BlockSpec((1, length, size), at),
                pl.BlockSpec((1, length, size), at),
                pl.BlockSpec((1, per_group, length), lambda q: (c, q, 0)),
                pl.BlockSpec((per_group, 1), lambda q: (q, 0)),
                pl.BlockSpec((per_group, 1), lambda q: (q, 0)),
                pl.BlockSpec((taps, wide), lambda q: (0, q)),
                pl.BlockSpec((2, taps, size), lambda q: (0, 0, q)),
                *[anywhere] * len(tokens),
            ],
            out_specs=[
                pl.BlockSpec((length, wide), lambda q: (0, q)),
                pl.BlockSpec((length, size), lambda q: (0, q)),
                pl.BlockSpec((length, size), lambda q: (0, q)),
                pl.BlockSpec((per_group, length), lambda q: (q, 0)),
                pl.BlockSpec((1, length, per_group), lambda q: (q, 0, 0)),
            ],
            out_shape=[
                pltpu.HBM(x_in.shape[1:], jnp.bfloat16),
                pltpu.HBM(b_in.shape[1:], jnp.bfloat16),
                pltpu.HBM(c_in.shape[1:], jnp.bfloat16),
                pltpu.HBM(dt_in.shape[1:], jnp.float32),
                pltpu.HBM((groups, length, per_group), jnp.float32),
            ],
            scratch_shapes=[pltpu.VMEM((8 + length, size), jnp.float32)],
            compiler_params=params,
            cost_estimate=pl.CostEstimate(
                flops=40 * length * columns,
                bytes_accessed=4 * length * columns,
                transcendentals=2 * length * columns,
            ),
            name="conv",
        )(*operands, *tokens)

    def mix(c, early, states, tokens):
        x_conv, b_conv, c_conv, row, column = map(stay, early)
        at = lambda q: (0, q)
        tail_at = SPLIT[0] * width // tail_lines
        operands = [
            x_conv, x_in, b_conv, b_in, c_conv, c_in, row, column, skip_row, conv_x, conv_bc,
            states,
        ]
        return pl.pallas_call(
            functools.partial(drop_tokens, functools.partial(mix_kernel, lines), 12, len(tokens)),
            grid=(groups,),
            in_specs=[
                pl.BlockSpec((length, wide), at),
                pl.BlockSpec((1, FIX, wide), lambda q: (c, 0, q)),
                pl.BlockSpec((length, size), at),
                pl.BlockSpec((1, FIX, size), lambda q: (c, 0, q)),
                pl.BlockSpec((length, size), at),
                pl.BlockSpec((1, FIX, size), lambda q: (c, 0, q)),
                pl.BlockSpec((per_group, length), lambda q: (q, 0)),
                pl.BlockSpec((1, length, per_group), lambda q: (q, 0, 0)),
                pl.BlockSpec((1, wide), at),
                pl.BlockSpec((taps, wide), at),
                pl.BlockSpec((2, taps, size), lambda q: (0, 0, q)),
                pl.BlockSpec((1, 1, tail_lines, size), lambda q: (q, c, tail_at, 0)),
                *[anywhere] * len(tokens),
            ],
            out_specs=[pl.BlockSpec((length, wide), at), pl.BlockSpec((length, size), at)],
            out_shape=[
                pltpu.HBM((length, columns), jnp.float32),
                pltpu.HBM((length, groups * size), jnp.bfloat16),
            ],
            scratch_shapes=[
                pltpu.VMEM((8 + FIX, size), jnp.float32),
            ],
            compiler_params=params,
            cost_estimate=pl.CostEstimate(
                flops=4 * heads * length * length * width,
                bytes_accessed=6 * length * columns,
                transcendentals=heads * length * length,
            ),
            name="mix",
        )(*operands, *tokens)

    def finish(k, states, early, mixed, result):
        part, offset = SPLIT[k], offsets[k]
        chunk = part * width
        at = lambda q: (0, q * (per_group // part) + offset // part)
        operands, specs = [], []
        for c in range(kids):
            operands += [states, *map(stay, (mixed[c][1], early[c][4], mixed[c][0]))]
            specs += [
                pl.BlockSpec((1, 1, chunk, size), lambda q, c=c: (q, c, 0, 0)),
                pl.BlockSpec((length, size), lambda q: (0, q)),
                pl.BlockSpec((1, length, per_group), lambda q: (q, 0, 0)),
                pl.BlockSpec((length, chunk), at),
            ]
        alias = {}
        if result is not None:
            alias = {len(operands): 0}
            operands.append(result)
            specs.append(anywhere)
        return pl.pallas_call(
            functools.partial(state_kernel, offset),
            grid=(groups,),
            in_specs=specs,
            out_specs=pl.BlockSpec((kids, length, chunk), lambda q: (0, *at(q))),
            out_shape=jax.ShapeDtypeStruct(x_in.shape, jnp.bfloat16),
            input_output_aliases=alias,
            compiler_params=params,
            cost_estimate=pl.CostEstimate(
                flops=2 * kids * groups * length * chunk * size,
                bytes_accessed=6 * kids * groups * length * chunk,
                transcendentals=kids * groups * length * chunk,
            ),
            name="add_states",
        )(*operands)

    skip_row = jnp.repeat(d_skip, width)[None, :]
    rows = [SPLIT[0] * width + tail_lines, SPLIT[1] * width]
    quarters = [0, 1, 2, 3]
    sent_a = cast(quarters, [0], [])
    crossed_a = [swap(sent_a[j], j + 4) for j in quarters]
    whole = cast_whole([sent_a[0]])
    inside = gather_half(whole)
    early = [convolve(0, [whole])]
    early.append(convolve(1, [stay(early[0][3])]))
    sent_b = cast(quarters, [1], [*crossed_a, stay(early[1][3])])
    crossed_b = [swap(sent_b[j], j + 4) for j in quarters]
    picked_a, states_a = pick(rows[0], 0, inside, crossed_a, [sent_b[0]])
    picked_b, states_b = pick(rows[1], rows[0], inside, crossed_b, [picked_a])
    mixed = [mix(0, early[0], states_a, [picked_b])]
    mixed.append(mix(1, early[1], states_a, [stay(mixed[0][1])]))
    result = finish(0, states_a, early, mixed, None)
    return finish(1, states_b, early, mixed, result)


def solution(mesh):
    rows, cols = P(("groups", "batch"), None, "head"), P(("groups", "batch"), "head")
    placed = (
        rows, rows, rows, cols, P("head"), P("head"), P("head"), P(None, "head"),
        P(None, None, "head"), cols, rows, P(("groups", "batch"), None, None, "head"),
        P("groups"), P("groups"),
    )
    local = local_halves if mesh.shape["batch"] == 8 else local_any
    return jax.shard_map(local, mesh=mesh, in_specs=placed, out_specs=rows, check_vma=False)
```

```python
import functools

import jax
import jax.numpy as jnp
from jax import lax
from jax.experimental import pallas as pl
from jax.experimental.pallas import tpu as pltpu
from jax.sharding import PartitionSpec as P

VMEM_LIMIT = 10 * 1024 * 1024
SPLIT = (8, 8)
FIX = 16


def drop_tokens(kernel, keep, tokens, *refs):
    kernel(*refs[:keep], *refs[keep + tokens :])


def parent_of(counts, order):
    index = jnp.arange(counts.shape[0], dtype=jnp.int32)
    bounds = jnp.sum(jnp.where(index[None, :] <= index[:, None], counts[None, :], 0), axis=1)
    return jnp.sum((bounds[None, :] <= order[:, None]).astype(jnp.int32), axis=1)


def conv_silu(padded, tail, rows, taps):
    length = rows.shape[0]
    reach = taps.shape[0] - 1
    padded[8 - reach : 8, :] = jnp.broadcast_to(tail, (reach, rows.shape[1])).astype(jnp.float32)
    padded[8 : 8 + length, :] = rows.astype(jnp.float32)
    total = padded[8 - reach : 8 - reach + length, :] * taps[0:1, :]
    for k in range(1, reach + 1):
        total = total + padded[8 - reach + k : 8 - reach + k + length, :] * taps[k : k + 1, :]
    half = 0.5 * total
    return (half + half * jnp.tanh(half)).astype(jnp.bfloat16)


def early_kernel(
    x_ref, b_ref, c_ref, dt_ref, bias_ref, alog_ref, skip_ref, taps_x_ref, taps_bc_ref,
    mixed_ref, c_out_ref, column_ref, first_ref, padded,
):
    length, wide = mixed_ref.shape
    heads = dt_ref.shape[1]
    width = wide // heads
    half = length // 2

    def convolve(rows, taps):
        bulk = conv_silu(padded, 0.0, rows, taps)[FIX:]
        return jnp.concatenate([jnp.zeros((FIX, rows.shape[1]), jnp.bfloat16), bulk])

    b_conv = convolve(b_ref[0], taps_bc_ref[0])
    c_conv = convolve(c_ref[0], taps_bc_ref[1])
    c_out_ref[...] = c_conv
    scores = lax.dot_general(
        c_conv, b_conv, (((1,), (1,)), ((), ())), preferred_element_type=jnp.float32
    )
    raw = dt_ref[0] + bias_ref[...]
    step = jnp.maximum(raw, 0.0) + jnp.log1p(jnp.exp(-jnp.abs(raw)))
    per_token = step * (-jnp.exp(alog_ref[...]))
    upper = lax.broadcasted_iota(jnp.int32, (length, length), 0) <= lax.broadcasted_iota(
        jnp.int32, (length, length), 1
    )
    total = lax.dot_general(
        per_token,
        upper.astype(jnp.float32),
        (((1,), (0,)), ((), ())),
        precision=lax.Precision.HIGHEST,
        preferred_element_type=jnp.float32,
    )
    row = total - jnp.log(step)
    columns = total.T
    column_ref[0] = columns
    causal = lax.broadcasted_iota(jnp.int32, (half, half), 0) >= lax.broadcasted_iota(
        jnp.int32, (half, half), 1
    )
    low = lax.broadcasted_iota(jnp.int32, (length, 2 * width), 1) < width
    for pair in range(heads // 2):
        lanes = slice(pair * 2 * width, (pair + 1) * 2 * width)
        x_conv = convolve(x_ref[0, :, lanes], taps_x_ref[:, lanes])
        parts = []
        for head in (2 * pair, 2 * pair + 1):
            column = jnp.broadcast_to(columns[:, head : head + 1], (length, half))
            rows = row[head : head + 1, :]
            near = jnp.exp(jnp.where(causal, column[:half] - rows[:, :half], -1e30))
            far = jnp.exp(column[half:] - rows[:, :half])
            last = jnp.exp(jnp.where(causal, column[half:] - rows[:, half:], -1e30))
            spot = slice(head * FIX, (head + 1) * FIX)
            first_ref[0, :half, spot] = near[:, :FIX]
            first_ref[0, half:, spot] = far[:, :FIX]
            top = (scores[:half, :half] * near).astype(jnp.bfloat16)
            left = (scores[half:, :half] * far).astype(jnp.bfloat16)
            right = (scores[half:, half:] * last).astype(jnp.bfloat16)
            below = jnp.concatenate([left, right], axis=1)
            parts.append(
                jnp.concatenate(
                    [
                        jnp.dot(top, x_conv[:half], preferred_element_type=jnp.float32),
                        jnp.dot(below, x_conv, preferred_element_type=jnp.float32),
                    ]
                )
            )
        mixed_ref[:, lanes] = jnp.where(low, parts[0], parts[1]) + skip_ref[
            :, lanes
        ] * x_conv.astype(jnp.float32)


def late_kernel(offset, lines, x_ref, b_ref, c_ref, skip_ref, taps_x_ref, taps_bc_ref, *refs):
    y_ref, padded = refs[-2:]
    kids, length, wide = y_ref.shape
    width = 64
    heads = wide // width
    reach = taps_x_ref.shape[0] - 1
    low = lax.broadcasted_iota(jnp.int32, (length, 2 * width), 1) < width
    low_first = lax.broadcasted_iota(jnp.int32, (FIX, 2 * width), 1) < width
    contract = (((1,), (1,)), ((), ()))
    for kid in range(kids):
        state_ref, tail_ref, held_ref, column_ref, first_ref, mixed_ref = refs[6 * kid : 6 * kid + 6]
        tail = tail_ref[0, 0].astype(jnp.float32)

        def opening(rows, taps, at):
            tap_rows = [tail[k * lines + at : k * lines + at + 1] for k in range(reach)]
            return conv_silu(padded, jnp.concatenate(tap_rows), rows, taps)

        b_first = opening(b_ref[kid], taps_bc_ref[0], lines - 2)
        c_first = opening(c_ref[kid], taps_bc_ref[1], lines - 1)
        c_conv = jnp.concatenate([c_first, held_ref[FIX:]])
        term = lax.dot_general(
            c_conv, state_ref[0, 0], contract, preferred_element_type=jnp.float32
        )
        scores = lax.dot_general(
            c_conv,
            jnp.concatenate([b_first] * heads),
            contract,
            preferred_element_type=jnp.float32,
        )
        mixing = (scores * first_ref[0]).astype(jnp.bfloat16)
        for pair in range(heads // 2):
            lanes = slice(pair * 2 * width, (pair + 1) * 2 * width)
            x_first = opening(
                x_ref[kid, :, lanes], taps_x_ref[:, lanes], offset * width // 128 + pair
            ).astype(jnp.float32)
            stacked = [jnp.where(low_first, x_first, 0.0), jnp.where(low_first, 0.0, x_first)]
            if pair > 0:
                stacked = [jnp.zeros((2 * pair * FIX, 2 * width), jnp.float32)] + stacked
            if 2 * pair + 2 < heads:
                spare = (heads - 2 * pair - 2) * FIX
                stacked = stacked + [jnp.zeros((spare, 2 * width), jnp.float32)]
            part = jnp.dot(
                mixing,
                jnp.concatenate(stacked).astype(jnp.bfloat16),
                preferred_element_type=jnp.float32,
            )
            part = jnp.concatenate([part[:FIX] + skip_ref[:, lanes] * x_first, part[FIX:]])
            head = offset + 2 * pair
            grow = jnp.where(
                low, column_ref[0, :, head : head + 1], column_ref[0, :, head + 1 : head + 2]
            )
            carried = (term[:, lanes] * jnp.exp(grow)).astype(jnp.bfloat16).astype(jnp.float32)
            y_ref[kid, :, lanes] = (mixed_ref[:, lanes] + part + carried).astype(jnp.bfloat16)


def cast_kernel(parts, tailed, reach, lines, *refs):
    count = len(tailed)
    ins, outs = refs[:-count], refs[-count:]
    states, tails = ins[: parts * count], ins[parts * count :]
    for j, out_ref in enumerate(outs):
        start = 0
        for at in range(parts):
            state = states[parts * j + at][0]
            rows = state.shape[0] * state.shape[1]
            out_ref[start : start + rows] = state.reshape(rows, state.shape[2]).astype(jnp.bfloat16)
            start += rows
            if at == 0 and tailed[j]:
                x_tail = tails[2 * j][0].astype(jnp.float32)
                bc_tail = tails[2 * j + 1][0].astype(jnp.float32)
                pieces = []
                for k in range(reach):
                    pieces += [x_tail[k : k + 1, i * 128 : i * 128 + 128] for i in range(lines - 2)]
                    pieces.append(bc_tail[k])
                spare = tailed[j] - lines * reach
                pieces.append(jnp.zeros((spare, 128), jnp.float32))
                out_ref[start : start + tailed[j]] = jnp.concatenate(pieces).astype(jnp.bfloat16)
                start += tailed[j]


def pick_rows_kernel(start, slots_ref, inside_ref, *refs):
    crossed, out, sems = refs[:-2], refs[-2], refs[-1]
    spots, rows = out.shape[:2]
    held = [inside_ref.at[source, pl.ds(start, rows)] for source in range(4)]
    held += list(crossed) if len(crossed) == 4 else [crossed[0].at[source] for source in range(4)]
    for i in range(spots):
        for source in range(8):

            @pl.when(slots_ref[i] == source)
            def _(source=source, i=i):
                pltpu.make_async_copy(held[source], out.at[i], sems.at[i]).start()

    for i in range(spots):
        pltpu.make_async_copy(held[0], out.at[i], sems.at[i]).wait()


def slice_kernel(start, in_ref, out_ref, sem):
    copy = pltpu.make_async_copy(in_ref.at[:, pl.ds(start, out_ref.shape[1])], out_ref, sem)
    copy.start()
    copy.wait()


def within_kernel(
    parent_ref,
    x_ref,
    b_ref,
    c_ref,
    dt_ref,
    bias_ref,
    alog_ref,
    skip_ref,
    taps_x_ref,
    taps_bc_ref,
    tail_x_ref,
    tail_bc_ref,
    mixed_ref,
    c_out_ref,
    grow_ref,
    padded,
):
    length = x_ref.shape[1]
    heads = dt_ref.shape[1]
    width = x_ref.shape[2] // heads
    b_conv = conv_silu(padded, tail_bc_ref[0, 0], b_ref[0], taps_bc_ref[0])
    c_conv = conv_silu(padded, tail_bc_ref[0, 1], c_ref[0], taps_bc_ref[1])
    c_out_ref[0] = c_conv
    scores = lax.dot_general(
        c_conv, b_conv, (((1,), (1,)), ((), ())), preferred_element_type=jnp.float32
    )
    raw = dt_ref[0] + bias_ref[...]
    step = jnp.maximum(raw, 0.0) + jnp.log1p(jnp.exp(-jnp.abs(raw)))
    per_token = step * (-jnp.exp(alog_ref[...]))
    row = lax.broadcasted_iota(jnp.int32, (length, length), 0)
    col = lax.broadcasted_iota(jnp.int32, (length, length), 1)
    upper = (row <= col).astype(jnp.float32)
    total = lax.dot_general(
        per_token,
        upper,
        (((1,), (0,)), ((), ())),
        precision=lax.Precision.HIGHEST,
        preferred_element_type=jnp.float32,
    )
    total_t = total.T
    grow_ref[0, 0] = jnp.exp(total_t)
    causal = row >= col
    low = lax.broadcasted_iota(jnp.int32, (length, 2 * width), 1) < width
    for pair in range(heads // 2):
        lanes = slice(pair * 2 * width, (pair + 1) * 2 * width)
        x_conv = conv_silu(
            padded, tail_x_ref[0, :, lanes], x_ref[0, :, lanes], taps_x_ref[:, lanes]
        )
        parts = []
        for head in (2 * pair, 2 * pair + 1):
            gap = total_t[:, head : head + 1] - total[head : head + 1, :]
            factor = jnp.exp(jnp.where(causal, gap, -1e30))
            mixing = (scores * factor * step[head : head + 1, :]).astype(jnp.bfloat16)
            parts.append(jnp.dot(mixing, x_conv, preferred_element_type=jnp.float32))
        mixed_ref[0, :, lanes] = (
            jnp.where(low, parts[0], parts[1]) + skip_ref[:, lanes] * x_conv.astype(jnp.float32)
        )


def carried_kernel(state_ref, c_ref, grow_ref, mixed_ref, y_ref):
    sources, _, part, width, size = state_ref.shape
    length = c_ref.shape[1]
    low = lax.broadcasted_iota(jnp.int32, (length, 2 * width), 1) < width
    c_conv = c_ref[0]
    for source in range(sources):
        state = state_ref[source, 0].reshape(part * width, size)
        term = lax.dot_general(
            c_conv, state, (((1,), (1,)), ((), ())), preferred_element_type=jnp.float32
        )
        for pair in range(part // 2):
            head = source * part + 2 * pair
            grow = jnp.where(
                low, grow_ref[0, 0, :, head : head + 1], grow_ref[0, 0, :, head + 1 : head + 2]
            )
            here = slice(2 * pair * width, (2 * pair + 2) * width)
            lanes = slice(head * width, (head + 2) * width)
            carried = (term[:, here] * grow).astype(jnp.bfloat16).astype(jnp.float32)
            y_ref[0, :, lanes] = (mixed_ref[0, :, lanes] + carried).astype(jnp.bfloat16)


def pick_kernel(parent_ref, state_ref, out_ref):
    out_ref[...] = state_ref[...]


def local_any(
    x_in,
    b_in,
    c_in,
    dt_in,
    dt_bias,
    a_log,
    d_skip,
    conv_x,
    conv_bc,
    par_state,
    tail_x,
    tail_bc,
    counts,
    order,
):
    kids, length, columns = x_in.shape
    heads = dt_in.shape[1]
    width, size = par_state.shape[2:]
    ways = lax.axis_size("batch")
    groups = b_in.shape[2] // size
    per_group = heads // groups
    part = heads // ways
    wide = per_group * width
    reach = tail_x.shape[1]
    parents_all = counts.shape[0]
    kids_all = order.shape[0]

    parent = parent_of(counts, order)
    own = lax.dynamic_slice_in_dim(parent, lax.axis_index("batch") * kids, kids)

    sent = par_state.astype(jnp.bfloat16).reshape(ways, part, width, size)
    shares = lax.all_to_all(sent, "batch", split_axis=0, concat_axis=0, tiled=True)

    tails = jnp.concatenate([tail_x.reshape(-1), tail_bc.reshape(-1)])
    tails = jnp.broadcast_to(tails[None], (ways, tails.shape[0]))
    tails = lax.all_to_all(tails, "batch", split_axis=0, concat_axis=0, tiled=True)
    tails_x = tails[:, : reach * columns].reshape(parents_all, reach, columns)
    tails_bc = tails[:, reach * columns :].reshape(parents_all, 2, reach, groups * size)

    picked = pl.pallas_call(
        pick_kernel,
        grid_spec=pltpu.PrefetchScalarGridSpec(
            num_scalar_prefetch=1,
            grid=(kids_all,),
            in_specs=[pl.BlockSpec((1, part, width, size), lambda i, p: (p[i], 0, 0, 0))],
            out_specs=pl.BlockSpec((1, part, width, size), lambda i, p: (i, 0, 0, 0)),
        ),
        out_shape=jax.ShapeDtypeStruct((kids_all, part, width, size), jnp.bfloat16),
        cost_estimate=pl.CostEstimate(
            flops=0, bytes_accessed=4 * kids_all * part * width * size, transcendentals=0
        ),
        name="pick_states",
    )(parent, shares)
    states = lax.all_to_all(
        picked.reshape(ways, kids, part, width, size), "batch", split_axis=0, concat_axis=0, tiled=True
    )

    skip_row = jnp.repeat(d_skip, width)[None, :]
    mixed, c_conv, grow = pl.pallas_call(
        within_kernel,
        grid_spec=pltpu.PrefetchScalarGridSpec(
            num_scalar_prefetch=1,
            grid=(kids, groups),
            in_specs=[
                pl.BlockSpec((1, length, wide), lambda c, q, p: (c, 0, q)),
                pl.BlockSpec((1, length, size), lambda c, q, p: (c, 0, q)),
                pl.BlockSpec((1, length, size), lambda c, q, p: (c, 0, q)),
                pl.BlockSpec((1, per_group, length), lambda c, q, p: (c, q, 0)),
                pl.BlockSpec((per_group, 1), lambda c, q, p: (q, 0)),
                pl.BlockSpec((per_group, 1), lambda c, q, p: (q, 0)),
                pl.BlockSpec((1, wide), lambda c, q, p: (0, q)),
                pl.BlockSpec((reach + 1, wide), lambda c, q, p: (0, q)),
                pl.BlockSpec((2, reach + 1, size), lambda c, q, p: (0, 0, q)),
                pl.BlockSpec((1, reach, wide), lambda c, q, p: (p[c], 0, q)),
                pl.BlockSpec((1, 2, reach, size), lambda c, q, p: (p[c], 0, 0, q)),
            ],
            out_specs=[
                pl.BlockSpec((1, length, wide), lambda c, q, p: (c, 0, q)),
                pl.BlockSpec((1, length, size), lambda c, q, p: (c, 0, q)),
                pl.BlockSpec((1, 1, length, per_group), lambda c, q, p: (c, q, 0, 0)),
            ],
            scratch_shapes=[pltpu.VMEM((8 + length, size), jnp.float32)],
        ),
        out_shape=[
            jax.ShapeDtypeStruct((kids, length, columns), jnp.float32),
            jax.ShapeDtypeStruct((kids, length, groups * size), jnp.bfloat16),
            jax.ShapeDtypeStruct((kids, groups, length, per_group), jnp.float32),
        ],
        compiler_params=pltpu.CompilerParams(vmem_limit_bytes=4 * VMEM_LIMIT),
        cost_estimate=pl.CostEstimate(
            flops=4 * kids * heads * length * length * width,
            bytes_accessed=6 * kids * length * columns,
            transcendentals=kids * heads * length * length,
        ),
        name="within",
    )(
        own,
        x_in,
        b_in,
        c_in,
        dt_in,
        dt_bias[:, None],
        a_log[:, None],
        skip_row,
        conv_x,
        conv_bc,
        tails_x,
        tails_bc,
    )

    sources = per_group // part
    return pl.pallas_call(
        carried_kernel,
        grid=(kids, groups),
        in_specs=[
            pl.BlockSpec((sources, 1, part, width, size), lambda c, q: (q, c, 0, 0, 0)),
            pl.BlockSpec((1, length, size), lambda c, q: (c, 0, q)),
            pl.BlockSpec((1, 1, length, per_group), lambda c, q: (c, q, 0, 0)),
            pl.BlockSpec((1, length, wide), lambda c, q: (c, 0, q)),
        ],
        out_specs=pl.BlockSpec((1, length, wide), lambda c, q: (c, 0, q)),
        out_shape=jax.ShapeDtypeStruct((kids, length, columns), jnp.bfloat16),
        compiler_params=pltpu.CompilerParams(vmem_limit_bytes=4 * VMEM_LIMIT),
        cost_estimate=pl.CostEstimate(
            flops=2 * kids * length * columns * size,
            bytes_accessed=8 * kids * length * columns,
            transcendentals=0,
        ),
        name="carried",
    )(states, c_conv, grow, mixed)


def local_halves(
    x_in, b_in, c_in, dt_in, dt_bias, a_log, d_skip, conv_x, conv_bc,
    par_state, tail_x, tail_bc, counts, order,
):
    kids, length, columns = x_in.shape
    heads = dt_in.shape[1]
    width, size = par_state.shape[2:]
    groups = b_in.shape[2] // size
    per_group = heads // groups
    wide = per_group * width
    taps = conv_x.shape[0]
    reach = taps - 1
    lines = (wide + 2 * size) // 128
    tail_lines = -(-lines * reach // 16) * 16
    params = pltpu.CompilerParams(vmem_limit_bytes=VMEM_LIMIT)
    anywhere = pl.BlockSpec(memory_space=pl.ANY)

    stay = lambda x: pltpu.with_memory_space_constraint(x, pltpu.HBM)
    x_in, b_in, c_in, dt_in, conv_x, conv_bc = map(stay, (x_in, b_in, c_in, dt_in, conv_x, conv_bc))

    me = lax.axis_index("batch")
    parent = parent_of(counts, order)
    side = me // 4 * 4
    owner = lax.dynamic_slice_in_dim(parent, side * kids, 4 * kids)
    here = owner // 4 * 4 == side
    slots_a = jnp.where(here, owner % 4, 4 + (owner ^ me) % 4)
    slots_b = jnp.where(here, owner % 4, 4 + owner % 4)
    place = (me % 4).astype(jnp.int32)[None]

    state = stay(par_state.reshape(groups, per_group, width, size))
    x_tails, bc_tails = stay(tail_x), stay(tail_bc.transpose(0, 2, 1, 3))
    offsets = [sum(SPLIT[:k]) for k in range(len(SPLIT))]

    def swap(value, r):
        return lax.ppermute(value, "batch", perm=[(i, i ^ r) for i in range(8)])

    def cast(quarters, chunks, tokens):
        tailed = [tail_lines if chunks[0] == 0 else 0] * len(quarters)
        rows = sum(SPLIT[k] for k in chunks) * width + tailed[0]
        operands, specs = [], []
        for j in quarters:
            for k in chunks:
                part, at = SPLIT[k], offsets[k] // SPLIT[k]
                operands.append(state)
                specs.append(
                    pl.BlockSpec(
                        (1, part, width, size), lambda i, p, j=j, at=at: (p[0] ^ j, at, 0, 0)
                    )
                )
        if tailed[0]:
            for j in quarters:
                operands += [x_tails, bc_tails]
                specs += [
                    pl.BlockSpec((1, reach, wide), lambda i, p, j=j: (0, 0, p[0] ^ j)),
                    pl.BlockSpec((1, reach, 2, size), lambda i, p, j=j: (0, 0, 0, p[0] ^ j)),
                ]
        kernel = functools.partial(cast_kernel, len(chunks), tailed, reach, lines)
        return pl.pallas_call(
            functools.partial(
                drop_tokens, lambda place_ref, *refs: kernel(*refs), 1 + len(operands), len(tokens)
            ),
            grid_spec=pltpu.PrefetchScalarGridSpec(
                num_scalar_prefetch=1,
                grid=(1,),
                in_specs=specs + [anywhere] * len(tokens),
                out_specs=[pl.BlockSpec((rows, size), lambda i, p: (0, 0))] * len(quarters),
            ),
            out_shape=[jax.ShapeDtypeStruct((rows, size), jnp.bfloat16)] * len(quarters),
            compiler_params=params,
            cost_estimate=pl.CostEstimate(
                flops=0, bytes_accessed=6 * len(quarters) * rows * size, transcendentals=0
            ),
            name="cast_states",
        )(place, *operands, *tokens)

    def cast_whole(tokens):
        rows = per_group * width + tail_lines

        def kernel(*refs):
            out_ref = refs[-1]
            for q in range(groups):
                cast_kernel(2, [tail_lines], reach, lines, *refs[4 * q : 4 * q + 4], out_ref.at[q])

        operands, specs = [], []
        for q in range(groups):
            operands += [state, state, x_tails, bc_tails]
            specs += [
                pl.BlockSpec((1, SPLIT[0], width, size), lambda i, q=q: (q, 0, 0, 0)),
                pl.BlockSpec((1, SPLIT[1], width, size), lambda i, q=q: (q, 1, 0, 0)),
                pl.BlockSpec((1, reach, wide), lambda i, q=q: (0, 0, q)),
                pl.BlockSpec((1, reach, 2, size), lambda i, q=q: (0, 0, 0, q)),
            ]
        return pl.pallas_call(
            functools.partial(drop_tokens, kernel, len(operands), len(tokens)),
            grid=(1,),
            in_specs=specs + [anywhere] * len(tokens),
            out_specs=pl.BlockSpec((groups, rows, size), lambda i: (0, 0, 0)),
            out_shape=jax.ShapeDtypeStruct((groups, rows, size), jnp.bfloat16),
            compiler_params=params,
            cost_estimate=pl.CostEstimate(
                flops=0, bytes_accessed=6 * groups * rows * size, transcendentals=0
            ),
            name="cast_states",
        )(*operands, *tokens)

    def chunk_b(inside, tokens):
        rows = SPLIT[1] * width
        return pl.pallas_call(
            functools.partial(
                drop_tokens, functools.partial(slice_kernel, inside.shape[1] - rows), 1, len(tokens)
            ),
            grid=(1,),
            in_specs=[anywhere]
            + [anywhere] * len(tokens),
            out_specs=pl.BlockSpec((4, rows, size), lambda i: (0, 0, 0)),
            out_shape=jax.ShapeDtypeStruct((4, rows, size), jnp.bfloat16),
            scratch_shapes=[pltpu.SemaphoreType.DMA],
            compiler_params=params,
            cost_estimate=pl.CostEstimate(
                flops=0, bytes_accessed=16 * rows * size, transcendentals=0
            ),
            name="chunk_b",
        )(inside, *tokens)

    def gather_half(value):
        return lax.all_to_all(
            value,
            "batch",
            split_axis=0,
            concat_axis=0,
            tiled=True,
            axis_index_groups=[[0, 1, 2, 3], [4, 5, 6, 7]],
        )

    def pick(rows, start, slots, inside, crossed, tokens):
        spots = 4 * kids
        picked = pl.pallas_call(
            functools.partial(
                drop_tokens, functools.partial(pick_rows_kernel, start), 2 + len(crossed), len(tokens)
            ),
            grid_spec=pltpu.PrefetchScalarGridSpec(
                num_scalar_prefetch=1,
                grid=(1,),
                in_specs=[anywhere] * (1 + len(crossed) + len(tokens)),
                out_specs=pl.BlockSpec((spots, rows, size), lambda i, s: (0, 0, 0)),
                scratch_shapes=[pltpu.SemaphoreType.DMA((spots,))],
            ),
            out_shape=jax.ShapeDtypeStruct((spots, rows, size), jnp.bfloat16),
            compiler_params=params,
            cost_estimate=pl.CostEstimate(
                flops=0, bytes_accessed=4 * spots * rows * size, transcendentals=0
            ),
            name="pick_states",
        )(slots, inside, *crossed, *tokens)
        return picked, gather_half(picked).reshape(4, kids, rows, size)

    def early(c, tokens):
        at = lambda q: (c, 0, q)
        operands = [
            x_in, b_in, c_in, dt_in, dt_bias[:, None], a_log[:, None], skip_row, conv_x, conv_bc
        ]
        return pl.pallas_call(
            functools.partial(drop_tokens, early_kernel, len(operands), len(tokens)),
            grid=(groups,),
            in_specs=[
                pl.BlockSpec((1, length, wide), at),
                pl.BlockSpec((1, length, size), at),
                pl.BlockSpec((1, length, size), at),
                pl.BlockSpec((1, per_group, length), lambda q: (c, q, 0)),
                pl.BlockSpec((per_group, 1), lambda q: (q, 0)),
                pl.BlockSpec((per_group, 1), lambda q: (q, 0)),
                pl.BlockSpec((1, wide), lambda q: (0, q)),
                pl.BlockSpec((taps, wide), lambda q: (0, q)),
                pl.BlockSpec((2, taps, size), lambda q: (0, 0, q)),
                *[anywhere] * len(tokens),
            ],
            out_specs=[
                pl.BlockSpec((length, wide), lambda q: (0, q)),
                pl.BlockSpec((length, size), lambda q: (0, q)),
                pl.BlockSpec((1, length, per_group), lambda q: (q, 0, 0)),
                pl.BlockSpec((1, length, per_group * FIX), lambda q: (q, 0, 0)),
            ],
            out_shape=[
                jax.ShapeDtypeStruct((length, columns), jnp.float32),
                jax.ShapeDtypeStruct((length, groups * size), jnp.bfloat16),
                jax.ShapeDtypeStruct((groups, length, per_group), jnp.float32),
                jax.ShapeDtypeStruct((groups, length, per_group * FIX), jnp.float32),
            ],
            scratch_shapes=[pltpu.VMEM((8 + length, size), jnp.float32)],
            compiler_params=params,
            cost_estimate=pl.CostEstimate(
                flops=4 * heads * length * length * width,
                bytes_accessed=8 * length * columns,
                transcendentals=heads * length * length,
            ),
            name="early",
        )(*operands, *tokens)

    def late(k, states, states_first, parts, result, tokens):
        part, offset = SPLIT[k], offsets[k]
        chunk = part * width
        unit = offset // part
        at = lambda q: (0, q * (per_group // part) + unit)
        lane = lambda q: (0, 0, q * (per_group // part) + unit)
        tail_at = SPLIT[0] * width // tail_lines
        operands = [x_in, b_in, c_in, skip_row, conv_x, conv_bc]
        specs = [
            pl.BlockSpec((kids, FIX, chunk), lane),
            pl.BlockSpec((kids, FIX, size), lambda q: (0, 0, q)),
            pl.BlockSpec((kids, FIX, size), lambda q: (0, 0, q)),
            pl.BlockSpec((1, chunk), at),
            pl.BlockSpec((taps, chunk), at),
            pl.BlockSpec((2, taps, size), lambda q: (0, 0, q)),
        ]
        for c in range(kids):
            mixed, held, column, first = parts[c]
            operands += [states, states_first, held, column, first, mixed]
            specs += [
                pl.BlockSpec((1, 1, chunk, size), lambda q, c=c: (q, c, 0, 0)),
                pl.BlockSpec((1, 1, tail_lines, size), lambda q, c=c: (q, c, tail_at, 0)),
                pl.BlockSpec((length, size), lambda q: (0, q)),
                pl.BlockSpec((1, length, per_group), lambda q: (q, 0, 0)),
                pl.BlockSpec((1, length, part * FIX), lambda q: (q, 0, unit)),
                pl.BlockSpec((length, chunk), at),
            ]
        keep = len(operands)
        operands += tokens
        specs += [anywhere] * len(tokens)
        alias = {}
        if result is not None:
            alias = {len(operands): 0}
            operands.append(result)
            specs.append(anywhere)
        return pl.pallas_call(
            functools.partial(
                drop_tokens,
                functools.partial(late_kernel, offset, lines),
                keep,
                len(operands) - keep,
            ),
            grid=(groups,),
            in_specs=specs,
            out_specs=pl.BlockSpec((kids, length, chunk), lane),
            out_shape=jax.ShapeDtypeStruct(x_in.shape, jnp.bfloat16),
            input_output_aliases=alias,
            scratch_shapes=[pltpu.VMEM((8 + FIX, size), jnp.float32)],
            compiler_params=params,
            cost_estimate=pl.CostEstimate(
                flops=4 * kids * groups * length * chunk * size,
                bytes_accessed=6 * kids * groups * length * chunk,
                transcendentals=kids * groups * length * chunk,
            ),
            name="late",
        )(*operands)

    skip_row = jnp.repeat(d_skip, width)[None, :]
    rows = [SPLIT[0] * width + tail_lines, SPLIT[1] * width]
    quarters = [0, 1, 2, 3]
    sent_a = cast(quarters, [0], [])
    crossed_a = [swap(sent_a[j], j + 4) for j in quarters]
    whole = cast_whole([sent_a[0]])
    inside = gather_half(whole)
    parts = [early(0, [whole])]
    sent_b = chunk_b(inside, [parts[0][1]])
    crossed_b = swap(sent_b, 4)
    picked_a, states_a = pick(rows[0], 0, slots_a, inside, crossed_a, [sent_b])
    parts.append(early(1, [picked_a]))
    picked_b, states_b = pick(rows[1], rows[0], slots_b, inside, [crossed_b], [parts[1][1]])
    result = late(0, states_a, states_a, parts, None, [picked_b])
    return late(1, states_b, states_a, parts, result, [])


def solution(mesh):
    rows, cols = P(("groups", "batch"), None, "head"), P(("groups", "batch"), "head")
    placed = (
        rows, rows, rows, cols, P("head"), P("head"), P("head"), P(None, "head"),
        P(None, None, "head"), cols, rows, P(("groups", "batch"), None, None, "head"),
        P("groups"), P("groups"),
    )
    local = local_halves if mesh.shape["batch"] == 8 else local_any
    return jax.shard_map(local, mesh=mesh, in_specs=placed, out_specs=rows, check_vma=False)
```

```python
import functools

import jax
import jax.numpy as jnp
from jax import lax
from jax.experimental import pallas as pl
from jax.experimental.pallas import tpu as pltpu
from jax.sharding import PartitionSpec as P

VMEM_LIMIT = 10 * 1024 * 1024
SPLIT = (8, 8)
FIX = 16


def drop_tokens(kernel, keep, tokens, *refs):
    kernel(*refs[:keep], *refs[keep + tokens :])


def parent_of(counts, order):
    index = jnp.arange(counts.shape[0], dtype=jnp.int32)
    bounds = jnp.sum(jnp.where(index[None, :] <= index[:, None], counts[None, :], 0), axis=1)
    return jnp.sum((bounds[None, :] <= order[:, None]).astype(jnp.int32), axis=1)


def conv_silu(padded, tail, rows, taps):
    length = rows.shape[0]
    reach = taps.shape[0] - 1
    padded[8 - reach : 8, :] = jnp.broadcast_to(tail, (reach, rows.shape[1])).astype(jnp.float32)
    padded[8 : 8 + length, :] = rows.astype(jnp.float32)
    total = padded[8 - reach : 8 - reach + length, :] * taps[0:1, :]
    for k in range(1, reach + 1):
        total = total + padded[8 - reach + k : 8 - reach + k + length, :] * taps[k : k + 1, :]
    half = 0.5 * total
    return (half + half * jnp.tanh(half)).astype(jnp.bfloat16)


def early_kernel(
    x_ref, b_ref, c_ref, dt_ref, bias_ref, alog_ref, skip_ref, taps_x_ref, taps_bc_ref,
    mixed_ref, c_out_ref, column_ref, first_ref, padded,
):
    length, wide = mixed_ref.shape
    heads = dt_ref.shape[1]
    width = wide // heads
    half = length // 2

    def convolve(rows, taps):
        bulk = conv_silu(padded, 0.0, rows, taps)[FIX:]
        return jnp.concatenate([jnp.zeros((FIX, rows.shape[1]), jnp.bfloat16), bulk])

    b_conv = convolve(b_ref[0], taps_bc_ref[0])
    c_conv = convolve(c_ref[0], taps_bc_ref[1])
    c_out_ref[...] = c_conv
    scores = lax.dot_general(
        c_conv, b_conv, (((1,), (1,)), ((), ())), preferred_element_type=jnp.float32
    )
    raw = dt_ref[0] + bias_ref[...]
    step = jnp.maximum(raw, 0.0) + jnp.log1p(jnp.exp(-jnp.abs(raw)))
    per_token = step * (-jnp.exp(alog_ref[...]))
    upper = lax.broadcasted_iota(jnp.int32, (length, length), 0) <= lax.broadcasted_iota(
        jnp.int32, (length, length), 1
    )
    total = lax.dot_general(
        per_token,
        upper.astype(jnp.float32),
        (((1,), (0,)), ((), ())),
        precision=lax.Precision.HIGHEST,
        preferred_element_type=jnp.float32,
    )
    row = total - jnp.log(step)
    columns = total.T
    column_ref[0] = columns
    causal = lax.broadcasted_iota(jnp.int32, (half, half), 0) >= lax.broadcasted_iota(
        jnp.int32, (half, half), 1
    )
    low = lax.broadcasted_iota(jnp.int32, (length, 2 * width), 1) < width
    for pair in range(heads // 2):
        lanes = slice(pair * 2 * width, (pair + 1) * 2 * width)
        x_conv = convolve(x_ref[0, :, lanes], taps_x_ref[:, lanes])
        parts = []
        for head in (2 * pair, 2 * pair + 1):
            column = jnp.broadcast_to(columns[:, head : head + 1], (length, half))
            rows = row[head : head + 1, :]
            near = jnp.exp(jnp.where(causal, column[:half] - rows[:, :half], -1e30))
            far = jnp.exp(column[half:] - rows[:, :half])
            last = jnp.exp(jnp.where(causal, column[half:] - rows[:, half:], -1e30))
            spot = slice(head * FIX, (head + 1) * FIX)
            first_ref[0, :half, spot] = near[:, :FIX]
            first_ref[0, half:, spot] = far[:, :FIX]
            top = (scores[:half, :half] * near).astype(jnp.bfloat16)
            left = (scores[half:, :half] * far).astype(jnp.bfloat16)
            right = (scores[half:, half:] * last).astype(jnp.bfloat16)
            below = jnp.concatenate([left, right], axis=1)
            parts.append(
                jnp.concatenate(
                    [
                        jnp.dot(top, x_conv[:half], preferred_element_type=jnp.float32),
                        jnp.dot(below, x_conv, preferred_element_type=jnp.float32),
                    ]
                )
            )
        mixed_ref[:, lanes] = jnp.where(low, parts[0], parts[1]) + skip_ref[
            :, lanes
        ] * x_conv.astype(jnp.float32)


def late_kernel(offset, lines, x_ref, b_ref, c_ref, skip_ref, taps_x_ref, taps_bc_ref, *refs):
    y_ref, padded = refs[-2:]
    kids, length, wide = y_ref.shape
    width = 64
    heads = wide // width
    reach = taps_x_ref.shape[0] - 1
    low = lax.broadcasted_iota(jnp.int32, (length, 2 * width), 1) < width
    low_first = lax.broadcasted_iota(jnp.int32, (FIX, 2 * width), 1) < width
    contract = (((1,), (1,)), ((), ()))
    for kid in range(kids):
        state_ref, tail_ref, held_ref, column_ref, first_ref, mixed_ref = refs[6 * kid : 6 * kid + 6]
        tail = tail_ref[0, 0].astype(jnp.float32)

        def opening(rows, taps, at):
            tap_rows = [tail[k * lines + at : k * lines + at + 1] for k in range(reach)]
            return conv_silu(padded, jnp.concatenate(tap_rows), rows, taps)

        b_first = opening(b_ref[kid], taps_bc_ref[0], lines - 2)
        c_first = opening(c_ref[kid], taps_bc_ref[1], lines - 1)
        c_conv = jnp.concatenate([c_first, held_ref[FIX:]])
        term = lax.dot_general(
            c_conv, state_ref[0, 0], contract, preferred_element_type=jnp.float32
        )
        scores = lax.dot_general(
            c_conv,
            jnp.concatenate([b_first] * heads),
            contract,
            preferred_element_type=jnp.float32,
        )
        mixing = (scores * first_ref[0]).astype(jnp.bfloat16)
        for pair in range(heads // 2):
            lanes = slice(pair * 2 * width, (pair + 1) * 2 * width)
            x_first = opening(
                x_ref[kid, :, lanes], taps_x_ref[:, lanes], offset * width // 128 + pair
            ).astype(jnp.float32)
            stacked = [jnp.where(low_first, x_first, 0.0), jnp.where(low_first, 0.0, x_first)]
            if pair > 0:
                stacked = [jnp.zeros((2 * pair * FIX, 2 * width), jnp.float32)] + stacked
            if 2 * pair + 2 < heads:
                spare = (heads - 2 * pair - 2) * FIX
                stacked = stacked + [jnp.zeros((spare, 2 * width), jnp.float32)]
            part = jnp.dot(
                mixing,
                jnp.concatenate(stacked).astype(jnp.bfloat16),
                preferred_element_type=jnp.float32,
            )
            part = jnp.concatenate([part[:FIX] + skip_ref[:, lanes] * x_first, part[FIX:]])
            head = offset + 2 * pair
            grow = jnp.where(
                low, column_ref[0, :, head : head + 1], column_ref[0, :, head + 1 : head + 2]
            )
            carried = (term[:, lanes] * jnp.exp(grow)).astype(jnp.bfloat16).astype(jnp.float32)
            y_ref[kid, :, lanes] = (mixed_ref[:, lanes] + part + carried).astype(jnp.bfloat16)


def cast_kernel(parts, tailed, reach, lines, *refs):
    count = len(tailed)
    ins, outs = refs[:-count], refs[-count:]
    states, tails = ins[: parts * count], ins[parts * count :]
    for j, out_ref in enumerate(outs):
        start = 0
        for at in range(parts):
            state = states[parts * j + at][0]
            rows = state.shape[0] * state.shape[1]
            out_ref[start : start + rows] = state.reshape(rows, state.shape[2]).astype(jnp.bfloat16)
            start += rows
            if at == 0 and tailed[j]:
                x_tail = tails[2 * j][0].astype(jnp.float32)
                bc_tail = tails[2 * j + 1][0].astype(jnp.float32)
                pieces = []
                for k in range(reach):
                    pieces += [x_tail[k : k + 1, i * 128 : i * 128 + 128] for i in range(lines - 2)]
                    pieces.append(bc_tail[k])
                spare = tailed[j] - lines * reach
                pieces.append(jnp.zeros((spare, 128), jnp.float32))
                out_ref[start : start + tailed[j]] = jnp.concatenate(pieces).astype(jnp.bfloat16)
                start += tailed[j]


def pick_rows_kernel(start, slots_ref, inside_ref, *refs):
    crossed, out, sems = refs[:-2], refs[-2], refs[-1]
    spots, rows = out.shape[:2]
    held = [inside_ref.at[source, pl.ds(start, rows)] for source in range(4)]
    held += list(crossed) if len(crossed) == 4 else [crossed[0].at[source] for source in range(4)]
    for i in range(spots):
        for source in range(8):

            @pl.when(slots_ref[i] == source)
            def _(source=source, i=i):
                pltpu.make_async_copy(held[source], out.at[i], sems.at[i]).start()

    for i in range(spots):
        pltpu.make_async_copy(held[0], out.at[i], sems.at[i]).wait()


def slice_kernel(start, in_ref, out_ref, sem):
    copy = pltpu.make_async_copy(in_ref.at[:, pl.ds(start, out_ref.shape[1])], out_ref, sem)
    copy.start()
    copy.wait()


def within_kernel(
    parent_ref,
    x_ref,
    b_ref,
    c_ref,
    dt_ref,
    bias_ref,
    alog_ref,
    skip_ref,
    taps_x_ref,
    taps_bc_ref,
    tail_x_ref,
    tail_bc_ref,
    mixed_ref,
    c_out_ref,
    grow_ref,
    padded,
):
    length = x_ref.shape[1]
    heads = dt_ref.shape[1]
    width = x_ref.shape[2] // heads
    b_conv = conv_silu(padded, tail_bc_ref[0, 0], b_ref[0], taps_bc_ref[0])
    c_conv = conv_silu(padded, tail_bc_ref[0, 1], c_ref[0], taps_bc_ref[1])
    c_out_ref[0] = c_conv
    scores = lax.dot_general(
        c_conv, b_conv, (((1,), (1,)), ((), ())), preferred_element_type=jnp.float32
    )
    raw = dt_ref[0] + bias_ref[...]
    step = jnp.maximum(raw, 0.0) + jnp.log1p(jnp.exp(-jnp.abs(raw)))
    per_token = step * (-jnp.exp(alog_ref[...]))
    row = lax.broadcasted_iota(jnp.int32, (length, length), 0)
    col = lax.broadcasted_iota(jnp.int32, (length, length), 1)
    upper = (row <= col).astype(jnp.float32)
    total = lax.dot_general(
        per_token,
        upper,
        (((1,), (0,)), ((), ())),
        precision=lax.Precision.HIGHEST,
        preferred_element_type=jnp.float32,
    )
    total_t = total.T
    grow_ref[0, 0] = jnp.exp(total_t)
    causal = row >= col
    low = lax.broadcasted_iota(jnp.int32, (length, 2 * width), 1) < width
    for pair in range(heads // 2):
        lanes = slice(pair * 2 * width, (pair + 1) * 2 * width)
        x_conv = conv_silu(
            padded, tail_x_ref[0, :, lanes], x_ref[0, :, lanes], taps_x_ref[:, lanes]
        )
        parts = []
        for head in (2 * pair, 2 * pair + 1):
            gap = total_t[:, head : head + 1] - total[head : head + 1, :]
            factor = jnp.exp(jnp.where(causal, gap, -1e30))
            mixing = (scores * factor * step[head : head + 1, :]).astype(jnp.bfloat16)
            parts.append(jnp.dot(mixing, x_conv, preferred_element_type=jnp.float32))
        mixed_ref[0, :, lanes] = (
            jnp.where(low, parts[0], parts[1]) + skip_ref[:, lanes] * x_conv.astype(jnp.float32)
        )


def carried_kernel(state_ref, c_ref, grow_ref, mixed_ref, y_ref):
    sources, _, part, width, size = state_ref.shape
    length = c_ref.shape[1]
    low = lax.broadcasted_iota(jnp.int32, (length, 2 * width), 1) < width
    c_conv = c_ref[0]
    for source in range(sources):
        state = state_ref[source, 0].reshape(part * width, size)
        term = lax.dot_general(
            c_conv, state, (((1,), (1,)), ((), ())), preferred_element_type=jnp.float32
        )
        for pair in range(part // 2):
            head = source * part + 2 * pair
            grow = jnp.where(
                low, grow_ref[0, 0, :, head : head + 1], grow_ref[0, 0, :, head + 1 : head + 2]
            )
            here = slice(2 * pair * width, (2 * pair + 2) * width)
            lanes = slice(head * width, (head + 2) * width)
            carried = (term[:, here] * grow).astype(jnp.bfloat16).astype(jnp.float32)
            y_ref[0, :, lanes] = (mixed_ref[0, :, lanes] + carried).astype(jnp.bfloat16)


def pick_kernel(parent_ref, state_ref, out_ref):
    out_ref[...] = state_ref[...]


def local_any(
    x_in,
    b_in,
    c_in,
    dt_in,
    dt_bias,
    a_log,
    d_skip,
    conv_x,
    conv_bc,
    par_state,
    tail_x,
    tail_bc,
    counts,
    order,
):
    kids, length, columns = x_in.shape
    heads = dt_in.shape[1]
    width, size = par_state.shape[2:]
    ways = lax.axis_size("batch")
    groups = b_in.shape[2] // size
    per_group = heads // groups
    part = heads // ways
    wide = per_group * width
    reach = tail_x.shape[1]
    parents_all = counts.shape[0]
    kids_all = order.shape[0]

    parent = parent_of(counts, order)
    own = lax.dynamic_slice_in_dim(parent, lax.axis_index("batch") * kids, kids)

    sent = par_state.astype(jnp.bfloat16).reshape(ways, part, width, size)
    shares = lax.all_to_all(sent, "batch", split_axis=0, concat_axis=0, tiled=True)

    tails = jnp.concatenate([tail_x.reshape(-1), tail_bc.reshape(-1)])
    tails = jnp.broadcast_to(tails[None], (ways, tails.shape[0]))
    tails = lax.all_to_all(tails, "batch", split_axis=0, concat_axis=0, tiled=True)
    tails_x = tails[:, : reach * columns].reshape(parents_all, reach, columns)
    tails_bc = tails[:, reach * columns :].reshape(parents_all, 2, reach, groups * size)

    picked = pl.pallas_call(
        pick_kernel,
        grid_spec=pltpu.PrefetchScalarGridSpec(
            num_scalar_prefetch=1,
            grid=(kids_all,),
            in_specs=[pl.BlockSpec((1, part, width, size), lambda i, p: (p[i], 0, 0, 0))],
            out_specs=pl.BlockSpec((1, part, width, size), lambda i, p: (i, 0, 0, 0)),
        ),
        out_shape=jax.ShapeDtypeStruct((kids_all, part, width, size), jnp.bfloat16),
        cost_estimate=pl.CostEstimate(
            flops=0, bytes_accessed=4 * kids_all * part * width * size, transcendentals=0
        ),
        name="pick_states",
    )(parent, shares)
    states = lax.all_to_all(
        picked.reshape(ways, kids, part, width, size), "batch", split_axis=0, concat_axis=0, tiled=True
    )

    skip_row = jnp.repeat(d_skip, width)[None, :]
    mixed, c_conv, grow = pl.pallas_call(
        within_kernel,
        grid_spec=pltpu.PrefetchScalarGridSpec(
            num_scalar_prefetch=1,
            grid=(kids, groups),
            in_specs=[
                pl.BlockSpec((1, length, wide), lambda c, q, p: (c, 0, q)),
                pl.BlockSpec((1, length, size), lambda c, q, p: (c, 0, q)),
                pl.BlockSpec((1, length, size), lambda c, q, p: (c, 0, q)),
                pl.BlockSpec((1, per_group, length), lambda c, q, p: (c, q, 0)),
                pl.BlockSpec((per_group, 1), lambda c, q, p: (q, 0)),
                pl.BlockSpec((per_group, 1), lambda c, q, p: (q, 0)),
                pl.BlockSpec((1, wide), lambda c, q, p: (0, q)),
                pl.BlockSpec((reach + 1, wide), lambda c, q, p: (0, q)),
                pl.BlockSpec((2, reach + 1, size), lambda c, q, p: (0, 0, q)),
                pl.BlockSpec((1, reach, wide), lambda c, q, p: (p[c], 0, q)),
                pl.BlockSpec((1, 2, reach, size), lambda c, q, p: (p[c], 0, 0, q)),
            ],
            out_specs=[
                pl.BlockSpec((1, length, wide), lambda c, q, p: (c, 0, q)),
                pl.BlockSpec((1, length, size), lambda c, q, p: (c, 0, q)),
                pl.BlockSpec((1, 1, length, per_group), lambda c, q, p: (c, q, 0, 0)),
            ],
            scratch_shapes=[pltpu.VMEM((8 + length, size), jnp.float32)],
        ),
        out_shape=[
            jax.ShapeDtypeStruct((kids, length, columns), jnp.float32),
            jax.ShapeDtypeStruct((kids, length, groups * size), jnp.bfloat16),
            jax.ShapeDtypeStruct((kids, groups, length, per_group), jnp.float32),
        ],
        compiler_params=pltpu.CompilerParams(vmem_limit_bytes=4 * VMEM_LIMIT),
        cost_estimate=pl.CostEstimate(
            flops=4 * kids * heads * length * length * width,
            bytes_accessed=6 * kids * length * columns,
            transcendentals=kids * heads * length * length,
        ),
        name="within",
    )(
        own,
        x_in,
        b_in,
        c_in,
        dt_in,
        dt_bias[:, None],
        a_log[:, None],
        skip_row,
        conv_x,
        conv_bc,
        tails_x,
        tails_bc,
    )

    sources = per_group // part
    return pl.pallas_call(
        carried_kernel,
        grid=(kids, groups),
        in_specs=[
            pl.BlockSpec((sources, 1, part, width, size), lambda c, q: (q, c, 0, 0, 0)),
            pl.BlockSpec((1, length, size), lambda c, q: (c, 0, q)),
            pl.BlockSpec((1, 1, length, per_group), lambda c, q: (c, q, 0, 0)),
            pl.BlockSpec((1, length, wide), lambda c, q: (c, 0, q)),
        ],
        out_specs=pl.BlockSpec((1, length, wide), lambda c, q: (c, 0, q)),
        out_shape=jax.ShapeDtypeStruct((kids, length, columns), jnp.bfloat16),
        compiler_params=pltpu.CompilerParams(vmem_limit_bytes=4 * VMEM_LIMIT),
        cost_estimate=pl.CostEstimate(
            flops=2 * kids * length * columns * size,
            bytes_accessed=8 * kids * length * columns,
            transcendentals=0,
        ),
        name="carried",
    )(states, c_conv, grow, mixed)


def local_halves(
    x_in, b_in, c_in, dt_in, dt_bias, a_log, d_skip, conv_x, conv_bc,
    par_state, tail_x, tail_bc, counts, order,
):
    kids, length, columns = x_in.shape
    heads = dt_in.shape[1]
    width, size = par_state.shape[2:]
    groups = b_in.shape[2] // size
    per_group = heads // groups
    wide = per_group * width
    taps = conv_x.shape[0]
    reach = taps - 1
    lines = (wide + 2 * size) // 128
    tail_lines = -(-lines * reach // 16) * 16
    params = pltpu.CompilerParams(vmem_limit_bytes=VMEM_LIMIT)
    anywhere = pl.BlockSpec(memory_space=pl.ANY)
    small = pl.CostEstimate(flops=1, bytes_accessed=1, transcendentals=0)

    stay = lambda x: pltpu.with_memory_space_constraint(x, pltpu.HBM)
    x_in, b_in, c_in, dt_in, conv_x, conv_bc = map(stay, (x_in, b_in, c_in, dt_in, conv_x, conv_bc))

    me = lax.axis_index("batch")
    parent = parent_of(counts, order)
    side = me // 4 * 4
    owner = lax.dynamic_slice_in_dim(parent, side * kids, 4 * kids)
    here = owner // 4 * 4 == side
    slots_a = jnp.where(here, owner % 4, 4 + (owner ^ me) % 4)
    slots_b = jnp.where(here, owner % 4, 4 + owner % 4)
    place = (me % 4).astype(jnp.int32)[None]

    state = stay(par_state.reshape(groups, per_group, width, size))
    x_tails, bc_tails = stay(tail_x), stay(tail_bc.transpose(0, 2, 1, 3))
    offsets = [sum(SPLIT[:k]) for k in range(len(SPLIT))]

    def swap(value, r):
        return lax.ppermute(value, "batch", perm=[(i, i ^ r) for i in range(8)])

    def cast(quarters, chunks, tokens):
        tailed = [tail_lines if chunks[0] == 0 else 0] * len(quarters)
        rows = sum(SPLIT[k] for k in chunks) * width + tailed[0]
        operands, specs = [], []
        for j in quarters:
            for k in chunks:
                part, at = SPLIT[k], offsets[k] // SPLIT[k]
                operands.append(state)
                specs.append(
                    pl.BlockSpec(
                        (1, part, width, size), lambda i, p, j=j, at=at: (p[0] ^ j, at, 0, 0)
                    )
                )
        if tailed[0]:
            for j in quarters:
                operands += [x_tails, bc_tails]
                specs += [
                    pl.BlockSpec((1, reach, wide), lambda i, p, j=j: (0, 0, p[0] ^ j)),
                    pl.BlockSpec((1, reach, 2, size), lambda i, p, j=j: (0, 0, 0, p[0] ^ j)),
                ]
        kernel = functools.partial(cast_kernel, len(chunks), tailed, reach, lines)
        return pl.pallas_call(
            functools.partial(
                drop_tokens, lambda place_ref, *refs: kernel(*refs), 1 + len(operands), len(tokens)
            ),
            grid_spec=pltpu.PrefetchScalarGridSpec(
                num_scalar_prefetch=1,
                grid=(1,),
                in_specs=specs + [anywhere] * len(tokens),
                out_specs=[pl.BlockSpec((rows, size), lambda i, p: (0, 0))] * len(quarters),
            ),
            out_shape=[jax.ShapeDtypeStruct((rows, size), jnp.bfloat16)] * len(quarters),
            compiler_params=params,
            cost_estimate=small,
            name="cast_states",
        )(place, *operands, *tokens)

    def cast_whole(tokens):
        rows = per_group * width + tail_lines

        def kernel(*refs):
            out_ref = refs[-1]
            for q in range(groups):
                cast_kernel(2, [tail_lines], reach, lines, *refs[4 * q : 4 * q + 4], out_ref.at[q])

        operands, specs = [], []
        for q in range(groups):
            operands += [state, state, x_tails, bc_tails]
            specs += [
                pl.BlockSpec((1, SPLIT[0], width, size), lambda i, q=q: (q, 0, 0, 0)),
                pl.BlockSpec((1, SPLIT[1], width, size), lambda i, q=q: (q, 1, 0, 0)),
                pl.BlockSpec((1, reach, wide), lambda i, q=q: (0, 0, q)),
                pl.BlockSpec((1, reach, 2, size), lambda i, q=q: (0, 0, 0, q)),
            ]
        return pl.pallas_call(
            functools.partial(drop_tokens, kernel, len(operands), len(tokens)),
            grid=(1,),
            in_specs=specs + [anywhere] * len(tokens),
            out_specs=pl.BlockSpec((groups, rows, size), lambda i: (0, 0, 0)),
            out_shape=jax.ShapeDtypeStruct((groups, rows, size), jnp.bfloat16),
            compiler_params=params,
            cost_estimate=small,
            name="cast_states",
        )(*operands, *tokens)

    def chunk_b(inside, tokens):
        rows = SPLIT[1] * width
        return pl.pallas_call(
            functools.partial(
                drop_tokens, functools.partial(slice_kernel, inside.shape[1] - rows), 1, len(tokens)
            ),
            grid=(1,),
            in_specs=[anywhere]
            + [anywhere] * len(tokens),
            out_specs=pl.BlockSpec((4, rows, size), lambda i: (0, 0, 0)),
            out_shape=jax.ShapeDtypeStruct((4, rows, size), jnp.bfloat16),
            scratch_shapes=[pltpu.SemaphoreType.DMA],
            compiler_params=params,
            cost_estimate=small,
            name="chunk_b",
        )(inside, *tokens)

    def gather_half(value):
        return lax.all_to_all(
            value,
            "batch",
            split_axis=0,
            concat_axis=0,
            tiled=True,
            axis_index_groups=[[0, 1, 2, 3], [4, 5, 6, 7]],
        )

    def pick(rows, start, slots, inside, crossed, tokens):
        spots = 4 * kids
        picked = pl.pallas_call(
            functools.partial(
                drop_tokens, functools.partial(pick_rows_kernel, start), 2 + len(crossed), len(tokens)
            ),
            grid_spec=pltpu.PrefetchScalarGridSpec(
                num_scalar_prefetch=1,
                grid=(1,),
                in_specs=[anywhere] * (1 + len(crossed) + len(tokens)),
                out_specs=pl.BlockSpec((spots, rows, size), lambda i, s: (0, 0, 0)),
                scratch_shapes=[pltpu.SemaphoreType.DMA((spots,))],
            ),
            out_shape=jax.ShapeDtypeStruct((spots, rows, size), jnp.bfloat16),
            compiler_params=params,
            cost_estimate=small,
            name="pick_states",
        )(slots, inside, *crossed, *tokens)
        return picked, gather_half(picked).reshape(4, kids, rows, size)

    def early(c, tokens):
        at = lambda q: (c, 0, q)
        operands = [
            x_in, b_in, c_in, dt_in, dt_bias[:, None], a_log[:, None], skip_row, conv_x, conv_bc
        ]
        return pl.pallas_call(
            functools.partial(drop_tokens, early_kernel, len(operands), len(tokens)),
            grid=(groups,),
            in_specs=[
                pl.BlockSpec((1, length, wide), at),
                pl.BlockSpec((1, length, size), at),
                pl.BlockSpec((1, length, size), at),
                pl.BlockSpec((1, per_group, length), lambda q: (c, q, 0)),
                pl.BlockSpec((per_group, 1), lambda q: (q, 0)),
                pl.BlockSpec((per_group, 1), lambda q: (q, 0)),
                pl.BlockSpec((1, wide), lambda q: (0, q)),
                pl.BlockSpec((taps, wide), lambda q: (0, q)),
                pl.BlockSpec((2, taps, size), lambda q: (0, 0, q)),
                *[anywhere] * len(tokens),
            ],
            out_specs=[
                pl.BlockSpec((length, wide), lambda q: (0, q)),
                pl.BlockSpec((length, size), lambda q: (0, q)),
                pl.BlockSpec((1, length, per_group), lambda q: (q, 0, 0)),
                pl.BlockSpec((1, length, per_group * FIX), lambda q: (q, 0, 0)),
            ],
            out_shape=[
                pltpu.HBM((length, columns), jnp.float32),
                pltpu.HBM((length, groups * size), jnp.bfloat16),
                pltpu.HBM((groups, length, per_group), jnp.float32),
                pltpu.HBM((groups, length, per_group * FIX), jnp.float32),
            ],
            scratch_shapes=[pltpu.VMEM((8 + length, size), jnp.float32)],
            compiler_params=params,
            cost_estimate=small,
            name="early",
        )(*operands, *tokens)

    def late(k, states, states_first, parts, result, tokens):
        part, offset = SPLIT[k], offsets[k]
        chunk = part * width
        unit = offset // part
        at = lambda q: (0, q * (per_group // part) + unit)
        lane = lambda q: (0, 0, q * (per_group // part) + unit)
        tail_at = SPLIT[0] * width // tail_lines
        operands = [x_in, b_in, c_in, skip_row, conv_x, conv_bc]
        specs = [
            pl.BlockSpec((kids, FIX, chunk), lane),
            pl.BlockSpec((kids, FIX, size), lambda q: (0, 0, q)),
            pl.BlockSpec((kids, FIX, size), lambda q: (0, 0, q)),
            pl.BlockSpec((1, chunk), at),
            pl.BlockSpec((taps, chunk), at),
            pl.BlockSpec((2, taps, size), lambda q: (0, 0, q)),
        ]
        for c in range(kids):
            mixed, held, column, first = map(stay, parts[c])
            operands += [states, states_first, held, column, first, mixed]
            specs += [
                pl.BlockSpec((1, 1, chunk, size), lambda q, c=c: (q, c, 0, 0)),
                pl.BlockSpec((1, 1, tail_lines, size), lambda q, c=c: (q, c, tail_at, 0)),
                pl.BlockSpec((length, size), lambda q: (0, q)),
                pl.BlockSpec((1, length, per_group), lambda q: (q, 0, 0)),
                pl.BlockSpec((1, length, part * FIX), lambda q: (q, 0, unit)),
                pl.BlockSpec((length, chunk), at),
            ]
        keep = len(operands)
        operands += tokens
        specs += [anywhere] * len(tokens)
        alias = {}
        if result is not None:
            alias = {len(operands): 0}
            operands.append(result)
            specs.append(anywhere)
        return pl.pallas_call(
            functools.partial(
                drop_tokens,
                functools.partial(late_kernel, offset, lines),
                keep,
                len(operands) - keep,
            ),
            grid=(groups,),
            in_specs=specs,
            out_specs=pl.BlockSpec((kids, length, chunk), lane),
            out_shape=jax.ShapeDtypeStruct(x_in.shape, jnp.bfloat16),
            input_output_aliases=alias,
            scratch_shapes=[pltpu.VMEM((8 + FIX, size), jnp.float32)],
            compiler_params=params,
            cost_estimate=small,
            name="late",
        )(*operands)

    skip_row = jnp.repeat(d_skip, width)[None, :]
    rows = [SPLIT[0] * width + tail_lines, SPLIT[1] * width]
    quarters = [0, 1, 2, 3]
    sent_a = cast(quarters, [0], [])
    crossed_a = [swap(sent_a[j], j + 4) for j in quarters]
    whole = cast_whole([sent_a[0]])
    inside = gather_half(whole)
    parts = [early(0, [whole])]
    sent_b = chunk_b(inside, [stay(parts[0][1])])
    crossed_b = swap(sent_b, 4)
    picked_a, states_a = pick(rows[0], 0, slots_a, inside, crossed_a, [sent_b])
    parts.append(early(1, [picked_a]))
    picked_b, states_b = pick(rows[1], rows[0], slots_b, inside, [crossed_b], [stay(parts[1][1])])
    result = late(0, states_a, states_a, parts, None, [picked_b])
    return late(1, states_b, states_a, parts, result, [])


def solution(mesh):
    rows, cols = P(("groups", "batch"), None, "head"), P(("groups", "batch"), "head")
    placed = (
        rows, rows, rows, cols, P("head"), P("head"), P("head"), P(None, "head"),
        P(None, None, "head"), cols, rows, P(("groups", "batch"), None, None, "head"),
        P("groups"), P("groups"),
    )
    local = local_halves if mesh.shape["batch"] == 8 else local_any
    return jax.shard_map(local, mesh=mesh, in_specs=placed, out_specs=rows, check_vma=False)
```

```python
import functools

import jax
import jax.numpy as jnp
from jax import lax
from jax.experimental import pallas as pl
from jax.experimental.pallas import tpu as pltpu
from jax.sharding import PartitionSpec as P

VMEM_LIMIT = 10 * 1024 * 1024
SPLIT = (8, 8)
FIX = 16


def drop_tokens(kernel, keep, tokens, *refs):
    kernel(*refs[:keep], *refs[keep + tokens :])


def parent_of(counts, order):
    index = jnp.arange(counts.shape[0], dtype=jnp.int32)
    bounds = jnp.sum(jnp.where(index[None, :] <= index[:, None], counts[None, :], 0), axis=1)
    return jnp.sum((bounds[None, :] <= order[:, None]).astype(jnp.int32), axis=1)


def conv_silu(padded, tail, rows, taps):
    length = rows.shape[0]
    reach = taps.shape[0] - 1
    padded[8 - reach : 8, :] = jnp.broadcast_to(tail, (reach, rows.shape[1])).astype(jnp.float32)
    padded[8 : 8 + length, :] = rows.astype(jnp.float32)
    total = padded[8 - reach : 8 - reach + length, :] * taps[0:1, :]
    for k in range(1, reach + 1):
        total = total + padded[8 - reach + k : 8 - reach + k + length, :] * taps[k : k + 1, :]
    half = 0.5 * total
    return (half + half * jnp.tanh(half)).astype(jnp.bfloat16)


def early_kernel(
    x_ref, b_ref, c_ref, dt_ref, bias_ref, alog_ref, skip_ref, taps_x_ref, taps_bc_ref,
    mixed_ref, c_out_ref, column_ref, first_ref, padded,
):
    length, wide = mixed_ref.shape
    heads = dt_ref.shape[1]
    width = wide // heads
    half = length // 2

    def convolve(rows, taps):
        bulk = conv_silu(padded, 0.0, rows, taps)[FIX:]
        return jnp.concatenate([jnp.zeros((FIX, rows.shape[1]), jnp.bfloat16), bulk])

    b_conv = convolve(b_ref[0], taps_bc_ref[0])
    c_conv = convolve(c_ref[0], taps_bc_ref[1])
    c_out_ref[...] = c_conv
    scores = lax.dot_general(
        c_conv, b_conv, (((1,), (1,)), ((), ())), preferred_element_type=jnp.float32
    )
    raw = dt_ref[0] + bias_ref[...]
    step = jnp.maximum(raw, 0.0) + jnp.log1p(jnp.exp(-jnp.abs(raw)))
    per_token = step * (-jnp.exp(alog_ref[...]))
    upper = lax.broadcasted_iota(jnp.int32, (length, length), 0) <= lax.broadcasted_iota(
        jnp.int32, (length, length), 1
    )
    total = lax.dot_general(
        per_token,
        upper.astype(jnp.float32),
        (((1,), (0,)), ((), ())),
        precision=lax.Precision.HIGHEST,
        preferred_element_type=jnp.float32,
    )
    row = total - jnp.log(step)
    columns = total.T
    column_ref[0] = total
    causal = lax.broadcasted_iota(jnp.int32, (half, half), 0) >= lax.broadcasted_iota(
        jnp.int32, (half, half), 1
    )
    low = lax.broadcasted_iota(jnp.int32, (length, 2 * width), 1) < width
    for pair in range(heads // 2):
        lanes = slice(pair * 2 * width, (pair + 1) * 2 * width)
        x_conv = convolve(x_ref[0, :, lanes], taps_x_ref[:, lanes])
        parts = []
        for head in (2 * pair, 2 * pair + 1):
            column = jnp.broadcast_to(columns[:, head : head + 1], (length, half))
            rows = row[head : head + 1, :]
            near = jnp.exp(jnp.where(causal, column[:half] - rows[:, :half], -1e30))
            far = jnp.exp(column[half:] - rows[:, :half])
            last = jnp.exp(jnp.where(causal, column[half:] - rows[:, half:], -1e30))
            spot = slice(head * FIX, (head + 1) * FIX)
            first_ref[0, :half, spot] = near[:, :FIX]
            first_ref[0, half:, spot] = far[:, :FIX]
            top = (scores[:half, :half] * near).astype(jnp.bfloat16)
            left = (scores[half:, :half] * far).astype(jnp.bfloat16)
            right = (scores[half:, half:] * last).astype(jnp.bfloat16)
            below = jnp.concatenate([left, right], axis=1)
            parts.append(
                jnp.concatenate(
                    [
                        jnp.dot(top, x_conv[:half], preferred_element_type=jnp.float32),
                        jnp.dot(below, x_conv, preferred_element_type=jnp.float32),
                    ]
                )
            )
        mixed_ref[:, lanes] = jnp.where(low, parts[0], parts[1]) + skip_ref[
            :, lanes
        ] * x_conv.astype(jnp.float32)


def late_kernel(offset, lines, x_ref, b_ref, c_ref, skip_ref, taps_x_ref, taps_bc_ref, tail_ref, *refs):
    y_ref, padded = refs[-2:]
    kids, length, wide = y_ref.shape
    width = 64
    heads = wide // width
    reach = taps_x_ref.shape[0] - 1
    low = lax.broadcasted_iota(jnp.int32, (length, 2 * width), 1) < width
    low_first = lax.broadcasted_iota(jnp.int32, (FIX, 2 * width), 1) < width
    contract = (((1,), (1,)), ((), ()))
    q = pl.program_id(0)
    size = c_ref.shape[2] // pl.num_programs(0)
    group_lanes = pl.ds(pl.multiple_of(q * size, 128), size)
    stride = skip_ref.shape[1] // pl.num_programs(0)
    for kid in range(kids):
        state_ref, held_ref, column_ref, first_ref, mixed_ref = refs[5 * kid : 5 * kid + 5]
        tail = tail_ref[q, kid].astype(jnp.float32)

        def opening(rows, taps, at):
            tap_rows = [tail[k * lines + at : k * lines + at + 1] for k in range(reach)]
            return conv_silu(padded, jnp.concatenate(tap_rows), rows, taps)

        b_first = opening(b_ref[kid, :, group_lanes], taps_bc_ref[0, :, group_lanes], lines - 2)
        c_first = opening(c_ref[kid, :, group_lanes], taps_bc_ref[1, :, group_lanes], lines - 1)
        c_conv = jnp.concatenate([c_first, held_ref[FIX:]])
        columns = column_ref[q].T
        term = lax.dot_general(
            c_conv, state_ref[0, 0], contract, preferred_element_type=jnp.float32
        )
        scores = lax.dot_general(
            c_conv,
            jnp.concatenate([b_first] * heads),
            contract,
            preferred_element_type=jnp.float32,
        )
        mixing = (scores * first_ref[0]).astype(jnp.bfloat16)
        for pair in range(heads // 2):
            lanes = slice(pair * 2 * width, (pair + 1) * 2 * width)
            start = pl.multiple_of(q * stride + (offset + 2 * pair) * width, 128)
            whole = pl.ds(start, 2 * width)
            x_first = opening(
                x_ref[kid, :, whole], taps_x_ref[:, whole], offset * width // 128 + pair
            ).astype(jnp.float32)
            stacked = [jnp.where(low_first, x_first, 0.0), jnp.where(low_first, 0.0, x_first)]
            if pair > 0:
                stacked = [jnp.zeros((2 * pair * FIX, 2 * width), jnp.float32)] + stacked
            if 2 * pair + 2 < heads:
                spare = (heads - 2 * pair - 2) * FIX
                stacked = stacked + [jnp.zeros((spare, 2 * width), jnp.float32)]
            part = jnp.dot(
                mixing,
                jnp.concatenate(stacked).astype(jnp.bfloat16),
                preferred_element_type=jnp.float32,
            )
            part = jnp.concatenate([part[:FIX] + skip_ref[:, whole] * x_first, part[FIX:]])
            head = offset + 2 * pair
            grow = jnp.where(
                low, columns[:, head : head + 1], columns[:, head + 1 : head + 2]
            )
            carried = (term[:, lanes] * jnp.exp(grow)).astype(jnp.bfloat16).astype(jnp.float32)
            y_ref[kid, :, lanes] = (mixed_ref[:, lanes] + part + carried).astype(jnp.bfloat16)


def cast_kernel(parts, tailed, reach, lines, *refs):
    count = len(tailed)
    ins, outs = refs[:-count], refs[-count:]
    states, tails = ins[: parts * count], ins[parts * count :]
    for j, out_ref in enumerate(outs):
        start = 0
        for at in range(parts):
            state = states[parts * j + at][0]
            rows = state.shape[0] * state.shape[1]
            out_ref[start : start + rows] = state.reshape(rows, state.shape[2]).astype(jnp.bfloat16)
            start += rows
            if at == 0 and tailed[j]:
                x_tail = tails[2 * j][0].astype(jnp.float32)
                bc_tail = tails[2 * j + 1][0].astype(jnp.float32)
                pieces = []
                for k in range(reach):
                    pieces += [x_tail[k : k + 1, i * 128 : i * 128 + 128] for i in range(lines - 2)]
                    pieces.append(bc_tail[k])
                spare = tailed[j] - lines * reach
                pieces.append(jnp.zeros((spare, 128), jnp.float32))
                out_ref[start : start + tailed[j]] = jnp.concatenate(pieces).astype(jnp.bfloat16)
                start += tailed[j]


def pick_rows_kernel(start, slots_ref, inside_ref, *refs):
    crossed, out, sems = refs[:-2], refs[-2], refs[-1]
    spots, rows = out.shape[:2]
    held = [inside_ref.at[source, pl.ds(start, rows)] for source in range(4)]
    held += list(crossed) if len(crossed) == 4 else [crossed[0].at[source] for source in range(4)]
    for i in range(spots):
        for source in range(8):

            @pl.when(slots_ref[i] == source)
            def _(source=source, i=i):
                pltpu.make_async_copy(held[source], out.at[i], sems.at[i]).start()

    for i in range(spots):
        pltpu.make_async_copy(held[0], out.at[i], sems.at[i]).wait()


def slice_kernel(start, in_ref, out_ref, tick_ref, sem):
    tick_ref[...] = jnp.zeros(tick_ref.shape, tick_ref.dtype)
    copy = pltpu.make_async_copy(in_ref.at[:, pl.ds(start, out_ref.shape[1])], out_ref, sem)
    copy.start()
    copy.wait()


def within_kernel(
    parent_ref,
    x_ref,
    b_ref,
    c_ref,
    dt_ref,
    bias_ref,
    alog_ref,
    skip_ref,
    taps_x_ref,
    taps_bc_ref,
    tail_x_ref,
    tail_bc_ref,
    mixed_ref,
    c_out_ref,
    grow_ref,
    padded,
):
    length = x_ref.shape[1]
    heads = dt_ref.shape[1]
    width = x_ref.shape[2] // heads
    b_conv = conv_silu(padded, tail_bc_ref[0, 0], b_ref[0], taps_bc_ref[0])
    c_conv = conv_silu(padded, tail_bc_ref[0, 1], c_ref[0], taps_bc_ref[1])
    c_out_ref[0] = c_conv
    scores = lax.dot_general(
        c_conv, b_conv, (((1,), (1,)), ((), ())), preferred_element_type=jnp.float32
    )
    raw = dt_ref[0] + bias_ref[...]
    step = jnp.maximum(raw, 0.0) + jnp.log1p(jnp.exp(-jnp.abs(raw)))
    per_token = step * (-jnp.exp(alog_ref[...]))
    row = lax.broadcasted_iota(jnp.int32, (length, length), 0)
    col = lax.broadcasted_iota(jnp.int32, (length, length), 1)
    upper = (row <= col).astype(jnp.float32)
    total = lax.dot_general(
        per_token,
        upper,
        (((1,), (0,)), ((), ())),
        precision=lax.Precision.HIGHEST,
        preferred_element_type=jnp.float32,
    )
    total_t = total.T
    grow_ref[0, 0] = jnp.exp(total_t)
    causal = row >= col
    low = lax.broadcasted_iota(jnp.int32, (length, 2 * width), 1) < width
    for pair in range(heads // 2):
        lanes = slice(pair * 2 * width, (pair + 1) * 2 * width)
        x_conv = conv_silu(
            padded, tail_x_ref[0, :, lanes], x_ref[0, :, lanes], taps_x_ref[:, lanes]
        )
        parts = []
        for head in (2 * pair, 2 * pair + 1):
            gap = total_t[:, head : head + 1] - total[head : head + 1, :]
            factor = jnp.exp(jnp.where(causal, gap, -1e30))
            mixing = (scores * factor * step[head : head + 1, :]).astype(jnp.bfloat16)
            parts.append(jnp.dot(mixing, x_conv, preferred_element_type=jnp.float32))
        mixed_ref[0, :, lanes] = (
            jnp.where(low, parts[0], parts[1]) + skip_ref[:, lanes] * x_conv.astype(jnp.float32)
        )


def carried_kernel(state_ref, c_ref, grow_ref, mixed_ref, y_ref):
    sources, _, part, width, size = state_ref.shape
    length = c_ref.shape[1]
    low = lax.broadcasted_iota(jnp.int32, (length, 2 * width), 1) < width
    c_conv = c_ref[0]
    for source in range(sources):
        state = state_ref[source, 0].reshape(part * width, size)
        term = lax.dot_general(
            c_conv, state, (((1,), (1,)), ((), ())), preferred_element_type=jnp.float32
        )
        for pair in range(part // 2):
            head = source * part + 2 * pair
            grow = jnp.where(
                low, grow_ref[0, 0, :, head : head + 1], grow_ref[0, 0, :, head + 1 : head + 2]
            )
            here = slice(2 * pair * width, (2 * pair + 2) * width)
            lanes = slice(head * width, (head + 2) * width)
            carried = (term[:, here] * grow).astype(jnp.bfloat16).astype(jnp.float32)
            y_ref[0, :, lanes] = (mixed_ref[0, :, lanes] + carried).astype(jnp.bfloat16)


def pick_kernel(parent_ref, state_ref, out_ref):
    out_ref[...] = state_ref[...]


def local_any(
    x_in,
    b_in,
    c_in,
    dt_in,
    dt_bias,
    a_log,
    d_skip,
    conv_x,
    conv_bc,
    par_state,
    tail_x,
    tail_bc,
    counts,
    order,
):
    kids, length, columns = x_in.shape
    heads = dt_in.shape[1]
    width, size = par_state.shape[2:]
    ways = lax.axis_size("batch")
    groups = b_in.shape[2] // size
    per_group = heads // groups
    part = heads // ways
    wide = per_group * width
    reach = tail_x.shape[1]
    parents_all = counts.shape[0]
    kids_all = order.shape[0]

    parent = parent_of(counts, order)
    own = lax.dynamic_slice_in_dim(parent, lax.axis_index("batch") * kids, kids)

    sent = par_state.astype(jnp.bfloat16).reshape(ways, part, width, size)
    shares = lax.all_to_all(sent, "batch", split_axis=0, concat_axis=0, tiled=True)

    tails = jnp.concatenate([tail_x.reshape(-1), tail_bc.reshape(-1)])
    tails = jnp.broadcast_to(tails[None], (ways, tails.shape[0]))
    tails = lax.all_to_all(tails, "batch", split_axis=0, concat_axis=0, tiled=True)
    tails_x = tails[:, : reach * columns].reshape(parents_all, reach, columns)
    tails_bc = tails[:, reach * columns :].reshape(parents_all, 2, reach, groups * size)

    picked = pl.pallas_call(
        pick_kernel,
        grid_spec=pltpu.PrefetchScalarGridSpec(
            num_scalar_prefetch=1,
            grid=(kids_all,),
            in_specs=[pl.BlockSpec((1, part, width, size), lambda i, p: (p[i], 0, 0, 0))],
            out_specs=pl.BlockSpec((1, part, width, size), lambda i, p: (i, 0, 0, 0)),
        ),
        out_shape=jax.ShapeDtypeStruct((kids_all, part, width, size), jnp.bfloat16),
        cost_estimate=pl.CostEstimate(
            flops=0, bytes_accessed=4 * kids_all * part * width * size, transcendentals=0
        ),
        name="pick_states",
    )(parent, shares)
    states = lax.all_to_all(
        picked.reshape(ways, kids, part, width, size), "batch", split_axis=0, concat_axis=0, tiled=True
    )

    skip_row = jnp.repeat(d_skip, width)[None, :]
    mixed, c_conv, grow = pl.pallas_call(
        within_kernel,
        grid_spec=pltpu.PrefetchScalarGridSpec(
            num_scalar_prefetch=1,
            grid=(kids, groups),
            in_specs=[
                pl.BlockSpec((1, length, wide), lambda c, q, p: (c, 0, q)),
                pl.BlockSpec((1, length, size), lambda c, q, p: (c, 0, q)),
                pl.BlockSpec((1, length, size), lambda c, q, p: (c, 0, q)),
                pl.BlockSpec((1, per_group, length), lambda c, q, p: (c, q, 0)),
                pl.BlockSpec((per_group, 1), lambda c, q, p: (q, 0)),
                pl.BlockSpec((per_group, 1), lambda c, q, p: (q, 0)),
                pl.BlockSpec((1, wide), lambda c, q, p: (0, q)),
                pl.BlockSpec((reach + 1, wide), lambda c, q, p: (0, q)),
                pl.BlockSpec((2, reach + 1, size), lambda c, q, p: (0, 0, q)),
                pl.BlockSpec((1, reach, wide), lambda c, q, p: (p[c], 0, q)),
                pl.BlockSpec((1, 2, reach, size), lambda c, q, p: (p[c], 0, 0, q)),
            ],
            out_specs=[
                pl.BlockSpec((1, length, wide), lambda c, q, p: (c, 0, q)),
                pl.BlockSpec((1, length, size), lambda c, q, p: (c, 0, q)),
                pl.BlockSpec((1, 1, length, per_group), lambda c, q, p: (c, q, 0, 0)),
            ],
            scratch_shapes=[pltpu.VMEM((8 + length, size), jnp.float32)],
        ),
        out_shape=[
            jax.ShapeDtypeStruct((kids, length, columns), jnp.float32),
            jax.ShapeDtypeStruct((kids, length, groups * size), jnp.bfloat16),
            jax.ShapeDtypeStruct((kids, groups, length, per_group), jnp.float32),
        ],
        compiler_params=pltpu.CompilerParams(vmem_limit_bytes=4 * VMEM_LIMIT),
        cost_estimate=pl.CostEstimate(
            flops=4 * kids * heads * length * length * width,
            bytes_accessed=6 * kids * length * columns,
            transcendentals=kids * heads * length * length,
        ),
        name="within",
    )(
        own,
        x_in,
        b_in,
        c_in,
        dt_in,
        dt_bias[:, None],
        a_log[:, None],
        skip_row,
        conv_x,
        conv_bc,
        tails_x,
        tails_bc,
    )

    sources = per_group // part
    return pl.pallas_call(
        carried_kernel,
        grid=(kids, groups),
        in_specs=[
            pl.BlockSpec((sources, 1, part, width, size), lambda c, q: (q, c, 0, 0, 0)),
            pl.BlockSpec((1, length, size), lambda c, q: (c, 0, q)),
            pl.BlockSpec((1, 1, length, per_group), lambda c, q: (c, q, 0, 0)),
            pl.BlockSpec((1, length, wide), lambda c, q: (c, 0, q)),
        ],
        out_specs=pl.BlockSpec((1, length, wide), lambda c, q: (c, 0, q)),
        out_shape=jax.ShapeDtypeStruct((kids, length, columns), jnp.bfloat16),
        compiler_params=pltpu.CompilerParams(vmem_limit_bytes=4 * VMEM_LIMIT),
        cost_estimate=pl.CostEstimate(
            flops=2 * kids * length * columns * size,
            bytes_accessed=8 * kids * length * columns,
            transcendentals=0,
        ),
        name="carried",
    )(states, c_conv, grow, mixed)


def local_halves(
    x_in, b_in, c_in, dt_in, dt_bias, a_log, d_skip, conv_x, conv_bc,
    par_state, tail_x, tail_bc, counts, order,
):
    kids, length, columns = x_in.shape
    heads = dt_in.shape[1]
    width, size = par_state.shape[2:]
    groups = b_in.shape[2] // size
    per_group = heads // groups
    wide = per_group * width
    taps = conv_x.shape[0]
    reach = taps - 1
    lines = (wide + 2 * size) // 128
    tail_lines = -(-lines * reach // 16) * 16
    params = pltpu.CompilerParams(vmem_limit_bytes=VMEM_LIMIT)
    anywhere = pl.BlockSpec(memory_space=pl.ANY)
    small = pl.CostEstimate(flops=1, bytes_accessed=1, transcendentals=0)

    stay = lambda x: pltpu.with_memory_space_constraint(x, pltpu.HBM)
    x_in, b_in, c_in, dt_in, conv_x, conv_bc = map(stay, (x_in, b_in, c_in, dt_in, conv_x, conv_bc))

    me = lax.axis_index("batch")
    parent = parent_of(counts, order)
    side = me // 4 * 4
    owner = lax.dynamic_slice_in_dim(parent, side * kids, 4 * kids)
    here = owner // 4 * 4 == side
    slots_a = jnp.where(here, owner % 4, 4 + (owner ^ me) % 4)
    slots_b = jnp.where(here, owner % 4, 4 + owner % 4)
    place = (me % 4).astype(jnp.int32)[None]

    state = stay(par_state.reshape(groups, per_group, width, size))
    x_tails, bc_tails = stay(tail_x), stay(tail_bc.transpose(0, 2, 1, 3))
    offsets = [sum(SPLIT[:k]) for k in range(len(SPLIT))]

    def swap(value, r):
        return lax.ppermute(value, "batch", perm=[(i, i ^ r) for i in range(8)])

    def cast(quarters, chunks, tokens):
        tailed = [tail_lines if chunks[0] == 0 else 0] * len(quarters)
        rows = sum(SPLIT[k] for k in chunks) * width + tailed[0]
        operands, specs = [], []
        for j in quarters:
            for k in chunks:
                part, at = SPLIT[k], offsets[k] // SPLIT[k]
                operands.append(state)
                specs.append(
                    pl.BlockSpec(
                        (1, part, width, size), lambda i, p, j=j, at=at: (p[0] ^ j, at, 0, 0)
                    )
                )
        if tailed[0]:
            for j in quarters:
                operands += [x_tails, bc_tails]
                specs += [
                    pl.BlockSpec((1, reach, wide), lambda i, p, j=j: (0, 0, p[0] ^ j)),
                    pl.BlockSpec((1, reach, 2, size), lambda i, p, j=j: (0, 0, 0, p[0] ^ j)),
                ]
        def kernel(*refs):
            cast_kernel(len(chunks), tailed, reach, lines, *refs[:-1])
            refs[-1][...] = jnp.zeros(refs[-1].shape, jnp.bfloat16)

        return pl.pallas_call(
            functools.partial(
                drop_tokens, lambda place_ref, *refs: kernel(*refs), 1 + len(operands), len(tokens)
            ),
            grid_spec=pltpu.PrefetchScalarGridSpec(
                num_scalar_prefetch=1,
                grid=(1,),
                in_specs=specs + [anywhere] * len(tokens),
                out_specs=[pl.BlockSpec(memory_space=pltpu.VMEM)] * (len(quarters) + 1),
            ),
            out_shape=[pltpu.VMEM((rows, size), jnp.bfloat16)] * len(quarters)
            + [pltpu.VMEM((16, size), jnp.bfloat16)],
            compiler_params=params,
            cost_estimate=small,
            name="cast_states",
        )(place, *operands, *tokens)

    def cast_whole(tokens):
        rows = per_group * width + tail_lines

        def kernel(*refs):
            out_ref = refs[-1]
            for q in range(groups):
                cast_kernel(2, [tail_lines], reach, lines, *refs[4 * q : 4 * q + 4], out_ref.at[q])

        operands, specs = [], []
        for q in range(groups):
            operands += [state, state, x_tails, bc_tails]
            specs += [
                pl.BlockSpec((1, SPLIT[0], width, size), lambda i, q=q: (q, 0, 0, 0)),
                pl.BlockSpec((1, SPLIT[1], width, size), lambda i, q=q: (q, 1, 0, 0)),
                pl.BlockSpec((1, reach, wide), lambda i, q=q: (0, 0, q)),
                pl.BlockSpec((1, reach, 2, size), lambda i, q=q: (0, 0, 0, q)),
            ]
        return pl.pallas_call(
            functools.partial(drop_tokens, kernel, len(operands), len(tokens)),
            grid=(1,),
            in_specs=specs + [anywhere] * len(tokens),
            out_specs=pl.BlockSpec(memory_space=pltpu.VMEM),
            out_shape=pltpu.VMEM((groups, rows, size), jnp.bfloat16),
            compiler_params=params,
            cost_estimate=small,
            name="cast_states",
        )(*operands, *tokens)

    def chunk_b(inside, tokens):
        rows = SPLIT[1] * width
        return pl.pallas_call(
            functools.partial(
                drop_tokens, functools.partial(slice_kernel, inside.shape[1] - rows), 1, len(tokens)
            ),
            grid=(1,),
            in_specs=[anywhere]
            + [anywhere] * len(tokens),
            out_specs=[pl.BlockSpec(memory_space=pltpu.VMEM)] * 2,
            out_shape=[
                pltpu.VMEM((4, rows, size), jnp.bfloat16),
                pltpu.VMEM((16, size), jnp.bfloat16),
            ],
            scratch_shapes=[pltpu.SemaphoreType.DMA],
            compiler_params=params,
            cost_estimate=small,
            name="chunk_b",
        )(inside, *tokens)

    def gather_half(value):
        return lax.all_to_all(
            value,
            "batch",
            split_axis=0,
            concat_axis=0,
            tiled=True,
            axis_index_groups=[[0, 1, 2, 3], [4, 5, 6, 7]],
        )

    def pick(rows, start, slots, inside, crossed, tokens):
        spots = 4 * kids
        picked = pl.pallas_call(
            functools.partial(
                drop_tokens, functools.partial(pick_rows_kernel, start), 2 + len(crossed), len(tokens)
            ),
            grid_spec=pltpu.PrefetchScalarGridSpec(
                num_scalar_prefetch=1,
                grid=(1,),
                in_specs=[anywhere] * (1 + len(crossed) + len(tokens)),
                out_specs=pl.BlockSpec(memory_space=pltpu.VMEM),
                scratch_shapes=[pltpu.SemaphoreType.DMA((spots,))],
            ),
            out_shape=pltpu.VMEM((spots, rows, size), jnp.bfloat16),
            compiler_params=params,
            cost_estimate=small,
            name="pick_states",
        )(slots, inside, *crossed, *tokens)
        return picked, gather_half(picked).reshape(4, kids, rows, size)

    def early(c, tokens):
        at = lambda q: (c, 0, q)
        operands = [
            x_in, b_in, c_in, dt_in, dt_bias[:, None], a_log[:, None], skip_row, conv_x, conv_bc
        ]
        return pl.pallas_call(
            functools.partial(drop_tokens, early_kernel, len(operands), len(tokens)),
            grid=(groups,),
            in_specs=[
                pl.BlockSpec((1, length, wide), at),
                pl.BlockSpec((1, length, size), at),
                pl.BlockSpec((1, length, size), at),
                pl.BlockSpec((1, per_group, length), lambda q: (c, q, 0)),
                pl.BlockSpec((per_group, 1), lambda q: (q, 0)),
                pl.BlockSpec((per_group, 1), lambda q: (q, 0)),
                pl.BlockSpec((1, wide), lambda q: (0, q)),
                pl.BlockSpec((taps, wide), lambda q: (0, q)),
                pl.BlockSpec((2, taps, size), lambda q: (0, 0, q)),
                *[anywhere] * len(tokens),
            ],
            out_specs=[
                pl.BlockSpec((length, wide), lambda q: (0, q)),
                pl.BlockSpec((length, size), lambda q: (0, q)),
                pl.BlockSpec((1, per_group, length), lambda q: (q, 0, 0)),
                pl.BlockSpec((1, length, per_group * FIX), lambda q: (q, 0, 0)),
            ],
            out_shape=[
                pltpu.HBM((length, columns), jnp.float32),
                pltpu.HBM((length, groups * size), jnp.bfloat16),
                pltpu.HBM((groups, per_group, length), jnp.float32),
                pltpu.HBM((groups, length, per_group * FIX), jnp.float32),
            ],
            scratch_shapes=[pltpu.VMEM((8 + length, size), jnp.float32)],
            compiler_params=params,
            cost_estimate=small,
            name="early",
        )(*operands, *tokens)

    def late(k, states, states_first, parts, result, tokens):
        part, offset = SPLIT[k], offsets[k]
        chunk = part * width
        unit = offset // part
        at = lambda q: (0, q * (per_group // part) + unit)
        lane = lambda q: (0, 0, q * (per_group // part) + unit)
        tail_at = SPLIT[0] * width // tail_lines
        operands = [x_in, b_in, c_in, skip_row, conv_x, conv_bc, states_first]
        specs = [
            pl.BlockSpec((kids, FIX, columns), lambda q: (0, 0, 0)),
            pl.BlockSpec((kids, FIX, groups * size), lambda q: (0, 0, 0)),
            pl.BlockSpec((kids, FIX, groups * size), lambda q: (0, 0, 0)),
            pl.BlockSpec((1, columns), lambda q: (0, 0)),
            pl.BlockSpec((taps, columns), lambda q: (0, 0)),
            pl.BlockSpec((2, taps, groups * size), lambda q: (0, 0, 0)),
            pl.BlockSpec((groups, kids, tail_lines, size), lambda q: (0, 0, tail_at, 0)),
        ]
        for c in range(kids):
            mixed, held, column, first = map(stay, parts[c])
            operands += [states, held, column, first, mixed]
            specs += [
                pl.BlockSpec((1, 1, chunk, size), lambda q, c=c: (q, c, 0, 0)),
                pl.BlockSpec((length, size), lambda q: (0, q)),
                pl.BlockSpec((groups, per_group, length), lambda q: (0, 0, 0)),
                pl.BlockSpec((1, length, part * FIX), lambda q: (q, 0, unit)),
                pl.BlockSpec((length, chunk), at),
            ]
        keep = len(operands)
        operands += tokens
        specs += [anywhere] * len(tokens)
        alias = {}
        if result is not None:
            alias = {len(operands): 0}
            operands.append(result)
            specs.append(anywhere)
        return pl.pallas_call(
            functools.partial(
                drop_tokens,
                functools.partial(late_kernel, offset, lines),
                keep,
                len(operands) - keep,
            ),
            grid=(groups,),
            in_specs=specs,
            out_specs=pl.BlockSpec((kids, length, chunk), lane),
            out_shape=jax.ShapeDtypeStruct(x_in.shape, jnp.bfloat16),
            input_output_aliases=alias,
            scratch_shapes=[pltpu.VMEM((8 + FIX, size), jnp.float32)],
            compiler_params=params,
            cost_estimate=small,
            name="late",
        )(*operands)

    skip_row = jnp.repeat(d_skip, width)[None, :]
    rows = [SPLIT[0] * width + tail_lines, SPLIT[1] * width]
    quarters = [0, 1, 2, 3]
    sent_a = cast(quarters, [0], [])
    *sent_a, tick = sent_a
    crossed_a = [swap(sent_a[j], j + 4) for j in quarters]
    whole = cast_whole([swap(tick, 1)])
    inside = gather_half(whole)
    parts = [early(0, [whole])]
    sent_b, tick = chunk_b(inside, [stay(parts[0][1])])
    crossed_b = swap(sent_b, 4)
    picked_a, states_a = pick(rows[0], 0, slots_a, inside, crossed_a, [swap(tick, 1)])
    parts.append(early(1, [picked_a]))
    picked_b, states_b = pick(rows[1], rows[0], slots_b, inside, [crossed_b], [stay(parts[1][1])])
    result = late(0, states_a, states_a, parts, None, [picked_b])
    return late(1, states_b, states_a, parts, result, [])


def solution(mesh):
    rows, cols = P(("groups", "batch"), None, "head"), P(("groups", "batch"), "head")
    placed = (
        rows, rows, rows, cols, P("head"), P("head"), P("head"), P(None, "head"),
        P(None, None, "head"), cols, rows, P(("groups", "batch"), None, None, "head"),
        P("groups"), P("groups"),
    )
    local = local_halves if mesh.shape["batch"] == 8 else local_any
    return jax.shard_map(local, mesh=mesh, in_specs=placed, out_specs=rows, check_vma=False)
```

```python
import functools

import jax
import jax.numpy as jnp
from jax import lax
from jax.experimental import pallas as pl
from jax.experimental.pallas import tpu as pltpu
from jax.sharding import PartitionSpec as P

VMEM_LIMIT = 16 * 1024 * 1024
SPLIT = (8, 8)
FIX = 16
LOG2_E = 1.4426950408889634


def drop_tokens(kernel, keep, tokens, *refs):
    kernel(*refs[:keep], *refs[keep + tokens :])


def parent_of(counts, order):
    index = jnp.arange(counts.shape[0], dtype=jnp.int32)
    bounds = jnp.sum(jnp.where(index[None, :] <= index[:, None], counts[None, :], 0), axis=1)
    return jnp.sum((bounds[None, :] <= order[:, None]).astype(jnp.int32), axis=1)


def conv_silu(padded, tail, rows, taps):
    length = rows.shape[0]
    reach = taps.shape[0] - 1
    padded[8 - reach : 8, :] = jnp.broadcast_to(tail, (reach, rows.shape[1])).astype(jnp.float32)
    padded[8 : 8 + length, :] = rows.astype(jnp.float32)
    total = padded[8 - reach : 8 - reach + length, :] * taps[0:1, :]
    for k in range(1, reach + 1):
        total = total + padded[8 - reach + k : 8 - reach + k + length, :] * taps[k : k + 1, :]
    half = 0.5 * total
    return (half + half * jnp.tanh(half)).astype(jnp.bfloat16)


def early_kernel(
    x_ref, b_ref, c_ref, dt_ref, bias_ref, alog_ref, skip_ref, taps_x_ref, taps_bc_ref,
    mixed_ref, c_out_ref, column_ref, first_ref, padded,
):
    length, wide = x_ref.shape[1:]
    heads = dt_ref.shape[1]
    q = pl.program_id(0)
    width = wide // heads
    half = length // 2

    def convolve(rows, taps):
        bulk = conv_silu(padded, 0.0, rows, taps)[FIX:]
        return jnp.concatenate([jnp.zeros((FIX, rows.shape[1]), jnp.bfloat16), bulk])

    b_conv = convolve(b_ref[0], taps_bc_ref[0])
    c_conv = convolve(c_ref[0], taps_bc_ref[1])
    c_out_ref[q] = c_conv
    scores = lax.dot_general(
        c_conv, b_conv, (((1,), (1,)), ((), ())), preferred_element_type=jnp.float32
    )
    raw = dt_ref[0] + bias_ref[...]
    step = jnp.maximum(raw, 0.0) + jnp.log1p(jnp.exp(-jnp.abs(raw)))
    per_token = step * (-jnp.exp(alog_ref[...]))
    upper = lax.broadcasted_iota(jnp.int32, (length, length), 0) <= lax.broadcasted_iota(
        jnp.int32, (length, length), 1
    )
    total = lax.dot_general(
        per_token,
        upper.astype(jnp.float32),
        (((1,), (0,)), ((), ())),
        precision=lax.Precision.HIGHEST,
        preferred_element_type=jnp.float32,
    )
    total = total * LOG2_E
    row = total - jnp.log(step) * LOG2_E
    columns = total.T
    column_ref[q] = total
    causal = lax.broadcasted_iota(jnp.int32, (half, half), 0) >= lax.broadcasted_iota(
        jnp.int32, (half, half), 1
    )
    low = lax.broadcasted_iota(jnp.int32, (length, 2 * width), 1) < width
    for pair in range(heads // 2):
        lanes = slice(pair * 2 * width, (pair + 1) * 2 * width)
        x_conv = convolve(x_ref[0, :, lanes], taps_x_ref[:, lanes])
        parts = []
        for head in (2 * pair, 2 * pair + 1):
            column = jnp.broadcast_to(columns[:, head : head + 1], (length, half))
            rows = row[head : head + 1, :]
            near = jnp.exp2(jnp.where(causal, column[:half] - rows[:, :half], -1e30))
            far = jnp.exp2(column[half:] - rows[:, :half])
            last = jnp.exp2(jnp.where(causal, column[half:] - rows[:, half:], -1e30))
            spot = slice(head * FIX, (head + 1) * FIX)
            first_ref[q, :half, spot] = near[:, :FIX]
            first_ref[q, half:, spot] = far[:, :FIX]
            top = (scores[:half, :half] * near).astype(jnp.bfloat16)
            left = (scores[half:, :half] * far).astype(jnp.bfloat16)
            right = (scores[half:, half:] * last).astype(jnp.bfloat16)
            below = jnp.concatenate([left, right], axis=1)
            parts.append(
                jnp.concatenate(
                    [
                        jnp.dot(top, x_conv[:half], preferred_element_type=jnp.float32),
                        jnp.dot(below, x_conv, preferred_element_type=jnp.float32),
                    ]
                )
            )
        mixed_ref[q, :, lanes] = jnp.where(low, parts[0], parts[1]) + skip_ref[
            :, lanes
        ] * x_conv.astype(jnp.float32)


def late_kernel(
    offset, lines, place_ref, x_ref, b_ref, c_ref, skip_ref, taps_x_ref, taps_bc_ref, *refs
):
    tails, states, parts, (y_ref, padded) = refs[:4], refs[4:8], refs[8:-2], refs[-2:]
    kids, length, wide = y_ref.shape
    width = 64
    heads = wide // width
    reach = taps_x_ref.shape[0] - 1
    q = pl.program_id(0)
    far = q ^ place_ref[0]
    size = c_ref.shape[2] // pl.num_programs(0)
    stride = skip_ref.shape[1] // pl.num_programs(0)
    group_lanes = pl.ds(pl.multiple_of(q * size, 128), size)
    low_first = lax.broadcasted_iota(jnp.int32, (FIX, 2 * width), 1) < width
    spread_row = lax.broadcasted_iota(jnp.int32, (4 * heads, wide), 0)
    spread_lane = lax.broadcasted_iota(jnp.int32, (4 * heads, wide), 1)
    spread = (spread_row % heads == spread_lane // width).astype(jnp.bfloat16)
    contract = (((1,), (1,)), ((), ()))

    def choose(blocks):
        near = jnp.where(far == 0, blocks[0], blocks[1])
        return jnp.where(far <= 1, near, jnp.where(far == 2, blocks[2], blocks[3]))

    for kid in range(kids):
        held_ref, column_ref, first_ref, mixed_ref = parts[4 * kid : 4 * kid + 4]
        tail = choose([ref[kid] for ref in tails]).astype(jnp.float32)
        state = choose([ref[kid] for ref in states])

        def opening(rows, taps, at):
            tap_rows = [tail[k * lines + at : k * lines + at + 1] for k in range(reach)]
            return conv_silu(padded, jnp.concatenate(tap_rows), rows, taps)

        b_first = opening(b_ref[kid, :, group_lanes], taps_bc_ref[0, :, group_lanes], lines - 2)
        c_first = opening(c_ref[kid, :, group_lanes], taps_bc_ref[1, :, group_lanes], lines - 1)
        c_conv = jnp.concatenate([c_first, held_ref[q, FIX:]])
        grow = jnp.exp2(column_ref[q, offset : offset + heads, :])
        terms = []
        for _ in range(3):
            terms.append(grow.astype(jnp.bfloat16).astype(jnp.float32))
            grow = grow - terms[-1]
        terms = jnp.concatenate(terms + [jnp.zeros_like(grow)]).T.astype(jnp.bfloat16)
        grow = jnp.dot(terms, spread, preferred_element_type=jnp.float32)
        term = lax.dot_general(c_conv, state, contract, preferred_element_type=jnp.float32)
        carried = (term * grow).astype(jnp.bfloat16)
        scores = lax.dot_general(
            c_conv,
            jnp.concatenate([b_first] * heads),
            contract,
            preferred_element_type=jnp.float32,
        )
        unit = offset // heads * heads * FIX
        mixing = (scores * first_ref[q, :, unit : unit + heads * FIX]).astype(jnp.bfloat16)
        for pair in range(heads // 2):
            lanes = slice(pair * 2 * width, (pair + 1) * 2 * width)
            start = pl.multiple_of(q * stride + (offset + 2 * pair) * width, 128)
            whole = pl.ds(start, 2 * width)
            x_first = opening(
                x_ref[kid, :, whole], taps_x_ref[:, whole], offset * width // 128 + pair
            ).astype(jnp.float32)
            stacked = [jnp.where(low_first, x_first, 0.0), jnp.where(low_first, 0.0, x_first)]
            if pair > 0:
                stacked = [jnp.zeros((2 * pair * FIX, 2 * width), jnp.float32)] + stacked
            if 2 * pair + 2 < heads:
                spare = (heads - 2 * pair - 2) * FIX
                stacked = stacked + [jnp.zeros((spare, 2 * width), jnp.float32)]
            part = jnp.dot(
                mixing,
                jnp.concatenate(stacked).astype(jnp.bfloat16),
                preferred_element_type=jnp.float32,
            )
            part = jnp.concatenate([part[:FIX] + skip_ref[:, whole] * x_first, part[FIX:]])
            here = slice(offset * width + lanes.start, offset * width + lanes.stop)
            y_ref[kid, :, lanes] = (
                mixed_ref[q, :, here] + part + carried[:, lanes].astype(jnp.float32)
            ).astype(jnp.bfloat16)


def cast_kernel(parts, tailed, reach, lines, *refs):
    count = len(tailed)
    ins, outs = refs[:-count], refs[-count:]
    states, tails = ins[: parts * count], ins[parts * count :]
    for j, out_ref in enumerate(outs):
        start = 0
        for at in range(parts):
            state = states[parts * j + at][0]
            rows = state.shape[0] * state.shape[1]
            out_ref[start : start + rows] = state.reshape(rows, state.shape[2]).astype(jnp.bfloat16)
            start += rows
            if at == 0 and tailed[j]:
                x_tail = tails[2 * j][0].astype(jnp.float32)
                bc_tail = tails[2 * j + 1][0].astype(jnp.float32)
                pieces = []
                for k in range(reach):
                    pieces += [x_tail[k : k + 1, i * 128 : i * 128 + 128] for i in range(lines - 2)]
                    pieces.append(bc_tail[k])
                spare = tailed[j] - lines * reach
                pieces.append(jnp.zeros((spare, 128), jnp.float32))
                out_ref[start : start + tailed[j]] = jnp.concatenate(pieces).astype(jnp.bfloat16)
                start += tailed[j]


def pick_rows_kernel(start, slots_ref, inside_ref, *refs):
    crossed, outs, sems = refs[:-5], refs[-5:-1], refs[-1]
    kids, rows = outs[0].shape[:2]
    held = [inside_ref.at[source, pl.ds(start, rows)] for source in range(4)]
    held += list(crossed) if len(crossed) == 4 else [crossed[0].at[source] for source in range(4)]
    for j, out in enumerate(outs):
        for kid in range(kids):
            for source in range(8):

                @pl.when(slots_ref[j * kids + kid] == source)
                def _(source=source, out=out, j=j, kid=kid):
                    pltpu.make_async_copy(held[source], out.at[kid], sems.at[j, kid]).start()

    for j, out in enumerate(outs):
        for kid in range(kids):
            pltpu.make_async_copy(held[0], out.at[kid], sems.at[j, kid]).wait()


def slice_kernel(start, in_ref, out_ref, sem):
    copy = pltpu.make_async_copy(in_ref.at[:, pl.ds(start, out_ref.shape[1])], out_ref, sem)
    copy.start()
    copy.wait()


def within_kernel(
    parent_ref,
    x_ref,
    b_ref,
    c_ref,
    dt_ref,
    bias_ref,
    alog_ref,
    skip_ref,
    taps_x_ref,
    taps_bc_ref,
    tail_x_ref,
    tail_bc_ref,
    mixed_ref,
    c_out_ref,
    grow_ref,
    padded,
):
    length = x_ref.shape[1]
    heads = dt_ref.shape[1]
    width = x_ref.shape[2] // heads
    b_conv = conv_silu(padded, tail_bc_ref[0, 0], b_ref[0], taps_bc_ref[0])
    c_conv = conv_silu(padded, tail_bc_ref[0, 1], c_ref[0], taps_bc_ref[1])
    c_out_ref[0] = c_conv
    scores = lax.dot_general(
        c_conv, b_conv, (((1,), (1,)), ((), ())), preferred_element_type=jnp.float32
    )
    raw = dt_ref[0] + bias_ref[...]
    step = jnp.maximum(raw, 0.0) + jnp.log1p(jnp.exp(-jnp.abs(raw)))
    per_token = step * (-jnp.exp(alog_ref[...]))
    row = lax.broadcasted_iota(jnp.int32, (length, length), 0)
    col = lax.broadcasted_iota(jnp.int32, (length, length), 1)
    upper = (row <= col).astype(jnp.float32)
    total = lax.dot_general(
        per_token,
        upper,
        (((1,), (0,)), ((), ())),
        precision=lax.Precision.HIGHEST,
        preferred_element_type=jnp.float32,
    )
    total_t = total.T
    grow_ref[0, 0] = jnp.exp(total_t)
    causal = row >= col
    low = lax.broadcasted_iota(jnp.int32, (length, 2 * width), 1) < width
    for pair in range(heads // 2):
        lanes = slice(pair * 2 * width, (pair + 1) * 2 * width)
        x_conv = conv_silu(
            padded, tail_x_ref[0, :, lanes], x_ref[0, :, lanes], taps_x_ref[:, lanes]
        )
        parts = []
        for head in (2 * pair, 2 * pair + 1):
            gap = total_t[:, head : head + 1] - total[head : head + 1, :]
            factor = jnp.exp(jnp.where(causal, gap, -1e30))
            mixing = (scores * factor * step[head : head + 1, :]).astype(jnp.bfloat16)
            parts.append(jnp.dot(mixing, x_conv, preferred_element_type=jnp.float32))
        mixed_ref[0, :, lanes] = (
            jnp.where(low, parts[0], parts[1]) + skip_ref[:, lanes] * x_conv.astype(jnp.float32)
        )


def carried_kernel(state_ref, c_ref, grow_ref, mixed_ref, y_ref):
    sources, _, part, width, size = state_ref.shape
    length = c_ref.shape[1]
    low = lax.broadcasted_iota(jnp.int32, (length, 2 * width), 1) < width
    c_conv = c_ref[0]
    for source in range(sources):
        state = state_ref[source, 0].reshape(part * width, size)
        term = lax.dot_general(
            c_conv, state, (((1,), (1,)), ((), ())), preferred_element_type=jnp.float32
        )
        for pair in range(part // 2):
            head = source * part + 2 * pair
            grow = jnp.where(
                low, grow_ref[0, 0, :, head : head + 1], grow_ref[0, 0, :, head + 1 : head + 2]
            )
            here = slice(2 * pair * width, (2 * pair + 2) * width)
            lanes = slice(head * width, (head + 2) * width)
            carried = (term[:, here] * grow).astype(jnp.bfloat16).astype(jnp.float32)
            y_ref[0, :, lanes] = (mixed_ref[0, :, lanes] + carried).astype(jnp.bfloat16)


def pick_kernel(parent_ref, state_ref, out_ref):
    out_ref[...] = state_ref[...]


def local_any(
    x_in,
    b_in,
    c_in,
    dt_in,
    dt_bias,
    a_log,
    d_skip,
    conv_x,
    conv_bc,
    par_state,
    tail_x,
    tail_bc,
    counts,
    order,
):
    kids, length, columns = x_in.shape
    heads = dt_in.shape[1]
    width, size = par_state.shape[2:]
    ways = lax.axis_size("batch")
    groups = b_in.shape[2] // size
    per_group = heads // groups
    part = heads // ways
    wide = per_group * width
    reach = tail_x.shape[1]
    parents_all = counts.shape[0]
    kids_all = order.shape[0]

    parent = parent_of(counts, order)
    own = lax.dynamic_slice_in_dim(parent, lax.axis_index("batch") * kids, kids)

    sent = par_state.astype(jnp.bfloat16).reshape(ways, part, width, size)
    shares = lax.all_to_all(sent, "batch", split_axis=0, concat_axis=0, tiled=True)

    tails = jnp.concatenate([tail_x.reshape(-1), tail_bc.reshape(-1)])
    tails = jnp.broadcast_to(tails[None], (ways, tails.shape[0]))
    tails = lax.all_to_all(tails, "batch", split_axis=0, concat_axis=0, tiled=True)
    tails_x = tails[:, : reach * columns].reshape(parents_all, reach, columns)
    tails_bc = tails[:, reach * columns :].reshape(parents_all, 2, reach, groups * size)

    picked = pl.pallas_call(
        pick_kernel,
        grid_spec=pltpu.PrefetchScalarGridSpec(
            num_scalar_prefetch=1,
            grid=(kids_all,),
            in_specs=[pl.BlockSpec((1, part, width, size), lambda i, p: (p[i], 0, 0, 0))],
            out_specs=pl.BlockSpec((1, part, width, size), lambda i, p: (i, 0, 0, 0)),
        ),
        out_shape=jax.ShapeDtypeStruct((kids_all, part, width, size), jnp.bfloat16),
        cost_estimate=pl.CostEstimate(
            flops=0, bytes_accessed=4 * kids_all * part * width * size, transcendentals=0
        ),
        name="pick_states",
    )(parent, shares)
    states = lax.all_to_all(
        picked.reshape(ways, kids, part, width, size), "batch", split_axis=0, concat_axis=0, tiled=True
    )

    skip_row = jnp.repeat(d_skip, width)[None, :]
    mixed, c_conv, grow = pl.pallas_call(
        within_kernel,
        grid_spec=pltpu.PrefetchScalarGridSpec(
            num_scalar_prefetch=1,
            grid=(kids, groups),
            in_specs=[
                pl.BlockSpec((1, length, wide), lambda c, q, p: (c, 0, q)),
                pl.BlockSpec((1, length, size), lambda c, q, p: (c, 0, q)),
                pl.BlockSpec((1, length, size), lambda c, q, p: (c, 0, q)),
                pl.BlockSpec((1, per_group, length), lambda c, q, p: (c, q, 0)),
                pl.BlockSpec((per_group, 1), lambda c, q, p: (q, 0)),
                pl.BlockSpec((per_group, 1), lambda c, q, p: (q, 0)),
                pl.BlockSpec((1, wide), lambda c, q, p: (0, q)),
                pl.BlockSpec((reach + 1, wide), lambda c, q, p: (0, q)),
                pl.BlockSpec((2, reach + 1, size), lambda c, q, p: (0, 0, q)),
                pl.BlockSpec((1, reach, wide), lambda c, q, p: (p[c], 0, q)),
                pl.BlockSpec((1, 2, reach, size), lambda c, q, p: (p[c], 0, 0, q)),
            ],
            out_specs=[
                pl.BlockSpec((1, length, wide), lambda c, q, p: (c, 0, q)),
                pl.BlockSpec((1, length, size), lambda c, q, p: (c, 0, q)),
                pl.BlockSpec((1, 1, length, per_group), lambda c, q, p: (c, q, 0, 0)),
            ],
            scratch_shapes=[pltpu.VMEM((8 + length, size), jnp.float32)],
        ),
        out_shape=[
            jax.ShapeDtypeStruct((kids, length, columns), jnp.float32),
            jax.ShapeDtypeStruct((kids, length, groups * size), jnp.bfloat16),
            jax.ShapeDtypeStruct((kids, groups, length, per_group), jnp.float32),
        ],
        compiler_params=pltpu.CompilerParams(vmem_limit_bytes=4 * VMEM_LIMIT),
        cost_estimate=pl.CostEstimate(
            flops=4 * kids * heads * length * length * width,
            bytes_accessed=6 * kids * length * columns,
            transcendentals=kids * heads * length * length,
        ),
        name="within",
    )(
        own,
        x_in,
        b_in,
        c_in,
        dt_in,
        dt_bias[:, None],
        a_log[:, None],
        skip_row,
        conv_x,
        conv_bc,
        tails_x,
        tails_bc,
    )

    sources = per_group // part
    return pl.pallas_call(
        carried_kernel,
        grid=(kids, groups),
        in_specs=[
            pl.BlockSpec((sources, 1, part, width, size), lambda c, q: (q, c, 0, 0, 0)),
            pl.BlockSpec((1, length, size), lambda c, q: (c, 0, q)),
            pl.BlockSpec((1, 1, length, per_group), lambda c, q: (c, q, 0, 0)),
            pl.BlockSpec((1, length, wide), lambda c, q: (c, 0, q)),
        ],
        out_specs=pl.BlockSpec((1, length, wide), lambda c, q: (c, 0, q)),
        out_shape=jax.ShapeDtypeStruct((kids, length, columns), jnp.bfloat16),
        compiler_params=pltpu.CompilerParams(vmem_limit_bytes=4 * VMEM_LIMIT),
        cost_estimate=pl.CostEstimate(
            flops=2 * kids * length * columns * size,
            bytes_accessed=8 * kids * length * columns,
            transcendentals=0,
        ),
        name="carried",
    )(states, c_conv, grow, mixed)


def local_halves(
    x_in, b_in, c_in, dt_in, dt_bias, a_log, d_skip, conv_x, conv_bc,
    par_state, tail_x, tail_bc, counts, order,
):
    kids, length, columns = x_in.shape
    heads = dt_in.shape[1]
    width, size = par_state.shape[2:]
    groups = b_in.shape[2] // size
    per_group = heads // groups
    wide = per_group * width
    taps = conv_x.shape[0]
    reach = taps - 1
    lines = (wide + 2 * size) // 128
    tail_lines = -(-lines * reach // 16) * 16
    params = pltpu.CompilerParams(vmem_limit_bytes=VMEM_LIMIT)
    anywhere = pl.BlockSpec(memory_space=pl.ANY)
    small = pl.CostEstimate(flops=1, bytes_accessed=1, transcendentals=0)

    stay = lambda x: pltpu.with_memory_space_constraint(x, pltpu.HBM)
    keep_in_vmem = lambda x: pltpu.with_memory_space_constraint(x, pltpu.VMEM)
    x_in, b_in, c_in, dt_in, conv_x, conv_bc = map(stay, (x_in, b_in, c_in, dt_in, conv_x, conv_bc))

    me = lax.axis_index("batch")
    parent = parent_of(counts, order)
    side = me // 4 * 4
    child = (jnp.arange(4 * kids, dtype=jnp.int32) // kids ^ me) * kids
    child = child + jnp.arange(4 * kids, dtype=jnp.int32) % kids
    catalog = jnp.arange(4 * 2 * kids, dtype=jnp.int32)
    owner = jnp.sum(jnp.where(child[:, None] == catalog[None, :], parent[None, :], 0), axis=1)
    here = owner // 4 * 4 == side
    slots_a = jnp.where(here, owner % 4, 4 + (owner ^ me) % 4)
    slots_b = jnp.where(here, owner % 4, 4 + owner % 4)
    place = (me % 4).astype(jnp.int32)[None]

    state = stay(par_state.reshape(groups, per_group, width, size))
    x_tails, bc_tails = stay(tail_x), stay(tail_bc.transpose(0, 2, 1, 3))
    offsets = [sum(SPLIT[:k]) for k in range(len(SPLIT))]

    def swap(value, r):
        return lax.ppermute(value, "batch", perm=[(i, i ^ r) for i in range(8)])

    def cast():
        rows = per_group * width + tail_lines
        rows_a = SPLIT[0] * width + tail_lines

        def kernel(place_ref, *refs):
            whole_ref, outs = refs[-5], refs[-4:]
            for q in range(groups):
                cast_kernel(2, [tail_lines], reach, lines, *refs[4 * q : 4 * q + 4], whole_ref.at[q])
            for j, out_ref in enumerate(outs):
                out_ref[...] = whole_ref[place_ref[0] ^ j, :rows_a]

        operands, specs = [], []
        for q in range(groups):
            operands += [state, state, x_tails, bc_tails]
            specs += [
                pl.BlockSpec((1, SPLIT[0], width, size), lambda i, p, q=q: (q, 0, 0, 0)),
                pl.BlockSpec((1, SPLIT[1], width, size), lambda i, p, q=q: (q, 1, 0, 0)),
                pl.BlockSpec((1, reach, wide), lambda i, p, q=q: (0, 0, q)),
                pl.BlockSpec((1, reach, 2, size), lambda i, p, q=q: (0, 0, 0, q)),
            ]
        return pl.pallas_call(
            kernel,
            grid_spec=pltpu.PrefetchScalarGridSpec(
                num_scalar_prefetch=1,
                grid=(1,),
                in_specs=specs,
                out_specs=[pl.BlockSpec((groups, rows, size), lambda i, p: (0, 0, 0))]
                + [pl.BlockSpec(memory_space=pltpu.VMEM)] * 4,
            ),
            out_shape=[jax.ShapeDtypeStruct((groups, rows, size), jnp.bfloat16)]
            + [pltpu.VMEM((rows_a, size), jnp.bfloat16)] * 4,
            compiler_params=params,
            cost_estimate=small,
            name="cast_states",
        )(place, *operands)

    def chunk_b(inside, tokens):
        rows = SPLIT[1] * width
        return pl.pallas_call(
            functools.partial(
                drop_tokens, functools.partial(slice_kernel, inside.shape[1] - rows), 1, len(tokens)
            ),
            grid=(1,),
            in_specs=[anywhere]
            + [anywhere] * len(tokens),
            out_specs=pl.BlockSpec(memory_space=pltpu.VMEM),
            out_shape=pltpu.VMEM((4, rows, size), jnp.bfloat16),
            scratch_shapes=[pltpu.SemaphoreType.DMA],
            compiler_params=params,
            cost_estimate=small,
            name="chunk_b",
        )(inside, *tokens)

    def gather_half(value):
        return lax.all_to_all(
            value,
            "batch",
            split_axis=0,
            concat_axis=0,
            tiled=True,
            axis_index_groups=[[0, 1, 2, 3], [4, 5, 6, 7]],
        )

    def pick(rows, start, slots, inside, crossed, tokens):
        picked = pl.pallas_call(
            functools.partial(
                drop_tokens,
                functools.partial(pick_rows_kernel, start),
                2 + len(crossed),
                len(tokens),
            ),
            grid_spec=pltpu.PrefetchScalarGridSpec(
                num_scalar_prefetch=1,
                grid=(1,),
                in_specs=[anywhere] * (1 + len(crossed) + len(tokens)),
                out_specs=[pl.BlockSpec(memory_space=pltpu.VMEM)] * 4,
                scratch_shapes=[pltpu.SemaphoreType.DMA((4, kids))],
            ),
            out_shape=[pltpu.VMEM((kids, rows, size), jnp.bfloat16)] * 4,
            compiler_params=params,
            cost_estimate=small,
            name="pick_states",
        )(slots, inside, *crossed, *tokens)
        return [picked[0]] + [swap(picked[j], j) for j in range(1, 4)]

    def early(c, tokens):
        at = lambda q: (c, 0, q)
        operands = [
            x_in, b_in, c_in, dt_in, dt_bias[:, None], a_log[:, None], skip_row, conv_x, conv_bc
        ]
        return pl.pallas_call(
            functools.partial(drop_tokens, early_kernel, len(operands), len(tokens)),
            grid=(groups,),
            in_specs=[
                pl.BlockSpec((1, length, wide), at),
                pl.BlockSpec((1, length, size), at),
                pl.BlockSpec((1, length, size), at),
                pl.BlockSpec((1, per_group, length), lambda q: (c, q, 0)),
                pl.BlockSpec((per_group, 1), lambda q: (q, 0)),
                pl.BlockSpec((per_group, 1), lambda q: (q, 0)),
                pl.BlockSpec((1, wide), lambda q: (0, q)),
                pl.BlockSpec((taps, wide), lambda q: (0, q)),
                pl.BlockSpec((2, taps, size), lambda q: (0, 0, q)),
                *[anywhere] * len(tokens),
            ],
            out_specs=[pl.BlockSpec(memory_space=pltpu.VMEM)] * 4,
            out_shape=[
                pltpu.VMEM((groups, length, wide), jnp.float32),
                pltpu.VMEM((groups, length, size), jnp.bfloat16),
                pltpu.VMEM((groups, per_group, length), jnp.float32),
                pltpu.VMEM((groups, length, per_group * FIX), jnp.float32),
            ],
            scratch_shapes=[pltpu.VMEM((8 + length, size), jnp.float32)],
            compiler_params=params,
            cost_estimate=small,
            name="early",
        )(*operands, *tokens)

    def late(k, states, states_first, parts, result, tokens):
        part, offset = SPLIT[k], offsets[k]
        chunk = part * width
        unit = offset // part
        lane = lambda q, p: (0, 0, q * (per_group // part) + unit)
        tail_at = SPLIT[0] * width // tail_lines
        in_vmem = pl.BlockSpec(memory_space=pltpu.VMEM)
        operands = [x_in, b_in, c_in, skip_row, conv_x, conv_bc, *states_first, *states]
        specs = [
            pl.BlockSpec((kids, FIX, columns), lambda q, p: (0, 0, 0)),
            pl.BlockSpec((kids, FIX, groups * size), lambda q, p: (0, 0, 0)),
            pl.BlockSpec((kids, FIX, groups * size), lambda q, p: (0, 0, 0)),
            pl.BlockSpec((1, columns), lambda q, p: (0, 0)),
            pl.BlockSpec((taps, columns), lambda q, p: (0, 0)),
            pl.BlockSpec((2, taps, groups * size), lambda q, p: (0, 0, 0)),
            *[pl.BlockSpec((kids, tail_lines, size), lambda q, p: (0, tail_at, 0))] * 4,
            *[pl.BlockSpec((kids, chunk, size), lambda q, p: (0, 0, 0))] * 4,
        ]
        for c in range(kids):
            mixed, held, column, first = parts[c]
            operands += [keep_in_vmem(a) for a in (held, column, first, mixed)]
            specs += [in_vmem] * 4
        keep = 1 + len(operands)
        operands += tokens
        specs += [anywhere] * len(tokens)
        alias = {}
        if result is not None:
            alias = {1 + len(operands): 0}
            operands.append(result)
            specs.append(anywhere)
        return pl.pallas_call(
            functools.partial(
                drop_tokens,
                functools.partial(late_kernel, offset, lines),
                keep,
                1 + len(operands) - keep,
            ),
            grid_spec=pltpu.PrefetchScalarGridSpec(
                num_scalar_prefetch=1,
                grid=(groups,),
                in_specs=specs,
                out_specs=pl.BlockSpec((kids, length, chunk), lane),
                scratch_shapes=[pltpu.VMEM((8 + FIX, size), jnp.float32)],
            ),
            out_shape=jax.ShapeDtypeStruct(x_in.shape, jnp.bfloat16),
            input_output_aliases=alias,
            compiler_params=params,
            cost_estimate=small,
            name="late",
        )(place, *operands)

    skip_row = jnp.repeat(d_skip, width)[None, :]
    rows = [SPLIT[0] * width + tail_lines, SPLIT[1] * width]
    whole, *sent_a = cast()
    crossed_a = [swap(sent_a[j], j + 4) for j in range(4)]
    inside = gather_half(whole)
    parts = [early(0, [whole])]
    sent_b = chunk_b(inside, [parts[0][1]])
    crossed_b = swap(sent_b, 4)
    states_a = pick(rows[0], 0, slots_a, inside, crossed_a, [sent_b])
    parts.append(early(1, [states_a[0]]))
    states_b = pick(rows[1], rows[0], slots_b, inside, [crossed_b], [parts[1][1]])
    result = late(0, states_a, states_a, parts, None, [states_b[0]])
    return late(1, states_b, states_a, parts, result, [])


def solution(mesh):
    rows, cols = P(("groups", "batch"), None, "head"), P(("groups", "batch"), "head")
    placed = (
        rows, rows, rows, cols, P("head"), P("head"), P("head"), P(None, "head"),
        P(None, None, "head"), cols, rows, P(("groups", "batch"), None, None, "head"),
        P("groups"), P("groups"),
    )
    local = local_halves if mesh.shape["batch"] == 8 else local_any
    return jax.shard_map(local, mesh=mesh, in_specs=placed, out_specs=rows, check_vma=False)
```

```python
import functools

import jax
import jax.numpy as jnp
from jax import lax
from jax.experimental import pallas as pl
from jax.experimental.pallas import tpu as pltpu
from jax.sharding import PartitionSpec as P

VMEM_LIMIT = 16 * 1024 * 1024
SPLIT = (8, 8)
FIX = 16
LOG2_E = 1.4426950408889634


def drop_tokens(kernel, keep, tokens, *refs):
    kernel(*refs[:keep], *refs[keep + tokens :])


def parent_of(counts, order):
    index = jnp.arange(counts.shape[0], dtype=jnp.int32)
    bounds = jnp.sum(jnp.where(index[None, :] <= index[:, None], counts[None, :], 0), axis=1)
    return jnp.sum((bounds[None, :] <= order[:, None]).astype(jnp.int32), axis=1)


def conv_silu(padded, tail, rows, taps):
    length = rows.shape[0]
    reach = taps.shape[0] - 1
    padded[8 - reach : 8, :] = jnp.broadcast_to(tail, (reach, rows.shape[1])).astype(jnp.float32)
    padded[8 : 8 + length, :] = rows.astype(jnp.float32)
    total = padded[8 - reach : 8 - reach + length, :] * taps[0:1, :]
    for k in range(1, reach + 1):
        total = total + padded[8 - reach + k : 8 - reach + k + length, :] * taps[k : k + 1, :]
    half = 0.5 * total
    return (half + half * jnp.tanh(half)).astype(jnp.bfloat16)


def early_kernel(
    x_ref, b_ref, c_ref, dt_ref, bias_ref, alog_ref, skip_ref, taps_x_ref, taps_bc_ref,
    mixed_ref, c_out_ref, column_ref, first_ref, padded,
):
    length, wide = x_ref.shape[1:]
    heads = dt_ref.shape[1]
    q = pl.program_id(0)
    width = wide // heads
    half = length // 2

    def convolve(rows, taps):
        bulk = conv_silu(padded, 0.0, rows, taps)[FIX:]
        return jnp.concatenate([jnp.zeros((FIX, rows.shape[1]), jnp.bfloat16), bulk])

    b_conv = convolve(b_ref[0], taps_bc_ref[0])
    c_conv = convolve(c_ref[0], taps_bc_ref[1])
    c_out_ref[q] = c_conv
    scores = lax.dot_general(
        c_conv, b_conv, (((1,), (1,)), ((), ())), preferred_element_type=jnp.float32
    )
    raw = dt_ref[0] + bias_ref[...]
    step = jnp.maximum(raw, 0.0) + jnp.log1p(jnp.exp(-jnp.abs(raw)))
    per_token = step * (-jnp.exp(alog_ref[...]))
    upper = lax.broadcasted_iota(jnp.int32, (length, length), 0) <= lax.broadcasted_iota(
        jnp.int32, (length, length), 1
    )
    total = lax.dot_general(
        per_token,
        upper.astype(jnp.float32),
        (((1,), (0,)), ((), ())),
        precision=lax.Precision.HIGHEST,
        preferred_element_type=jnp.float32,
    )
    total = total * LOG2_E
    row = total - jnp.log(step) * LOG2_E
    columns = total.T
    column_ref[q] = total
    causal = lax.broadcasted_iota(jnp.int32, (half, half), 0) >= lax.broadcasted_iota(
        jnp.int32, (half, half), 1
    )
    low = lax.broadcasted_iota(jnp.int32, (length, 2 * width), 1) < width
    for pair in range(heads // 2):
        lanes = slice(pair * 2 * width, (pair + 1) * 2 * width)
        x_conv = convolve(x_ref[0, :, lanes], taps_x_ref[:, lanes])
        parts = []
        for head in (2 * pair, 2 * pair + 1):
            column = jnp.broadcast_to(columns[:, head : head + 1], (length, half))
            rows = row[head : head + 1, :]
            near = jnp.exp2(jnp.where(causal, column[:half] - rows[:, :half], -1e30))
            far = jnp.exp2(column[half:] - rows[:, :half])
            last = jnp.exp2(jnp.where(causal, column[half:] - rows[:, half:], -1e30))
            spot = slice(head * FIX, (head + 1) * FIX)
            first_ref[q, :half, spot] = near[:, :FIX]
            first_ref[q, half:, spot] = far[:, :FIX]
            top = (scores[:half, :half] * near).astype(jnp.bfloat16)
            left = (scores[half:, :half] * far).astype(jnp.bfloat16)
            right = (scores[half:, half:] * last).astype(jnp.bfloat16)
            below = jnp.concatenate([left, right], axis=1)
            parts.append(
                jnp.concatenate(
                    [
                        jnp.dot(top, x_conv[:half], preferred_element_type=jnp.float32),
                        jnp.dot(below, x_conv, preferred_element_type=jnp.float32),
                    ]
                )
            )
        mixed_ref[q, :, lanes] = jnp.where(low, parts[0], parts[1]) + skip_ref[
            :, lanes
        ] * x_conv.astype(jnp.float32)


def late_kernel(
    offset, lines, place_ref, x_ref, b_ref, c_ref, skip_ref, taps_x_ref, taps_bc_ref, *refs
):
    tails, states, parts, (y_ref, padded) = refs[:4], refs[4:8], refs[8:-2], refs[-2:]
    kids, length, wide = y_ref.shape
    width = 64
    heads = wide // width
    reach = taps_x_ref.shape[0] - 1
    q = pl.program_id(0)
    far = q ^ place_ref[0]
    size = c_ref.shape[2] // pl.num_programs(0)
    stride = skip_ref.shape[1] // pl.num_programs(0)
    group_lanes = pl.ds(pl.multiple_of(q * size, 128), size)
    low_first = lax.broadcasted_iota(jnp.int32, (FIX, 2 * width), 1) < width
    spread_row = lax.broadcasted_iota(jnp.int32, (4 * heads, wide), 0)
    spread_lane = lax.broadcasted_iota(jnp.int32, (4 * heads, wide), 1)
    spread = (spread_row % heads == spread_lane // width).astype(jnp.bfloat16)
    contract = (((1,), (1,)), ((), ()))

    def choose(blocks):
        near = jnp.where(far == 0, blocks[0], blocks[1])
        return jnp.where(far <= 1, near, jnp.where(far == 2, blocks[2], blocks[3]))

    for kid in range(kids):
        held_ref, column_ref, first_ref, mixed_ref = parts[4 * kid : 4 * kid + 4]
        tail = choose([ref[kid] for ref in tails]).astype(jnp.float32)
        state = choose([ref[kid] for ref in states])

        def opening(rows, taps, at):
            tap_rows = [tail[k * lines + at : k * lines + at + 1] for k in range(reach)]
            return conv_silu(padded, jnp.concatenate(tap_rows), rows, taps)

        b_first = opening(b_ref[kid, :, group_lanes], taps_bc_ref[0, :, group_lanes], lines - 2)
        c_first = opening(c_ref[kid, :, group_lanes], taps_bc_ref[1, :, group_lanes], lines - 1)
        c_conv = jnp.concatenate([c_first, held_ref[q, FIX:]])
        grow = jnp.exp2(column_ref[q, offset : offset + heads, :])
        terms = []
        for _ in range(3):
            terms.append(grow.astype(jnp.bfloat16).astype(jnp.float32))
            grow = grow - terms[-1]
        terms = jnp.concatenate(terms + [jnp.zeros_like(grow)]).T.astype(jnp.bfloat16)
        grow = jnp.dot(terms, spread, preferred_element_type=jnp.float32)
        term = lax.dot_general(c_conv, state, contract, preferred_element_type=jnp.float32)
        carried = (term * grow).astype(jnp.bfloat16)
        scores = lax.dot_general(
            c_conv,
            jnp.concatenate([b_first] * heads),
            contract,
            preferred_element_type=jnp.float32,
        )
        unit = offset // heads * heads * FIX
        mixing = (scores * first_ref[q, :, unit : unit + heads * FIX]).astype(jnp.bfloat16)
        for pair in range(heads // 2):
            lanes = slice(pair * 2 * width, (pair + 1) * 2 * width)
            start = pl.multiple_of(q * stride + (offset + 2 * pair) * width, 128)
            whole = pl.ds(start, 2 * width)
            x_first = opening(
                x_ref[kid, :, whole], taps_x_ref[:, whole], offset * width // 128 + pair
            ).astype(jnp.float32)
            stacked = [jnp.where(low_first, x_first, 0.0), jnp.where(low_first, 0.0, x_first)]
            if pair > 0:
                stacked = [jnp.zeros((2 * pair * FIX, 2 * width), jnp.float32)] + stacked
            if 2 * pair + 2 < heads:
                spare = (heads - 2 * pair - 2) * FIX
                stacked = stacked + [jnp.zeros((spare, 2 * width), jnp.float32)]
            part = jnp.dot(
                mixing,
                jnp.concatenate(stacked).astype(jnp.bfloat16),
                preferred_element_type=jnp.float32,
            )
            part = jnp.concatenate([part[:FIX] + skip_ref[:, whole] * x_first, part[FIX:]])
            here = slice(offset * width + lanes.start, offset * width + lanes.stop)
            y_ref[kid, :, lanes] = (
                mixed_ref[q, :, here] + part + carried[:, lanes].astype(jnp.float32)
            ).astype(jnp.bfloat16)


def cast_kernel(parts, tailed, reach, lines, *refs):
    count = len(tailed)
    ins, outs = refs[:-count], refs[-count:]
    states, tails = ins[: parts * count], ins[parts * count :]
    for j, out_ref in enumerate(outs):
        start = 0
        for at in range(parts):
            state = states[parts * j + at][0]
            rows = state.shape[0] * state.shape[1]
            out_ref[start : start + rows] = state.reshape(rows, state.shape[2]).astype(jnp.bfloat16)
            start += rows
            if at == 0 and tailed[j]:
                x_tail = tails[2 * j][0].astype(jnp.float32)
                bc_tail = tails[2 * j + 1][0].astype(jnp.float32)
                pieces = []
                for k in range(reach):
                    pieces += [x_tail[k : k + 1, i * 128 : i * 128 + 128] for i in range(lines - 2)]
                    pieces.append(bc_tail[k])
                spare = tailed[j] - lines * reach
                pieces.append(jnp.zeros((spare, 128), jnp.float32))
                out_ref[start : start + tailed[j]] = jnp.concatenate(pieces).astype(jnp.bfloat16)
                start += tailed[j]


def pick_rows_kernel(start, slots_ref, inside_ref, *refs):
    crossed, outs, sems = refs[:-5], refs[-5:-1], refs[-1]
    kids, rows = outs[0].shape[:2]
    held = [inside_ref.at[source, pl.ds(start, rows)] for source in range(4)]
    held += list(crossed) if len(crossed) == 4 else [crossed[0].at[source] for source in range(4)]
    for j, out in enumerate(outs):
        for kid in range(kids):
            for source in range(8):

                @pl.when(slots_ref[j * kids + kid] == source)
                def _(source=source, out=out, j=j, kid=kid):
                    pltpu.make_async_copy(held[source], out.at[kid], sems.at[j, kid]).start()

    for j, out in enumerate(outs):
        for kid in range(kids):
            pltpu.make_async_copy(held[0], out.at[kid], sems.at[j, kid]).wait()


def slice_kernel(start, in_ref, out_ref, sem):
    copy = pltpu.make_async_copy(in_ref.at[:, pl.ds(start, out_ref.shape[1])], out_ref, sem)
    copy.start()
    copy.wait()


def within_kernel(
    parent_ref,
    x_ref,
    b_ref,
    c_ref,
    dt_ref,
    bias_ref,
    alog_ref,
    skip_ref,
    taps_x_ref,
    taps_bc_ref,
    tail_x_ref,
    tail_bc_ref,
    mixed_ref,
    c_out_ref,
    grow_ref,
    padded,
):
    length = x_ref.shape[1]
    heads = dt_ref.shape[1]
    width = x_ref.shape[2] // heads
    b_conv = conv_silu(padded, tail_bc_ref[0, 0], b_ref[0], taps_bc_ref[0])
    c_conv = conv_silu(padded, tail_bc_ref[0, 1], c_ref[0], taps_bc_ref[1])
    c_out_ref[0] = c_conv
    scores = lax.dot_general(
        c_conv, b_conv, (((1,), (1,)), ((), ())), preferred_element_type=jnp.float32
    )
    raw = dt_ref[0] + bias_ref[...]
    step = jnp.maximum(raw, 0.0) + jnp.log1p(jnp.exp(-jnp.abs(raw)))
    per_token = step * (-jnp.exp(alog_ref[...]))
    row = lax.broadcasted_iota(jnp.int32, (length, length), 0)
    col = lax.broadcasted_iota(jnp.int32, (length, length), 1)
    upper = (row <= col).astype(jnp.float32)
    total = lax.dot_general(
        per_token,
        upper,
        (((1,), (0,)), ((), ())),
        precision=lax.Precision.HIGHEST,
        preferred_element_type=jnp.float32,
    )
    total_t = total.T
    grow_ref[0, 0] = jnp.exp(total_t)
    causal = row >= col
    low = lax.broadcasted_iota(jnp.int32, (length, 2 * width), 1) < width
    for pair in range(heads // 2):
        lanes = slice(pair * 2 * width, (pair + 1) * 2 * width)
        x_conv = conv_silu(
            padded, tail_x_ref[0, :, lanes], x_ref[0, :, lanes], taps_x_ref[:, lanes]
        )
        parts = []
        for head in (2 * pair, 2 * pair + 1):
            gap = total_t[:, head : head + 1] - total[head : head + 1, :]
            factor = jnp.exp(jnp.where(causal, gap, -1e30))
            mixing = (scores * factor * step[head : head + 1, :]).astype(jnp.bfloat16)
            parts.append(jnp.dot(mixing, x_conv, preferred_element_type=jnp.float32))
        mixed_ref[0, :, lanes] = (
            jnp.where(low, parts[0], parts[1]) + skip_ref[:, lanes] * x_conv.astype(jnp.float32)
        )


def carried_kernel(state_ref, c_ref, grow_ref, mixed_ref, y_ref):
    sources, _, part, width, size = state_ref.shape
    length = c_ref.shape[1]
    low = lax.broadcasted_iota(jnp.int32, (length, 2 * width), 1) < width
    c_conv = c_ref[0]
    for source in range(sources):
        state = state_ref[source, 0].reshape(part * width, size)
        term = lax.dot_general(
            c_conv, state, (((1,), (1,)), ((), ())), preferred_element_type=jnp.float32
        )
        for pair in range(part // 2):
            head = source * part + 2 * pair
            grow = jnp.where(
                low, grow_ref[0, 0, :, head : head + 1], grow_ref[0, 0, :, head + 1 : head + 2]
            )
            here = slice(2 * pair * width, (2 * pair + 2) * width)
            lanes = slice(head * width, (head + 2) * width)
            carried = (term[:, here] * grow).astype(jnp.bfloat16).astype(jnp.float32)
            y_ref[0, :, lanes] = (mixed_ref[0, :, lanes] + carried).astype(jnp.bfloat16)


def pick_kernel(parent_ref, state_ref, out_ref):
    out_ref[...] = state_ref[...]


def local_any(
    x_in,
    b_in,
    c_in,
    dt_in,
    dt_bias,
    a_log,
    d_skip,
    conv_x,
    conv_bc,
    par_state,
    tail_x,
    tail_bc,
    counts,
    order,
):
    kids, length, columns = x_in.shape
    heads = dt_in.shape[1]
    width, size = par_state.shape[2:]
    ways = lax.axis_size("batch")
    groups = b_in.shape[2] // size
    per_group = heads // groups
    part = heads // ways
    wide = per_group * width
    reach = tail_x.shape[1]
    parents_all = counts.shape[0]
    kids_all = order.shape[0]

    parent = parent_of(counts, order)
    own = lax.dynamic_slice_in_dim(parent, lax.axis_index("batch") * kids, kids)

    sent = par_state.astype(jnp.bfloat16).reshape(ways, part, width, size)
    shares = lax.all_to_all(sent, "batch", split_axis=0, concat_axis=0, tiled=True)

    tails = jnp.concatenate([tail_x.reshape(-1), tail_bc.reshape(-1)])
    tails = jnp.broadcast_to(tails[None], (ways, tails.shape[0]))
    tails = lax.all_to_all(tails, "batch", split_axis=0, concat_axis=0, tiled=True)
    tails_x = tails[:, : reach * columns].reshape(parents_all, reach, columns)
    tails_bc = tails[:, reach * columns :].reshape(parents_all, 2, reach, groups * size)

    picked = pl.pallas_call(
        pick_kernel,
        grid_spec=pltpu.PrefetchScalarGridSpec(
            num_scalar_prefetch=1,
            grid=(kids_all,),
            in_specs=[pl.BlockSpec((1, part, width, size), lambda i, p: (p[i], 0, 0, 0))],
            out_specs=pl.BlockSpec((1, part, width, size), lambda i, p: (i, 0, 0, 0)),
        ),
        out_shape=jax.ShapeDtypeStruct((kids_all, part, width, size), jnp.bfloat16),
        cost_estimate=pl.CostEstimate(
            flops=0, bytes_accessed=4 * kids_all * part * width * size, transcendentals=0
        ),
        name="pick_states",
    )(parent, shares)
    states = lax.all_to_all(
        picked.reshape(ways, kids, part, width, size), "batch", split_axis=0, concat_axis=0, tiled=True
    )

    skip_row = jnp.repeat(d_skip, width)[None, :]
    mixed, c_conv, grow = pl.pallas_call(
        within_kernel,
        grid_spec=pltpu.PrefetchScalarGridSpec(
            num_scalar_prefetch=1,
            grid=(kids, groups),
            in_specs=[
                pl.BlockSpec((1, length, wide), lambda c, q, p: (c, 0, q)),
                pl.BlockSpec((1, length, size), lambda c, q, p: (c, 0, q)),
                pl.BlockSpec((1, length, size), lambda c, q, p: (c, 0, q)),
                pl.BlockSpec((1, per_group, length), lambda c, q, p: (c, q, 0)),
                pl.BlockSpec((per_group, 1), lambda c, q, p: (q, 0)),
                pl.BlockSpec((per_group, 1), lambda c, q, p: (q, 0)),
                pl.BlockSpec((1, wide), lambda c, q, p: (0, q)),
                pl.BlockSpec((reach + 1, wide), lambda c, q, p: (0, q)),
                pl.BlockSpec((2, reach + 1, size), lambda c, q, p: (0, 0, q)),
                pl.BlockSpec((1, reach, wide), lambda c, q, p: (p[c], 0, q)),
                pl.BlockSpec((1, 2, reach, size), lambda c, q, p: (p[c], 0, 0, q)),
            ],
            out_specs=[
                pl.BlockSpec((1, length, wide), lambda c, q, p: (c, 0, q)),
                pl.BlockSpec((1, length, size), lambda c, q, p: (c, 0, q)),
                pl.BlockSpec((1, 1, length, per_group), lambda c, q, p: (c, q, 0, 0)),
            ],
            scratch_shapes=[pltpu.VMEM((8 + length, size), jnp.float32)],
        ),
        out_shape=[
            jax.ShapeDtypeStruct((kids, length, columns), jnp.float32),
            jax.ShapeDtypeStruct((kids, length, groups * size), jnp.bfloat16),
            jax.ShapeDtypeStruct((kids, groups, length, per_group), jnp.float32),
        ],
        compiler_params=pltpu.CompilerParams(vmem_limit_bytes=4 * VMEM_LIMIT),
        cost_estimate=pl.CostEstimate(
            flops=4 * kids * heads * length * length * width,
            bytes_accessed=6 * kids * length * columns,
            transcendentals=kids * heads * length * length,
        ),
        name="within",
    )(
        own,
        x_in,
        b_in,
        c_in,
        dt_in,
        dt_bias[:, None],
        a_log[:, None],
        skip_row,
        conv_x,
        conv_bc,
        tails_x,
        tails_bc,
    )

    sources = per_group // part
    return pl.pallas_call(
        carried_kernel,
        grid=(kids, groups),
        in_specs=[
            pl.BlockSpec((sources, 1, part, width, size), lambda c, q: (q, c, 0, 0, 0)),
            pl.BlockSpec((1, length, size), lambda c, q: (c, 0, q)),
            pl.BlockSpec((1, 1, length, per_group), lambda c, q: (c, q, 0, 0)),
            pl.BlockSpec((1, length, wide), lambda c, q: (c, 0, q)),
        ],
        out_specs=pl.BlockSpec((1, length, wide), lambda c, q: (c, 0, q)),
        out_shape=jax.ShapeDtypeStruct((kids, length, columns), jnp.bfloat16),
        compiler_params=pltpu.CompilerParams(vmem_limit_bytes=4 * VMEM_LIMIT),
        cost_estimate=pl.CostEstimate(
            flops=2 * kids * length * columns * size,
            bytes_accessed=8 * kids * length * columns,
            transcendentals=0,
        ),
        name="carried",
    )(states, c_conv, grow, mixed)


def local_halves(
    x_in, b_in, c_in, dt_in, dt_bias, a_log, d_skip, conv_x, conv_bc,
    par_state, tail_x, tail_bc, counts, order,
):
    kids, length, columns = x_in.shape
    heads = dt_in.shape[1]
    width, size = par_state.shape[2:]
    groups = b_in.shape[2] // size
    per_group = heads // groups
    wide = per_group * width
    taps = conv_x.shape[0]
    reach = taps - 1
    lines = (wide + 2 * size) // 128
    tail_lines = -(-lines * reach // 16) * 16
    params = pltpu.CompilerParams(vmem_limit_bytes=VMEM_LIMIT)
    anywhere = pl.BlockSpec(memory_space=pl.ANY)
    small = pl.CostEstimate(flops=1, bytes_accessed=1, transcendentals=0)

    stay = lambda x: pltpu.with_memory_space_constraint(x, pltpu.HBM)
    keep_in_vmem = lambda x: pltpu.with_memory_space_constraint(x, pltpu.VMEM)
    x_in, b_in, c_in, dt_in, conv_x, conv_bc = map(stay, (x_in, b_in, c_in, dt_in, conv_x, conv_bc))

    me = lax.axis_index("batch")
    parent = parent_of(counts, order)
    side = me // 4 * 4
    child = (jnp.arange(4 * kids, dtype=jnp.int32) // kids ^ me) * kids
    child = child + jnp.arange(4 * kids, dtype=jnp.int32) % kids
    catalog = jnp.arange(4 * 2 * kids, dtype=jnp.int32)
    owner = jnp.sum(jnp.where(child[:, None] == catalog[None, :], parent[None, :], 0), axis=1)
    here = owner // 4 * 4 == side
    slots_a = jnp.where(here, owner % 4, 4 + (owner ^ me) % 4)
    slots_b = jnp.where(here, owner % 4, 4 + owner % 4)
    place = (me % 4).astype(jnp.int32)[None]

    state = stay(par_state.reshape(groups, per_group, width, size))
    x_tails, bc_tails = stay(tail_x), stay(tail_bc.transpose(0, 2, 1, 3))
    offsets = [sum(SPLIT[:k]) for k in range(len(SPLIT))]

    def swap(value, r):
        return lax.ppermute(value, "batch", perm=[(i, i ^ r) for i in range(8)])

    def cast():
        rows = per_group * width + tail_lines
        rows_a = SPLIT[0] * width + tail_lines

        def kernel(place_ref, *refs):
            whole_ref, outs = refs[-5], refs[-4:]
            for q in range(groups):
                cast_kernel(2, [tail_lines], reach, lines, *refs[4 * q : 4 * q + 4], whole_ref.at[q])
            for j, out_ref in enumerate(outs):
                out_ref[...] = whole_ref[place_ref[0] ^ j, :rows_a]

        operands, specs = [], []
        for q in range(groups):
            operands += [state, state, x_tails, bc_tails]
            specs += [
                pl.BlockSpec((1, SPLIT[0], width, size), lambda i, p, q=q: (q, 0, 0, 0)),
                pl.BlockSpec((1, SPLIT[1], width, size), lambda i, p, q=q: (q, 1, 0, 0)),
                pl.BlockSpec((1, reach, wide), lambda i, p, q=q: (0, 0, q)),
                pl.BlockSpec((1, reach, 2, size), lambda i, p, q=q: (0, 0, 0, q)),
            ]
        return pl.pallas_call(
            kernel,
            grid_spec=pltpu.PrefetchScalarGridSpec(
                num_scalar_prefetch=1,
                grid=(1,),
                in_specs=specs,
                out_specs=[pl.BlockSpec((groups, rows, size), lambda i, p: (0, 0, 0))]
                + [pl.BlockSpec(memory_space=pltpu.VMEM)] * 4,
            ),
            out_shape=[jax.ShapeDtypeStruct((groups, rows, size), jnp.bfloat16)]
            + [pltpu.VMEM((rows_a, size), jnp.bfloat16)] * 4,
            compiler_params=params,
            cost_estimate=small,
            name="cast_states",
        )(place, *operands)

    def chunk_b(inside, tokens):
        rows = SPLIT[1] * width
        return pl.pallas_call(
            functools.partial(
                drop_tokens, functools.partial(slice_kernel, inside.shape[1] - rows), 1, len(tokens)
            ),
            grid=(1,),
            in_specs=[anywhere]
            + [anywhere] * len(tokens),
            out_specs=pl.BlockSpec(memory_space=pltpu.VMEM),
            out_shape=pltpu.VMEM((4, rows, size), jnp.bfloat16),
            scratch_shapes=[pltpu.SemaphoreType.DMA],
            compiler_params=params,
            cost_estimate=small,
            name="chunk_b",
        )(inside, *tokens)

    def gather_half(value):
        return lax.all_to_all(
            value,
            "batch",
            split_axis=0,
            concat_axis=0,
            tiled=True,
            axis_index_groups=[[0, 1, 2, 3], [4, 5, 6, 7]],
        )

    def pick(rows, start, slots, inside, crossed, tokens):
        picked = pl.pallas_call(
            functools.partial(
                drop_tokens,
                functools.partial(pick_rows_kernel, start),
                2 + len(crossed),
                len(tokens),
            ),
            grid_spec=pltpu.PrefetchScalarGridSpec(
                num_scalar_prefetch=1,
                grid=(1,),
                in_specs=[anywhere] * (1 + len(crossed) + len(tokens)),
                out_specs=[pl.BlockSpec(memory_space=pltpu.VMEM)] * 4,
                scratch_shapes=[pltpu.SemaphoreType.DMA((4, kids))],
            ),
            out_shape=[pltpu.VMEM((kids, rows, size), jnp.bfloat16)] * 4,
            compiler_params=params,
            cost_estimate=small,
            name="pick_states",
        )(slots, inside, *crossed, *tokens)
        return [picked[0]] + [swap(picked[j], j) for j in range(1, 4)]

    def early(c, tokens):
        at = lambda q: (c, 0, q)
        operands = [
            x_in, b_in, c_in, dt_in, dt_bias[:, None], a_log[:, None], skip_row, conv_x, conv_bc
        ]
        return pl.pallas_call(
            functools.partial(drop_tokens, early_kernel, len(operands), len(tokens)),
            grid=(groups,),
            in_specs=[
                pl.BlockSpec((1, length, wide), at),
                pl.BlockSpec((1, length, size), at),
                pl.BlockSpec((1, length, size), at),
                pl.BlockSpec((1, per_group, length), lambda q: (c, q, 0)),
                pl.BlockSpec((per_group, 1), lambda q: (q, 0)),
                pl.BlockSpec((per_group, 1), lambda q: (q, 0)),
                pl.BlockSpec((1, wide), lambda q: (0, q)),
                pl.BlockSpec((taps, wide), lambda q: (0, q)),
                pl.BlockSpec((2, taps, size), lambda q: (0, 0, q)),
                *[anywhere] * len(tokens),
            ],
            out_specs=[pl.BlockSpec(memory_space=pltpu.VMEM)] * 4,
            out_shape=[
                pltpu.VMEM((groups, length, wide), jnp.float32),
                pltpu.VMEM((groups, length, size), jnp.bfloat16),
                pltpu.VMEM((groups, per_group, length), jnp.float32),
                pltpu.VMEM((groups, length, per_group * FIX), jnp.float32),
            ],
            scratch_shapes=[pltpu.VMEM((8 + length, size), jnp.float32)],
            compiler_params=params,
            cost_estimate=small,
            name="early",
        )(*operands, *tokens)

    def late(k, states, states_first, parts, result, tokens):
        part, offset = SPLIT[k], offsets[k]
        chunk = part * width
        unit = offset // part
        lane = lambda q, p: (0, 0, q * (per_group // part) + unit)
        tail_at = SPLIT[0] * width // tail_lines
        in_vmem = pl.BlockSpec(memory_space=pltpu.VMEM)
        operands = [x_in, b_in, c_in, skip_row, conv_x, conv_bc, *states_first, *states]
        specs = [
            pl.BlockSpec((kids, FIX, columns), lambda q, p: (0, 0, 0)),
            pl.BlockSpec((kids, FIX, groups * size), lambda q, p: (0, 0, 0)),
            pl.BlockSpec((kids, FIX, groups * size), lambda q, p: (0, 0, 0)),
            pl.BlockSpec((1, columns), lambda q, p: (0, 0)),
            pl.BlockSpec((taps, columns), lambda q, p: (0, 0)),
            pl.BlockSpec((2, taps, groups * size), lambda q, p: (0, 0, 0)),
            *[pl.BlockSpec((kids, tail_lines, size), lambda q, p: (0, tail_at, 0))] * 4,
            *[pl.BlockSpec((kids, chunk, size), lambda q, p: (0, 0, 0))] * 4,
        ]
        for c in range(kids):
            mixed, held, column, first = parts[c]
            operands += [keep_in_vmem(a) for a in (held, column, first, mixed)]
            specs += [in_vmem] * 4
        keep = 1 + len(operands)
        operands += tokens
        specs += [anywhere] * len(tokens)
        alias = {}
        if result is not None:
            alias = {1 + len(operands): 0}
            operands.append(result)
            specs.append(anywhere)
        return pl.pallas_call(
            functools.partial(
                drop_tokens,
                functools.partial(late_kernel, offset, lines),
                keep,
                1 + len(operands) - keep,
            ),
            grid_spec=pltpu.PrefetchScalarGridSpec(
                num_scalar_prefetch=1,
                grid=(groups,),
                in_specs=specs,
                out_specs=pl.BlockSpec((kids, length, chunk), lane),
                scratch_shapes=[pltpu.VMEM((8 + FIX, size), jnp.float32)],
            ),
            out_shape=jax.ShapeDtypeStruct(x_in.shape, jnp.bfloat16),
            input_output_aliases=alias,
            compiler_params=params,
            cost_estimate=small,
            name="late",
        )(place, *operands)

    skip_row = jnp.repeat(d_skip, width)[None, :]
    rows = [SPLIT[0] * width + tail_lines, SPLIT[1] * width]
    whole, *sent_a = cast()
    crossed_a = [swap(sent_a[j], j + 4) for j in range(4)]
    inside = gather_half(whole)
    parts = [early(0, [whole, slots_a, slots_b])]
    sent_b = chunk_b(inside, [parts[0][1], *crossed_a])
    crossed_b = swap(sent_b, 4)
    states_a = pick(rows[0], 0, slots_a, inside, crossed_a, [sent_b])
    parts.append(early(1, [states_a[0]]))
    states_b = pick(rows[1], rows[0], slots_b, inside, [crossed_b], [parts[1][1]])
    result = late(0, states_a, states_a, parts, None, [states_b[0]])
    return late(1, states_b, states_a, parts, result, [])


def solution(mesh):
    rows, cols = P(("groups", "batch"), None, "head"), P(("groups", "batch"), "head")
    placed = (
        rows, rows, rows, cols, P("head"), P("head"), P("head"), P(None, "head"),
        P(None, None, "head"), cols, rows, P(("groups", "batch"), None, None, "head"),
        P("groups"), P("groups"),
    )
    local = local_halves if mesh.shape["batch"] == 8 else local_any
    return jax.shard_map(local, mesh=mesh, in_specs=placed, out_specs=rows, check_vma=False)
```

```python
import functools

import jax
import jax.numpy as jnp
from jax import lax
from jax.experimental import pallas as pl
from jax.experimental.pallas import tpu as pltpu
from jax.sharding import PartitionSpec as P

VMEM_LIMIT = 12 * 1024 * 1024
SPLIT = (8, 8)
FIX = 16
LOG2_E = 1.4426950408889634


def drop_tokens(kernel, keep, tokens, *refs):
    kernel(*refs[:keep], *refs[keep + tokens :])


def parent_of(counts, order):
    index = jnp.arange(counts.shape[0], dtype=jnp.int32)
    bounds = jnp.sum(jnp.where(index[None, :] <= index[:, None], counts[None, :], 0), axis=1)
    return jnp.sum((bounds[None, :] <= order[:, None]).astype(jnp.int32), axis=1)


def conv_silu(padded, tail, rows, taps):
    length = rows.shape[0]
    reach = taps.shape[0] - 1
    padded[8 - reach : 8, :] = jnp.broadcast_to(tail, (reach, rows.shape[1])).astype(jnp.float32)
    padded[8 : 8 + length, :] = rows.astype(jnp.float32)
    total = padded[8 - reach : 8 - reach + length, :] * taps[0:1, :]
    for k in range(1, reach + 1):
        total = total + padded[8 - reach + k : 8 - reach + k + length, :] * taps[k : k + 1, :]
    half = 0.5 * total
    return (half + half * jnp.tanh(half)).astype(jnp.bfloat16)


def early_kernel(
    base, x_ref, b_ref, c_ref, dt_ref, bias_ref, alog_ref, skip_ref, taps_x_ref, taps_bc_ref,
    mixed_ref, c_out_ref, column_ref, first_ref, padded,
):
    length, wide = x_ref.shape[1:]
    heads = dt_ref.shape[1]
    q = base + pl.program_id(0)
    width = wide // heads
    half = length // 2

    def convolve(rows, taps):
        bulk = conv_silu(padded, 0.0, rows, taps)[FIX:]
        return jnp.concatenate([jnp.zeros((FIX, rows.shape[1]), jnp.bfloat16), bulk])

    b_conv = convolve(b_ref[0], taps_bc_ref[0])
    c_conv = convolve(c_ref[0], taps_bc_ref[1])
    c_out_ref[q] = c_conv
    scores = lax.dot_general(
        c_conv, b_conv, (((1,), (1,)), ((), ())), preferred_element_type=jnp.float32
    )
    raw = dt_ref[0] + bias_ref[...]
    step = jnp.maximum(raw, 0.0) + jnp.log1p(jnp.exp(-jnp.abs(raw)))
    per_token = step * (-jnp.exp(alog_ref[...]))
    upper = lax.broadcasted_iota(jnp.int32, (length, length), 0) <= lax.broadcasted_iota(
        jnp.int32, (length, length), 1
    )
    total = lax.dot_general(
        per_token,
        upper.astype(jnp.float32),
        (((1,), (0,)), ((), ())),
        precision=lax.Precision.HIGHEST,
        preferred_element_type=jnp.float32,
    )
    total = total * LOG2_E
    row = total - jnp.log(step) * LOG2_E
    columns = total.T
    column_ref[q] = total
    causal = lax.broadcasted_iota(jnp.int32, (half, half), 0) >= lax.broadcasted_iota(
        jnp.int32, (half, half), 1
    )
    low = lax.broadcasted_iota(jnp.int32, (length, 2 * width), 1) < width
    for pair in range(heads // 2):
        lanes = slice(pair * 2 * width, (pair + 1) * 2 * width)
        x_conv = convolve(x_ref[0, :, lanes], taps_x_ref[:, lanes])
        parts = []
        for head in (2 * pair, 2 * pair + 1):
            column = jnp.broadcast_to(columns[:, head : head + 1], (length, half))
            rows = row[head : head + 1, :]
            near = jnp.exp2(jnp.where(causal, column[:half] - rows[:, :half], -1e30))
            far = jnp.exp2(column[half:] - rows[:, :half])
            last = jnp.exp2(jnp.where(causal, column[half:] - rows[:, half:], -1e30))
            spot = slice(head * FIX, (head + 1) * FIX)
            first_ref[q, :half, spot] = near[:, :FIX]
            first_ref[q, half:, spot] = far[:, :FIX]
            top = (scores[:half, :half] * near).astype(jnp.bfloat16)
            left = (scores[half:, :half] * far).astype(jnp.bfloat16)
            right = (scores[half:, half:] * last).astype(jnp.bfloat16)
            below = jnp.concatenate([left, right], axis=1)
            parts.append(
                jnp.concatenate(
                    [
                        jnp.dot(top, x_conv[:half], preferred_element_type=jnp.float32),
                        jnp.dot(below, x_conv, preferred_element_type=jnp.float32),
                    ]
                )
            )
        mixed_ref[q, :, lanes] = jnp.where(low, parts[0], parts[1]) + skip_ref[
            :, lanes
        ] * x_conv.astype(jnp.float32)


def late_kernel(
    offset, lines, place_ref, x_ref, b_ref, c_ref, skip_ref, taps_x_ref, taps_bc_ref, *refs
):
    tails, states, parts, (y_ref, padded) = refs[:4], refs[4:8], refs[8:-2], refs[-2:]
    kids, length, wide = y_ref.shape
    width = 64
    heads = wide // width
    reach = taps_x_ref.shape[0] - 1
    q = pl.program_id(0)
    far = q ^ place_ref[0]
    size = c_ref.shape[2] // pl.num_programs(0)
    stride = skip_ref.shape[1] // pl.num_programs(0)
    group_lanes = pl.ds(pl.multiple_of(q * size, 128), size)
    low_first = lax.broadcasted_iota(jnp.int32, (FIX, 2 * width), 1) < width
    spread_row = lax.broadcasted_iota(jnp.int32, (4 * heads, wide), 0)
    spread_lane = lax.broadcasted_iota(jnp.int32, (4 * heads, wide), 1)
    spread = (spread_row % heads == spread_lane // width).astype(jnp.bfloat16)
    contract = (((1,), (1,)), ((), ()))

    def choose(blocks):
        near = jnp.where(far == 0, blocks[0], blocks[1])
        return jnp.where(far <= 1, near, jnp.where(far == 2, blocks[2], blocks[3]))

    for kid in range(kids):
        held_ref, column_ref, first_ref, mixed_ref = parts[4 * kid : 4 * kid + 4]
        tail = choose([ref[kid] for ref in tails]).astype(jnp.float32)
        state = choose([ref[kid] for ref in states])

        def opening(rows, taps, at):
            tap_rows = [tail[k * lines + at : k * lines + at + 1] for k in range(reach)]
            return conv_silu(padded, jnp.concatenate(tap_rows), rows, taps)

        b_first = opening(b_ref[kid, :, group_lanes], taps_bc_ref[0, :, group_lanes], lines - 2)
        c_first = opening(c_ref[kid, :, group_lanes], taps_bc_ref[1, :, group_lanes], lines - 1)
        c_conv = jnp.concatenate([c_first, held_ref[q, FIX:]])
        grow = jnp.exp2(column_ref[q, offset : offset + heads, :])
        terms = []
        for _ in range(3):
            terms.append(grow.astype(jnp.bfloat16).astype(jnp.float32))
            grow = grow - terms[-1]
        terms = jnp.concatenate(terms + [jnp.zeros_like(grow)]).T.astype(jnp.bfloat16)
        grow = jnp.dot(terms, spread, preferred_element_type=jnp.float32)
        term = lax.dot_general(c_conv, state, contract, preferred_element_type=jnp.float32)
        carried = (term * grow).astype(jnp.bfloat16)
        scores = lax.dot_general(
            c_conv,
            jnp.concatenate([b_first] * heads),
            contract,
            preferred_element_type=jnp.float32,
        )
        unit = offset // heads * heads * FIX
        mixing = (scores * first_ref[q, :, unit : unit + heads * FIX]).astype(jnp.bfloat16)
        for pair in range(heads // 2):
            lanes = slice(pair * 2 * width, (pair + 1) * 2 * width)
            start = pl.multiple_of(q * stride + (offset + 2 * pair) * width, 128)
            whole = pl.ds(start, 2 * width)
            x_first = opening(
                x_ref[kid, :, whole], taps_x_ref[:, whole], offset * width // 128 + pair
            ).astype(jnp.float32)
            stacked = [jnp.where(low_first, x_first, 0.0), jnp.where(low_first, 0.0, x_first)]
            if pair > 0:
                stacked = [jnp.zeros((2 * pair * FIX, 2 * width), jnp.float32)] + stacked
            if 2 * pair + 2 < heads:
                spare = (heads - 2 * pair - 2) * FIX
                stacked = stacked + [jnp.zeros((spare, 2 * width), jnp.float32)]
            part = jnp.dot(
                mixing,
                jnp.concatenate(stacked).astype(jnp.bfloat16),
                preferred_element_type=jnp.float32,
            )
            part = jnp.concatenate([part[:FIX] + skip_ref[:, whole] * x_first, part[FIX:]])
            here = slice(offset * width + lanes.start, offset * width + lanes.stop)
            y_ref[kid, :, lanes] = (
                mixed_ref[q, :, here] + part + carried[:, lanes].astype(jnp.float32)
            ).astype(jnp.bfloat16)


def cast_kernel(parts, tailed, reach, lines, *refs):
    count = len(tailed)
    ins, outs = refs[:-count], refs[-count:]
    states, tails = ins[: parts * count], ins[parts * count :]
    for j, out_ref in enumerate(outs):
        start = 0
        for at in range(parts):
            state = states[parts * j + at][0]
            rows = state.shape[0] * state.shape[1]
            out_ref[start : start + rows] = state.reshape(rows, state.shape[2]).astype(jnp.bfloat16)
            start += rows
            if at == 0 and tailed[j]:
                x_tail = tails[2 * j][0].astype(jnp.float32)
                bc_tail = tails[2 * j + 1][0].astype(jnp.float32)
                pieces = []
                for k in range(reach):
                    pieces += [x_tail[k : k + 1, i * 128 : i * 128 + 128] for i in range(lines - 2)]
                    pieces.append(bc_tail[k])
                spare = tailed[j] - lines * reach
                pieces.append(jnp.zeros((spare, 128), jnp.float32))
                out_ref[start : start + tailed[j]] = jnp.concatenate(pieces).astype(jnp.bfloat16)
                start += tailed[j]


def within_kernel(
    parent_ref,
    x_ref,
    b_ref,
    c_ref,
    dt_ref,
    bias_ref,
    alog_ref,
    skip_ref,
    taps_x_ref,
    taps_bc_ref,
    tail_x_ref,
    tail_bc_ref,
    mixed_ref,
    c_out_ref,
    grow_ref,
    padded,
):
    length = x_ref.shape[1]
    heads = dt_ref.shape[1]
    width = x_ref.shape[2] // heads
    b_conv = conv_silu(padded, tail_bc_ref[0, 0], b_ref[0], taps_bc_ref[0])
    c_conv = conv_silu(padded, tail_bc_ref[0, 1], c_ref[0], taps_bc_ref[1])
    c_out_ref[0] = c_conv
    scores = lax.dot_general(
        c_conv, b_conv, (((1,), (1,)), ((), ())), preferred_element_type=jnp.float32
    )
    raw = dt_ref[0] + bias_ref[...]
    step = jnp.maximum(raw, 0.0) + jnp.log1p(jnp.exp(-jnp.abs(raw)))
    per_token = step * (-jnp.exp(alog_ref[...]))
    row = lax.broadcasted_iota(jnp.int32, (length, length), 0)
    col = lax.broadcasted_iota(jnp.int32, (length, length), 1)
    upper = (row <= col).astype(jnp.float32)
    total = lax.dot_general(
        per_token,
        upper,
        (((1,), (0,)), ((), ())),
        precision=lax.Precision.HIGHEST,
        preferred_element_type=jnp.float32,
    )
    total_t = total.T
    grow_ref[0, 0] = jnp.exp(total_t)
    causal = row >= col
    low = lax.broadcasted_iota(jnp.int32, (length, 2 * width), 1) < width
    for pair in range(heads // 2):
        lanes = slice(pair * 2 * width, (pair + 1) * 2 * width)
        x_conv = conv_silu(
            padded, tail_x_ref[0, :, lanes], x_ref[0, :, lanes], taps_x_ref[:, lanes]
        )
        parts = []
        for head in (2 * pair, 2 * pair + 1):
            gap = total_t[:, head : head + 1] - total[head : head + 1, :]
            factor = jnp.exp(jnp.where(causal, gap, -1e30))
            mixing = (scores * factor * step[head : head + 1, :]).astype(jnp.bfloat16)
            parts.append(jnp.dot(mixing, x_conv, preferred_element_type=jnp.float32))
        mixed_ref[0, :, lanes] = (
            jnp.where(low, parts[0], parts[1]) + skip_ref[:, lanes] * x_conv.astype(jnp.float32)
        )


def carried_kernel(state_ref, c_ref, grow_ref, mixed_ref, y_ref):
    sources, _, part, width, size = state_ref.shape
    length = c_ref.shape[1]
    low = lax.broadcasted_iota(jnp.int32, (length, 2 * width), 1) < width
    c_conv = c_ref[0]
    for source in range(sources):
        state = state_ref[source, 0].reshape(part * width, size)
        term = lax.dot_general(
            c_conv, state, (((1,), (1,)), ((), ())), preferred_element_type=jnp.float32
        )
        for pair in range(part // 2):
            head = source * part + 2 * pair
            grow = jnp.where(
                low, grow_ref[0, 0, :, head : head + 1], grow_ref[0, 0, :, head + 1 : head + 2]
            )
            here = slice(2 * pair * width, (2 * pair + 2) * width)
            lanes = slice(head * width, (head + 2) * width)
            carried = (term[:, here] * grow).astype(jnp.bfloat16).astype(jnp.float32)
            y_ref[0, :, lanes] = (mixed_ref[0, :, lanes] + carried).astype(jnp.bfloat16)


def pick_kernel(parent_ref, state_ref, out_ref):
    out_ref[...] = state_ref[...]


def local_any(
    x_in,
    b_in,
    c_in,
    dt_in,
    dt_bias,
    a_log,
    d_skip,
    conv_x,
    conv_bc,
    par_state,
    tail_x,
    tail_bc,
    counts,
    order,
):
    kids, length, columns = x_in.shape
    heads = dt_in.shape[1]
    width, size = par_state.shape[2:]
    ways = lax.axis_size("batch")
    groups = b_in.shape[2] // size
    per_group = heads // groups
    part = heads // ways
    wide = per_group * width
    reach = tail_x.shape[1]
    parents_all = counts.shape[0]
    kids_all = order.shape[0]

    parent = parent_of(counts, order)
    own = lax.dynamic_slice_in_dim(parent, lax.axis_index("batch") * kids, kids)

    sent = par_state.astype(jnp.bfloat16).reshape(ways, part, width, size)
    shares = lax.all_to_all(sent, "batch", split_axis=0, concat_axis=0, tiled=True)

    tails = jnp.concatenate([tail_x.reshape(-1), tail_bc.reshape(-1)])
    tails = jnp.broadcast_to(tails[None], (ways, tails.shape[0]))
    tails = lax.all_to_all(tails, "batch", split_axis=0, concat_axis=0, tiled=True)
    tails_x = tails[:, : reach * columns].reshape(parents_all, reach, columns)
    tails_bc = tails[:, reach * columns :].reshape(parents_all, 2, reach, groups * size)

    picked = pl.pallas_call(
        pick_kernel,
        grid_spec=pltpu.PrefetchScalarGridSpec(
            num_scalar_prefetch=1,
            grid=(kids_all,),
            in_specs=[pl.BlockSpec((1, part, width, size), lambda i, p: (p[i], 0, 0, 0))],
            out_specs=pl.BlockSpec((1, part, width, size), lambda i, p: (i, 0, 0, 0)),
        ),
        out_shape=jax.ShapeDtypeStruct((kids_all, part, width, size), jnp.bfloat16),
        cost_estimate=pl.CostEstimate(
            flops=0, bytes_accessed=4 * kids_all * part * width * size, transcendentals=0
        ),
        name="pick_states",
    )(parent, shares)
    states = lax.all_to_all(
        picked.reshape(ways, kids, part, width, size), "batch", split_axis=0, concat_axis=0, tiled=True
    )

    skip_row = jnp.repeat(d_skip, width)[None, :]
    mixed, c_conv, grow = pl.pallas_call(
        within_kernel,
        grid_spec=pltpu.PrefetchScalarGridSpec(
            num_scalar_prefetch=1,
            grid=(kids, groups),
            in_specs=[
                pl.BlockSpec((1, length, wide), lambda c, q, p: (c, 0, q)),
                pl.BlockSpec((1, length, size), lambda c, q, p: (c, 0, q)),
                pl.BlockSpec((1, length, size), lambda c, q, p: (c, 0, q)),
                pl.BlockSpec((1, per_group, length), lambda c, q, p: (c, q, 0)),
                pl.BlockSpec((per_group, 1), lambda c, q, p: (q, 0)),
                pl.BlockSpec((per_group, 1), lambda c, q, p: (q, 0)),
                pl.BlockSpec((1, wide), lambda c, q, p: (0, q)),
                pl.BlockSpec((reach + 1, wide), lambda c, q, p: (0, q)),
                pl.BlockSpec((2, reach + 1, size), lambda c, q, p: (0, 0, q)),
                pl.BlockSpec((1, reach, wide), lambda c, q, p: (p[c], 0, q)),
                pl.BlockSpec((1, 2, reach, size), lambda c, q, p: (p[c], 0, 0, q)),
            ],
            out_specs=[
                pl.BlockSpec((1, length, wide), lambda c, q, p: (c, 0, q)),
                pl.BlockSpec((1, length, size), lambda c, q, p: (c, 0, q)),
                pl.BlockSpec((1, 1, length, per_group), lambda c, q, p: (c, q, 0, 0)),
            ],
            scratch_shapes=[pltpu.VMEM((8 + length, size), jnp.float32)],
        ),
        out_shape=[
            jax.ShapeDtypeStruct((kids, length, columns), jnp.float32),
            jax.ShapeDtypeStruct((kids, length, groups * size), jnp.bfloat16),
            jax.ShapeDtypeStruct((kids, groups, length, per_group), jnp.float32),
        ],
        compiler_params=pltpu.CompilerParams(vmem_limit_bytes=4 * VMEM_LIMIT),
        cost_estimate=pl.CostEstimate(
            flops=4 * kids * heads * length * length * width,
            bytes_accessed=6 * kids * length * columns,
            transcendentals=kids * heads * length * length,
        ),
        name="within",
    )(
        own,
        x_in,
        b_in,
        c_in,
        dt_in,
        dt_bias[:, None],
        a_log[:, None],
        skip_row,
        conv_x,
        conv_bc,
        tails_x,
        tails_bc,
    )

    sources = per_group // part
    return pl.pallas_call(
        carried_kernel,
        grid=(kids, groups),
        in_specs=[
            pl.BlockSpec((sources, 1, part, width, size), lambda c, q: (q, c, 0, 0, 0)),
            pl.BlockSpec((1, length, size), lambda c, q: (c, 0, q)),
            pl.BlockSpec((1, 1, length, per_group), lambda c, q: (c, q, 0, 0)),
            pl.BlockSpec((1, length, wide), lambda c, q: (c, 0, q)),
        ],
        out_specs=pl.BlockSpec((1, length, wide), lambda c, q: (c, 0, q)),
        out_shape=jax.ShapeDtypeStruct((kids, length, columns), jnp.bfloat16),
        compiler_params=pltpu.CompilerParams(vmem_limit_bytes=4 * VMEM_LIMIT),
        cost_estimate=pl.CostEstimate(
            flops=2 * kids * length * columns * size,
            bytes_accessed=8 * kids * length * columns,
            transcendentals=0,
        ),
        name="carried",
    )(states, c_conv, grow, mixed)


def local_halves(
    x_in, b_in, c_in, dt_in, dt_bias, a_log, d_skip, conv_x, conv_bc,
    par_state, tail_x, tail_bc, counts, order,
):
    kids, length, columns = x_in.shape
    heads = dt_in.shape[1]
    width, size = par_state.shape[2:]
    groups = b_in.shape[2] // size
    per_group = heads // groups
    wide = per_group * width
    taps = conv_x.shape[0]
    reach = taps - 1
    lines = (wide + 2 * size) // 128
    tail_lines = -(-lines * reach // 16) * 16
    params = pltpu.CompilerParams(vmem_limit_bytes=VMEM_LIMIT)
    anywhere = pl.BlockSpec(memory_space=pl.ANY)
    small = pl.CostEstimate(flops=1, bytes_accessed=1, transcendentals=0)

    stay = lambda x: pltpu.with_memory_space_constraint(x, pltpu.HBM)
    keep_in_vmem = lambda x: pltpu.with_memory_space_constraint(x, pltpu.VMEM)
    x_in, b_in, c_in, dt_in, conv_x, conv_bc = map(stay, (x_in, b_in, c_in, dt_in, conv_x, conv_bc))

    me = lax.axis_index("batch")
    parent = parent_of(counts, order)
    child = (jnp.arange(4 * kids, dtype=jnp.int32) // kids ^ me) * kids
    child = child + jnp.arange(4 * kids, dtype=jnp.int32) % kids
    catalog = jnp.arange(4 * 2 * kids, dtype=jnp.int32)
    owner = jnp.sum(jnp.where(child[:, None] == catalog[None, :], parent[None, :], 0), axis=1)
    slots = owner ^ me
    place = (me % 4).astype(jnp.int32)[None]

    state = stay(par_state.reshape(groups, per_group, width, size))
    x_tails, bc_tails = stay(tail_x), stay(tail_bc.transpose(0, 2, 1, 3))
    offsets = [sum(SPLIT[:k]) for k in range(len(SPLIT))]

    def swap(value, r):
        return lax.ppermute(value, "batch", perm=[(i, i ^ r) for i in range(8)])

    def cast(quarters, chunks, stacked, tokens):
        part = sum(SPLIT[k] for k in chunks)
        rows = part * width + tail_lines
        block = [SPLIT[k] for k in chunks]

        def kernel(place_ref, *refs):
            count = len(chunks) + 2
            ins, outs = refs[: count * 4], refs[count * 4 :]
            for n in range(4):
                out_ref = outs[0].at[n] if stacked else outs[n]
                cast_kernel(
                    len(chunks), [tail_lines], reach, lines, *ins[count * n : count * n + count], out_ref
                )

        operands, specs = [], []
        for n in range(4):
            which = (lambda i, p, n=n: n) if stacked else (lambda i, p, n=n: p[0] ^ n)
            for k in chunks:
                operands.append(state)
                specs.append(
                    pl.BlockSpec(
                        (1, SPLIT[k], width, size),
                        lambda i, p, w=which, at=offsets[k] // SPLIT[k]: (w(i, p), at, 0, 0),
                    )
                )
            operands += [x_tails, bc_tails]
            specs += [
                pl.BlockSpec((1, reach, wide), lambda i, p, w=which: (0, 0, w(i, p))),
                pl.BlockSpec((1, reach, 2, size), lambda i, p, w=which: (0, 0, 0, w(i, p))),
            ]
        shapes = [(4, rows, size)] if stacked else [(rows, size)] * 4
        return pl.pallas_call(
            functools.partial(drop_tokens, kernel, 1 + len(operands), len(tokens)),
            grid_spec=pltpu.PrefetchScalarGridSpec(
                num_scalar_prefetch=1,
                grid=(1,),
                in_specs=specs + [anywhere] * len(tokens),
                out_specs=[pl.BlockSpec(memory_space=pltpu.VMEM)] * len(shapes),
            ),
            out_shape=[pltpu.VMEM(shape, jnp.bfloat16) for shape in shapes],
            compiler_params=params,
            cost_estimate=small,
            name="cast_states",
        )(place, *operands, *tokens)

    def rearrange(scalars, sources, moves, shapes, tokens, name):
        def kernel(scalars_ref, *refs):
            held, outs, sems = refs[: len(sources)], refs[len(sources) : -1], refs[-1]

            def copy(move, source):
                out, at, _, _ = moves[move]
                number, take = source
                ref = held[number].at[take] if take is not None else held[number]
                target = outs[out].at[at] if at is not None else outs[out]
                return pltpu.make_async_copy(ref, target, sems.at[move])

            for move, (_, _, scalar, choices) in enumerate(moves):
                if scalar is None:
                    copy(move, choices[0]).start()
                    continue
                for value, source in enumerate(choices):

                    @pl.when(scalars_ref[scalar] == value)
                    def _(move=move, source=source):
                        copy(move, source).start()

            for move in range(len(moves)):
                copy(move, moves[move][3][0]).wait()

        return pl.pallas_call(
            functools.partial(drop_tokens, kernel, 1 + len(sources), len(tokens)),
            grid_spec=pltpu.PrefetchScalarGridSpec(
                num_scalar_prefetch=1,
                grid=(1,),
                in_specs=[anywhere] * (len(sources) + len(tokens)),
                out_specs=[pl.BlockSpec(memory_space=pltpu.VMEM)] * len(shapes),
                scratch_shapes=[pltpu.SemaphoreType.DMA((len(moves),))],
            ),
            out_shape=[pltpu.VMEM(shape, jnp.bfloat16) for shape in shapes],
            compiler_params=params,
            cost_estimate=small,
            name=name,
        )(scalars, *sources, *tokens)

    def pick(rows, sources, choices, tokens):
        moves = [
            (j, kid, j * kids + kid, choices) for j in range(4) for kid in range(kids)
        ]
        picked = rearrange(
            slots, sources, moves, [(kids, rows, size)] * 4, tokens, "pick_states"
        )
        return [picked[0]] + [swap(picked[j], j) for j in range(1, 4)]

    def early(c, piece, before, tokens):
        per = groups // 2
        at = lambda q: (c, 0, per * piece + q)
        operands = [
            x_in, b_in, c_in, dt_in, dt_bias[:, None], a_log[:, None], skip_row, conv_x, conv_bc
        ]
        keep = len(operands)
        tokens = list(tokens) + [keep_in_vmem(a) for a in before]
        first = keep + len(tokens) - len(before)
        return pl.pallas_call(
            functools.partial(
                drop_tokens, functools.partial(early_kernel, per * piece), keep, len(tokens)
            ),
            grid=(per,),
            in_specs=[
                pl.BlockSpec((1, length, wide), at),
                pl.BlockSpec((1, length, size), at),
                pl.BlockSpec((1, length, size), at),
                pl.BlockSpec((1, per_group, length), lambda q: (c, per * piece + q, 0)),
                pl.BlockSpec((per_group, 1), lambda q: (per * piece + q, 0)),
                pl.BlockSpec((per_group, 1), lambda q: (per * piece + q, 0)),
                pl.BlockSpec((1, wide), lambda q: (0, per * piece + q)),
                pl.BlockSpec((taps, wide), lambda q: (0, per * piece + q)),
                pl.BlockSpec((2, taps, size), lambda q: (0, 0, per * piece + q)),
                *[anywhere] * len(tokens),
            ],
            out_specs=[pl.BlockSpec(memory_space=pltpu.VMEM)] * 4,
            out_shape=[
                pltpu.VMEM((groups, length, wide), jnp.float32),
                pltpu.VMEM((groups, length, size), jnp.bfloat16),
                pltpu.VMEM((groups, per_group, length), jnp.float32),
                pltpu.VMEM((groups, length, per_group * FIX), jnp.float32),
            ],
            input_output_aliases={first + i: i for i in range(len(before))},
            scratch_shapes=[pltpu.VMEM((8 + length, size), jnp.float32)],
            compiler_params=params,
            cost_estimate=small,
            name="early",
        )(*operands, *tokens)

    def late(k, states, states_first, parts, result, tokens):
        part, offset = SPLIT[k], offsets[k]
        chunk = part * width
        unit = offset // part
        lane = lambda q, p: (0, 0, q * (per_group // part) + unit)
        tail_at = SPLIT[0] * width // tail_lines
        in_vmem = pl.BlockSpec(memory_space=pltpu.VMEM)
        operands = [x_in, b_in, c_in, skip_row, conv_x, conv_bc, *states_first, *states]
        specs = [
            pl.BlockSpec((kids, FIX, columns), lambda q, p: (0, 0, 0)),
            pl.BlockSpec((kids, FIX, groups * size), lambda q, p: (0, 0, 0)),
            pl.BlockSpec((kids, FIX, groups * size), lambda q, p: (0, 0, 0)),
            pl.BlockSpec((1, columns), lambda q, p: (0, 0)),
            pl.BlockSpec((taps, columns), lambda q, p: (0, 0)),
            pl.BlockSpec((2, taps, groups * size), lambda q, p: (0, 0, 0)),
            *[pl.BlockSpec((kids, tail_lines, size), lambda q, p: (0, tail_at, 0))] * 4,
            *[pl.BlockSpec((kids, chunk, size), lambda q, p: (0, 0, 0))] * 4,
        ]
        for c in range(kids):
            mixed, held, column, first = parts[c]
            operands += [keep_in_vmem(a) for a in (held, column, first, mixed)]
            specs += [in_vmem] * 4
        keep = 1 + len(operands)
        operands += tokens
        specs += [anywhere] * len(tokens)
        alias = {}
        if result is not None:
            alias = {1 + len(operands): 0}
            operands.append(result)
            specs.append(anywhere)
        return pl.pallas_call(
            functools.partial(
                drop_tokens,
                functools.partial(late_kernel, offset, lines),
                keep,
                1 + len(operands) - keep,
            ),
            grid_spec=pltpu.PrefetchScalarGridSpec(
                num_scalar_prefetch=1,
                grid=(groups,),
                in_specs=specs,
                out_specs=pl.BlockSpec((kids, length, chunk), lane),
                scratch_shapes=[pltpu.VMEM((8 + FIX, size), jnp.float32)],
            ),
            out_shape=jax.ShapeDtypeStruct(x_in.shape, jnp.bfloat16),
            input_output_aliases=alias,
            compiler_params=params,
            cost_estimate=small,
            name="late",
        )(place, *operands)

    skip_row = jnp.repeat(d_skip, width)[None, :]
    rows = [SPLIT[0] * width + tail_lines, SPLIT[1] * width]
    chunk_a, chunk_b = pl.ds(0, rows[0]), pl.ds(rows[0], rows[1])

    (sent_a,) = cast(range(4), [0], True, [])
    crossed_a = swap(sent_a, 4)
    own = cast(range(4), [0, 1], False, [sent_a])
    inside = [own[0]] + [swap(own[j], j) for j in range(1, 4)]
    first = early(0, 0, [], [own[0], slots])
    first = early(0, 1, first, [])
    second = early(1, 0, [], [first[1]])
    moves = [(0, j, None, [(j, chunk_b)]) for j in range(4)]
    (sent_b,) = rearrange(
        place, inside, moves, [(4, rows[1], size)], [second[1], crossed_a], "stack_b"
    )
    crossed_b = swap(sent_b, 4)
    moves = [(j, None, 0, [(0, n ^ j) for n in range(4)]) for j in range(4)]
    spread = rearrange(
        place, [crossed_a], moves, [(rows[0], size)] * 4, [sent_b], "split_a"
    )
    spread = [spread[0]] + [swap(spread[j], j) for j in range(1, 4)]
    second = early(1, 1, second, [spread[0]])
    choices = [(j, chunk_a) for j in range(4)] + [(4 + j, None) for j in range(4)]
    states_a = pick(rows[0], [*inside, *spread], choices, [second[1]])
    choices = [(j, chunk_b) for j in range(4)] + [(4, j) for j in range(4)]
    states_b = pick(rows[1], [*inside, crossed_b], choices, [states_a[0]])
    parts = [first, second]
    result = late(0, states_a, states_a, parts, None, [states_b[0]])
    return late(1, states_b, states_a, parts, result, [])


def solution(mesh):
    rows, cols = P(("groups", "batch"), None, "head"), P(("groups", "batch"), "head")
    placed = (
        rows, rows, rows, cols, P("head"), P("head"), P("head"), P(None, "head"),
        P(None, None, "head"), cols, rows, P(("groups", "batch"), None, None, "head"),
        P("groups"), P("groups"),
    )
    local = local_halves if mesh.shape["batch"] == 8 else local_any
    return jax.shard_map(local, mesh=mesh, in_specs=placed, out_specs=rows, check_vma=False)
```

```python
import functools

import jax
import jax.numpy as jnp
from jax import lax
from jax.experimental import pallas as pl
from jax.experimental.pallas import tpu as pltpu
from jax.sharding import PartitionSpec as P

VMEM_LIMIT = 12 * 1024 * 1024
SPLIT = (8, 8)
FIX = 16
LOG2_E = 1.4426950408889634


def drop_tokens(kernel, keep, tokens, *refs):
    kernel(*refs[:keep], *refs[keep + tokens :])


def parent_of(counts, order):
    index = jnp.arange(counts.shape[0], dtype=jnp.int32)
    bounds = jnp.sum(jnp.where(index[None, :] <= index[:, None], counts[None, :], 0), axis=1)
    return jnp.sum((bounds[None, :] <= order[:, None]).astype(jnp.int32), axis=1)


def three_terms(value):
    terms = []
    for _ in range(3):
        terms.append(value.astype(jnp.bfloat16).astype(jnp.float32))
        value = value - terms[-1]
    return jnp.concatenate(terms)


def conv_silu(padded, tail, rows, taps):
    length = rows.shape[0]
    reach = taps.shape[0] - 1
    padded[8 - reach : 8, :] = jnp.broadcast_to(tail, (reach, rows.shape[1])).astype(jnp.float32)
    padded[8 : 8 + length, :] = rows.astype(jnp.float32)
    total = padded[8 - reach : 8 - reach + length, :] * taps[0:1, :]
    for k in range(1, reach + 1):
        total = total + padded[8 - reach + k : 8 - reach + k + length, :] * taps[k : k + 1, :]
    half = 0.5 * total
    return (half + half * jnp.tanh(half)).astype(jnp.bfloat16)


def early_kernel(
    base, x_ref, b_ref, c_ref, dt_ref, bias_ref, alog_ref, skip_ref, taps_x_ref, taps_bc_ref,
    mixed_ref, c_out_ref, column_ref, first_ref, padded,
):
    length, wide = x_ref.shape[1:]
    heads = dt_ref.shape[1]
    q = base + pl.program_id(0)
    width = wide // heads
    half = length // 2

    def convolve(rows, taps, slot):
        bulk = conv_silu(padded.at[slot % 2], 0.0, rows, taps)[FIX:]
        return jnp.concatenate([jnp.zeros((FIX, rows.shape[1]), jnp.bfloat16), bulk])

    b_conv = convolve(b_ref[0], taps_bc_ref[0], 0)
    c_conv = convolve(c_ref[0], taps_bc_ref[1], 1)
    c_out_ref[q] = c_conv
    scores = lax.dot_general(
        c_conv, b_conv, (((1,), (1,)), ((), ())), preferred_element_type=jnp.float32
    )
    raw = dt_ref[0] + bias_ref[...]
    step = jnp.maximum(raw, 0.0) + jnp.log1p(jnp.exp(-jnp.abs(raw)))
    per_token = step * (-jnp.exp(alog_ref[...]))
    upper = lax.broadcasted_iota(jnp.int32, (length, length), 0) <= lax.broadcasted_iota(
        jnp.int32, (length, length), 1
    )
    sums = jnp.dot(
        three_terms(per_token).astype(jnp.bfloat16),
        upper.astype(jnp.float32).astype(jnp.bfloat16),
        preferred_element_type=jnp.float32,
    )
    total = (sums[:heads] + sums[heads : 2 * heads]) + sums[2 * heads :]
    total = total * LOG2_E
    row = total - jnp.log(step) * LOG2_E
    columns = total.T
    column_ref[q] = total
    causal = lax.broadcasted_iota(jnp.int32, (half, half), 0) >= lax.broadcasted_iota(
        jnp.int32, (half, half), 1
    )
    low = lax.broadcasted_iota(jnp.int32, (length, 2 * width), 1) < width
    for pair in range(heads // 2):
        lanes = slice(pair * 2 * width, (pair + 1) * 2 * width)
        x_conv = convolve(x_ref[0, :, lanes], taps_x_ref[:, lanes], pair)
        parts = []
        for head in (2 * pair, 2 * pair + 1):
            column = jnp.broadcast_to(columns[:, head : head + 1], (length, half))
            rows = row[head : head + 1, :]
            near = jnp.exp2(jnp.where(causal, column[:half] - rows[:, :half], -1e30))
            far = jnp.exp2(column[half:] - rows[:, :half])
            last = jnp.exp2(jnp.where(causal, column[half:] - rows[:, half:], -1e30))
            spot = slice(head * FIX, (head + 1) * FIX)
            first_ref[q, :half, spot] = near[:, :FIX]
            first_ref[q, half:, spot] = far[:, :FIX]
            top = (scores[:half, :half] * near).astype(jnp.bfloat16)
            left = (scores[half:, :half] * far).astype(jnp.bfloat16)
            right = (scores[half:, half:] * last).astype(jnp.bfloat16)
            below = jnp.concatenate([left, right], axis=1)
            parts.append(
                jnp.concatenate(
                    [
                        jnp.dot(top, x_conv[:half], preferred_element_type=jnp.float32),
                        jnp.dot(below, x_conv, preferred_element_type=jnp.float32),
                    ]
                )
            )
        mixed_ref[q, :, lanes] = jnp.where(low, parts[0], parts[1]) + skip_ref[
            :, lanes
        ] * x_conv.astype(jnp.float32)


def late_kernel(
    offset, lines, place_ref, x_ref, b_ref, c_ref, skip_ref, taps_x_ref, taps_bc_ref, *refs
):
    tails, states, parts, (y_ref, padded) = refs[:4], refs[4:8], refs[8:-2], refs[-2:]
    kids, length, wide = y_ref.shape
    width = 64
    heads = wide // width
    reach = taps_x_ref.shape[0] - 1
    q = pl.program_id(0)
    far = q ^ place_ref[0]
    size = c_ref.shape[2] // pl.num_programs(0)
    stride = skip_ref.shape[1] // pl.num_programs(0)
    group_lanes = pl.ds(pl.multiple_of(q * size, 128), size)
    low_first = lax.broadcasted_iota(jnp.int32, (FIX, 2 * width), 1) < width
    spread_row = lax.broadcasted_iota(jnp.int32, (4 * heads, wide), 0)
    spread_lane = lax.broadcasted_iota(jnp.int32, (4 * heads, wide), 1)
    spread = (spread_row % heads == spread_lane // width).astype(jnp.bfloat16)
    contract = (((1,), (1,)), ((), ()))

    def choose(blocks):
        near = jnp.where(far == 0, blocks[0], blocks[1])
        return jnp.where(far <= 1, near, jnp.where(far == 2, blocks[2], blocks[3]))

    for kid in range(kids):
        held_ref, column_ref, first_ref, mixed_ref = parts[4 * kid : 4 * kid + 4]
        tail = choose([ref[kid] for ref in tails]).astype(jnp.float32)
        state = choose([ref[kid] for ref in states])

        def opening(scratch, rows, taps, at, count):
            tap_rows = []
            for k in range(reach):
                here = [tail[k * lines + at + n : k * lines + at + n + 1] for n in range(count)]
                tap_rows.append(jnp.concatenate(here, axis=1))
            return conv_silu(scratch, jnp.concatenate(tap_rows), rows, taps)

        start = pl.multiple_of(q * stride + offset * width, 128)
        chunk_lanes = pl.ds(start, wide)
        blocks = wide // 128
        bc_first = opening(
            padded.at[kid, :, wide : wide + 2 * size],
            jnp.concatenate([b_ref[kid, :, group_lanes], c_ref[kid, :, group_lanes]], axis=1),
            jnp.concatenate([taps_bc_ref[0, :, group_lanes], taps_bc_ref[1, :, group_lanes]], axis=1),
            lines - 2,
            2,
        )
        b_first, c_first = bc_first[:, :size], bc_first[:, size:]
        x_all = opening(
            padded.at[kid, :, :wide],
            x_ref[kid, :, chunk_lanes],
            taps_x_ref[:, chunk_lanes],
            offset * width // 128,
            blocks,
        ).astype(jnp.float32)
        skipped = skip_ref[:, chunk_lanes] * x_all
        c_conv = jnp.concatenate([c_first, held_ref[q, FIX:]])
        grow = jnp.exp2(column_ref[q, offset : offset + heads, :])
        terms = jnp.concatenate([three_terms(grow), jnp.zeros_like(grow)])
        terms = terms.T.astype(jnp.bfloat16)
        grow = jnp.dot(terms, spread, preferred_element_type=jnp.float32)
        term = lax.dot_general(c_conv, state, contract, preferred_element_type=jnp.float32)
        carried = (term * grow).astype(jnp.bfloat16)
        scores = lax.dot_general(
            c_conv,
            jnp.concatenate([b_first] * heads),
            contract,
            preferred_element_type=jnp.float32,
        )
        unit = offset // heads * heads * FIX
        mixing = (scores * first_ref[q, :, unit : unit + heads * FIX]).astype(jnp.bfloat16)
        for pair in range(heads // 2):
            lanes = slice(pair * 2 * width, (pair + 1) * 2 * width)
            x_first = x_all[:, lanes]
            stacked = [jnp.where(low_first, x_first, 0.0), jnp.where(low_first, 0.0, x_first)]
            if pair > 0:
                stacked = [jnp.zeros((2 * pair * FIX, 2 * width), jnp.float32)] + stacked
            if 2 * pair + 2 < heads:
                spare = (heads - 2 * pair - 2) * FIX
                stacked = stacked + [jnp.zeros((spare, 2 * width), jnp.float32)]
            part = jnp.dot(
                mixing,
                jnp.concatenate(stacked).astype(jnp.bfloat16),
                preferred_element_type=jnp.float32,
            )
            part = jnp.concatenate([part[:FIX] + skipped[:, lanes], part[FIX:]])
            here = slice(offset * width + lanes.start, offset * width + lanes.stop)
            y_ref[kid, :, lanes] = (
                mixed_ref[q, :, here] + part + carried[:, lanes].astype(jnp.float32)
            ).astype(jnp.bfloat16)


def cast_kernel(parts, tailed, reach, lines, *refs):
    count = len(tailed)
    ins, outs = refs[:-count], refs[-count:]
    states, tails = ins[: parts * count], ins[parts * count :]
    for j, out_ref in enumerate(outs):
        start = 0
        for at in range(parts):
            state = states[parts * j + at][0]
            rows = state.shape[0] * state.shape[1]
            out_ref[start : start + rows] = state.reshape(rows, state.shape[2]).astype(jnp.bfloat16)
            start += rows
            if at == 0 and tailed[j]:
                x_tail = tails[2 * j][0].astype(jnp.float32)
                bc_tail = tails[2 * j + 1][0].astype(jnp.float32)
                pieces = []
                for k in range(reach):
                    pieces += [x_tail[k : k + 1, i * 128 : i * 128 + 128] for i in range(lines - 2)]
                    pieces.append(bc_tail[k])
                spare = tailed[j] - lines * reach
                pieces.append(jnp.zeros((spare, 128), jnp.float32))
                out_ref[start : start + tailed[j]] = jnp.concatenate(pieces).astype(jnp.bfloat16)
                start += tailed[j]


def within_kernel(
    parent_ref,
    x_ref,
    b_ref,
    c_ref,
    dt_ref,
    bias_ref,
    alog_ref,
    skip_ref,
    taps_x_ref,
    taps_bc_ref,
    tail_x_ref,
    tail_bc_ref,
    mixed_ref,
    c_out_ref,
    grow_ref,
    padded,
):
    length = x_ref.shape[1]
    heads = dt_ref.shape[1]
    width = x_ref.shape[2] // heads
    b_conv = conv_silu(padded, tail_bc_ref[0, 0], b_ref[0], taps_bc_ref[0])
    c_conv = conv_silu(padded, tail_bc_ref[0, 1], c_ref[0], taps_bc_ref[1])
    c_out_ref[0] = c_conv
    scores = lax.dot_general(
        c_conv, b_conv, (((1,), (1,)), ((), ())), preferred_element_type=jnp.float32
    )
    raw = dt_ref[0] + bias_ref[...]
    step = jnp.maximum(raw, 0.0) + jnp.log1p(jnp.exp(-jnp.abs(raw)))
    per_token = step * (-jnp.exp(alog_ref[...]))
    row = lax.broadcasted_iota(jnp.int32, (length, length), 0)
    col = lax.broadcasted_iota(jnp.int32, (length, length), 1)
    upper = (row <= col).astype(jnp.float32)
    total = lax.dot_general(
        per_token,
        upper,
        (((1,), (0,)), ((), ())),
        precision=lax.Precision.HIGHEST,
        preferred_element_type=jnp.float32,
    )
    total_t = total.T
    grow_ref[0, 0] = jnp.exp(total_t)
    causal = row >= col
    low = lax.broadcasted_iota(jnp.int32, (length, 2 * width), 1) < width
    for pair in range(heads // 2):
        lanes = slice(pair * 2 * width, (pair + 1) * 2 * width)
        x_conv = conv_silu(
            padded, tail_x_ref[0, :, lanes], x_ref[0, :, lanes], taps_x_ref[:, lanes]
        )
        parts = []
        for head in (2 * pair, 2 * pair + 1):
            gap = total_t[:, head : head + 1] - total[head : head + 1, :]
            factor = jnp.exp(jnp.where(causal, gap, -1e30))
            mixing = (scores * factor * step[head : head + 1, :]).astype(jnp.bfloat16)
            parts.append(jnp.dot(mixing, x_conv, preferred_element_type=jnp.float32))
        mixed_ref[0, :, lanes] = (
            jnp.where(low, parts[0], parts[1]) + skip_ref[:, lanes] * x_conv.astype(jnp.float32)
        )


def carried_kernel(state_ref, c_ref, grow_ref, mixed_ref, y_ref):
    sources, _, part, width, size = state_ref.shape
    length = c_ref.shape[1]
    low = lax.broadcasted_iota(jnp.int32, (length, 2 * width), 1) < width
    c_conv = c_ref[0]
    for source in range(sources):
        state = state_ref[source, 0].reshape(part * width, size)
        term = lax.dot_general(
            c_conv, state, (((1,), (1,)), ((), ())), preferred_element_type=jnp.float32
        )
        for pair in range(part // 2):
            head = source * part + 2 * pair
            grow = jnp.where(
                low, grow_ref[0, 0, :, head : head + 1], grow_ref[0, 0, :, head + 1 : head + 2]
            )
            here = slice(2 * pair * width, (2 * pair + 2) * width)
            lanes = slice(head * width, (head + 2) * width)
            carried = (term[:, here] * grow).astype(jnp.bfloat16).astype(jnp.float32)
            y_ref[0, :, lanes] = (mixed_ref[0, :, lanes] + carried).astype(jnp.bfloat16)


def pick_kernel(parent_ref, state_ref, out_ref):
    out_ref[...] = state_ref[...]


def local_any(
    x_in,
    b_in,
    c_in,
    dt_in,
    dt_bias,
    a_log,
    d_skip,
    conv_x,
    conv_bc,
    par_state,
    tail_x,
    tail_bc,
    counts,
    order,
):
    kids, length, columns = x_in.shape
    heads = dt_in.shape[1]
    width, size = par_state.shape[2:]
    ways = lax.axis_size("batch")
    groups = b_in.shape[2] // size
    per_group = heads // groups
    part = heads // ways
    wide = per_group * width
    reach = tail_x.shape[1]
    parents_all = counts.shape[0]
    kids_all = order.shape[0]

    parent = parent_of(counts, order)
    own = lax.dynamic_slice_in_dim(parent, lax.axis_index("batch") * kids, kids)

    sent = par_state.astype(jnp.bfloat16).reshape(ways, part, width, size)
    shares = lax.all_to_all(sent, "batch", split_axis=0, concat_axis=0, tiled=True)

    tails = jnp.concatenate([tail_x.reshape(-1), tail_bc.reshape(-1)])
    tails = jnp.broadcast_to(tails[None], (ways, tails.shape[0]))
    tails = lax.all_to_all(tails, "batch", split_axis=0, concat_axis=0, tiled=True)
    tails_x = tails[:, : reach * columns].reshape(parents_all, reach, columns)
    tails_bc = tails[:, reach * columns :].reshape(parents_all, 2, reach, groups * size)

    picked = pl.pallas_call(
        pick_kernel,
        grid_spec=pltpu.PrefetchScalarGridSpec(
            num_scalar_prefetch=1,
            grid=(kids_all,),
            in_specs=[pl.BlockSpec((1, part, width, size), lambda i, p: (p[i], 0, 0, 0))],
            out_specs=pl.BlockSpec((1, part, width, size), lambda i, p: (i, 0, 0, 0)),
        ),
        out_shape=jax.ShapeDtypeStruct((kids_all, part, width, size), jnp.bfloat16),
        cost_estimate=pl.CostEstimate(
            flops=0, bytes_accessed=4 * kids_all * part * width * size, transcendentals=0
        ),
        name="pick_states",
    )(parent, shares)
    states = lax.all_to_all(
        picked.reshape(ways, kids, part, width, size), "batch", split_axis=0, concat_axis=0, tiled=True
    )

    skip_row = jnp.repeat(d_skip, width)[None, :]
    mixed, c_conv, grow = pl.pallas_call(
        within_kernel,
        grid_spec=pltpu.PrefetchScalarGridSpec(
            num_scalar_prefetch=1,
            grid=(kids, groups),
            in_specs=[
                pl.BlockSpec((1, length, wide), lambda c, q, p: (c, 0, q)),
                pl.BlockSpec((1, length, size), lambda c, q, p: (c, 0, q)),
                pl.BlockSpec((1, length, size), lambda c, q, p: (c, 0, q)),
                pl.BlockSpec((1, per_group, length), lambda c, q, p: (c, q, 0)),
                pl.BlockSpec((per_group, 1), lambda c, q, p: (q, 0)),
                pl.BlockSpec((per_group, 1), lambda c, q, p: (q, 0)),
                pl.BlockSpec((1, wide), lambda c, q, p: (0, q)),
                pl.BlockSpec((reach + 1, wide), lambda c, q, p: (0, q)),
                pl.BlockSpec((2, reach + 1, size), lambda c, q, p: (0, 0, q)),
                pl.BlockSpec((1, reach, wide), lambda c, q, p: (p[c], 0, q)),
                pl.BlockSpec((1, 2, reach, size), lambda c, q, p: (p[c], 0, 0, q)),
            ],
            out_specs=[
                pl.BlockSpec((1, length, wide), lambda c, q, p: (c, 0, q)),
                pl.BlockSpec((1, length, size), lambda c, q, p: (c, 0, q)),
                pl.BlockSpec((1, 1, length, per_group), lambda c, q, p: (c, q, 0, 0)),
            ],
            scratch_shapes=[pltpu.VMEM((8 + length, size), jnp.float32)],
        ),
        out_shape=[
            jax.ShapeDtypeStruct((kids, length, columns), jnp.float32),
            jax.ShapeDtypeStruct((kids, length, groups * size), jnp.bfloat16),
            jax.ShapeDtypeStruct((kids, groups, length, per_group), jnp.float32),
        ],
        compiler_params=pltpu.CompilerParams(vmem_limit_bytes=4 * VMEM_LIMIT),
        cost_estimate=pl.CostEstimate(
            flops=4 * kids * heads * length * length * width,
            bytes_accessed=6 * kids * length * columns,
            transcendentals=kids * heads * length * length,
        ),
        name="within",
    )(
        own,
        x_in,
        b_in,
        c_in,
        dt_in,
        dt_bias[:, None],
        a_log[:, None],
        skip_row,
        conv_x,
        conv_bc,
        tails_x,
        tails_bc,
    )

    sources = per_group // part
    return pl.pallas_call(
        carried_kernel,
        grid=(kids, groups),
        in_specs=[
            pl.BlockSpec((sources, 1, part, width, size), lambda c, q: (q, c, 0, 0, 0)),
            pl.BlockSpec((1, length, size), lambda c, q: (c, 0, q)),
            pl.BlockSpec((1, 1, length, per_group), lambda c, q: (c, q, 0, 0)),
            pl.BlockSpec((1, length, wide), lambda c, q: (c, 0, q)),
        ],
        out_specs=pl.BlockSpec((1, length, wide), lambda c, q: (c, 0, q)),
        out_shape=jax.ShapeDtypeStruct((kids, length, columns), jnp.bfloat16),
        compiler_params=pltpu.CompilerParams(vmem_limit_bytes=4 * VMEM_LIMIT),
        cost_estimate=pl.CostEstimate(
            flops=2 * kids * length * columns * size,
            bytes_accessed=8 * kids * length * columns,
            transcendentals=0,
        ),
        name="carried",
    )(states, c_conv, grow, mixed)


def local_halves(
    x_in, b_in, c_in, dt_in, dt_bias, a_log, d_skip, conv_x, conv_bc,
    par_state, tail_x, tail_bc, counts, order,
):
    kids, length, columns = x_in.shape
    heads = dt_in.shape[1]
    width, size = par_state.shape[2:]
    groups = b_in.shape[2] // size
    per_group = heads // groups
    wide = per_group * width
    taps = conv_x.shape[0]
    reach = taps - 1
    lines = (wide + 2 * size) // 128
    tail_lines = -(-lines * reach // 16) * 16
    params = pltpu.CompilerParams(vmem_limit_bytes=VMEM_LIMIT)
    anywhere = pl.BlockSpec(memory_space=pl.ANY)
    small = pl.CostEstimate(flops=1, bytes_accessed=1, transcendentals=0)

    stay = lambda x: pltpu.with_memory_space_constraint(x, pltpu.HBM)
    keep_in_vmem = lambda x: pltpu.with_memory_space_constraint(x, pltpu.VMEM)
    x_in, b_in, c_in, dt_in, conv_x, conv_bc = map(stay, (x_in, b_in, c_in, dt_in, conv_x, conv_bc))

    me = lax.axis_index("batch")
    parent = parent_of(counts, order)
    child = (jnp.arange(4 * kids, dtype=jnp.int32) // kids ^ me) * kids
    child = child + jnp.arange(4 * kids, dtype=jnp.int32) % kids
    catalog = jnp.arange(4 * 2 * kids, dtype=jnp.int32)
    owner = jnp.sum(jnp.where(child[:, None] == catalog[None, :], parent[None, :], 0), axis=1)
    slots = owner ^ me
    place = (me % 4).astype(jnp.int32)[None]

    state = stay(par_state.reshape(groups, per_group, width, size))
    x_tails, bc_tails = stay(tail_x), stay(tail_bc.transpose(0, 2, 1, 3))
    offsets = [sum(SPLIT[:k]) for k in range(len(SPLIT))]

    def swap(value, r):
        return lax.ppermute(value, "batch", perm=[(i, i ^ r) for i in range(8)])

    def cast(chunks, paired, tokens):
        part = sum(SPLIT[k] for k in chunks)
        rows = part * width + tail_lines
        block = [SPLIT[k] for k in chunks]

        def kernel(place_ref, *refs):
            count = len(chunks) + 2
            ins, outs = refs[: count * 4], refs[count * 4 :]
            for n in range(4):
                out_ref = outs[n // 2].at[n % 2] if paired else outs[n]
                cast_kernel(
                    len(chunks), [tail_lines], reach, lines, *ins[count * n : count * n + count], out_ref
                )

        operands, specs = [], []
        for n in range(4):
            which = lambda i, p, n=n: p[0] ^ n
            for k in chunks:
                operands.append(state)
                specs.append(
                    pl.BlockSpec(
                        (1, SPLIT[k], width, size),
                        lambda i, p, w=which, at=offsets[k] // SPLIT[k]: (w(i, p), at, 0, 0),
                    )
                )
            operands += [x_tails, bc_tails]
            specs += [
                pl.BlockSpec((1, reach, wide), lambda i, p, w=which: (0, 0, w(i, p))),
                pl.BlockSpec((1, reach, 2, size), lambda i, p, w=which: (0, 0, 0, w(i, p))),
            ]
        shapes = [(2, rows, size)] * 2 if paired else [(rows, size)] * 4
        return pl.pallas_call(
            functools.partial(drop_tokens, kernel, 1 + len(operands), len(tokens)),
            grid_spec=pltpu.PrefetchScalarGridSpec(
                num_scalar_prefetch=1,
                grid=(1,),
                in_specs=specs + [anywhere] * len(tokens),
                out_specs=[pl.BlockSpec(memory_space=pltpu.VMEM)] * len(shapes),
            ),
            out_shape=[pltpu.VMEM(shape, jnp.bfloat16) for shape in shapes],
            compiler_params=params,
            cost_estimate=small,
            name="cast_states",
        )(place, *operands, *tokens)

    def rearrange(scalars, sources, moves, shapes, tokens, name):
        def kernel(scalars_ref, *refs):
            held, outs, sems = refs[: len(sources)], refs[len(sources) : -1], refs[-1]

            def copy(move, source):
                out, at, _, _ = moves[move]
                number, take = source
                ref = held[number].at[take] if take is not None else held[number]
                target = outs[out].at[at] if at is not None else outs[out]
                return pltpu.make_async_copy(ref, target, sems.at[move])

            for move, (_, _, scalar, choices) in enumerate(moves):
                if scalar is None:
                    copy(move, choices[0]).start()
                    continue
                for value, source in enumerate(choices):

                    @pl.when(scalars_ref[scalar] == value)
                    def _(move=move, source=source):
                        copy(move, source).start()

            for move in range(len(moves)):
                copy(move, moves[move][3][0]).wait()

        return pl.pallas_call(
            functools.partial(drop_tokens, kernel, 1 + len(sources), len(tokens)),
            grid_spec=pltpu.PrefetchScalarGridSpec(
                num_scalar_prefetch=1,
                grid=(1,),
                in_specs=[anywhere] * (len(sources) + len(tokens)),
                out_specs=[pl.BlockSpec(memory_space=pltpu.VMEM)] * len(shapes),
                scratch_shapes=[pltpu.SemaphoreType.DMA((len(moves),))],
            ),
            out_shape=[pltpu.VMEM(shape, jnp.bfloat16) for shape in shapes],
            compiler_params=params,
            cost_estimate=small,
            name=name,
        )(scalars, *sources, *tokens)

    def pick(rows, sources, choices, tokens):
        moves = [
            (j, kid, j * kids + kid, choices) for j in range(4) for kid in range(kids)
        ]
        picked = rearrange(
            slots, sources, moves, [(kids, rows, size)] * 4, tokens, "pick_states"
        )
        return [picked[0]] + [swap(picked[j], j) for j in range(1, 4)]

    def early(c, piece, before, tokens):
        per = groups // 2
        at = lambda q: (c, 0, per * piece + q)
        operands = [
            x_in, b_in, c_in, dt_in, dt_bias[:, None], a_log[:, None], skip_row, conv_x, conv_bc
        ]
        keep = len(operands)
        tokens = list(tokens) + [keep_in_vmem(a) for a in before]
        first = keep + len(tokens) - len(before)
        return pl.pallas_call(
            functools.partial(
                drop_tokens, functools.partial(early_kernel, per * piece), keep, len(tokens)
            ),
            grid=(per,),
            in_specs=[
                pl.BlockSpec((1, length, wide), at),
                pl.BlockSpec((1, length, size), at),
                pl.BlockSpec((1, length, size), at),
                pl.BlockSpec((1, per_group, length), lambda q: (c, per * piece + q, 0)),
                pl.BlockSpec((per_group, 1), lambda q: (per * piece + q, 0)),
                pl.BlockSpec((per_group, 1), lambda q: (per * piece + q, 0)),
                pl.BlockSpec((1, wide), lambda q: (0, per * piece + q)),
                pl.BlockSpec((taps, wide), lambda q: (0, per * piece + q)),
                pl.BlockSpec((2, taps, size), lambda q: (0, 0, per * piece + q)),
                *[anywhere] * len(tokens),
            ],
            out_specs=[pl.BlockSpec(memory_space=pltpu.VMEM)] * 4,
            out_shape=[
                pltpu.VMEM((groups, length, wide), jnp.float32),
                pltpu.VMEM((groups, length, size), jnp.bfloat16),
                pltpu.VMEM((groups, per_group, length), jnp.float32),
                pltpu.VMEM((groups, length, per_group * FIX), jnp.float32),
            ],
            input_output_aliases={first + i: i for i in range(len(before))},
            scratch_shapes=[pltpu.VMEM((2, 8 + length, size), jnp.float32)],
            compiler_params=params,
            cost_estimate=small,
            name="early",
        )(*operands, *tokens)

    def late(k, states, states_first, parts, result, tokens):
        part, offset = SPLIT[k], offsets[k]
        chunk = part * width
        unit = offset // part
        lane = lambda q, p: (0, 0, q * (per_group // part) + unit)
        tail_at = SPLIT[0] * width // tail_lines
        in_vmem = pl.BlockSpec(memory_space=pltpu.VMEM)
        operands = [x_in, b_in, c_in, skip_row, conv_x, conv_bc, *states_first, *states]
        specs = [
            pl.BlockSpec((kids, FIX, columns), lambda q, p: (0, 0, 0)),
            pl.BlockSpec((kids, FIX, groups * size), lambda q, p: (0, 0, 0)),
            pl.BlockSpec((kids, FIX, groups * size), lambda q, p: (0, 0, 0)),
            pl.BlockSpec((1, columns), lambda q, p: (0, 0)),
            pl.BlockSpec((taps, columns), lambda q, p: (0, 0)),
            pl.BlockSpec((2, taps, groups * size), lambda q, p: (0, 0, 0)),
            *[pl.BlockSpec((kids, tail_lines, size), lambda q, p: (0, tail_at, 0))] * 4,
            *[pl.BlockSpec((kids, chunk, size), lambda q, p: (0, 0, 0))] * 4,
        ]
        for c in range(kids):
            mixed, held, column, first = parts[c]
            operands += [keep_in_vmem(a) for a in (held, column, first, mixed)]
            specs += [in_vmem] * 4
        keep = 1 + len(operands)
        operands += tokens
        specs += [anywhere] * len(tokens)
        alias = {}
        if result is not None:
            alias = {1 + len(operands): 0}
            operands.append(result)
            specs.append(anywhere)
        return pl.pallas_call(
            functools.partial(
                drop_tokens,
                functools.partial(late_kernel, offset, lines),
                keep,
                1 + len(operands) - keep,
            ),
            grid_spec=pltpu.PrefetchScalarGridSpec(
                num_scalar_prefetch=1,
                grid=(groups,),
                in_specs=specs,
                out_specs=pl.BlockSpec((kids, length, chunk), lane),
                scratch_shapes=[pltpu.VMEM((kids, 8 + FIX, chunk + 2 * size), jnp.float32)],
            ),
            out_shape=jax.ShapeDtypeStruct(x_in.shape, jnp.bfloat16),
            input_output_aliases=alias,
            compiler_params=params,
            cost_estimate=small,
            name="late",
        )(place, *operands)

    skip_row = jnp.repeat(d_skip, width)[None, :]
    rows = [SPLIT[0] * width + tail_lines, SPLIT[1] * width]
    chunk_a, chunk_b = pl.ds(0, rows[0]), pl.ds(rows[0], rows[1])

    sent_a = cast([0], True, [])
    crossed_a = [swap(sent_a[0], 4), swap(sent_a[1], 6)]
    own = cast([0, 1], False, [sent_a[0]])
    inside = [own[0]] + [swap(own[j], j) for j in range(1, 4)]
    first = early(0, 0, [], [own[0], slots])
    first = early(0, 1, first, [])
    second = early(1, 0, [], [first[1]])
    moves = [(0, j, None, [(j, chunk_b)]) for j in range(4)]
    (sent_b,) = rearrange(
        place, inside, moves, [(4, rows[1], size)], [second[1], *crossed_a], "stack_b"
    )
    crossed_b = swap(sent_b, 4)
    moves = [(0, n, None, [(n, 1)]) for n in range(2)]
    (spread,) = rearrange(
        place, crossed_a, moves, [(2, rows[0], size)], [sent_b], "stack_a"
    )
    passed = swap(spread, 1)
    second = early(1, 1, second, [spread])
    choices = [(j, chunk_a) for j in range(4)] + [(4, 0), (6, 0), (5, 0), (6, 1)]
    states_a = pick(rows[0], [*inside, *crossed_a, passed], choices, [second[1]])
    choices = [(j, chunk_b) for j in range(4)] + [(4, j) for j in range(4)]
    states_b = pick(rows[1], [*inside, crossed_b], choices, [states_a[0]])
    parts = [first, second]
    result = late(0, states_a, states_a, parts, None, [states_b[0]])
    return late(1, states_b, states_a, parts, result, [])


def solution(mesh):
    rows, cols = P(("groups", "batch"), None, "head"), P(("groups", "batch"), "head")
    placed = (
        rows, rows, rows, cols, P("head"), P("head"), P("head"), P(None, "head"),
        P(None, None, "head"), cols, rows, P(("groups", "batch"), None, None, "head"),
        P("groups"), P("groups"),
    )
    local = local_halves if mesh.shape["batch"] == 8 else local_any
    return jax.shard_map(local, mesh=mesh, in_specs=placed, out_specs=rows, check_vma=False)
```

```python
import functools

import jax
import jax.numpy as jnp
from jax import lax
from jax.experimental import pallas as pl
from jax.experimental.pallas import tpu as pltpu
from jax.sharding import PartitionSpec as P

VMEM_LIMIT = 12 * 1024 * 1024
SPLIT = (8, 4, 4)
FIX = 16
LOG2_E = 1.4426950408889634


def drop_tokens(kernel, keep, tokens, *refs):
    kernel(*refs[:keep], *refs[keep + tokens :])


def parent_of(counts, order):
    index = jnp.arange(counts.shape[0], dtype=jnp.int32)
    bounds = jnp.sum(jnp.where(index[None, :] <= index[:, None], counts[None, :], 0), axis=1)
    return jnp.sum((bounds[None, :] <= order[:, None]).astype(jnp.int32), axis=1)


def three_terms(value):
    terms = []
    for _ in range(3):
        terms.append(value.astype(jnp.bfloat16).astype(jnp.float32))
        value = value - terms[-1]
    return jnp.concatenate(terms)


def conv_silu(padded, tail, rows, taps):
    length = rows.shape[0]
    reach = taps.shape[0] - 1
    padded[8 - reach : 8, :] = jnp.broadcast_to(tail, (reach, rows.shape[1])).astype(jnp.float32)
    padded[8 : 8 + length, :] = rows.astype(jnp.float32)
    total = padded[8 - reach : 8 - reach + length, :] * taps[0:1, :]
    for k in range(1, reach + 1):
        total = total + padded[8 - reach + k : 8 - reach + k + length, :] * taps[k : k + 1, :]
    half = 0.5 * total
    return (half + half * jnp.tanh(half)).astype(jnp.bfloat16)


def early_kernel(
    base, x_ref, b_ref, c_ref, dt_ref, bias_ref, alog_ref, skip_ref, taps_x_ref, taps_bc_ref,
    mixed_ref, c_out_ref, column_ref, first_ref, opening_ref, weights_ref, padded,
):
    length, wide = x_ref.shape[1:]
    heads = dt_ref.shape[1]
    q = base + pl.program_id(0)
    width = wide // heads
    half = length // 2

    def convolve(rows, taps, slot):
        bulk = conv_silu(padded.at[slot % 2], 0.0, rows, taps)[FIX:]
        return jnp.concatenate([jnp.zeros((FIX, rows.shape[1]), jnp.bfloat16), bulk])

    b_conv = convolve(b_ref[0], taps_bc_ref[0], 0)
    c_conv = convolve(c_ref[0], taps_bc_ref[1], 1)
    c_out_ref[q] = c_conv
    size = b_ref.shape[2]
    taps = taps_x_ref.shape[0]
    opening_ref[q, :, :wide] = x_ref[0, :FIX]
    opening_ref[q, :, wide : wide + size] = b_ref[0, :FIX]
    opening_ref[q, :, wide + size :] = c_ref[0, :FIX]
    weights_ref[q, :taps, :wide] = taps_x_ref[...]
    weights_ref[q, :taps, wide : wide + size] = taps_bc_ref[0]
    weights_ref[q, :taps, wide + size :] = taps_bc_ref[1]
    weights_ref[q, taps : taps + 1, :wide] = skip_ref[...]
    scores = lax.dot_general(
        c_conv, b_conv, (((1,), (1,)), ((), ())), preferred_element_type=jnp.float32
    )
    raw = dt_ref[0] + bias_ref[...]
    step = jnp.maximum(raw, 0.0) + jnp.log1p(jnp.exp(-jnp.abs(raw)))
    per_token = step * (-jnp.exp(alog_ref[...]))
    upper = lax.broadcasted_iota(jnp.int32, (length, length), 0) <= lax.broadcasted_iota(
        jnp.int32, (length, length), 1
    )
    sums = jnp.dot(
        three_terms(per_token).astype(jnp.bfloat16),
        upper.astype(jnp.float32).astype(jnp.bfloat16),
        preferred_element_type=jnp.float32,
    )
    total = (sums[:heads] + sums[heads : 2 * heads]) + sums[2 * heads :]
    total = total * LOG2_E
    row = total - jnp.log(step) * LOG2_E
    columns = total.T
    column_ref[q] = total
    causal = lax.broadcasted_iota(jnp.int32, (half, half), 0) >= lax.broadcasted_iota(
        jnp.int32, (half, half), 1
    )
    low = lax.broadcasted_iota(jnp.int32, (length, 2 * width), 1) < width
    for pair in range(heads // 2):
        lanes = slice(pair * 2 * width, (pair + 1) * 2 * width)
        x_conv = convolve(x_ref[0, :, lanes], taps_x_ref[:, lanes], pair)
        parts = []
        for head in (2 * pair, 2 * pair + 1):
            column = jnp.broadcast_to(columns[:, head : head + 1], (length, half))
            rows = row[head : head + 1, :]
            near = jnp.exp2(jnp.where(causal, column[:half] - rows[:, :half], -1e30))
            far = jnp.exp2(column[half:] - rows[:, :half])
            last = jnp.exp2(jnp.where(causal, column[half:] - rows[:, half:], -1e30))
            spot = slice(head * FIX, (head + 1) * FIX)
            first_ref[q, :half, spot] = near[:, :FIX]
            first_ref[q, half:, spot] = far[:, :FIX]
            top = (scores[:half, :half] * near).astype(jnp.bfloat16)
            left = (scores[half:, :half] * far).astype(jnp.bfloat16)
            right = (scores[half:, half:] * last).astype(jnp.bfloat16)
            below = jnp.concatenate([left, right], axis=1)
            parts.append(
                jnp.concatenate(
                    [
                        jnp.dot(top, x_conv[:half], preferred_element_type=jnp.float32),
                        jnp.dot(below, x_conv, preferred_element_type=jnp.float32),
                    ]
                )
            )
        mixed_ref[q, :, lanes] = jnp.where(low, parts[0], parts[1]) + skip_ref[
            :, lanes
        ] * x_conv.astype(jnp.float32)


def late_kernel(offset, heads, lines, reach, tail_at, place_ref, *refs):
    tails, states, parts, (y_ref, padded) = refs[:4], refs[4:8], refs[8:-2], refs[-2:]
    kids, length, wide = y_ref.shape
    width = wide // heads
    q = pl.program_id(0)
    far = q ^ place_ref[0]
    low_first = lax.broadcasted_iota(jnp.int32, (FIX, 2 * width), 1) < width
    contract = (((1,), (1,)), ((), ()))

    def choose(blocks):
        near = jnp.where(far == 0, blocks[0], blocks[1])
        return jnp.where(far <= 1, near, jnp.where(far == 2, blocks[2], blocks[3]))

    for kid in range(kids):
        mixed_ref, held_ref, column_ref, first_ref, opening_ref, weights_ref = parts[
            6 * kid : 6 * kid + 6
        ]
        size = held_ref.shape[2]
        per_group = column_ref.shape[1]
        group_wide = opening_ref.shape[2] - 2 * size
        tail_rows = pl.ds(tail_at, -(-lines * reach // 16) * 16)
        tail = choose([ref[kid, tail_rows] for ref in tails]).astype(jnp.float32)
        state = choose([ref[kid, : heads * width] for ref in states])

        def opening(start, stop, at):
            tap_rows = []
            for k in range(reach):
                first = k * lines + at
                count = (stop - start) // 128
                here = [tail[first + n : first + n + 1] for n in range(count)]
                tap_rows.append(jnp.concatenate(here, axis=1))
            return conv_silu(
                padded.at[kid, :, : stop - start],
                jnp.concatenate(tap_rows),
                opening_ref[q, :, start:stop],
                weights_ref[q, : reach + 1, start:stop],
            )

        bc_first = opening(group_wide, group_wide + 2 * size, lines - 2)
        b_first, c_first = bc_first[:, :size], bc_first[:, size:]
        start = offset * width
        x_all = opening(start, start + wide, start // 128).astype(jnp.float32)
        skipped = weights_ref[q, reach + 1 : reach + 2, start : start + wide] * x_all
        c_conv = jnp.concatenate([c_first, held_ref[q, FIX:]])
        terms = three_terms(jnp.exp2(column_ref[q]))
        terms = jnp.concatenate([terms, jnp.zeros((per_group, length), jnp.float32)])
        spread_row = lax.broadcasted_iota(jnp.int32, (4 * per_group, wide), 0)
        spread_lane = lax.broadcasted_iota(jnp.int32, (4 * per_group, wide), 1)
        spread = spread_row % per_group == offset + spread_lane // width
        grow = jnp.dot(
            terms.T.astype(jnp.bfloat16),
            spread.astype(jnp.float32).astype(jnp.bfloat16),
            preferred_element_type=jnp.float32,
        )
        term = lax.dot_general(c_conv, state, contract, preferred_element_type=jnp.float32)
        carried = (term * grow).astype(jnp.bfloat16)
        scores = lax.dot_general(
            c_conv,
            jnp.concatenate([b_first] * heads),
            contract,
            preferred_element_type=jnp.float32,
        )
        here = slice(offset * FIX, (offset + heads) * FIX)
        mixing = (scores * first_ref[q, :, here]).astype(jnp.bfloat16)
        for pair in range(heads // 2):
            lanes = slice(pair * 2 * width, (pair + 1) * 2 * width)
            x_first = x_all[:, lanes]
            stacked = [jnp.where(low_first, x_first, 0.0), jnp.where(low_first, 0.0, x_first)]
            if pair > 0:
                stacked = [jnp.zeros((2 * pair * FIX, 2 * width), jnp.float32)] + stacked
            if 2 * pair + 2 < heads:
                spare = (heads - 2 * pair - 2) * FIX
                stacked = stacked + [jnp.zeros((spare, 2 * width), jnp.float32)]
            part = jnp.dot(
                mixing,
                jnp.concatenate(stacked).astype(jnp.bfloat16),
                preferred_element_type=jnp.float32,
            )
            part = jnp.concatenate([part[:FIX] + skipped[:, lanes], part[FIX:]])
            whole = slice(start + lanes.start, start + lanes.stop)
            y_ref[kid, :, lanes] = (
                mixed_ref[q, :, whole] + part + carried[:, lanes].astype(jnp.float32)
            ).astype(jnp.bfloat16)


def cast_kernel(parts, tailed, reach, lines, *refs):
    count = len(tailed)
    ins, outs = refs[:-count], refs[-count:]
    states, tails = ins[: parts * count], ins[parts * count :]
    for j, out_ref in enumerate(outs):
        start = 0
        for at in range(parts):
            state = states[parts * j + at][0]
            rows = state.shape[0] * state.shape[1]
            out_ref[start : start + rows] = state.reshape(rows, state.shape[2]).astype(jnp.bfloat16)
            start += rows
            if at == 0 and tailed[j]:
                x_tail = tails[2 * j][0].astype(jnp.float32)
                bc_tail = tails[2 * j + 1][0].astype(jnp.float32)
                pieces = []
                for k in range(reach):
                    pieces += [x_tail[k : k + 1, i * 128 : i * 128 + 128] for i in range(lines - 2)]
                    pieces.append(bc_tail[k])
                spare = tailed[j] - lines * reach
                pieces.append(jnp.zeros((spare, 128), jnp.float32))
                out_ref[start : start + tailed[j]] = jnp.concatenate(pieces).astype(jnp.bfloat16)
                start += tailed[j]


def within_kernel(
    parent_ref,
    x_ref,
    b_ref,
    c_ref,
    dt_ref,
    bias_ref,
    alog_ref,
    skip_ref,
    taps_x_ref,
    taps_bc_ref,
    tail_x_ref,
    tail_bc_ref,
    mixed_ref,
    c_out_ref,
    grow_ref,
    padded,
):
    length = x_ref.shape[1]
    heads = dt_ref.shape[1]
    width = x_ref.shape[2] // heads
    b_conv = conv_silu(padded, tail_bc_ref[0, 0], b_ref[0], taps_bc_ref[0])
    c_conv = conv_silu(padded, tail_bc_ref[0, 1], c_ref[0], taps_bc_ref[1])
    c_out_ref[0] = c_conv
    scores = lax.dot_general(
        c_conv, b_conv, (((1,), (1,)), ((), ())), preferred_element_type=jnp.float32
    )
    raw = dt_ref[0] + bias_ref[...]
    step = jnp.maximum(raw, 0.0) + jnp.log1p(jnp.exp(-jnp.abs(raw)))
    per_token = step * (-jnp.exp(alog_ref[...]))
    row = lax.broadcasted_iota(jnp.int32, (length, length), 0)
    col = lax.broadcasted_iota(jnp.int32, (length, length), 1)
    upper = (row <= col).astype(jnp.float32)
    total = lax.dot_general(
        per_token,
        upper,
        (((1,), (0,)), ((), ())),
        precision=lax.Precision.HIGHEST,
        preferred_element_type=jnp.float32,
    )
    total_t = total.T
    grow_ref[0, 0] = jnp.exp(total_t)
    causal = row >= col
    low = lax.broadcasted_iota(jnp.int32, (length, 2 * width), 1) < width
    for pair in range(heads // 2):
        lanes = slice(pair * 2 * width, (pair + 1) * 2 * width)
        x_conv = conv_silu(
            padded, tail_x_ref[0, :, lanes], x_ref[0, :, lanes], taps_x_ref[:, lanes]
        )
        parts = []
        for head in (2 * pair, 2 * pair + 1):
            gap = total_t[:, head : head + 1] - total[head : head + 1, :]
            factor = jnp.exp(jnp.where(causal, gap, -1e30))
            mixing = (scores * factor * step[head : head + 1, :]).astype(jnp.bfloat16)
            parts.append(jnp.dot(mixing, x_conv, preferred_element_type=jnp.float32))
        mixed_ref[0, :, lanes] = (
            jnp.where(low, parts[0], parts[1]) + skip_ref[:, lanes] * x_conv.astype(jnp.float32)
        )


def carried_kernel(state_ref, c_ref, grow_ref, mixed_ref, y_ref):
    sources, _, part, width, size = state_ref.shape
    length = c_ref.shape[1]
    low = lax.broadcasted_iota(jnp.int32, (length, 2 * width), 1) < width
    c_conv = c_ref[0]
    for source in range(sources):
        state = state_ref[source, 0].reshape(part * width, size)
        term = lax.dot_general(
            c_conv, state, (((1,), (1,)), ((), ())), preferred_element_type=jnp.float32
        )
        for pair in range(part // 2):
            head = source * part + 2 * pair
            grow = jnp.where(
                low, grow_ref[0, 0, :, head : head + 1], grow_ref[0, 0, :, head + 1 : head + 2]
            )
            here = slice(2 * pair * width, (2 * pair + 2) * width)
            lanes = slice(head * width, (head + 2) * width)
            carried = (term[:, here] * grow).astype(jnp.bfloat16).astype(jnp.float32)
            y_ref[0, :, lanes] = (mixed_ref[0, :, lanes] + carried).astype(jnp.bfloat16)


def pick_kernel(parent_ref, state_ref, out_ref):
    out_ref[...] = state_ref[...]


def local_any(
    x_in,
    b_in,
    c_in,
    dt_in,
    dt_bias,
    a_log,
    d_skip,
    conv_x,
    conv_bc,
    par_state,
    tail_x,
    tail_bc,
    counts,
    order,
):
    kids, length, columns = x_in.shape
    heads = dt_in.shape[1]
    width, size = par_state.shape[2:]
    ways = lax.axis_size("batch")
    groups = b_in.shape[2] // size
    per_group = heads // groups
    part = heads // ways
    wide = per_group * width
    reach = tail_x.shape[1]
    parents_all = counts.shape[0]
    kids_all = order.shape[0]

    parent = parent_of(counts, order)
    own = lax.dynamic_slice_in_dim(parent, lax.axis_index("batch") * kids, kids)

    sent = par_state.astype(jnp.bfloat16).reshape(ways, part, width, size)
    shares = lax.all_to_all(sent, "batch", split_axis=0, concat_axis=0, tiled=True)

    tails = jnp.concatenate([tail_x.reshape(-1), tail_bc.reshape(-1)])
    tails = jnp.broadcast_to(tails[None], (ways, tails.shape[0]))
    tails = lax.all_to_all(tails, "batch", split_axis=0, concat_axis=0, tiled=True)
    tails_x = tails[:, : reach * columns].reshape(parents_all, reach, columns)
    tails_bc = tails[:, reach * columns :].reshape(parents_all, 2, reach, groups * size)

    picked = pl.pallas_call(
        pick_kernel,
        grid_spec=pltpu.PrefetchScalarGridSpec(
            num_scalar_prefetch=1,
            grid=(kids_all,),
            in_specs=[pl.BlockSpec((1, part, width, size), lambda i, p: (p[i], 0, 0, 0))],
            out_specs=pl.BlockSpec((1, part, width, size), lambda i, p: (i, 0, 0, 0)),
        ),
        out_shape=jax.ShapeDtypeStruct((kids_all, part, width, size), jnp.bfloat16),
        cost_estimate=pl.CostEstimate(
            flops=0, bytes_accessed=4 * kids_all * part * width * size, transcendentals=0
        ),
        name="pick_states",
    )(parent, shares)
    states = lax.all_to_all(
        picked.reshape(ways, kids, part, width, size), "batch", split_axis=0, concat_axis=0, tiled=True
    )

    skip_row = jnp.repeat(d_skip, width)[None, :]
    mixed, c_conv, grow = pl.pallas_call(
        within_kernel,
        grid_spec=pltpu.PrefetchScalarGridSpec(
            num_scalar_prefetch=1,
            grid=(kids, groups),
            in_specs=[
                pl.BlockSpec((1, length, wide), lambda c, q, p: (c, 0, q)),
                pl.BlockSpec((1, length, size), lambda c, q, p: (c, 0, q)),
                pl.BlockSpec((1, length, size), lambda c, q, p: (c, 0, q)),
                pl.BlockSpec((1, per_group, length), lambda c, q, p: (c, q, 0)),
                pl.BlockSpec((per_group, 1), lambda c, q, p: (q, 0)),
                pl.BlockSpec((per_group, 1), lambda c, q, p: (q, 0)),
                pl.BlockSpec((1, wide), lambda c, q, p: (0, q)),
                pl.BlockSpec((reach + 1, wide), lambda c, q, p: (0, q)),
                pl.BlockSpec((2, reach + 1, size), lambda c, q, p: (0, 0, q)),
                pl.BlockSpec((1, reach, wide), lambda c, q, p: (p[c], 0, q)),
                pl.BlockSpec((1, 2, reach, size), lambda c, q, p: (p[c], 0, 0, q)),
            ],
            out_specs=[
                pl.BlockSpec((1, length, wide), lambda c, q, p: (c, 0, q)),
                pl.BlockSpec((1, length, size), lambda c, q, p: (c, 0, q)),
                pl.BlockSpec((1, 1, length, per_group), lambda c, q, p: (c, q, 0, 0)),
            ],
            scratch_shapes=[pltpu.VMEM((8 + length, size), jnp.float32)],
        ),
        out_shape=[
            jax.ShapeDtypeStruct((kids, length, columns), jnp.float32),
            jax.ShapeDtypeStruct((kids, length, groups * size), jnp.bfloat16),
            jax.ShapeDtypeStruct((kids, groups, length, per_group), jnp.float32),
        ],
        compiler_params=pltpu.CompilerParams(vmem_limit_bytes=4 * VMEM_LIMIT),
        cost_estimate=pl.CostEstimate(
            flops=4 * kids * heads * length * length * width,
            bytes_accessed=6 * kids * length * columns,
            transcendentals=kids * heads * length * length,
        ),
        name="within",
    )(
        own,
        x_in,
        b_in,
        c_in,
        dt_in,
        dt_bias[:, None],
        a_log[:, None],
        skip_row,
        conv_x,
        conv_bc,
        tails_x,
        tails_bc,
    )

    sources = per_group // part
    return pl.pallas_call(
        carried_kernel,
        grid=(kids, groups),
        in_specs=[
            pl.BlockSpec((sources, 1, part, width, size), lambda c, q: (q, c, 0, 0, 0)),
            pl.BlockSpec((1, length, size), lambda c, q: (c, 0, q)),
            pl.BlockSpec((1, 1, length, per_group), lambda c, q: (c, q, 0, 0)),
            pl.BlockSpec((1, length, wide), lambda c, q: (c, 0, q)),
        ],
        out_specs=pl.BlockSpec((1, length, wide), lambda c, q: (c, 0, q)),
        out_shape=jax.ShapeDtypeStruct((kids, length, columns), jnp.bfloat16),
        compiler_params=pltpu.CompilerParams(vmem_limit_bytes=4 * VMEM_LIMIT),
        cost_estimate=pl.CostEstimate(
            flops=2 * kids * length * columns * size,
            bytes_accessed=8 * kids * length * columns,
            transcendentals=0,
        ),
        name="carried",
    )(states, c_conv, grow, mixed)


def local_halves(
    x_in, b_in, c_in, dt_in, dt_bias, a_log, d_skip, conv_x, conv_bc,
    par_state, tail_x, tail_bc, counts, order,
):
    kids, length, columns = x_in.shape
    heads = dt_in.shape[1]
    width, size = par_state.shape[2:]
    groups = b_in.shape[2] // size
    per_group = heads // groups
    wide = per_group * width
    taps = conv_x.shape[0]
    reach = taps - 1
    lines = (wide + 2 * size) // 128
    tail_lines = -(-lines * reach // 16) * 16
    params = pltpu.CompilerParams(vmem_limit_bytes=VMEM_LIMIT)
    anywhere = pl.BlockSpec(memory_space=pl.ANY)
    small = pl.CostEstimate(flops=1, bytes_accessed=1, transcendentals=0)

    stay = lambda x: pltpu.with_memory_space_constraint(x, pltpu.HBM)
    keep_in_vmem = lambda x: pltpu.with_memory_space_constraint(x, pltpu.VMEM)
    x_in, b_in, c_in, dt_in, conv_x, conv_bc = map(stay, (x_in, b_in, c_in, dt_in, conv_x, conv_bc))

    me = lax.axis_index("batch")
    parent = parent_of(counts, order)
    child = (jnp.arange(4 * kids, dtype=jnp.int32) // kids ^ me) * kids
    child = child + jnp.arange(4 * kids, dtype=jnp.int32) % kids
    catalog = jnp.arange(4 * 2 * kids, dtype=jnp.int32)
    owner = jnp.sum(jnp.where(child[:, None] == catalog[None, :], parent[None, :], 0), axis=1)
    slots = owner ^ me
    place = (me % 4).astype(jnp.int32)[None]

    state = stay(par_state.reshape(groups, per_group, width, size))
    x_tails, bc_tails = stay(tail_x), stay(tail_bc.transpose(0, 2, 1, 3))
    offsets = [sum(SPLIT[:k]) for k in range(len(SPLIT))]

    def swap(value, r):
        return lax.ppermute(value, "batch", perm=[(i, i ^ r) for i in range(8)])

    def cast():
        rows = per_group * width + tail_lines
        rows_a = SPLIT[0] * width + tail_lines
        count = len(SPLIT) + 2

        def kernel(place_ref, *refs):
            ins, outs = refs[: 4 * count], refs[4 * count :]
            for n in range(4):
                cast_kernel(
                    len(SPLIT), [tail_lines], reach, lines, *ins[count * n : count * n + count], outs[n]
                )
                outs[4 + n // 2][n % 2] = outs[n][:rows_a]

        operands, specs = [], []
        for n in range(4):
            for part, offset in zip(SPLIT, offsets):
                operands.append(state)
                specs.append(
                    pl.BlockSpec(
                        (1, part, width, size),
                        lambda i, p, n=n, at=offset // part: (p[0] ^ n, at, 0, 0),
                    )
                )
            operands += [x_tails, bc_tails]
            specs += [
                pl.BlockSpec((1, reach, wide), lambda i, p, n=n: (0, 0, p[0] ^ n)),
                pl.BlockSpec((1, reach, 2, size), lambda i, p, n=n: (0, 0, 0, p[0] ^ n)),
            ]
        shapes = [(rows, size)] * 4 + [(2, rows_a, size)] * 2
        return pl.pallas_call(
            kernel,
            grid_spec=pltpu.PrefetchScalarGridSpec(
                num_scalar_prefetch=1,
                grid=(1,),
                in_specs=specs,
                out_specs=[pl.BlockSpec(memory_space=pltpu.VMEM)] * len(shapes),
            ),
            out_shape=[pltpu.VMEM(shape, jnp.bfloat16) for shape in shapes],
            compiler_params=params,
            cost_estimate=small,
            name="cast_states",
        )(place, *operands)

    def rearrange(scalars, sources, moves, shapes, tokens, name):
        def kernel(scalars_ref, *refs):
            held, outs, sems = refs[: len(sources)], refs[len(sources) : -1], refs[-1]

            def copy(move, source):
                out, at, _, _ = moves[move]
                number, take = source
                ref = held[number].at[take] if take is not None else held[number]
                target = outs[out].at[at] if at is not None else outs[out]
                return pltpu.make_async_copy(ref, target, sems.at[move])

            for move, (_, _, scalar, choices) in enumerate(moves):
                if scalar is None:
                    copy(move, choices[0]).start()
                    continue
                for value, source in enumerate(choices):

                    @pl.when(scalars_ref[scalar] == value)
                    def _(move=move, source=source):
                        copy(move, source).start()

            for move in range(len(moves)):
                copy(move, moves[move][3][0]).wait()

        return pl.pallas_call(
            functools.partial(drop_tokens, kernel, 1 + len(sources), len(tokens)),
            grid_spec=pltpu.PrefetchScalarGridSpec(
                num_scalar_prefetch=1,
                grid=(1,),
                in_specs=[anywhere] * (len(sources) + len(tokens)),
                out_specs=[pl.BlockSpec(memory_space=pltpu.VMEM)] * len(shapes),
                scratch_shapes=[pltpu.SemaphoreType.DMA((len(moves),))],
            ),
            out_shape=[pltpu.VMEM(shape, jnp.bfloat16) for shape in shapes],
            compiler_params=params,
            cost_estimate=small,
            name=name,
        )(scalars, *sources, *tokens)

    def pick(rows, sources, choices, tokens):
        moves = [
            (j, kid, j * kids + kid, choices) for j in range(4) for kid in range(kids)
        ]
        picked = rearrange(
            slots, sources, moves, [(kids, rows, size)] * 4, tokens, "pick_states"
        )
        return [picked[0]] + [swap(picked[j], j) for j in range(1, 4)]

    def early(c, piece, before, tokens):
        per = groups // 2
        at = lambda q: (c, 0, per * piece + q)
        operands = [
            x_in, b_in, c_in, dt_in, dt_bias[:, None], a_log[:, None], skip_row, conv_x, conv_bc
        ]
        keep = len(operands)
        tokens = list(tokens) + [keep_in_vmem(a) for a in before]
        first = keep + len(tokens) - len(before)
        return pl.pallas_call(
            functools.partial(
                drop_tokens, functools.partial(early_kernel, per * piece), keep, len(tokens)
            ),
            grid=(per,),
            in_specs=[
                pl.BlockSpec((1, length, wide), at),
                pl.BlockSpec((1, length, size), at),
                pl.BlockSpec((1, length, size), at),
                pl.BlockSpec((1, per_group, length), lambda q: (c, per * piece + q, 0)),
                pl.BlockSpec((per_group, 1), lambda q: (per * piece + q, 0)),
                pl.BlockSpec((per_group, 1), lambda q: (per * piece + q, 0)),
                pl.BlockSpec((1, wide), lambda q: (0, per * piece + q)),
                pl.BlockSpec((taps, wide), lambda q: (0, per * piece + q)),
                pl.BlockSpec((2, taps, size), lambda q: (0, 0, per * piece + q)),
                *[anywhere] * len(tokens),
            ],
            out_specs=[pl.BlockSpec(memory_space=pltpu.VMEM)] * 6,
            out_shape=[
                pltpu.VMEM((groups, length, wide), jnp.float32),
                pltpu.VMEM((groups, length, size), jnp.bfloat16),
                pltpu.VMEM((groups, per_group, length), jnp.float32),
                pltpu.VMEM((groups, length, per_group * FIX), jnp.float32),
                pltpu.VMEM((groups, FIX, wide + 2 * size), jnp.bfloat16),
                pltpu.VMEM((groups, 8, wide + 2 * size), jnp.float32),
            ],
            input_output_aliases={first + i: i for i in range(len(before))},
            scratch_shapes=[pltpu.VMEM((2, 8 + length, size), jnp.float32)],
            compiler_params=params,
            cost_estimate=small,
            name="early",
        )(*operands, *tokens)

    def late(k, states, states_first, parts, result, tokens):
        part, offset = SPLIT[k], offsets[k]
        chunk = part * width
        lane = lambda q, p: (0, 0, q * (per_group // part) + offset // part)
        operands = [keep_in_vmem(a) for a in (*states_first, *states, *parts[0], *parts[1])]
        specs = [pl.BlockSpec(memory_space=pltpu.VMEM)] * len(operands)
        keep = 1 + len(operands)
        operands += tokens
        specs += [anywhere] * len(tokens)
        alias = {}
        if result is not None:
            alias = {1 + len(operands): 0}
            operands.append(result)
            specs.append(anywhere)
        kernel = functools.partial(late_kernel, offset, part, lines, reach, SPLIT[0] * width)
        return pl.pallas_call(
            functools.partial(drop_tokens, kernel, keep, 1 + len(operands) - keep),
            grid_spec=pltpu.PrefetchScalarGridSpec(
                num_scalar_prefetch=1,
                grid=(groups,),
                in_specs=specs,
                out_specs=pl.BlockSpec((kids, length, chunk), lane),
                scratch_shapes=[pltpu.VMEM((kids, 8 + FIX, max(chunk, 2 * size)), jnp.float32)],
            ),
            out_shape=jax.ShapeDtypeStruct(x_in.shape, jnp.bfloat16),
            input_output_aliases=alias,
            compiler_params=params,
            cost_estimate=small,
            name="late",
        )(place, *operands)

    skip_row = jnp.repeat(d_skip, width)[None, :]
    rows = [SPLIT[0] * width + tail_lines] + [part * width for part in SPLIT[1:]]
    chunks = [pl.ds(sum(rows[:k]), rows[k]) for k in range(len(SPLIT))]
    *own, sent_4, sent_6 = cast()
    crossed_a = [swap(sent_4, 4), swap(sent_6, 6)]
    inside = [own[0]] + [swap(own[j], j) for j in range(1, 4)]

    def cross(k, tokens):
        moves = [(0, j, None, [(j, chunks[k])]) for j in range(4)]
        (sent,) = rearrange(place, inside, moves, [(4, rows[k], size)], tokens, "stack_later")
        return sent, swap(sent, 4)

    def pick_later(k, crossed, tokens):
        choices = [(j, chunks[k]) for j in range(4)] + [(4, j) for j in range(4)]
        return pick(rows[k], [*inside, crossed], choices, tokens)

    first = early(0, 0, [], [own[0], slots])
    first = early(0, 1, first, [])
    second = early(1, 0, [], [first[1]])
    sent_b, crossed_b = cross(1, [second[1], *crossed_a])
    moves = [(0, n, None, [(n, 1)]) for n in range(2)]
    (spread,) = rearrange(place, crossed_a, moves, [(2, rows[0], size)], [sent_b], "stack_first")
    passed = swap(spread, 1)
    choices = [(j, chunks[0]) for j in range(4)] + [(4, 0), (6, 0), (5, 0), (6, 1)]
    states_a = pick(rows[0], [*inside, *crossed_a, passed], choices, [])
    sent_c, crossed_c = cross(2, [states_a[0], crossed_b])
    states_b = pick_later(1, crossed_b, [sent_c])
    second = early(1, 1, second, [states_b[0]])
    states_c = pick_later(2, crossed_c, [second[1]])
    parts = [first, second]
    result = late(0, states_a, states_a, parts, None, [states_c[0]])
    result = late(1, states_b, states_a, parts, result, [])
    return late(2, states_c, states_a, parts, result, [])


def solution(mesh):
    rows, cols = P(("groups", "batch"), None, "head"), P(("groups", "batch"), "head")
    placed = (
        rows, rows, rows, cols, P("head"), P("head"), P("head"), P(None, "head"),
        P(None, None, "head"), cols, rows, P(("groups", "batch"), None, None, "head"),
        P("groups"), P("groups"),
    )
    local = local_halves if mesh.shape["batch"] == 8 else local_any
    return jax.shard_map(local, mesh=mesh, in_specs=placed, out_specs=rows, check_vma=False)
```

```python
import functools

import jax
import jax.numpy as jnp
from jax import lax
from jax.experimental import pallas as pl
from jax.experimental.pallas import tpu as pltpu
from jax.sharding import PartitionSpec as P

VMEM_LIMIT = 12 * 1024 * 1024
SPLIT = (8, 4, 4)
FIX = 16
LOG2_E = 1.4426950408889634


def drop_tokens(kernel, keep, tokens, *refs):
    kernel(*refs[:keep], *refs[keep + tokens :])


def parent_of(counts, order):
    index = jnp.arange(counts.shape[0], dtype=jnp.int32)
    bounds = jnp.sum(jnp.where(index[None, :] <= index[:, None], counts[None, :], 0), axis=1)
    return jnp.sum((bounds[None, :] <= order[:, None]).astype(jnp.int32), axis=1)


def three_terms(value):
    terms = []
    for _ in range(3):
        terms.append(value.astype(jnp.bfloat16).astype(jnp.float32))
        value = value - terms[-1]
    return jnp.concatenate(terms)


def conv_silu(padded, tail, rows, taps):
    length = rows.shape[0]
    reach = taps.shape[0] - 1
    padded[8 - reach : 8, :] = jnp.broadcast_to(tail, (reach, rows.shape[1])).astype(jnp.float32)
    padded[8 : 8 + length, :] = rows.astype(jnp.float32)
    total = padded[8 - reach : 8 - reach + length, :] * taps[0:1, :]
    for k in range(1, reach + 1):
        total = total + padded[8 - reach + k : 8 - reach + k + length, :] * taps[k : k + 1, :]
    half = 0.5 * total
    return (half + half * jnp.tanh(half)).astype(jnp.bfloat16)


def early_kernel(
    base, x_ref, b_ref, c_ref, dt_ref, bias_ref, alog_ref, skip_ref, taps_x_ref, taps_bc_ref,
    mixed_ref, c_out_ref, column_ref, first_ref, opening_ref, weights_ref, padded,
):
    length, wide = x_ref.shape[1:]
    heads = dt_ref.shape[1]
    q = base + pl.program_id(0)
    width = wide // heads
    half = length // 2

    def convolve(rows, taps, slot):
        bulk = conv_silu(padded.at[slot % 2], 0.0, rows, taps)[FIX:]
        return jnp.concatenate([jnp.zeros((FIX, rows.shape[1]), jnp.bfloat16), bulk])

    b_conv = convolve(b_ref[0], taps_bc_ref[0], 0)
    c_conv = convolve(c_ref[0], taps_bc_ref[1], 1)
    c_out_ref[q] = c_conv
    size = b_ref.shape[2]
    taps = taps_x_ref.shape[0]
    opening_ref[q, :, :wide] = x_ref[0, :FIX]
    opening_ref[q, :, wide : wide + size] = b_ref[0, :FIX]
    opening_ref[q, :, wide + size :] = c_ref[0, :FIX]
    weights_ref[q, :taps, :wide] = taps_x_ref[...]
    weights_ref[q, :taps, wide : wide + size] = taps_bc_ref[0]
    weights_ref[q, :taps, wide + size :] = taps_bc_ref[1]
    weights_ref[q, taps : taps + 1, :wide] = skip_ref[...]
    scores = lax.dot_general(
        c_conv, b_conv, (((1,), (1,)), ((), ())), preferred_element_type=jnp.float32
    )
    raw = dt_ref[0] + bias_ref[...]
    step = jnp.maximum(raw, 0.0) + jnp.log1p(jnp.exp(-jnp.abs(raw)))
    per_token = step * (-jnp.exp(alog_ref[...]))
    upper = lax.broadcasted_iota(jnp.int32, (length, length), 0) <= lax.broadcasted_iota(
        jnp.int32, (length, length), 1
    )
    sums = jnp.dot(
        three_terms(per_token).astype(jnp.bfloat16),
        upper.astype(jnp.float32).astype(jnp.bfloat16),
        preferred_element_type=jnp.float32,
    )
    total = (sums[:heads] + sums[heads : 2 * heads]) + sums[2 * heads :]
    total = total * LOG2_E
    row = total - jnp.log(step) * LOG2_E
    columns = total.T
    column_ref[q] = total
    causal = lax.broadcasted_iota(jnp.int32, (half, half), 0) >= lax.broadcasted_iota(
        jnp.int32, (half, half), 1
    )
    low = lax.broadcasted_iota(jnp.int32, (length, 2 * width), 1) < width
    for pair in range(heads // 2):
        lanes = slice(pair * 2 * width, (pair + 1) * 2 * width)
        x_conv = convolve(x_ref[0, :, lanes], taps_x_ref[:, lanes], pair)
        parts = []
        for head in (2 * pair, 2 * pair + 1):
            column = jnp.broadcast_to(columns[:, head : head + 1], (length, half))
            rows = row[head : head + 1, :]
            near = jnp.exp2(jnp.where(causal, column[:half] - rows[:, :half], -1e30))
            far = jnp.exp2(column[half:] - rows[:, :half])
            last = jnp.exp2(jnp.where(causal, column[half:] - rows[:, half:], -1e30))
            spot = slice(head * FIX, (head + 1) * FIX)
            first_ref[q, :half, spot] = near[:, :FIX]
            first_ref[q, half:, spot] = far[:, :FIX]
            top = (scores[:half, :half] * near).astype(jnp.bfloat16)
            left = (scores[half:, :half] * far).astype(jnp.bfloat16)
            right = (scores[half:, half:] * last).astype(jnp.bfloat16)
            below = jnp.concatenate([left, right], axis=1)
            parts.append(
                jnp.concatenate(
                    [
                        jnp.dot(top, x_conv[:half], preferred_element_type=jnp.float32),
                        jnp.dot(below, x_conv, preferred_element_type=jnp.float32),
                    ]
                )
            )
        mixed_ref[q, :, lanes] = jnp.where(low, parts[0], parts[1]) + skip_ref[
            :, lanes
        ] * x_conv.astype(jnp.float32)


def late_kernel(offset, heads, lines, reach, tail_at, place_ref, *refs):
    tails, states, parts = refs[:4], refs[4:8], refs[8:-4]
    y_ref, padded, y_part, sems = refs[-4:]
    _, kids, length, wide = y_part.shape
    width = wide // heads
    low_first = lax.broadcasted_iota(jnp.int32, (FIX, 2 * width), 1) < width
    contract = (((1,), (1,)), ((), ()))

    def add(j, kid):
        q = place_ref[0] ^ j
        mixed_ref, held_ref, column_ref, first_ref, opening_ref, weights_ref = parts[
            6 * kid : 6 * kid + 6
        ]
        size = held_ref.shape[2]
        per_group = column_ref.shape[1]
        group_wide = opening_ref.shape[2] - 2 * size
        tail_rows = pl.ds(tail_at, -(-lines * reach // 16) * 16)
        tail = tails[j][kid, tail_rows].astype(jnp.float32)
        state = states[j][kid, : heads * width]

        def opening(start, stop, at):
            tap_rows = []
            for k in range(reach):
                first = k * lines + at
                count = (stop - start) // 128
                here = [tail[first + n : first + n + 1] for n in range(count)]
                tap_rows.append(jnp.concatenate(here, axis=1))
            return conv_silu(
                padded.at[j, kid, :, : stop - start],
                jnp.concatenate(tap_rows),
                opening_ref[q, :, start:stop],
                weights_ref[q, : reach + 1, start:stop],
            )

        bc_first = opening(group_wide, group_wide + 2 * size, lines - 2)
        b_first, c_first = bc_first[:, :size], bc_first[:, size:]
        start = offset * width
        x_all = opening(start, start + wide, start // 128).astype(jnp.float32)
        skipped = weights_ref[q, reach + 1 : reach + 2, start : start + wide] * x_all
        c_conv = jnp.concatenate([c_first, held_ref[q, FIX:]])
        terms = three_terms(jnp.exp2(column_ref[q]))
        terms = jnp.concatenate([terms, jnp.zeros((per_group, length), jnp.float32)])
        spread_row = lax.broadcasted_iota(jnp.int32, (4 * per_group, wide), 0)
        spread_lane = lax.broadcasted_iota(jnp.int32, (4 * per_group, wide), 1)
        spread = spread_row % per_group == offset + spread_lane // width
        grow = jnp.dot(
            terms.T.astype(jnp.bfloat16),
            spread.astype(jnp.float32).astype(jnp.bfloat16),
            preferred_element_type=jnp.float32,
        )
        term = lax.dot_general(c_conv, state, contract, preferred_element_type=jnp.float32)
        carried = (term * grow).astype(jnp.bfloat16)
        scores = lax.dot_general(
            c_conv,
            jnp.concatenate([b_first] * heads),
            contract,
            preferred_element_type=jnp.float32,
        )
        here = slice(offset * FIX, (offset + heads) * FIX)
        mixing = (scores * first_ref[q, :, here]).astype(jnp.bfloat16)
        for pair in range(heads // 2):
            lanes = slice(pair * 2 * width, (pair + 1) * 2 * width)
            x_first = x_all[:, lanes]
            stacked = [jnp.where(low_first, x_first, 0.0), jnp.where(low_first, 0.0, x_first)]
            if pair > 0:
                stacked = [jnp.zeros((2 * pair * FIX, 2 * width), jnp.float32)] + stacked
            if 2 * pair + 2 < heads:
                spare = (heads - 2 * pair - 2) * FIX
                stacked = stacked + [jnp.zeros((spare, 2 * width), jnp.float32)]
            part = jnp.dot(
                mixing,
                jnp.concatenate(stacked).astype(jnp.bfloat16),
                preferred_element_type=jnp.float32,
            )
            part = jnp.concatenate([part[:FIX] + skipped[:, lanes], part[FIX:]])
            whole = slice(start + lanes.start, start + lanes.stop)
            y_part[j, kid, :, lanes] = (
                mixed_ref[q, :, whole] + part + carried[:, lanes].astype(jnp.float32)
            ).astype(jnp.bfloat16)

    copies = []
    for j in range(4):
        for kid in range(kids):
            add(j, kid)
        start = (place_ref[0] ^ j) * (y_ref.shape[2] // 4) + offset * width
        lanes = pl.ds(pl.multiple_of(start, 128), wide)
        copies.append(pltpu.make_async_copy(y_part.at[j], y_ref.at[:, :, lanes], sems.at[j]))
        copies[-1].start()
    for copy in copies:
        copy.wait()


def cast_kernel(parts, tailed, reach, lines, *refs):
    count = len(tailed)
    ins, outs = refs[:-count], refs[-count:]
    states, tails = ins[: parts * count], ins[parts * count :]
    for j, out_ref in enumerate(outs):
        start = 0
        for at in range(parts):
            state = states[parts * j + at][0]
            rows = state.shape[0] * state.shape[1]
            out_ref[start : start + rows] = state.reshape(rows, state.shape[2]).astype(jnp.bfloat16)
            start += rows
            if at == 0 and tailed[j]:
                x_tail = tails[2 * j][0].astype(jnp.float32)
                bc_tail = tails[2 * j + 1][0].astype(jnp.float32)
                pieces = []
                for k in range(reach):
                    pieces += [x_tail[k : k + 1, i * 128 : i * 128 + 128] for i in range(lines - 2)]
                    pieces.append(bc_tail[k])
                spare = tailed[j] - lines * reach
                pieces.append(jnp.zeros((spare, 128), jnp.float32))
                out_ref[start : start + tailed[j]] = jnp.concatenate(pieces).astype(jnp.bfloat16)
                start += tailed[j]


def within_kernel(
    parent_ref,
    x_ref,
    b_ref,
    c_ref,
    dt_ref,
    bias_ref,
    alog_ref,
    skip_ref,
    taps_x_ref,
    taps_bc_ref,
    tail_x_ref,
    tail_bc_ref,
    mixed_ref,
    c_out_ref,
    grow_ref,
    padded,
):
    length = x_ref.shape[1]
    heads = dt_ref.shape[1]
    width = x_ref.shape[2] // heads
    b_conv = conv_silu(padded, tail_bc_ref[0, 0], b_ref[0], taps_bc_ref[0])
    c_conv = conv_silu(padded, tail_bc_ref[0, 1], c_ref[0], taps_bc_ref[1])
    c_out_ref[0] = c_conv
    scores = lax.dot_general(
        c_conv, b_conv, (((1,), (1,)), ((), ())), preferred_element_type=jnp.float32
    )
    raw = dt_ref[0] + bias_ref[...]
    step = jnp.maximum(raw, 0.0) + jnp.log1p(jnp.exp(-jnp.abs(raw)))
    per_token = step * (-jnp.exp(alog_ref[...]))
    row = lax.broadcasted_iota(jnp.int32, (length, length), 0)
    col = lax.broadcasted_iota(jnp.int32, (length, length), 1)
    upper = (row <= col).astype(jnp.float32)
    total = lax.dot_general(
        per_token,
        upper,
        (((1,), (0,)), ((), ())),
        precision=lax.Precision.HIGHEST,
        preferred_element_type=jnp.float32,
    )
    total_t = total.T
    grow_ref[0, 0] = jnp.exp(total_t)
    causal = row >= col
    low = lax.broadcasted_iota(jnp.int32, (length, 2 * width), 1) < width
    for pair in range(heads // 2):
        lanes = slice(pair * 2 * width, (pair + 1) * 2 * width)
        x_conv = conv_silu(
            padded, tail_x_ref[0, :, lanes], x_ref[0, :, lanes], taps_x_ref[:, lanes]
        )
        parts = []
        for head in (2 * pair, 2 * pair + 1):
            gap = total_t[:, head : head + 1] - total[head : head + 1, :]
            factor = jnp.exp(jnp.where(causal, gap, -1e30))
            mixing = (scores * factor * step[head : head + 1, :]).astype(jnp.bfloat16)
            parts.append(jnp.dot(mixing, x_conv, preferred_element_type=jnp.float32))
        mixed_ref[0, :, lanes] = (
            jnp.where(low, parts[0], parts[1]) + skip_ref[:, lanes] * x_conv.astype(jnp.float32)
        )


def carried_kernel(state_ref, c_ref, grow_ref, mixed_ref, y_ref):
    sources, _, part, width, size = state_ref.shape
    length = c_ref.shape[1]
    low = lax.broadcasted_iota(jnp.int32, (length, 2 * width), 1) < width
    c_conv = c_ref[0]
    for source in range(sources):
        state = state_ref[source, 0].reshape(part * width, size)
        term = lax.dot_general(
            c_conv, state, (((1,), (1,)), ((), ())), preferred_element_type=jnp.float32
        )
        for pair in range(part // 2):
            head = source * part + 2 * pair
            grow = jnp.where(
                low, grow_ref[0, 0, :, head : head + 1], grow_ref[0, 0, :, head + 1 : head + 2]
            )
            here = slice(2 * pair * width, (2 * pair + 2) * width)
            lanes = slice(head * width, (head + 2) * width)
            carried = (term[:, here] * grow).astype(jnp.bfloat16).astype(jnp.float32)
            y_ref[0, :, lanes] = (mixed_ref[0, :, lanes] + carried).astype(jnp.bfloat16)


def pick_kernel(parent_ref, state_ref, out_ref):
    out_ref[...] = state_ref[...]


def local_any(
    x_in,
    b_in,
    c_in,
    dt_in,
    dt_bias,
    a_log,
    d_skip,
    conv_x,
    conv_bc,
    par_state,
    tail_x,
    tail_bc,
    counts,
    order,
):
    kids, length, columns = x_in.shape
    heads = dt_in.shape[1]
    width, size = par_state.shape[2:]
    ways = lax.axis_size("batch")
    groups = b_in.shape[2] // size
    per_group = heads // groups
    part = heads // ways
    wide = per_group * width
    reach = tail_x.shape[1]
    parents_all = counts.shape[0]
    kids_all = order.shape[0]

    parent = parent_of(counts, order)
    own = lax.dynamic_slice_in_dim(parent, lax.axis_index("batch") * kids, kids)

    sent = par_state.astype(jnp.bfloat16).reshape(ways, part, width, size)
    shares = lax.all_to_all(sent, "batch", split_axis=0, concat_axis=0, tiled=True)

    tails = jnp.concatenate([tail_x.reshape(-1), tail_bc.reshape(-1)])
    tails = jnp.broadcast_to(tails[None], (ways, tails.shape[0]))
    tails = lax.all_to_all(tails, "batch", split_axis=0, concat_axis=0, tiled=True)
    tails_x = tails[:, : reach * columns].reshape(parents_all, reach, columns)
    tails_bc = tails[:, reach * columns :].reshape(parents_all, 2, reach, groups * size)

    picked = pl.pallas_call(
        pick_kernel,
        grid_spec=pltpu.PrefetchScalarGridSpec(
            num_scalar_prefetch=1,
            grid=(kids_all,),
            in_specs=[pl.BlockSpec((1, part, width, size), lambda i, p: (p[i], 0, 0, 0))],
            out_specs=pl.BlockSpec((1, part, width, size), lambda i, p: (i, 0, 0, 0)),
        ),
        out_shape=jax.ShapeDtypeStruct((kids_all, part, width, size), jnp.bfloat16),
        cost_estimate=pl.CostEstimate(
            flops=0, bytes_accessed=4 * kids_all * part * width * size, transcendentals=0
        ),
        name="pick_states",
    )(parent, shares)
    states = lax.all_to_all(
        picked.reshape(ways, kids, part, width, size), "batch", split_axis=0, concat_axis=0, tiled=True
    )

    skip_row = jnp.repeat(d_skip, width)[None, :]
    mixed, c_conv, grow = pl.pallas_call(
        within_kernel,
        grid_spec=pltpu.PrefetchScalarGridSpec(
            num_scalar_prefetch=1,
            grid=(kids, groups),
            in_specs=[
                pl.BlockSpec((1, length, wide), lambda c, q, p: (c, 0, q)),
                pl.BlockSpec((1, length, size), lambda c, q, p: (c, 0, q)),
                pl.BlockSpec((1, length, size), lambda c, q, p: (c, 0, q)),
                pl.BlockSpec((1, per_group, length), lambda c, q, p: (c, q, 0)),
                pl.BlockSpec((per_group, 1), lambda c, q, p: (q, 0)),
                pl.BlockSpec((per_group, 1), lambda c, q, p: (q, 0)),
                pl.BlockSpec((1, wide), lambda c, q, p: (0, q)),
                pl.BlockSpec((reach + 1, wide), lambda c, q, p: (0, q)),
                pl.BlockSpec((2, reach + 1, size), lambda c, q, p: (0, 0, q)),
                pl.BlockSpec((1, reach, wide), lambda c, q, p: (p[c], 0, q)),
                pl.BlockSpec((1, 2, reach, size), lambda c, q, p: (p[c], 0, 0, q)),
            ],
            out_specs=[
                pl.BlockSpec((1, length, wide), lambda c, q, p: (c, 0, q)),
                pl.BlockSpec((1, length, size), lambda c, q, p: (c, 0, q)),
                pl.BlockSpec((1, 1, length, per_group), lambda c, q, p: (c, q, 0, 0)),
            ],
            scratch_shapes=[pltpu.VMEM((8 + length, size), jnp.float32)],
        ),
        out_shape=[
            jax.ShapeDtypeStruct((kids, length, columns), jnp.float32),
            jax.ShapeDtypeStruct((kids, length, groups * size), jnp.bfloat16),
            jax.ShapeDtypeStruct((kids, groups, length, per_group), jnp.float32),
        ],
        compiler_params=pltpu.CompilerParams(vmem_limit_bytes=4 * VMEM_LIMIT),
        cost_estimate=pl.CostEstimate(
            flops=4 * kids * heads * length * length * width,
            bytes_accessed=6 * kids * length * columns,
            transcendentals=kids * heads * length * length,
        ),
        name="within",
    )(
        own,
        x_in,
        b_in,
        c_in,
        dt_in,
        dt_bias[:, None],
        a_log[:, None],
        skip_row,
        conv_x,
        conv_bc,
        tails_x,
        tails_bc,
    )

    sources = per_group // part
    return pl.pallas_call(
        carried_kernel,
        grid=(kids, groups),
        in_specs=[
            pl.BlockSpec((sources, 1, part, width, size), lambda c, q: (q, c, 0, 0, 0)),
            pl.BlockSpec((1, length, size), lambda c, q: (c, 0, q)),
            pl.BlockSpec((1, 1, length, per_group), lambda c, q: (c, q, 0, 0)),
            pl.BlockSpec((1, length, wide), lambda c, q: (c, 0, q)),
        ],
        out_specs=pl.BlockSpec((1, length, wide), lambda c, q: (c, 0, q)),
        out_shape=jax.ShapeDtypeStruct((kids, length, columns), jnp.bfloat16),
        compiler_params=pltpu.CompilerParams(vmem_limit_bytes=4 * VMEM_LIMIT),
        cost_estimate=pl.CostEstimate(
            flops=2 * kids * length * columns * size,
            bytes_accessed=8 * kids * length * columns,
            transcendentals=0,
        ),
        name="carried",
    )(states, c_conv, grow, mixed)


def local_halves(
    x_in, b_in, c_in, dt_in, dt_bias, a_log, d_skip, conv_x, conv_bc,
    par_state, tail_x, tail_bc, counts, order,
):
    kids, length, columns = x_in.shape
    heads = dt_in.shape[1]
    width, size = par_state.shape[2:]
    groups = b_in.shape[2] // size
    per_group = heads // groups
    wide = per_group * width
    taps = conv_x.shape[0]
    reach = taps - 1
    lines = (wide + 2 * size) // 128
    tail_lines = -(-lines * reach // 16) * 16
    params = pltpu.CompilerParams(vmem_limit_bytes=VMEM_LIMIT)
    anywhere = pl.BlockSpec(memory_space=pl.ANY)
    small = pl.CostEstimate(flops=1, bytes_accessed=1, transcendentals=0)

    stay = lambda x: pltpu.with_memory_space_constraint(x, pltpu.HBM)
    keep_in_vmem = lambda x: pltpu.with_memory_space_constraint(x, pltpu.VMEM)
    x_in, b_in, c_in, dt_in, conv_x, conv_bc = map(stay, (x_in, b_in, c_in, dt_in, conv_x, conv_bc))

    me = lax.axis_index("batch")
    parent = parent_of(counts, order)
    child = (jnp.arange(4 * kids, dtype=jnp.int32) // kids ^ me) * kids
    child = child + jnp.arange(4 * kids, dtype=jnp.int32) % kids
    catalog = jnp.arange(4 * 2 * kids, dtype=jnp.int32)
    owner = jnp.sum(jnp.where(child[:, None] == catalog[None, :], parent[None, :], 0), axis=1)
    slots = owner ^ me
    place = (me % 4).astype(jnp.int32)[None]

    state = stay(par_state.reshape(groups, per_group, width, size))
    x_tails, bc_tails = stay(tail_x), stay(tail_bc.transpose(0, 2, 1, 3))
    offsets = [sum(SPLIT[:k]) for k in range(len(SPLIT))]

    def swap(value, r):
        return lax.ppermute(value, "batch", perm=[(i, i ^ r) for i in range(8)])

    def cast():
        rows = per_group * width + tail_lines
        rows_a = SPLIT[0] * width + tail_lines
        count = len(SPLIT) + 2

        def kernel(place_ref, *refs):
            ins, outs = refs[: 4 * count], refs[4 * count :]
            for n in range(4):
                cast_kernel(
                    len(SPLIT), [tail_lines], reach, lines, *ins[count * n : count * n + count], outs[n]
                )
                outs[4 + n // 2][n % 2] = outs[n][:rows_a]

        operands, specs = [], []
        for n in range(4):
            for part, offset in zip(SPLIT, offsets):
                operands.append(state)
                specs.append(
                    pl.BlockSpec(
                        (1, part, width, size),
                        lambda i, p, n=n, at=offset // part: (p[0] ^ n, at, 0, 0),
                    )
                )
            operands += [x_tails, bc_tails]
            specs += [
                pl.BlockSpec((1, reach, wide), lambda i, p, n=n: (0, 0, p[0] ^ n)),
                pl.BlockSpec((1, reach, 2, size), lambda i, p, n=n: (0, 0, 0, p[0] ^ n)),
            ]
        shapes = [(rows, size)] * 4 + [(2, rows_a, size)] * 2
        return pl.pallas_call(
            kernel,
            grid_spec=pltpu.PrefetchScalarGridSpec(
                num_scalar_prefetch=1,
                grid=(1,),
                in_specs=specs,
                out_specs=[pl.BlockSpec(memory_space=pltpu.VMEM)] * len(shapes),
            ),
            out_shape=[pltpu.VMEM(shape, jnp.bfloat16) for shape in shapes],
            compiler_params=params,
            cost_estimate=small,
            name="cast_states",
        )(place, *operands)

    def rearrange(scalars, sources, moves, shapes, tokens, name):
        def kernel(scalars_ref, *refs):
            held, outs = refs[: len(sources)], refs[len(sources) :]
            for out, at, scalar, choices in moves:
                for value, (number, take) in enumerate(choices):

                    def copy(out=out, at=at, number=number, take=take):
                        rows = held[number][...] if take is None else held[number][take]
                        if at is None:
                            outs[out][...] = rows
                        else:
                            outs[out][at] = rows

                    if scalar is None:
                        copy()
                    else:
                        pl.when(scalars_ref[scalar] == value)(copy)

        return pl.pallas_call(
            functools.partial(drop_tokens, kernel, 1 + len(sources), len(tokens)),
            grid_spec=pltpu.PrefetchScalarGridSpec(
                num_scalar_prefetch=1,
                grid=(1,),
                in_specs=[pl.BlockSpec(memory_space=pltpu.VMEM)] * len(sources)
                + [anywhere] * len(tokens),
                out_specs=[pl.BlockSpec(memory_space=pltpu.VMEM)] * len(shapes),
            ),
            out_shape=[pltpu.VMEM(shape, jnp.bfloat16) for shape in shapes],
            compiler_params=params,
            cost_estimate=small,
            name=name,
        )(scalars, *map(keep_in_vmem, sources), *tokens)

    def pick(rows, sources, choices, tokens):
        moves = [
            (j, kid, j * kids + kid, choices) for j in range(4) for kid in range(kids)
        ]
        picked = rearrange(
            slots, sources, moves, [(kids, rows, size)] * 4, tokens, "pick_states"
        )
        return [picked[0]] + [swap(picked[j], j) for j in range(1, 4)]

    def early(c, piece, before, tokens):
        per = groups // 2
        at = lambda q: (c, 0, per * piece + q)
        operands = [
            x_in, b_in, c_in, dt_in, dt_bias[:, None], a_log[:, None], skip_row, conv_x, conv_bc
        ]
        keep = len(operands)
        tokens = list(tokens) + [keep_in_vmem(a) for a in before]
        first = keep + len(tokens) - len(before)
        return pl.pallas_call(
            functools.partial(
                drop_tokens, functools.partial(early_kernel, per * piece), keep, len(tokens)
            ),
            grid=(per,),
            in_specs=[
                pl.BlockSpec((1, length, wide), at),
                pl.BlockSpec((1, length, size), at),
                pl.BlockSpec((1, length, size), at),
                pl.BlockSpec((1, per_group, length), lambda q: (c, per * piece + q, 0)),
                pl.BlockSpec((per_group, 1), lambda q: (per * piece + q, 0)),
                pl.BlockSpec((per_group, 1), lambda q: (per * piece + q, 0)),
                pl.BlockSpec((1, wide), lambda q: (0, per * piece + q)),
                pl.BlockSpec((taps, wide), lambda q: (0, per * piece + q)),
                pl.BlockSpec((2, taps, size), lambda q: (0, 0, per * piece + q)),
                *[anywhere] * len(tokens),
            ],
            out_specs=[pl.BlockSpec(memory_space=pltpu.VMEM)] * 6,
            out_shape=[
                pltpu.VMEM((groups, length, wide), jnp.float32),
                pltpu.VMEM((groups, length, size), jnp.bfloat16),
                pltpu.VMEM((groups, per_group, length), jnp.float32),
                pltpu.VMEM((groups, length, per_group * FIX), jnp.float32),
                pltpu.VMEM((groups, FIX, wide + 2 * size), jnp.bfloat16),
                pltpu.VMEM((groups, 8, wide + 2 * size), jnp.float32),
            ],
            input_output_aliases={first + i: i for i in range(len(before))},
            scratch_shapes=[pltpu.VMEM((2, 8 + length, size), jnp.float32)],
            compiler_params=params,
            cost_estimate=small,
            name="early",
        )(*operands, *tokens)

    def late(k, states, states_first, parts, result, tokens):
        part, offset = SPLIT[k], offsets[k]
        chunk = part * width
        operands = [keep_in_vmem(a) for a in (*states_first, *states, *parts[0], *parts[1])]
        specs = [pl.BlockSpec(memory_space=pltpu.VMEM)] * len(operands)
        keep = 1 + len(operands)
        operands += tokens
        specs += [anywhere] * len(tokens)
        alias = {}
        if result is not None:
            alias = {1 + len(operands): 0}
            operands.append(result)
            specs.append(anywhere)
        kernel = functools.partial(late_kernel, offset, part, lines, reach, SPLIT[0] * width)
        return pl.pallas_call(
            functools.partial(drop_tokens, kernel, keep, 1 + len(operands) - keep),
            grid_spec=pltpu.PrefetchScalarGridSpec(
                num_scalar_prefetch=1,
                grid=(1,),
                in_specs=specs,
                out_specs=anywhere,
                scratch_shapes=[
                    pltpu.VMEM((groups, kids, 8 + FIX, max(chunk, 2 * size)), jnp.float32),
                    pltpu.VMEM((groups, kids, length, chunk), jnp.bfloat16),
                    pltpu.SemaphoreType.DMA((groups,)),
                ],
            ),
            out_shape=jax.ShapeDtypeStruct(x_in.shape, jnp.bfloat16),
            input_output_aliases=alias,
            compiler_params=params,
            cost_estimate=small,
            name="late",
        )(place, *operands)

    skip_row = jnp.repeat(d_skip, width)[None, :]
    rows = [SPLIT[0] * width + tail_lines] + [part * width for part in SPLIT[1:]]
    chunks = [pl.ds(sum(rows[:k]), rows[k]) for k in range(len(SPLIT))]
    *own, sent_4, sent_6 = cast()
    crossed_a = [swap(sent_4, 4), swap(sent_6, 6)]
    inside = [own[0]] + [swap(own[j], j) for j in range(1, 4)]

    def cross(k, tokens):
        moves = [(0, j, None, [(j, chunks[k])]) for j in range(4)]
        (sent,) = rearrange(place, inside, moves, [(4, rows[k], size)], tokens, "stack_later")
        return sent, swap(sent, 4)

    def pick_later(k, crossed, tokens):
        choices = [(j, chunks[k]) for j in range(4)] + [(4, j) for j in range(4)]
        return pick(rows[k], [*inside, crossed], choices, tokens)

    first = early(0, 0, [], [own[0], slots])
    first = early(0, 1, first, [])
    second = early(1, 0, [], [first[1]])
    sent_b, crossed_b = cross(1, [second[1], *crossed_a])
    moves = [(0, n, None, [(n, 1)]) for n in range(2)]
    (spread,) = rearrange(place, crossed_a, moves, [(2, rows[0], size)], [sent_b], "stack_first")
    passed = swap(spread, 1)
    choices = [(j, chunks[0]) for j in range(4)] + [(4, 0), (6, 0), (5, 0), (6, 1)]
    states_a = pick(rows[0], [*inside, *crossed_a, passed], choices, [])
    sent_c, crossed_c = cross(2, [states_a[0], crossed_b])
    states_b = pick_later(1, crossed_b, [sent_c])
    second = early(1, 1, second, [states_b[0]])
    parts = [first, second]
    result = late(0, states_a, states_a, parts, None, [states_b[0]])
    states_c = pick_later(2, crossed_c, [stay(result)])
    result = late(1, states_b, states_a, parts, result, [states_c[0]])
    return late(2, states_c, states_a, parts, result, [])


def solution(mesh):
    rows, cols = P(("groups", "batch"), None, "head"), P(("groups", "batch"), "head")
    placed = (
        rows, rows, rows, cols, P("head"), P("head"), P("head"), P(None, "head"),
        P(None, None, "head"), cols, rows, P(("groups", "batch"), None, None, "head"),
        P("groups"), P("groups"),
    )
    local = local_halves if mesh.shape["batch"] == 8 else local_any
    return jax.shard_map(local, mesh=mesh, in_specs=placed, out_specs=rows, check_vma=False)
```

```python
import functools

import jax
import jax.numpy as jnp
from jax import lax
from jax.experimental import pallas as pl
from jax.experimental.pallas import tpu as pltpu
from jax.sharding import PartitionSpec as P

VMEM_LIMIT = 12 * 1024 * 1024
SPLIT = (8, 4, 4)
FIX = 16
LOG2_E = 1.4426950408889634


def drop_tokens(kernel, keep, tokens, *refs):
    kernel(*refs[:keep], *refs[keep + tokens :])


def parent_of(counts, order):
    index = jnp.arange(counts.shape[0], dtype=jnp.int32)
    bounds = jnp.sum(jnp.where(index[None, :] <= index[:, None], counts[None, :], 0), axis=1)
    return jnp.sum((bounds[None, :] <= order[:, None]).astype(jnp.int32), axis=1)


def three_terms(value):
    terms = []
    for _ in range(3):
        terms.append(value.astype(jnp.bfloat16).astype(jnp.float32))
        value = value - terms[-1]
    return jnp.concatenate(terms)


def conv_silu(padded, tail, rows, taps):
    length = rows.shape[0]
    reach = taps.shape[0] - 1
    padded[8 - reach : 8, :] = jnp.broadcast_to(tail, (reach, rows.shape[1])).astype(jnp.float32)
    padded[8 : 8 + length, :] = rows.astype(jnp.float32)
    total = padded[8 - reach : 8 - reach + length, :] * taps[0:1, :]
    for k in range(1, reach + 1):
        total = total + padded[8 - reach + k : 8 - reach + k + length, :] * taps[k : k + 1, :]
    half = 0.5 * total
    return (half + half * jnp.tanh(half)).astype(jnp.bfloat16)


def early_kernel(
    x_ref, b_ref, c_ref, dt_ref, bias_ref, alog_ref, skip_ref, taps_x_ref, taps_bc_ref,
    mixed_ref, c_out_ref, column_ref, first_ref, opening_ref, weights_ref, padded,
):
    length, wide = x_ref.shape[1:]
    heads = dt_ref.shape[1]
    q = pl.program_id(0)
    width = wide // heads
    half = length // 2

    def convolve(rows, taps, slot):
        bulk = conv_silu(padded.at[slot % 2], 0.0, rows, taps)[FIX:]
        return jnp.concatenate([jnp.zeros((FIX, rows.shape[1]), jnp.bfloat16), bulk])

    b_conv = convolve(b_ref[0], taps_bc_ref[0], 0)
    c_conv = convolve(c_ref[0], taps_bc_ref[1], 1)
    c_out_ref[q] = c_conv
    size = b_ref.shape[2]
    taps = taps_x_ref.shape[0]
    opening_ref[q, :, :wide] = x_ref[0, :FIX]
    opening_ref[q, :, wide : wide + size] = b_ref[0, :FIX]
    opening_ref[q, :, wide + size :] = c_ref[0, :FIX]
    weights_ref[q, :taps, :wide] = taps_x_ref[...]
    weights_ref[q, :taps, wide : wide + size] = taps_bc_ref[0]
    weights_ref[q, :taps, wide + size :] = taps_bc_ref[1]
    weights_ref[q, taps : taps + 1, :wide] = skip_ref[...]
    scores = lax.dot_general(
        c_conv, b_conv, (((1,), (1,)), ((), ())), preferred_element_type=jnp.float32
    )
    raw = dt_ref[0] + bias_ref[...]
    step = jnp.maximum(raw, 0.0) + jnp.log1p(jnp.exp(-jnp.abs(raw)))
    per_token = step * (-jnp.exp(alog_ref[...]))
    upper = lax.broadcasted_iota(jnp.int32, (length, length), 0) <= lax.broadcasted_iota(
        jnp.int32, (length, length), 1
    )
    sums = jnp.dot(
        three_terms(per_token).astype(jnp.bfloat16),
        upper.astype(jnp.float32).astype(jnp.bfloat16),
        preferred_element_type=jnp.float32,
    )
    total = (sums[:heads] + sums[heads : 2 * heads]) + sums[2 * heads :]
    total = total * LOG2_E
    row = total - jnp.log(step) * LOG2_E
    columns = total.T
    column_ref[q] = total
    causal = lax.broadcasted_iota(jnp.int32, (half, half), 0) >= lax.broadcasted_iota(
        jnp.int32, (half, half), 1
    )
    low = lax.broadcasted_iota(jnp.int32, (length, 2 * width), 1) < width
    for pair in range(heads // 2):
        lanes = slice(pair * 2 * width, (pair + 1) * 2 * width)
        x_conv = convolve(x_ref[0, :, lanes], taps_x_ref[:, lanes], pair)
        parts = []
        for head in (2 * pair, 2 * pair + 1):
            column = jnp.broadcast_to(columns[:, head : head + 1], (length, half))
            rows = row[head : head + 1, :]
            near = jnp.exp2(jnp.where(causal, column[:half] - rows[:, :half], -1e30))
            far = jnp.exp2(column[half:] - rows[:, :half])
            last = jnp.exp2(jnp.where(causal, column[half:] - rows[:, half:], -1e30))
            spot = slice(head * FIX, (head + 1) * FIX)
            first_ref[q, :half, spot] = near[:, :FIX]
            first_ref[q, half:, spot] = far[:, :FIX]
            top = (scores[:half, :half] * near).astype(jnp.bfloat16)
            left = (scores[half:, :half] * far).astype(jnp.bfloat16)
            right = (scores[half:, half:] * last).astype(jnp.bfloat16)
            below = jnp.concatenate([left, right], axis=1)
            parts.append(
                jnp.concatenate(
                    [
                        jnp.dot(top, x_conv[:half], preferred_element_type=jnp.float32),
                        jnp.dot(below, x_conv, preferred_element_type=jnp.float32),
                    ]
                )
            )
        mixed_ref[q, :, lanes] = jnp.where(low, parts[0], parts[1]) + skip_ref[
            :, lanes
        ] * x_conv.astype(jnp.float32)


def late_kernel(offset, heads, lines, reach, tail_at, place_ref, *refs):
    tails, states, parts = refs[:4], refs[4:8], refs[8:-4]
    y_ref, padded, y_part, sems = refs[-4:]
    _, kids, length, wide = y_part.shape
    width = wide // heads
    low_first = lax.broadcasted_iota(jnp.int32, (FIX, 2 * width), 1) < width
    contract = (((1,), (1,)), ((), ()))

    def add(j, kid):
        q = place_ref[0] ^ j
        mixed_ref, held_ref, column_ref, first_ref, opening_ref, weights_ref = parts[
            6 * kid : 6 * kid + 6
        ]
        size = held_ref.shape[2]
        per_group = column_ref.shape[1]
        group_wide = opening_ref.shape[2] - 2 * size
        tail_rows = pl.ds(tail_at, -(-lines * reach // 16) * 16)
        tail = tails[j][kid, tail_rows].astype(jnp.float32)
        state = states[j][kid, : heads * width]

        def opening(start, stop, at):
            tap_rows = []
            for k in range(reach):
                first = k * lines + at
                count = (stop - start) // 128
                here = [tail[first + n : first + n + 1] for n in range(count)]
                tap_rows.append(jnp.concatenate(here, axis=1))
            return conv_silu(
                padded.at[j, kid, :, : stop - start],
                jnp.concatenate(tap_rows),
                opening_ref[q, :, start:stop],
                weights_ref[q, : reach + 1, start:stop],
            )

        bc_first = opening(group_wide, group_wide + 2 * size, lines - 2)
        b_first, c_first = bc_first[:, :size], bc_first[:, size:]
        start = offset * width
        x_all = opening(start, start + wide, start // 128).astype(jnp.float32)
        skipped = weights_ref[q, reach + 1 : reach + 2, start : start + wide] * x_all
        c_conv = jnp.concatenate([c_first, held_ref[q, FIX:]])
        terms = three_terms(jnp.exp2(column_ref[q]))
        terms = jnp.concatenate([terms, jnp.zeros((per_group, length), jnp.float32)])
        spread_row = lax.broadcasted_iota(jnp.int32, (4 * per_group, wide), 0)
        spread_lane = lax.broadcasted_iota(jnp.int32, (4 * per_group, wide), 1)
        spread = spread_row % per_group == offset + spread_lane // width
        grow = jnp.dot(
            terms.T.astype(jnp.bfloat16),
            spread.astype(jnp.float32).astype(jnp.bfloat16),
            preferred_element_type=jnp.float32,
        )
        term = lax.dot_general(c_conv, state, contract, preferred_element_type=jnp.float32)
        carried = (term * grow).astype(jnp.bfloat16)
        scores = lax.dot_general(
            c_conv,
            jnp.concatenate([b_first] * heads),
            contract,
            preferred_element_type=jnp.float32,
        )
        here = slice(offset * FIX, (offset + heads) * FIX)
        mixing = (scores * first_ref[q, :, here]).astype(jnp.bfloat16)
        for pair in range(heads // 2):
            lanes = slice(pair * 2 * width, (pair + 1) * 2 * width)
            x_first = x_all[:, lanes]
            stacked = [jnp.where(low_first, x_first, 0.0), jnp.where(low_first, 0.0, x_first)]
            if pair > 0:
                stacked = [jnp.zeros((2 * pair * FIX, 2 * width), jnp.float32)] + stacked
            if 2 * pair + 2 < heads:
                spare = (heads - 2 * pair - 2) * FIX
                stacked = stacked + [jnp.zeros((spare, 2 * width), jnp.float32)]
            part = jnp.dot(
                mixing,
                jnp.concatenate(stacked).astype(jnp.bfloat16),
                preferred_element_type=jnp.float32,
            )
            part = jnp.concatenate([part[:FIX] + skipped[:, lanes], part[FIX:]])
            whole = slice(start + lanes.start, start + lanes.stop)
            y_part[j, kid, :, lanes] = (
                mixed_ref[q, :, whole] + part + carried[:, lanes].astype(jnp.float32)
            ).astype(jnp.bfloat16)

    copies = []
    for j in range(4):
        for kid in range(kids):
            add(j, kid)
        start = (place_ref[0] ^ j) * (y_ref.shape[2] // 4) + offset * width
        lanes = pl.ds(pl.multiple_of(start, 128), wide)
        copies.append(pltpu.make_async_copy(y_part.at[j], y_ref.at[:, :, lanes], sems.at[j]))
        copies[-1].start()
    for copy in copies:
        copy.wait()


def cast_kernel(parts, tailed, reach, lines, *refs):
    count = len(tailed)
    ins, outs = refs[:-count], refs[-count:]
    states, tails = ins[: parts * count], ins[parts * count :]
    for j, out_ref in enumerate(outs):
        start = 0
        for at in range(parts):
            state = states[parts * j + at][0]
            rows = state.shape[0] * state.shape[1]
            out_ref[start : start + rows] = state.reshape(rows, state.shape[2]).astype(jnp.bfloat16)
            start += rows
            if at == 0 and tailed[j]:
                x_tail = tails[2 * j][0].astype(jnp.float32)
                bc_tail = tails[2 * j + 1][0].astype(jnp.float32)
                pieces = []
                for k in range(reach):
                    pieces += [x_tail[k : k + 1, i * 128 : i * 128 + 128] for i in range(lines - 2)]
                    pieces.append(bc_tail[k])
                spare = tailed[j] - lines * reach
                pieces.append(jnp.zeros((spare, 128), jnp.float32))
                out_ref[start : start + tailed[j]] = jnp.concatenate(pieces).astype(jnp.bfloat16)
                start += tailed[j]


def within_kernel(
    parent_ref,
    x_ref,
    b_ref,
    c_ref,
    dt_ref,
    bias_ref,
    alog_ref,
    skip_ref,
    taps_x_ref,
    taps_bc_ref,
    tail_x_ref,
    tail_bc_ref,
    mixed_ref,
    c_out_ref,
    grow_ref,
    padded,
):
    length = x_ref.shape[1]
    heads = dt_ref.shape[1]
    width = x_ref.shape[2] // heads
    b_conv = conv_silu(padded, tail_bc_ref[0, 0], b_ref[0], taps_bc_ref[0])
    c_conv = conv_silu(padded, tail_bc_ref[0, 1], c_ref[0], taps_bc_ref[1])
    c_out_ref[0] = c_conv
    scores = lax.dot_general(
        c_conv, b_conv, (((1,), (1,)), ((), ())), preferred_element_type=jnp.float32
    )
    raw = dt_ref[0] + bias_ref[...]
    step = jnp.maximum(raw, 0.0) + jnp.log1p(jnp.exp(-jnp.abs(raw)))
    per_token = step * (-jnp.exp(alog_ref[...]))
    row = lax.broadcasted_iota(jnp.int32, (length, length), 0)
    col = lax.broadcasted_iota(jnp.int32, (length, length), 1)
    upper = (row <= col).astype(jnp.float32)
    total = lax.dot_general(
        per_token,
        upper,
        (((1,), (0,)), ((), ())),
        precision=lax.Precision.HIGHEST,
        preferred_element_type=jnp.float32,
    )
    total_t = total.T
    grow_ref[0, 0] = jnp.exp(total_t)
    causal = row >= col
    low = lax.broadcasted_iota(jnp.int32, (length, 2 * width), 1) < width
    for pair in range(heads // 2):
        lanes = slice(pair * 2 * width, (pair + 1) * 2 * width)
        x_conv = conv_silu(
            padded, tail_x_ref[0, :, lanes], x_ref[0, :, lanes], taps_x_ref[:, lanes]
        )
        parts = []
        for head in (2 * pair, 2 * pair + 1):
            gap = total_t[:, head : head + 1] - total[head : head + 1, :]
            factor = jnp.exp(jnp.where(causal, gap, -1e30))
            mixing = (scores * factor * step[head : head + 1, :]).astype(jnp.bfloat16)
            parts.append(jnp.dot(mixing, x_conv, preferred_element_type=jnp.float32))
        mixed_ref[0, :, lanes] = (
            jnp.where(low, parts[0], parts[1]) + skip_ref[:, lanes] * x_conv.astype(jnp.float32)
        )


def carried_kernel(state_ref, c_ref, grow_ref, mixed_ref, y_ref):
    sources, _, part, width, size = state_ref.shape
    length = c_ref.shape[1]
    low = lax.broadcasted_iota(jnp.int32, (length, 2 * width), 1) < width
    c_conv = c_ref[0]
    for source in range(sources):
        state = state_ref[source, 0].reshape(part * width, size)
        term = lax.dot_general(
            c_conv, state, (((1,), (1,)), ((), ())), preferred_element_type=jnp.float32
        )
        for pair in range(part // 2):
            head = source * part + 2 * pair
            grow = jnp.where(
                low, grow_ref[0, 0, :, head : head + 1], grow_ref[0, 0, :, head + 1 : head + 2]
            )
            here = slice(2 * pair * width, (2 * pair + 2) * width)
            lanes = slice(head * width, (head + 2) * width)
            carried = (term[:, here] * grow).astype(jnp.bfloat16).astype(jnp.float32)
            y_ref[0, :, lanes] = (mixed_ref[0, :, lanes] + carried).astype(jnp.bfloat16)


def pick_kernel(parent_ref, state_ref, out_ref):
    out_ref[...] = state_ref[...]


def local_any(
    x_in,
    b_in,
    c_in,
    dt_in,
    dt_bias,
    a_log,
    d_skip,
    conv_x,
    conv_bc,
    par_state,
    tail_x,
    tail_bc,
    counts,
    order,
):
    kids, length, columns = x_in.shape
    heads = dt_in.shape[1]
    width, size = par_state.shape[2:]
    ways = lax.axis_size("batch")
    groups = b_in.shape[2] // size
    per_group = heads // groups
    part = heads // ways
    wide = per_group * width
    reach = tail_x.shape[1]
    parents_all = counts.shape[0]
    kids_all = order.shape[0]

    parent = parent_of(counts, order)
    own = lax.dynamic_slice_in_dim(parent, lax.axis_index("batch") * kids, kids)

    sent = par_state.astype(jnp.bfloat16).reshape(ways, part, width, size)
    shares = lax.all_to_all(sent, "batch", split_axis=0, concat_axis=0, tiled=True)

    tails = jnp.concatenate([tail_x.reshape(-1), tail_bc.reshape(-1)])
    tails = jnp.broadcast_to(tails[None], (ways, tails.shape[0]))
    tails = lax.all_to_all(tails, "batch", split_axis=0, concat_axis=0, tiled=True)
    tails_x = tails[:, : reach * columns].reshape(parents_all, reach, columns)
    tails_bc = tails[:, reach * columns :].reshape(parents_all, 2, reach, groups * size)

    picked = pl.pallas_call(
        pick_kernel,
        grid_spec=pltpu.PrefetchScalarGridSpec(
            num_scalar_prefetch=1,
            grid=(kids_all,),
            in_specs=[pl.BlockSpec((1, part, width, size), lambda i, p: (p[i], 0, 0, 0))],
            out_specs=pl.BlockSpec((1, part, width, size), lambda i, p: (i, 0, 0, 0)),
        ),
        out_shape=jax.ShapeDtypeStruct((kids_all, part, width, size), jnp.bfloat16),
        cost_estimate=pl.CostEstimate(
            flops=0, bytes_accessed=4 * kids_all * part * width * size, transcendentals=0
        ),
        name="pick_states",
    )(parent, shares)
    states = lax.all_to_all(
        picked.reshape(ways, kids, part, width, size), "batch", split_axis=0, concat_axis=0, tiled=True
    )

    skip_row = jnp.repeat(d_skip, width)[None, :]
    mixed, c_conv, grow = pl.pallas_call(
        within_kernel,
        grid_spec=pltpu.PrefetchScalarGridSpec(
            num_scalar_prefetch=1,
            grid=(kids, groups),
            in_specs=[
                pl.BlockSpec((1, length, wide), lambda c, q, p: (c, 0, q)),
                pl.BlockSpec((1, length, size), lambda c, q, p: (c, 0, q)),
                pl.BlockSpec((1, length, size), lambda c, q, p: (c, 0, q)),
                pl.BlockSpec((1, per_group, length), lambda c, q, p: (c, q, 0)),
                pl.BlockSpec((per_group, 1), lambda c, q, p: (q, 0)),
                pl.BlockSpec((per_group, 1), lambda c, q, p: (q, 0)),
                pl.BlockSpec((1, wide), lambda c, q, p: (0, q)),
                pl.BlockSpec((reach + 1, wide), lambda c, q, p: (0, q)),
                pl.BlockSpec((2, reach + 1, size), lambda c, q, p: (0, 0, q)),
                pl.BlockSpec((1, reach, wide), lambda c, q, p: (p[c], 0, q)),
                pl.BlockSpec((1, 2, reach, size), lambda c, q, p: (p[c], 0, 0, q)),
            ],
            out_specs=[
                pl.BlockSpec((1, length, wide), lambda c, q, p: (c, 0, q)),
                pl.BlockSpec((1, length, size), lambda c, q, p: (c, 0, q)),
                pl.BlockSpec((1, 1, length, per_group), lambda c, q, p: (c, q, 0, 0)),
            ],
            scratch_shapes=[pltpu.VMEM((8 + length, size), jnp.float32)],
        ),
        out_shape=[
            jax.ShapeDtypeStruct((kids, length, columns), jnp.float32),
            jax.ShapeDtypeStruct((kids, length, groups * size), jnp.bfloat16),
            jax.ShapeDtypeStruct((kids, groups, length, per_group), jnp.float32),
        ],
        compiler_params=pltpu.CompilerParams(vmem_limit_bytes=4 * VMEM_LIMIT),
        cost_estimate=pl.CostEstimate(
            flops=4 * kids * heads * length * length * width,
            bytes_accessed=6 * kids * length * columns,
            transcendentals=kids * heads * length * length,
        ),
        name="within",
    )(
        own,
        x_in,
        b_in,
        c_in,
        dt_in,
        dt_bias[:, None],
        a_log[:, None],
        skip_row,
        conv_x,
        conv_bc,
        tails_x,
        tails_bc,
    )

    sources = per_group // part
    return pl.pallas_call(
        carried_kernel,
        grid=(kids, groups),
        in_specs=[
            pl.BlockSpec((sources, 1, part, width, size), lambda c, q: (q, c, 0, 0, 0)),
            pl.BlockSpec((1, length, size), lambda c, q: (c, 0, q)),
            pl.BlockSpec((1, 1, length, per_group), lambda c, q: (c, q, 0, 0)),
            pl.BlockSpec((1, length, wide), lambda c, q: (c, 0, q)),
        ],
        out_specs=pl.BlockSpec((1, length, wide), lambda c, q: (c, 0, q)),
        out_shape=jax.ShapeDtypeStruct((kids, length, columns), jnp.bfloat16),
        compiler_params=pltpu.CompilerParams(vmem_limit_bytes=4 * VMEM_LIMIT),
        cost_estimate=pl.CostEstimate(
            flops=2 * kids * length * columns * size,
            bytes_accessed=8 * kids * length * columns,
            transcendentals=0,
        ),
        name="carried",
    )(states, c_conv, grow, mixed)


def local_halves(
    x_in, b_in, c_in, dt_in, dt_bias, a_log, d_skip, conv_x, conv_bc,
    par_state, tail_x, tail_bc, counts, order,
):
    kids, length, columns = x_in.shape
    heads = dt_in.shape[1]
    width, size = par_state.shape[2:]
    groups = b_in.shape[2] // size
    per_group = heads // groups
    wide = per_group * width
    taps = conv_x.shape[0]
    reach = taps - 1
    lines = (wide + 2 * size) // 128
    tail_lines = -(-lines * reach // 16) * 16
    params = pltpu.CompilerParams(vmem_limit_bytes=VMEM_LIMIT)
    anywhere = pl.BlockSpec(memory_space=pl.ANY)
    small = pl.CostEstimate(flops=1, bytes_accessed=1, transcendentals=0)

    stay = lambda x: pltpu.with_memory_space_constraint(x, pltpu.HBM)
    keep_in_vmem = lambda x: pltpu.with_memory_space_constraint(x, pltpu.VMEM)
    x_in, b_in, c_in, dt_in, conv_x, conv_bc = map(stay, (x_in, b_in, c_in, dt_in, conv_x, conv_bc))

    me = lax.axis_index("batch")
    parent = parent_of(counts, order)
    child = (jnp.arange(4 * kids, dtype=jnp.int32) // kids ^ me) * kids
    child = child + jnp.arange(4 * kids, dtype=jnp.int32) % kids
    catalog = jnp.arange(4 * 2 * kids, dtype=jnp.int32)
    owner = jnp.sum(jnp.where(child[:, None] == catalog[None, :], parent[None, :], 0), axis=1)
    slots = owner ^ me
    place = (me % 4).astype(jnp.int32)[None]

    state = stay(par_state.reshape(groups, per_group, width, size))
    x_tails, bc_tails = stay(tail_x), stay(tail_bc.transpose(0, 2, 1, 3))
    offsets = [sum(SPLIT[:k]) for k in range(len(SPLIT))]

    def swap(value, r):
        return lax.ppermute(value, "batch", perm=[(i, i ^ r) for i in range(8)])

    def cast():
        rows = per_group * width + tail_lines + 48
        rows_a = SPLIT[0] * width + tail_lines
        count = len(SPLIT) + 2

        def kernel(place_ref, *refs):
            ins, outs = refs[: 4 * count], refs[4 * count :]
            for n in range(4):
                cast_kernel(
                    len(SPLIT), [tail_lines], reach, lines, *ins[count * n : count * n + count], outs[n]
                )
                outs[4 + n // 2][n % 2] = outs[n][:rows_a]

        operands, specs = [], []
        for n in range(4):
            for part, offset in zip(SPLIT, offsets):
                operands.append(state)
                specs.append(
                    pl.BlockSpec(
                        (1, part, width, size),
                        lambda i, p, n=n, at=offset // part: (p[0] ^ n, at, 0, 0),
                    )
                )
            operands += [x_tails, bc_tails]
            specs += [
                pl.BlockSpec((1, reach, wide), lambda i, p, n=n: (0, 0, p[0] ^ n)),
                pl.BlockSpec((1, reach, 2, size), lambda i, p, n=n: (0, 0, 0, p[0] ^ n)),
            ]
        shapes = [(rows, size)] * 4 + [(2, rows_a, size)] * 2
        return pl.pallas_call(
            kernel,
            grid_spec=pltpu.PrefetchScalarGridSpec(
                num_scalar_prefetch=1,
                grid=(1,),
                in_specs=specs,
                out_specs=[pl.BlockSpec(memory_space=pltpu.VMEM)] * len(shapes),
            ),
            out_shape=[pltpu.VMEM(shape, jnp.bfloat16) for shape in shapes],
            compiler_params=params,
            cost_estimate=small,
            name="cast_states",
        )(place, *operands)

    def rearrange(scalars, sources, moves, shapes, tokens, name):
        def kernel(scalars_ref, *refs):
            held, outs = refs[: len(sources)], refs[len(sources) :]
            for out, at, scalar, choices in moves:
                for value, (number, take) in enumerate(choices):

                    def copy(out=out, at=at, number=number, take=take):
                        rows = held[number][...] if take is None else held[number][take]
                        if at is None:
                            outs[out][...] = rows
                        else:
                            outs[out][at] = rows

                    if scalar is None:
                        copy()
                    else:
                        pl.when(scalars_ref[scalar] == value)(copy)

        return pl.pallas_call(
            functools.partial(drop_tokens, kernel, 1 + len(sources), len(tokens)),
            grid_spec=pltpu.PrefetchScalarGridSpec(
                num_scalar_prefetch=1,
                grid=(1,),
                in_specs=[pl.BlockSpec(memory_space=pltpu.VMEM)] * len(sources)
                + [anywhere] * len(tokens),
                out_specs=[pl.BlockSpec(memory_space=pltpu.VMEM)] * len(shapes),
            ),
            out_shape=[pltpu.VMEM(shape, jnp.bfloat16) for shape in shapes],
            compiler_params=params,
            cost_estimate=small,
            name=name,
        )(scalars, *map(keep_in_vmem, sources), *tokens)

    def pick(rows, sources, choices, tokens):
        moves = [
            (j, kid, j * kids + kid, choices) for j in range(4) for kid in range(kids)
        ]
        picked = rearrange(
            slots, sources, moves, [(kids, rows, size)] * 4, tokens, "pick_states"
        )
        return [picked[0]] + [swap(picked[j], j) for j in range(1, 4)]

    def early(c, tokens):
        at = lambda q: (c, 0, q)
        operands = [
            x_in, b_in, c_in, dt_in, dt_bias[:, None], a_log[:, None], skip_row, conv_x, conv_bc
        ]
        return pl.pallas_call(
            functools.partial(drop_tokens, early_kernel, len(operands), len(tokens)),
            grid=(groups,),
            in_specs=[
                pl.BlockSpec((1, length, wide), at),
                pl.BlockSpec((1, length, size), at),
                pl.BlockSpec((1, length, size), at),
                pl.BlockSpec((1, per_group, length), lambda q: (c, q, 0)),
                pl.BlockSpec((per_group, 1), lambda q: (q, 0)),
                pl.BlockSpec((per_group, 1), lambda q: (q, 0)),
                pl.BlockSpec((1, wide), lambda q: (0, q)),
                pl.BlockSpec((taps, wide), lambda q: (0, q)),
                pl.BlockSpec((2, taps, size), lambda q: (0, 0, q)),
                *[anywhere] * len(tokens),
            ],
            out_specs=[pl.BlockSpec(memory_space=pltpu.VMEM)] * 6,
            out_shape=[
                pltpu.VMEM((groups, length, wide), jnp.float32),
                pltpu.VMEM((groups, length, size), jnp.bfloat16),
                pltpu.VMEM((groups, per_group, length), jnp.float32),
                pltpu.VMEM((groups, length, per_group * FIX), jnp.float32),
                pltpu.VMEM((groups, FIX, wide + 2 * size), jnp.bfloat16),
                pltpu.VMEM((groups, 8, wide + 2 * size), jnp.float32),
            ],
            scratch_shapes=[pltpu.VMEM((2, 8 + length, size), jnp.float32)],
            compiler_params=params,
            cost_estimate=small,
            name="early",
        )(*operands, *tokens)

    def late(k, states, states_first, parts, result, tokens):
        part, offset = SPLIT[k], offsets[k]
        chunk = part * width
        operands = [keep_in_vmem(a) for a in (*states_first, *states, *parts[0], *parts[1])]
        specs = [pl.BlockSpec(memory_space=pltpu.VMEM)] * len(operands)
        keep = 1 + len(operands)
        operands += tokens
        specs += [anywhere] * len(tokens)
        alias = {}
        if result is not None:
            alias = {1 + len(operands): 0}
            operands.append(result)
            specs.append(anywhere)
        kernel = functools.partial(late_kernel, offset, part, lines, reach, SPLIT[0] * width)
        return pl.pallas_call(
            functools.partial(drop_tokens, kernel, keep, 1 + len(operands) - keep),
            grid_spec=pltpu.PrefetchScalarGridSpec(
                num_scalar_prefetch=1,
                grid=(1,),
                in_specs=specs,
                out_specs=anywhere,
                scratch_shapes=[
                    pltpu.VMEM((groups, kids, 8 + FIX, max(chunk, 2 * size)), jnp.float32),
                    pltpu.VMEM((groups, kids, length, chunk), jnp.bfloat16),
                    pltpu.SemaphoreType.DMA((groups,)),
                ],
            ),
            out_shape=jax.ShapeDtypeStruct(x_in.shape, jnp.bfloat16),
            input_output_aliases=alias,
            compiler_params=params,
            cost_estimate=small,
            name="late",
        )(place, *operands)

    skip_row = jnp.repeat(d_skip, width)[None, :]
    rows = [SPLIT[0] * width + tail_lines] + [part * width for part in SPLIT[1:]]
    chunks = [pl.ds(sum(rows[:k]), rows[k]) for k in range(len(SPLIT))]
    *own, sent_4, sent_6 = cast()
    inside = [own[0]] + [swap(own[j], j) for j in range(1, 4)]
    crossed_a = [swap(sent_4, 4), swap(sent_6, 6)]

    def cross(k, tokens):
        moves = [(0, j, None, [(j, chunks[k])]) for j in range(4)]
        (sent,) = rearrange(place, inside, moves, [(4, rows[k], size)], tokens, "stack_later")
        return sent, swap(sent, 4)

    def pick_later(k, crossed, tokens):
        choices = [(j, chunks[k]) for j in range(4)] + [(4, j) for j in range(4)]
        return pick(rows[k], [*inside, crossed], choices, tokens)

    parts = [early(0, [own[0], slots])]
    parts.append(early(1, [parts[0][1]]))
    moves = [(0, n, None, [(n, 1)]) for n in range(2)]
    (spread,) = rearrange(
        place, crossed_a, moves, [(2, rows[0], size)], [parts[1][1]], "stack_first"
    )
    passed = swap(spread, 1)
    sent_b, crossed_b = cross(1, [spread])
    choices = [(j, chunks[0]) for j in range(4)] + [(4, 0), (6, 0), (5, 0), (6, 1)]
    states_a = pick(rows[0], [*inside, *crossed_a, passed], choices, [sent_b])
    sent_c, crossed_c = cross(2, [states_a[0], crossed_b])
    states_b = pick_later(1, crossed_b, [sent_c])
    states_c = pick_later(2, crossed_c, [states_b[0]])
    result = late(0, states_a, states_a, parts, None, [states_c[0]])
    result = late(1, states_b, states_a, parts, result, [])
    return late(2, states_c, states_a, parts, result, [])


def solution(mesh):
    rows, cols = P(("groups", "batch"), None, "head"), P(("groups", "batch"), "head")
    placed = (
        rows, rows, rows, cols, P("head"), P("head"), P("head"), P(None, "head"),
        P(None, None, "head"), cols, rows, P(("groups", "batch"), None, None, "head"),
        P("groups"), P("groups"),
    )
    local = local_halves if mesh.shape["batch"] == 8 else local_any
    return jax.shard_map(local, mesh=mesh, in_specs=placed, out_specs=rows, check_vma=False)
```

```python
import functools

import jax
import jax.numpy as jnp
from jax import lax
from jax.experimental import pallas as pl
from jax.experimental.pallas import tpu as pltpu
from jax.sharding import PartitionSpec as P

VMEM_LIMIT = 12 * 1024 * 1024
SPLIT = (4, 8, 4)
FIX = 16
LOG2_E = 1.4426950408889634


def drop_tokens(kernel, keep, tokens, *refs):
    kernel(*refs[:keep], *refs[keep + tokens :])


def parent_of(counts, order):
    index = jnp.arange(counts.shape[0], dtype=jnp.int32)
    bounds = jnp.sum(jnp.where(index[None, :] <= index[:, None], counts[None, :], 0), axis=1)
    return jnp.sum((bounds[None, :] <= order[:, None]).astype(jnp.int32), axis=1)


def three_terms(value):
    terms = []
    for _ in range(3):
        terms.append(value.astype(jnp.bfloat16).astype(jnp.float32))
        value = value - terms[-1]
    return jnp.concatenate(terms)


def conv_silu(padded, tail, rows, taps):
    length = rows.shape[0]
    reach = taps.shape[0] - 1
    padded[8 - reach : 8, :] = jnp.broadcast_to(tail, (reach, rows.shape[1])).astype(jnp.float32)
    padded[8 : 8 + length, :] = rows.astype(jnp.float32)
    total = padded[8 - reach : 8 - reach + length, :] * taps[0:1, :]
    for k in range(1, reach + 1):
        total = total + padded[8 - reach + k : 8 - reach + k + length, :] * taps[k : k + 1, :]
    half = 0.5 * total
    return (half + half * jnp.tanh(half)).astype(jnp.bfloat16)


def early_kernel(
    x_ref, b_ref, c_ref, dt_ref, bias_ref, alog_ref, skip_ref, taps_x_ref, taps_bc_ref,
    mixed_ref, c_out_ref, column_ref, first_ref, opening_ref, weights_ref, padded,
):
    length, wide = x_ref.shape[1:]
    heads = dt_ref.shape[1]
    q = pl.program_id(0)
    width = wide // heads
    half = length // 2

    def convolve(rows, taps, slot):
        bulk = conv_silu(padded.at[slot % 2], 0.0, rows, taps)[FIX:]
        return jnp.concatenate([jnp.zeros((FIX, rows.shape[1]), jnp.bfloat16), bulk])

    b_conv = convolve(b_ref[0], taps_bc_ref[0], 0)
    c_conv = convolve(c_ref[0], taps_bc_ref[1], 1)
    c_out_ref[q] = c_conv
    size = b_ref.shape[2]
    taps = taps_x_ref.shape[0]
    opening_ref[q, :, :wide] = x_ref[0, :FIX]
    opening_ref[q, :, wide : wide + size] = b_ref[0, :FIX]
    opening_ref[q, :, wide + size :] = c_ref[0, :FIX]
    weights_ref[q, :taps, :wide] = taps_x_ref[...]
    weights_ref[q, :taps, wide : wide + size] = taps_bc_ref[0]
    weights_ref[q, :taps, wide + size :] = taps_bc_ref[1]
    weights_ref[q, taps : taps + 1, :wide] = skip_ref[...]
    scores = lax.dot_general(
        c_conv, b_conv, (((1,), (1,)), ((), ())), preferred_element_type=jnp.float32
    )
    raw = dt_ref[0] + bias_ref[...]
    step = jnp.maximum(raw, 0.0) + jnp.log1p(jnp.exp(-jnp.abs(raw)))
    per_token = step * (-jnp.exp(alog_ref[...]))
    upper = lax.broadcasted_iota(jnp.int32, (length, length), 0) <= lax.broadcasted_iota(
        jnp.int32, (length, length), 1
    )
    sums = jnp.dot(
        three_terms(per_token).astype(jnp.bfloat16),
        upper.astype(jnp.float32).astype(jnp.bfloat16),
        preferred_element_type=jnp.float32,
    )
    total = (sums[:heads] + sums[heads : 2 * heads]) + sums[2 * heads :]
    total = total * LOG2_E
    row = total - jnp.log(step) * LOG2_E
    columns = total.T
    column_ref[q] = total
    causal = lax.broadcasted_iota(jnp.int32, (half, half), 0) >= lax.broadcasted_iota(
        jnp.int32, (half, half), 1
    )
    low = lax.broadcasted_iota(jnp.int32, (length, 2 * width), 1) < width
    for pair in range(heads // 2):
        lanes = slice(pair * 2 * width, (pair + 1) * 2 * width)
        x_conv = convolve(x_ref[0, :, lanes], taps_x_ref[:, lanes], pair)
        parts = []
        for head in (2 * pair, 2 * pair + 1):
            column = jnp.broadcast_to(columns[:, head : head + 1], (length, half))
            rows = row[head : head + 1, :]
            near = jnp.exp2(jnp.where(causal, column[:half] - rows[:, :half], -1e30))
            far = jnp.exp2(column[half:] - rows[:, :half])
            last = jnp.exp2(jnp.where(causal, column[half:] - rows[:, half:], -1e30))
            spot = slice(head * FIX, (head + 1) * FIX)
            first_ref[q, :half, spot] = near[:, :FIX]
            first_ref[q, half:, spot] = far[:, :FIX]
            top = (scores[:half, :half] * near).astype(jnp.bfloat16)
            left = (scores[half:, :half] * far).astype(jnp.bfloat16)
            right = (scores[half:, half:] * last).astype(jnp.bfloat16)
            below = jnp.concatenate([left, right], axis=1)
            parts.append(
                jnp.concatenate(
                    [
                        jnp.dot(top, x_conv[:half], preferred_element_type=jnp.float32),
                        jnp.dot(below, x_conv, preferred_element_type=jnp.float32),
                    ]
                )
            )
        mixed_ref[q, :, lanes] = jnp.where(low, parts[0], parts[1]) + skip_ref[
            :, lanes
        ] * x_conv.astype(jnp.float32)


def late_kernel(offset, heads, lines, reach, tail_at, place_ref, *refs):
    tails, states, parts = refs[:4], refs[4:8], refs[8:-4]
    y_ref, padded, y_part, sems = refs[-4:]
    _, kids, length, wide = y_part.shape
    width = wide // heads
    low_first = lax.broadcasted_iota(jnp.int32, (FIX, 2 * width), 1) < width
    contract = (((1,), (1,)), ((), ()))

    def add(j, kid):
        q = place_ref[0] ^ j
        mixed_ref, held_ref, column_ref, first_ref, opening_ref, weights_ref = parts[
            6 * kid : 6 * kid + 6
        ]
        size = held_ref.shape[2]
        per_group = column_ref.shape[1]
        group_wide = opening_ref.shape[2] - 2 * size
        tail_rows = pl.ds(tail_at, -(-lines * reach // 16) * 16)
        tail = tails[j][kid, tail_rows].astype(jnp.float32)
        state = states[j][kid, : heads * width]

        def opening(start, stop, at):
            tap_rows = []
            for k in range(reach):
                first = k * lines + at
                count = (stop - start) // 128
                here = [tail[first + n : first + n + 1] for n in range(count)]
                tap_rows.append(jnp.concatenate(here, axis=1))
            return conv_silu(
                padded.at[j, kid, :, : stop - start],
                jnp.concatenate(tap_rows),
                opening_ref[q, :, start:stop],
                weights_ref[q, : reach + 1, start:stop],
            )

        bc_first = opening(group_wide, group_wide + 2 * size, lines - 2)
        b_first, c_first = bc_first[:, :size], bc_first[:, size:]
        start = offset * width
        x_all = opening(start, start + wide, start // 128).astype(jnp.float32)
        skipped = weights_ref[q, reach + 1 : reach + 2, start : start + wide] * x_all
        c_conv = jnp.concatenate([c_first, held_ref[q, FIX:]])
        terms = three_terms(jnp.exp2(column_ref[q]))
        terms = jnp.concatenate([terms, jnp.zeros((per_group, length), jnp.float32)])
        spread_row = lax.broadcasted_iota(jnp.int32, (4 * per_group, wide), 0)
        spread_lane = lax.broadcasted_iota(jnp.int32, (4 * per_group, wide), 1)
        spread = spread_row % per_group == offset + spread_lane // width
        grow = jnp.dot(
            terms.T.astype(jnp.bfloat16),
            spread.astype(jnp.float32).astype(jnp.bfloat16),
            preferred_element_type=jnp.float32,
        )
        term = lax.dot_general(c_conv, state, contract, preferred_element_type=jnp.float32)
        carried = (term * grow).astype(jnp.bfloat16)
        scores = lax.dot_general(
            c_conv,
            jnp.concatenate([b_first] * heads),
            contract,
            preferred_element_type=jnp.float32,
        )
        here = slice(offset * FIX, (offset + heads) * FIX)
        mixing = (scores * first_ref[q, :, here]).astype(jnp.bfloat16)
        for pair in range(heads // 2):
            lanes = slice(pair * 2 * width, (pair + 1) * 2 * width)
            x_first = x_all[:, lanes]
            stacked = [jnp.where(low_first, x_first, 0.0), jnp.where(low_first, 0.0, x_first)]
            if pair > 0:
                stacked = [jnp.zeros((2 * pair * FIX, 2 * width), jnp.float32)] + stacked
            if 2 * pair + 2 < heads:
                spare = (heads - 2 * pair - 2) * FIX
                stacked = stacked + [jnp.zeros((spare, 2 * width), jnp.float32)]
            part = jnp.dot(
                mixing,
                jnp.concatenate(stacked).astype(jnp.bfloat16),
                preferred_element_type=jnp.float32,
            )
            part = jnp.concatenate([part[:FIX] + skipped[:, lanes], part[FIX:]])
            whole = slice(start + lanes.start, start + lanes.stop)
            y_part[j, kid, :, lanes] = (
                mixed_ref[q, :, whole] + part + carried[:, lanes].astype(jnp.float32)
            ).astype(jnp.bfloat16)

    copies = []
    for j in range(4):
        for kid in range(kids):
            add(j, kid)
        start = (place_ref[0] ^ j) * (y_ref.shape[2] // 4) + offset * width
        lanes = pl.ds(pl.multiple_of(start, 128), wide)
        copies.append(pltpu.make_async_copy(y_part.at[j], y_ref.at[:, :, lanes], sems.at[j]))
        copies[-1].start()
    for copy in copies:
        copy.wait()


def cast_kernel(parts, tailed, reach, lines, *refs):
    count = len(tailed)
    ins, outs = refs[:-count], refs[-count:]
    states, tails = ins[: parts * count], ins[parts * count :]
    for j, out_ref in enumerate(outs):
        start = 0
        for at in range(parts):
            state = states[parts * j + at][0]
            rows = state.shape[0] * state.shape[1]
            out_ref[start : start + rows] = state.reshape(rows, state.shape[2]).astype(jnp.bfloat16)
            start += rows
            if at == 0 and tailed[j]:
                x_tail = tails[2 * j][0].astype(jnp.float32)
                bc_tail = tails[2 * j + 1][0].astype(jnp.float32)
                pieces = []
                for k in range(reach):
                    pieces += [x_tail[k : k + 1, i * 128 : i * 128 + 128] for i in range(lines - 2)]
                    pieces.append(bc_tail[k])
                spare = tailed[j] - lines * reach
                pieces.append(jnp.zeros((spare, 128), jnp.float32))
                out_ref[start : start + tailed[j]] = jnp.concatenate(pieces).astype(jnp.bfloat16)
                start += tailed[j]


def within_kernel(
    parent_ref,
    x_ref,
    b_ref,
    c_ref,
    dt_ref,
    bias_ref,
    alog_ref,
    skip_ref,
    taps_x_ref,
    taps_bc_ref,
    tail_x_ref,
    tail_bc_ref,
    mixed_ref,
    c_out_ref,
    grow_ref,
    padded,
):
    length = x_ref.shape[1]
    heads = dt_ref.shape[1]
    width = x_ref.shape[2] // heads
    b_conv = conv_silu(padded, tail_bc_ref[0, 0], b_ref[0], taps_bc_ref[0])
    c_conv = conv_silu(padded, tail_bc_ref[0, 1], c_ref[0], taps_bc_ref[1])
    c_out_ref[0] = c_conv
    scores = lax.dot_general(
        c_conv, b_conv, (((1,), (1,)), ((), ())), preferred_element_type=jnp.float32
    )
    raw = dt_ref[0] + bias_ref[...]
    step = jnp.maximum(raw, 0.0) + jnp.log1p(jnp.exp(-jnp.abs(raw)))
    per_token = step * (-jnp.exp(alog_ref[...]))
    row = lax.broadcasted_iota(jnp.int32, (length, length), 0)
    col = lax.broadcasted_iota(jnp.int32, (length, length), 1)
    upper = (row <= col).astype(jnp.float32)
    total = lax.dot_general(
        per_token,
        upper,
        (((1,), (0,)), ((), ())),
        precision=lax.Precision.HIGHEST,
        preferred_element_type=jnp.float32,
    )
    total_t = total.T
    grow_ref[0, 0] = jnp.exp(total_t)
    causal = row >= col
    low = lax.broadcasted_iota(jnp.int32, (length, 2 * width), 1) < width
    for pair in range(heads // 2):
        lanes = slice(pair * 2 * width, (pair + 1) * 2 * width)
        x_conv = conv_silu(
            padded, tail_x_ref[0, :, lanes], x_ref[0, :, lanes], taps_x_ref[:, lanes]
        )
        parts = []
        for head in (2 * pair, 2 * pair + 1):
            gap = total_t[:, head : head + 1] - total[head : head + 1, :]
            factor = jnp.exp(jnp.where(causal, gap, -1e30))
            mixing = (scores * factor * step[head : head + 1, :]).astype(jnp.bfloat16)
            parts.append(jnp.dot(mixing, x_conv, preferred_element_type=jnp.float32))
        mixed_ref[0, :, lanes] = (
            jnp.where(low, parts[0], parts[1]) + skip_ref[:, lanes] * x_conv.astype(jnp.float32)
        )


def carried_kernel(state_ref, c_ref, grow_ref, mixed_ref, y_ref):
    sources, _, part, width, size = state_ref.shape
    length = c_ref.shape[1]
    low = lax.broadcasted_iota(jnp.int32, (length, 2 * width), 1) < width
    c_conv = c_ref[0]
    for source in range(sources):
        state = state_ref[source, 0].reshape(part * width, size)
        term = lax.dot_general(
            c_conv, state, (((1,), (1,)), ((), ())), preferred_element_type=jnp.float32
        )
        for pair in range(part // 2):
            head = source * part + 2 * pair
            grow = jnp.where(
                low, grow_ref[0, 0, :, head : head + 1], grow_ref[0, 0, :, head + 1 : head + 2]
            )
            here = slice(2 * pair * width, (2 * pair + 2) * width)
            lanes = slice(head * width, (head + 2) * width)
            carried = (term[:, here] * grow).astype(jnp.bfloat16).astype(jnp.float32)
            y_ref[0, :, lanes] = (mixed_ref[0, :, lanes] + carried).astype(jnp.bfloat16)


def pick_kernel(parent_ref, state_ref, out_ref):
    out_ref[...] = state_ref[...]


def local_any(
    x_in,
    b_in,
    c_in,
    dt_in,
    dt_bias,
    a_log,
    d_skip,
    conv_x,
    conv_bc,
    par_state,
    tail_x,
    tail_bc,
    counts,
    order,
):
    kids, length, columns = x_in.shape
    heads = dt_in.shape[1]
    width, size = par_state.shape[2:]
    ways = lax.axis_size("batch")
    groups = b_in.shape[2] // size
    per_group = heads // groups
    part = heads // ways
    wide = per_group * width
    reach = tail_x.shape[1]
    parents_all = counts.shape[0]
    kids_all = order.shape[0]

    parent = parent_of(counts, order)
    own = lax.dynamic_slice_in_dim(parent, lax.axis_index("batch") * kids, kids)

    sent = par_state.astype(jnp.bfloat16).reshape(ways, part, width, size)
    shares = lax.all_to_all(sent, "batch", split_axis=0, concat_axis=0, tiled=True)

    tails = jnp.concatenate([tail_x.reshape(-1), tail_bc.reshape(-1)])
    tails = jnp.broadcast_to(tails[None], (ways, tails.shape[0]))
    tails = lax.all_to_all(tails, "batch", split_axis=0, concat_axis=0, tiled=True)
    tails_x = tails[:, : reach * columns].reshape(parents_all, reach, columns)
    tails_bc = tails[:, reach * columns :].reshape(parents_all, 2, reach, groups * size)

    picked = pl.pallas_call(
        pick_kernel,
        grid_spec=pltpu.PrefetchScalarGridSpec(
            num_scalar_prefetch=1,
            grid=(kids_all,),
            in_specs=[pl.BlockSpec((1, part, width, size), lambda i, p: (p[i], 0, 0, 0))],
            out_specs=pl.BlockSpec((1, part, width, size), lambda i, p: (i, 0, 0, 0)),
        ),
        out_shape=jax.ShapeDtypeStruct((kids_all, part, width, size), jnp.bfloat16),
        cost_estimate=pl.CostEstimate(
            flops=0, bytes_accessed=4 * kids_all * part * width * size, transcendentals=0
        ),
        name="pick_states",
    )(parent, shares)
    states = lax.all_to_all(
        picked.reshape(ways, kids, part, width, size), "batch", split_axis=0, concat_axis=0, tiled=True
    )

    skip_row = jnp.repeat(d_skip, width)[None, :]
    mixed, c_conv, grow = pl.pallas_call(
        within_kernel,
        grid_spec=pltpu.PrefetchScalarGridSpec(
            num_scalar_prefetch=1,
            grid=(kids, groups),
            in_specs=[
                pl.BlockSpec((1, length, wide), lambda c, q, p: (c, 0, q)),
                pl.BlockSpec((1, length, size), lambda c, q, p: (c, 0, q)),
                pl.BlockSpec((1, length, size), lambda c, q, p: (c, 0, q)),
                pl.BlockSpec((1, per_group, length), lambda c, q, p: (c, q, 0)),
                pl.BlockSpec((per_group, 1), lambda c, q, p: (q, 0)),
                pl.BlockSpec((per_group, 1), lambda c, q, p: (q, 0)),
                pl.BlockSpec((1, wide), lambda c, q, p: (0, q)),
                pl.BlockSpec((reach + 1, wide), lambda c, q, p: (0, q)),
                pl.BlockSpec((2, reach + 1, size), lambda c, q, p: (0, 0, q)),
                pl.BlockSpec((1, reach, wide), lambda c, q, p: (p[c], 0, q)),
                pl.BlockSpec((1, 2, reach, size), lambda c, q, p: (p[c], 0, 0, q)),
            ],
            out_specs=[
                pl.BlockSpec((1, length, wide), lambda c, q, p: (c, 0, q)),
                pl.BlockSpec((1, length, size), lambda c, q, p: (c, 0, q)),
                pl.BlockSpec((1, 1, length, per_group), lambda c, q, p: (c, q, 0, 0)),
            ],
            scratch_shapes=[pltpu.VMEM((8 + length, size), jnp.float32)],
        ),
        out_shape=[
            jax.ShapeDtypeStruct((kids, length, columns), jnp.float32),
            jax.ShapeDtypeStruct((kids, length, groups * size), jnp.bfloat16),
            jax.ShapeDtypeStruct((kids, groups, length, per_group), jnp.float32),
        ],
        compiler_params=pltpu.CompilerParams(vmem_limit_bytes=4 * VMEM_LIMIT),
        cost_estimate=pl.CostEstimate(
            flops=4 * kids * heads * length * length * width,
            bytes_accessed=6 * kids * length * columns,
            transcendentals=kids * heads * length * length,
        ),
        name="within",
    )(
        own,
        x_in,
        b_in,
        c_in,
        dt_in,
        dt_bias[:, None],
        a_log[:, None],
        skip_row,
        conv_x,
        conv_bc,
        tails_x,
        tails_bc,
    )

    sources = per_group // part
    return pl.pallas_call(
        carried_kernel,
        grid=(kids, groups),
        in_specs=[
            pl.BlockSpec((sources, 1, part, width, size), lambda c, q: (q, c, 0, 0, 0)),
            pl.BlockSpec((1, length, size), lambda c, q: (c, 0, q)),
            pl.BlockSpec((1, 1, length, per_group), lambda c, q: (c, q, 0, 0)),
            pl.BlockSpec((1, length, wide), lambda c, q: (c, 0, q)),
        ],
        out_specs=pl.BlockSpec((1, length, wide), lambda c, q: (c, 0, q)),
        out_shape=jax.ShapeDtypeStruct((kids, length, columns), jnp.bfloat16),
        compiler_params=pltpu.CompilerParams(vmem_limit_bytes=4 * VMEM_LIMIT),
        cost_estimate=pl.CostEstimate(
            flops=2 * kids * length * columns * size,
            bytes_accessed=8 * kids * length * columns,
            transcendentals=0,
        ),
        name="carried",
    )(states, c_conv, grow, mixed)


def local_halves(
    x_in, b_in, c_in, dt_in, dt_bias, a_log, d_skip, conv_x, conv_bc,
    par_state, tail_x, tail_bc, counts, order,
):
    kids, length, columns = x_in.shape
    heads = dt_in.shape[1]
    width, size = par_state.shape[2:]
    groups = b_in.shape[2] // size
    per_group = heads // groups
    wide = per_group * width
    taps = conv_x.shape[0]
    reach = taps - 1
    lines = (wide + 2 * size) // 128
    tail_lines = -(-lines * reach // 16) * 16
    params = pltpu.CompilerParams(vmem_limit_bytes=VMEM_LIMIT)
    anywhere = pl.BlockSpec(memory_space=pl.ANY)
    small = pl.CostEstimate(flops=1, bytes_accessed=1, transcendentals=0)

    stay = lambda x: pltpu.with_memory_space_constraint(x, pltpu.HBM)
    keep_in_vmem = lambda x: pltpu.with_memory_space_constraint(x, pltpu.VMEM)
    x_in, b_in, c_in, dt_in, conv_x, conv_bc = map(stay, (x_in, b_in, c_in, dt_in, conv_x, conv_bc))

    me = lax.axis_index("batch")
    parent = parent_of(counts, order)
    child = (jnp.arange(4 * kids, dtype=jnp.int32) // kids ^ me) * kids
    child = child + jnp.arange(4 * kids, dtype=jnp.int32) % kids
    catalog = jnp.arange(4 * 2 * kids, dtype=jnp.int32)
    owner = jnp.sum(jnp.where(child[:, None] == catalog[None, :], parent[None, :], 0), axis=1)
    slots = owner ^ me
    place = (me % 4).astype(jnp.int32)[None]

    state = stay(par_state.reshape(groups, per_group, width, size))
    x_tails, bc_tails = stay(tail_x), stay(tail_bc.transpose(0, 2, 1, 3))
    offsets = [sum(SPLIT[:k]) for k in range(len(SPLIT))]

    def swap(value, r):
        return lax.ppermute(value, "batch", perm=[(i, i ^ r) for i in range(8)])

    def cast():
        rows = per_group * width + tail_lines
        rows_a = SPLIT[0] * width + tail_lines
        blocks = [(0, SPLIT[0])] + [(at, 4) for at in range(SPLIT[0], per_group, 4)]
        count = len(blocks) + 2

        def kernel(place_ref, *refs):
            ins, outs = refs[: 4 * count], refs[4 * count :]
            for n in range(4):
                cast_kernel(
                    len(blocks), [tail_lines], reach, lines, *ins[count * n : count * n + count], outs[n]
                )
                outs[4 + n // 2][n % 2] = outs[n][:rows_a]

        operands, specs = [], []
        for n in range(4):
            for offset, part in blocks:
                operands.append(state)
                specs.append(
                    pl.BlockSpec(
                        (1, part, width, size),
                        lambda i, p, n=n, at=offset // part: (p[0] ^ n, at, 0, 0),
                    )
                )
            operands += [x_tails, bc_tails]
            specs += [
                pl.BlockSpec((1, reach, wide), lambda i, p, n=n: (0, 0, p[0] ^ n)),
                pl.BlockSpec((1, reach, 2, size), lambda i, p, n=n: (0, 0, 0, p[0] ^ n)),
            ]
        shapes = [(rows, size)] * 4 + [(2, rows_a, size)] * 2
        return pl.pallas_call(
            kernel,
            grid_spec=pltpu.PrefetchScalarGridSpec(
                num_scalar_prefetch=1,
                grid=(1,),
                in_specs=specs,
                out_specs=[pl.BlockSpec(memory_space=pltpu.VMEM)] * len(shapes),
            ),
            out_shape=[pltpu.VMEM(shape, jnp.bfloat16) for shape in shapes],
            compiler_params=params,
            cost_estimate=small,
            name="cast_states",
        )(place, *operands)

    def rearrange(scalars, sources, moves, shapes, tokens, name):
        def kernel(scalars_ref, *refs):
            held, outs = refs[: len(sources)], refs[len(sources) :]
            for out, at, scalar, choices in moves:
                for value, (number, take) in enumerate(choices):

                    def copy(out=out, at=at, number=number, take=take):
                        rows = held[number][...] if take is None else held[number][take]
                        if at is None:
                            outs[out][...] = rows
                        else:
                            outs[out][at] = rows

                    if scalar is None:
                        copy()
                    else:
                        pl.when(scalars_ref[scalar] == value)(copy)

        return pl.pallas_call(
            functools.partial(drop_tokens, kernel, 1 + len(sources), len(tokens)),
            grid_spec=pltpu.PrefetchScalarGridSpec(
                num_scalar_prefetch=1,
                grid=(1,),
                in_specs=[pl.BlockSpec(memory_space=pltpu.VMEM)] * len(sources)
                + [anywhere] * len(tokens),
                out_specs=[pl.BlockSpec(memory_space=pltpu.VMEM)] * len(shapes),
            ),
            out_shape=[pltpu.VMEM(shape, jnp.bfloat16) for shape in shapes],
            compiler_params=params,
            cost_estimate=small,
            name=name,
        )(scalars, *map(keep_in_vmem, sources), *tokens)

    def pick(rows, sources, choices, tokens):
        moves = [
            (j, kid, j * kids + kid, choices) for j in range(4) for kid in range(kids)
        ]
        picked = rearrange(
            slots, sources, moves, [(kids, rows, size)] * 4, tokens, "pick_states"
        )
        return [picked[0]] + [swap(picked[j], j) for j in range(1, 4)]

    def early(c, tokens):
        at = lambda q: (c, 0, q)
        operands = [
            x_in, b_in, c_in, dt_in, dt_bias[:, None], a_log[:, None], skip_row, conv_x, conv_bc
        ]
        return pl.pallas_call(
            functools.partial(drop_tokens, early_kernel, len(operands), len(tokens)),
            grid=(groups,),
            in_specs=[
                pl.BlockSpec((1, length, wide), at),
                pl.BlockSpec((1, length, size), at),
                pl.BlockSpec((1, length, size), at),
                pl.BlockSpec((1, per_group, length), lambda q: (c, q, 0)),
                pl.BlockSpec((per_group, 1), lambda q: (q, 0)),
                pl.BlockSpec((per_group, 1), lambda q: (q, 0)),
                pl.BlockSpec((1, wide), lambda q: (0, q)),
                pl.BlockSpec((taps, wide), lambda q: (0, q)),
                pl.BlockSpec((2, taps, size), lambda q: (0, 0, q)),
                *[anywhere] * len(tokens),
            ],
            out_specs=[pl.BlockSpec(memory_space=pltpu.VMEM)] * 6,
            out_shape=[
                pltpu.VMEM((groups, length, wide), jnp.float32),
                pltpu.VMEM((groups, length, size), jnp.bfloat16),
                pltpu.VMEM((groups, per_group, length), jnp.float32),
                pltpu.VMEM((groups, length, per_group * FIX), jnp.float32),
                pltpu.VMEM((groups, FIX, wide + 2 * size), jnp.bfloat16),
                pltpu.VMEM((groups, 8, wide + 2 * size), jnp.float32),
            ],
            scratch_shapes=[pltpu.VMEM((2, 8 + length, size), jnp.float32)],
            compiler_params=params,
            cost_estimate=small,
            name="early",
        )(*operands, *tokens)

    def late(k, states, states_first, parts, result, tokens):
        part, offset = SPLIT[k], offsets[k]
        chunk = part * width
        operands = [keep_in_vmem(a) for a in (*states_first, *states, *parts[0], *parts[1])]
        specs = [pl.BlockSpec(memory_space=pltpu.VMEM)] * len(operands)
        keep = 1 + len(operands)
        operands += tokens
        specs += [anywhere] * len(tokens)
        alias = {}
        if result is not None:
            alias = {1 + len(operands): 0}
            operands.append(result)
            specs.append(anywhere)
        kernel = functools.partial(late_kernel, offset, part, lines, reach, SPLIT[0] * width)
        return pl.pallas_call(
            functools.partial(drop_tokens, kernel, keep, 1 + len(operands) - keep),
            grid_spec=pltpu.PrefetchScalarGridSpec(
                num_scalar_prefetch=1,
                grid=(1,),
                in_specs=specs,
                out_specs=anywhere,
                scratch_shapes=[
                    pltpu.VMEM((groups, kids, 8 + FIX, max(chunk, 2 * size)), jnp.float32),
                    pltpu.VMEM((groups, kids, length, chunk), jnp.bfloat16),
                    pltpu.SemaphoreType.DMA((groups,)),
                ],
            ),
            out_shape=jax.ShapeDtypeStruct(x_in.shape, jnp.bfloat16),
            input_output_aliases=alias,
            compiler_params=params,
            cost_estimate=small,
            name="late",
        )(place, *operands)

    skip_row = jnp.repeat(d_skip, width)[None, :]
    rows = [SPLIT[0] * width + tail_lines] + [part * width for part in SPLIT[1:]]
    chunks = [pl.ds(sum(rows[:k]), rows[k]) for k in range(len(SPLIT))]
    *own, sent_4, sent_6 = cast()
    inside = [own[0]] + [swap(own[j], j) for j in range(1, 4)]
    crossed_a = [swap(sent_4, 4), swap(sent_6, 6)]

    def cross(k, tokens):
        moves = [(0, j, None, [(j, chunks[k])]) for j in range(4)]
        (sent,) = rearrange(place, inside, moves, [(4, rows[k], size)], tokens, "stack_later")
        return sent, swap(sent, 4)

    def pick_later(k, crossed, tokens):
        choices = [(j, chunks[k]) for j in range(4)] + [(4, j) for j in range(4)]
        return pick(rows[k], [*inside, crossed], choices, tokens)

    parts = [early(0, [own[0], slots])]
    moves = [(0, n, None, [(n, 1)]) for n in range(2)]
    (spread,) = rearrange(
        place, crossed_a, moves, [(2, rows[0], size)], [parts[0][1]], "stack_first"
    )
    passed = swap(spread, 1)
    sent_b, crossed_b = cross(1, [spread])
    parts.append(early(1, [sent_b]))
    choices = [(j, chunks[0]) for j in range(4)] + [(4, 0), (6, 0), (5, 0), (6, 1)]
    states_a = pick(rows[0], [*inside, *crossed_a, passed], choices, [parts[1][1]])
    sent_c, crossed_c = cross(2, [states_a[0], crossed_b])
    states_b = pick_later(1, crossed_b, [sent_c])
    result = late(0, states_a, states_a, parts, None, [states_b[0]])
    states_c = pick_later(2, crossed_c, [stay(result)])
    result = late(1, states_b, states_a, parts, result, [states_c[0]])
    return late(2, states_c, states_a, parts, result, [])


def solution(mesh):
    rows, cols = P(("groups", "batch"), None, "head"), P(("groups", "batch"), "head")
    placed = (
        rows, rows, rows, cols, P("head"), P("head"), P("head"), P(None, "head"),
        P(None, None, "head"), cols, rows, P(("groups", "batch"), None, None, "head"),
        P("groups"), P("groups"),
    )
    local = local_halves if mesh.shape["batch"] == 8 else local_any
    return jax.shard_map(local, mesh=mesh, in_specs=placed, out_specs=rows, check_vma=False)
```

```python
import functools

import jax
import jax.numpy as jnp
from jax import lax
from jax.experimental import pallas as pl
from jax.experimental.pallas import tpu as pltpu
from jax.sharding import PartitionSpec as P

VMEM_LIMIT = 12 * 1024 * 1024
SPLIT = (8, 4, 4)
FIX = 16
LOG2_E = 1.4426950408889634


def drop_tokens(kernel, keep, tokens, *refs):
    kernel(*refs[:keep], *refs[keep + tokens :])


def parent_of(counts, order):
    index = jnp.arange(counts.shape[0], dtype=jnp.int32)
    bounds = jnp.sum(jnp.where(index[None, :] <= index[:, None], counts[None, :], 0), axis=1)
    return jnp.sum((bounds[None, :] <= order[:, None]).astype(jnp.int32), axis=1)


def three_terms(value):
    terms = []
    for _ in range(3):
        terms.append(value.astype(jnp.bfloat16).astype(jnp.float32))
        value = value - terms[-1]
    return jnp.concatenate(terms)


def conv_silu(padded, tail, rows, taps):
    length = rows.shape[0]
    reach = taps.shape[0] - 1
    padded[8 - reach : 8, :] = jnp.broadcast_to(tail, (reach, rows.shape[1])).astype(jnp.float32)
    padded[8 : 8 + length, :] = rows.astype(jnp.float32)
    total = padded[8 - reach : 8 - reach + length, :] * taps[0:1, :]
    for k in range(1, reach + 1):
        total = total + padded[8 - reach + k : 8 - reach + k + length, :] * taps[k : k + 1, :]
    half = 0.5 * total
    return (half + half * jnp.tanh(half)).astype(jnp.bfloat16)


def early_kernel(
    base, x_ref, b_ref, c_ref, dt_ref, bias_ref, alog_ref, skip_ref, taps_x_ref, taps_bc_ref,
    mixed_ref, c_out_ref, column_ref, first_ref, opening_ref, weights_ref, padded,
):
    length, wide = x_ref.shape[1:]
    heads = dt_ref.shape[1]
    q = base + pl.program_id(0)
    width = wide // heads
    half = length // 2

    def convolve(rows, taps, slot):
        bulk = conv_silu(padded.at[slot % 2], 0.0, rows, taps)[FIX:]
        return jnp.concatenate([jnp.zeros((FIX, rows.shape[1]), jnp.bfloat16), bulk])

    b_conv = convolve(b_ref[0], taps_bc_ref[0], 0)
    c_conv = convolve(c_ref[0], taps_bc_ref[1], 1)
    c_out_ref[q] = c_conv
    size = b_ref.shape[2]
    taps = taps_x_ref.shape[0]
    opening_ref[q, :, :wide] = x_ref[0, :FIX]
    opening_ref[q, :, wide : wide + size] = b_ref[0, :FIX]
    opening_ref[q, :, wide + size :] = c_ref[0, :FIX]
    weights_ref[q, :taps, :wide] = taps_x_ref[...]
    weights_ref[q, :taps, wide : wide + size] = taps_bc_ref[0]
    weights_ref[q, :taps, wide + size :] = taps_bc_ref[1]
    weights_ref[q, taps : taps + 1, :wide] = skip_ref[...]
    scores = lax.dot_general(
        c_conv, b_conv, (((1,), (1,)), ((), ())), preferred_element_type=jnp.float32
    )
    raw = dt_ref[0] + bias_ref[...]
    step = jnp.maximum(raw, 0.0) + jnp.log1p(jnp.exp(-jnp.abs(raw)))
    per_token = step * (-jnp.exp(alog_ref[...]))
    upper = lax.broadcasted_iota(jnp.int32, (length, length), 0) <= lax.broadcasted_iota(
        jnp.int32, (length, length), 1
    )
    sums = jnp.dot(
        three_terms(per_token).astype(jnp.bfloat16),
        upper.astype(jnp.float32).astype(jnp.bfloat16),
        preferred_element_type=jnp.float32,
    )
    total = (sums[:heads] + sums[heads : 2 * heads]) + sums[2 * heads :]
    total = total * LOG2_E
    row = total - jnp.log(step) * LOG2_E
    columns = total.T
    column_ref[q] = total
    causal = lax.broadcasted_iota(jnp.int32, (half, half), 0) >= lax.broadcasted_iota(
        jnp.int32, (half, half), 1
    )
    low = lax.broadcasted_iota(jnp.int32, (length, 2 * width), 1) < width
    for pair in range(heads // 2):
        lanes = slice(pair * 2 * width, (pair + 1) * 2 * width)
        x_conv = convolve(x_ref[0, :, lanes], taps_x_ref[:, lanes], pair)
        parts = []
        for head in (2 * pair, 2 * pair + 1):
            column = jnp.broadcast_to(columns[:, head : head + 1], (length, half))
            rows = row[head : head + 1, :]
            near = jnp.exp2(jnp.where(causal, column[:half] - rows[:, :half], -1e30))
            far = jnp.exp2(column[half:] - rows[:, :half])
            last = jnp.exp2(jnp.where(causal, column[half:] - rows[:, half:], -1e30))
            spot = slice(head * FIX, (head + 1) * FIX)
            first_ref[q, :half, spot] = near[:, :FIX]
            first_ref[q, half:, spot] = far[:, :FIX]
            top = (scores[:half, :half] * near).astype(jnp.bfloat16)
            left = (scores[half:, :half] * far).astype(jnp.bfloat16)
            right = (scores[half:, half:] * last).astype(jnp.bfloat16)
            below = jnp.concatenate([left, right], axis=1)
            parts.append(
                jnp.concatenate(
                    [
                        jnp.dot(top, x_conv[:half], preferred_element_type=jnp.float32),
                        jnp.dot(below, x_conv, preferred_element_type=jnp.float32),
                    ]
                )
            )
        mixed_ref[q, :, lanes] = jnp.where(low, parts[0], parts[1]) + skip_ref[
            :, lanes
        ] * x_conv.astype(jnp.float32)


def late_kernel(offset, heads, lines, reach, tail_at, place_ref, *refs):
    count = len(heads)
    tails, states, parts = refs[:4], refs[4 : 4 + 4 * count], refs[4 + 4 * count : -4]
    y_ref, padded, y_part, sems = refs[-4:]
    _, kids, length, wide = y_part.shape
    rows, heads = heads, sum(heads)
    width = wide // heads
    rows = [part * width for part in rows]
    low_first = lax.broadcasted_iota(jnp.int32, (FIX, 2 * width), 1) < width
    contract = (((1,), (1,)), ((), ()))

    def add(j, kid):
        q = place_ref[0] ^ j
        mixed_ref, held_ref, column_ref, first_ref, opening_ref, weights_ref = parts[
            6 * kid : 6 * kid + 6
        ]
        size = held_ref.shape[2]
        per_group = column_ref.shape[1]
        group_wide = opening_ref.shape[2] - 2 * size
        tail_rows = pl.ds(tail_at, -(-lines * reach // 16) * 16)
        tail = tails[j][kid, tail_rows].astype(jnp.float32)
        state = jnp.concatenate([states[4 * n + j][kid, : rows[n]] for n in range(count)])

        def opening(start, stop, at):
            tap_rows = []
            for k in range(reach):
                first = k * lines + at
                count = (stop - start) // 128
                here = [tail[first + n : first + n + 1] for n in range(count)]
                tap_rows.append(jnp.concatenate(here, axis=1))
            return conv_silu(
                padded.at[j, kid, :, : stop - start],
                jnp.concatenate(tap_rows),
                opening_ref[q, :, start:stop],
                weights_ref[q, : reach + 1, start:stop],
            )

        bc_first = opening(group_wide, group_wide + 2 * size, lines - 2)
        b_first, c_first = bc_first[:, :size], bc_first[:, size:]
        start = offset * width
        x_all = opening(start, start + wide, start // 128).astype(jnp.float32)
        skipped = weights_ref[q, reach + 1 : reach + 2, start : start + wide] * x_all
        c_conv = jnp.concatenate([c_first, held_ref[q, FIX:]])
        terms = three_terms(jnp.exp2(column_ref[q]))
        terms = jnp.concatenate([terms, jnp.zeros((per_group, length), jnp.float32)])
        spread_row = lax.broadcasted_iota(jnp.int32, (4 * per_group, wide), 0)
        spread_lane = lax.broadcasted_iota(jnp.int32, (4 * per_group, wide), 1)
        spread = spread_row % per_group == offset + spread_lane // width
        grow = jnp.dot(
            terms.T.astype(jnp.bfloat16),
            spread.astype(jnp.float32).astype(jnp.bfloat16),
            preferred_element_type=jnp.float32,
        )
        term = lax.dot_general(c_conv, state, contract, preferred_element_type=jnp.float32)
        carried = (term * grow).astype(jnp.bfloat16)
        scores = lax.dot_general(
            c_conv,
            jnp.concatenate([b_first] * heads),
            contract,
            preferred_element_type=jnp.float32,
        )
        here = slice(offset * FIX, (offset + heads) * FIX)
        mixing = (scores * first_ref[q, :, here]).astype(jnp.bfloat16)
        for pair in range(heads // 2):
            lanes = slice(pair * 2 * width, (pair + 1) * 2 * width)
            x_first = x_all[:, lanes]
            stacked = [jnp.where(low_first, x_first, 0.0), jnp.where(low_first, 0.0, x_first)]
            if pair > 0:
                stacked = [jnp.zeros((2 * pair * FIX, 2 * width), jnp.float32)] + stacked
            if 2 * pair + 2 < heads:
                spare = (heads - 2 * pair - 2) * FIX
                stacked = stacked + [jnp.zeros((spare, 2 * width), jnp.float32)]
            part = jnp.dot(
                mixing,
                jnp.concatenate(stacked).astype(jnp.bfloat16),
                preferred_element_type=jnp.float32,
            )
            part = jnp.concatenate([part[:FIX] + skipped[:, lanes], part[FIX:]])
            whole = slice(start + lanes.start, start + lanes.stop)
            y_part[j, kid, :, lanes] = (
                mixed_ref[q, :, whole] + part + carried[:, lanes].astype(jnp.float32)
            ).astype(jnp.bfloat16)

    copies = []
    for j in range(4):
        for kid in range(kids):
            add(j, kid)
        start = (place_ref[0] ^ j) * (y_ref.shape[2] // 4) + offset * width
        lanes = pl.ds(pl.multiple_of(start, 128), wide)
        copies.append(pltpu.make_async_copy(y_part.at[j], y_ref.at[:, :, lanes], sems.at[j]))
        copies[-1].start()
    for copy in copies:
        copy.wait()


def cast_kernel(parts, tailed, reach, lines, *refs):
    count = len(tailed)
    ins, outs = refs[:-count], refs[-count:]
    states, tails = ins[: parts * count], ins[parts * count :]
    for j, out_ref in enumerate(outs):
        start = 0
        for at in range(parts):
            state = states[parts * j + at][0]
            rows = state.shape[0] * state.shape[1]
            out_ref[start : start + rows] = state.reshape(rows, state.shape[2]).astype(jnp.bfloat16)
            start += rows
            if at == 0 and tailed[j]:
                x_tail = tails[2 * j][0].astype(jnp.float32)
                bc_tail = tails[2 * j + 1][0].astype(jnp.float32)
                pieces = []
                for k in range(reach):
                    pieces += [x_tail[k : k + 1, i * 128 : i * 128 + 128] for i in range(lines - 2)]
                    pieces.append(bc_tail[k])
                spare = tailed[j] - lines * reach
                pieces.append(jnp.zeros((spare, 128), jnp.float32))
                out_ref[start : start + tailed[j]] = jnp.concatenate(pieces).astype(jnp.bfloat16)
                start += tailed[j]


def within_kernel(
    parent_ref,
    x_ref,
    b_ref,
    c_ref,
    dt_ref,
    bias_ref,
    alog_ref,
    skip_ref,
    taps_x_ref,
    taps_bc_ref,
    tail_x_ref,
    tail_bc_ref,
    mixed_ref,
    c_out_ref,
    grow_ref,
    padded,
):
    length = x_ref.shape[1]
    heads = dt_ref.shape[1]
    width = x_ref.shape[2] // heads
    b_conv = conv_silu(padded, tail_bc_ref[0, 0], b_ref[0], taps_bc_ref[0])
    c_conv = conv_silu(padded, tail_bc_ref[0, 1], c_ref[0], taps_bc_ref[1])
    c_out_ref[0] = c_conv
    scores = lax.dot_general(
        c_conv, b_conv, (((1,), (1,)), ((), ())), preferred_element_type=jnp.float32
    )
    raw = dt_ref[0] + bias_ref[...]
    step = jnp.maximum(raw, 0.0) + jnp.log1p(jnp.exp(-jnp.abs(raw)))
    per_token = step * (-jnp.exp(alog_ref[...]))
    row = lax.broadcasted_iota(jnp.int32, (length, length), 0)
    col = lax.broadcasted_iota(jnp.int32, (length, length), 1)
    upper = (row <= col).astype(jnp.float32)
    total = lax.dot_general(
        per_token,
        upper,
        (((1,), (0,)), ((), ())),
        precision=lax.Precision.HIGHEST,
        preferred_element_type=jnp.float32,
    )
    total_t = total.T
    grow_ref[0, 0] = jnp.exp(total_t)
    causal = row >= col
    low = lax.broadcasted_iota(jnp.int32, (length, 2 * width), 1) < width
    for pair in range(heads // 2):
        lanes = slice(pair * 2 * width, (pair + 1) * 2 * width)
        x_conv = conv_silu(
            padded, tail_x_ref[0, :, lanes], x_ref[0, :, lanes], taps_x_ref[:, lanes]
        )
        parts = []
        for head in (2 * pair, 2 * pair + 1):
            gap = total_t[:, head : head + 1] - total[head : head + 1, :]
            factor = jnp.exp(jnp.where(causal, gap, -1e30))
            mixing = (scores * factor * step[head : head + 1, :]).astype(jnp.bfloat16)
            parts.append(jnp.dot(mixing, x_conv, preferred_element_type=jnp.float32))
        mixed_ref[0, :, lanes] = (
            jnp.where(low, parts[0], parts[1]) + skip_ref[:, lanes] * x_conv.astype(jnp.float32)
        )


def carried_kernel(state_ref, c_ref, grow_ref, mixed_ref, y_ref):
    sources, _, part, width, size = state_ref.shape
    length = c_ref.shape[1]
    low = lax.broadcasted_iota(jnp.int32, (length, 2 * width), 1) < width
    c_conv = c_ref[0]
    for source in range(sources):
        state = state_ref[source, 0].reshape(part * width, size)
        term = lax.dot_general(
            c_conv, state, (((1,), (1,)), ((), ())), preferred_element_type=jnp.float32
        )
        for pair in range(part // 2):
            head = source * part + 2 * pair
            grow = jnp.where(
                low, grow_ref[0, 0, :, head : head + 1], grow_ref[0, 0, :, head + 1 : head + 2]
            )
            here = slice(2 * pair * width, (2 * pair + 2) * width)
            lanes = slice(head * width, (head + 2) * width)
            carried = (term[:, here] * grow).astype(jnp.bfloat16).astype(jnp.float32)
            y_ref[0, :, lanes] = (mixed_ref[0, :, lanes] + carried).astype(jnp.bfloat16)


def pick_kernel(parent_ref, state_ref, out_ref):
    out_ref[...] = state_ref[...]


def local_any(
    x_in,
    b_in,
    c_in,
    dt_in,
    dt_bias,
    a_log,
    d_skip,
    conv_x,
    conv_bc,
    par_state,
    tail_x,
    tail_bc,
    counts,
    order,
):
    kids, length, columns = x_in.shape
    heads = dt_in.shape[1]
    width, size = par_state.shape[2:]
    ways = lax.axis_size("batch")
    groups = b_in.shape[2] // size
    per_group = heads // groups
    part = heads // ways
    wide = per_group * width
    reach = tail_x.shape[1]
    parents_all = counts.shape[0]
    kids_all = order.shape[0]

    parent = parent_of(counts, order)
    own = lax.dynamic_slice_in_dim(parent, lax.axis_index("batch") * kids, kids)

    sent = par_state.astype(jnp.bfloat16).reshape(ways, part, width, size)
    shares = lax.all_to_all(sent, "batch", split_axis=0, concat_axis=0, tiled=True)

    tails = jnp.concatenate([tail_x.reshape(-1), tail_bc.reshape(-1)])
    tails = jnp.broadcast_to(tails[None], (ways, tails.shape[0]))
    tails = lax.all_to_all(tails, "batch", split_axis=0, concat_axis=0, tiled=True)
    tails_x = tails[:, : reach * columns].reshape(parents_all, reach, columns)
    tails_bc = tails[:, reach * columns :].reshape(parents_all, 2, reach, groups * size)

    picked = pl.pallas_call(
        pick_kernel,
        grid_spec=pltpu.PrefetchScalarGridSpec(
            num_scalar_prefetch=1,
            grid=(kids_all,),
            in_specs=[pl.BlockSpec((1, part, width, size), lambda i, p: (p[i], 0, 0, 0))],
            out_specs=pl.BlockSpec((1, part, width, size), lambda i, p: (i, 0, 0, 0)),
        ),
        out_shape=jax.ShapeDtypeStruct((kids_all, part, width, size), jnp.bfloat16),
        cost_estimate=pl.CostEstimate(
            flops=0, bytes_accessed=4 * kids_all * part * width * size, transcendentals=0
        ),
        name="pick_states",
    )(parent, shares)
    states = lax.all_to_all(
        picked.reshape(ways, kids, part, width, size), "batch", split_axis=0, concat_axis=0, tiled=True
    )

    skip_row = jnp.repeat(d_skip, width)[None, :]
    mixed, c_conv, grow = pl.pallas_call(
        within_kernel,
        grid_spec=pltpu.PrefetchScalarGridSpec(
            num_scalar_prefetch=1,
            grid=(kids, groups),
            in_specs=[
                pl.BlockSpec((1, length, wide), lambda c, q, p: (c, 0, q)),
                pl.BlockSpec((1, length, size), lambda c, q, p: (c, 0, q)),
                pl.BlockSpec((1, length, size), lambda c, q, p: (c, 0, q)),
                pl.BlockSpec((1, per_group, length), lambda c, q, p: (c, q, 0)),
                pl.BlockSpec((per_group, 1), lambda c, q, p: (q, 0)),
                pl.BlockSpec((per_group, 1), lambda c, q, p: (q, 0)),
                pl.BlockSpec((1, wide), lambda c, q, p: (0, q)),
                pl.BlockSpec((reach + 1, wide), lambda c, q, p: (0, q)),
                pl.BlockSpec((2, reach + 1, size), lambda c, q, p: (0, 0, q)),
                pl.BlockSpec((1, reach, wide), lambda c, q, p: (p[c], 0, q)),
                pl.BlockSpec((1, 2, reach, size), lambda c, q, p: (p[c], 0, 0, q)),
            ],
            out_specs=[
                pl.BlockSpec((1, length, wide), lambda c, q, p: (c, 0, q)),
                pl.BlockSpec((1, length, size), lambda c, q, p: (c, 0, q)),
                pl.BlockSpec((1, 1, length, per_group), lambda c, q, p: (c, q, 0, 0)),
            ],
            scratch_shapes=[pltpu.VMEM((8 + length, size), jnp.float32)],
        ),
        out_shape=[
            jax.ShapeDtypeStruct((kids, length, columns), jnp.float32),
            jax.ShapeDtypeStruct((kids, length, groups * size), jnp.bfloat16),
            jax.ShapeDtypeStruct((kids, groups, length, per_group), jnp.float32),
        ],
        compiler_params=pltpu.CompilerParams(vmem_limit_bytes=4 * VMEM_LIMIT),
        cost_estimate=pl.CostEstimate(
            flops=4 * kids * heads * length * length * width,
            bytes_accessed=6 * kids * length * columns,
            transcendentals=kids * heads * length * length,
        ),
        name="within",
    )(
        own,
        x_in,
        b_in,
        c_in,
        dt_in,
        dt_bias[:, None],
        a_log[:, None],
        skip_row,
        conv_x,
        conv_bc,
        tails_x,
        tails_bc,
    )

    sources = per_group // part
    return pl.pallas_call(
        carried_kernel,
        grid=(kids, groups),
        in_specs=[
            pl.BlockSpec((sources, 1, part, width, size), lambda c, q: (q, c, 0, 0, 0)),
            pl.BlockSpec((1, length, size), lambda c, q: (c, 0, q)),
            pl.BlockSpec((1, 1, length, per_group), lambda c, q: (c, q, 0, 0)),
            pl.BlockSpec((1, length, wide), lambda c, q: (c, 0, q)),
        ],
        out_specs=pl.BlockSpec((1, length, wide), lambda c, q: (c, 0, q)),
        out_shape=jax.ShapeDtypeStruct((kids, length, columns), jnp.bfloat16),
        compiler_params=pltpu.CompilerParams(vmem_limit_bytes=4 * VMEM_LIMIT),
        cost_estimate=pl.CostEstimate(
            flops=2 * kids * length * columns * size,
            bytes_accessed=8 * kids * length * columns,
            transcendentals=0,
        ),
        name="carried",
    )(states, c_conv, grow, mixed)


def local_halves(
    x_in, b_in, c_in, dt_in, dt_bias, a_log, d_skip, conv_x, conv_bc,
    par_state, tail_x, tail_bc, counts, order,
):
    kids, length, columns = x_in.shape
    heads = dt_in.shape[1]
    width, size = par_state.shape[2:]
    groups = b_in.shape[2] // size
    per_group = heads // groups
    wide = per_group * width
    taps = conv_x.shape[0]
    reach = taps - 1
    lines = (wide + 2 * size) // 128
    tail_lines = -(-lines * reach // 16) * 16
    params = pltpu.CompilerParams(vmem_limit_bytes=VMEM_LIMIT)
    anywhere = pl.BlockSpec(memory_space=pl.ANY)
    small = pl.CostEstimate(flops=1, bytes_accessed=1, transcendentals=0)

    stay = lambda x: pltpu.with_memory_space_constraint(x, pltpu.HBM)
    keep_in_vmem = lambda x: pltpu.with_memory_space_constraint(x, pltpu.VMEM)
    x_in, b_in, c_in, dt_in, conv_x, conv_bc = map(stay, (x_in, b_in, c_in, dt_in, conv_x, conv_bc))

    me = lax.axis_index("batch")
    parent = parent_of(counts, order)
    child = (jnp.arange(4 * kids, dtype=jnp.int32) // kids ^ me) * kids
    child = child + jnp.arange(4 * kids, dtype=jnp.int32) % kids
    catalog = jnp.arange(4 * 2 * kids, dtype=jnp.int32)
    owner = jnp.sum(jnp.where(child[:, None] == catalog[None, :], parent[None, :], 0), axis=1)
    slots = owner ^ me
    place = (me % 4).astype(jnp.int32)[None]

    state = stay(par_state.reshape(groups, per_group, width, size))
    x_tails, bc_tails = stay(tail_x), stay(tail_bc.transpose(0, 2, 1, 3))
    offsets = [sum(SPLIT[:k]) for k in range(len(SPLIT))]

    def swap(value, r):
        return lax.ppermute(value, "batch", perm=[(i, i ^ r) for i in range(8)])

    def cast():
        rows = per_group * width + tail_lines
        rows_a = SPLIT[0] * width + tail_lines
        blocks = [(0, SPLIT[0])] + [(at, 4) for at in range(SPLIT[0], per_group, 4)]
        count = len(blocks) + 2

        def kernel(place_ref, *refs):
            ins, outs = refs[: 4 * count], refs[4 * count :]
            quarters = [outs[0], outs[2].at[0], outs[1], outs[2].at[1]]
            for n, out_ref in enumerate(quarters):
                cast_kernel(
                    len(blocks), [tail_lines], reach, lines, *ins[count * n : count * n + count], out_ref
                )
                outs[3 + n // 2][n % 2] = out_ref[:rows_a]

        operands, specs = [], []
        for n in range(4):
            for offset, part in blocks:
                operands.append(state)
                specs.append(
                    pl.BlockSpec(
                        (1, part, width, size),
                        lambda i, p, n=n, at=offset // part: (p[0] ^ n, at, 0, 0),
                    )
                )
            operands += [x_tails, bc_tails]
            specs += [
                pl.BlockSpec((1, reach, wide), lambda i, p, n=n: (0, 0, p[0] ^ n)),
                pl.BlockSpec((1, reach, 2, size), lambda i, p, n=n: (0, 0, 0, p[0] ^ n)),
            ]
        shapes = [(rows, size)] * 2 + [(2, rows, size)] + [(2, rows_a, size)] * 2
        return pl.pallas_call(
            kernel,
            grid_spec=pltpu.PrefetchScalarGridSpec(
                num_scalar_prefetch=1,
                grid=(1,),
                in_specs=specs,
                out_specs=[pl.BlockSpec(memory_space=pltpu.VMEM)] * len(shapes),
            ),
            out_shape=[pltpu.VMEM(shape, jnp.bfloat16) for shape in shapes],
            compiler_params=params,
            cost_estimate=small,
            name="cast_states",
        )(place, *operands)

    def rearrange(scalars, sources, moves, shapes, tokens, name):
        def kernel(scalars_ref, *refs):
            held, outs = refs[: len(sources)], refs[len(sources) :]
            for out, at, scalar, choices in moves:
                for value, (number, take) in enumerate(choices):

                    def copy(out=out, at=at, number=number, take=take):
                        rows = held[number][...] if take is None else held[number][take]
                        if at is None:
                            outs[out][...] = rows
                        else:
                            outs[out][at] = rows

                    if scalar is None:
                        copy()
                    else:
                        pl.when(scalars_ref[scalar] == value)(copy)

        return pl.pallas_call(
            functools.partial(drop_tokens, kernel, 1 + len(sources), len(tokens)),
            grid_spec=pltpu.PrefetchScalarGridSpec(
                num_scalar_prefetch=1,
                grid=(1,),
                in_specs=[pl.BlockSpec(memory_space=pltpu.VMEM)] * len(sources)
                + [anywhere] * len(tokens),
                out_specs=[pl.BlockSpec(memory_space=pltpu.VMEM)] * len(shapes),
            ),
            out_shape=[pltpu.VMEM(shape, jnp.bfloat16) for shape in shapes],
            compiler_params=params,
            cost_estimate=small,
            name=name,
        )(scalars, *map(keep_in_vmem, sources), *tokens)

    def pick(rows, sources, choices, tokens):
        moves = [
            (j, kid, j * kids + kid, choices) for j in range(4) for kid in range(kids)
        ]
        picked = rearrange(
            slots, sources, moves, [(kids, rows, size)] * 4, tokens, "pick_states"
        )
        return [picked[0]] + [swap(picked[j], j) for j in range(1, 4)]

    def early(c, pieces, piece, before, tokens):
        per = groups // pieces
        at = lambda q: (c, 0, per * piece + q)
        operands = [
            x_in, b_in, c_in, dt_in, dt_bias[:, None], a_log[:, None], skip_row, conv_x, conv_bc
        ]
        keep = len(operands)
        tokens = list(tokens) + [keep_in_vmem(a) for a in before]
        first = keep + len(tokens) - len(before)
        return pl.pallas_call(
            functools.partial(
                drop_tokens, functools.partial(early_kernel, per * piece), keep, len(tokens)
            ),
            grid=(per,),
            in_specs=[
                pl.BlockSpec((1, length, wide), at),
                pl.BlockSpec((1, length, size), at),
                pl.BlockSpec((1, length, size), at),
                pl.BlockSpec((1, per_group, length), lambda q: (c, per * piece + q, 0)),
                pl.BlockSpec((per_group, 1), lambda q: (per * piece + q, 0)),
                pl.BlockSpec((per_group, 1), lambda q: (per * piece + q, 0)),
                pl.BlockSpec((1, wide), lambda q: (0, per * piece + q)),
                pl.BlockSpec((taps, wide), lambda q: (0, per * piece + q)),
                pl.BlockSpec((2, taps, size), lambda q: (0, 0, per * piece + q)),
                *[anywhere] * len(tokens),
            ],
            out_specs=[pl.BlockSpec(memory_space=pltpu.VMEM)] * 6,
            out_shape=[
                pltpu.VMEM((groups, length, wide), jnp.float32),
                pltpu.VMEM((groups, length, size), jnp.bfloat16),
                pltpu.VMEM((groups, per_group, length), jnp.float32),
                pltpu.VMEM((groups, length, per_group * FIX), jnp.float32),
                pltpu.VMEM((groups, FIX, wide + 2 * size), jnp.bfloat16),
                pltpu.VMEM((groups, 8, wide + 2 * size), jnp.float32),
            ],
            input_output_aliases={first + i: i for i in range(len(before))},
            scratch_shapes=[pltpu.VMEM((2, 8 + length, size), jnp.float32)],
            compiler_params=params,
            cost_estimate=small,
            name="early",
        )(*operands, *tokens)

    def late(ks, states, parts, result, tokens):
        offset = offsets[ks[0]]
        chunk = sum(SPLIT[k] for k in ks) * width
        operands = [keep_in_vmem(a) for a in (*states[0], *sum((states[k] for k in ks), []), *parts[0], *parts[1])]
        specs = [pl.BlockSpec(memory_space=pltpu.VMEM)] * len(operands)
        keep = 1 + len(operands)
        operands += tokens
        specs += [anywhere] * len(tokens)
        alias = {}
        if result is not None:
            alias = {1 + len(operands): 0}
            operands.append(result)
            specs.append(anywhere)
        kernel = functools.partial(
            late_kernel, offset, [SPLIT[k] for k in ks], lines, reach, SPLIT[0] * width
        )
        return pl.pallas_call(
            functools.partial(drop_tokens, kernel, keep, 1 + len(operands) - keep),
            grid_spec=pltpu.PrefetchScalarGridSpec(
                num_scalar_prefetch=1,
                grid=(1,),
                in_specs=specs,
                out_specs=anywhere,
                scratch_shapes=[
                    pltpu.VMEM((groups, kids, 8 + FIX, max(chunk, 2 * size)), jnp.float32),
                    pltpu.VMEM((groups, kids, length, chunk), jnp.bfloat16),
                    pltpu.SemaphoreType.DMA((groups,)),
                ],
            ),
            out_shape=jax.ShapeDtypeStruct(x_in.shape, jnp.bfloat16),
            input_output_aliases=alias,
            compiler_params=params,
            cost_estimate=small,
            name="late",
        )(place, *operands)

    skip_row = jnp.repeat(d_skip, width)[None, :]
    rows = [SPLIT[0] * width + tail_lines] + [part * width for part in SPLIT[1:]]
    chunks = [pl.ds(sum(rows[:k]), rows[k]) for k in range(len(SPLIT))]
    own, own_2, own_13, sent_4, sent_6 = cast()
    crossed_a = [swap(sent_4, 4), swap(sent_6, 6)]
    along_y, along_z = swap(own_13, 1), swap(own_2, 2)
    parts = [early(0, 1, 0, [], [own, slots])]
    (turn,) = rearrange(
        place, [along_y], [(0, None, None, [(0, 1)])], [own.shape], [parts[0][1]], "stack_turn"
    )
    inside = [own, along_y, along_z, swap(turn, 2)]

    def inside_rows(k):
        return [(0, chunks[k]), (1, (0, chunks[k])), (2, chunks[k]), (3, chunks[k])]

    def cross(k, tokens):
        moves = [(0, j, None, [choice]) for j, choice in enumerate(inside_rows(k))]
        (sent,) = rearrange(place, inside, moves, [(4, rows[k], size)], tokens, "stack_later")
        return sent, swap(sent, 4)

    def pick_later(k, crossed, tokens):
        choices = inside_rows(k) + [(4, j) for j in range(4)]
        return pick(rows[k], [*inside, crossed], choices, tokens)

    second = early(1, 2, 0, [], [turn])
    moves = [(0, n, None, [(n, 1)]) for n in range(2)]
    (spread,) = rearrange(
        place, crossed_a, moves, [(2, rows[0], size)], [second[1]], "stack_first"
    )
    passed = swap(spread, 1)
    sent_b, crossed_b = cross(1, [spread])
    second = early(1, 2, 1, second, [sent_b])
    parts.append(second)
    choices = inside_rows(0) + [(4, 0), (6, 0), (5, 0), (6, 1)]
    states = [pick(rows[0], [*inside, *crossed_a, passed], choices, [second[1]])]
    sent_c, crossed_c = cross(2, [states[0][0], crossed_b])
    states.append(pick_later(1, crossed_b, [sent_c]))
    states.append(pick_later(2, crossed_c, [states[1][0]]))
    result = late([0, 1], states, parts, None, [states[2][0]])
    return late([2], states, parts, result, [])


def solution(mesh):
    rows, cols = P(("groups", "batch"), None, "head"), P(("groups", "batch"), "head")
    placed = (
        rows, rows, rows, cols, P("head"), P("head"), P("head"), P(None, "head"),
        P(None, None, "head"), cols, rows, P(("groups", "batch"), None, None, "head"),
        P("groups"), P("groups"),
    )
    local = local_halves if mesh.shape["batch"] == 8 else local_any
    return jax.shard_map(local, mesh=mesh, in_specs=placed, out_specs=rows, check_vma=False)
```

```python
import functools

import jax
import jax.numpy as jnp
from jax import lax
from jax.experimental import pallas as pl
from jax.experimental.pallas import tpu as pltpu
from jax.sharding import PartitionSpec as P

VMEM_LIMIT = 12 * 1024 * 1024
SPLIT = (8, 4, 4)
FIX = 16
LOG2_E = 1.4426950408889634


def drop_tokens(kernel, keep, tokens, *refs):
    kernel(*refs[:keep], *refs[keep + tokens :])


def parent_of(counts, order):
    index = jnp.arange(counts.shape[0], dtype=jnp.int32)
    bounds = jnp.sum(jnp.where(index[None, :] <= index[:, None], counts[None, :], 0), axis=1)
    return jnp.sum((bounds[None, :] <= order[:, None]).astype(jnp.int32), axis=1)


def three_terms(value):
    terms = []
    for _ in range(3):
        terms.append(value.astype(jnp.bfloat16).astype(jnp.float32))
        value = value - terms[-1]
    return jnp.concatenate(terms)


def conv_silu(padded, tail, rows, taps):
    length = rows.shape[0]
    reach = taps.shape[0] - 1
    padded[8 - reach : 8, :] = jnp.broadcast_to(tail, (reach, rows.shape[1])).astype(jnp.float32)
    padded[8 : 8 + length, :] = rows.astype(jnp.float32)
    total = padded[8 - reach : 8 - reach + length, :] * taps[0:1, :]
    for k in range(1, reach + 1):
        total = total + padded[8 - reach + k : 8 - reach + k + length, :] * taps[k : k + 1, :]
    half = 0.5 * total
    return (half + half * jnp.tanh(half)).astype(jnp.bfloat16)


def early_kernel(
    base, x_ref, b_ref, c_ref, dt_ref, bias_ref, alog_ref, skip_ref, taps_x_ref, taps_bc_ref,
    mixed_ref, c_out_ref, column_ref, first_ref, opening_ref, weights_ref, padded,
):
    length, wide = x_ref.shape[1:]
    heads = dt_ref.shape[1]
    q = base + pl.program_id(0)
    width = wide // heads
    half = length // 2

    def convolve(rows, taps, slot):
        bulk = conv_silu(padded.at[slot % 2], 0.0, rows, taps)[FIX:]
        return jnp.concatenate([jnp.zeros((FIX, rows.shape[1]), jnp.bfloat16), bulk])

    b_conv = convolve(b_ref[0], taps_bc_ref[0], 0)
    c_conv = convolve(c_ref[0], taps_bc_ref[1], 1)
    c_out_ref[q] = c_conv
    size = b_ref.shape[2]
    taps = taps_x_ref.shape[0]
    opening_ref[q, :, :wide] = x_ref[0, :FIX]
    opening_ref[q, :, wide : wide + size] = b_ref[0, :FIX]
    opening_ref[q, :, wide + size :] = c_ref[0, :FIX]
    weights_ref[q, :taps, :wide] = taps_x_ref[...]
    weights_ref[q, :taps, wide : wide + size] = taps_bc_ref[0]
    weights_ref[q, :taps, wide + size :] = taps_bc_ref[1]
    weights_ref[q, taps : taps + 1, :wide] = skip_ref[...]
    scores = lax.dot_general(
        c_conv, b_conv, (((1,), (1,)), ((), ())), preferred_element_type=jnp.float32
    )
    raw = dt_ref[0] + bias_ref[...]
    step = jnp.maximum(raw, 0.0) + jnp.log1p(jnp.exp(-jnp.abs(raw)))
    per_token = step * (-jnp.exp(alog_ref[...]))
    upper = lax.broadcasted_iota(jnp.int32, (length, length), 0) <= lax.broadcasted_iota(
        jnp.int32, (length, length), 1
    )
    sums = jnp.dot(
        three_terms(per_token).astype(jnp.bfloat16),
        upper.astype(jnp.float32).astype(jnp.bfloat16),
        preferred_element_type=jnp.float32,
    )
    total = (sums[:heads] + sums[heads : 2 * heads]) + sums[2 * heads :]
    total = total * LOG2_E
    row = total - jnp.log(step) * LOG2_E
    columns = total.T
    column_ref[q] = total
    causal = lax.broadcasted_iota(jnp.int32, (half, half), 0) >= lax.broadcasted_iota(
        jnp.int32, (half, half), 1
    )
    low = lax.broadcasted_iota(jnp.int32, (length, 2 * width), 1) < width
    for pair in range(heads // 2):
        lanes = slice(pair * 2 * width, (pair + 1) * 2 * width)
        x_conv = convolve(x_ref[0, :, lanes], taps_x_ref[:, lanes], pair)
        parts = []
        for head in (2 * pair, 2 * pair + 1):
            column = jnp.broadcast_to(columns[:, head : head + 1], (length, half))
            rows = row[head : head + 1, :]
            near = jnp.exp2(jnp.where(causal, column[:half] - rows[:, :half], -1e30))
            far = jnp.exp2(column[half:] - rows[:, :half])
            last = jnp.exp2(jnp.where(causal, column[half:] - rows[:, half:], -1e30))
            spot = slice(head * FIX, (head + 1) * FIX)
            first_ref[q, :half, spot] = near[:, :FIX]
            first_ref[q, half:, spot] = far[:, :FIX]
            top = (scores[:half, :half] * near).astype(jnp.bfloat16)
            left = (scores[half:, :half] * far).astype(jnp.bfloat16)
            right = (scores[half:, half:] * last).astype(jnp.bfloat16)
            below = jnp.concatenate([left, right], axis=1)
            parts.append(
                jnp.concatenate(
                    [
                        jnp.dot(top, x_conv[:half], preferred_element_type=jnp.float32),
                        jnp.dot(below, x_conv, preferred_element_type=jnp.float32),
                    ]
                )
            )
        mixed_ref[q, :, lanes] = jnp.where(low, parts[0], parts[1]) + skip_ref[
            :, lanes
        ] * x_conv.astype(jnp.float32)


def late_kernel(offset, heads, lines, reach, tail_at, place_ref, *refs):
    count = len(heads)
    tails, states, parts = refs[:4], refs[4 : 4 + 4 * count], refs[4 + 4 * count : -4]
    y_ref, padded, y_part, sems = refs[-4:]
    _, kids, length, wide = y_part.shape
    rows, heads = heads, sum(heads)
    width = wide // heads
    rows = [part * width for part in rows]
    low_first = lax.broadcasted_iota(jnp.int32, (FIX, 2 * width), 1) < width
    contract = (((1,), (1,)), ((), ()))

    def add(j, kid):
        q = place_ref[0] ^ j
        mixed_ref, held_ref, column_ref, first_ref, opening_ref, weights_ref = parts[
            6 * kid : 6 * kid + 6
        ]
        size = held_ref.shape[2]
        per_group = column_ref.shape[1]
        group_wide = opening_ref.shape[2] - 2 * size
        tail_rows = pl.ds(tail_at, -(-lines * reach // 16) * 16)
        tail = tails[j][kid, tail_rows].astype(jnp.float32)
        state = jnp.concatenate([states[4 * n + j][kid, : rows[n]] for n in range(count)])

        def opening(start, stop, at):
            tap_rows = []
            for k in range(reach):
                first = k * lines + at
                count = (stop - start) // 128
                here = [tail[first + n : first + n + 1] for n in range(count)]
                tap_rows.append(jnp.concatenate(here, axis=1))
            return conv_silu(
                padded.at[j, kid, :, : stop - start],
                jnp.concatenate(tap_rows),
                opening_ref[q, :, start:stop],
                weights_ref[q, : reach + 1, start:stop],
            )

        bc_first = opening(group_wide, group_wide + 2 * size, lines - 2)
        b_first, c_first = bc_first[:, :size], bc_first[:, size:]
        start = offset * width
        x_all = opening(start, start + wide, start // 128).astype(jnp.float32)
        skipped = weights_ref[q, reach + 1 : reach + 2, start : start + wide] * x_all
        c_conv = jnp.concatenate([c_first, held_ref[q, FIX:]])
        terms = three_terms(jnp.exp2(column_ref[q]))
        terms = jnp.concatenate([terms, jnp.zeros((per_group, length), jnp.float32)])
        spread_row = lax.broadcasted_iota(jnp.int32, (4 * per_group, wide), 0)
        spread_lane = lax.broadcasted_iota(jnp.int32, (4 * per_group, wide), 1)
        spread = spread_row % per_group == offset + spread_lane // width
        grow = jnp.dot(
            terms.T.astype(jnp.bfloat16),
            spread.astype(jnp.float32).astype(jnp.bfloat16),
            preferred_element_type=jnp.float32,
        )
        term = lax.dot_general(c_conv, state, contract, preferred_element_type=jnp.float32)
        carried = (term * grow).astype(jnp.bfloat16)
        scores = lax.dot_general(
            c_conv,
            jnp.concatenate([b_first] * heads),
            contract,
            preferred_element_type=jnp.float32,
        )
        here = slice(offset * FIX, (offset + heads) * FIX)
        mixing = (scores * first_ref[q, :, here]).astype(jnp.bfloat16)
        for pair in range(heads // 2):
            lanes = slice(pair * 2 * width, (pair + 1) * 2 * width)
            x_first = x_all[:, lanes]
            stacked = [jnp.where(low_first, x_first, 0.0), jnp.where(low_first, 0.0, x_first)]
            if pair > 0:
                stacked = [jnp.zeros((2 * pair * FIX, 2 * width), jnp.float32)] + stacked
            if 2 * pair + 2 < heads:
                spare = (heads - 2 * pair - 2) * FIX
                stacked = stacked + [jnp.zeros((spare, 2 * width), jnp.float32)]
            part = jnp.dot(
                mixing,
                jnp.concatenate(stacked).astype(jnp.bfloat16),
                preferred_element_type=jnp.float32,
            )
            part = jnp.concatenate([part[:FIX] + skipped[:, lanes], part[FIX:]])
            whole = slice(start + lanes.start, start + lanes.stop)
            y_part[j, kid, :, lanes] = (
                mixed_ref[q, :, whole] + part + carried[:, lanes].astype(jnp.float32)
            ).astype(jnp.bfloat16)

    copies = []
    for j in range(4):
        for kid in range(kids):
            add(j, kid)
        start = (place_ref[0] ^ j) * (y_ref.shape[2] // 4) + offset * width
        lanes = pl.ds(pl.multiple_of(start, 128), wide)
        copies.append(pltpu.make_async_copy(y_part.at[j], y_ref.at[:, :, lanes], sems.at[j]))
        copies[-1].start()
    for copy in copies:
        copy.wait()


def cast_kernel(parts, tailed, reach, lines, *refs):
    count = len(tailed)
    ins, outs = refs[:-count], refs[-count:]
    states, tails = ins[: parts * count], ins[parts * count :]
    for j, out_ref in enumerate(outs):
        start = 0
        for at in range(parts):
            state = states[parts * j + at][0]
            rows = state.shape[0] * state.shape[1]
            out_ref[start : start + rows] = state.reshape(rows, state.shape[2]).astype(jnp.bfloat16)
            start += rows
            if at == 0 and tailed[j]:
                x_tail = tails[2 * j][0].astype(jnp.float32)
                bc_tail = tails[2 * j + 1][0].astype(jnp.float32)
                pieces = []
                for k in range(reach):
                    pieces += [x_tail[k : k + 1, i * 128 : i * 128 + 128] for i in range(lines - 2)]
                    pieces.append(bc_tail[k])
                spare = tailed[j] - lines * reach
                pieces.append(jnp.zeros((spare, 128), jnp.float32))
                out_ref[start : start + tailed[j]] = jnp.concatenate(pieces).astype(jnp.bfloat16)
                start += tailed[j]


def within_kernel(
    parent_ref,
    x_ref,
    b_ref,
    c_ref,
    dt_ref,
    bias_ref,
    alog_ref,
    skip_ref,
    taps_x_ref,
    taps_bc_ref,
    tail_x_ref,
    tail_bc_ref,
    mixed_ref,
    c_out_ref,
    grow_ref,
    padded,
):
    length = x_ref.shape[1]
    heads = dt_ref.shape[1]
    width = x_ref.shape[2] // heads
    b_conv = conv_silu(padded, tail_bc_ref[0, 0], b_ref[0], taps_bc_ref[0])
    c_conv = conv_silu(padded, tail_bc_ref[0, 1], c_ref[0], taps_bc_ref[1])
    c_out_ref[0] = c_conv
    scores = lax.dot_general(
        c_conv, b_conv, (((1,), (1,)), ((), ())), preferred_element_type=jnp.float32
    )
    raw = dt_ref[0] + bias_ref[...]
    step = jnp.maximum(raw, 0.0) + jnp.log1p(jnp.exp(-jnp.abs(raw)))
    per_token = step * (-jnp.exp(alog_ref[...]))
    row = lax.broadcasted_iota(jnp.int32, (length, length), 0)
    col = lax.broadcasted_iota(jnp.int32, (length, length), 1)
    upper = (row <= col).astype(jnp.float32)
    total = lax.dot_general(
        per_token,
        upper,
        (((1,), (0,)), ((), ())),
        precision=lax.Precision.HIGHEST,
        preferred_element_type=jnp.float32,
    )
    total_t = total.T
    grow_ref[0, 0] = jnp.exp(total_t)
    causal = row >= col
    low = lax.broadcasted_iota(jnp.int32, (length, 2 * width), 1) < width
    for pair in range(heads // 2):
        lanes = slice(pair * 2 * width, (pair + 1) * 2 * width)
        x_conv = conv_silu(
            padded, tail_x_ref[0, :, lanes], x_ref[0, :, lanes], taps_x_ref[:, lanes]
        )
        parts = []
        for head in (2 * pair, 2 * pair + 1):
            gap = total_t[:, head : head + 1] - total[head : head + 1, :]
            factor = jnp.exp(jnp.where(causal, gap, -1e30))
            mixing = (scores * factor * step[head : head + 1, :]).astype(jnp.bfloat16)
            parts.append(jnp.dot(mixing, x_conv, preferred_element_type=jnp.float32))
        mixed_ref[0, :, lanes] = (
            jnp.where(low, parts[0], parts[1]) + skip_ref[:, lanes] * x_conv.astype(jnp.float32)
        )


def carried_kernel(state_ref, c_ref, grow_ref, mixed_ref, y_ref):
    sources, _, part, width, size = state_ref.shape
    length = c_ref.shape[1]
    low = lax.broadcasted_iota(jnp.int32, (length, 2 * width), 1) < width
    c_conv = c_ref[0]
    for source in range(sources):
        state = state_ref[source, 0].reshape(part * width, size)
        term = lax.dot_general(
            c_conv, state, (((1,), (1,)), ((), ())), preferred_element_type=jnp.float32
        )
        for pair in range(part // 2):
            head = source * part + 2 * pair
            grow = jnp.where(
                low, grow_ref[0, 0, :, head : head + 1], grow_ref[0, 0, :, head + 1 : head + 2]
            )
            here = slice(2 * pair * width, (2 * pair + 2) * width)
            lanes = slice(head * width, (head + 2) * width)
            carried = (term[:, here] * grow).astype(jnp.bfloat16).astype(jnp.float32)
            y_ref[0, :, lanes] = (mixed_ref[0, :, lanes] + carried).astype(jnp.bfloat16)


def pick_kernel(parent_ref, state_ref, out_ref):
    out_ref[...] = state_ref[...]


def local_any(
    x_in,
    b_in,
    c_in,
    dt_in,
    dt_bias,
    a_log,
    d_skip,
    conv_x,
    conv_bc,
    par_state,
    tail_x,
    tail_bc,
    counts,
    order,
):
    kids, length, columns = x_in.shape
    heads = dt_in.shape[1]
    width, size = par_state.shape[2:]
    ways = lax.axis_size("batch")
    groups = b_in.shape[2] // size
    per_group = heads // groups
    part = heads // ways
    wide = per_group * width
    reach = tail_x.shape[1]
    parents_all = counts.shape[0]
    kids_all = order.shape[0]

    parent = parent_of(counts, order)
    own = lax.dynamic_slice_in_dim(parent, lax.axis_index("batch") * kids, kids)

    sent = par_state.astype(jnp.bfloat16).reshape(ways, part, width, size)
    shares = lax.all_to_all(sent, "batch", split_axis=0, concat_axis=0, tiled=True)

    tails = jnp.concatenate([tail_x.reshape(-1), tail_bc.reshape(-1)])
    tails = jnp.broadcast_to(tails[None], (ways, tails.shape[0]))
    tails = lax.all_to_all(tails, "batch", split_axis=0, concat_axis=0, tiled=True)
    tails_x = tails[:, : reach * columns].reshape(parents_all, reach, columns)
    tails_bc = tails[:, reach * columns :].reshape(parents_all, 2, reach, groups * size)

    picked = pl.pallas_call(
        pick_kernel,
        grid_spec=pltpu.PrefetchScalarGridSpec(
            num_scalar_prefetch=1,
            grid=(kids_all,),
            in_specs=[pl.BlockSpec((1, part, width, size), lambda i, p: (p[i], 0, 0, 0))],
            out_specs=pl.BlockSpec((1, part, width, size), lambda i, p: (i, 0, 0, 0)),
        ),
        out_shape=jax.ShapeDtypeStruct((kids_all, part, width, size), jnp.bfloat16),
        cost_estimate=pl.CostEstimate(
            flops=0, bytes_accessed=4 * kids_all * part * width * size, transcendentals=0
        ),
        name="pick_states",
    )(parent, shares)
    states = lax.all_to_all(
        picked.reshape(ways, kids, part, width, size), "batch", split_axis=0, concat_axis=0, tiled=True
    )

    skip_row = jnp.repeat(d_skip, width)[None, :]
    mixed, c_conv, grow = pl.pallas_call(
        within_kernel,
        grid_spec=pltpu.PrefetchScalarGridSpec(
            num_scalar_prefetch=1,
            grid=(kids, groups),
            in_specs=[
                pl.BlockSpec((1, length, wide), lambda c, q, p: (c, 0, q)),
                pl.BlockSpec((1, length, size), lambda c, q, p: (c, 0, q)),
                pl.BlockSpec((1, length, size), lambda c, q, p: (c, 0, q)),
                pl.BlockSpec((1, per_group, length), lambda c, q, p: (c, q, 0)),
                pl.BlockSpec((per_group, 1), lambda c, q, p: (q, 0)),
                pl.BlockSpec((per_group, 1), lambda c, q, p: (q, 0)),
                pl.BlockSpec((1, wide), lambda c, q, p: (0, q)),
                pl.BlockSpec((reach + 1, wide), lambda c, q, p: (0, q)),
                pl.BlockSpec((2, reach + 1, size), lambda c, q, p: (0, 0, q)),
                pl.BlockSpec((1, reach, wide), lambda c, q, p: (p[c], 0, q)),
                pl.BlockSpec((1, 2, reach, size), lambda c, q, p: (p[c], 0, 0, q)),
            ],
            out_specs=[
                pl.BlockSpec((1, length, wide), lambda c, q, p: (c, 0, q)),
                pl.BlockSpec((1, length, size), lambda c, q, p: (c, 0, q)),
                pl.BlockSpec((1, 1, length, per_group), lambda c, q, p: (c, q, 0, 0)),
            ],
            scratch_shapes=[pltpu.VMEM((8 + length, size), jnp.float32)],
        ),
        out_shape=[
            jax.ShapeDtypeStruct((kids, length, columns), jnp.float32),
            jax.ShapeDtypeStruct((kids, length, groups * size), jnp.bfloat16),
            jax.ShapeDtypeStruct((kids, groups, length, per_group), jnp.float32),
        ],
        compiler_params=pltpu.CompilerParams(vmem_limit_bytes=4 * VMEM_LIMIT),
        cost_estimate=pl.CostEstimate(
            flops=4 * kids * heads * length * length * width,
            bytes_accessed=6 * kids * length * columns,
            transcendentals=kids * heads * length * length,
        ),
        name="within",
    )(
        own,
        x_in,
        b_in,
        c_in,
        dt_in,
        dt_bias[:, None],
        a_log[:, None],
        skip_row,
        conv_x,
        conv_bc,
        tails_x,
        tails_bc,
    )

    sources = per_group // part
    return pl.pallas_call(
        carried_kernel,
        grid=(kids, groups),
        in_specs=[
            pl.BlockSpec((sources, 1, part, width, size), lambda c, q: (q, c, 0, 0, 0)),
            pl.BlockSpec((1, length, size), lambda c, q: (c, 0, q)),
            pl.BlockSpec((1, 1, length, per_group), lambda c, q: (c, q, 0, 0)),
            pl.BlockSpec((1, length, wide), lambda c, q: (c, 0, q)),
        ],
        out_specs=pl.BlockSpec((1, length, wide), lambda c, q: (c, 0, q)),
        out_shape=jax.ShapeDtypeStruct((kids, length, columns), jnp.bfloat16),
        compiler_params=pltpu.CompilerParams(vmem_limit_bytes=4 * VMEM_LIMIT),
        cost_estimate=pl.CostEstimate(
            flops=2 * kids * length * columns * size,
            bytes_accessed=8 * kids * length * columns,
            transcendentals=0,
        ),
        name="carried",
    )(states, c_conv, grow, mixed)


def local_halves(
    x_in, b_in, c_in, dt_in, dt_bias, a_log, d_skip, conv_x, conv_bc,
    par_state, tail_x, tail_bc, counts, order,
):
    kids, length, columns = x_in.shape
    heads = dt_in.shape[1]
    width, size = par_state.shape[2:]
    groups = b_in.shape[2] // size
    per_group = heads // groups
    wide = per_group * width
    taps = conv_x.shape[0]
    reach = taps - 1
    lines = (wide + 2 * size) // 128
    tail_lines = -(-lines * reach // 16) * 16
    params = pltpu.CompilerParams(vmem_limit_bytes=VMEM_LIMIT)
    anywhere = pl.BlockSpec(memory_space=pl.ANY)
    small = pl.CostEstimate(flops=1, bytes_accessed=1, transcendentals=0)

    stay = lambda x: pltpu.with_memory_space_constraint(x, pltpu.HBM)
    keep_in_vmem = lambda x: pltpu.with_memory_space_constraint(x, pltpu.VMEM)
    x_in, b_in, c_in, dt_in, conv_x, conv_bc = map(stay, (x_in, b_in, c_in, dt_in, conv_x, conv_bc))

    me = lax.axis_index("batch")
    parent = parent_of(counts, order)
    child = (jnp.arange(4 * kids, dtype=jnp.int32) // kids ^ me) * kids
    child = child + jnp.arange(4 * kids, dtype=jnp.int32) % kids
    catalog = jnp.arange(4 * 2 * kids, dtype=jnp.int32)
    owner = jnp.sum(jnp.where(child[:, None] == catalog[None, :], parent[None, :], 0), axis=1)
    slots = owner ^ me
    place = (me % 4).astype(jnp.int32)[None]

    state = stay(par_state.reshape(groups, per_group, width, size))
    x_tails, bc_tails = stay(tail_x), stay(tail_bc.transpose(0, 2, 1, 3))
    offsets = [sum(SPLIT[:k]) for k in range(len(SPLIT))]

    def swap(value, r):
        return lax.ppermute(value, "batch", perm=[(i, i ^ r) for i in range(8)])

    def cast():
        rows = per_group * width + tail_lines
        rows_a = SPLIT[0] * width + tail_lines
        blocks = [(0, SPLIT[0])] + [(at, 4) for at in range(SPLIT[0], per_group, 4)]
        count = len(blocks) + 2

        def kernel(place_ref, *refs):
            ins, outs = refs[: 4 * count], refs[4 * count :]
            quarters = [outs[0], outs[2].at[0], outs[1], outs[2].at[1]]
            for n, out_ref in enumerate(quarters):
                cast_kernel(
                    len(blocks), [tail_lines], reach, lines, *ins[count * n : count * n + count], out_ref
                )
                outs[3 + n // 2][n % 2] = out_ref[:rows_a]

        operands, specs = [], []
        for n in range(4):
            for offset, part in blocks:
                operands.append(state)
                specs.append(
                    pl.BlockSpec(
                        (1, part, width, size),
                        lambda i, p, n=n, at=offset // part: (p[0] ^ n, at, 0, 0),
                    )
                )
            operands += [x_tails, bc_tails]
            specs += [
                pl.BlockSpec((1, reach, wide), lambda i, p, n=n: (0, 0, p[0] ^ n)),
                pl.BlockSpec((1, reach, 2, size), lambda i, p, n=n: (0, 0, 0, p[0] ^ n)),
            ]
        shapes = [(rows, size)] * 2 + [(2, rows, size)] + [(2, rows_a, size)] * 2
        return pl.pallas_call(
            kernel,
            grid_spec=pltpu.PrefetchScalarGridSpec(
                num_scalar_prefetch=1,
                grid=(1,),
                in_specs=specs,
                out_specs=[pl.BlockSpec(memory_space=pltpu.VMEM)] * len(shapes),
            ),
            out_shape=[pltpu.VMEM(shape, jnp.bfloat16) for shape in shapes],
            compiler_params=params,
            cost_estimate=small,
            name="cast_states",
        )(place, *operands)

    def rearrange(scalars, sources, moves, shapes, tokens, name):
        def kernel(scalars_ref, *refs):
            held, outs = refs[: len(sources)], refs[len(sources) :]
            for out, at, scalar, choices in moves:
                for value, (number, take) in enumerate(choices):

                    def copy(out=out, at=at, number=number, take=take):
                        rows = held[number][...] if take is None else held[number][take]
                        if at is None:
                            outs[out][...] = rows
                        else:
                            outs[out][at] = rows

                    if scalar is None:
                        copy()
                    else:
                        pl.when(scalars_ref[scalar] == value)(copy)

        return pl.pallas_call(
            functools.partial(drop_tokens, kernel, 1 + len(sources), len(tokens)),
            grid_spec=pltpu.PrefetchScalarGridSpec(
                num_scalar_prefetch=1,
                grid=(1,),
                in_specs=[pl.BlockSpec(memory_space=pltpu.VMEM)] * len(sources)
                + [anywhere] * len(tokens),
                out_specs=[pl.BlockSpec(memory_space=pltpu.VMEM)] * len(shapes),
            ),
            out_shape=[pltpu.VMEM(shape, jnp.bfloat16) for shape in shapes],
            compiler_params=params,
            cost_estimate=small,
            name=name,
        )(scalars, *map(keep_in_vmem, sources), *tokens)

    def pick(rows, sources, choices, tokens):
        moves = [
            (j, kid, j * kids + kid, choices) for j in range(4) for kid in range(kids)
        ]
        picked = rearrange(
            slots, sources, moves, [(kids, rows, size)] * 4, tokens, "pick_states"
        )
        return [picked[0]] + [swap(picked[j], j) for j in range(1, 4)]

    def early(c, pieces, piece, before, tokens):
        per = groups // pieces
        at = lambda q: (c, 0, per * piece + q)
        operands = [
            x_in, b_in, c_in, dt_in, dt_bias[:, None], a_log[:, None], skip_row, conv_x, conv_bc
        ]
        keep = len(operands)
        tokens = list(tokens) + [keep_in_vmem(a) for a in before]
        first = keep + len(tokens) - len(before)
        return pl.pallas_call(
            functools.partial(
                drop_tokens, functools.partial(early_kernel, per * piece), keep, len(tokens)
            ),
            grid=(per,),
            in_specs=[
                pl.BlockSpec((1, length, wide), at),
                pl.BlockSpec((1, length, size), at),
                pl.BlockSpec((1, length, size), at),
                pl.BlockSpec((1, per_group, length), lambda q: (c, per * piece + q, 0)),
                pl.BlockSpec((per_group, 1), lambda q: (per * piece + q, 0)),
                pl.BlockSpec((per_group, 1), lambda q: (per * piece + q, 0)),
                pl.BlockSpec((1, wide), lambda q: (0, per * piece + q)),
                pl.BlockSpec((taps, wide), lambda q: (0, per * piece + q)),
                pl.BlockSpec((2, taps, size), lambda q: (0, 0, per * piece + q)),
                *[anywhere] * len(tokens),
            ],
            out_specs=[pl.BlockSpec(memory_space=pltpu.VMEM)] * 6,
            out_shape=[
                pltpu.VMEM((groups, length, wide), jnp.float32),
                pltpu.VMEM((groups, length, size), jnp.bfloat16),
                pltpu.VMEM((groups, per_group, length), jnp.float32),
                pltpu.VMEM((groups, length, per_group * FIX), jnp.float32),
                pltpu.VMEM((groups, FIX, wide + 2 * size), jnp.bfloat16),
                pltpu.VMEM((groups, 8, wide + 2 * size), jnp.float32),
            ],
            input_output_aliases={first + i: i for i in range(len(before))},
            scratch_shapes=[pltpu.VMEM((2, 8 + length, size), jnp.float32)],
            compiler_params=params,
            cost_estimate=small,
            name="early",
        )(*operands, *tokens)

    def late(ks, states, parts, result, tokens):
        offset = offsets[ks[0]]
        chunk = sum(SPLIT[k] for k in ks) * width
        operands = [keep_in_vmem(a) for a in (*states[0], *sum((states[k] for k in ks), []), *parts[0], *parts[1])]
        specs = [pl.BlockSpec(memory_space=pltpu.VMEM)] * len(operands)
        keep = 1 + len(operands)
        operands += tokens
        specs += [anywhere] * len(tokens)
        alias = {}
        if result is not None:
            alias = {1 + len(operands): 0}
            operands.append(result)
            specs.append(anywhere)
        kernel = functools.partial(
            late_kernel, offset, [SPLIT[k] for k in ks], lines, reach, SPLIT[0] * width
        )
        return pl.pallas_call(
            functools.partial(drop_tokens, kernel, keep, 1 + len(operands) - keep),
            grid_spec=pltpu.PrefetchScalarGridSpec(
                num_scalar_prefetch=1,
                grid=(1,),
                in_specs=specs,
                out_specs=anywhere,
                scratch_shapes=[
                    pltpu.VMEM((groups, kids, 8 + FIX, max(chunk, 2 * size)), jnp.float32),
                    pltpu.VMEM((groups, kids, length, chunk), jnp.bfloat16),
                    pltpu.SemaphoreType.DMA((groups,)),
                ],
            ),
            out_shape=jax.ShapeDtypeStruct(x_in.shape, jnp.bfloat16),
            input_output_aliases=alias,
            compiler_params=params,
            cost_estimate=small,
            name="late",
        )(place, *operands)

    skip_row = jnp.repeat(d_skip, width)[None, :]
    rows = [SPLIT[0] * width + tail_lines] + [part * width for part in SPLIT[1:]]
    chunks = [pl.ds(sum(rows[:k]), rows[k]) for k in range(len(SPLIT))]
    own, own_2, own_13, sent_4, sent_6 = cast()
    crossed_a = [swap(sent_4, 4), swap(sent_6, 6)]
    along_y, along_z = swap(own_13, 1), swap(own_2, 2)
    first = early(0, 2, 0, [], [own, slots])
    (turn,) = rearrange(
        place, [along_y], [(0, None, None, [(0, 1)])], [own.shape], [first[1]], "stack_turn"
    )
    inside = [own, along_y, along_z, swap(turn, 2)]

    def inside_rows(k):
        return [(0, chunks[k]), (1, (0, chunks[k])), (2, chunks[k]), (3, chunks[k])]

    def cross(k, tokens):
        moves = [(0, j, None, [choice]) for j, choice in enumerate(inside_rows(k))]
        (sent,) = rearrange(place, inside, moves, [(4, rows[k], size)], tokens, "stack_later")
        return sent, swap(sent, 4)

    def pick_later(k, crossed, tokens):
        choices = inside_rows(k) + [(4, j) for j in range(4)]
        return pick(rows[k], [*inside, crossed], choices, tokens)

    first = early(0, 2, 1, first, [turn])
    sent_b, crossed_b = cross(1, [first[1]])
    second = early(1, 2, 0, [], [sent_b])
    moves = [(0, n, None, [(n, 1)]) for n in range(2)]
    (spread,) = rearrange(
        place, crossed_a, moves, [(2, rows[0], size)], [second[1]], "stack_first"
    )
    passed = swap(spread, 1)
    sent_c, crossed_c = cross(2, [spread])
    second = early(1, 2, 1, second, [sent_c])
    choices = inside_rows(0) + [(4, 0), (6, 0), (5, 0), (6, 1)]
    states = [pick(rows[0], [*inside, *crossed_a, passed], choices, [second[1]])]
    states.append(pick_later(1, crossed_b, [states[0][0]]))
    states.append(pick_later(2, crossed_c, [states[1][0], *states[0]]))
    parts = [first, second]
    result = late([0, 1], states, parts, None, [states[2][0]])
    return late([2], states, parts, result, [])


def solution(mesh):
    rows, cols = P(("groups", "batch"), None, "head"), P(("groups", "batch"), "head")
    placed = (
        rows, rows, rows, cols, P("head"), P("head"), P("head"), P(None, "head"),
        P(None, None, "head"), cols, rows, P(("groups", "batch"), None, None, "head"),
        P("groups"), P("groups"),
    )
    local = local_halves if mesh.shape["batch"] == 8 else local_any
    return jax.shard_map(local, mesh=mesh, in_specs=placed, out_specs=rows, check_vma=False)
```

```python
import functools

import jax
import jax.numpy as jnp
from jax import lax
from jax.experimental import pallas as pl
from jax.experimental.pallas import tpu as pltpu
from jax.sharding import PartitionSpec as P

VMEM_LIMIT = 12 * 1024 * 1024
SPLIT = (8, 6, 2)
FIX = 16
LOG2_E = 1.4426950408889634


def drop_tokens(kernel, keep, tokens, *refs):
    kernel(*refs[:keep], *refs[keep + tokens :])


def parent_of(counts, order):
    index = jnp.arange(counts.shape[0], dtype=jnp.int32)
    bounds = jnp.sum(jnp.where(index[None, :] <= index[:, None], counts[None, :], 0), axis=1)
    return jnp.sum((bounds[None, :] <= order[:, None]).astype(jnp.int32), axis=1)


def three_terms(value):
    terms = []
    for _ in range(3):
        terms.append(value.astype(jnp.bfloat16).astype(jnp.float32))
        value = value - terms[-1]
    return jnp.concatenate(terms)


def conv_silu(padded, tail, rows, taps):
    length = rows.shape[0]
    reach = taps.shape[0] - 1
    padded[8 - reach : 8, :] = jnp.broadcast_to(tail, (reach, rows.shape[1])).astype(jnp.float32)
    padded[8 : 8 + length, :] = rows.astype(jnp.float32)
    total = padded[8 - reach : 8 - reach + length, :] * taps[0:1, :]
    for k in range(1, reach + 1):
        total = total + padded[8 - reach + k : 8 - reach + k + length, :] * taps[k : k + 1, :]
    half = 0.5 * total
    return (half + half * jnp.tanh(half)).astype(jnp.bfloat16)


def early_kernel(
    base, x_ref, b_ref, c_ref, dt_ref, bias_ref, alog_ref, skip_ref, taps_x_ref, taps_bc_ref,
    mixed_ref, c_out_ref, column_ref, first_ref, opening_ref, weights_ref, padded,
):
    length, wide = x_ref.shape[1:]
    heads = dt_ref.shape[1]
    q = base + pl.program_id(0)
    width = wide // heads
    half = length // 2

    def convolve(rows, taps, slot):
        bulk = conv_silu(padded.at[slot % 2], 0.0, rows, taps)[FIX:]
        return jnp.concatenate([jnp.zeros((FIX, rows.shape[1]), jnp.bfloat16), bulk])

    b_conv = convolve(b_ref[0], taps_bc_ref[0], 0)
    c_conv = convolve(c_ref[0], taps_bc_ref[1], 1)
    c_out_ref[q] = c_conv
    size = b_ref.shape[2]
    taps = taps_x_ref.shape[0]
    opening_ref[q, :, :wide] = x_ref[0, :FIX]
    opening_ref[q, :, wide : wide + size] = b_ref[0, :FIX]
    opening_ref[q, :, wide + size :] = c_ref[0, :FIX]
    weights_ref[q, :taps, :wide] = taps_x_ref[...]
    weights_ref[q, :taps, wide : wide + size] = taps_bc_ref[0]
    weights_ref[q, :taps, wide + size :] = taps_bc_ref[1]
    weights_ref[q, taps : taps + 1, :wide] = skip_ref[...]
    scores = lax.dot_general(
        c_conv, b_conv, (((1,), (1,)), ((), ())), preferred_element_type=jnp.float32
    )
    raw = dt_ref[0] + bias_ref[...]
    step = jnp.maximum(raw, 0.0) + jnp.log1p(jnp.exp(-jnp.abs(raw)))
    per_token = step * (-jnp.exp(alog_ref[...]))
    upper = lax.broadcasted_iota(jnp.int32, (length, length), 0) <= lax.broadcasted_iota(
        jnp.int32, (length, length), 1
    )
    sums = jnp.dot(
        three_terms(per_token).astype(jnp.bfloat16),
        upper.astype(jnp.float32).astype(jnp.bfloat16),
        preferred_element_type=jnp.float32,
    )
    total = (sums[:heads] + sums[heads : 2 * heads]) + sums[2 * heads :]
    total = total * LOG2_E
    row = total - jnp.log(step) * LOG2_E
    columns = total.T
    column_ref[q] = total
    causal = lax.broadcasted_iota(jnp.int32, (half, half), 0) >= lax.broadcasted_iota(
        jnp.int32, (half, half), 1
    )
    low = lax.broadcasted_iota(jnp.int32, (length, 2 * width), 1) < width
    for pair in range(heads // 2):
        lanes = slice(pair * 2 * width, (pair + 1) * 2 * width)
        x_conv = convolve(x_ref[0, :, lanes], taps_x_ref[:, lanes], pair)
        parts = []
        for head in (2 * pair, 2 * pair + 1):
            column = jnp.broadcast_to(columns[:, head : head + 1], (length, half))
            rows = row[head : head + 1, :]
            near = jnp.exp2(jnp.where(causal, column[:half] - rows[:, :half], -1e30))
            far = jnp.exp2(column[half:] - rows[:, :half])
            last = jnp.exp2(jnp.where(causal, column[half:] - rows[:, half:], -1e30))
            spot = slice(head * FIX, (head + 1) * FIX)
            first_ref[q, :half, spot] = near[:, :FIX]
            first_ref[q, half:, spot] = far[:, :FIX]
            top = (scores[:half, :half] * near).astype(jnp.bfloat16)
            left = (scores[half:, :half] * far).astype(jnp.bfloat16)
            right = (scores[half:, half:] * last).astype(jnp.bfloat16)
            below = jnp.concatenate([left, right], axis=1)
            parts.append(
                jnp.concatenate(
                    [
                        jnp.dot(top, x_conv[:half], preferred_element_type=jnp.float32),
                        jnp.dot(below, x_conv, preferred_element_type=jnp.float32),
                    ]
                )
            )
        mixed_ref[q, :, lanes] = jnp.where(low, parts[0], parts[1]) + skip_ref[
            :, lanes
        ] * x_conv.astype(jnp.float32)


def late_kernel(offset, heads, lines, reach, tail_at, place_ref, *refs):
    count = len(heads)
    tails, states, parts = refs[:4], refs[4 : 4 + 4 * count], refs[4 + 4 * count : -4]
    y_ref, padded, y_part, sems = refs[-4:]
    _, kids, length, wide = y_part.shape
    rows, heads = heads, sum(heads)
    width = wide // heads
    rows = [part * width for part in rows]
    low_first = lax.broadcasted_iota(jnp.int32, (FIX, 2 * width), 1) < width
    contract = (((1,), (1,)), ((), ()))

    def add(j, kid):
        q = place_ref[0] ^ j
        mixed_ref, held_ref, column_ref, first_ref, opening_ref, weights_ref = parts[
            6 * kid : 6 * kid + 6
        ]
        size = held_ref.shape[2]
        per_group = column_ref.shape[1]
        group_wide = opening_ref.shape[2] - 2 * size
        tail_rows = pl.ds(tail_at, -(-lines * reach // 16) * 16)
        tail = tails[j][kid, tail_rows].astype(jnp.float32)
        state = jnp.concatenate([states[4 * n + j][kid, : rows[n]] for n in range(count)])

        def opening(start, stop, at):
            tap_rows = []
            for k in range(reach):
                first = k * lines + at
                count = (stop - start) // 128
                here = [tail[first + n : first + n + 1] for n in range(count)]
                tap_rows.append(jnp.concatenate(here, axis=1))
            return conv_silu(
                padded.at[j, kid, :, : stop - start],
                jnp.concatenate(tap_rows),
                opening_ref[q, :, start:stop],
                weights_ref[q, : reach + 1, start:stop],
            )

        bc_first = opening(group_wide, group_wide + 2 * size, lines - 2)
        b_first, c_first = bc_first[:, :size], bc_first[:, size:]
        start = offset * width
        x_all = opening(start, start + wide, start // 128).astype(jnp.float32)
        skipped = weights_ref[q, reach + 1 : reach + 2, start : start + wide] * x_all
        c_conv = jnp.concatenate([c_first, held_ref[q, FIX:]])
        terms = three_terms(jnp.exp2(column_ref[q]))
        terms = jnp.concatenate([terms, jnp.zeros((per_group, length), jnp.float32)])
        spread_row = lax.broadcasted_iota(jnp.int32, (4 * per_group, wide), 0)
        spread_lane = lax.broadcasted_iota(jnp.int32, (4 * per_group, wide), 1)
        spread = spread_row % per_group == offset + spread_lane // width
        grow = jnp.dot(
            terms.T.astype(jnp.bfloat16),
            spread.astype(jnp.float32).astype(jnp.bfloat16),
            preferred_element_type=jnp.float32,
        )
        term = lax.dot_general(c_conv, state, contract, preferred_element_type=jnp.float32)
        carried = (term * grow).astype(jnp.bfloat16)
        scores = lax.dot_general(
            c_conv,
            jnp.concatenate([b_first] * heads),
            contract,
            preferred_element_type=jnp.float32,
        )
        here = slice(offset * FIX, (offset + heads) * FIX)
        mixing = (scores * first_ref[q, :, here]).astype(jnp.bfloat16)
        for pair in range(heads // 2):
            lanes = slice(pair * 2 * width, (pair + 1) * 2 * width)
            x_first = x_all[:, lanes]
            stacked = [jnp.where(low_first, x_first, 0.0), jnp.where(low_first, 0.0, x_first)]
            if pair > 0:
                stacked = [jnp.zeros((2 * pair * FIX, 2 * width), jnp.float32)] + stacked
            if 2 * pair + 2 < heads:
                spare = (heads - 2 * pair - 2) * FIX
                stacked = stacked + [jnp.zeros((spare, 2 * width), jnp.float32)]
            part = jnp.dot(
                mixing,
                jnp.concatenate(stacked).astype(jnp.bfloat16),
                preferred_element_type=jnp.float32,
            )
            part = jnp.concatenate([part[:FIX] + skipped[:, lanes], part[FIX:]])
            whole = slice(start + lanes.start, start + lanes.stop)
            y_part[j, kid, :, lanes] = (
                mixed_ref[q, :, whole] + part + carried[:, lanes].astype(jnp.float32)
            ).astype(jnp.bfloat16)

    copies = []
    for j in range(4):
        for kid in range(kids):
            add(j, kid)
        start = (place_ref[0] ^ j) * (y_ref.shape[2] // 4) + offset * width
        lanes = pl.ds(pl.multiple_of(start, 128), wide)
        copies.append(pltpu.make_async_copy(y_part.at[j], y_ref.at[:, :, lanes], sems.at[j]))
        copies[-1].start()
    for copy in copies:
        copy.wait()


def cast_kernel(parts, tailed, reach, lines, *refs):
    count = len(tailed)
    ins, outs = refs[:-count], refs[-count:]
    states, tails = ins[: parts * count], ins[parts * count :]
    for j, out_ref in enumerate(outs):
        start = 0
        for at in range(parts):
            state = states[parts * j + at][0]
            rows = state.shape[0] * state.shape[1]
            out_ref[start : start + rows] = state.reshape(rows, state.shape[2]).astype(jnp.bfloat16)
            start += rows
            if at == 0 and tailed[j]:
                x_tail = tails[2 * j][0].astype(jnp.float32)
                bc_tail = tails[2 * j + 1][0].astype(jnp.float32)
                pieces = []
                for k in range(reach):
                    pieces += [x_tail[k : k + 1, i * 128 : i * 128 + 128] for i in range(lines - 2)]
                    pieces.append(bc_tail[k])
                spare = tailed[j] - lines * reach
                pieces.append(jnp.zeros((spare, 128), jnp.float32))
                out_ref[start : start + tailed[j]] = jnp.concatenate(pieces).astype(jnp.bfloat16)
                start += tailed[j]


def within_kernel(
    parent_ref,
    x_ref,
    b_ref,
    c_ref,
    dt_ref,
    bias_ref,
    alog_ref,
    skip_ref,
    taps_x_ref,
    taps_bc_ref,
    tail_x_ref,
    tail_bc_ref,
    mixed_ref,
    c_out_ref,
    grow_ref,
    padded,
):
    length = x_ref.shape[1]
    heads = dt_ref.shape[1]
    width = x_ref.shape[2] // heads
    b_conv = conv_silu(padded, tail_bc_ref[0, 0], b_ref[0], taps_bc_ref[0])
    c_conv = conv_silu(padded, tail_bc_ref[0, 1], c_ref[0], taps_bc_ref[1])
    c_out_ref[0] = c_conv
    scores = lax.dot_general(
        c_conv, b_conv, (((1,), (1,)), ((), ())), preferred_element_type=jnp.float32
    )
    raw = dt_ref[0] + bias_ref[...]
    step = jnp.maximum(raw, 0.0) + jnp.log1p(jnp.exp(-jnp.abs(raw)))
    per_token = step * (-jnp.exp(alog_ref[...]))
    row = lax.broadcasted_iota(jnp.int32, (length, length), 0)
    col = lax.broadcasted_iota(jnp.int32, (length, length), 1)
    upper = (row <= col).astype(jnp.float32)
    total = lax.dot_general(
        per_token,
        upper,
        (((1,), (0,)), ((), ())),
        precision=lax.Precision.HIGHEST,
        preferred_element_type=jnp.float32,
    )
    total_t = total.T
    grow_ref[0, 0] = jnp.exp(total_t)
    causal = row >= col
    low = lax.broadcasted_iota(jnp.int32, (length, 2 * width), 1) < width
    for pair in range(heads // 2):
        lanes = slice(pair * 2 * width, (pair + 1) * 2 * width)
        x_conv = conv_silu(
            padded, tail_x_ref[0, :, lanes], x_ref[0, :, lanes], taps_x_ref[:, lanes]
        )
        parts = []
        for head in (2 * pair, 2 * pair + 1):
            gap = total_t[:, head : head + 1] - total[head : head + 1, :]
            factor = jnp.exp(jnp.where(causal, gap, -1e30))
            mixing = (scores * factor * step[head : head + 1, :]).astype(jnp.bfloat16)
            parts.append(jnp.dot(mixing, x_conv, preferred_element_type=jnp.float32))
        mixed_ref[0, :, lanes] = (
            jnp.where(low, parts[0], parts[1]) + skip_ref[:, lanes] * x_conv.astype(jnp.float32)
        )


def carried_kernel(state_ref, c_ref, grow_ref, mixed_ref, y_ref):
    sources, _, part, width, size = state_ref.shape
    length = c_ref.shape[1]
    low = lax.broadcasted_iota(jnp.int32, (length, 2 * width), 1) < width
    c_conv = c_ref[0]
    for source in range(sources):
        state = state_ref[source, 0].reshape(part * width, size)
        term = lax.dot_general(
            c_conv, state, (((1,), (1,)), ((), ())), preferred_element_type=jnp.float32
        )
        for pair in range(part // 2):
            head = source * part + 2 * pair
            grow = jnp.where(
                low, grow_ref[0, 0, :, head : head + 1], grow_ref[0, 0, :, head + 1 : head + 2]
            )
            here = slice(2 * pair * width, (2 * pair + 2) * width)
            lanes = slice(head * width, (head + 2) * width)
            carried = (term[:, here] * grow).astype(jnp.bfloat16).astype(jnp.float32)
            y_ref[0, :, lanes] = (mixed_ref[0, :, lanes] + carried).astype(jnp.bfloat16)


def pick_kernel(parent_ref, state_ref, out_ref):
    out_ref[...] = state_ref[...]


def local_any(
    x_in,
    b_in,
    c_in,
    dt_in,
    dt_bias,
    a_log,
    d_skip,
    conv_x,
    conv_bc,
    par_state,
    tail_x,
    tail_bc,
    counts,
    order,
):
    kids, length, columns = x_in.shape
    heads = dt_in.shape[1]
    width, size = par_state.shape[2:]
    ways = lax.axis_size("batch")
    groups = b_in.shape[2] // size
    per_group = heads // groups
    part = heads // ways
    wide = per_group * width
    reach = tail_x.shape[1]
    parents_all = counts.shape[0]
    kids_all = order.shape[0]

    parent = parent_of(counts, order)
    own = lax.dynamic_slice_in_dim(parent, lax.axis_index("batch") * kids, kids)

    sent = par_state.astype(jnp.bfloat16).reshape(ways, part, width, size)
    shares = lax.all_to_all(sent, "batch", split_axis=0, concat_axis=0, tiled=True)

    tails = jnp.concatenate([tail_x.reshape(-1), tail_bc.reshape(-1)])
    tails = jnp.broadcast_to(tails[None], (ways, tails.shape[0]))
    tails = lax.all_to_all(tails, "batch", split_axis=0, concat_axis=0, tiled=True)
    tails_x = tails[:, : reach * columns].reshape(parents_all, reach, columns)
    tails_bc = tails[:, reach * columns :].reshape(parents_all, 2, reach, groups * size)

    picked = pl.pallas_call(
        pick_kernel,
        grid_spec=pltpu.PrefetchScalarGridSpec(
            num_scalar_prefetch=1,
            grid=(kids_all,),
            in_specs=[pl.BlockSpec((1, part, width, size), lambda i, p: (p[i], 0, 0, 0))],
            out_specs=pl.BlockSpec((1, part, width, size), lambda i, p: (i, 0, 0, 0)),
        ),
        out_shape=jax.ShapeDtypeStruct((kids_all, part, width, size), jnp.bfloat16),
        cost_estimate=pl.CostEstimate(
            flops=0, bytes_accessed=4 * kids_all * part * width * size, transcendentals=0
        ),
        name="pick_states",
    )(parent, shares)
    states = lax.all_to_all(
        picked.reshape(ways, kids, part, width, size), "batch", split_axis=0, concat_axis=0, tiled=True
    )

    skip_row = jnp.repeat(d_skip, width)[None, :]
    mixed, c_conv, grow = pl.pallas_call(
        within_kernel,
        grid_spec=pltpu.PrefetchScalarGridSpec(
            num_scalar_prefetch=1,
            grid=(kids, groups),
            in_specs=[
                pl.BlockSpec((1, length, wide), lambda c, q, p: (c, 0, q)),
                pl.BlockSpec((1, length, size), lambda c, q, p: (c, 0, q)),
                pl.BlockSpec((1, length, size), lambda c, q, p: (c, 0, q)),
                pl.BlockSpec((1, per_group, length), lambda c, q, p: (c, q, 0)),
                pl.BlockSpec((per_group, 1), lambda c, q, p: (q, 0)),
                pl.BlockSpec((per_group, 1), lambda c, q, p: (q, 0)),
                pl.BlockSpec((1, wide), lambda c, q, p: (0, q)),
                pl.BlockSpec((reach + 1, wide), lambda c, q, p: (0, q)),
                pl.BlockSpec((2, reach + 1, size), lambda c, q, p: (0, 0, q)),
                pl.BlockSpec((1, reach, wide), lambda c, q, p: (p[c], 0, q)),
                pl.BlockSpec((1, 2, reach, size), lambda c, q, p: (p[c], 0, 0, q)),
            ],
            out_specs=[
                pl.BlockSpec((1, length, wide), lambda c, q, p: (c, 0, q)),
                pl.BlockSpec((1, length, size), lambda c, q, p: (c, 0, q)),
                pl.BlockSpec((1, 1, length, per_group), lambda c, q, p: (c, q, 0, 0)),
            ],
            scratch_shapes=[pltpu.VMEM((8 + length, size), jnp.float32)],
        ),
        out_shape=[
            jax.ShapeDtypeStruct((kids, length, columns), jnp.float32),
            jax.ShapeDtypeStruct((kids, length, groups * size), jnp.bfloat16),
            jax.ShapeDtypeStruct((kids, groups, length, per_group), jnp.float32),
        ],
        compiler_params=pltpu.CompilerParams(vmem_limit_bytes=4 * VMEM_LIMIT),
        cost_estimate=pl.CostEstimate(
            flops=4 * kids * heads * length * length * width,
            bytes_accessed=6 * kids * length * columns,
            transcendentals=kids * heads * length * length,
        ),
        name="within",
    )(
        own,
        x_in,
        b_in,
        c_in,
        dt_in,
        dt_bias[:, None],
        a_log[:, None],
        skip_row,
        conv_x,
        conv_bc,
        tails_x,
        tails_bc,
    )

    sources = per_group // part
    return pl.pallas_call(
        carried_kernel,
        grid=(kids, groups),
        in_specs=[
            pl.BlockSpec((sources, 1, part, width, size), lambda c, q: (q, c, 0, 0, 0)),
            pl.BlockSpec((1, length, size), lambda c, q: (c, 0, q)),
            pl.BlockSpec((1, 1, length, per_group), lambda c, q: (c, q, 0, 0)),
            pl.BlockSpec((1, length, wide), lambda c, q: (c, 0, q)),
        ],
        out_specs=pl.BlockSpec((1, length, wide), lambda c, q: (c, 0, q)),
        out_shape=jax.ShapeDtypeStruct((kids, length, columns), jnp.bfloat16),
        compiler_params=pltpu.CompilerParams(vmem_limit_bytes=4 * VMEM_LIMIT),
        cost_estimate=pl.CostEstimate(
            flops=2 * kids * length * columns * size,
            bytes_accessed=8 * kids * length * columns,
            transcendentals=0,
        ),
        name="carried",
    )(states, c_conv, grow, mixed)


def local_halves(
    x_in, b_in, c_in, dt_in, dt_bias, a_log, d_skip, conv_x, conv_bc,
    par_state, tail_x, tail_bc, counts, order,
):
    kids, length, columns = x_in.shape
    heads = dt_in.shape[1]
    width, size = par_state.shape[2:]
    groups = b_in.shape[2] // size
    per_group = heads // groups
    wide = per_group * width
    taps = conv_x.shape[0]
    reach = taps - 1
    lines = (wide + 2 * size) // 128
    tail_lines = -(-lines * reach // 16) * 16
    params = pltpu.CompilerParams(vmem_limit_bytes=VMEM_LIMIT)
    anywhere = pl.BlockSpec(memory_space=pl.ANY)
    small = pl.CostEstimate(flops=1, bytes_accessed=1, transcendentals=0)

    stay = lambda x: pltpu.with_memory_space_constraint(x, pltpu.HBM)
    keep_in_vmem = lambda x: pltpu.with_memory_space_constraint(x, pltpu.VMEM)
    x_in, b_in, c_in, dt_in, conv_x, conv_bc = map(stay, (x_in, b_in, c_in, dt_in, conv_x, conv_bc))

    me = lax.axis_index("batch")
    parent = parent_of(counts, order)
    child = (jnp.arange(4 * kids, dtype=jnp.int32) // kids ^ me) * kids
    child = child + jnp.arange(4 * kids, dtype=jnp.int32) % kids
    catalog = jnp.arange(4 * 2 * kids, dtype=jnp.int32)
    owner = jnp.sum(jnp.where(child[:, None] == catalog[None, :], parent[None, :], 0), axis=1)
    slots = owner ^ me
    place = (me % 4).astype(jnp.int32)[None]

    state = stay(par_state.reshape(groups, per_group, width, size))
    x_tails, bc_tails = stay(tail_x), stay(tail_bc.transpose(0, 2, 1, 3))
    offsets = [sum(SPLIT[:k]) for k in range(len(SPLIT))]

    def swap(value, r):
        return lax.ppermute(value, "batch", perm=[(i, i ^ r) for i in range(8)])

    def cast():
        rows = per_group * width + tail_lines
        rows_a = SPLIT[0] * width + tail_lines
        blocks = [(0, SPLIT[0])] + [(at, 2) for at in range(SPLIT[0], per_group, 2)]
        count = len(blocks) + 2

        def kernel(place_ref, *refs):
            ins, outs = refs[: 4 * count], refs[4 * count :]
            quarters = [outs[0], outs[2].at[0], outs[1], outs[2].at[1]]
            for n, out_ref in enumerate(quarters):
                cast_kernel(
                    len(blocks), [tail_lines], reach, lines, *ins[count * n : count * n + count], out_ref
                )
                outs[3 + n // 2][n % 2] = out_ref[:rows_a]

        operands, specs = [], []
        for n in range(4):
            for offset, part in blocks:
                operands.append(state)
                specs.append(
                    pl.BlockSpec(
                        (1, part, width, size),
                        lambda i, p, n=n, at=offset // part: (p[0] ^ n, at, 0, 0),
                    )
                )
            operands += [x_tails, bc_tails]
            specs += [
                pl.BlockSpec((1, reach, wide), lambda i, p, n=n: (0, 0, p[0] ^ n)),
                pl.BlockSpec((1, reach, 2, size), lambda i, p, n=n: (0, 0, 0, p[0] ^ n)),
            ]
        shapes = [(rows, size)] * 2 + [(2, rows, size)] + [(2, rows_a, size)] * 2
        return pl.pallas_call(
            kernel,
            grid_spec=pltpu.PrefetchScalarGridSpec(
                num_scalar_prefetch=1,
                grid=(1,),
                in_specs=specs,
                out_specs=[pl.BlockSpec(memory_space=pltpu.VMEM)] * len(shapes),
            ),
            out_shape=[pltpu.VMEM(shape, jnp.bfloat16) for shape in shapes],
            compiler_params=params,
            cost_estimate=small,
            name="cast_states",
        )(place, *operands)

    def rearrange(scalars, sources, moves, shapes, tokens, name):
        def kernel(scalars_ref, *refs):
            held, outs = refs[: len(sources)], refs[len(sources) :]
            for out, at, scalar, choices in moves:
                for value, (number, take) in enumerate(choices):

                    def copy(out=out, at=at, number=number, take=take):
                        rows = held[number][...] if take is None else held[number][take]
                        if at is None:
                            outs[out][...] = rows
                        else:
                            outs[out][at] = rows

                    if scalar is None:
                        copy()
                    else:
                        pl.when(scalars_ref[scalar] == value)(copy)

        return pl.pallas_call(
            functools.partial(drop_tokens, kernel, 1 + len(sources), len(tokens)),
            grid_spec=pltpu.PrefetchScalarGridSpec(
                num_scalar_prefetch=1,
                grid=(1,),
                in_specs=[pl.BlockSpec(memory_space=pltpu.VMEM)] * len(sources)
                + [anywhere] * len(tokens),
                out_specs=[pl.BlockSpec(memory_space=pltpu.VMEM)] * len(shapes),
            ),
            out_shape=[pltpu.VMEM(shape, jnp.bfloat16) for shape in shapes],
            compiler_params=params,
            cost_estimate=small,
            name=name,
        )(scalars, *map(keep_in_vmem, sources), *tokens)

    def pick(rows, sources, choices, tokens):
        moves = [
            (j, kid, j * kids + kid, choices) for j in range(4) for kid in range(kids)
        ]
        picked = rearrange(
            slots, sources, moves, [(kids, rows, size)] * 4, tokens, "pick_states"
        )
        return [picked[0]] + [swap(picked[j], j) for j in range(1, 4)]

    def early(c, pieces, piece, before, tokens):
        per = groups // pieces
        at = lambda q: (c, 0, per * piece + q)
        operands = [
            x_in, b_in, c_in, dt_in, dt_bias[:, None], a_log[:, None], skip_row, conv_x, conv_bc
        ]
        keep = len(operands)
        tokens = list(tokens) + [keep_in_vmem(a) for a in before]
        first = keep + len(tokens) - len(before)
        return pl.pallas_call(
            functools.partial(
                drop_tokens, functools.partial(early_kernel, per * piece), keep, len(tokens)
            ),
            grid=(per,),
            in_specs=[
                pl.BlockSpec((1, length, wide), at),
                pl.BlockSpec((1, length, size), at),
                pl.BlockSpec((1, length, size), at),
                pl.BlockSpec((1, per_group, length), lambda q: (c, per * piece + q, 0)),
                pl.BlockSpec((per_group, 1), lambda q: (per * piece + q, 0)),
                pl.BlockSpec((per_group, 1), lambda q: (per * piece + q, 0)),
                pl.BlockSpec((1, wide), lambda q: (0, per * piece + q)),
                pl.BlockSpec((taps, wide), lambda q: (0, per * piece + q)),
                pl.BlockSpec((2, taps, size), lambda q: (0, 0, per * piece + q)),
                *[anywhere] * len(tokens),
            ],
            out_specs=[pl.BlockSpec(memory_space=pltpu.VMEM)] * 6,
            out_shape=[
                pltpu.VMEM((groups, length, wide), jnp.float32),
                pltpu.VMEM((groups, length, size), jnp.bfloat16),
                pltpu.VMEM((groups, per_group, length), jnp.float32),
                pltpu.VMEM((groups, length, per_group * FIX), jnp.float32),
                pltpu.VMEM((groups, FIX, wide + 2 * size), jnp.bfloat16),
                pltpu.VMEM((groups, 8, wide + 2 * size), jnp.float32),
            ],
            input_output_aliases={first + i: i for i in range(len(before))},
            scratch_shapes=[pltpu.VMEM((2, 8 + length, size), jnp.float32)],
            compiler_params=params,
            cost_estimate=small,
            name="early",
        )(*operands, *tokens)

    def late(ks, states, parts, result, tokens):
        offset = offsets[ks[0]]
        chunk = sum(SPLIT[k] for k in ks) * width
        operands = [keep_in_vmem(a) for a in (*states[0], *sum((states[k] for k in ks), []), *parts[0], *parts[1])]
        specs = [pl.BlockSpec(memory_space=pltpu.VMEM)] * len(operands)
        keep = 1 + len(operands)
        operands += tokens
        specs += [anywhere] * len(tokens)
        alias = {}
        if result is not None:
            alias = {1 + len(operands): 0}
            operands.append(result)
            specs.append(anywhere)
        kernel = functools.partial(
            late_kernel, offset, [SPLIT[k] for k in ks], lines, reach, SPLIT[0] * width
        )
        return pl.pallas_call(
            functools.partial(drop_tokens, kernel, keep, 1 + len(operands) - keep),
            grid_spec=pltpu.PrefetchScalarGridSpec(
                num_scalar_prefetch=1,
                grid=(1,),
                in_specs=specs,
                out_specs=anywhere,
                scratch_shapes=[
                    pltpu.VMEM((groups, kids, 8 + FIX, max(chunk, 2 * size)), jnp.float32),
                    pltpu.VMEM((groups, kids, length, chunk), jnp.bfloat16),
                    pltpu.SemaphoreType.DMA((groups,)),
                ],
            ),
            out_shape=jax.ShapeDtypeStruct(x_in.shape, jnp.bfloat16),
            input_output_aliases=alias,
            compiler_params=params,
            cost_estimate=small,
            name="late",
        )(place, *operands)

    skip_row = jnp.repeat(d_skip, width)[None, :]
    rows = [SPLIT[0] * width + tail_lines] + [part * width for part in SPLIT[1:]]
    chunks = [pl.ds(sum(rows[:k]), rows[k]) for k in range(len(SPLIT))]
    own, own_2, own_13, sent_4, sent_6 = cast()
    crossed_a = [swap(sent_4, 4), swap(sent_6, 6)]
    along_y, along_z = swap(own_13, 1), swap(own_2, 2)
    parts = [early(0, 1, 0, [], [own, slots])]
    (turn,) = rearrange(
        place, [along_y], [(0, None, None, [(0, 1)])], [own.shape], [parts[0][1]], "stack_turn"
    )
    inside = [own, along_y, along_z, swap(turn, 2)]

    def inside_rows(k):
        return [(0, chunks[k]), (1, (0, chunks[k])), (2, chunks[k]), (3, chunks[k])]

    def cross(k, tokens):
        moves = [(0, j, None, [choice]) for j, choice in enumerate(inside_rows(k))]
        (sent,) = rearrange(place, inside, moves, [(4, rows[k], size)], tokens, "stack_later")
        return sent, swap(sent, 4)

    def pick_later(k, crossed, tokens):
        choices = inside_rows(k) + [(4, j) for j in range(4)]
        return pick(rows[k], [*inside, crossed], choices, tokens)

    second = early(1, 2, 0, [], [turn])
    moves = [(0, n, None, [(n, 1)]) for n in range(2)]
    (spread,) = rearrange(
        place, crossed_a, moves, [(2, rows[0], size)], [second[1]], "stack_first"
    )
    passed = swap(spread, 1)
    sent_b, crossed_b = cross(1, [spread])
    second = early(1, 2, 1, second, [sent_b])
    parts.append(second)
    choices = inside_rows(0) + [(4, 0), (6, 0), (5, 0), (6, 1)]
    states = [pick(rows[0], [*inside, *crossed_a, passed], choices, [second[1]])]
    sent_c, crossed_c = cross(2, [states[0][0], crossed_b])
    states.append(pick_later(1, crossed_b, [sent_c]))
    states.append(pick_later(2, crossed_c, [states[1][0]]))
    result = late([0], states, parts, None, [states[2][0]])
    return late([1, 2], states, parts, result, [])


def solution(mesh):
    rows, cols = P(("groups", "batch"), None, "head"), P(("groups", "batch"), "head")
    placed = (
        rows, rows, rows, cols, P("head"), P("head"), P("head"), P(None, "head"),
        P(None, None, "head"), cols, rows, P(("groups", "batch"), None, None, "head"),
        P("groups"), P("groups"),
    )
    local = local_halves if mesh.shape["batch"] == 8 else local_any
    return jax.shard_map(local, mesh=mesh, in_specs=placed, out_specs=rows, check_vma=False)
```

```python
import functools

import jax
import jax.numpy as jnp
from jax import lax
from jax.experimental import pallas as pl
from jax.experimental.pallas import tpu as pltpu
from jax.sharding import PartitionSpec as P

VMEM_LIMIT = 12 * 1024 * 1024
SPLIT = (6, 6, 4)
FIX = 16
LOG2_E = 1.4426950408889634


def drop_tokens(kernel, keep, tokens, *refs):
    kernel(*refs[:keep], *refs[keep + tokens :])


def parent_of(counts, order):
    index = jnp.arange(counts.shape[0], dtype=jnp.int32)
    bounds = jnp.sum(jnp.where(index[None, :] <= index[:, None], counts[None, :], 0), axis=1)
    return jnp.sum((bounds[None, :] <= order[:, None]).astype(jnp.int32), axis=1)


def three_terms(value):
    terms = []
    for _ in range(3):
        terms.append(value.astype(jnp.bfloat16).astype(jnp.float32))
        value = value - terms[-1]
    return jnp.concatenate(terms)


def conv_silu(padded, tail, rows, taps):
    length = rows.shape[0]
    reach = taps.shape[0] - 1
    padded[8 - reach : 8, :] = jnp.broadcast_to(tail, (reach, rows.shape[1])).astype(jnp.float32)
    padded[8 : 8 + length, :] = rows.astype(jnp.float32)
    total = padded[8 - reach : 8 - reach + length, :] * taps[0:1, :]
    for k in range(1, reach + 1):
        total = total + padded[8 - reach + k : 8 - reach + k + length, :] * taps[k : k + 1, :]
    half = 0.5 * total
    return (half + half * jnp.tanh(half)).astype(jnp.bfloat16)


def early_kernel(
    base, x_ref, b_ref, c_ref, dt_ref, bias_ref, alog_ref, skip_ref, taps_x_ref, taps_bc_ref,
    mixed_ref, c_out_ref, column_ref, first_ref, opening_ref, weights_ref, padded,
):
    length, wide = x_ref.shape[1:]
    heads = dt_ref.shape[1]
    q = base + pl.program_id(0)
    width = wide // heads
    half = length // 2

    def convolve(rows, taps, slot):
        bulk = conv_silu(padded.at[slot % 2], 0.0, rows, taps)[FIX:]
        return jnp.concatenate([jnp.zeros((FIX, rows.shape[1]), jnp.bfloat16), bulk])

    b_conv = convolve(b_ref[0], taps_bc_ref[0], 0)
    c_conv = convolve(c_ref[0], taps_bc_ref[1], 1)
    c_out_ref[q] = c_conv
    size = b_ref.shape[2]
    taps = taps_x_ref.shape[0]
    opening_ref[q, :, :wide] = x_ref[0, :FIX]
    opening_ref[q, :, wide : wide + size] = b_ref[0, :FIX]
    opening_ref[q, :, wide + size :] = c_ref[0, :FIX]
    weights_ref[q, :taps, :wide] = taps_x_ref[...]
    weights_ref[q, :taps, wide : wide + size] = taps_bc_ref[0]
    weights_ref[q, :taps, wide + size :] = taps_bc_ref[1]
    weights_ref[q, taps : taps + 1, :wide] = skip_ref[...]
    scores = lax.dot_general(
        c_conv, b_conv, (((1,), (1,)), ((), ())), preferred_element_type=jnp.float32
    )
    raw = dt_ref[0] + bias_ref[...]
    step = jnp.maximum(raw, 0.0) + jnp.log1p(jnp.exp(-jnp.abs(raw)))
    per_token = step * (-jnp.exp(alog_ref[...]))
    upper = lax.broadcasted_iota(jnp.int32, (length, length), 0) <= lax.broadcasted_iota(
        jnp.int32, (length, length), 1
    )
    sums = jnp.dot(
        three_terms(per_token).astype(jnp.bfloat16),
        upper.astype(jnp.float32).astype(jnp.bfloat16),
        preferred_element_type=jnp.float32,
    )
    total = (sums[:heads] + sums[heads : 2 * heads]) + sums[2 * heads :]
    total = total * LOG2_E
    row = total - jnp.log(step) * LOG2_E
    columns = total.T
    column_ref[q] = total
    causal = lax.broadcasted_iota(jnp.int32, (half, half), 0) >= lax.broadcasted_iota(
        jnp.int32, (half, half), 1
    )
    low = lax.broadcasted_iota(jnp.int32, (length, 2 * width), 1) < width
    for pair in range(heads // 2):
        lanes = slice(pair * 2 * width, (pair + 1) * 2 * width)
        x_conv = convolve(x_ref[0, :, lanes], taps_x_ref[:, lanes], pair)
        parts = []
        for head in (2 * pair, 2 * pair + 1):
            column = jnp.broadcast_to(columns[:, head : head + 1], (length, half))
            rows = row[head : head + 1, :]
            near = jnp.exp2(jnp.where(causal, column[:half] - rows[:, :half], -1e30))
            far = jnp.exp2(column[half:] - rows[:, :half])
            last = jnp.exp2(jnp.where(causal, column[half:] - rows[:, half:], -1e30))
            spot = slice(head * FIX, (head + 1) * FIX)
            first_ref[q, :half, spot] = near[:, :FIX]
            first_ref[q, half:, spot] = far[:, :FIX]
            top = (scores[:half, :half] * near).astype(jnp.bfloat16)
            left = (scores[half:, :half] * far).astype(jnp.bfloat16)
            right = (scores[half:, half:] * last).astype(jnp.bfloat16)
            below = jnp.concatenate([left, right], axis=1)
            parts.append(
                jnp.concatenate(
                    [
                        jnp.dot(top, x_conv[:half], preferred_element_type=jnp.float32),
                        jnp.dot(below, x_conv, preferred_element_type=jnp.float32),
                    ]
                )
            )
        mixed_ref[q, :, lanes] = jnp.where(low, parts[0], parts[1]) + skip_ref[
            :, lanes
        ] * x_conv.astype(jnp.float32)


def late_kernel(offset, heads, lines, reach, tail_at, place_ref, *refs):
    count = len(heads)
    tails, states, parts = refs[:4], refs[4 : 4 + 4 * count], refs[4 + 4 * count : -4]
    y_ref, padded, y_part, sems = refs[-4:]
    _, kids, length, wide = y_part.shape
    rows, heads = heads, sum(heads)
    width = wide // heads
    rows = [part * width for part in rows]
    low_first = lax.broadcasted_iota(jnp.int32, (FIX, 2 * width), 1) < width
    contract = (((1,), (1,)), ((), ()))

    def add(j, kid):
        q = place_ref[0] ^ j
        mixed_ref, held_ref, column_ref, first_ref, opening_ref, weights_ref = parts[
            6 * kid : 6 * kid + 6
        ]
        size = held_ref.shape[2]
        per_group = column_ref.shape[1]
        group_wide = opening_ref.shape[2] - 2 * size
        tail_rows = pl.ds(tail_at, -(-lines * reach // 16) * 16)
        tail = tails[j][kid, tail_rows].astype(jnp.float32)
        state = jnp.concatenate([states[4 * n + j][kid, : rows[n]] for n in range(count)])

        def opening(start, stop, at):
            tap_rows = []
            for k in range(reach):
                first = k * lines + at
                count = (stop - start) // 128
                here = [tail[first + n : first + n + 1] for n in range(count)]
                tap_rows.append(jnp.concatenate(here, axis=1))
            return conv_silu(
                padded.at[j, kid, :, : stop - start],
                jnp.concatenate(tap_rows),
                opening_ref[q, :, start:stop],
                weights_ref[q, : reach + 1, start:stop],
            )

        bc_first = opening(group_wide, group_wide + 2 * size, lines - 2)
        b_first, c_first = bc_first[:, :size], bc_first[:, size:]
        start = offset * width
        x_all = opening(start, start + wide, start // 128).astype(jnp.float32)
        skipped = weights_ref[q, reach + 1 : reach + 2, start : start + wide] * x_all
        c_conv = jnp.concatenate([c_first, held_ref[q, FIX:]])
        terms = three_terms(jnp.exp2(column_ref[q]))
        terms = jnp.concatenate([terms, jnp.zeros((per_group, length), jnp.float32)])
        spread_row = lax.broadcasted_iota(jnp.int32, (4 * per_group, wide), 0)
        spread_lane = lax.broadcasted_iota(jnp.int32, (4 * per_group, wide), 1)
        spread = spread_row % per_group == offset + spread_lane // width
        grow = jnp.dot(
            terms.T.astype(jnp.bfloat16),
            spread.astype(jnp.float32).astype(jnp.bfloat16),
            preferred_element_type=jnp.float32,
        )
        term = lax.dot_general(c_conv, state, contract, preferred_element_type=jnp.float32)
        carried = (term * grow).astype(jnp.bfloat16)
        scores = lax.dot_general(
            c_conv,
            jnp.concatenate([b_first] * heads),
            contract,
            preferred_element_type=jnp.float32,
        )
        here = slice(offset * FIX, (offset + heads) * FIX)
        mixing = (scores * first_ref[q, :, here]).astype(jnp.bfloat16)
        for pair in range(heads // 2):
            lanes = slice(pair * 2 * width, (pair + 1) * 2 * width)
            x_first = x_all[:, lanes]
            stacked = [jnp.where(low_first, x_first, 0.0), jnp.where(low_first, 0.0, x_first)]
            if pair > 0:
                stacked = [jnp.zeros((2 * pair * FIX, 2 * width), jnp.float32)] + stacked
            if 2 * pair + 2 < heads:
                spare = (heads - 2 * pair - 2) * FIX
                stacked = stacked + [jnp.zeros((spare, 2 * width), jnp.float32)]
            part = jnp.dot(
                mixing,
                jnp.concatenate(stacked).astype(jnp.bfloat16),
                preferred_element_type=jnp.float32,
            )
            part = jnp.concatenate([part[:FIX] + skipped[:, lanes], part[FIX:]])
            whole = slice(start + lanes.start, start + lanes.stop)
            y_part[j, kid, :, lanes] = (
                mixed_ref[q, :, whole] + part + carried[:, lanes].astype(jnp.float32)
            ).astype(jnp.bfloat16)

    copies = []
    for j in range(4):
        for kid in range(kids):
            add(j, kid)
        start = (place_ref[0] ^ j) * (y_ref.shape[2] // 4) + offset * width
        lanes = pl.ds(pl.multiple_of(start, 128), wide)
        copies.append(pltpu.make_async_copy(y_part.at[j], y_ref.at[:, :, lanes], sems.at[j]))
        copies[-1].start()
    for copy in copies:
        copy.wait()


def cast_kernel(parts, tailed, reach, lines, *refs):
    count = len(tailed)
    ins, outs = refs[:-count], refs[-count:]
    states, tails = ins[: parts * count], ins[parts * count :]
    for j, out_ref in enumerate(outs):
        start = 0
        for at in range(parts):
            state = states[parts * j + at][0]
            rows = state.shape[0] * state.shape[1]
            out_ref[start : start + rows] = state.reshape(rows, state.shape[2]).astype(jnp.bfloat16)
            start += rows
            if at == 0 and tailed[j]:
                x_tail = tails[2 * j][0].astype(jnp.float32)
                bc_tail = tails[2 * j + 1][0].astype(jnp.float32)
                pieces = []
                for k in range(reach):
                    pieces += [x_tail[k : k + 1, i * 128 : i * 128 + 128] for i in range(lines - 2)]
                    pieces.append(bc_tail[k])
                spare = tailed[j] - lines * reach
                pieces.append(jnp.zeros((spare, 128), jnp.float32))
                out_ref[start : start + tailed[j]] = jnp.concatenate(pieces).astype(jnp.bfloat16)
                start += tailed[j]


def within_kernel(
    parent_ref,
    x_ref,
    b_ref,
    c_ref,
    dt_ref,
    bias_ref,
    alog_ref,
    skip_ref,
    taps_x_ref,
    taps_bc_ref,
    tail_x_ref,
    tail_bc_ref,
    mixed_ref,
    c_out_ref,
    grow_ref,
    padded,
):
    length = x_ref.shape[1]
    heads = dt_ref.shape[1]
    width = x_ref.shape[2] // heads
    b_conv = conv_silu(padded, tail_bc_ref[0, 0], b_ref[0], taps_bc_ref[0])
    c_conv = conv_silu(padded, tail_bc_ref[0, 1], c_ref[0], taps_bc_ref[1])
    c_out_ref[0] = c_conv
    scores = lax.dot_general(
        c_conv, b_conv, (((1,), (1,)), ((), ())), preferred_element_type=jnp.float32
    )
    raw = dt_ref[0] + bias_ref[...]
    step = jnp.maximum(raw, 0.0) + jnp.log1p(jnp.exp(-jnp.abs(raw)))
    per_token = step * (-jnp.exp(alog_ref[...]))
    row = lax.broadcasted_iota(jnp.int32, (length, length), 0)
    col = lax.broadcasted_iota(jnp.int32, (length, length), 1)
    upper = (row <= col).astype(jnp.float32)
    total = lax.dot_general(
        per_token,
        upper,
        (((1,), (0,)), ((), ())),
        precision=lax.Precision.HIGHEST,
        preferred_element_type=jnp.float32,
    )
    total_t = total.T
    grow_ref[0, 0] = jnp.exp(total_t)
    causal = row >= col
    low = lax.broadcasted_iota(jnp.int32, (length, 2 * width), 1) < width
    for pair in range(heads // 2):
        lanes = slice(pair * 2 * width, (pair + 1) * 2 * width)
        x_conv = conv_silu(
            padded, tail_x_ref[0, :, lanes], x_ref[0, :, lanes], taps_x_ref[:, lanes]
        )
        parts = []
        for head in (2 * pair, 2 * pair + 1):
            gap = total_t[:, head : head + 1] - total[head : head + 1, :]
            factor = jnp.exp(jnp.where(causal, gap, -1e30))
            mixing = (scores * factor * step[head : head + 1, :]).astype(jnp.bfloat16)
            parts.append(jnp.dot(mixing, x_conv, preferred_element_type=jnp.float32))
        mixed_ref[0, :, lanes] = (
            jnp.where(low, parts[0], parts[1]) + skip_ref[:, lanes] * x_conv.astype(jnp.float32)
        )


def carried_kernel(state_ref, c_ref, grow_ref, mixed_ref, y_ref):
    sources, _, part, width, size = state_ref.shape
    length = c_ref.shape[1]
    low = lax.broadcasted_iota(jnp.int32, (length, 2 * width), 1) < width
    c_conv = c_ref[0]
    for source in range(sources):
        state = state_ref[source, 0].reshape(part * width, size)
        term = lax.dot_general(
            c_conv, state, (((1,), (1,)), ((), ())), preferred_element_type=jnp.float32
        )
        for pair in range(part // 2):
            head = source * part + 2 * pair
            grow = jnp.where(
                low, grow_ref[0, 0, :, head : head + 1], grow_ref[0, 0, :, head + 1 : head + 2]
            )
            here = slice(2 * pair * width, (2 * pair + 2) * width)
            lanes = slice(head * width, (head + 2) * width)
            carried = (term[:, here] * grow).astype(jnp.bfloat16).astype(jnp.float32)
            y_ref[0, :, lanes] = (mixed_ref[0, :, lanes] + carried).astype(jnp.bfloat16)


def pick_kernel(parent_ref, state_ref, out_ref):
    out_ref[...] = state_ref[...]


def local_any(
    x_in,
    b_in,
    c_in,
    dt_in,
    dt_bias,
    a_log,
    d_skip,
    conv_x,
    conv_bc,
    par_state,
    tail_x,
    tail_bc,
    counts,
    order,
):
    kids, length, columns = x_in.shape
    heads = dt_in.shape[1]
    width, size = par_state.shape[2:]
    ways = lax.axis_size("batch")
    groups = b_in.shape[2] // size
    per_group = heads // groups
    part = heads // ways
    wide = per_group * width
    reach = tail_x.shape[1]
    parents_all = counts.shape[0]
    kids_all = order.shape[0]

    parent = parent_of(counts, order)
    own = lax.dynamic_slice_in_dim(parent, lax.axis_index("batch") * kids, kids)

    sent = par_state.astype(jnp.bfloat16).reshape(ways, part, width, size)
    shares = lax.all_to_all(sent, "batch", split_axis=0, concat_axis=0, tiled=True)

    tails = jnp.concatenate([tail_x.reshape(-1), tail_bc.reshape(-1)])
    tails = jnp.broadcast_to(tails[None], (ways, tails.shape[0]))
    tails = lax.all_to_all(tails, "batch", split_axis=0, concat_axis=0, tiled=True)
    tails_x = tails[:, : reach * columns].reshape(parents_all, reach, columns)
    tails_bc = tails[:, reach * columns :].reshape(parents_all, 2, reach, groups * size)

    picked = pl.pallas_call(
        pick_kernel,
        grid_spec=pltpu.PrefetchScalarGridSpec(
            num_scalar_prefetch=1,
            grid=(kids_all,),
            in_specs=[pl.BlockSpec((1, part, width, size), lambda i, p: (p[i], 0, 0, 0))],
            out_specs=pl.BlockSpec((1, part, width, size), lambda i, p: (i, 0, 0, 0)),
        ),
        out_shape=jax.ShapeDtypeStruct((kids_all, part, width, size), jnp.bfloat16),
        cost_estimate=pl.CostEstimate(
            flops=0, bytes_accessed=4 * kids_all * part * width * size, transcendentals=0
        ),
        name="pick_states",
    )(parent, shares)
    states = lax.all_to_all(
        picked.reshape(ways, kids, part, width, size), "batch", split_axis=0, concat_axis=0, tiled=True
    )

    skip_row = jnp.repeat(d_skip, width)[None, :]
    mixed, c_conv, grow = pl.pallas_call(
        within_kernel,
        grid_spec=pltpu.PrefetchScalarGridSpec(
            num_scalar_prefetch=1,
            grid=(kids, groups),
            in_specs=[
                pl.BlockSpec((1, length, wide), lambda c, q, p: (c, 0, q)),
                pl.BlockSpec((1, length, size), lambda c, q, p: (c, 0, q)),
                pl.BlockSpec((1, length, size), lambda c, q, p: (c, 0, q)),
                pl.BlockSpec((1, per_group, length), lambda c, q, p: (c, q, 0)),
                pl.BlockSpec((per_group, 1), lambda c, q, p: (q, 0)),
                pl.BlockSpec((per_group, 1), lambda c, q, p: (q, 0)),
                pl.BlockSpec((1, wide), lambda c, q, p: (0, q)),
                pl.BlockSpec((reach + 1, wide), lambda c, q, p: (0, q)),
                pl.BlockSpec((2, reach + 1, size), lambda c, q, p: (0, 0, q)),
                pl.BlockSpec((1, reach, wide), lambda c, q, p: (p[c], 0, q)),
                pl.BlockSpec((1, 2, reach, size), lambda c, q, p: (p[c], 0, 0, q)),
            ],
            out_specs=[
                pl.BlockSpec((1, length, wide), lambda c, q, p: (c, 0, q)),
                pl.BlockSpec((1, length, size), lambda c, q, p: (c, 0, q)),
                pl.BlockSpec((1, 1, length, per_group), lambda c, q, p: (c, q, 0, 0)),
            ],
            scratch_shapes=[pltpu.VMEM((8 + length, size), jnp.float32)],
        ),
        out_shape=[
            jax.ShapeDtypeStruct((kids, length, columns), jnp.float32),
            jax.ShapeDtypeStruct((kids, length, groups * size), jnp.bfloat16),
            jax.ShapeDtypeStruct((kids, groups, length, per_group), jnp.float32),
        ],
        compiler_params=pltpu.CompilerParams(vmem_limit_bytes=4 * VMEM_LIMIT),
        cost_estimate=pl.CostEstimate(
            flops=4 * kids * heads * length * length * width,
            bytes_accessed=6 * kids * length * columns,
            transcendentals=kids * heads * length * length,
        ),
        name="within",
    )(
        own,
        x_in,
        b_in,
        c_in,
        dt_in,
        dt_bias[:, None],
        a_log[:, None],
        skip_row,
        conv_x,
        conv_bc,
        tails_x,
        tails_bc,
    )

    sources = per_group // part
    return pl.pallas_call(
        carried_kernel,
        grid=(kids, groups),
        in_specs=[
            pl.BlockSpec((sources, 1, part, width, size), lambda c, q: (q, c, 0, 0, 0)),
            pl.BlockSpec((1, length, size), lambda c, q: (c, 0, q)),
            pl.BlockSpec((1, 1, length, per_group), lambda c, q: (c, q, 0, 0)),
            pl.BlockSpec((1, length, wide), lambda c, q: (c, 0, q)),
        ],
        out_specs=pl.BlockSpec((1, length, wide), lambda c, q: (c, 0, q)),
        out_shape=jax.ShapeDtypeStruct((kids, length, columns), jnp.bfloat16),
        compiler_params=pltpu.CompilerParams(vmem_limit_bytes=4 * VMEM_LIMIT),
        cost_estimate=pl.CostEstimate(
            flops=2 * kids * length * columns * size,
            bytes_accessed=8 * kids * length * columns,
            transcendentals=0,
        ),
        name="carried",
    )(states, c_conv, grow, mixed)


def local_halves(
    x_in, b_in, c_in, dt_in, dt_bias, a_log, d_skip, conv_x, conv_bc,
    par_state, tail_x, tail_bc, counts, order,
):
    kids, length, columns = x_in.shape
    heads = dt_in.shape[1]
    width, size = par_state.shape[2:]
    groups = b_in.shape[2] // size
    per_group = heads // groups
    wide = per_group * width
    taps = conv_x.shape[0]
    reach = taps - 1
    lines = (wide + 2 * size) // 128
    tail_lines = -(-lines * reach // 16) * 16
    params = pltpu.CompilerParams(vmem_limit_bytes=VMEM_LIMIT)
    anywhere = pl.BlockSpec(memory_space=pl.ANY)
    small = pl.CostEstimate(flops=1, bytes_accessed=1, transcendentals=0)

    stay = lambda x: pltpu.with_memory_space_constraint(x, pltpu.HBM)
    keep_in_vmem = lambda x: pltpu.with_memory_space_constraint(x, pltpu.VMEM)
    x_in, b_in, c_in, dt_in, conv_x, conv_bc = map(stay, (x_in, b_in, c_in, dt_in, conv_x, conv_bc))

    me = lax.axis_index("batch")
    parent = parent_of(counts, order)
    child = (jnp.arange(4 * kids, dtype=jnp.int32) // kids ^ me) * kids
    child = child + jnp.arange(4 * kids, dtype=jnp.int32) % kids
    catalog = jnp.arange(4 * 2 * kids, dtype=jnp.int32)
    owner = jnp.sum(jnp.where(child[:, None] == catalog[None, :], parent[None, :], 0), axis=1)
    slots = owner ^ me
    place = (me % 4).astype(jnp.int32)[None]

    state = stay(par_state.reshape(groups, per_group, width, size))
    x_tails, bc_tails = stay(tail_x), stay(tail_bc.transpose(0, 2, 1, 3))
    offsets = [sum(SPLIT[:k]) for k in range(len(SPLIT))]

    def swap(value, r):
        return lax.ppermute(value, "batch", perm=[(i, i ^ r) for i in range(8)])

    def cast():
        rows = per_group * width + tail_lines
        rows_a = SPLIT[0] * width + tail_lines
        blocks = [(0, SPLIT[0])] + [(at, 2) for at in range(SPLIT[0], per_group, 2)]
        count = len(blocks) + 2

        def kernel(place_ref, *refs):
            ins, outs = refs[: 4 * count], refs[4 * count :]
            quarters = [outs[0], outs[2].at[0], outs[1], outs[2].at[1]]
            for n, out_ref in enumerate(quarters):
                cast_kernel(
                    len(blocks), [tail_lines], reach, lines, *ins[count * n : count * n + count], out_ref
                )
                outs[3 + n // 2][n % 2] = out_ref[:rows_a]

        operands, specs = [], []
        for n in range(4):
            for offset, part in blocks:
                operands.append(state)
                specs.append(
                    pl.BlockSpec(
                        (1, part, width, size),
                        lambda i, p, n=n, at=offset // part: (p[0] ^ n, at, 0, 0),
                    )
                )
            operands += [x_tails, bc_tails]
            specs += [
                pl.BlockSpec((1, reach, wide), lambda i, p, n=n: (0, 0, p[0] ^ n)),
                pl.BlockSpec((1, reach, 2, size), lambda i, p, n=n: (0, 0, 0, p[0] ^ n)),
            ]
        shapes = [(rows, size)] * 2 + [(2, rows, size)] + [(2, rows_a, size)] * 2
        return pl.pallas_call(
            kernel,
            grid_spec=pltpu.PrefetchScalarGridSpec(
                num_scalar_prefetch=1,
                grid=(1,),
                in_specs=specs,
                out_specs=[pl.BlockSpec(memory_space=pltpu.VMEM)] * len(shapes),
            ),
            out_shape=[pltpu.VMEM(shape, jnp.bfloat16) for shape in shapes],
            compiler_params=params,
            cost_estimate=small,
            name="cast_states",
        )(place, *operands)

    def rearrange(scalars, sources, moves, shapes, tokens, name):
        def kernel(scalars_ref, *refs):
            held, outs = refs[: len(sources)], refs[len(sources) :]
            for out, at, scalar, choices in moves:
                for value, (number, take) in enumerate(choices):

                    def copy(out=out, at=at, number=number, take=take):
                        rows = held[number][...] if take is None else held[number][take]
                        if at is None:
                            outs[out][...] = rows
                        else:
                            outs[out][at] = rows

                    if scalar is None:
                        copy()
                    else:
                        pl.when(scalars_ref[scalar] == value)(copy)

        return pl.pallas_call(
            functools.partial(drop_tokens, kernel, 1 + len(sources), len(tokens)),
            grid_spec=pltpu.PrefetchScalarGridSpec(
                num_scalar_prefetch=1,
                grid=(1,),
                in_specs=[pl.BlockSpec(memory_space=pltpu.VMEM)] * len(sources)
                + [anywhere] * len(tokens),
                out_specs=[pl.BlockSpec(memory_space=pltpu.VMEM)] * len(shapes),
            ),
            out_shape=[pltpu.VMEM(shape, jnp.bfloat16) for shape in shapes],
            compiler_params=params,
            cost_estimate=small,
            name=name,
        )(scalars, *map(keep_in_vmem, sources), *tokens)

    def pick(rows, sources, choices, tokens):
        moves = [
            (j, kid, j * kids + kid, choices) for j in range(4) for kid in range(kids)
        ]
        picked = rearrange(
            slots, sources, moves, [(kids, rows, size)] * 4, tokens, "pick_states"
        )
        return [picked[0]] + [swap(picked[j], j) for j in range(1, 4)]

    def early(c, pieces, piece, before, tokens):
        per = groups // pieces
        at = lambda q: (c, 0, per * piece + q)
        operands = [
            x_in, b_in, c_in, dt_in, dt_bias[:, None], a_log[:, None], skip_row, conv_x, conv_bc
        ]
        keep = len(operands)
        tokens = list(tokens) + [keep_in_vmem(a) for a in before]
        first = keep + len(tokens) - len(before)
        return pl.pallas_call(
            functools.partial(
                drop_tokens, functools.partial(early_kernel, per * piece), keep, len(tokens)
            ),
            grid=(per,),
            in_specs=[
                pl.BlockSpec((1, length, wide), at),
                pl.BlockSpec((1, length, size), at),
                pl.BlockSpec((1, length, size), at),
                pl.BlockSpec((1, per_group, length), lambda q: (c, per * piece + q, 0)),
                pl.BlockSpec((per_group, 1), lambda q: (per * piece + q, 0)),
                pl.BlockSpec((per_group, 1), lambda q: (per * piece + q, 0)),
                pl.BlockSpec((1, wide), lambda q: (0, per * piece + q)),
                pl.BlockSpec((taps, wide), lambda q: (0, per * piece + q)),
                pl.BlockSpec((2, taps, size), lambda q: (0, 0, per * piece + q)),
                *[anywhere] * len(tokens),
            ],
            out_specs=[pl.BlockSpec(memory_space=pltpu.VMEM)] * 6,
            out_shape=[
                pltpu.VMEM((groups, length, wide), jnp.float32),
                pltpu.VMEM((groups, length, size), jnp.bfloat16),
                pltpu.VMEM((groups, per_group, length), jnp.float32),
                pltpu.VMEM((groups, length, per_group * FIX), jnp.float32),
                pltpu.VMEM((groups, FIX, wide + 2 * size), jnp.bfloat16),
                pltpu.VMEM((groups, 8, wide + 2 * size), jnp.float32),
            ],
            input_output_aliases={first + i: i for i in range(len(before))},
            scratch_shapes=[pltpu.VMEM((2, 8 + length, size), jnp.float32)],
            compiler_params=params,
            cost_estimate=small,
            name="early",
        )(*operands, *tokens)

    def late(ks, states, parts, result, tokens):
        offset = offsets[ks[0]]
        chunk = sum(SPLIT[k] for k in ks) * width
        operands = [keep_in_vmem(a) for a in (*states[0], *sum((states[k] for k in ks), []), *parts[0], *parts[1])]
        specs = [pl.BlockSpec(memory_space=pltpu.VMEM)] * len(operands)
        keep = 1 + len(operands)
        operands += tokens
        specs += [anywhere] * len(tokens)
        alias = {}
        if result is not None:
            alias = {1 + len(operands): 0}
            operands.append(result)
            specs.append(anywhere)
        kernel = functools.partial(
            late_kernel, offset, [SPLIT[k] for k in ks], lines, reach, SPLIT[0] * width
        )
        return pl.pallas_call(
            functools.partial(drop_tokens, kernel, keep, 1 + len(operands) - keep),
            grid_spec=pltpu.PrefetchScalarGridSpec(
                num_scalar_prefetch=1,
                grid=(1,),
                in_specs=specs,
                out_specs=anywhere,
                scratch_shapes=[
                    pltpu.VMEM((groups, kids, 8 + FIX, max(chunk, 2 * size)), jnp.float32),
                    pltpu.VMEM((groups, kids, length, chunk), jnp.bfloat16),
                    pltpu.SemaphoreType.DMA((groups,)),
                ],
            ),
            out_shape=jax.ShapeDtypeStruct(x_in.shape, jnp.bfloat16),
            input_output_aliases=alias,
            compiler_params=params,
            cost_estimate=small,
            name="late",
        )(place, *operands)

    skip_row = jnp.repeat(d_skip, width)[None, :]
    rows = [SPLIT[0] * width + tail_lines] + [part * width for part in SPLIT[1:]]
    chunks = [pl.ds(sum(rows[:k]), rows[k]) for k in range(len(SPLIT))]
    own, own_2, own_13, sent_4, sent_6 = cast()
    crossed_a = [swap(sent_4, 4), swap(sent_6, 6)]
    along_y, along_z = swap(own_13, 1), swap(own_2, 2)
    parts = [early(0, 1, 0, [], [own, slots])]
    spare = sum(rows[1:])
    turn = rearrange(
        place,
        [along_y],
        [(0, None, None, [(0, (1, chunks[0]))]), (1, None, None, [(0, (1, pl.ds(rows[0], spare)))])],
        [(rows[0], size), (spare, size)],
        [parts[0][1]],
        "stack_turn",
    )
    inside = [own, along_y, along_z, swap(turn[0], 2), swap(turn[1], 2)]

    def inside_rows(k):
        last = (3, None) if k == 0 else (4, pl.ds(sum(rows[1:k]), rows[k]))
        return [(0, chunks[k]), (1, (0, chunks[k])), (2, chunks[k]), last]

    def cross(k, tokens):
        moves = [(0, j, None, [choice]) for j, choice in enumerate(inside_rows(k))]
        (sent,) = rearrange(place, inside, moves, [(4, rows[k], size)], tokens, "stack_later")
        return sent, swap(sent, 4)

    def pick_later(k, crossed, tokens):
        choices = inside_rows(k) + [(5, j) for j in range(4)]
        return pick(rows[k], [*inside, crossed], choices, tokens)

    moves = [(0, n, None, [(n, 1)]) for n in range(2)]
    (spread,) = rearrange(place, crossed_a, moves, [(2, rows[0], size)], [turn[0]], "stack_first")
    passed = swap(spread, 1)
    second = early(1, 2, 0, [], [spread])
    sent_b, crossed_b = cross(1, [second[1], passed])
    choices = inside_rows(0) + [(5, 0), (7, 0), (6, 0), (7, 1)]
    states = [pick(rows[0], [*inside, *crossed_a, passed], choices, [sent_b])]
    second = early(1, 2, 1, second, [states[0][0]])
    parts.append(second)
    sent_c, crossed_c = cross(2, [second[1], crossed_b])
    states.append(pick_later(1, crossed_b, [sent_c, *states[0]]))
    result = late([0], states, parts, None, [states[1][0]])
    states.append(pick_later(2, crossed_c, [stay(result)]))
    result = late([1], states, parts, result, [states[2][0]])
    return late([2], states, parts, result, [])


def solution(mesh):
    rows, cols = P(("groups", "batch"), None, "head"), P(("groups", "batch"), "head")
    placed = (
        rows, rows, rows, cols, P("head"), P("head"), P("head"), P(None, "head"),
        P(None, None, "head"), cols, rows, P(("groups", "batch"), None, None, "head"),
        P("groups"), P("groups"),
    )
    local = local_halves if mesh.shape["batch"] == 8 else local_any
    return jax.shard_map(local, mesh=mesh, in_specs=placed, out_specs=rows, check_vma=False)
```

```python
import functools

import jax
import jax.numpy as jnp
from jax import lax
from jax.experimental import pallas as pl
from jax.experimental.pallas import tpu as pltpu
from jax.sharding import PartitionSpec as P

VMEM_LIMIT = 12 * 1024 * 1024
SPLIT = (6, 6, 4)
FIX = 16
LOG2_E = 1.4426950408889634


def drop_tokens(kernel, keep, tokens, *refs):
    kernel(*refs[:keep], *refs[keep + tokens :])


def parent_of(counts, order):
    index = jnp.arange(counts.shape[0], dtype=jnp.int32)
    bounds = jnp.sum(jnp.where(index[None, :] <= index[:, None], counts[None, :], 0), axis=1)
    return jnp.sum((bounds[None, :] <= order[:, None]).astype(jnp.int32), axis=1)


def three_terms(value):
    terms = []
    for _ in range(3):
        terms.append(value.astype(jnp.bfloat16).astype(jnp.float32))
        value = value - terms[-1]
    return jnp.concatenate(terms)


def conv_silu(padded, tail, rows, taps):
    length = rows.shape[0]
    reach = taps.shape[0] - 1
    padded[8 - reach : 8, :] = jnp.broadcast_to(tail, (reach, rows.shape[1])).astype(jnp.float32)
    padded[8 : 8 + length, :] = rows.astype(jnp.float32)
    total = padded[8 - reach : 8 - reach + length, :] * taps[0:1, :]
    for k in range(1, reach + 1):
        total = total + padded[8 - reach + k : 8 - reach + k + length, :] * taps[k : k + 1, :]
    half = 0.5 * total
    return (half + half * jnp.tanh(half)).astype(jnp.bfloat16)


def early_kernel(
    base, x_ref, b_ref, c_ref, dt_ref, bias_ref, alog_ref, skip_ref, taps_x_ref, taps_bc_ref,
    mixed_ref, c_out_ref, column_ref, first_ref, opening_ref, weights_ref, padded,
):
    length, wide = x_ref.shape[1:]
    heads = dt_ref.shape[1]
    q = base + pl.program_id(0)
    width = wide // heads
    half = length // 2

    def convolve(rows, taps, slot):
        bulk = conv_silu(padded.at[slot % 2], 0.0, rows, taps)[FIX:]
        return jnp.concatenate([jnp.zeros((FIX, rows.shape[1]), jnp.bfloat16), bulk])

    b_conv = convolve(b_ref[0], taps_bc_ref[0], 0)
    c_conv = convolve(c_ref[0], taps_bc_ref[1], 1)
    c_out_ref[q] = c_conv
    size = b_ref.shape[2]
    taps = taps_x_ref.shape[0]
    opening_ref[q, :, :wide] = x_ref[0, :FIX]
    opening_ref[q, :, wide : wide + size] = b_ref[0, :FIX]
    opening_ref[q, :, wide + size :] = c_ref[0, :FIX]
    weights_ref[q, :taps, :wide] = taps_x_ref[...]
    weights_ref[q, :taps, wide : wide + size] = taps_bc_ref[0]
    weights_ref[q, :taps, wide + size :] = taps_bc_ref[1]
    weights_ref[q, taps : taps + 1, :wide] = skip_ref[...]
    scores = lax.dot_general(
        c_conv, b_conv, (((1,), (1,)), ((), ())), preferred_element_type=jnp.float32
    )
    raw = dt_ref[0] + bias_ref[...]
    step = jnp.maximum(raw, 0.0) + jnp.log1p(jnp.exp(-jnp.abs(raw)))
    per_token = step * (-jnp.exp(alog_ref[...]))
    upper = lax.broadcasted_iota(jnp.int32, (length, length), 0) <= lax.broadcasted_iota(
        jnp.int32, (length, length), 1
    )
    sums = jnp.dot(
        three_terms(per_token).astype(jnp.bfloat16),
        upper.astype(jnp.float32).astype(jnp.bfloat16),
        preferred_element_type=jnp.float32,
    )
    total = (sums[:heads] + sums[heads : 2 * heads]) + sums[2 * heads :]
    total = total * LOG2_E
    row = total - jnp.log(step) * LOG2_E
    columns = total.T
    column_ref[q] = total
    causal = lax.broadcasted_iota(jnp.int32, (half, half), 0) >= lax.broadcasted_iota(
        jnp.int32, (half, half), 1
    )
    low = lax.broadcasted_iota(jnp.int32, (length, 2 * width), 1) < width
    for pair in range(heads // 2):
        lanes = slice(pair * 2 * width, (pair + 1) * 2 * width)
        x_conv = convolve(x_ref[0, :, lanes], taps_x_ref[:, lanes], pair)
        parts = []
        for head in (2 * pair, 2 * pair + 1):
            column = jnp.broadcast_to(columns[:, head : head + 1], (length, half))
            rows = row[head : head + 1, :]
            near = jnp.exp2(jnp.where(causal, column[:half] - rows[:, :half], -1e30))
            far = jnp.exp2(column[half:] - rows[:, :half])
            last = jnp.exp2(jnp.where(causal, column[half:] - rows[:, half:], -1e30))
            spot = slice(head * FIX, (head + 1) * FIX)
            first_ref[q, :half, spot] = near[:, :FIX]
            first_ref[q, half:, spot] = far[:, :FIX]
            top = (scores[:half, :half] * near).astype(jnp.bfloat16)
            left = (scores[half:, :half] * far).astype(jnp.bfloat16)
            right = (scores[half:, half:] * last).astype(jnp.bfloat16)
            below = jnp.concatenate([left, right], axis=1)
            parts.append(
                jnp.concatenate(
                    [
                        jnp.dot(top, x_conv[:half], preferred_element_type=jnp.float32),
                        jnp.dot(below, x_conv, preferred_element_type=jnp.float32),
                    ]
                )
            )
        mixed_ref[q, :, lanes] = jnp.where(low, parts[0], parts[1]) + skip_ref[
            :, lanes
        ] * x_conv.astype(jnp.float32)


def late_kernel(offset, heads, lines, reach, tail_at, place_ref, *refs):
    count = len(heads)
    tails, states, parts = refs[:4], refs[4 : 4 + 4 * count], refs[4 + 4 * count : -4]
    y_ref, padded, y_part, sems = refs[-4:]
    _, kids, length, wide = y_part.shape
    rows, heads = heads, sum(heads)
    width = wide // heads
    rows = [part * width for part in rows]
    low_first = lax.broadcasted_iota(jnp.int32, (FIX, 2 * width), 1) < width
    contract = (((1,), (1,)), ((), ()))

    def add(j, kid):
        q = place_ref[0] ^ j
        mixed_ref, held_ref, column_ref, first_ref, opening_ref, weights_ref = parts[
            6 * kid : 6 * kid + 6
        ]
        size = held_ref.shape[2]
        per_group = column_ref.shape[1]
        group_wide = opening_ref.shape[2] - 2 * size
        tail_rows = pl.ds(tail_at, -(-lines * reach // 16) * 16)
        tail = tails[j][kid, tail_rows].astype(jnp.float32)
        state = jnp.concatenate([states[4 * n + j][kid, : rows[n]] for n in range(count)])

        def opening(start, stop, at):
            tap_rows = []
            for k in range(reach):
                first = k * lines + at
                count = (stop - start) // 128
                here = [tail[first + n : first + n + 1] for n in range(count)]
                tap_rows.append(jnp.concatenate(here, axis=1))
            return conv_silu(
                padded.at[j, kid, :, : stop - start],
                jnp.concatenate(tap_rows),
                opening_ref[q, :, start:stop],
                weights_ref[q, : reach + 1, start:stop],
            )

        bc_first = opening(group_wide, group_wide + 2 * size, lines - 2)
        b_first, c_first = bc_first[:, :size], bc_first[:, size:]
        start = offset * width
        x_all = opening(start, start + wide, start // 128).astype(jnp.float32)
        skipped = weights_ref[q, reach + 1 : reach + 2, start : start + wide] * x_all
        c_conv = jnp.concatenate([c_first, held_ref[q, FIX:]])
        terms = three_terms(jnp.exp2(column_ref[q]))
        terms = jnp.concatenate([terms, jnp.zeros((per_group, length), jnp.float32)])
        spread_row = lax.broadcasted_iota(jnp.int32, (4 * per_group, wide), 0)
        spread_lane = lax.broadcasted_iota(jnp.int32, (4 * per_group, wide), 1)
        spread = spread_row % per_group == offset + spread_lane // width
        grow = jnp.dot(
            terms.T.astype(jnp.bfloat16),
            spread.astype(jnp.float32).astype(jnp.bfloat16),
            preferred_element_type=jnp.float32,
        )
        term = lax.dot_general(c_conv, state, contract, preferred_element_type=jnp.float32)
        carried = (term * grow).astype(jnp.bfloat16)
        scores = lax.dot_general(
            c_conv,
            jnp.concatenate([b_first] * heads),
            contract,
            preferred_element_type=jnp.float32,
        )
        here = slice(offset * FIX, (offset + heads) * FIX)
        mixing = (scores * first_ref[q, :, here]).astype(jnp.bfloat16)
        for pair in range(heads // 2):
            lanes = slice(pair * 2 * width, (pair + 1) * 2 * width)
            x_first = x_all[:, lanes]
            stacked = [jnp.where(low_first, x_first, 0.0), jnp.where(low_first, 0.0, x_first)]
            if pair > 0:
                stacked = [jnp.zeros((2 * pair * FIX, 2 * width), jnp.float32)] + stacked
            if 2 * pair + 2 < heads:
                spare = (heads - 2 * pair - 2) * FIX
                stacked = stacked + [jnp.zeros((spare, 2 * width), jnp.float32)]
            part = jnp.dot(
                mixing,
                jnp.concatenate(stacked).astype(jnp.bfloat16),
                preferred_element_type=jnp.float32,
            )
            part = jnp.concatenate([part[:FIX] + skipped[:, lanes], part[FIX:]])
            whole = slice(start + lanes.start, start + lanes.stop)
            y_part[j, kid, :, lanes] = (
                mixed_ref[q, :, whole] + part + carried[:, lanes].astype(jnp.float32)
            ).astype(jnp.bfloat16)

    copies = []
    for j in range(4):
        for kid in range(kids):
            add(j, kid)
        start = (place_ref[0] ^ j) * (y_ref.shape[2] // 4) + offset * width
        lanes = pl.ds(pl.multiple_of(start, 128), wide)
        copies.append(pltpu.make_async_copy(y_part.at[j], y_ref.at[:, :, lanes], sems.at[j]))
        copies[-1].start()
    for copy in copies:
        copy.wait()


def cast_kernel(parts, tailed, reach, lines, *refs):
    count = len(tailed)
    ins, outs = refs[:-count], refs[-count:]
    states, tails = ins[: parts * count], ins[parts * count :]
    for j, out_ref in enumerate(outs):
        start = 0
        for at in range(parts):
            state = states[parts * j + at][0]
            rows = state.shape[0] * state.shape[1]
            out_ref[start : start + rows] = state.reshape(rows, state.shape[2]).astype(jnp.bfloat16)
            start += rows
            if at == 0 and tailed[j]:
                x_tail = tails[2 * j][0].astype(jnp.float32)
                bc_tail = tails[2 * j + 1][0].astype(jnp.float32)
                pieces = []
                for k in range(reach):
                    pieces += [x_tail[k : k + 1, i * 128 : i * 128 + 128] for i in range(lines - 2)]
                    pieces.append(bc_tail[k])
                spare = tailed[j] - lines * reach
                pieces.append(jnp.zeros((spare, 128), jnp.float32))
                out_ref[start : start + tailed[j]] = jnp.concatenate(pieces).astype(jnp.bfloat16)
                start += tailed[j]


def within_kernel(
    parent_ref,
    x_ref,
    b_ref,
    c_ref,
    dt_ref,
    bias_ref,
    alog_ref,
    skip_ref,
    taps_x_ref,
    taps_bc_ref,
    tail_x_ref,
    tail_bc_ref,
    mixed_ref,
    c_out_ref,
    grow_ref,
    padded,
):
    length = x_ref.shape[1]
    heads = dt_ref.shape[1]
    width = x_ref.shape[2] // heads
    b_conv = conv_silu(padded, tail_bc_ref[0, 0], b_ref[0], taps_bc_ref[0])
    c_conv = conv_silu(padded, tail_bc_ref[0, 1], c_ref[0], taps_bc_ref[1])
    c_out_ref[0] = c_conv
    scores = lax.dot_general(
        c_conv, b_conv, (((1,), (1,)), ((), ())), preferred_element_type=jnp.float32
    )
    raw = dt_ref[0] + bias_ref[...]
    step = jnp.maximum(raw, 0.0) + jnp.log1p(jnp.exp(-jnp.abs(raw)))
    per_token = step * (-jnp.exp(alog_ref[...]))
    row = lax.broadcasted_iota(jnp.int32, (length, length), 0)
    col = lax.broadcasted_iota(jnp.int32, (length, length), 1)
    upper = (row <= col).astype(jnp.float32)
    total = lax.dot_general(
        per_token,
        upper,
        (((1,), (0,)), ((), ())),
        precision=lax.Precision.HIGHEST,
        preferred_element_type=jnp.float32,
    )
    total_t = total.T
    grow_ref[0, 0] = jnp.exp(total_t)
    causal = row >= col
    low = lax.broadcasted_iota(jnp.int32, (length, 2 * width), 1) < width
    for pair in range(heads // 2):
        lanes = slice(pair * 2 * width, (pair + 1) * 2 * width)
        x_conv = conv_silu(
            padded, tail_x_ref[0, :, lanes], x_ref[0, :, lanes], taps_x_ref[:, lanes]
        )
        parts = []
        for head in (2 * pair, 2 * pair + 1):
            gap = total_t[:, head : head + 1] - total[head : head + 1, :]
            factor = jnp.exp(jnp.where(causal, gap, -1e30))
            mixing = (scores * factor * step[head : head + 1, :]).astype(jnp.bfloat16)
            parts.append(jnp.dot(mixing, x_conv, preferred_element_type=jnp.float32))
        mixed_ref[0, :, lanes] = (
            jnp.where(low, parts[0], parts[1]) + skip_ref[:, lanes] * x_conv.astype(jnp.float32)
        )


def carried_kernel(state_ref, c_ref, grow_ref, mixed_ref, y_ref):
    sources, _, part, width, size = state_ref.shape
    length = c_ref.shape[1]
    low = lax.broadcasted_iota(jnp.int32, (length, 2 * width), 1) < width
    c_conv = c_ref[0]
    for source in range(sources):
        state = state_ref[source, 0].reshape(part * width, size)
        term = lax.dot_general(
            c_conv, state, (((1,), (1,)), ((), ())), preferred_element_type=jnp.float32
        )
        for pair in range(part // 2):
            head = source * part + 2 * pair
            grow = jnp.where(
                low, grow_ref[0, 0, :, head : head + 1], grow_ref[0, 0, :, head + 1 : head + 2]
            )
            here = slice(2 * pair * width, (2 * pair + 2) * width)
            lanes = slice(head * width, (head + 2) * width)
            carried = (term[:, here] * grow).astype(jnp.bfloat16).astype(jnp.float32)
            y_ref[0, :, lanes] = (mixed_ref[0, :, lanes] + carried).astype(jnp.bfloat16)


def pick_kernel(parent_ref, state_ref, out_ref):
    out_ref[...] = state_ref[...]


def local_any(
    x_in,
    b_in,
    c_in,
    dt_in,
    dt_bias,
    a_log,
    d_skip,
    conv_x,
    conv_bc,
    par_state,
    tail_x,
    tail_bc,
    counts,
    order,
):
    kids, length, columns = x_in.shape
    heads = dt_in.shape[1]
    width, size = par_state.shape[2:]
    ways = lax.axis_size("batch")
    groups = b_in.shape[2] // size
    per_group = heads // groups
    part = heads // ways
    wide = per_group * width
    reach = tail_x.shape[1]
    parents_all = counts.shape[0]
    kids_all = order.shape[0]

    parent = parent_of(counts, order)
    own = lax.dynamic_slice_in_dim(parent, lax.axis_index("batch") * kids, kids)

    sent = par_state.astype(jnp.bfloat16).reshape(ways, part, width, size)
    shares = lax.all_to_all(sent, "batch", split_axis=0, concat_axis=0, tiled=True)

    tails = jnp.concatenate([tail_x.reshape(-1), tail_bc.reshape(-1)])
    tails = jnp.broadcast_to(tails[None], (ways, tails.shape[0]))
    tails = lax.all_to_all(tails, "batch", split_axis=0, concat_axis=0, tiled=True)
    tails_x = tails[:, : reach * columns].reshape(parents_all, reach, columns)
    tails_bc = tails[:, reach * columns :].reshape(parents_all, 2, reach, groups * size)

    picked = pl.pallas_call(
        pick_kernel,
        grid_spec=pltpu.PrefetchScalarGridSpec(
            num_scalar_prefetch=1,
            grid=(kids_all,),
            in_specs=[pl.BlockSpec((1, part, width, size), lambda i, p: (p[i], 0, 0, 0))],
            out_specs=pl.BlockSpec((1, part, width, size), lambda i, p: (i, 0, 0, 0)),
        ),
        out_shape=jax.ShapeDtypeStruct((kids_all, part, width, size), jnp.bfloat16),
        cost_estimate=pl.CostEstimate(
            flops=0, bytes_accessed=4 * kids_all * part * width * size, transcendentals=0
        ),
        name="pick_states",
    )(parent, shares)
    states = lax.all_to_all(
        picked.reshape(ways, kids, part, width, size), "batch", split_axis=0, concat_axis=0, tiled=True
    )

    skip_row = jnp.repeat(d_skip, width)[None, :]
    mixed, c_conv, grow = pl.pallas_call(
        within_kernel,
        grid_spec=pltpu.PrefetchScalarGridSpec(
            num_scalar_prefetch=1,
            grid=(kids, groups),
            in_specs=[
                pl.BlockSpec((1, length, wide), lambda c, q, p: (c, 0, q)),
                pl.BlockSpec((1, length, size), lambda c, q, p: (c, 0, q)),
                pl.BlockSpec((1, length, size), lambda c, q, p: (c, 0, q)),
                pl.BlockSpec((1, per_group, length), lambda c, q, p: (c, q, 0)),
                pl.BlockSpec((per_group, 1), lambda c, q, p: (q, 0)),
                pl.BlockSpec((per_group, 1), lambda c, q, p: (q, 0)),
                pl.BlockSpec((1, wide), lambda c, q, p: (0, q)),
                pl.BlockSpec((reach + 1, wide), lambda c, q, p: (0, q)),
                pl.BlockSpec((2, reach + 1, size), lambda c, q, p: (0, 0, q)),
                pl.BlockSpec((1, reach, wide), lambda c, q, p: (p[c], 0, q)),
                pl.BlockSpec((1, 2, reach, size), lambda c, q, p: (p[c], 0, 0, q)),
            ],
            out_specs=[
                pl.BlockSpec((1, length, wide), lambda c, q, p: (c, 0, q)),
                pl.BlockSpec((1, length, size), lambda c, q, p: (c, 0, q)),
                pl.BlockSpec((1, 1, length, per_group), lambda c, q, p: (c, q, 0, 0)),
            ],
            scratch_shapes=[pltpu.VMEM((8 + length, size), jnp.float32)],
        ),
        out_shape=[
            jax.ShapeDtypeStruct((kids, length, columns), jnp.float32),
            jax.ShapeDtypeStruct((kids, length, groups * size), jnp.bfloat16),
            jax.ShapeDtypeStruct((kids, groups, length, per_group), jnp.float32),
        ],
        compiler_params=pltpu.CompilerParams(vmem_limit_bytes=4 * VMEM_LIMIT),
        cost_estimate=pl.CostEstimate(
            flops=4 * kids * heads * length * length * width,
            bytes_accessed=6 * kids * length * columns,
            transcendentals=kids * heads * length * length,
        ),
        name="within",
    )(
        own,
        x_in,
        b_in,
        c_in,
        dt_in,
        dt_bias[:, None],
        a_log[:, None],
        skip_row,
        conv_x,
        conv_bc,
        tails_x,
        tails_bc,
    )

    sources = per_group // part
    return pl.pallas_call(
        carried_kernel,
        grid=(kids, groups),
        in_specs=[
            pl.BlockSpec((sources, 1, part, width, size), lambda c, q: (q, c, 0, 0, 0)),
            pl.BlockSpec((1, length, size), lambda c, q: (c, 0, q)),
            pl.BlockSpec((1, 1, length, per_group), lambda c, q: (c, q, 0, 0)),
            pl.BlockSpec((1, length, wide), lambda c, q: (c, 0, q)),
        ],
        out_specs=pl.BlockSpec((1, length, wide), lambda c, q: (c, 0, q)),
        out_shape=jax.ShapeDtypeStruct((kids, length, columns), jnp.bfloat16),
        compiler_params=pltpu.CompilerParams(vmem_limit_bytes=4 * VMEM_LIMIT),
        cost_estimate=pl.CostEstimate(
            flops=2 * kids * length * columns * size,
            bytes_accessed=8 * kids * length * columns,
            transcendentals=0,
        ),
        name="carried",
    )(states, c_conv, grow, mixed)


def local_halves(
    x_in, b_in, c_in, dt_in, dt_bias, a_log, d_skip, conv_x, conv_bc,
    par_state, tail_x, tail_bc, counts, order,
):
    kids, length, columns = x_in.shape
    heads = dt_in.shape[1]
    width, size = par_state.shape[2:]
    groups = b_in.shape[2] // size
    per_group = heads // groups
    wide = per_group * width
    taps = conv_x.shape[0]
    reach = taps - 1
    lines = (wide + 2 * size) // 128
    tail_lines = -(-lines * reach // 16) * 16
    params = pltpu.CompilerParams(vmem_limit_bytes=VMEM_LIMIT)
    anywhere = pl.BlockSpec(memory_space=pl.ANY)
    small = pl.CostEstimate(flops=1, bytes_accessed=1, transcendentals=0)

    stay = lambda x: pltpu.with_memory_space_constraint(x, pltpu.HBM)
    keep_in_vmem = lambda x: pltpu.with_memory_space_constraint(x, pltpu.VMEM)
    x_in, b_in, c_in, dt_in, conv_x, conv_bc = map(stay, (x_in, b_in, c_in, dt_in, conv_x, conv_bc))

    me = lax.axis_index("batch")
    parent = parent_of(counts, order)
    child = (jnp.arange(4 * kids, dtype=jnp.int32) // kids ^ me) * kids
    child = child + jnp.arange(4 * kids, dtype=jnp.int32) % kids
    catalog = jnp.arange(4 * 2 * kids, dtype=jnp.int32)
    owner = jnp.sum(jnp.where(child[:, None] == catalog[None, :], parent[None, :], 0), axis=1)
    slots = owner ^ me
    place = (me % 4).astype(jnp.int32)[None]

    state = stay(par_state.reshape(groups, per_group, width, size))
    x_tails, bc_tails = stay(tail_x), stay(tail_bc.transpose(0, 2, 1, 3))
    offsets = [sum(SPLIT[:k]) for k in range(len(SPLIT))]

    def swap(value, r):
        return lax.ppermute(value, "batch", perm=[(i, i ^ r) for i in range(8)])

    def cast():
        rows = per_group * width + tail_lines
        rows_a = SPLIT[0] * width + tail_lines
        blocks = [(0, SPLIT[0])] + [(at, 2) for at in range(SPLIT[0], per_group, 2)]
        count = len(blocks) + 2

        def kernel(place_ref, *refs):
            ins, outs = refs[: 4 * count], refs[4 * count :]
            quarters = [outs[0], outs[2].at[0], outs[1], outs[2].at[1]]
            for n, out_ref in enumerate(quarters):
                cast_kernel(
                    len(blocks), [tail_lines], reach, lines, *ins[count * n : count * n + count], out_ref
                )
                outs[3 + n // 2][n % 2] = out_ref[:rows_a]

        operands, specs = [], []
        for n in range(4):
            for offset, part in blocks:
                operands.append(state)
                specs.append(
                    pl.BlockSpec(
                        (1, part, width, size),
                        lambda i, p, n=n, at=offset // part: (p[0] ^ n, at, 0, 0),
                    )
                )
            operands += [x_tails, bc_tails]
            specs += [
                pl.BlockSpec((1, reach, wide), lambda i, p, n=n: (0, 0, p[0] ^ n)),
                pl.BlockSpec((1, reach, 2, size), lambda i, p, n=n: (0, 0, 0, p[0] ^ n)),
            ]
        shapes = [(rows, size)] * 2 + [(2, rows, size)] + [(2, rows_a, size)] * 2
        return pl.pallas_call(
            kernel,
            grid_spec=pltpu.PrefetchScalarGridSpec(
                num_scalar_prefetch=1,
                grid=(1,),
                in_specs=specs,
                out_specs=[pl.BlockSpec(memory_space=pltpu.VMEM)] * len(shapes),
            ),
            out_shape=[pltpu.VMEM(shape, jnp.bfloat16) for shape in shapes],
            compiler_params=params,
            cost_estimate=small,
            name="cast_states",
        )(place, *operands)

    def rearrange(scalars, sources, moves, shapes, tokens, name):
        def kernel(scalars_ref, *refs):
            held, outs = refs[: len(sources)], refs[len(sources) :]
            for out, at, scalar, choices in moves:
                for value, (number, take) in enumerate(choices):

                    def copy(out=out, at=at, number=number, take=take):
                        rows = held[number][...] if take is None else held[number][take]
                        if at is None:
                            outs[out][...] = rows
                        else:
                            outs[out][at] = rows

                    if scalar is None:
                        copy()
                    else:
                        pl.when(scalars_ref[scalar] == value)(copy)

        return pl.pallas_call(
            functools.partial(drop_tokens, kernel, 1 + len(sources), len(tokens)),
            grid_spec=pltpu.PrefetchScalarGridSpec(
                num_scalar_prefetch=1,
                grid=(1,),
                in_specs=[pl.BlockSpec(memory_space=pltpu.VMEM)] * len(sources)
                + [anywhere] * len(tokens),
                out_specs=[pl.BlockSpec(memory_space=pltpu.VMEM)] * len(shapes),
            ),
            out_shape=[pltpu.VMEM(shape, jnp.bfloat16) for shape in shapes],
            compiler_params=params,
            cost_estimate=small,
            name=name,
        )(scalars, *map(keep_in_vmem, sources), *tokens)

    def pick(rows, sources, choices, tokens):
        moves = [
            (j, kid, j * kids + kid, choices) for j in range(4) for kid in range(kids)
        ]
        picked = rearrange(
            slots, sources, moves, [(kids, rows, size)] * 4, tokens, "pick_states"
        )
        return [picked[0]] + [swap(picked[j], j) for j in range(1, 4)]

    def early(c, pieces, piece, before, tokens):
        per = groups // pieces
        at = lambda q: (c, 0, per * piece + q)
        operands = [
            x_in, b_in, c_in, dt_in, dt_bias[:, None], a_log[:, None], skip_row, conv_x, conv_bc
        ]
        keep = len(operands)
        tokens = list(tokens) + [keep_in_vmem(a) for a in before]
        first = keep + len(tokens) - len(before)
        return pl.pallas_call(
            functools.partial(
                drop_tokens, functools.partial(early_kernel, per * piece), keep, len(tokens)
            ),
            grid=(per,),
            in_specs=[
                pl.BlockSpec((1, length, wide), at),
                pl.BlockSpec((1, length, size), at),
                pl.BlockSpec((1, length, size), at),
                pl.BlockSpec((1, per_group, length), lambda q: (c, per * piece + q, 0)),
                pl.BlockSpec((per_group, 1), lambda q: (per * piece + q, 0)),
                pl.BlockSpec((per_group, 1), lambda q: (per * piece + q, 0)),
                pl.BlockSpec((1, wide), lambda q: (0, per * piece + q)),
                pl.BlockSpec((taps, wide), lambda q: (0, per * piece + q)),
                pl.BlockSpec((2, taps, size), lambda q: (0, 0, per * piece + q)),
                *[anywhere] * len(tokens),
            ],
            out_specs=[pl.BlockSpec(memory_space=pltpu.VMEM)] * 6,
            out_shape=[
                pltpu.VMEM((groups, length, wide), jnp.float32),
                pltpu.VMEM((groups, length, size), jnp.bfloat16),
                pltpu.VMEM((groups, per_group, length), jnp.float32),
                pltpu.VMEM((groups, length, per_group * FIX), jnp.float32),
                pltpu.VMEM((groups, FIX, wide + 2 * size), jnp.bfloat16),
                pltpu.VMEM((groups, 8, wide + 2 * size), jnp.float32),
            ],
            input_output_aliases={first + i: i for i in range(len(before))},
            scratch_shapes=[pltpu.VMEM((2, 8 + length, size), jnp.float32)],
            compiler_params=params,
            cost_estimate=small,
            name="early",
        )(*operands, *tokens)

    def late(ks, states, parts, result, tokens):
        offset = offsets[ks[0]]
        chunk = sum(SPLIT[k] for k in ks) * width
        operands = [keep_in_vmem(a) for a in (*states[0], *sum((states[k] for k in ks), []), *parts[0], *parts[1])]
        specs = [pl.BlockSpec(memory_space=pltpu.VMEM)] * len(operands)
        keep = 1 + len(operands)
        operands += tokens
        specs += [anywhere] * len(tokens)
        alias = {}
        if result is not None:
            alias = {1 + len(operands): 0}
            operands.append(result)
            specs.append(anywhere)
        kernel = functools.partial(
            late_kernel, offset, [SPLIT[k] for k in ks], lines, reach, SPLIT[0] * width
        )
        return pl.pallas_call(
            functools.partial(drop_tokens, kernel, keep, 1 + len(operands) - keep),
            grid_spec=pltpu.PrefetchScalarGridSpec(
                num_scalar_prefetch=1,
                grid=(1,),
                in_specs=specs,
                out_specs=anywhere,
                scratch_shapes=[
                    pltpu.VMEM((groups, kids, 8 + FIX, max(chunk, 2 * size)), jnp.float32),
                    pltpu.VMEM((groups, kids, length, chunk), jnp.bfloat16),
                    pltpu.SemaphoreType.DMA((groups,)),
                ],
            ),
            out_shape=jax.ShapeDtypeStruct(x_in.shape, jnp.bfloat16),
            input_output_aliases=alias,
            compiler_params=params,
            cost_estimate=small,
            name="late",
        )(place, *operands)

    skip_row = jnp.repeat(d_skip, width)[None, :]
    rows = [SPLIT[0] * width + tail_lines] + [part * width for part in SPLIT[1:]]
    chunks = [pl.ds(sum(rows[:k]), rows[k]) for k in range(len(SPLIT))]
    own, own_2, own_13, sent_4, sent_6 = cast()
    crossed_a = [swap(sent_4, 4), swap(sent_6, 6)]
    along_y, along_z = swap(own_13, 1), swap(own_2, 2)
    parts = [early(0, 1, 0, [], [own, slots])]
    spare = sum(rows[1:])
    turn = rearrange(
        place,
        [along_y],
        [(0, None, None, [(0, (1, chunks[0]))]), (1, None, None, [(0, (1, pl.ds(rows[0], spare)))])],
        [(rows[0], size), (spare, size)],
        [parts[0][1]],
        "stack_turn",
    )
    inside = [own, along_y, along_z, swap(turn[0], 2), swap(turn[1], 2)]

    def inside_rows(k):
        last = (3, None) if k == 0 else (4, pl.ds(sum(rows[1:k]), rows[k]))
        return [(0, chunks[k]), (1, (0, chunks[k])), (2, chunks[k]), last]

    def cross(k, tokens):
        moves = [(0, j, None, [choice]) for j, choice in enumerate(inside_rows(k))]
        (sent,) = rearrange(place, inside, moves, [(4, rows[k], size)], tokens, "stack_later")
        return sent, swap(sent, 4)

    def pick_later(k, crossed, tokens):
        choices = inside_rows(k) + [(5, j) for j in range(4)]
        return pick(rows[k], [*inside, crossed], choices, tokens)

    moves = [(0, n, None, [(n, 1)]) for n in range(2)]
    (spread,) = rearrange(place, crossed_a, moves, [(2, rows[0], size)], [turn[0]], "stack_first")
    passed = swap(spread, 1)
    second = early(1, 2, 0, [], [spread])
    sent_b, crossed_b = cross(1, [second[1], passed])
    choices = inside_rows(0) + [(5, 0), (7, 0), (6, 0), (7, 1)]
    states = [pick(rows[0], [*inside, *crossed_a, passed], choices, [sent_b])]
    sent_c, crossed_c = cross(2, [states[0][0]])
    second = early(1, 2, 1, second, [sent_c])
    parts.append(second)
    states.append(pick_later(1, crossed_b, [second[1], *states[0]]))
    states.append(pick_later(2, crossed_c, [states[1][0]]))
    result = late([0, 1], states, parts, None, [states[2][0]])
    return late([2], states, parts, result, [])


def solution(mesh):
    rows, cols = P(("groups", "batch"), None, "head"), P(("groups", "batch"), "head")
    placed = (
        rows, rows, rows, cols, P("head"), P("head"), P("head"), P(None, "head"),
        P(None, None, "head"), cols, rows, P(("groups", "batch"), None, None, "head"),
        P("groups"), P("groups"),
    )
    local = local_halves if mesh.shape["batch"] == 8 else local_any
    return jax.shard_map(local, mesh=mesh, in_specs=placed, out_specs=rows, check_vma=False)
```

```python
import functools

import jax
import jax.numpy as jnp
from jax import lax
from jax.experimental import pallas as pl
from jax.experimental.pallas import tpu as pltpu
from jax.sharding import PartitionSpec as P

VMEM_LIMIT = 12 * 1024 * 1024
SPLIT = (8, 4, 4)
FIX = 16
LOG2_E = 1.4426950408889634


def drop_tokens(kernel, keep, tokens, *refs):
    kernel(*refs[:keep], *refs[keep + tokens :])


def parent_of(counts, order):
    index = jnp.arange(counts.shape[0], dtype=jnp.int32)
    bounds = jnp.sum(jnp.where(index[None, :] <= index[:, None], counts[None, :], 0), axis=1)
    return jnp.sum((bounds[None, :] <= order[:, None]).astype(jnp.int32), axis=1)


def three_terms(value):
    terms = []
    for _ in range(3):
        terms.append(value.astype(jnp.bfloat16).astype(jnp.float32))
        value = value - terms[-1]
    return jnp.concatenate(terms)


def conv_silu(padded, tail, rows, taps):
    length = rows.shape[0]
    reach = taps.shape[0] - 1
    padded[8 - reach : 8, :] = jnp.broadcast_to(tail, (reach, rows.shape[1])).astype(jnp.float32)
    padded[8 : 8 + length, :] = rows.astype(jnp.float32)
    total = padded[8 - reach : 8 - reach + length, :] * taps[0:1, :]
    for k in range(1, reach + 1):
        total = total + padded[8 - reach + k : 8 - reach + k + length, :] * taps[k : k + 1, :]
    half = 0.5 * total
    return (half + half * jnp.tanh(half)).astype(jnp.bfloat16)


def early_kernel(
    base, x_ref, b_ref, c_ref, dt_ref, bias_ref, alog_ref, skip_ref, taps_x_ref, taps_bc_ref,
    mixed_ref, c_out_ref, column_ref, first_ref, opening_ref, weights_ref, padded,
):
    length, wide = x_ref.shape[1:]
    heads = dt_ref.shape[1]
    q = base + pl.program_id(0)
    width = wide // heads
    half = length // 2

    def convolve(rows, taps, slot):
        bulk = conv_silu(padded.at[slot % 2], 0.0, rows, taps)[FIX:]
        return jnp.concatenate([jnp.zeros((FIX, rows.shape[1]), jnp.bfloat16), bulk])

    b_conv = convolve(b_ref[0], taps_bc_ref[0], 0)
    c_conv = convolve(c_ref[0], taps_bc_ref[1], 1)
    c_out_ref[q] = c_conv
    size = b_ref.shape[2]
    taps = taps_x_ref.shape[0]
    opening_ref[q, :, :wide] = x_ref[0, :FIX]
    opening_ref[q, :, wide : wide + size] = b_ref[0, :FIX]
    opening_ref[q, :, wide + size :] = c_ref[0, :FIX]
    weights_ref[q, :taps, :wide] = taps_x_ref[...]
    weights_ref[q, :taps, wide : wide + size] = taps_bc_ref[0]
    weights_ref[q, :taps, wide + size :] = taps_bc_ref[1]
    weights_ref[q, taps : taps + 1, :wide] = skip_ref[...]
    scores = lax.dot_general(
        c_conv, b_conv, (((1,), (1,)), ((), ())), preferred_element_type=jnp.float32
    )
    raw = dt_ref[0] + bias_ref[...]
    step = jnp.maximum(raw, 0.0) + jnp.log1p(jnp.exp(-jnp.abs(raw)))
    per_token = step * (-jnp.exp(alog_ref[...]))
    upper = lax.broadcasted_iota(jnp.int32, (length, length), 0) <= lax.broadcasted_iota(
        jnp.int32, (length, length), 1
    )
    sums = jnp.dot(
        three_terms(per_token).astype(jnp.bfloat16),
        upper.astype(jnp.float32).astype(jnp.bfloat16),
        preferred_element_type=jnp.float32,
    )
    total = (sums[:heads] + sums[heads : 2 * heads]) + sums[2 * heads :]
    total = total * LOG2_E
    row = total - jnp.log(step) * LOG2_E
    columns = total.T
    column_ref[q] = total
    causal = lax.broadcasted_iota(jnp.int32, (half, half), 0) >= lax.broadcasted_iota(
        jnp.int32, (half, half), 1
    )
    low = lax.broadcasted_iota(jnp.int32, (length, 2 * width), 1) < width
    for pair in range(heads // 2):
        lanes = slice(pair * 2 * width, (pair + 1) * 2 * width)
        x_conv = convolve(x_ref[0, :, lanes], taps_x_ref[:, lanes], pair)
        parts = []
        for head in (2 * pair, 2 * pair + 1):
            column = jnp.broadcast_to(columns[:, head : head + 1], (length, half))
            rows = row[head : head + 1, :]
            near = jnp.exp2(jnp.where(causal, column[:half] - rows[:, :half], -1e30))
            far = jnp.exp2(column[half:] - rows[:, :half])
            last = jnp.exp2(jnp.where(causal, column[half:] - rows[:, half:], -1e30))
            spot = slice(head * FIX, (head + 1) * FIX)
            first_ref[q, :half, spot] = near[:, :FIX]
            first_ref[q, half:, spot] = far[:, :FIX]
            top = (scores[:half, :half] * near).astype(jnp.bfloat16)
            left = (scores[half:, :half] * far).astype(jnp.bfloat16)
            right = (scores[half:, half:] * last).astype(jnp.bfloat16)
            below = jnp.concatenate([left, right], axis=1)
            parts.append(
                jnp.concatenate(
                    [
                        jnp.dot(top, x_conv[:half], preferred_element_type=jnp.float32),
                        jnp.dot(below, x_conv, preferred_element_type=jnp.float32),
                    ]
                )
            )
        mixed_ref[q, :, lanes] = jnp.where(low, parts[0], parts[1]) + skip_ref[
            :, lanes
        ] * x_conv.astype(jnp.float32)


def late_kernel(places, offset, heads, lines, reach, tail_at, place_ref, *refs):
    count = len(heads)
    tails, states, parts = refs[:4], refs[4 : 4 + 4 * count], refs[4 + 4 * count : -4]
    y_ref, padded, y_part, sems = refs[-4:]
    _, kids, length, wide = y_part.shape
    rows, heads = heads, sum(heads)
    width = wide // heads
    rows = [part * width for part in rows]
    low_first = lax.broadcasted_iota(jnp.int32, (FIX, 2 * width), 1) < width
    contract = (((1,), (1,)), ((), ()))

    def add(j, kid):
        q = place_ref[0] ^ j
        mixed_ref, held_ref, column_ref, first_ref, opening_ref, weights_ref = parts[
            6 * kid : 6 * kid + 6
        ]
        size = held_ref.shape[2]
        per_group = column_ref.shape[1]
        group_wide = opening_ref.shape[2] - 2 * size
        tail_rows = pl.ds(tail_at, -(-lines * reach // 16) * 16)
        tail = tails[places[0].index(j)][kid, tail_rows].astype(jnp.float32)
        blocks = [states[4 * n + places[1 + n].index(j)] for n in range(count)]
        state = jnp.concatenate([ref[kid, : rows[n]] for n, ref in enumerate(blocks)])

        def opening(start, stop, at):
            tap_rows = []
            for k in range(reach):
                first = k * lines + at
                count = (stop - start) // 128
                here = [tail[first + n : first + n + 1] for n in range(count)]
                tap_rows.append(jnp.concatenate(here, axis=1))
            return conv_silu(
                padded.at[j, kid, :, : stop - start],
                jnp.concatenate(tap_rows),
                opening_ref[q, :, start:stop],
                weights_ref[q, : reach + 1, start:stop],
            )

        bc_first = opening(group_wide, group_wide + 2 * size, lines - 2)
        b_first, c_first = bc_first[:, :size], bc_first[:, size:]
        start = offset * width
        x_all = opening(start, start + wide, start // 128).astype(jnp.float32)
        skipped = weights_ref[q, reach + 1 : reach + 2, start : start + wide] * x_all
        c_conv = jnp.concatenate([c_first, held_ref[q, FIX:]])
        terms = three_terms(jnp.exp2(column_ref[q]))
        terms = jnp.concatenate([terms, jnp.zeros((per_group, length), jnp.float32)])
        spread_row = lax.broadcasted_iota(jnp.int32, (4 * per_group, wide), 0)
        spread_lane = lax.broadcasted_iota(jnp.int32, (4 * per_group, wide), 1)
        spread = spread_row % per_group == offset + spread_lane // width
        grow = jnp.dot(
            terms.T.astype(jnp.bfloat16),
            spread.astype(jnp.float32).astype(jnp.bfloat16),
            preferred_element_type=jnp.float32,
        )
        term = lax.dot_general(c_conv, state, contract, preferred_element_type=jnp.float32)
        carried = (term * grow).astype(jnp.bfloat16)
        scores = lax.dot_general(
            c_conv,
            jnp.concatenate([b_first] * heads),
            contract,
            preferred_element_type=jnp.float32,
        )
        here = slice(offset * FIX, (offset + heads) * FIX)
        mixing = (scores * first_ref[q, :, here]).astype(jnp.bfloat16)
        for pair in range(heads // 2):
            lanes = slice(pair * 2 * width, (pair + 1) * 2 * width)
            x_first = x_all[:, lanes]
            stacked = [jnp.where(low_first, x_first, 0.0), jnp.where(low_first, 0.0, x_first)]
            if pair > 0:
                stacked = [jnp.zeros((2 * pair * FIX, 2 * width), jnp.float32)] + stacked
            if 2 * pair + 2 < heads:
                spare = (heads - 2 * pair - 2) * FIX
                stacked = stacked + [jnp.zeros((spare, 2 * width), jnp.float32)]
            part = jnp.dot(
                mixing,
                jnp.concatenate(stacked).astype(jnp.bfloat16),
                preferred_element_type=jnp.float32,
            )
            part = jnp.concatenate([part[:FIX] + skipped[:, lanes], part[FIX:]])
            whole = slice(start + lanes.start, start + lanes.stop)
            y_part[j, kid, :, lanes] = (
                mixed_ref[q, :, whole] + part + carried[:, lanes].astype(jnp.float32)
            ).astype(jnp.bfloat16)

    copies = []
    for j in range(4):
        for kid in range(kids):
            add(j, kid)
        start = (place_ref[0] ^ j) * (y_ref.shape[2] // 4) + offset * width
        lanes = pl.ds(pl.multiple_of(start, 128), wide)
        copies.append(pltpu.make_async_copy(y_part.at[j], y_ref.at[:, :, lanes], sems.at[j]))
        copies[-1].start()
    for copy in copies:
        copy.wait()


def cast_kernel(parts, tailed, reach, lines, *refs):
    count = len(tailed)
    ins, outs = refs[:-count], refs[-count:]
    states, tails = ins[: parts * count], ins[parts * count :]
    for j, out_ref in enumerate(outs):
        start = 0
        for at in range(parts):
            state = states[parts * j + at][0]
            rows = state.shape[0] * state.shape[1]
            out_ref[start : start + rows] = state.reshape(rows, state.shape[2]).astype(jnp.bfloat16)
            start += rows
            if at == 0 and tailed[j]:
                x_tail = tails[2 * j][0].astype(jnp.float32)
                bc_tail = tails[2 * j + 1][0].astype(jnp.float32)
                pieces = []
                for k in range(reach):
                    pieces += [x_tail[k : k + 1, i * 128 : i * 128 + 128] for i in range(lines - 2)]
                    pieces.append(bc_tail[k])
                spare = tailed[j] - lines * reach
                pieces.append(jnp.zeros((spare, 128), jnp.float32))
                out_ref[start : start + tailed[j]] = jnp.concatenate(pieces).astype(jnp.bfloat16)
                start += tailed[j]


def within_kernel(
    parent_ref,
    x_ref,
    b_ref,
    c_ref,
    dt_ref,
    bias_ref,
    alog_ref,
    skip_ref,
    taps_x_ref,
    taps_bc_ref,
    tail_x_ref,
    tail_bc_ref,
    mixed_ref,
    c_out_ref,
    grow_ref,
    padded,
):
    length = x_ref.shape[1]
    heads = dt_ref.shape[1]
    width = x_ref.shape[2] // heads
    b_conv = conv_silu(padded, tail_bc_ref[0, 0], b_ref[0], taps_bc_ref[0])
    c_conv = conv_silu(padded, tail_bc_ref[0, 1], c_ref[0], taps_bc_ref[1])
    c_out_ref[0] = c_conv
    scores = lax.dot_general(
        c_conv, b_conv, (((1,), (1,)), ((), ())), preferred_element_type=jnp.float32
    )
    raw = dt_ref[0] + bias_ref[...]
    step = jnp.maximum(raw, 0.0) + jnp.log1p(jnp.exp(-jnp.abs(raw)))
    per_token = step * (-jnp.exp(alog_ref[...]))
    row = lax.broadcasted_iota(jnp.int32, (length, length), 0)
    col = lax.broadcasted_iota(jnp.int32, (length, length), 1)
    upper = (row <= col).astype(jnp.float32)
    total = lax.dot_general(
        per_token,
        upper,
        (((1,), (0,)), ((), ())),
        precision=lax.Precision.HIGHEST,
        preferred_element_type=jnp.float32,
    )
    total_t = total.T
    grow_ref[0, 0] = jnp.exp(total_t)
    causal = row >= col
    low = lax.broadcasted_iota(jnp.int32, (length, 2 * width), 1) < width
    for pair in range(heads // 2):
        lanes = slice(pair * 2 * width, (pair + 1) * 2 * width)
        x_conv = conv_silu(
            padded, tail_x_ref[0, :, lanes], x_ref[0, :, lanes], taps_x_ref[:, lanes]
        )
        parts = []
        for head in (2 * pair, 2 * pair + 1):
            gap = total_t[:, head : head + 1] - total[head : head + 1, :]
            factor = jnp.exp(jnp.where(causal, gap, -1e30))
            mixing = (scores * factor * step[head : head + 1, :]).astype(jnp.bfloat16)
            parts.append(jnp.dot(mixing, x_conv, preferred_element_type=jnp.float32))
        mixed_ref[0, :, lanes] = (
            jnp.where(low, parts[0], parts[1]) + skip_ref[:, lanes] * x_conv.astype(jnp.float32)
        )


def carried_kernel(state_ref, c_ref, grow_ref, mixed_ref, y_ref):
    sources, _, part, width, size = state_ref.shape
    length = c_ref.shape[1]
    low = lax.broadcasted_iota(jnp.int32, (length, 2 * width), 1) < width
    c_conv = c_ref[0]
    for source in range(sources):
        state = state_ref[source, 0].reshape(part * width, size)
        term = lax.dot_general(
            c_conv, state, (((1,), (1,)), ((), ())), preferred_element_type=jnp.float32
        )
        for pair in range(part // 2):
            head = source * part + 2 * pair
            grow = jnp.where(
                low, grow_ref[0, 0, :, head : head + 1], grow_ref[0, 0, :, head + 1 : head + 2]
            )
            here = slice(2 * pair * width, (2 * pair + 2) * width)
            lanes = slice(head * width, (head + 2) * width)
            carried = (term[:, here] * grow).astype(jnp.bfloat16).astype(jnp.float32)
            y_ref[0, :, lanes] = (mixed_ref[0, :, lanes] + carried).astype(jnp.bfloat16)


def pick_kernel(parent_ref, state_ref, out_ref):
    out_ref[...] = state_ref[...]


def local_any(
    x_in,
    b_in,
    c_in,
    dt_in,
    dt_bias,
    a_log,
    d_skip,
    conv_x,
    conv_bc,
    par_state,
    tail_x,
    tail_bc,
    counts,
    order,
):
    kids, length, columns = x_in.shape
    heads = dt_in.shape[1]
    width, size = par_state.shape[2:]
    ways = lax.axis_size("batch")
    groups = b_in.shape[2] // size
    per_group = heads // groups
    part = heads // ways
    wide = per_group * width
    reach = tail_x.shape[1]
    parents_all = counts.shape[0]
    kids_all = order.shape[0]

    parent = parent_of(counts, order)
    own = lax.dynamic_slice_in_dim(parent, lax.axis_index("batch") * kids, kids)

    sent = par_state.astype(jnp.bfloat16).reshape(ways, part, width, size)
    shares = lax.all_to_all(sent, "batch", split_axis=0, concat_axis=0, tiled=True)

    tails = jnp.concatenate([tail_x.reshape(-1), tail_bc.reshape(-1)])
    tails = jnp.broadcast_to(tails[None], (ways, tails.shape[0]))
    tails = lax.all_to_all(tails, "batch", split_axis=0, concat_axis=0, tiled=True)
    tails_x = tails[:, : reach * columns].reshape(parents_all, reach, columns)
    tails_bc = tails[:, reach * columns :].reshape(parents_all, 2, reach, groups * size)

    picked = pl.pallas_call(
        pick_kernel,
        grid_spec=pltpu.PrefetchScalarGridSpec(
            num_scalar_prefetch=1,
            grid=(kids_all,),
            in_specs=[pl.BlockSpec((1, part, width, size), lambda i, p: (p[i], 0, 0, 0))],
            out_specs=pl.BlockSpec((1, part, width, size), lambda i, p: (i, 0, 0, 0)),
        ),
        out_shape=jax.ShapeDtypeStruct((kids_all, part, width, size), jnp.bfloat16),
        cost_estimate=pl.CostEstimate(
            flops=0, bytes_accessed=4 * kids_all * part * width * size, transcendentals=0
        ),
        name="pick_states",
    )(parent, shares)
    states = lax.all_to_all(
        picked.reshape(ways, kids, part, width, size), "batch", split_axis=0, concat_axis=0, tiled=True
    )

    skip_row = jnp.repeat(d_skip, width)[None, :]
    mixed, c_conv, grow = pl.pallas_call(
        within_kernel,
        grid_spec=pltpu.PrefetchScalarGridSpec(
            num_scalar_prefetch=1,
            grid=(kids, groups),
            in_specs=[
                pl.BlockSpec((1, length, wide), lambda c, q, p: (c, 0, q)),
                pl.BlockSpec((1, length, size), lambda c, q, p: (c, 0, q)),
                pl.BlockSpec((1, length, size), lambda c, q, p: (c, 0, q)),
                pl.BlockSpec((1, per_group, length), lambda c, q, p: (c, q, 0)),
                pl.BlockSpec((per_group, 1), lambda c, q, p: (q, 0)),
                pl.BlockSpec((per_group, 1), lambda c, q, p: (q, 0)),
                pl.BlockSpec((1, wide), lambda c, q, p: (0, q)),
                pl.BlockSpec((reach + 1, wide), lambda c, q, p: (0, q)),
                pl.BlockSpec((2, reach + 1, size), lambda c, q, p: (0, 0, q)),
                pl.BlockSpec((1, reach, wide), lambda c, q, p: (p[c], 0, q)),
                pl.BlockSpec((1, 2, reach, size), lambda c, q, p: (p[c], 0, 0, q)),
            ],
            out_specs=[
                pl.BlockSpec((1, length, wide), lambda c, q, p: (c, 0, q)),
                pl.BlockSpec((1, length, size), lambda c, q, p: (c, 0, q)),
                pl.BlockSpec((1, 1, length, per_group), lambda c, q, p: (c, q, 0, 0)),
            ],
            scratch_shapes=[pltpu.VMEM((8 + length, size), jnp.float32)],
        ),
        out_shape=[
            jax.ShapeDtypeStruct((kids, length, columns), jnp.float32),
            jax.ShapeDtypeStruct((kids, length, groups * size), jnp.bfloat16),
            jax.ShapeDtypeStruct((kids, groups, length, per_group), jnp.float32),
        ],
        compiler_params=pltpu.CompilerParams(vmem_limit_bytes=4 * VMEM_LIMIT),
        cost_estimate=pl.CostEstimate(
            flops=4 * kids * heads * length * length * width,
            bytes_accessed=6 * kids * length * columns,
            transcendentals=kids * heads * length * length,
        ),
        name="within",
    )(
        own,
        x_in,
        b_in,
        c_in,
        dt_in,
        dt_bias[:, None],
        a_log[:, None],
        skip_row,
        conv_x,
        conv_bc,
        tails_x,
        tails_bc,
    )

    sources = per_group // part
    return pl.pallas_call(
        carried_kernel,
        grid=(kids, groups),
        in_specs=[
            pl.BlockSpec((sources, 1, part, width, size), lambda c, q: (q, c, 0, 0, 0)),
            pl.BlockSpec((1, length, size), lambda c, q: (c, 0, q)),
            pl.BlockSpec((1, 1, length, per_group), lambda c, q: (c, q, 0, 0)),
            pl.BlockSpec((1, length, wide), lambda c, q: (c, 0, q)),
        ],
        out_specs=pl.BlockSpec((1, length, wide), lambda c, q: (c, 0, q)),
        out_shape=jax.ShapeDtypeStruct((kids, length, columns), jnp.bfloat16),
        compiler_params=pltpu.CompilerParams(vmem_limit_bytes=4 * VMEM_LIMIT),
        cost_estimate=pl.CostEstimate(
            flops=2 * kids * length * columns * size,
            bytes_accessed=8 * kids * length * columns,
            transcendentals=0,
        ),
        name="carried",
    )(states, c_conv, grow, mixed)


def local_halves(
    x_in, b_in, c_in, dt_in, dt_bias, a_log, d_skip, conv_x, conv_bc,
    par_state, tail_x, tail_bc, counts, order,
):
    kids, length, columns = x_in.shape
    heads = dt_in.shape[1]
    width, size = par_state.shape[2:]
    groups = b_in.shape[2] // size
    per_group = heads // groups
    wide = per_group * width
    taps = conv_x.shape[0]
    reach = taps - 1
    lines = (wide + 2 * size) // 128
    tail_lines = -(-lines * reach // 16) * 16
    params = pltpu.CompilerParams(vmem_limit_bytes=VMEM_LIMIT)
    anywhere = pl.BlockSpec(memory_space=pl.ANY)
    small = pl.CostEstimate(flops=1, bytes_accessed=1, transcendentals=0)

    stay = lambda x: pltpu.with_memory_space_constraint(x, pltpu.HBM)
    keep_in_vmem = lambda x: pltpu.with_memory_space_constraint(x, pltpu.VMEM)
    x_in, b_in, c_in, dt_in, conv_x, conv_bc = map(stay, (x_in, b_in, c_in, dt_in, conv_x, conv_bc))

    me = lax.axis_index("batch")
    parent = parent_of(counts, order)
    child = (jnp.arange(4 * kids, dtype=jnp.int32) // kids ^ me) * kids
    child = child + jnp.arange(4 * kids, dtype=jnp.int32) % kids
    catalog = jnp.arange(4 * 2 * kids, dtype=jnp.int32)
    owner = jnp.sum(jnp.where(child[:, None] == catalog[None, :], parent[None, :], 0), axis=1)
    slots = owner ^ me
    place = (me % 4).astype(jnp.int32)[None]

    state = stay(par_state.reshape(groups, per_group, width, size))
    x_tails, bc_tails = stay(tail_x), stay(tail_bc.transpose(0, 2, 1, 3))
    offsets = [sum(SPLIT[:k]) for k in range(len(SPLIT))]

    def swap(value, r):
        return lax.ppermute(value, "batch", perm=[(i, i ^ r) for i in range(8)])

    def cast():
        rows = per_group * width + tail_lines
        rows_a = SPLIT[0] * width + tail_lines
        blocks = [(0, SPLIT[0])] + [(at, 4) for at in range(SPLIT[0], per_group, 4)]
        count = len(blocks) + 2

        def kernel(place_ref, *refs):
            ins, outs = refs[: 4 * count], refs[4 * count :]
            quarters = [outs[0], outs[2].at[0], outs[1], outs[2].at[1]]
            for n, out_ref in enumerate(quarters):
                cast_kernel(
                    len(blocks), [tail_lines], reach, lines, *ins[count * n : count * n + count], out_ref
                )
                outs[3 + n // 2][n % 2] = out_ref[:rows_a]

        operands, specs = [], []
        for n in range(4):
            for offset, part in blocks:
                operands.append(state)
                specs.append(
                    pl.BlockSpec(
                        (1, part, width, size),
                        lambda i, p, n=n, at=offset // part: (p[0] ^ n, at, 0, 0),
                    )
                )
            operands += [x_tails, bc_tails]
            specs += [
                pl.BlockSpec((1, reach, wide), lambda i, p, n=n: (0, 0, p[0] ^ n)),
                pl.BlockSpec((1, reach, 2, size), lambda i, p, n=n: (0, 0, 0, p[0] ^ n)),
            ]
        shapes = [(rows, size)] * 2 + [(2, rows, size)] + [(2, rows_a, size)] * 2
        return pl.pallas_call(
            kernel,
            grid_spec=pltpu.PrefetchScalarGridSpec(
                num_scalar_prefetch=1,
                grid=(1,),
                in_specs=specs,
                out_specs=[pl.BlockSpec(memory_space=pltpu.VMEM)] * len(shapes),
            ),
            out_shape=[pltpu.VMEM(shape, jnp.bfloat16) for shape in shapes],
            compiler_params=params,
            cost_estimate=small,
            name="cast_states",
        )(place, *operands)

    def rearrange(scalars, sources, moves, shapes, tokens, name):
        def kernel(scalars_ref, *refs):
            held, outs = refs[: len(sources)], refs[len(sources) :]
            for out, at, scalar, choices in moves:
                for value, (number, take) in enumerate(choices):

                    def copy(out=out, at=at, number=number, take=take):
                        rows = held[number][...] if take is None else held[number][take]
                        if at is None:
                            outs[out][...] = rows
                        else:
                            outs[out][at] = rows

                    if scalar is None:
                        copy()
                    else:
                        pl.when(scalars_ref[scalar] == value)(copy)

        return pl.pallas_call(
            functools.partial(drop_tokens, kernel, 1 + len(sources), len(tokens)),
            grid_spec=pltpu.PrefetchScalarGridSpec(
                num_scalar_prefetch=1,
                grid=(1,),
                in_specs=[pl.BlockSpec(memory_space=pltpu.VMEM)] * len(sources)
                + [anywhere] * len(tokens),
                out_specs=[pl.BlockSpec(memory_space=pltpu.VMEM)] * len(shapes),
            ),
            out_shape=[pltpu.VMEM(shape, jnp.bfloat16) for shape in shapes],
            compiler_params=params,
            cost_estimate=small,
            name=name,
        )(scalars, *map(keep_in_vmem, sources), *tokens)

    def pick(rows, sources, choices, tokens, order=(1, 2, 3)):
        moves = [
            (j, kid, j * kids + kid, choices) for j in range(4) for kid in range(kids)
        ]
        picked = rearrange(
            slots, sources, moves, [(kids, rows, size)] * 4, tokens, "pick_states"
        )
        return [(0, picked[0])] + [(j, swap(picked[j], j)) for j in order]

    def early(c, pieces, piece, before, tokens):
        per = groups // pieces
        at = lambda q: (c, 0, per * piece + q)
        operands = [
            x_in, b_in, c_in, dt_in, dt_bias[:, None], a_log[:, None], skip_row, conv_x, conv_bc
        ]
        keep = len(operands)
        tokens = list(tokens) + [keep_in_vmem(a) for a in before]
        first = keep + len(tokens) - len(before)
        return pl.pallas_call(
            functools.partial(
                drop_tokens, functools.partial(early_kernel, per * piece), keep, len(tokens)
            ),
            grid=(per,),
            in_specs=[
                pl.BlockSpec((1, length, wide), at),
                pl.BlockSpec((1, length, size), at),
                pl.BlockSpec((1, length, size), at),
                pl.BlockSpec((1, per_group, length), lambda q: (c, per * piece + q, 0)),
                pl.BlockSpec((per_group, 1), lambda q: (per * piece + q, 0)),
                pl.BlockSpec((per_group, 1), lambda q: (per * piece + q, 0)),
                pl.BlockSpec((1, wide), lambda q: (0, per * piece + q)),
                pl.BlockSpec((taps, wide), lambda q: (0, per * piece + q)),
                pl.BlockSpec((2, taps, size), lambda q: (0, 0, per * piece + q)),
                *[anywhere] * len(tokens),
            ],
            out_specs=[pl.BlockSpec(memory_space=pltpu.VMEM)] * 6,
            out_shape=[
                pltpu.VMEM((groups, length, wide), jnp.float32),
                pltpu.VMEM((groups, length, size), jnp.bfloat16),
                pltpu.VMEM((groups, per_group, length), jnp.float32),
                pltpu.VMEM((groups, length, per_group * FIX), jnp.float32),
                pltpu.VMEM((groups, FIX, wide + 2 * size), jnp.bfloat16),
                pltpu.VMEM((groups, 8, wide + 2 * size), jnp.float32),
            ],
            input_output_aliases={first + i: i for i in range(len(before))},
            scratch_shapes=[pltpu.VMEM((2, 8 + length, size), jnp.float32)],
            compiler_params=params,
            cost_estimate=small,
            name="early",
        )(*operands, *tokens)

    def late(ks, states, parts, result, tokens):
        offset = offsets[ks[0]]
        chunk = sum(SPLIT[k] for k in ks) * width
        places = [[j for j, _ in chunk_states] for chunk_states in states]
        held = [array for chunk_states in states for _, array in chunk_states]
        operands = [keep_in_vmem(a) for a in (*held[:4], *sum((held[4 * k : 4 * k + 4] for k in ks), []), *parts[0], *parts[1])]
        specs = [pl.BlockSpec(memory_space=pltpu.VMEM)] * len(operands)
        keep = 1 + len(operands)
        operands += tokens
        specs += [anywhere] * len(tokens)
        alias = {}
        if result is not None:
            alias = {1 + len(operands): 0}
            operands.append(result)
            specs.append(anywhere)
        kernel = functools.partial(
            late_kernel, [places[0]] + [places[k] for k in ks], offset, [SPLIT[k] for k in ks], lines, reach, SPLIT[0] * width
        )
        return pl.pallas_call(
            functools.partial(drop_tokens, kernel, keep, 1 + len(operands) - keep),
            grid_spec=pltpu.PrefetchScalarGridSpec(
                num_scalar_prefetch=1,
                grid=(1,),
                in_specs=specs,
                out_specs=anywhere,
                scratch_shapes=[
                    pltpu.VMEM((groups, kids, 8 + FIX, max(chunk, 2 * size)), jnp.float32),
                    pltpu.VMEM((groups, kids, length, chunk), jnp.bfloat16),
                    pltpu.SemaphoreType.DMA((groups,)),
                ],
            ),
            out_shape=jax.ShapeDtypeStruct(x_in.shape, jnp.bfloat16),
            input_output_aliases=alias,
            compiler_params=params,
            cost_estimate=small,
            name="late",
        )(place, *operands)

    skip_row = jnp.repeat(d_skip, width)[None, :]
    rows = [SPLIT[0] * width + tail_lines] + [part * width for part in SPLIT[1:]]
    chunks = [pl.ds(sum(rows[:k]), rows[k]) for k in range(len(SPLIT))]
    own, own_2, own_13, sent_4, sent_6 = cast()
    crossed_a = [swap(sent_4, 4), swap(sent_6, 6)]
    along_y, along_z = swap(own_13, 1), swap(own_2, 2)
    parts = [early(0, 1, 0, [], [own, slots])]
    (turn,) = rearrange(
        place, [along_y], [(0, None, None, [(0, 1)])], [own.shape], [parts[0][1]], "stack_turn"
    )
    inside = [own, along_y, along_z, swap(turn, 2)]

    def inside_rows(k):
        return [(0, chunks[k]), (1, (0, chunks[k])), (2, chunks[k]), (3, chunks[k])]

    def cross(k, tokens):
        moves = [(0, j, None, [choice]) for j, choice in enumerate(inside_rows(k))]
        (sent,) = rearrange(place, inside, moves, [(4, rows[k], size)], tokens, "stack_later")
        return sent, swap(sent, 4)

    def pick_later(k, crossed, tokens):
        choices = inside_rows(k) + [(4, j) for j in range(4)]
        return pick(rows[k], [*inside, crossed], choices, tokens, (3, 2, 1))

    second = early(1, 2, 0, [], [turn])
    moves = [(0, n, None, [(n, 1)]) for n in range(2)]
    (spread,) = rearrange(
        place, crossed_a, moves, [(2, rows[0], size)], [second[1]], "stack_first"
    )
    passed = swap(spread, 1)
    sent_b, crossed_b = cross(1, [spread])
    second = early(1, 2, 1, second, [sent_b])
    parts.append(second)
    choices = inside_rows(0) + [(4, 0), (6, 0), (5, 0), (6, 1)]
    states = [pick(rows[0], [*inside, *crossed_a, passed], choices, [second[1]])]
    sent_c, crossed_c = cross(2, [states[0][0][1], crossed_b])
    states.append(pick_later(1, crossed_b, [sent_c]))
    states.append(pick_later(2, crossed_c, [states[1][0][1]]))
    result = late([0, 1], states, parts, None, [states[2][0][1]])
    return late([2], states, parts, result, [])


def solution(mesh):
    rows, cols = P(("groups", "batch"), None, "head"), P(("groups", "batch"), "head")
    placed = (
        rows, rows, rows, cols, P("head"), P("head"), P("head"), P(None, "head"),
        P(None, None, "head"), cols, rows, P(("groups", "batch"), None, None, "head"),
        P("groups"), P("groups"),
    )
    local = local_halves if mesh.shape["batch"] == 8 else local_any
    return jax.shard_map(local, mesh=mesh, in_specs=placed, out_specs=rows, check_vma=False)
```

```python
import functools

import jax
import jax.numpy as jnp
from jax import lax
from jax.experimental import pallas as pl
from jax.experimental.pallas import tpu as pltpu
from jax.sharding import PartitionSpec as P

VMEM_LIMIT = 12 * 1024 * 1024
SPLIT = (8, 8)
FIX = 16
LOG2_E = 1.4426950408889634


def drop_tokens(kernel, keep, tokens, *refs):
    kernel(*refs[:keep], *refs[keep + tokens :])


def parent_of(counts, order):
    index = jnp.arange(counts.shape[0], dtype=jnp.int32)
    bounds = jnp.sum(jnp.where(index[None, :] <= index[:, None], counts[None, :], 0), axis=1)
    return jnp.sum((bounds[None, :] <= order[:, None]).astype(jnp.int32), axis=1)


def three_terms(value):
    terms = []
    for _ in range(3):
        terms.append(value.astype(jnp.bfloat16).astype(jnp.float32))
        value = value - terms[-1]
    return jnp.concatenate(terms)


def conv_silu(padded, tail, rows, taps):
    length = rows.shape[0]
    reach = taps.shape[0] - 1
    padded[8 - reach : 8, :] = jnp.broadcast_to(tail, (reach, rows.shape[1])).astype(jnp.float32)
    padded[8 : 8 + length, :] = rows.astype(jnp.float32)
    total = padded[8 - reach : 8 - reach + length, :] * taps[0:1, :]
    for k in range(1, reach + 1):
        total = total + padded[8 - reach + k : 8 - reach + k + length, :] * taps[k : k + 1, :]
    half = 0.5 * total
    return (half + half * jnp.tanh(half)).astype(jnp.bfloat16)


def early_kernel(
    base, x_ref, b_ref, c_ref, dt_ref, bias_ref, alog_ref, skip_ref, taps_x_ref, taps_bc_ref,
    mixed_ref, c_out_ref, column_ref, first_ref, opening_ref, weights_ref, padded,
):
    length, wide = x_ref.shape[1:]
    heads = dt_ref.shape[1]
    q = base + pl.program_id(0)
    width = wide // heads
    half = length // 2

    def convolve(rows, taps, slot):
        bulk = conv_silu(padded.at[slot % 2], 0.0, rows, taps)[FIX:]
        return jnp.concatenate([jnp.zeros((FIX, rows.shape[1]), jnp.bfloat16), bulk])

    b_conv = convolve(b_ref[0], taps_bc_ref[0], 0)
    c_conv = convolve(c_ref[0], taps_bc_ref[1], 1)
    c_out_ref[q] = c_conv
    size = b_ref.shape[2]
    taps = taps_x_ref.shape[0]
    opening_ref[q, :, :wide] = x_ref[0, :FIX]
    opening_ref[q, :, wide : wide + size] = b_ref[0, :FIX]
    opening_ref[q, :, wide + size :] = c_ref[0, :FIX]
    weights_ref[q, :taps, :wide] = taps_x_ref[...]
    weights_ref[q, :taps, wide : wide + size] = taps_bc_ref[0]
    weights_ref[q, :taps, wide + size :] = taps_bc_ref[1]
    weights_ref[q, taps : taps + 1, :wide] = skip_ref[...]
    scores = lax.dot_general(
        c_conv, b_conv, (((1,), (1,)), ((), ())), preferred_element_type=jnp.float32
    )
    raw = dt_ref[0] + bias_ref[...]
    step = jnp.maximum(raw, 0.0) + jnp.log1p(jnp.exp(-jnp.abs(raw)))
    per_token = step * (-jnp.exp(alog_ref[...]))
    upper = lax.broadcasted_iota(jnp.int32, (length, length), 0) <= lax.broadcasted_iota(
        jnp.int32, (length, length), 1
    )
    sums = jnp.dot(
        three_terms(per_token).astype(jnp.bfloat16),
        upper.astype(jnp.float32).astype(jnp.bfloat16),
        preferred_element_type=jnp.float32,
    )
    total = (sums[:heads] + sums[heads : 2 * heads]) + sums[2 * heads :]
    total = total * LOG2_E
    row = total - jnp.log(step) * LOG2_E
    columns = total.T
    column_ref[q] = total
    causal = lax.broadcasted_iota(jnp.int32, (half, half), 0) >= lax.broadcasted_iota(
        jnp.int32, (half, half), 1
    )
    low = lax.broadcasted_iota(jnp.int32, (length, 2 * width), 1) < width
    for pair in range(heads // 2):
        lanes = slice(pair * 2 * width, (pair + 1) * 2 * width)
        x_conv = convolve(x_ref[0, :, lanes], taps_x_ref[:, lanes], pair)
        parts = []
        for head in (2 * pair, 2 * pair + 1):
            column = jnp.broadcast_to(columns[:, head : head + 1], (length, half))
            rows = row[head : head + 1, :]
            near = jnp.exp2(jnp.where(causal, column[:half] - rows[:, :half], -1e30))
            far = jnp.exp2(column[half:] - rows[:, :half])
            last = jnp.exp2(jnp.where(causal, column[half:] - rows[:, half:], -1e30))
            spot = slice(head * FIX, (head + 1) * FIX)
            first_ref[q, :half, spot] = near[:, :FIX]
            first_ref[q, half:, spot] = far[:, :FIX]
            top = (scores[:half, :half] * near).astype(jnp.bfloat16)
            left = (scores[half:, :half] * far).astype(jnp.bfloat16)
            right = (scores[half:, half:] * last).astype(jnp.bfloat16)
            below = jnp.concatenate([left, right], axis=1)
            parts.append(
                jnp.concatenate(
                    [
                        jnp.dot(top, x_conv[:half], preferred_element_type=jnp.float32),
                        jnp.dot(below, x_conv, preferred_element_type=jnp.float32),
                    ]
                )
            )
        mixed_ref[q, :, lanes] = jnp.where(low, parts[0], parts[1]) + skip_ref[
            :, lanes
        ] * x_conv.astype(jnp.float32)


def late_kernel(places, offset, heads, lines, reach, tail_at, place_ref, *refs):
    count = len(heads)
    tails, states, parts = refs[:4], refs[4 : 4 + 4 * count], refs[4 + 4 * count : -4]
    y_ref, padded, y_part, sems = refs[-4:]
    _, kids, length, wide = y_part.shape
    rows, heads = heads, sum(heads)
    width = wide // heads
    rows = [part * width for part in rows]
    low_first = lax.broadcasted_iota(jnp.int32, (FIX, 2 * width), 1) < width
    contract = (((1,), (1,)), ((), ()))

    def add(j, kid):
        q = place_ref[0] ^ j
        mixed_ref, held_ref, column_ref, first_ref, opening_ref, weights_ref = parts[
            6 * kid : 6 * kid + 6
        ]
        size = held_ref.shape[2]
        per_group = column_ref.shape[1]
        group_wide = opening_ref.shape[2] - 2 * size
        tail_rows = pl.ds(tail_at, -(-lines * reach // 16) * 16)
        tail = tails[places[0].index(j)][kid, tail_rows].astype(jnp.float32)
        blocks = [states[4 * n + places[1 + n].index(j)] for n in range(count)]
        state = jnp.concatenate([ref[kid, : rows[n]] for n, ref in enumerate(blocks)])

        def opening(start, stop, at):
            tap_rows = []
            for k in range(reach):
                first = k * lines + at
                count = (stop - start) // 128
                here = [tail[first + n : first + n + 1] for n in range(count)]
                tap_rows.append(jnp.concatenate(here, axis=1))
            return conv_silu(
                padded.at[j, kid, :, : stop - start],
                jnp.concatenate(tap_rows),
                opening_ref[q, :, start:stop],
                weights_ref[q, : reach + 1, start:stop],
            )

        bc_first = opening(group_wide, group_wide + 2 * size, lines - 2)
        b_first, c_first = bc_first[:, :size], bc_first[:, size:]
        start = offset * width
        x_all = opening(start, start + wide, start // 128).astype(jnp.float32)
        skipped = weights_ref[q, reach + 1 : reach + 2, start : start + wide] * x_all
        c_conv = jnp.concatenate([c_first, held_ref[q, FIX:]])
        terms = three_terms(jnp.exp2(column_ref[q]))
        terms = jnp.concatenate([terms, jnp.zeros((per_group, length), jnp.float32)])
        spread_row = lax.broadcasted_iota(jnp.int32, (4 * per_group, wide), 0)
        spread_lane = lax.broadcasted_iota(jnp.int32, (4 * per_group, wide), 1)
        spread = spread_row % per_group == offset + spread_lane // width
        grow = jnp.dot(
            terms.T.astype(jnp.bfloat16),
            spread.astype(jnp.float32).astype(jnp.bfloat16),
            preferred_element_type=jnp.float32,
        )
        term = lax.dot_general(c_conv, state, contract, preferred_element_type=jnp.float32)
        carried = (term * grow).astype(jnp.bfloat16)
        scores = lax.dot_general(
            c_conv,
            jnp.concatenate([b_first] * heads),
            contract,
            preferred_element_type=jnp.float32,
        )
        here = slice(offset * FIX, (offset + heads) * FIX)
        mixing = (scores * first_ref[q, :, here]).astype(jnp.bfloat16)
        for pair in range(heads // 2):
            lanes = slice(pair * 2 * width, (pair + 1) * 2 * width)
            x_first = x_all[:, lanes]
            stacked = [jnp.where(low_first, x_first, 0.0), jnp.where(low_first, 0.0, x_first)]
            if pair > 0:
                stacked = [jnp.zeros((2 * pair * FIX, 2 * width), jnp.float32)] + stacked
            if 2 * pair + 2 < heads:
                spare = (heads - 2 * pair - 2) * FIX
                stacked = stacked + [jnp.zeros((spare, 2 * width), jnp.float32)]
            part = jnp.dot(
                mixing,
                jnp.concatenate(stacked).astype(jnp.bfloat16),
                preferred_element_type=jnp.float32,
            )
            part = jnp.concatenate([part[:FIX] + skipped[:, lanes], part[FIX:]])
            whole = slice(start + lanes.start, start + lanes.stop)
            y_part[j, kid, :, lanes] = (
                mixed_ref[q, :, whole] + part + carried[:, lanes].astype(jnp.float32)
            ).astype(jnp.bfloat16)

    copies = []
    for j in range(4):
        for kid in range(kids):
            add(j, kid)
        start = (place_ref[0] ^ j) * (y_ref.shape[2] // 4) + offset * width
        lanes = pl.ds(pl.multiple_of(start, 128), wide)
        copies.append(pltpu.make_async_copy(y_part.at[j], y_ref.at[:, :, lanes], sems.at[j]))
        copies[-1].start()
    for copy in copies:
        copy.wait()


def cast_kernel(parts, tailed, reach, lines, *refs):
    count = len(tailed)
    ins, outs = refs[:-count], refs[-count:]
    states, tails = ins[: parts * count], ins[parts * count :]
    for j, out_ref in enumerate(outs):
        start = 0
        for at in range(parts):
            state = states[parts * j + at][0]
            rows = state.shape[0] * state.shape[1]
            out_ref[start : start + rows] = state.reshape(rows, state.shape[2]).astype(jnp.bfloat16)
            start += rows
            if at == 0 and tailed[j]:
                x_tail = tails[2 * j][0].astype(jnp.float32)
                bc_tail = tails[2 * j + 1][0].astype(jnp.float32)
                pieces = []
                for k in range(reach):
                    pieces += [x_tail[k : k + 1, i * 128 : i * 128 + 128] for i in range(lines - 2)]
                    pieces.append(bc_tail[k])
                spare = tailed[j] - lines * reach
                pieces.append(jnp.zeros((spare, 128), jnp.float32))
                out_ref[start : start + tailed[j]] = jnp.concatenate(pieces).astype(jnp.bfloat16)
                start += tailed[j]


def within_kernel(
    parent_ref,
    x_ref,
    b_ref,
    c_ref,
    dt_ref,
    bias_ref,
    alog_ref,
    skip_ref,
    taps_x_ref,
    taps_bc_ref,
    tail_x_ref,
    tail_bc_ref,
    mixed_ref,
    c_out_ref,
    grow_ref,
    padded,
):
    length = x_ref.shape[1]
    heads = dt_ref.shape[1]
    width = x_ref.shape[2] // heads
    b_conv = conv_silu(padded, tail_bc_ref[0, 0], b_ref[0], taps_bc_ref[0])
    c_conv = conv_silu(padded, tail_bc_ref[0, 1], c_ref[0], taps_bc_ref[1])
    c_out_ref[0] = c_conv
    scores = lax.dot_general(
        c_conv, b_conv, (((1,), (1,)), ((), ())), preferred_element_type=jnp.float32
    )
    raw = dt_ref[0] + bias_ref[...]
    step = jnp.maximum(raw, 0.0) + jnp.log1p(jnp.exp(-jnp.abs(raw)))
    per_token = step * (-jnp.exp(alog_ref[...]))
    row = lax.broadcasted_iota(jnp.int32, (length, length), 0)
    col = lax.broadcasted_iota(jnp.int32, (length, length), 1)
    upper = (row <= col).astype(jnp.float32)
    total = lax.dot_general(
        per_token,
        upper,
        (((1,), (0,)), ((), ())),
        precision=lax.Precision.HIGHEST,
        preferred_element_type=jnp.float32,
    )
    total_t = total.T
    grow_ref[0, 0] = jnp.exp(total_t)
    causal = row >= col
    low = lax.broadcasted_iota(jnp.int32, (length, 2 * width), 1) < width
    for pair in range(heads // 2):
        lanes = slice(pair * 2 * width, (pair + 1) * 2 * width)
        x_conv = conv_silu(
            padded, tail_x_ref[0, :, lanes], x_ref[0, :, lanes], taps_x_ref[:, lanes]
        )
        parts = []
        for head in (2 * pair, 2 * pair + 1):
            gap = total_t[:, head : head + 1] - total[head : head + 1, :]
            factor = jnp.exp(jnp.where(causal, gap, -1e30))
            mixing = (scores * factor * step[head : head + 1, :]).astype(jnp.bfloat16)
            parts.append(jnp.dot(mixing, x_conv, preferred_element_type=jnp.float32))
        mixed_ref[0, :, lanes] = (
            jnp.where(low, parts[0], parts[1]) + skip_ref[:, lanes] * x_conv.astype(jnp.float32)
        )


def carried_kernel(state_ref, c_ref, grow_ref, mixed_ref, y_ref):
    sources, _, part, width, size = state_ref.shape
    length = c_ref.shape[1]
    low = lax.broadcasted_iota(jnp.int32, (length, 2 * width), 1) < width
    c_conv = c_ref[0]
    for source in range(sources):
        state = state_ref[source, 0].reshape(part * width, size)
        term = lax.dot_general(
            c_conv, state, (((1,), (1,)), ((), ())), preferred_element_type=jnp.float32
        )
        for pair in range(part // 2):
            head = source * part + 2 * pair
            grow = jnp.where(
                low, grow_ref[0, 0, :, head : head + 1], grow_ref[0, 0, :, head + 1 : head + 2]
            )
            here = slice(2 * pair * width, (2 * pair + 2) * width)
            lanes = slice(head * width, (head + 2) * width)
            carried = (term[:, here] * grow).astype(jnp.bfloat16).astype(jnp.float32)
            y_ref[0, :, lanes] = (mixed_ref[0, :, lanes] + carried).astype(jnp.bfloat16)


def pick_kernel(parent_ref, state_ref, out_ref):
    out_ref[...] = state_ref[...]


def local_any(
    x_in,
    b_in,
    c_in,
    dt_in,
    dt_bias,
    a_log,
    d_skip,
    conv_x,
    conv_bc,
    par_state,
    tail_x,
    tail_bc,
    counts,
    order,
):
    kids, length, columns = x_in.shape
    heads = dt_in.shape[1]
    width, size = par_state.shape[2:]
    ways = lax.axis_size("batch")
    groups = b_in.shape[2] // size
    per_group = heads // groups
    part = heads // ways
    wide = per_group * width
    reach = tail_x.shape[1]
    parents_all = counts.shape[0]
    kids_all = order.shape[0]

    parent = parent_of(counts, order)
    own = lax.dynamic_slice_in_dim(parent, lax.axis_index("batch") * kids, kids)

    sent = par_state.astype(jnp.bfloat16).reshape(ways, part, width, size)
    shares = lax.all_to_all(sent, "batch", split_axis=0, concat_axis=0, tiled=True)

    tails = jnp.concatenate([tail_x.reshape(-1), tail_bc.reshape(-1)])
    tails = jnp.broadcast_to(tails[None], (ways, tails.shape[0]))
    tails = lax.all_to_all(tails, "batch", split_axis=0, concat_axis=0, tiled=True)
    tails_x = tails[:, : reach * columns].reshape(parents_all, reach, columns)
    tails_bc = tails[:, reach * columns :].reshape(parents_all, 2, reach, groups * size)

    picked = pl.pallas_call(
        pick_kernel,
        grid_spec=pltpu.PrefetchScalarGridSpec(
            num_scalar_prefetch=1,
            grid=(kids_all,),
            in_specs=[pl.BlockSpec((1, part, width, size), lambda i, p: (p[i], 0, 0, 0))],
            out_specs=pl.BlockSpec((1, part, width, size), lambda i, p: (i, 0, 0, 0)),
        ),
        out_shape=jax.ShapeDtypeStruct((kids_all, part, width, size), jnp.bfloat16),
        cost_estimate=pl.CostEstimate(
            flops=0, bytes_accessed=4 * kids_all * part * width * size, transcendentals=0
        ),
        name="pick_states",
    )(parent, shares)
    states = lax.all_to_all(
        picked.reshape(ways, kids, part, width, size), "batch", split_axis=0, concat_axis=0, tiled=True
    )

    skip_row = jnp.repeat(d_skip, width)[None, :]
    mixed, c_conv, grow = pl.pallas_call(
        within_kernel,
        grid_spec=pltpu.PrefetchScalarGridSpec(
            num_scalar_prefetch=1,
            grid=(kids, groups),
            in_specs=[
                pl.BlockSpec((1, length, wide), lambda c, q, p: (c, 0, q)),
                pl.BlockSpec((1, length, size), lambda c, q, p: (c, 0, q)),
                pl.BlockSpec((1, length, size), lambda c, q, p: (c, 0, q)),
                pl.BlockSpec((1, per_group, length), lambda c, q, p: (c, q, 0)),
                pl.BlockSpec((per_group, 1), lambda c, q, p: (q, 0)),
                pl.BlockSpec((per_group, 1), lambda c, q, p: (q, 0)),
                pl.BlockSpec((1, wide), lambda c, q, p: (0, q)),
                pl.BlockSpec((reach + 1, wide), lambda c, q, p: (0, q)),
                pl.BlockSpec((2, reach + 1, size), lambda c, q, p: (0, 0, q)),
                pl.BlockSpec((1, reach, wide), lambda c, q, p: (p[c], 0, q)),
                pl.BlockSpec((1, 2, reach, size), lambda c, q, p: (p[c], 0, 0, q)),
            ],
            out_specs=[
                pl.BlockSpec((1, length, wide), lambda c, q, p: (c, 0, q)),
                pl.BlockSpec((1, length, size), lambda c, q, p: (c, 0, q)),
                pl.BlockSpec((1, 1, length, per_group), lambda c, q, p: (c, q, 0, 0)),
            ],
            scratch_shapes=[pltpu.VMEM((8 + length, size), jnp.float32)],
        ),
        out_shape=[
            jax.ShapeDtypeStruct((kids, length, columns), jnp.float32),
            jax.ShapeDtypeStruct((kids, length, groups * size), jnp.bfloat16),
            jax.ShapeDtypeStruct((kids, groups, length, per_group), jnp.float32),
        ],
        compiler_params=pltpu.CompilerParams(vmem_limit_bytes=4 * VMEM_LIMIT),
        cost_estimate=pl.CostEstimate(
            flops=4 * kids * heads * length * length * width,
            bytes_accessed=6 * kids * length * columns,
            transcendentals=kids * heads * length * length,
        ),
        name="within",
    )(
        own,
        x_in,
        b_in,
        c_in,
        dt_in,
        dt_bias[:, None],
        a_log[:, None],
        skip_row,
        conv_x,
        conv_bc,
        tails_x,
        tails_bc,
    )

    sources = per_group // part
    return pl.pallas_call(
        carried_kernel,
        grid=(kids, groups),
        in_specs=[
            pl.BlockSpec((sources, 1, part, width, size), lambda c, q: (q, c, 0, 0, 0)),
            pl.BlockSpec((1, length, size), lambda c, q: (c, 0, q)),
            pl.BlockSpec((1, 1, length, per_group), lambda c, q: (c, q, 0, 0)),
            pl.BlockSpec((1, length, wide), lambda c, q: (c, 0, q)),
        ],
        out_specs=pl.BlockSpec((1, length, wide), lambda c, q: (c, 0, q)),
        out_shape=jax.ShapeDtypeStruct((kids, length, columns), jnp.bfloat16),
        compiler_params=pltpu.CompilerParams(vmem_limit_bytes=4 * VMEM_LIMIT),
        cost_estimate=pl.CostEstimate(
            flops=2 * kids * length * columns * size,
            bytes_accessed=8 * kids * length * columns,
            transcendentals=0,
        ),
        name="carried",
    )(states, c_conv, grow, mixed)


def local_halves(
    x_in, b_in, c_in, dt_in, dt_bias, a_log, d_skip, conv_x, conv_bc,
    par_state, tail_x, tail_bc, counts, order,
):
    kids, length, columns = x_in.shape
    heads = dt_in.shape[1]
    width, size = par_state.shape[2:]
    groups = b_in.shape[2] // size
    per_group = heads // groups
    wide = per_group * width
    taps = conv_x.shape[0]
    reach = taps - 1
    lines = (wide + 2 * size) // 128
    tail_lines = -(-lines * reach // 16) * 16
    params = pltpu.CompilerParams(vmem_limit_bytes=VMEM_LIMIT)
    anywhere = pl.BlockSpec(memory_space=pl.ANY)
    small = pl.CostEstimate(flops=1, bytes_accessed=1, transcendentals=0)

    stay = lambda x: pltpu.with_memory_space_constraint(x, pltpu.HBM)
    keep_in_vmem = lambda x: pltpu.with_memory_space_constraint(x, pltpu.VMEM)
    x_in, b_in, c_in, dt_in, conv_x, conv_bc = map(stay, (x_in, b_in, c_in, dt_in, conv_x, conv_bc))

    me = lax.axis_index("batch")
    parent = parent_of(counts, order)
    child = (jnp.arange(4 * kids, dtype=jnp.int32) // kids ^ me) * kids
    child = child + jnp.arange(4 * kids, dtype=jnp.int32) % kids
    catalog = jnp.arange(4 * 2 * kids, dtype=jnp.int32)
    owner = jnp.sum(jnp.where(child[:, None] == catalog[None, :], parent[None, :], 0), axis=1)
    slots = owner ^ me
    place = (me % 4).astype(jnp.int32)[None]

    state = stay(par_state.reshape(groups, per_group, width, size))
    x_tails, bc_tails = stay(tail_x), stay(tail_bc.transpose(0, 2, 1, 3))
    offsets = [sum(SPLIT[:k]) for k in range(len(SPLIT))]

    def swap(value, r):
        return lax.ppermute(value, "batch", perm=[(i, i ^ r) for i in range(8)])

    def cast():
        rows = per_group * width + tail_lines
        rows_a = SPLIT[0] * width + tail_lines
        blocks = [(0, SPLIT[0])] + [(at, 4) for at in range(SPLIT[0], per_group, 4)]
        count = len(blocks) + 2

        def kernel(place_ref, *refs):
            ins, outs = refs[: 4 * count], refs[4 * count :]
            quarters = [outs[0], outs[2].at[0], outs[1], outs[2].at[1]]
            for n, out_ref in enumerate(quarters):
                cast_kernel(
                    len(blocks), [tail_lines], reach, lines, *ins[count * n : count * n + count], out_ref
                )
                outs[3 + n // 2][n % 2] = out_ref[:rows_a]

        operands, specs = [], []
        for n in range(4):
            for offset, part in blocks:
                operands.append(state)
                specs.append(
                    pl.BlockSpec(
                        (1, part, width, size),
                        lambda i, p, n=n, at=offset // part: (p[0] ^ n, at, 0, 0),
                    )
                )
            operands += [x_tails, bc_tails]
            specs += [
                pl.BlockSpec((1, reach, wide), lambda i, p, n=n: (0, 0, p[0] ^ n)),
                pl.BlockSpec((1, reach, 2, size), lambda i, p, n=n: (0, 0, 0, p[0] ^ n)),
            ]
        shapes = [(rows, size)] * 2 + [(2, rows, size)] + [(2, rows_a, size)] * 2
        return pl.pallas_call(
            kernel,
            grid_spec=pltpu.PrefetchScalarGridSpec(
                num_scalar_prefetch=1,
                grid=(1,),
                in_specs=specs,
                out_specs=[pl.BlockSpec(memory_space=pltpu.VMEM)] * len(shapes),
            ),
            out_shape=[pltpu.VMEM(shape, jnp.bfloat16) for shape in shapes],
            compiler_params=params,
            cost_estimate=small,
            name="cast_states",
        )(place, *operands)

    def rearrange(scalars, sources, moves, shapes, tokens, name):
        def kernel(scalars_ref, *refs):
            held, outs = refs[: len(sources)], refs[len(sources) :]
            for out, at, scalar, choices in moves:
                for value, (number, take) in enumerate(choices):

                    def copy(out=out, at=at, number=number, take=take):
                        rows = held[number][...] if take is None else held[number][take]
                        if at is None:
                            outs[out][...] = rows
                        else:
                            outs[out][at] = rows

                    if scalar is None:
                        copy()
                    else:
                        pl.when(scalars_ref[scalar] == value)(copy)

        return pl.pallas_call(
            functools.partial(drop_tokens, kernel, 1 + len(sources), len(tokens)),
            grid_spec=pltpu.PrefetchScalarGridSpec(
                num_scalar_prefetch=1,
                grid=(1,),
                in_specs=[pl.BlockSpec(memory_space=pltpu.VMEM)] * len(sources)
                + [anywhere] * len(tokens),
                out_specs=[pl.BlockSpec(memory_space=pltpu.VMEM)] * len(shapes),
            ),
            out_shape=[pltpu.VMEM(shape, jnp.bfloat16) for shape in shapes],
            compiler_params=params,
            cost_estimate=small,
            name=name,
        )(scalars, *map(keep_in_vmem, sources), *tokens)

    def pick(rows, sources, choices, tokens, order=(1, 2, 3)):
        moves = [
            (j, kid, j * kids + kid, choices) for j in range(4) for kid in range(kids)
        ]
        picked = rearrange(
            slots, sources, moves, [(kids, rows, size)] * 4, tokens, "pick_states"
        )
        return [(0, picked[0])] + [(j, swap(picked[j], j)) for j in order]

    def early(c, pieces, piece, before, tokens):
        per = groups // pieces
        at = lambda q: (c, 0, per * piece + q)
        operands = [
            x_in, b_in, c_in, dt_in, dt_bias[:, None], a_log[:, None], skip_row, conv_x, conv_bc
        ]
        keep = len(operands)
        tokens = list(tokens) + [keep_in_vmem(a) for a in before]
        first = keep + len(tokens) - len(before)
        return pl.pallas_call(
            functools.partial(
                drop_tokens, functools.partial(early_kernel, per * piece), keep, len(tokens)
            ),
            grid=(per,),
            in_specs=[
                pl.BlockSpec((1, length, wide), at),
                pl.BlockSpec((1, length, size), at),
                pl.BlockSpec((1, length, size), at),
                pl.BlockSpec((1, per_group, length), lambda q: (c, per * piece + q, 0)),
                pl.BlockSpec((per_group, 1), lambda q: (per * piece + q, 0)),
                pl.BlockSpec((per_group, 1), lambda q: (per * piece + q, 0)),
                pl.BlockSpec((1, wide), lambda q: (0, per * piece + q)),
                pl.BlockSpec((taps, wide), lambda q: (0, per * piece + q)),
                pl.BlockSpec((2, taps, size), lambda q: (0, 0, per * piece + q)),
                *[anywhere] * len(tokens),
            ],
            out_specs=[pl.BlockSpec(memory_space=pltpu.VMEM)] * 6,
            out_shape=[
                pltpu.VMEM((groups, length, wide), jnp.float32),
                pltpu.VMEM((groups, length, size), jnp.bfloat16),
                pltpu.VMEM((groups, per_group, length), jnp.float32),
                pltpu.VMEM((groups, length, per_group * FIX), jnp.float32),
                pltpu.VMEM((groups, FIX, wide + 2 * size), jnp.bfloat16),
                pltpu.VMEM((groups, 8, wide + 2 * size), jnp.float32),
            ],
            input_output_aliases={first + i: i for i in range(len(before))},
            scratch_shapes=[pltpu.VMEM((2, 8 + length, size), jnp.float32)],
            compiler_params=params,
            cost_estimate=small,
            name="early",
        )(*operands, *tokens)

    def late(ks, states, parts, result, tokens):
        offset = offsets[ks[0]]
        chunk = sum(SPLIT[k] for k in ks) * width
        places = [[j for j, _ in chunk_states] for chunk_states in states]
        held = [array for chunk_states in states for _, array in chunk_states]
        operands = [keep_in_vmem(a) for a in (*held[:4], *sum((held[4 * k : 4 * k + 4] for k in ks), []), *parts[0], *parts[1])]
        specs = [pl.BlockSpec(memory_space=pltpu.VMEM)] * len(operands)
        keep = 1 + len(operands)
        operands += tokens
        specs += [anywhere] * len(tokens)
        alias = {}
        if result is not None:
            alias = {1 + len(operands): 0}
            operands.append(result)
            specs.append(anywhere)
        kernel = functools.partial(
            late_kernel, [places[0]] + [places[k] for k in ks], offset, [SPLIT[k] for k in ks], lines, reach, SPLIT[0] * width
        )
        return pl.pallas_call(
            functools.partial(drop_tokens, kernel, keep, 1 + len(operands) - keep),
            grid_spec=pltpu.PrefetchScalarGridSpec(
                num_scalar_prefetch=1,
                grid=(1,),
                in_specs=specs,
                out_specs=anywhere,
                scratch_shapes=[
                    pltpu.VMEM((groups, kids, 8 + FIX, max(chunk, 2 * size)), jnp.float32),
                    pltpu.VMEM((groups, kids, length, chunk), jnp.bfloat16),
                    pltpu.SemaphoreType.DMA((groups,)),
                ],
            ),
            out_shape=jax.ShapeDtypeStruct(x_in.shape, jnp.bfloat16),
            input_output_aliases=alias,
            compiler_params=params,
            cost_estimate=small,
            name="late",
        )(place, *operands)

    skip_row = jnp.repeat(d_skip, width)[None, :]
    rows = [SPLIT[0] * width + tail_lines] + [part * width for part in SPLIT[1:]]
    chunks = [pl.ds(sum(rows[:k]), rows[k]) for k in range(len(SPLIT))]
    own, own_2, own_13, sent_4, sent_6 = cast()
    crossed_a = [swap(sent_4, 4), swap(sent_6, 6)]
    along_y, along_z = swap(own_13, 1), swap(own_2, 2)
    parts = [early(0, 1, 0, [], [own, slots])]
    (turn,) = rearrange(
        place, [along_y], [(0, None, None, [(0, 1)])], [own.shape], [parts[0][1]], "stack_turn"
    )
    inside = [own, along_y, along_z, swap(turn, 2)]

    def inside_rows(k):
        return [(0, chunks[k]), (1, (0, chunks[k])), (2, chunks[k]), (3, chunks[k])]

    def cross(k, tokens):
        moves = [(0, j, None, [choice]) for j, choice in enumerate(inside_rows(k))]
        (sent,) = rearrange(place, inside, moves, [(4, rows[k], size)], tokens, "stack_later")
        return sent, swap(sent, 4)

    def pick_later(k, crossed, tokens):
        choices = inside_rows(k) + [(4, j) for j in range(4)]
        return pick(rows[k], [*inside, crossed], choices, tokens, (3, 2, 1))

    second = early(1, 2, 0, [], [turn])
    moves = [(0, n, None, [(n, 1)]) for n in range(2)]
    (spread,) = rearrange(
        place, crossed_a, moves, [(2, rows[0], size)], [second[1]], "stack_first"
    )
    passed = swap(spread, 1)
    sent_b, crossed_b = cross(1, [spread])
    second = early(1, 2, 1, second, [sent_b])
    parts.append(second)
    choices = inside_rows(0) + [(4, 0), (6, 0), (5, 0), (6, 1)]
    states = [pick(rows[0], [*inside, *crossed_a, passed], choices, [second[1]])]
    states.append(pick_later(1, crossed_b, [states[0][0][1]]))
    result = late([0], states, parts, None, [states[1][0][1]])
    return late([1], states, parts, result, [])


def solution(mesh):
    rows, cols = P(("groups", "batch"), None, "head"), P(("groups", "batch"), "head")
    placed = (
        rows, rows, rows, cols, P("head"), P("head"), P("head"), P(None, "head"),
        P(None, None, "head"), cols, rows, P(("groups", "batch"), None, None, "head"),
        P("groups"), P("groups"),
    )
    local = local_halves if mesh.shape["batch"] == 8 else local_any
    return jax.shard_map(local, mesh=mesh, in_specs=placed, out_specs=rows, check_vma=False)
```

```python
import functools

import jax
import jax.numpy as jnp
from jax import lax
from jax.experimental import pallas as pl
from jax.experimental.pallas import tpu as pltpu
from jax.sharding import PartitionSpec as P

VMEM_LIMIT = 12 * 1024 * 1024
SPLIT = (10, 6)
FIX = 16
LOG2_E = 1.4426950408889634


def drop_tokens(kernel, keep, tokens, *refs):
    kernel(*refs[:keep], *refs[keep + tokens :])


def parent_of(counts, order):
    index = jnp.arange(counts.shape[0], dtype=jnp.int32)
    bounds = jnp.sum(jnp.where(index[None, :] <= index[:, None], counts[None, :], 0), axis=1)
    return jnp.sum((bounds[None, :] <= order[:, None]).astype(jnp.int32), axis=1)


def three_terms(value):
    terms = []
    for _ in range(3):
        terms.append(value.astype(jnp.bfloat16).astype(jnp.float32))
        value = value - terms[-1]
    return jnp.concatenate(terms)


def conv_silu(padded, tail, rows, taps):
    length = rows.shape[0]
    reach = taps.shape[0] - 1
    padded[8 - reach : 8, :] = jnp.broadcast_to(tail, (reach, rows.shape[1])).astype(jnp.float32)
    padded[8 : 8 + length, :] = rows.astype(jnp.float32)
    total = padded[8 - reach : 8 - reach + length, :] * taps[0:1, :]
    for k in range(1, reach + 1):
        total = total + padded[8 - reach + k : 8 - reach + k + length, :] * taps[k : k + 1, :]
    half = 0.5 * total
    return (half + half * jnp.tanh(half)).astype(jnp.bfloat16)


def early_kernel(
    base, x_ref, b_ref, c_ref, dt_ref, bias_ref, alog_ref, skip_ref, taps_x_ref, taps_bc_ref,
    mixed_ref, c_out_ref, column_ref, first_ref, opening_ref, weights_ref, padded,
):
    length, wide = x_ref.shape[1:]
    heads = dt_ref.shape[1]
    q = base + pl.program_id(0)
    width = wide // heads
    half = length // 2

    def convolve(rows, taps, slot):
        bulk = conv_silu(padded.at[slot % 2], 0.0, rows, taps)[FIX:]
        return jnp.concatenate([jnp.zeros((FIX, rows.shape[1]), jnp.bfloat16), bulk])

    b_conv = convolve(b_ref[0], taps_bc_ref[0], 0)
    c_conv = convolve(c_ref[0], taps_bc_ref[1], 1)
    c_out_ref[q] = c_conv
    size = b_ref.shape[2]
    taps = taps_x_ref.shape[0]
    opening_ref[q, :, :wide] = x_ref[0, :FIX]
    opening_ref[q, :, wide : wide + size] = b_ref[0, :FIX]
    opening_ref[q, :, wide + size :] = c_ref[0, :FIX]
    weights_ref[q, :taps, :wide] = taps_x_ref[...]
    weights_ref[q, :taps, wide : wide + size] = taps_bc_ref[0]
    weights_ref[q, :taps, wide + size :] = taps_bc_ref[1]
    weights_ref[q, taps : taps + 1, :wide] = skip_ref[...]
    scores = lax.dot_general(
        c_conv, b_conv, (((1,), (1,)), ((), ())), preferred_element_type=jnp.float32
    )
    raw = dt_ref[0] + bias_ref[...]
    step = jnp.maximum(raw, 0.0) + jnp.log1p(jnp.exp(-jnp.abs(raw)))
    per_token = step * (-jnp.exp(alog_ref[...]))
    upper = lax.broadcasted_iota(jnp.int32, (length, length), 0) <= lax.broadcasted_iota(
        jnp.int32, (length, length), 1
    )
    sums = jnp.dot(
        three_terms(per_token).astype(jnp.bfloat16),
        upper.astype(jnp.float32).astype(jnp.bfloat16),
        preferred_element_type=jnp.float32,
    )
    total = (sums[:heads] + sums[heads : 2 * heads]) + sums[2 * heads :]
    total = total * LOG2_E
    row = total - jnp.log(step) * LOG2_E
    columns = total.T
    column_ref[q] = total
    causal = lax.broadcasted_iota(jnp.int32, (half, half), 0) >= lax.broadcasted_iota(
        jnp.int32, (half, half), 1
    )
    low = lax.broadcasted_iota(jnp.int32, (length, 2 * width), 1) < width
    for pair in range(heads // 2):
        lanes = slice(pair * 2 * width, (pair + 1) * 2 * width)
        x_conv = convolve(x_ref[0, :, lanes], taps_x_ref[:, lanes], pair)
        parts = []
        for head in (2 * pair, 2 * pair + 1):
            column = jnp.broadcast_to(columns[:, head : head + 1], (length, half))
            rows = row[head : head + 1, :]
            near = jnp.exp2(jnp.where(causal, column[:half] - rows[:, :half], -1e30))
            far = jnp.exp2(column[half:] - rows[:, :half])
            last = jnp.exp2(jnp.where(causal, column[half:] - rows[:, half:], -1e30))
            spot = slice(head * FIX, (head + 1) * FIX)
            first_ref[q, :half, spot] = near[:, :FIX]
            first_ref[q, half:, spot] = far[:, :FIX]
            top = (scores[:half, :half] * near).astype(jnp.bfloat16)
            left = (scores[half:, :half] * far).astype(jnp.bfloat16)
            right = (scores[half:, half:] * last).astype(jnp.bfloat16)
            below = jnp.concatenate([left, right], axis=1)
            parts.append(
                jnp.concatenate(
                    [
                        jnp.dot(top, x_conv[:half], preferred_element_type=jnp.float32),
                        jnp.dot(below, x_conv, preferred_element_type=jnp.float32),
                    ]
                )
            )
        mixed_ref[q, :, lanes] = jnp.where(low, parts[0], parts[1]) + skip_ref[
            :, lanes
        ] * x_conv.astype(jnp.float32)


def late_kernel(places, offset, heads, lines, reach, tail_at, place_ref, *refs):
    count = len(heads)
    tails, states, parts = refs[:4], refs[4 : 4 + 4 * count], refs[4 + 4 * count : -4]
    y_ref, padded, y_part, sems = refs[-4:]
    _, kids, length, wide = y_part.shape
    rows, heads = heads, sum(heads)
    width = wide // heads
    rows = [part * width for part in rows]
    low_first = lax.broadcasted_iota(jnp.int32, (FIX, 2 * width), 1) < width
    contract = (((1,), (1,)), ((), ()))

    def add(j, kid):
        q = place_ref[0] ^ j
        mixed_ref, held_ref, column_ref, first_ref, opening_ref, weights_ref = parts[
            6 * kid : 6 * kid + 6
        ]
        size = held_ref.shape[2]
        per_group = column_ref.shape[1]
        group_wide = opening_ref.shape[2] - 2 * size
        tail_rows = pl.ds(tail_at, -(-lines * reach // 16) * 16)
        tail = tails[places[0].index(j)][kid, tail_rows].astype(jnp.float32)
        blocks = [states[4 * n + places[1 + n].index(j)] for n in range(count)]
        state = jnp.concatenate([ref[kid, : rows[n]] for n, ref in enumerate(blocks)])

        def opening(start, stop, at):
            tap_rows = []
            for k in range(reach):
                first = k * lines + at
                count = (stop - start) // 128
                here = [tail[first + n : first + n + 1] for n in range(count)]
                tap_rows.append(jnp.concatenate(here, axis=1))
            return conv_silu(
                padded.at[j, kid, :, : stop - start],
                jnp.concatenate(tap_rows),
                opening_ref[q, :, start:stop],
                weights_ref[q, : reach + 1, start:stop],
            )

        bc_first = opening(group_wide, group_wide + 2 * size, lines - 2)
        b_first, c_first = bc_first[:, :size], bc_first[:, size:]
        start = offset * width
        x_all = opening(start, start + wide, start // 128).astype(jnp.float32)
        skipped = weights_ref[q, reach + 1 : reach + 2, start : start + wide] * x_all
        c_conv = jnp.concatenate([c_first, held_ref[q, FIX:]])
        terms = three_terms(jnp.exp2(column_ref[q]))
        terms = jnp.concatenate([terms, jnp.zeros((per_group, length), jnp.float32)])
        spread_row = lax.broadcasted_iota(jnp.int32, (4 * per_group, wide), 0)
        spread_lane = lax.broadcasted_iota(jnp.int32, (4 * per_group, wide), 1)
        spread = spread_row % per_group == offset + spread_lane // width
        grow = jnp.dot(
            terms.T.astype(jnp.bfloat16),
            spread.astype(jnp.float32).astype(jnp.bfloat16),
            preferred_element_type=jnp.float32,
        )
        term = lax.dot_general(c_conv, state, contract, preferred_element_type=jnp.float32)
        carried = (term * grow).astype(jnp.bfloat16)
        scores = lax.dot_general(
            c_conv,
            jnp.concatenate([b_first] * heads),
            contract,
            preferred_element_type=jnp.float32,
        )
        here = slice(offset * FIX, (offset + heads) * FIX)
        mixing = (scores * first_ref[q, :, here]).astype(jnp.bfloat16)
        for pair in range(heads // 2):
            lanes = slice(pair * 2 * width, (pair + 1) * 2 * width)
            x_first = x_all[:, lanes]
            stacked = [jnp.where(low_first, x_first, 0.0), jnp.where(low_first, 0.0, x_first)]
            if pair > 0:
                stacked = [jnp.zeros((2 * pair * FIX, 2 * width), jnp.float32)] + stacked
            if 2 * pair + 2 < heads:
                spare = (heads - 2 * pair - 2) * FIX
                stacked = stacked + [jnp.zeros((spare, 2 * width), jnp.float32)]
            part = jnp.dot(
                mixing,
                jnp.concatenate(stacked).astype(jnp.bfloat16),
                preferred_element_type=jnp.float32,
            )
            part = jnp.concatenate([part[:FIX] + skipped[:, lanes], part[FIX:]])
            whole = slice(start + lanes.start, start + lanes.stop)
            y_part[j, kid, :, lanes] = (
                mixed_ref[q, :, whole] + part + carried[:, lanes].astype(jnp.float32)
            ).astype(jnp.bfloat16)

    copies = []
    for j in range(4):
        for kid in range(kids):
            add(j, kid)
        start = (place_ref[0] ^ j) * (y_ref.shape[2] // 4) + offset * width
        lanes = pl.ds(pl.multiple_of(start, 128), wide)
        copies.append(pltpu.make_async_copy(y_part.at[j], y_ref.at[:, :, lanes], sems.at[j]))
        copies[-1].start()
    for copy in copies:
        copy.wait()


def cast_kernel(parts, tailed, reach, lines, *refs):
    count = len(tailed)
    ins, outs = refs[:-count], refs[-count:]
    states, tails = ins[: parts * count], ins[parts * count :]
    for j, out_ref in enumerate(outs):
        start = 0
        for at in range(parts):
            state = states[parts * j + at][0]
            rows = state.shape[0] * state.shape[1]
            out_ref[start : start + rows] = state.reshape(rows, state.shape[2]).astype(jnp.bfloat16)
            start += rows
            if at == 0 and tailed[j]:
                x_tail = tails[2 * j][0].astype(jnp.float32)
                bc_tail = tails[2 * j + 1][0].astype(jnp.float32)
                pieces = []
                for k in range(reach):
                    pieces += [x_tail[k : k + 1, i * 128 : i * 128 + 128] for i in range(lines - 2)]
                    pieces.append(bc_tail[k])
                spare = tailed[j] - lines * reach
                pieces.append(jnp.zeros((spare, 128), jnp.float32))
                out_ref[start : start + tailed[j]] = jnp.concatenate(pieces).astype(jnp.bfloat16)
                start += tailed[j]


def within_kernel(
    parent_ref,
    x_ref,
    b_ref,
    c_ref,
    dt_ref,
    bias_ref,
    alog_ref,
    skip_ref,
    taps_x_ref,
    taps_bc_ref,
    tail_x_ref,
    tail_bc_ref,
    mixed_ref,
    c_out_ref,
    grow_ref,
    padded,
):
    length = x_ref.shape[1]
    heads = dt_ref.shape[1]
    width = x_ref.shape[2] // heads
    b_conv = conv_silu(padded, tail_bc_ref[0, 0], b_ref[0], taps_bc_ref[0])
    c_conv = conv_silu(padded, tail_bc_ref[0, 1], c_ref[0], taps_bc_ref[1])
    c_out_ref[0] = c_conv
    scores = lax.dot_general(
        c_conv, b_conv, (((1,), (1,)), ((), ())), preferred_element_type=jnp.float32
    )
    raw = dt_ref[0] + bias_ref[...]
    step = jnp.maximum(raw, 0.0) + jnp.log1p(jnp.exp(-jnp.abs(raw)))
    per_token = step * (-jnp.exp(alog_ref[...]))
    row = lax.broadcasted_iota(jnp.int32, (length, length), 0)
    col = lax.broadcasted_iota(jnp.int32, (length, length), 1)
    upper = (row <= col).astype(jnp.float32)
    total = lax.dot_general(
        per_token,
        upper,
        (((1,), (0,)), ((), ())),
        precision=lax.Precision.HIGHEST,
        preferred_element_type=jnp.float32,
    )
    total_t = total.T
    grow_ref[0, 0] = jnp.exp(total_t)
    causal = row >= col
    low = lax.broadcasted_iota(jnp.int32, (length, 2 * width), 1) < width
    for pair in range(heads // 2):
        lanes = slice(pair * 2 * width, (pair + 1) * 2 * width)
        x_conv = conv_silu(
            padded, tail_x_ref[0, :, lanes], x_ref[0, :, lanes], taps_x_ref[:, lanes]
        )
        parts = []
        for head in (2 * pair, 2 * pair + 1):
            gap = total_t[:, head : head + 1] - total[head : head + 1, :]
            factor = jnp.exp(jnp.where(causal, gap, -1e30))
            mixing = (scores * factor * step[head : head + 1, :]).astype(jnp.bfloat16)
            parts.append(jnp.dot(mixing, x_conv, preferred_element_type=jnp.float32))
        mixed_ref[0, :, lanes] = (
            jnp.where(low, parts[0], parts[1]) + skip_ref[:, lanes] * x_conv.astype(jnp.float32)
        )


def carried_kernel(state_ref, c_ref, grow_ref, mixed_ref, y_ref):
    sources, _, part, width, size = state_ref.shape
    length = c_ref.shape[1]
    low = lax.broadcasted_iota(jnp.int32, (length, 2 * width), 1) < width
    c_conv = c_ref[0]
    for source in range(sources):
        state = state_ref[source, 0].reshape(part * width, size)
        term = lax.dot_general(
            c_conv, state, (((1,), (1,)), ((), ())), preferred_element_type=jnp.float32
        )
        for pair in range(part // 2):
            head = source * part + 2 * pair
            grow = jnp.where(
                low, grow_ref[0, 0, :, head : head + 1], grow_ref[0, 0, :, head + 1 : head + 2]
            )
            here = slice(2 * pair * width, (2 * pair + 2) * width)
            lanes = slice(head * width, (head + 2) * width)
            carried = (term[:, here] * grow).astype(jnp.bfloat16).astype(jnp.float32)
            y_ref[0, :, lanes] = (mixed_ref[0, :, lanes] + carried).astype(jnp.bfloat16)


def pick_kernel(parent_ref, state_ref, out_ref):
    out_ref[...] = state_ref[...]


def local_any(
    x_in,
    b_in,
    c_in,
    dt_in,
    dt_bias,
    a_log,
    d_skip,
    conv_x,
    conv_bc,
    par_state,
    tail_x,
    tail_bc,
    counts,
    order,
):
    kids, length, columns = x_in.shape
    heads = dt_in.shape[1]
    width, size = par_state.shape[2:]
    ways = lax.axis_size("batch")
    groups = b_in.shape[2] // size
    per_group = heads // groups
    part = heads // ways
    wide = per_group * width
    reach = tail_x.shape[1]
    parents_all = counts.shape[0]
    kids_all = order.shape[0]

    parent = parent_of(counts, order)
    own = lax.dynamic_slice_in_dim(parent, lax.axis_index("batch") * kids, kids)

    sent = par_state.astype(jnp.bfloat16).reshape(ways, part, width, size)
    shares = lax.all_to_all(sent, "batch", split_axis=0, concat_axis=0, tiled=True)

    tails = jnp.concatenate([tail_x.reshape(-1), tail_bc.reshape(-1)])
    tails = jnp.broadcast_to(tails[None], (ways, tails.shape[0]))
    tails = lax.all_to_all(tails, "batch", split_axis=0, concat_axis=0, tiled=True)
    tails_x = tails[:, : reach * columns].reshape(parents_all, reach, columns)
    tails_bc = tails[:, reach * columns :].reshape(parents_all, 2, reach, groups * size)

    picked = pl.pallas_call(
        pick_kernel,
        grid_spec=pltpu.PrefetchScalarGridSpec(
            num_scalar_prefetch=1,
            grid=(kids_all,),
            in_specs=[pl.BlockSpec((1, part, width, size), lambda i, p: (p[i], 0, 0, 0))],
            out_specs=pl.BlockSpec((1, part, width, size), lambda i, p: (i, 0, 0, 0)),
        ),
        out_shape=jax.ShapeDtypeStruct((kids_all, part, width, size), jnp.bfloat16),
        cost_estimate=pl.CostEstimate(
            flops=0, bytes_accessed=4 * kids_all * part * width * size, transcendentals=0
        ),
        name="pick_states",
    )(parent, shares)
    states = lax.all_to_all(
        picked.reshape(ways, kids, part, width, size), "batch", split_axis=0, concat_axis=0, tiled=True
    )

    skip_row = jnp.repeat(d_skip, width)[None, :]
    mixed, c_conv, grow = pl.pallas_call(
        within_kernel,
        grid_spec=pltpu.PrefetchScalarGridSpec(
            num_scalar_prefetch=1,
            grid=(kids, groups),
            in_specs=[
                pl.BlockSpec((1, length, wide), lambda c, q, p: (c, 0, q)),
                pl.BlockSpec((1, length, size), lambda c, q, p: (c, 0, q)),
                pl.BlockSpec((1, length, size), lambda c, q, p: (c, 0, q)),
                pl.BlockSpec((1, per_group, length), lambda c, q, p: (c, q, 0)),
                pl.BlockSpec((per_group, 1), lambda c, q, p: (q, 0)),
                pl.BlockSpec((per_group, 1), lambda c, q, p: (q, 0)),
                pl.BlockSpec((1, wide), lambda c, q, p: (0, q)),
                pl.BlockSpec((reach + 1, wide), lambda c, q, p: (0, q)),
                pl.BlockSpec((2, reach + 1, size), lambda c, q, p: (0, 0, q)),
                pl.BlockSpec((1, reach, wide), lambda c, q, p: (p[c], 0, q)),
                pl.BlockSpec((1, 2, reach, size), lambda c, q, p: (p[c], 0, 0, q)),
            ],
            out_specs=[
                pl.BlockSpec((1, length, wide), lambda c, q, p: (c, 0, q)),
                pl.BlockSpec((1, length, size), lambda c, q, p: (c, 0, q)),
                pl.BlockSpec((1, 1, length, per_group), lambda c, q, p: (c, q, 0, 0)),
            ],
            scratch_shapes=[pltpu.VMEM((8 + length, size), jnp.float32)],
        ),
        out_shape=[
            jax.ShapeDtypeStruct((kids, length, columns), jnp.float32),
            jax.ShapeDtypeStruct((kids, length, groups * size), jnp.bfloat16),
            jax.ShapeDtypeStruct((kids, groups, length, per_group), jnp.float32),
        ],
        compiler_params=pltpu.CompilerParams(vmem_limit_bytes=4 * VMEM_LIMIT),
        cost_estimate=pl.CostEstimate(
            flops=4 * kids * heads * length * length * width,
            bytes_accessed=6 * kids * length * columns,
            transcendentals=kids * heads * length * length,
        ),
        name="within",
    )(
        own,
        x_in,
        b_in,
        c_in,
        dt_in,
        dt_bias[:, None],
        a_log[:, None],
        skip_row,
        conv_x,
        conv_bc,
        tails_x,
        tails_bc,
    )

    sources = per_group // part
    return pl.pallas_call(
        carried_kernel,
        grid=(kids, groups),
        in_specs=[
            pl.BlockSpec((sources, 1, part, width, size), lambda c, q: (q, c, 0, 0, 0)),
            pl.BlockSpec((1, length, size), lambda c, q: (c, 0, q)),
            pl.BlockSpec((1, 1, length, per_group), lambda c, q: (c, q, 0, 0)),
            pl.BlockSpec((1, length, wide), lambda c, q: (c, 0, q)),
        ],
        out_specs=pl.BlockSpec((1, length, wide), lambda c, q: (c, 0, q)),
        out_shape=jax.ShapeDtypeStruct((kids, length, columns), jnp.bfloat16),
        compiler_params=pltpu.CompilerParams(vmem_limit_bytes=4 * VMEM_LIMIT),
        cost_estimate=pl.CostEstimate(
            flops=2 * kids * length * columns * size,
            bytes_accessed=8 * kids * length * columns,
            transcendentals=0,
        ),
        name="carried",
    )(states, c_conv, grow, mixed)


def local_halves(
    x_in, b_in, c_in, dt_in, dt_bias, a_log, d_skip, conv_x, conv_bc,
    par_state, tail_x, tail_bc, counts, order,
):
    kids, length, columns = x_in.shape
    heads = dt_in.shape[1]
    width, size = par_state.shape[2:]
    groups = b_in.shape[2] // size
    per_group = heads // groups
    wide = per_group * width
    taps = conv_x.shape[0]
    reach = taps - 1
    lines = (wide + 2 * size) // 128
    tail_lines = -(-lines * reach // 16) * 16
    params = pltpu.CompilerParams(vmem_limit_bytes=VMEM_LIMIT)
    anywhere = pl.BlockSpec(memory_space=pl.ANY)
    small = pl.CostEstimate(flops=1, bytes_accessed=1, transcendentals=0)

    stay = lambda x: pltpu.with_memory_space_constraint(x, pltpu.HBM)
    keep_in_vmem = lambda x: pltpu.with_memory_space_constraint(x, pltpu.VMEM)
    x_in, b_in, c_in, dt_in, conv_x, conv_bc = map(stay, (x_in, b_in, c_in, dt_in, conv_x, conv_bc))

    me = lax.axis_index("batch")
    parent = parent_of(counts, order)
    child = (jnp.arange(4 * kids, dtype=jnp.int32) // kids ^ me) * kids
    child = child + jnp.arange(4 * kids, dtype=jnp.int32) % kids
    catalog = jnp.arange(4 * 2 * kids, dtype=jnp.int32)
    owner = jnp.sum(jnp.where(child[:, None] == catalog[None, :], parent[None, :], 0), axis=1)
    slots = owner ^ me
    place = (me % 4).astype(jnp.int32)[None]

    state = stay(par_state.reshape(groups, per_group, width, size))
    x_tails, bc_tails = stay(tail_x), stay(tail_bc.transpose(0, 2, 1, 3))
    offsets = [sum(SPLIT[:k]) for k in range(len(SPLIT))]

    def swap(value, r):
        return lax.ppermute(value, "batch", perm=[(i, i ^ r) for i in range(8)])

    def cast():
        rows = per_group * width + tail_lines
        rows_a = SPLIT[0] * width + tail_lines
        blocks = [(0, SPLIT[0])] + [(at, 2) for at in range(SPLIT[0], per_group, 2)]
        count = len(blocks) + 2

        def kernel(place_ref, *refs):
            ins, outs = refs[: 4 * count], refs[4 * count :]
            quarters = [outs[0], outs[2].at[0], outs[1], outs[2].at[1]]
            for n, out_ref in enumerate(quarters):
                cast_kernel(
                    len(blocks), [tail_lines], reach, lines, *ins[count * n : count * n + count], out_ref
                )
                outs[3 + n // 2][n % 2] = out_ref[:rows_a]

        operands, specs = [], []
        for n in range(4):
            for offset, part in blocks:
                operands.append(state)
                specs.append(
                    pl.BlockSpec(
                        (1, part, width, size),
                        lambda i, p, n=n, at=offset // part: (p[0] ^ n, at, 0, 0),
                    )
                )
            operands += [x_tails, bc_tails]
            specs += [
                pl.BlockSpec((1, reach, wide), lambda i, p, n=n: (0, 0, p[0] ^ n)),
                pl.BlockSpec((1, reach, 2, size), lambda i, p, n=n: (0, 0, 0, p[0] ^ n)),
            ]
        shapes = [(rows, size)] * 2 + [(2, rows, size)] + [(2, rows_a, size)] * 2
        return pl.pallas_call(
            kernel,
            grid_spec=pltpu.PrefetchScalarGridSpec(
                num_scalar_prefetch=1,
                grid=(1,),
                in_specs=specs,
                out_specs=[pl.BlockSpec(memory_space=pltpu.VMEM)] * len(shapes),
            ),
            out_shape=[pltpu.VMEM(shape, jnp.bfloat16) for shape in shapes],
            compiler_params=params,
            cost_estimate=small,
            name="cast_states",
        )(place, *operands)

    def rearrange(scalars, sources, moves, shapes, tokens, name):
        def kernel(scalars_ref, *refs):
            held, outs = refs[: len(sources)], refs[len(sources) :]
            for out, at, scalar, choices in moves:
                for value, (number, take) in enumerate(choices):

                    def copy(out=out, at=at, number=number, take=take):
                        rows = held[number][...] if take is None else held[number][take]
                        if at is None:
                            outs[out][...] = rows
                        else:
                            outs[out][at] = rows

                    if scalar is None:
                        copy()
                    else:
                        pl.when(scalars_ref[scalar] == value)(copy)

        return pl.pallas_call(
            functools.partial(drop_tokens, kernel, 1 + len(sources), len(tokens)),
            grid_spec=pltpu.PrefetchScalarGridSpec(
                num_scalar_prefetch=1,
                grid=(1,),
                in_specs=[pl.BlockSpec(memory_space=pltpu.VMEM)] * len(sources)
                + [anywhere] * len(tokens),
                out_specs=[pl.BlockSpec(memory_space=pltpu.VMEM)] * len(shapes),
            ),
            out_shape=[pltpu.VMEM(shape, jnp.bfloat16) for shape in shapes],
            compiler_params=params,
            cost_estimate=small,
            name=name,
        )(scalars, *map(keep_in_vmem, sources), *tokens)

    def pick(rows, sources, choices, tokens, order=(1, 2, 3)):
        moves = [
            (j, kid, j * kids + kid, choices) for j in range(4) for kid in range(kids)
        ]
        picked = rearrange(
            slots, sources, moves, [(kids, rows, size)] * 4, tokens, "pick_states"
        )
        return [(0, picked[0])] + [(j, swap(picked[j], j)) for j in order]

    def early(c, pieces, piece, before, tokens):
        per = groups // pieces
        at = lambda q: (c, 0, per * piece + q)
        operands = [
            x_in, b_in, c_in, dt_in, dt_bias[:, None], a_log[:, None], skip_row, conv_x, conv_bc
        ]
        keep = len(operands)
        tokens = list(tokens) + [keep_in_vmem(a) for a in before]
        first = keep + len(tokens) - len(before)
        return pl.pallas_call(
            functools.partial(
                drop_tokens, functools.partial(early_kernel, per * piece), keep, len(tokens)
            ),
            grid=(per,),
            in_specs=[
                pl.BlockSpec((1, length, wide), at),
                pl.BlockSpec((1, length, size), at),
                pl.BlockSpec((1, length, size), at),
                pl.BlockSpec((1, per_group, length), lambda q: (c, per * piece + q, 0)),
                pl.BlockSpec((per_group, 1), lambda q: (per * piece + q, 0)),
                pl.BlockSpec((per_group, 1), lambda q: (per * piece + q, 0)),
                pl.BlockSpec((1, wide), lambda q: (0, per * piece + q)),
                pl.BlockSpec((taps, wide), lambda q: (0, per * piece + q)),
                pl.BlockSpec((2, taps, size), lambda q: (0, 0, per * piece + q)),
                *[anywhere] * len(tokens),
            ],
            out_specs=[pl.BlockSpec(memory_space=pltpu.VMEM)] * 6,
            out_shape=[
                pltpu.VMEM((groups, length, wide), jnp.float32),
                pltpu.VMEM((groups, length, size), jnp.bfloat16),
                pltpu.VMEM((groups, per_group, length), jnp.float32),
                pltpu.VMEM((groups, length, per_group * FIX), jnp.float32),
                pltpu.VMEM((groups, FIX, wide + 2 * size), jnp.bfloat16),
                pltpu.VMEM((groups, 8, wide + 2 * size), jnp.float32),
            ],
            input_output_aliases={first + i: i for i in range(len(before))},
            scratch_shapes=[pltpu.VMEM((2, 8 + length, size), jnp.float32)],
            compiler_params=params,
            cost_estimate=small,
            name="early",
        )(*operands, *tokens)

    def late(ks, states, parts, result, tokens):
        offset = offsets[ks[0]]
        chunk = sum(SPLIT[k] for k in ks) * width
        places = [[j for j, _ in chunk_states] for chunk_states in states]
        held = [array for chunk_states in states for _, array in chunk_states]
        operands = [keep_in_vmem(a) for a in (*held[:4], *sum((held[4 * k : 4 * k + 4] for k in ks), []), *parts[0], *parts[1])]
        specs = [pl.BlockSpec(memory_space=pltpu.VMEM)] * len(operands)
        keep = 1 + len(operands)
        operands += tokens
        specs += [anywhere] * len(tokens)
        alias = {}
        if result is not None:
            alias = {1 + len(operands): 0}
            operands.append(result)
            specs.append(anywhere)
        kernel = functools.partial(
            late_kernel, [places[0]] + [places[k] for k in ks], offset, [SPLIT[k] for k in ks], lines, reach, SPLIT[0] * width
        )
        return pl.pallas_call(
            functools.partial(drop_tokens, kernel, keep, 1 + len(operands) - keep),
            grid_spec=pltpu.PrefetchScalarGridSpec(
                num_scalar_prefetch=1,
                grid=(1,),
                in_specs=specs,
                out_specs=anywhere,
                scratch_shapes=[
                    pltpu.VMEM((groups, kids, 8 + FIX, max(chunk, 2 * size)), jnp.float32),
                    pltpu.VMEM((groups, kids, length, chunk), jnp.bfloat16),
                    pltpu.SemaphoreType.DMA((groups,)),
                ],
            ),
            out_shape=jax.ShapeDtypeStruct(x_in.shape, jnp.bfloat16),
            input_output_aliases=alias,
            compiler_params=params,
            cost_estimate=small,
            name="late",
        )(place, *operands)

    skip_row = jnp.repeat(d_skip, width)[None, :]
    rows = [SPLIT[0] * width + tail_lines] + [part * width for part in SPLIT[1:]]
    chunks = [pl.ds(sum(rows[:k]), rows[k]) for k in range(len(SPLIT))]
    own, own_2, own_13, sent_4, sent_6 = cast()
    crossed_a = [swap(sent_4, 4), swap(sent_6, 6)]
    along_y, along_z = swap(own_13, 1), swap(own_2, 2)
    parts = [early(0, 1, 0, [], [own, slots])]
    (turn,) = rearrange(
        place, [along_y], [(0, None, None, [(0, 1)])], [own.shape], [parts[0][1]], "stack_turn"
    )
    inside = [own, along_y, along_z, swap(turn, 2)]

    def inside_rows(k):
        return [(0, chunks[k]), (1, (0, chunks[k])), (2, chunks[k]), (3, chunks[k])]

    def cross(k, tokens):
        moves = [(0, j, None, [choice]) for j, choice in enumerate(inside_rows(k))]
        (sent,) = rearrange(place, inside, moves, [(4, rows[k], size)], tokens, "stack_later")
        return sent, swap(sent, 4)

    def pick_later(k, crossed, tokens):
        choices = inside_rows(k) + [(4, j) for j in range(4)]
        return pick(rows[k], [*inside, crossed], choices, tokens, (3, 2, 1))

    second = early(1, 2, 0, [], [turn])
    moves = [(0, n, None, [(n, 1)]) for n in range(2)]
    (spread,) = rearrange(
        place, crossed_a, moves, [(2, rows[0], size)], [second[1]], "stack_first"
    )
    passed = swap(spread, 1)
    sent_b, crossed_b = cross(1, [spread])
    second = early(1, 2, 1, second, [sent_b])
    parts.append(second)
    choices = inside_rows(0) + [(4, 0), (6, 0), (5, 0), (6, 1)]
    states = [pick(rows[0], [*inside, *crossed_a, passed], choices, [second[1]])]
    states.append(pick_later(1, crossed_b, [states[0][0][1]]))
    result = late([0], states, parts, None, [states[1][0][1]])
    return late([1], states, parts, result, [])


def solution(mesh):
    rows, cols = P(("groups", "batch"), None, "head"), P(("groups", "batch"), "head")
    placed = (
        rows, rows, rows, cols, P("head"), P("head"), P("head"), P(None, "head"),
        P(None, None, "head"), cols, rows, P(("groups", "batch"), None, None, "head"),
        P("groups"), P("groups"),
    )
    local = local_halves if mesh.shape["batch"] == 8 else local_any
    return jax.shard_map(local, mesh=mesh, in_specs=placed, out_specs=rows, check_vma=False)
```

```python
import functools

import jax
import jax.numpy as jnp
from jax import lax
from jax.experimental import pallas as pl
from jax.experimental.pallas import tpu as pltpu
from jax.sharding import PartitionSpec as P

VMEM_LIMIT = 12 * 1024 * 1024
SPLIT = (10, 6)
FIX = 16
LOG2_E = 1.4426950408889634


def drop_tokens(kernel, keep, tokens, *refs):
    kernel(*refs[:keep], *refs[keep + tokens :])


def parent_of(counts, order):
    index = jnp.arange(counts.shape[0], dtype=jnp.int32)
    bounds = jnp.sum(jnp.where(index[None, :] <= index[:, None], counts[None, :], 0), axis=1)
    return jnp.sum((bounds[None, :] <= order[:, None]).astype(jnp.int32), axis=1)


def three_terms(value):
    terms = []
    for _ in range(3):
        terms.append(value.astype(jnp.bfloat16).astype(jnp.float32))
        value = value - terms[-1]
    return jnp.concatenate(terms)


def conv_silu(padded, tail, rows, taps):
    length = rows.shape[0]
    reach = taps.shape[0] - 1
    padded[8 - reach : 8, :] = jnp.broadcast_to(tail, (reach, rows.shape[1])).astype(jnp.float32)
    padded[8 : 8 + length, :] = rows.astype(jnp.float32)
    total = padded[8 - reach : 8 - reach + length, :] * taps[0:1, :]
    for k in range(1, reach + 1):
        total = total + padded[8 - reach + k : 8 - reach + k + length, :] * taps[k : k + 1, :]
    half = 0.5 * total
    return (half + half * jnp.tanh(half)).astype(jnp.bfloat16)


def early_kernel(
    base, x_ref, b_ref, c_ref, dt_ref, bias_ref, alog_ref, skip_ref, taps_x_ref, taps_bc_ref,
    mixed_ref, c_out_ref, column_ref, first_ref, opening_ref, weights_ref, padded,
):
    length, wide = x_ref.shape[1:]
    heads = dt_ref.shape[1]
    q = base + pl.program_id(0)
    width = wide // heads
    half = length // 2

    def convolve(rows, taps, slot):
        bulk = conv_silu(padded.at[slot % 2], 0.0, rows, taps)[FIX:]
        return jnp.concatenate([jnp.zeros((FIX, rows.shape[1]), jnp.bfloat16), bulk])

    b_conv = convolve(b_ref[0], taps_bc_ref[0], 0)
    c_conv = convolve(c_ref[0], taps_bc_ref[1], 1)
    c_out_ref[q] = c_conv
    size = b_ref.shape[2]
    taps = taps_x_ref.shape[0]
    opening_ref[q, :, :wide] = x_ref[0, :FIX]
    opening_ref[q, :, wide : wide + size] = b_ref[0, :FIX]
    opening_ref[q, :, wide + size :] = c_ref[0, :FIX]
    weights_ref[q, :taps, :wide] = taps_x_ref[...]
    weights_ref[q, :taps, wide : wide + size] = taps_bc_ref[0]
    weights_ref[q, :taps, wide + size :] = taps_bc_ref[1]
    weights_ref[q, taps : taps + 1, :wide] = skip_ref[...]
    scores = lax.dot_general(
        c_conv, b_conv, (((1,), (1,)), ((), ())), preferred_element_type=jnp.float32
    )
    raw = dt_ref[0] + bias_ref[...]
    step = jnp.maximum(raw, 0.0) + jnp.log1p(jnp.exp(-jnp.abs(raw)))
    per_token = step * (-jnp.exp(alog_ref[...]))
    upper = lax.broadcasted_iota(jnp.int32, (length, length), 0) <= lax.broadcasted_iota(
        jnp.int32, (length, length), 1
    )
    sums = jnp.dot(
        three_terms(per_token).astype(jnp.bfloat16),
        upper.astype(jnp.float32).astype(jnp.bfloat16),
        preferred_element_type=jnp.float32,
    )
    total = (sums[:heads] + sums[heads : 2 * heads]) + sums[2 * heads :]
    total = total * LOG2_E
    row = total - jnp.log(step) * LOG2_E
    columns = total.T
    column_ref[q] = total
    causal = lax.broadcasted_iota(jnp.int32, (half, half), 0) >= lax.broadcasted_iota(
        jnp.int32, (half, half), 1
    )
    low = lax.broadcasted_iota(jnp.int32, (length, 2 * width), 1) < width
    for pair in range(heads // 2):
        lanes = slice(pair * 2 * width, (pair + 1) * 2 * width)
        x_conv = convolve(x_ref[0, :, lanes], taps_x_ref[:, lanes], pair)
        parts = []
        for head in (2 * pair, 2 * pair + 1):
            column = jnp.broadcast_to(columns[:, head : head + 1], (length, half))
            rows = row[head : head + 1, :]
            near = jnp.exp2(jnp.where(causal, column[:half] - rows[:, :half], -1e30))
            far = jnp.exp2(column[half:] - rows[:, :half])
            last = jnp.exp2(jnp.where(causal, column[half:] - rows[:, half:], -1e30))
            spot = slice(head * FIX, (head + 1) * FIX)
            first_ref[q, :half, spot] = near[:, :FIX]
            first_ref[q, half:, spot] = far[:, :FIX]
            top = (scores[:half, :half] * near).astype(jnp.bfloat16)
            left = (scores[half:, :half] * far).astype(jnp.bfloat16)
            right = (scores[half:, half:] * last).astype(jnp.bfloat16)
            below = jnp.concatenate([left, right], axis=1)
            parts.append(
                jnp.concatenate(
                    [
                        jnp.dot(top, x_conv[:half], preferred_element_type=jnp.float32),
                        jnp.dot(below, x_conv, preferred_element_type=jnp.float32),
                    ]
                )
            )
        mixed_ref[q, :, lanes] = jnp.where(low, parts[0], parts[1]) + skip_ref[
            :, lanes
        ] * x_conv.astype(jnp.float32)


def late_kernel(places, offset, heads, lines, reach, tail_at, place_ref, *refs):
    count = len(heads)
    tails, states, parts = refs[:4], refs[4 : 4 + 4 * count], refs[4 + 4 * count : -4]
    y_ref, padded, y_part, sems = refs[-4:]
    _, kids, length, wide = y_part.shape
    rows, heads = heads, sum(heads)
    width = wide // heads
    rows = [part * width for part in rows]
    low_first = lax.broadcasted_iota(jnp.int32, (FIX, 2 * width), 1) < width
    contract = (((1,), (1,)), ((), ()))

    def add(j, kid):
        q = place_ref[0] ^ j
        mixed_ref, held_ref, column_ref, first_ref, opening_ref, weights_ref = parts[
            6 * kid : 6 * kid + 6
        ]
        size = held_ref.shape[2]
        per_group = column_ref.shape[1]
        group_wide = opening_ref.shape[2] - 2 * size
        tail_rows = pl.ds(tail_at, -(-lines * reach // 16) * 16)
        tail = tails[places[0].index(j)][kid, tail_rows].astype(jnp.float32)
        blocks = [states[4 * n + places[1 + n].index(j)] for n in range(count)]
        state = jnp.concatenate([ref[kid, : rows[n]] for n, ref in enumerate(blocks)])

        def opening(start, stop, at):
            tap_rows = []
            for k in range(reach):
                first = k * lines + at
                count = (stop - start) // 128
                here = [tail[first + n : first + n + 1] for n in range(count)]
                tap_rows.append(jnp.concatenate(here, axis=1))
            return conv_silu(
                padded.at[j, kid, :, : stop - start],
                jnp.concatenate(tap_rows),
                opening_ref[q, :, start:stop],
                weights_ref[q, : reach + 1, start:stop],
            )

        bc_first = opening(group_wide, group_wide + 2 * size, lines - 2)
        b_first, c_first = bc_first[:, :size], bc_first[:, size:]
        start = offset * width
        x_all = opening(start, start + wide, start // 128).astype(jnp.float32)
        skipped = weights_ref[q, reach + 1 : reach + 2, start : start + wide] * x_all
        c_conv = jnp.concatenate([c_first, held_ref[q, FIX:]])
        terms = three_terms(jnp.exp2(column_ref[q]))
        terms = jnp.concatenate([terms, jnp.zeros((per_group, length), jnp.float32)])
        spread_row = lax.broadcasted_iota(jnp.int32, (4 * per_group, wide), 0)
        spread_lane = lax.broadcasted_iota(jnp.int32, (4 * per_group, wide), 1)
        spread = spread_row % per_group == offset + spread_lane // width
        grow = jnp.dot(
            terms.T.astype(jnp.bfloat16),
            spread.astype(jnp.float32).astype(jnp.bfloat16),
            preferred_element_type=jnp.float32,
        )
        term = lax.dot_general(c_conv, state, contract, preferred_element_type=jnp.float32)
        carried = (term * grow).astype(jnp.bfloat16)
        scores = lax.dot_general(
            c_conv,
            jnp.concatenate([b_first] * heads),
            contract,
            preferred_element_type=jnp.float32,
        )
        here = slice(offset * FIX, (offset + heads) * FIX)
        mixing = (scores * first_ref[q, :, here]).astype(jnp.bfloat16)
        for pair in range(heads // 2):
            lanes = slice(pair * 2 * width, (pair + 1) * 2 * width)
            x_first = x_all[:, lanes]
            stacked = [jnp.where(low_first, x_first, 0.0), jnp.where(low_first, 0.0, x_first)]
            if pair > 0:
                stacked = [jnp.zeros((2 * pair * FIX, 2 * width), jnp.float32)] + stacked
            if 2 * pair + 2 < heads:
                spare = (heads - 2 * pair - 2) * FIX
                stacked = stacked + [jnp.zeros((spare, 2 * width), jnp.float32)]
            part = jnp.dot(
                mixing,
                jnp.concatenate(stacked).astype(jnp.bfloat16),
                preferred_element_type=jnp.float32,
            )
            part = jnp.concatenate([part[:FIX] + skipped[:, lanes], part[FIX:]])
            whole = slice(start + lanes.start, start + lanes.stop)
            y_part[j, kid, :, lanes] = (
                mixed_ref[q, :, whole] + part + carried[:, lanes].astype(jnp.float32)
            ).astype(jnp.bfloat16)

    copies = []
    for j in range(4):
        for kid in range(kids):
            add(j, kid)
        start = (place_ref[0] ^ j) * (y_ref.shape[2] // 4) + offset * width
        lanes = pl.ds(pl.multiple_of(start, 128), wide)
        copies.append(pltpu.make_async_copy(y_part.at[j], y_ref.at[:, :, lanes], sems.at[j]))
        copies[-1].start()
    for copy in copies:
        copy.wait()


def cast_kernel(parts, tailed, reach, lines, *refs):
    count = len(tailed)
    ins, outs = refs[:-count], refs[-count:]
    states, tails = ins[: parts * count], ins[parts * count :]
    for j, out_ref in enumerate(outs):
        start = 0
        for at in range(parts):
            state = states[parts * j + at][0]
            rows = state.shape[0] * state.shape[1]
            out_ref[start : start + rows] = state.reshape(rows, state.shape[2]).astype(jnp.bfloat16)
            start += rows
            if at == 0 and tailed[j]:
                x_tail = tails[2 * j][0].astype(jnp.float32)
                bc_tail = tails[2 * j + 1][0].astype(jnp.float32)
                pieces = []
                for k in range(reach):
                    pieces += [x_tail[k : k + 1, i * 128 : i * 128 + 128] for i in range(lines - 2)]
                    pieces.append(bc_tail[k])
                spare = tailed[j] - lines * reach
                pieces.append(jnp.zeros((spare, 128), jnp.float32))
                out_ref[start : start + tailed[j]] = jnp.concatenate(pieces).astype(jnp.bfloat16)
                start += tailed[j]


def within_kernel(
    parent_ref,
    x_ref,
    b_ref,
    c_ref,
    dt_ref,
    bias_ref,
    alog_ref,
    skip_ref,
    taps_x_ref,
    taps_bc_ref,
    tail_x_ref,
    tail_bc_ref,
    mixed_ref,
    c_out_ref,
    grow_ref,
    padded,
):
    length = x_ref.shape[1]
    heads = dt_ref.shape[1]
    width = x_ref.shape[2] // heads
    b_conv = conv_silu(padded, tail_bc_ref[0, 0], b_ref[0], taps_bc_ref[0])
    c_conv = conv_silu(padded, tail_bc_ref[0, 1], c_ref[0], taps_bc_ref[1])
    c_out_ref[0] = c_conv
    scores = lax.dot_general(
        c_conv, b_conv, (((1,), (1,)), ((), ())), preferred_element_type=jnp.float32
    )
    raw = dt_ref[0] + bias_ref[...]
    step = jnp.maximum(raw, 0.0) + jnp.log1p(jnp.exp(-jnp.abs(raw)))
    per_token = step * (-jnp.exp(alog_ref[...]))
    row = lax.broadcasted_iota(jnp.int32, (length, length), 0)
    col = lax.broadcasted_iota(jnp.int32, (length, length), 1)
    upper = (row <= col).astype(jnp.float32)
    total = lax.dot_general(
        per_token,
        upper,
        (((1,), (0,)), ((), ())),
        precision=lax.Precision.HIGHEST,
        preferred_element_type=jnp.float32,
    )
    total_t = total.T
    grow_ref[0, 0] = jnp.exp(total_t)
    causal = row >= col
    low = lax.broadcasted_iota(jnp.int32, (length, 2 * width), 1) < width
    for pair in range(heads // 2):
        lanes = slice(pair * 2 * width, (pair + 1) * 2 * width)
        x_conv = conv_silu(
            padded, tail_x_ref[0, :, lanes], x_ref[0, :, lanes], taps_x_ref[:, lanes]
        )
        parts = []
        for head in (2 * pair, 2 * pair + 1):
            gap = total_t[:, head : head + 1] - total[head : head + 1, :]
            factor = jnp.exp(jnp.where(causal, gap, -1e30))
            mixing = (scores * factor * step[head : head + 1, :]).astype(jnp.bfloat16)
            parts.append(jnp.dot(mixing, x_conv, preferred_element_type=jnp.float32))
        mixed_ref[0, :, lanes] = (
            jnp.where(low, parts[0], parts[1]) + skip_ref[:, lanes] * x_conv.astype(jnp.float32)
        )


def carried_kernel(state_ref, c_ref, grow_ref, mixed_ref, y_ref):
    sources, _, part, width, size = state_ref.shape
    length = c_ref.shape[1]
    low = lax.broadcasted_iota(jnp.int32, (length, 2 * width), 1) < width
    c_conv = c_ref[0]
    for source in range(sources):
        state = state_ref[source, 0].reshape(part * width, size)
        term = lax.dot_general(
            c_conv, state, (((1,), (1,)), ((), ())), preferred_element_type=jnp.float32
        )
        for pair in range(part // 2):
            head = source * part + 2 * pair
            grow = jnp.where(
                low, grow_ref[0, 0, :, head : head + 1], grow_ref[0, 0, :, head + 1 : head + 2]
            )
            here = slice(2 * pair * width, (2 * pair + 2) * width)
            lanes = slice(head * width, (head + 2) * width)
            carried = (term[:, here] * grow).astype(jnp.bfloat16).astype(jnp.float32)
            y_ref[0, :, lanes] = (mixed_ref[0, :, lanes] + carried).astype(jnp.bfloat16)


def pick_kernel(parent_ref, state_ref, out_ref):
    out_ref[...] = state_ref[...]


def local_any(
    x_in,
    b_in,
    c_in,
    dt_in,
    dt_bias,
    a_log,
    d_skip,
    conv_x,
    conv_bc,
    par_state,
    tail_x,
    tail_bc,
    counts,
    order,
):
    kids, length, columns = x_in.shape
    heads = dt_in.shape[1]
    width, size = par_state.shape[2:]
    ways = lax.axis_size("batch")
    groups = b_in.shape[2] // size
    per_group = heads // groups
    part = heads // ways
    wide = per_group * width
    reach = tail_x.shape[1]
    parents_all = counts.shape[0]
    kids_all = order.shape[0]

    parent = parent_of(counts, order)
    own = lax.dynamic_slice_in_dim(parent, lax.axis_index("batch") * kids, kids)

    sent = par_state.astype(jnp.bfloat16).reshape(ways, part, width, size)
    shares = lax.all_to_all(sent, "batch", split_axis=0, concat_axis=0, tiled=True)

    tails = jnp.concatenate([tail_x.reshape(-1), tail_bc.reshape(-1)])
    tails = jnp.broadcast_to(tails[None], (ways, tails.shape[0]))
    tails = lax.all_to_all(tails, "batch", split_axis=0, concat_axis=0, tiled=True)
    tails_x = tails[:, : reach * columns].reshape(parents_all, reach, columns)
    tails_bc = tails[:, reach * columns :].reshape(parents_all, 2, reach, groups * size)

    picked = pl.pallas_call(
        pick_kernel,
        grid_spec=pltpu.PrefetchScalarGridSpec(
            num_scalar_prefetch=1,
            grid=(kids_all,),
            in_specs=[pl.BlockSpec((1, part, width, size), lambda i, p: (p[i], 0, 0, 0))],
            out_specs=pl.BlockSpec((1, part, width, size), lambda i, p: (i, 0, 0, 0)),
        ),
        out_shape=jax.ShapeDtypeStruct((kids_all, part, width, size), jnp.bfloat16),
        cost_estimate=pl.CostEstimate(
            flops=0, bytes_accessed=4 * kids_all * part * width * size, transcendentals=0
        ),
        name="pick_states",
    )(parent, shares)
    states = lax.all_to_all(
        picked.reshape(ways, kids, part, width, size), "batch", split_axis=0, concat_axis=0, tiled=True
    )

    skip_row = jnp.repeat(d_skip, width)[None, :]
    mixed, c_conv, grow = pl.pallas_call(
        within_kernel,
        grid_spec=pltpu.PrefetchScalarGridSpec(
            num_scalar_prefetch=1,
            grid=(kids, groups),
            in_specs=[
                pl.BlockSpec((1, length, wide), lambda c, q, p: (c, 0, q)),
                pl.BlockSpec((1, length, size), lambda c, q, p: (c, 0, q)),
                pl.BlockSpec((1, length, size), lambda c, q, p: (c, 0, q)),
                pl.BlockSpec((1, per_group, length), lambda c, q, p: (c, q, 0)),
                pl.BlockSpec((per_group, 1), lambda c, q, p: (q, 0)),
                pl.BlockSpec((per_group, 1), lambda c, q, p: (q, 0)),
                pl.BlockSpec((1, wide), lambda c, q, p: (0, q)),
                pl.BlockSpec((reach + 1, wide), lambda c, q, p: (0, q)),
                pl.BlockSpec((2, reach + 1, size), lambda c, q, p: (0, 0, q)),
                pl.BlockSpec((1, reach, wide), lambda c, q, p: (p[c], 0, q)),
                pl.BlockSpec((1, 2, reach, size), lambda c, q, p: (p[c], 0, 0, q)),
            ],
            out_specs=[
                pl.BlockSpec((1, length, wide), lambda c, q, p: (c, 0, q)),
                pl.BlockSpec((1, length, size), lambda c, q, p: (c, 0, q)),
                pl.BlockSpec((1, 1, length, per_group), lambda c, q, p: (c, q, 0, 0)),
            ],
            scratch_shapes=[pltpu.VMEM((8 + length, size), jnp.float32)],
        ),
        out_shape=[
            jax.ShapeDtypeStruct((kids, length, columns), jnp.float32),
            jax.ShapeDtypeStruct((kids, length, groups * size), jnp.bfloat16),
            jax.ShapeDtypeStruct((kids, groups, length, per_group), jnp.float32),
        ],
        compiler_params=pltpu.CompilerParams(vmem_limit_bytes=4 * VMEM_LIMIT),
        cost_estimate=pl.CostEstimate(
            flops=4 * kids * heads * length * length * width,
            bytes_accessed=6 * kids * length * columns,
            transcendentals=kids * heads * length * length,
        ),
        name="within",
    )(
        own,
        x_in,
        b_in,
        c_in,
        dt_in,
        dt_bias[:, None],
        a_log[:, None],
        skip_row,
        conv_x,
        conv_bc,
        tails_x,
        tails_bc,
    )

    sources = per_group // part
    return pl.pallas_call(
        carried_kernel,
        grid=(kids, groups),
        in_specs=[
            pl.BlockSpec((sources, 1, part, width, size), lambda c, q: (q, c, 0, 0, 0)),
            pl.BlockSpec((1, length, size), lambda c, q: (c, 0, q)),
            pl.BlockSpec((1, 1, length, per_group), lambda c, q: (c, q, 0, 0)),
            pl.BlockSpec((1, length, wide), lambda c, q: (c, 0, q)),
        ],
        out_specs=pl.BlockSpec((1, length, wide), lambda c, q: (c, 0, q)),
        out_shape=jax.ShapeDtypeStruct((kids, length, columns), jnp.bfloat16),
        compiler_params=pltpu.CompilerParams(vmem_limit_bytes=4 * VMEM_LIMIT),
        cost_estimate=pl.CostEstimate(
            flops=2 * kids * length * columns * size,
            bytes_accessed=8 * kids * length * columns,
            transcendentals=0,
        ),
        name="carried",
    )(states, c_conv, grow, mixed)


def local_halves(
    x_in, b_in, c_in, dt_in, dt_bias, a_log, d_skip, conv_x, conv_bc,
    par_state, tail_x, tail_bc, counts, order,
):
    kids, length, columns = x_in.shape
    heads = dt_in.shape[1]
    width, size = par_state.shape[2:]
    groups = b_in.shape[2] // size
    per_group = heads // groups
    wide = per_group * width
    taps = conv_x.shape[0]
    reach = taps - 1
    lines = (wide + 2 * size) // 128
    tail_lines = -(-lines * reach // 16) * 16
    params = pltpu.CompilerParams(vmem_limit_bytes=VMEM_LIMIT)
    anywhere = pl.BlockSpec(memory_space=pl.ANY)
    small = pl.CostEstimate(flops=1, bytes_accessed=1, transcendentals=0)

    stay = lambda x: pltpu.with_memory_space_constraint(x, pltpu.HBM)
    keep_in_vmem = lambda x: pltpu.with_memory_space_constraint(x, pltpu.VMEM)
    x_in, b_in, c_in, dt_in, conv_x, conv_bc = map(stay, (x_in, b_in, c_in, dt_in, conv_x, conv_bc))

    me = lax.axis_index("batch")
    parent = parent_of(counts, order)
    child = (jnp.arange(4 * kids, dtype=jnp.int32) // kids ^ me) * kids
    child = child + jnp.arange(4 * kids, dtype=jnp.int32) % kids
    catalog = jnp.arange(4 * 2 * kids, dtype=jnp.int32)
    owner = jnp.sum(jnp.where(child[:, None] == catalog[None, :], parent[None, :], 0), axis=1)
    slots = owner ^ me
    place = (me % 4).astype(jnp.int32)[None]

    state = stay(par_state.reshape(groups, per_group, width, size))
    x_tails, bc_tails = stay(tail_x), stay(tail_bc.transpose(0, 2, 1, 3))
    offsets = [sum(SPLIT[:k]) for k in range(len(SPLIT))]

    def swap(value, r):
        return lax.ppermute(value, "batch", perm=[(i, i ^ r) for i in range(8)])

    def cast():
        rows = per_group * width + tail_lines
        rows_a = SPLIT[0] * width + tail_lines
        blocks = [(0, SPLIT[0])] + [(at, 2) for at in range(SPLIT[0], per_group, 2)]
        count = len(blocks) + 2

        def kernel(place_ref, *refs):
            ins, outs = refs[: 4 * count], refs[4 * count :]
            quarters = [outs[0], outs[2].at[0], outs[1], outs[2].at[1]]
            for n, out_ref in enumerate(quarters):
                cast_kernel(
                    len(blocks), [tail_lines], reach, lines, *ins[count * n : count * n + count], out_ref
                )
                outs[3 + n // 2][n % 2] = out_ref[:rows_a]

        operands, specs = [], []
        for n in range(4):
            for offset, part in blocks:
                operands.append(state)
                specs.append(
                    pl.BlockSpec(
                        (1, part, width, size),
                        lambda i, p, n=n, at=offset // part: (p[0] ^ n, at, 0, 0),
                    )
                )
            operands += [x_tails, bc_tails]
            specs += [
                pl.BlockSpec((1, reach, wide), lambda i, p, n=n: (0, 0, p[0] ^ n)),
                pl.BlockSpec((1, reach, 2, size), lambda i, p, n=n: (0, 0, 0, p[0] ^ n)),
            ]
        shapes = [(rows, size)] * 2 + [(2, rows, size)] + [(2, rows_a, size)] * 2
        return pl.pallas_call(
            kernel,
            grid_spec=pltpu.PrefetchScalarGridSpec(
                num_scalar_prefetch=1,
                grid=(1,),
                in_specs=specs,
                out_specs=[pl.BlockSpec(memory_space=pltpu.VMEM)] * len(shapes),
            ),
            out_shape=[pltpu.VMEM(shape, jnp.bfloat16) for shape in shapes],
            compiler_params=params,
            cost_estimate=small,
            name="cast_states",
        )(place, *operands)

    def rearrange(scalars, sources, moves, shapes, tokens, name):
        def kernel(scalars_ref, *refs):
            held, outs = refs[: len(sources)], refs[len(sources) :]
            for out, at, scalar, choices in moves:
                for value, (number, take) in enumerate(choices):

                    def copy(out=out, at=at, number=number, take=take):
                        rows = held[number][...] if take is None else held[number][take]
                        if at is None:
                            outs[out][...] = rows
                        else:
                            outs[out][at] = rows

                    if scalar is None:
                        copy()
                    else:
                        pl.when(scalars_ref[scalar] == value)(copy)

        return pl.pallas_call(
            functools.partial(drop_tokens, kernel, 1 + len(sources), len(tokens)),
            grid_spec=pltpu.PrefetchScalarGridSpec(
                num_scalar_prefetch=1,
                grid=(1,),
                in_specs=[pl.BlockSpec(memory_space=pltpu.VMEM)] * len(sources)
                + [anywhere] * len(tokens),
                out_specs=[pl.BlockSpec(memory_space=pltpu.VMEM)] * len(shapes),
            ),
            out_shape=[pltpu.VMEM(shape, jnp.bfloat16) for shape in shapes],
            compiler_params=params,
            cost_estimate=small,
            name=name,
        )(scalars, *map(keep_in_vmem, sources), *tokens)

    def pick(rows, sources, choices, tokens, order=(1, 2, 3)):
        moves = [
            (j, kid, j * kids + kid, choices) for j in range(4) for kid in range(kids)
        ]
        picked = rearrange(
            slots, sources, moves, [(kids, rows, size)] * 4, tokens, "pick_states"
        )
        return [(0, picked[0])] + [(j, swap(picked[j], j)) for j in order]

    def early(c, pieces, piece, before, tokens):
        per = groups // pieces
        at = lambda q: (c, 0, per * piece + q)
        operands = [
            x_in, b_in, c_in, dt_in, dt_bias[:, None], a_log[:, None], skip_row, conv_x, conv_bc
        ]
        keep = len(operands)
        tokens = list(tokens) + [keep_in_vmem(a) for a in before]
        first = keep + len(tokens) - len(before)
        return pl.pallas_call(
            functools.partial(
                drop_tokens, functools.partial(early_kernel, per * piece), keep, len(tokens)
            ),
            grid=(per,),
            in_specs=[
                pl.BlockSpec((1, length, wide), at),
                pl.BlockSpec((1, length, size), at),
                pl.BlockSpec((1, length, size), at),
                pl.BlockSpec((1, per_group, length), lambda q: (c, per * piece + q, 0)),
                pl.BlockSpec((per_group, 1), lambda q: (per * piece + q, 0)),
                pl.BlockSpec((per_group, 1), lambda q: (per * piece + q, 0)),
                pl.BlockSpec((1, wide), lambda q: (0, per * piece + q)),
                pl.BlockSpec((taps, wide), lambda q: (0, per * piece + q)),
                pl.BlockSpec((2, taps, size), lambda q: (0, 0, per * piece + q)),
                *[anywhere] * len(tokens),
            ],
            out_specs=[pl.BlockSpec(memory_space=pltpu.VMEM)] * 6,
            out_shape=[
                pltpu.VMEM((groups, length, wide), jnp.float32),
                pltpu.VMEM((groups, length, size), jnp.bfloat16),
                pltpu.VMEM((groups, per_group, length), jnp.float32),
                pltpu.VMEM((groups, length, per_group * FIX), jnp.float32),
                pltpu.VMEM((groups, FIX, wide + 2 * size), jnp.bfloat16),
                pltpu.VMEM((groups, 8, wide + 2 * size), jnp.float32),
            ],
            input_output_aliases={first + i: i for i in range(len(before))},
            scratch_shapes=[pltpu.VMEM((2, 8 + length, size), jnp.float32)],
            compiler_params=params,
            cost_estimate=small,
            name="early",
        )(*operands, *tokens)

    def late(ks, states, parts, result, tokens):
        offset = offsets[ks[0]]
        chunk = sum(SPLIT[k] for k in ks) * width
        places = [[j for j, _ in chunk_states] for chunk_states in states]
        held = [array for chunk_states in states for _, array in chunk_states]
        operands = [keep_in_vmem(a) for a in (*held[:4], *sum((held[4 * k : 4 * k + 4] for k in ks), []), *parts[0], *parts[1])]
        specs = [pl.BlockSpec(memory_space=pltpu.VMEM)] * len(operands)
        keep = 1 + len(operands)
        operands += tokens
        specs += [anywhere] * len(tokens)
        alias = {}
        if result is not None:
            alias = {1 + len(operands): 0}
            operands.append(result)
            specs.append(anywhere)
        kernel = functools.partial(
            late_kernel, [places[0]] + [places[k] for k in ks], offset, [SPLIT[k] for k in ks], lines, reach, SPLIT[0] * width
        )
        return pl.pallas_call(
            functools.partial(drop_tokens, kernel, keep, 1 + len(operands) - keep),
            grid_spec=pltpu.PrefetchScalarGridSpec(
                num_scalar_prefetch=1,
                grid=(1,),
                in_specs=specs,
                out_specs=anywhere,
                scratch_shapes=[
                    pltpu.VMEM((groups, kids, 8 + FIX, max(chunk, 2 * size)), jnp.float32),
                    pltpu.VMEM((groups, kids, length, chunk), jnp.bfloat16),
                    pltpu.SemaphoreType.DMA((groups,)),
                ],
            ),
            out_shape=jax.ShapeDtypeStruct(x_in.shape, jnp.bfloat16),
            input_output_aliases=alias,
            compiler_params=params,
            cost_estimate=small,
            name="late",
        )(place, *operands)

    skip_row = jnp.repeat(d_skip, width)[None, :]
    rows = [SPLIT[0] * width + tail_lines] + [part * width for part in SPLIT[1:]]
    chunks = [pl.ds(sum(rows[:k]), rows[k]) for k in range(len(SPLIT))]
    own, own_2, own_13, sent_4, sent_6 = cast()
    crossed_a = [swap(sent_4, 4), swap(sent_6, 6)]
    along_y, along_z = swap(own_13, 1), swap(own_2, 2)
    parts = [early(0, 1, 0, [], [own, slots])]
    (turn,) = rearrange(
        place, [along_y], [(0, None, None, [(0, 1)])], [own.shape], [parts[0][1]], "stack_turn"
    )
    inside = [own, along_y, along_z, swap(turn, 2)]

    def inside_rows(k):
        return [(0, chunks[k]), (1, (0, chunks[k])), (2, chunks[k]), (3, chunks[k])]

    def cross(k, tokens):
        moves = [(0, j, None, [choice]) for j, choice in enumerate(inside_rows(k))]
        (sent,) = rearrange(place, inside, moves, [(4, rows[k], size)], tokens, "stack_later")
        return sent, swap(sent, 4)

    def pick_later(k, crossed, tokens):
        choices = inside_rows(k) + [(4, j) for j in range(4)]
        return pick(rows[k], [*inside, crossed], choices, tokens, (3, 2, 1))

    second = early(1, 2, 0, [], [turn])
    moves = [(n, None, None, [(n, 1)]) for n in range(2)]
    spread = rearrange(
        place, crossed_a, moves, [(rows[0], size)] * 2, [second[1]], "stack_first"
    )
    passed = [swap(spread[n], 1) for n in range(2)]
    sent_b, crossed_b = cross(1, [spread[0]])
    second = early(1, 2, 1, second, [sent_b])
    parts.append(second)
    choices = inside_rows(0) + [(4, 0), (6, None), (5, 0), (7, None)]
    states = [pick(rows[0], [*inside, *crossed_a, *passed], choices, [second[1]])]
    states.append(pick_later(1, crossed_b, [states[0][0][1]]))
    result = late([0], states, parts, None, [states[1][0][1]])
    return late([1], states, parts, result, [])


def solution(mesh):
    rows, cols = P(("groups", "batch"), None, "head"), P(("groups", "batch"), "head")
    placed = (
        rows, rows, rows, cols, P("head"), P("head"), P("head"), P(None, "head"),
        P(None, None, "head"), cols, rows, P(("groups", "batch"), None, None, "head"),
        P("groups"), P("groups"),
    )
    local = local_halves if mesh.shape["batch"] == 8 else local_any
    return jax.shard_map(local, mesh=mesh, in_specs=placed, out_specs=rows, check_vma=False)
```

```python
import functools

import jax
import jax.numpy as jnp
from jax import lax
from jax.experimental import pallas as pl
from jax.experimental.pallas import tpu as pltpu
from jax.sharding import PartitionSpec as P

VMEM_LIMIT = 12 * 1024 * 1024
SPLIT = (8, 4, 4)
FIX = 16
LOG2_E = 1.4426950408889634


def drop_tokens(kernel, keep, tokens, *refs):
    kernel(*refs[:keep], *refs[keep + tokens :])


def parent_of(counts, order):
    index = jnp.arange(counts.shape[0], dtype=jnp.int32)
    bounds = jnp.sum(jnp.where(index[None, :] <= index[:, None], counts[None, :], 0), axis=1)
    return jnp.sum((bounds[None, :] <= order[:, None]).astype(jnp.int32), axis=1)


def three_terms(value):
    terms = []
    for _ in range(3):
        terms.append(value.astype(jnp.bfloat16).astype(jnp.float32))
        value = value - terms[-1]
    return jnp.concatenate(terms)


def conv_silu(padded, tail, rows, taps):
    length = rows.shape[0]
    reach = taps.shape[0] - 1
    padded[8 - reach : 8, :] = jnp.broadcast_to(tail, (reach, rows.shape[1])).astype(jnp.float32)
    padded[8 : 8 + length, :] = rows.astype(jnp.float32)
    total = padded[8 - reach : 8 - reach + length, :] * taps[0:1, :]
    for k in range(1, reach + 1):
        total = total + padded[8 - reach + k : 8 - reach + k + length, :] * taps[k : k + 1, :]
    half = 0.5 * total
    return (half + half * jnp.tanh(half)).astype(jnp.bfloat16)


def early_kernel(
    base, x_ref, b_ref, c_ref, dt_ref, bias_ref, alog_ref, skip_ref, taps_x_ref, taps_bc_ref,
    mixed_ref, c_out_ref, column_ref, first_ref, opening_ref, weights_ref, padded,
):
    length, wide = x_ref.shape[1:]
    heads = dt_ref.shape[1]
    q = base + pl.program_id(0)
    width = wide // heads
    half = length // 2

    def convolve(rows, taps, slot):
        bulk = conv_silu(padded.at[slot % 2], 0.0, rows, taps)[FIX:]
        return jnp.concatenate([jnp.zeros((FIX, rows.shape[1]), jnp.bfloat16), bulk])

    b_conv = convolve(b_ref[0], taps_bc_ref[0], 0)
    c_conv = convolve(c_ref[0], taps_bc_ref[1], 1)
    c_out_ref[q] = c_conv
    size = b_ref.shape[2]
    taps = taps_x_ref.shape[0]
    opening_ref[q, :, :wide] = x_ref[0, :FIX]
    opening_ref[q, :, wide : wide + size] = b_ref[0, :FIX]
    opening_ref[q, :, wide + size :] = c_ref[0, :FIX]
    weights_ref[q, :taps, :wide] = taps_x_ref[...]
    weights_ref[q, :taps, wide : wide + size] = taps_bc_ref[0]
    weights_ref[q, :taps, wide + size :] = taps_bc_ref[1]
    weights_ref[q, taps : taps + 1, :wide] = skip_ref[...]
    scores = lax.dot_general(
        c_conv, b_conv, (((1,), (1,)), ((), ())), preferred_element_type=jnp.float32
    )
    raw = dt_ref[0] + bias_ref[...]
    step = jnp.maximum(raw, 0.0) + jnp.log1p(jnp.exp(-jnp.abs(raw)))
    per_token = step * (-jnp.exp(alog_ref[...]))
    upper = lax.broadcasted_iota(jnp.int32, (length, length), 0) <= lax.broadcasted_iota(
        jnp.int32, (length, length), 1
    )
    sums = jnp.dot(
        three_terms(per_token).astype(jnp.bfloat16),
        upper.astype(jnp.float32).astype(jnp.bfloat16),
        preferred_element_type=jnp.float32,
    )
    total = (sums[:heads] + sums[heads : 2 * heads]) + sums[2 * heads :]
    total = total * LOG2_E
    row = total - jnp.log(step) * LOG2_E
    columns = total.T
    column_ref[q] = total
    causal = lax.broadcasted_iota(jnp.int32, (half, half), 0) >= lax.broadcasted_iota(
        jnp.int32, (half, half), 1
    )
    low = lax.broadcasted_iota(jnp.int32, (length, 2 * width), 1) < width
    for pair in range(heads // 2):
        lanes = slice(pair * 2 * width, (pair + 1) * 2 * width)
        x_conv = convolve(x_ref[0, :, lanes], taps_x_ref[:, lanes], pair)
        parts = []
        for head in (2 * pair, 2 * pair + 1):
            column = jnp.broadcast_to(columns[:, head : head + 1], (length, half))
            rows = row[head : head + 1, :]
            near = jnp.exp2(jnp.where(causal, column[:half] - rows[:, :half], -1e30))
            far = jnp.exp2(column[half:] - rows[:, :half])
            last = jnp.exp2(jnp.where(causal, column[half:] - rows[:, half:], -1e30))
            spot = slice(head * FIX, (head + 1) * FIX)
            first_ref[q, :half, spot] = near[:, :FIX]
            first_ref[q, half:, spot] = far[:, :FIX]
            top = (scores[:half, :half] * near).astype(jnp.bfloat16)
            left = (scores[half:, :half] * far).astype(jnp.bfloat16)
            right = (scores[half:, half:] * last).astype(jnp.bfloat16)
            below = jnp.concatenate([left, right], axis=1)
            parts.append(
                jnp.concatenate(
                    [
                        jnp.dot(top, x_conv[:half], preferred_element_type=jnp.float32),
                        jnp.dot(below, x_conv, preferred_element_type=jnp.float32),
                    ]
                )
            )
        mixed_ref[q, :, lanes] = jnp.where(low, parts[0], parts[1]) + skip_ref[
            :, lanes
        ] * x_conv.astype(jnp.float32)


def late_kernel(places, offset, heads, lines, reach, tail_at, place_ref, *refs):
    count = len(heads)
    tails, states, parts = refs[:4], refs[4 : 4 + 4 * count], refs[4 + 4 * count : -4]
    y_ref, padded, y_part, sems = refs[-4:]
    _, kids, length, wide = y_part.shape
    rows, heads = heads, sum(heads)
    width = wide // heads
    rows = [part * width for part in rows]
    low_first = lax.broadcasted_iota(jnp.int32, (FIX, 2 * width), 1) < width
    contract = (((1,), (1,)), ((), ()))

    def add(j, kid):
        q = place_ref[0] ^ j
        mixed_ref, held_ref, column_ref, first_ref, opening_ref, weights_ref = parts[
            6 * kid : 6 * kid + 6
        ]
        size = held_ref.shape[2]
        per_group = column_ref.shape[1]
        group_wide = opening_ref.shape[2] - 2 * size
        tail_rows = pl.ds(tail_at, -(-lines * reach // 16) * 16)
        tail = tails[places[0].index(j)][kid, tail_rows].astype(jnp.float32)
        blocks = [states[4 * n + places[1 + n].index(j)] for n in range(count)]
        state = jnp.concatenate([ref[kid, : rows[n]] for n, ref in enumerate(blocks)])

        def opening(start, stop, at):
            tap_rows = []
            for k in range(reach):
                first = k * lines + at
                count = (stop - start) // 128
                here = [tail[first + n : first + n + 1] for n in range(count)]
                tap_rows.append(jnp.concatenate(here, axis=1))
            return conv_silu(
                padded.at[j, kid, :, : stop - start],
                jnp.concatenate(tap_rows),
                opening_ref[q, :, start:stop],
                weights_ref[q, : reach + 1, start:stop],
            )

        bc_first = opening(group_wide, group_wide + 2 * size, lines - 2)
        b_first, c_first = bc_first[:, :size], bc_first[:, size:]
        start = offset * width
        x_all = opening(start, start + wide, start // 128).astype(jnp.float32)
        skipped = weights_ref[q, reach + 1 : reach + 2, start : start + wide] * x_all
        c_conv = jnp.concatenate([c_first, held_ref[q, FIX:]])
        terms = three_terms(jnp.exp2(column_ref[q]))
        terms = jnp.concatenate([terms, jnp.zeros((per_group, length), jnp.float32)])
        spread_row = lax.broadcasted_iota(jnp.int32, (4 * per_group, wide), 0)
        spread_lane = lax.broadcasted_iota(jnp.int32, (4 * per_group, wide), 1)
        spread = spread_row % per_group == offset + spread_lane // width
        grow = jnp.dot(
            terms.T.astype(jnp.bfloat16),
            spread.astype(jnp.float32).astype(jnp.bfloat16),
            preferred_element_type=jnp.float32,
        )
        term = lax.dot_general(c_conv, state, contract, preferred_element_type=jnp.float32)
        carried = (term * grow).astype(jnp.bfloat16)
        scores = lax.dot_general(
            c_conv,
            jnp.concatenate([b_first] * heads),
            contract,
            preferred_element_type=jnp.float32,
        )
        here = slice(offset * FIX, (offset + heads) * FIX)
        mixing = (scores * first_ref[q, :, here]).astype(jnp.bfloat16)
        for pair in range(heads // 2):
            lanes = slice(pair * 2 * width, (pair + 1) * 2 * width)
            x_first = x_all[:, lanes]
            stacked = [jnp.where(low_first, x_first, 0.0), jnp.where(low_first, 0.0, x_first)]
            if pair > 0:
                stacked = [jnp.zeros((2 * pair * FIX, 2 * width), jnp.float32)] + stacked
            if 2 * pair + 2 < heads:
                spare = (heads - 2 * pair - 2) * FIX
                stacked = stacked + [jnp.zeros((spare, 2 * width), jnp.float32)]
            part = jnp.dot(
                mixing,
                jnp.concatenate(stacked).astype(jnp.bfloat16),
                preferred_element_type=jnp.float32,
            )
            part = jnp.concatenate([part[:FIX] + skipped[:, lanes], part[FIX:]])
            whole = slice(start + lanes.start, start + lanes.stop)
            y_part[j, kid, :, lanes] = (
                mixed_ref[q, :, whole] + part + carried[:, lanes].astype(jnp.float32)
            ).astype(jnp.bfloat16)

    copies = []
    for j in range(4):
        for kid in range(kids):
            add(j, kid)
        start = (place_ref[0] ^ j) * (y_ref.shape[2] // 4) + offset * width
        lanes = pl.ds(pl.multiple_of(start, 128), wide)
        copies.append(pltpu.make_async_copy(y_part.at[j], y_ref.at[:, :, lanes], sems.at[j]))
        copies[-1].start()
    for copy in copies:
        copy.wait()


def cast_kernel(parts, tailed, reach, lines, *refs):
    count = len(tailed)
    ins, outs = refs[:-count], refs[-count:]
    states, tails = ins[: parts * count], ins[parts * count :]
    for j, out_ref in enumerate(outs):
        start = 0
        for at in range(parts):
            state = states[parts * j + at][0]
            rows = state.shape[0] * state.shape[1]
            out_ref[start : start + rows] = state.reshape(rows, state.shape[2]).astype(jnp.bfloat16)
            start += rows
            if at == 0 and tailed[j]:
                x_tail = tails[2 * j][0].astype(jnp.float32)
                bc_tail = tails[2 * j + 1][0].astype(jnp.float32)
                pieces = []
                for k in range(reach):
                    pieces += [x_tail[k : k + 1, i * 128 : i * 128 + 128] for i in range(lines - 2)]
                    pieces.append(bc_tail[k])
                spare = tailed[j] - lines * reach
                pieces.append(jnp.zeros((spare, 128), jnp.float32))
                out_ref[start : start + tailed[j]] = jnp.concatenate(pieces).astype(jnp.bfloat16)
                start += tailed[j]


def within_kernel(
    parent_ref,
    x_ref,
    b_ref,
    c_ref,
    dt_ref,
    bias_ref,
    alog_ref,
    skip_ref,
    taps_x_ref,
    taps_bc_ref,
    tail_x_ref,
    tail_bc_ref,
    mixed_ref,
    c_out_ref,
    grow_ref,
    padded,
):
    length = x_ref.shape[1]
    heads = dt_ref.shape[1]
    width = x_ref.shape[2] // heads
    b_conv = conv_silu(padded, tail_bc_ref[0, 0], b_ref[0], taps_bc_ref[0])
    c_conv = conv_silu(padded, tail_bc_ref[0, 1], c_ref[0], taps_bc_ref[1])
    c_out_ref[0] = c_conv
    scores = lax.dot_general(
        c_conv, b_conv, (((1,), (1,)), ((), ())), preferred_element_type=jnp.float32
    )
    raw = dt_ref[0] + bias_ref[...]
    step = jnp.maximum(raw, 0.0) + jnp.log1p(jnp.exp(-jnp.abs(raw)))
    per_token = step * (-jnp.exp(alog_ref[...]))
    row = lax.broadcasted_iota(jnp.int32, (length, length), 0)
    col = lax.broadcasted_iota(jnp.int32, (length, length), 1)
    upper = (row <= col).astype(jnp.float32)
    total = lax.dot_general(
        per_token,
        upper,
        (((1,), (0,)), ((), ())),
        precision=lax.Precision.HIGHEST,
        preferred_element_type=jnp.float32,
    )
    total_t = total.T
    grow_ref[0, 0] = jnp.exp(total_t)
    causal = row >= col
    low = lax.broadcasted_iota(jnp.int32, (length, 2 * width), 1) < width
    for pair in range(heads // 2):
        lanes = slice(pair * 2 * width, (pair + 1) * 2 * width)
        x_conv = conv_silu(
            padded, tail_x_ref[0, :, lanes], x_ref[0, :, lanes], taps_x_ref[:, lanes]
        )
        parts = []
        for head in (2 * pair, 2 * pair + 1):
            gap = total_t[:, head : head + 1] - total[head : head + 1, :]
            factor = jnp.exp(jnp.where(causal, gap, -1e30))
            mixing = (scores * factor * step[head : head + 1, :]).astype(jnp.bfloat16)
            parts.append(jnp.dot(mixing, x_conv, preferred_element_type=jnp.float32))
        mixed_ref[0, :, lanes] = (
            jnp.where(low, parts[0], parts[1]) + skip_ref[:, lanes] * x_conv.astype(jnp.float32)
        )


def carried_kernel(state_ref, c_ref, grow_ref, mixed_ref, y_ref):
    sources, _, part, width, size = state_ref.shape
    length = c_ref.shape[1]
    low = lax.broadcasted_iota(jnp.int32, (length, 2 * width), 1) < width
    c_conv = c_ref[0]
    for source in range(sources):
        state = state_ref[source, 0].reshape(part * width, size)
        term = lax.dot_general(
            c_conv, state, (((1,), (1,)), ((), ())), preferred_element_type=jnp.float32
        )
        for pair in range(part // 2):
            head = source * part + 2 * pair
            grow = jnp.where(
                low, grow_ref[0, 0, :, head : head + 1], grow_ref[0, 0, :, head + 1 : head + 2]
            )
            here = slice(2 * pair * width, (2 * pair + 2) * width)
            lanes = slice(head * width, (head + 2) * width)
            carried = (term[:, here] * grow).astype(jnp.bfloat16).astype(jnp.float32)
            y_ref[0, :, lanes] = (mixed_ref[0, :, lanes] + carried).astype(jnp.bfloat16)


def pick_kernel(parent_ref, state_ref, out_ref):
    out_ref[...] = state_ref[...]


def local_any(
    x_in,
    b_in,
    c_in,
    dt_in,
    dt_bias,
    a_log,
    d_skip,
    conv_x,
    conv_bc,
    par_state,
    tail_x,
    tail_bc,
    counts,
    order,
):
    kids, length, columns = x_in.shape
    heads = dt_in.shape[1]
    width, size = par_state.shape[2:]
    ways = lax.axis_size("batch")
    groups = b_in.shape[2] // size
    per_group = heads // groups
    part = heads // ways
    wide = per_group * width
    reach = tail_x.shape[1]
    parents_all = counts.shape[0]
    kids_all = order.shape[0]

    parent = parent_of(counts, order)
    own = lax.dynamic_slice_in_dim(parent, lax.axis_index("batch") * kids, kids)

    sent = par_state.astype(jnp.bfloat16).reshape(ways, part, width, size)
    shares = lax.all_to_all(sent, "batch", split_axis=0, concat_axis=0, tiled=True)

    tails = jnp.concatenate([tail_x.reshape(-1), tail_bc.reshape(-1)])
    tails = jnp.broadcast_to(tails[None], (ways, tails.shape[0]))
    tails = lax.all_to_all(tails, "batch", split_axis=0, concat_axis=0, tiled=True)
    tails_x = tails[:, : reach * columns].reshape(parents_all, reach, columns)
    tails_bc = tails[:, reach * columns :].reshape(parents_all, 2, reach, groups * size)

    picked = pl.pallas_call(
        pick_kernel,
        grid_spec=pltpu.PrefetchScalarGridSpec(
            num_scalar_prefetch=1,
            grid=(kids_all,),
            in_specs=[pl.BlockSpec((1, part, width, size), lambda i, p: (p[i], 0, 0, 0))],
            out_specs=pl.BlockSpec((1, part, width, size), lambda i, p: (i, 0, 0, 0)),
        ),
        out_shape=jax.ShapeDtypeStruct((kids_all, part, width, size), jnp.bfloat16),
        cost_estimate=pl.CostEstimate(
            flops=0, bytes_accessed=4 * kids_all * part * width * size, transcendentals=0
        ),
        name="pick_states",
    )(parent, shares)
    states = lax.all_to_all(
        picked.reshape(ways, kids, part, width, size), "batch", split_axis=0, concat_axis=0, tiled=True
    )

    skip_row = jnp.repeat(d_skip, width)[None, :]
    mixed, c_conv, grow = pl.pallas_call(
        within_kernel,
        grid_spec=pltpu.PrefetchScalarGridSpec(
            num_scalar_prefetch=1,
            grid=(kids, groups),
            in_specs=[
                pl.BlockSpec((1, length, wide), lambda c, q, p: (c, 0, q)),
                pl.BlockSpec((1, length, size), lambda c, q, p: (c, 0, q)),
                pl.BlockSpec((1, length, size), lambda c, q, p: (c, 0, q)),
                pl.BlockSpec((1, per_group, length), lambda c, q, p: (c, q, 0)),
                pl.BlockSpec((per_group, 1), lambda c, q, p: (q, 0)),
                pl.BlockSpec((per_group, 1), lambda c, q, p: (q, 0)),
                pl.BlockSpec((1, wide), lambda c, q, p: (0, q)),
                pl.BlockSpec((reach + 1, wide), lambda c, q, p: (0, q)),
                pl.BlockSpec((2, reach + 1, size), lambda c, q, p: (0, 0, q)),
                pl.BlockSpec((1, reach, wide), lambda c, q, p: (p[c], 0, q)),
                pl.BlockSpec((1, 2, reach, size), lambda c, q, p: (p[c], 0, 0, q)),
            ],
            out_specs=[
                pl.BlockSpec((1, length, wide), lambda c, q, p: (c, 0, q)),
                pl.BlockSpec((1, length, size), lambda c, q, p: (c, 0, q)),
                pl.BlockSpec((1, 1, length, per_group), lambda c, q, p: (c, q, 0, 0)),
            ],
            scratch_shapes=[pltpu.VMEM((8 + length, size), jnp.float32)],
        ),
        out_shape=[
            jax.ShapeDtypeStruct((kids, length, columns), jnp.float32),
            jax.ShapeDtypeStruct((kids, length, groups * size), jnp.bfloat16),
            jax.ShapeDtypeStruct((kids, groups, length, per_group), jnp.float32),
        ],
        compiler_params=pltpu.CompilerParams(vmem_limit_bytes=4 * VMEM_LIMIT),
        cost_estimate=pl.CostEstimate(
            flops=4 * kids * heads * length * length * width,
            bytes_accessed=6 * kids * length * columns,
            transcendentals=kids * heads * length * length,
        ),
        name="within",
    )(
        own,
        x_in,
        b_in,
        c_in,
        dt_in,
        dt_bias[:, None],
        a_log[:, None],
        skip_row,
        conv_x,
        conv_bc,
        tails_x,
        tails_bc,
    )

    sources = per_group // part
    return pl.pallas_call(
        carried_kernel,
        grid=(kids, groups),
        in_specs=[
            pl.BlockSpec((sources, 1, part, width, size), lambda c, q: (q, c, 0, 0, 0)),
            pl.BlockSpec((1, length, size), lambda c, q: (c, 0, q)),
            pl.BlockSpec((1, 1, length, per_group), lambda c, q: (c, q, 0, 0)),
            pl.BlockSpec((1, length, wide), lambda c, q: (c, 0, q)),
        ],
        out_specs=pl.BlockSpec((1, length, wide), lambda c, q: (c, 0, q)),
        out_shape=jax.ShapeDtypeStruct((kids, length, columns), jnp.bfloat16),
        compiler_params=pltpu.CompilerParams(vmem_limit_bytes=4 * VMEM_LIMIT),
        cost_estimate=pl.CostEstimate(
            flops=2 * kids * length * columns * size,
            bytes_accessed=8 * kids * length * columns,
            transcendentals=0,
        ),
        name="carried",
    )(states, c_conv, grow, mixed)


def local_halves(
    x_in, b_in, c_in, dt_in, dt_bias, a_log, d_skip, conv_x, conv_bc,
    par_state, tail_x, tail_bc, counts, order,
):
    kids, length, columns = x_in.shape
    heads = dt_in.shape[1]
    width, size = par_state.shape[2:]
    groups = b_in.shape[2] // size
    per_group = heads // groups
    wide = per_group * width
    taps = conv_x.shape[0]
    reach = taps - 1
    lines = (wide + 2 * size) // 128
    tail_lines = -(-lines * reach // 16) * 16
    params = pltpu.CompilerParams(vmem_limit_bytes=VMEM_LIMIT)
    anywhere = pl.BlockSpec(memory_space=pl.ANY)
    small = pl.CostEstimate(flops=1, bytes_accessed=1, transcendentals=0)

    stay = lambda x: pltpu.with_memory_space_constraint(x, pltpu.HBM)
    keep_in_vmem = lambda x: pltpu.with_memory_space_constraint(x, pltpu.VMEM)
    x_in, b_in, c_in, dt_in, conv_x, conv_bc = map(stay, (x_in, b_in, c_in, dt_in, conv_x, conv_bc))

    me = lax.axis_index("batch")
    parent = parent_of(counts, order)
    child = (jnp.arange(4 * kids, dtype=jnp.int32) // kids ^ me) * kids
    child = child + jnp.arange(4 * kids, dtype=jnp.int32) % kids
    catalog = jnp.arange(4 * 2 * kids, dtype=jnp.int32)
    owner = jnp.sum(jnp.where(child[:, None] == catalog[None, :], parent[None, :], 0), axis=1)
    slots = owner ^ me
    place = (me % 4).astype(jnp.int32)[None]

    state = stay(par_state.reshape(groups, per_group, width, size))
    x_tails, bc_tails = stay(tail_x), stay(tail_bc.transpose(0, 2, 1, 3))
    offsets = [sum(SPLIT[:k]) for k in range(len(SPLIT))]

    def swap(value, r):
        return lax.ppermute(value, "batch", perm=[(i, i ^ r) for i in range(8)])

    def cast():
        rows = per_group * width + tail_lines
        rows_a = SPLIT[0] * width + tail_lines
        blocks = [(0, SPLIT[0])] + [(at, 4) for at in range(SPLIT[0], per_group, 4)]
        count = len(blocks) + 2

        def kernel(place_ref, *refs):
            ins, outs = refs[: 4 * count], refs[4 * count :]
            quarters = [outs[0], outs[2].at[0], outs[1], outs[2].at[1]]
            for n, out_ref in enumerate(quarters):
                cast_kernel(
                    len(blocks), [tail_lines], reach, lines, *ins[count * n : count * n + count], out_ref
                )
                outs[3 + n // 2][n % 2] = out_ref[:rows_a]

        operands, specs = [], []
        for n in range(4):
            for offset, part in blocks:
                operands.append(state)
                specs.append(
                    pl.BlockSpec(
                        (1, part, width, size),
                        lambda i, p, n=n, at=offset // part: (p[0] ^ n, at, 0, 0),
                    )
                )
            operands += [x_tails, bc_tails]
            specs += [
                pl.BlockSpec((1, reach, wide), lambda i, p, n=n: (0, 0, p[0] ^ n)),
                pl.BlockSpec((1, reach, 2, size), lambda i, p, n=n: (0, 0, 0, p[0] ^ n)),
            ]
        shapes = [(rows, size)] * 2 + [(2, rows, size)] + [(2, rows_a, size)] * 2
        return pl.pallas_call(
            kernel,
            grid_spec=pltpu.PrefetchScalarGridSpec(
                num_scalar_prefetch=1,
                grid=(1,),
                in_specs=specs,
                out_specs=[pl.BlockSpec(memory_space=pltpu.VMEM)] * len(shapes),
            ),
            out_shape=[pltpu.VMEM(shape, jnp.bfloat16) for shape in shapes],
            compiler_params=params,
            cost_estimate=small,
            name="cast_states",
        )(place, *operands)

    def rearrange(scalars, sources, moves, shapes, tokens, name):
        def kernel(scalars_ref, *refs):
            held, outs = refs[: len(sources)], refs[len(sources) :]
            for out, at, scalar, choices in moves:
                for value, (number, take) in enumerate(choices):

                    def copy(out=out, at=at, number=number, take=take):
                        rows = held[number][...] if take is None else held[number][take]
                        if at is None:
                            outs[out][...] = rows
                        else:
                            outs[out][at] = rows

                    if scalar is None:
                        copy()
                    else:
                        pl.when(scalars_ref[scalar] == value)(copy)

        return pl.pallas_call(
            functools.partial(drop_tokens, kernel, 1 + len(sources), len(tokens)),
            grid_spec=pltpu.PrefetchScalarGridSpec(
                num_scalar_prefetch=1,
                grid=(1,),
                in_specs=[pl.BlockSpec(memory_space=pltpu.VMEM)] * len(sources)
                + [anywhere] * len(tokens),
                out_specs=[pl.BlockSpec(memory_space=pltpu.VMEM)] * len(shapes),
            ),
            out_shape=[pltpu.VMEM(shape, jnp.bfloat16) for shape in shapes],
            compiler_params=params,
            cost_estimate=small,
            name=name,
        )(scalars, *map(keep_in_vmem, sources), *tokens)

    def pick(rows, sources, choices, tokens, order=(1, 2, 3)):
        moves = [
            (j, kid, j * kids + kid, choices) for j in range(4) for kid in range(kids)
        ]
        picked = rearrange(
            slots, sources, moves, [(kids, rows, size)] * 4, tokens, "pick_states"
        )
        return [(0, picked[0])] + [(j, swap(picked[j], j)) for j in order]

    def early(c, pieces, piece, before, tokens):
        per = groups // pieces
        at = lambda q: (c, 0, per * piece + q)
        operands = [
            x_in, b_in, c_in, dt_in, dt_bias[:, None], a_log[:, None], skip_row, conv_x, conv_bc
        ]
        keep = len(operands)
        tokens = list(tokens) + [keep_in_vmem(a) for a in before]
        first = keep + len(tokens) - len(before)
        return pl.pallas_call(
            functools.partial(
                drop_tokens, functools.partial(early_kernel, per * piece), keep, len(tokens)
            ),
            grid=(per,),
            in_specs=[
                pl.BlockSpec((1, length, wide), at),
                pl.BlockSpec((1, length, size), at),
                pl.BlockSpec((1, length, size), at),
                pl.BlockSpec((1, per_group, length), lambda q: (c, per * piece + q, 0)),
                pl.BlockSpec((per_group, 1), lambda q: (per * piece + q, 0)),
                pl.BlockSpec((per_group, 1), lambda q: (per * piece + q, 0)),
                pl.BlockSpec((1, wide), lambda q: (0, per * piece + q)),
                pl.BlockSpec((taps, wide), lambda q: (0, per * piece + q)),
                pl.BlockSpec((2, taps, size), lambda q: (0, 0, per * piece + q)),
                *[anywhere] * len(tokens),
            ],
            out_specs=[pl.BlockSpec(memory_space=pltpu.VMEM)] * 6,
            out_shape=[
                pltpu.VMEM((groups, length, wide), jnp.float32),
                pltpu.VMEM((groups, length, size), jnp.bfloat16),
                pltpu.VMEM((groups, per_group, length), jnp.float32),
                pltpu.VMEM((groups, length, per_group * FIX), jnp.float32),
                pltpu.VMEM((groups, FIX, wide + 2 * size), jnp.bfloat16),
                pltpu.VMEM((groups, 8, wide + 2 * size), jnp.float32),
            ],
            input_output_aliases={first + i: i for i in range(len(before))},
            scratch_shapes=[pltpu.VMEM((2, 8 + length, size), jnp.float32)],
            compiler_params=params,
            cost_estimate=small,
            name="early",
        )(*operands, *tokens)

    def late(ks, states, parts, result, tokens):
        offset = offsets[ks[0]]
        chunk = sum(SPLIT[k] for k in ks) * width
        places = [[j for j, _ in chunk_states] for chunk_states in states]
        held = [array for chunk_states in states for _, array in chunk_states]
        operands = [keep_in_vmem(a) for a in (*held[:4], *sum((held[4 * k : 4 * k + 4] for k in ks), []), *parts[0], *parts[1])]
        specs = [pl.BlockSpec(memory_space=pltpu.VMEM)] * len(operands)
        keep = 1 + len(operands)
        operands += tokens
        specs += [anywhere] * len(tokens)
        alias = {}
        if result is not None:
            alias = {1 + len(operands): 0}
            operands.append(result)
            specs.append(anywhere)
        kernel = functools.partial(
            late_kernel, [places[0]] + [places[k] for k in ks], offset, [SPLIT[k] for k in ks], lines, reach, SPLIT[0] * width
        )
        return pl.pallas_call(
            functools.partial(drop_tokens, kernel, keep, 1 + len(operands) - keep),
            grid_spec=pltpu.PrefetchScalarGridSpec(
                num_scalar_prefetch=1,
                grid=(1,),
                in_specs=specs,
                out_specs=anywhere,
                scratch_shapes=[
                    pltpu.VMEM((groups, kids, 8 + FIX, max(chunk, 2 * size)), jnp.float32),
                    pltpu.VMEM((groups, kids, length, chunk), jnp.bfloat16),
                    pltpu.SemaphoreType.DMA((groups,)),
                ],
            ),
            out_shape=jax.ShapeDtypeStruct(x_in.shape, jnp.bfloat16),
            input_output_aliases=alias,
            compiler_params=params,
            cost_estimate=small,
            name="late",
        )(place, *operands)

    skip_row = jnp.repeat(d_skip, width)[None, :]
    rows = [SPLIT[0] * width + tail_lines] + [part * width for part in SPLIT[1:]]
    chunks = [pl.ds(sum(rows[:k]), rows[k]) for k in range(len(SPLIT))]
    own, own_2, own_13, sent_4, sent_6 = cast()
    crossed_a = [swap(sent_4, 4), swap(sent_6, 6)]
    along_y, along_z = swap(own_13, 1), swap(own_2, 2)
    parts = [early(0, 1, 0, [], [own, slots])]
    (turn,) = rearrange(
        place, [along_y], [(0, None, None, [(0, 1)])], [own.shape], [parts[0][1]], "stack_turn"
    )
    inside = [own, along_y, along_z, swap(turn, 2)]

    def inside_rows(k):
        return [(0, chunks[k]), (1, (0, chunks[k])), (2, chunks[k]), (3, chunks[k])]

    def cross(k, tokens):
        moves = [(0, j, None, [choice]) for j, choice in enumerate(inside_rows(k))]
        (sent,) = rearrange(place, inside, moves, [(4, rows[k], size)], tokens, "stack_later")
        return sent, swap(sent, 4)

    def pick_later(k, crossed, tokens):
        choices = inside_rows(k) + [(4, j) for j in range(4)]
        return pick(rows[k], [*inside, crossed], choices, tokens, (3, 2, 1))

    second = early(1, 2, 0, [], [turn])
    moves = [(0, n, None, [(n, 1)]) for n in range(2)]
    (spread,) = rearrange(
        place, crossed_a, moves, [(2, rows[0], size)], [second[1]], "stack_first"
    )
    passed = swap(spread, 1)
    sent_b, crossed_b = cross(1, [spread])
    second = early(1, 2, 1, second, [sent_b])
    parts.append(second)
    choices = inside_rows(0) + [(4, 0), (6, 0), (5, 0), (6, 1)]
    states = [pick(rows[0], [*inside, *crossed_a, passed], choices, [second[1]])]
    sent_c, crossed_c = cross(2, [states[0][0][1], crossed_b])
    states.append(pick_later(1, crossed_b, [sent_c]))
    states.append(pick_later(2, crossed_c, [states[1][0][1]]))
    result = late([0], states, parts, None, [states[2][0][1]])
    return late([1, 2], states, parts, result, [])


def solution(mesh):
    rows, cols = P(("groups", "batch"), None, "head"), P(("groups", "batch"), "head")
    placed = (
        rows, rows, rows, cols, P("head"), P("head"), P("head"), P(None, "head"),
        P(None, None, "head"), cols, rows, P(("groups", "batch"), None, None, "head"),
        P("groups"), P("groups"),
    )
    local = local_halves if mesh.shape["batch"] == 8 else local_any
    return jax.shard_map(local, mesh=mesh, in_specs=placed, out_specs=rows, check_vma=False)
```

```python
import functools

import jax
import jax.numpy as jnp
from jax import lax
from jax.experimental import pallas as pl
from jax.experimental.pallas import tpu as pltpu
from jax.sharding import PartitionSpec as P

VMEM_LIMIT = 12 * 1024 * 1024
SPLIT = (8, 4, 4)
FIX = 16
LOG2_E = 1.4426950408889634


def drop_tokens(kernel, keep, tokens, *refs):
    kernel(*refs[:keep], *refs[keep + tokens :])


def parent_of(counts, order):
    index = jnp.arange(counts.shape[0], dtype=jnp.int32)
    bounds = jnp.sum(jnp.where(index[None, :] <= index[:, None], counts[None, :], 0), axis=1)
    return jnp.sum((bounds[None, :] <= order[:, None]).astype(jnp.int32), axis=1)


def three_terms(value):
    terms = []
    for _ in range(3):
        terms.append(value.astype(jnp.bfloat16).astype(jnp.float32))
        value = value - terms[-1]
    return jnp.concatenate(terms)


def conv_silu(padded, tail, rows, taps):
    length = rows.shape[0]
    reach = taps.shape[0] - 1
    padded[8 - reach : 8, :] = jnp.broadcast_to(tail, (reach, rows.shape[1])).astype(jnp.float32)
    padded[8 : 8 + length, :] = rows.astype(jnp.float32)
    total = padded[8 - reach : 8 - reach + length, :] * taps[0:1, :]
    for k in range(1, reach + 1):
        total = total + padded[8 - reach + k : 8 - reach + k + length, :] * taps[k : k + 1, :]
    half = 0.5 * total
    return (half + half * jnp.tanh(half)).astype(jnp.bfloat16)


def early_kernel(
    base, x_ref, b_ref, c_ref, dt_ref, bias_ref, alog_ref, skip_ref, taps_x_ref, taps_bc_ref,
    mixed_ref, c_out_ref, column_ref, first_ref, opening_ref, weights_ref, padded,
):
    length, wide = x_ref.shape[1:]
    heads = dt_ref.shape[1]
    q = base + pl.program_id(0)
    width = wide // heads
    half = length // 2

    def convolve(rows, taps, slot):
        bulk = conv_silu(padded.at[slot % 2], 0.0, rows, taps)[FIX:]
        return jnp.concatenate([jnp.zeros((FIX, rows.shape[1]), jnp.bfloat16), bulk])

    b_conv = convolve(b_ref[0], taps_bc_ref[0], 0)
    c_conv = convolve(c_ref[0], taps_bc_ref[1], 1)
    c_out_ref[q] = c_conv
    size = b_ref.shape[2]
    taps = taps_x_ref.shape[0]
    opening_ref[q, :, :wide] = x_ref[0, :FIX]
    opening_ref[q, :, wide : wide + size] = b_ref[0, :FIX]
    opening_ref[q, :, wide + size :] = c_ref[0, :FIX]
    weights_ref[q, :taps, :wide] = taps_x_ref[...]
    weights_ref[q, :taps, wide : wide + size] = taps_bc_ref[0]
    weights_ref[q, :taps, wide + size :] = taps_bc_ref[1]
    weights_ref[q, taps : taps + 1, :wide] = skip_ref[...]
    scores = lax.dot_general(
        c_conv, b_conv, (((1,), (1,)), ((), ())), preferred_element_type=jnp.float32
    )
    raw = dt_ref[0] + bias_ref[...]
    step = jnp.maximum(raw, 0.0) + jnp.log1p(jnp.exp(-jnp.abs(raw)))
    per_token = step * (-jnp.exp(alog_ref[...]))
    upper = lax.broadcasted_iota(jnp.int32, (length, length), 0) <= lax.broadcasted_iota(
        jnp.int32, (length, length), 1
    )
    sums = jnp.dot(
        three_terms(per_token).astype(jnp.bfloat16),
        upper.astype(jnp.float32).astype(jnp.bfloat16),
        preferred_element_type=jnp.float32,
    )
    total = (sums[:heads] + sums[heads : 2 * heads]) + sums[2 * heads :]
    total = total * LOG2_E
    row = total - jnp.log(step) * LOG2_E
    columns = total.T
    column_ref[q] = total
    causal = lax.broadcasted_iota(jnp.int32, (half, half), 0) >= lax.broadcasted_iota(
        jnp.int32, (half, half), 1
    )
    low = lax.broadcasted_iota(jnp.int32, (length, 2 * width), 1) < width
    for pair in range(heads // 2):
        lanes = slice(pair * 2 * width, (pair + 1) * 2 * width)
        x_conv = convolve(x_ref[0, :, lanes], taps_x_ref[:, lanes], pair)
        parts = []
        for head in (2 * pair, 2 * pair + 1):
            column = jnp.broadcast_to(columns[:, head : head + 1], (length, half))
            rows = row[head : head + 1, :]
            near = jnp.exp2(jnp.where(causal, column[:half] - rows[:, :half], -1e30))
            far = jnp.exp2(column[half:] - rows[:, :half])
            last = jnp.exp2(jnp.where(causal, column[half:] - rows[:, half:], -1e30))
            spot = slice(head * FIX, (head + 1) * FIX)
            first_ref[q, :half, spot] = near[:, :FIX]
            first_ref[q, half:, spot] = far[:, :FIX]
            top = (scores[:half, :half] * near).astype(jnp.bfloat16)
            left = (scores[half:, :half] * far).astype(jnp.bfloat16)
            right = (scores[half:, half:] * last).astype(jnp.bfloat16)
            below = jnp.concatenate([left, right], axis=1)
            parts.append(
                jnp.concatenate(
                    [
                        jnp.dot(top, x_conv[:half], preferred_element_type=jnp.float32),
                        jnp.dot(below, x_conv, preferred_element_type=jnp.float32),
                    ]
                )
            )
        mixed_ref[q, :, lanes] = jnp.where(low, parts[0], parts[1]) + skip_ref[
            :, lanes
        ] * x_conv.astype(jnp.float32)


def late_kernel(places, offset, heads, lines, reach, tail_at, place_ref, *refs):
    count = len(heads)
    tails, states, parts = refs[:4], refs[4 : 4 + 4 * count], refs[4 + 4 * count : -4]
    y_ref, padded, y_part, sems = refs[-4:]
    _, kids, length, wide = y_part.shape
    rows, heads = heads, sum(heads)
    width = wide // heads
    rows = [part * width for part in rows]
    low_first = lax.broadcasted_iota(jnp.int32, (FIX, 2 * width), 1) < width
    contract = (((1,), (1,)), ((), ()))

    def add(j, kid):
        q = place_ref[0] ^ j
        mixed_ref, held_ref, column_ref, first_ref, opening_ref, weights_ref = parts[
            6 * kid : 6 * kid + 6
        ]
        size = held_ref.shape[2]
        per_group = column_ref.shape[1]
        group_wide = opening_ref.shape[2] - 2 * size
        tail_rows = pl.ds(tail_at, -(-lines * reach // 16) * 16)
        tail = tails[places[0].index(j)][kid, tail_rows].astype(jnp.float32)
        blocks = [states[4 * n + places[1 + n].index(j)] for n in range(count)]
        state = jnp.concatenate([ref[kid, : rows[n]] for n, ref in enumerate(blocks)])

        def opening(start, stop, at):
            tap_rows = []
            for k in range(reach):
                first = k * lines + at
                count = (stop - start) // 128
                here = [tail[first + n : first + n + 1] for n in range(count)]
                tap_rows.append(jnp.concatenate(here, axis=1))
            return conv_silu(
                padded.at[j, kid, :, : stop - start],
                jnp.concatenate(tap_rows),
                opening_ref[q, :, start:stop],
                weights_ref[q, : reach + 1, start:stop],
            )

        bc_first = opening(group_wide, group_wide + 2 * size, lines - 2)
        b_first, c_first = bc_first[:, :size], bc_first[:, size:]
        start = offset * width
        x_all = opening(start, start + wide, start // 128).astype(jnp.float32)
        skipped = weights_ref[q, reach + 1 : reach + 2, start : start + wide] * x_all
        c_conv = jnp.concatenate([c_first, held_ref[q, FIX:]])
        terms = three_terms(jnp.exp2(column_ref[q]))
        terms = jnp.concatenate([terms, jnp.zeros((per_group, length), jnp.float32)])
        spread_row = lax.broadcasted_iota(jnp.int32, (4 * per_group, wide), 0)
        spread_lane = lax.broadcasted_iota(jnp.int32, (4 * per_group, wide), 1)
        spread = spread_row % per_group == offset + spread_lane // width
        grow = jnp.dot(
            terms.T.astype(jnp.bfloat16),
            spread.astype(jnp.float32).astype(jnp.bfloat16),
            preferred_element_type=jnp.float32,
        )
        term = lax.dot_general(c_conv, state, contract, preferred_element_type=jnp.float32)
        carried = (term * grow).astype(jnp.bfloat16)
        scores = lax.dot_general(
            c_conv,
            jnp.concatenate([b_first] * heads),
            contract,
            preferred_element_type=jnp.float32,
        )
        here = slice(offset * FIX, (offset + heads) * FIX)
        mixing = (scores * first_ref[q, :, here]).astype(jnp.bfloat16)
        for pair in range(heads // 2):
            lanes = slice(pair * 2 * width, (pair + 1) * 2 * width)
            x_first = x_all[:, lanes]
            stacked = [jnp.where(low_first, x_first, 0.0), jnp.where(low_first, 0.0, x_first)]
            if pair > 0:
                stacked = [jnp.zeros((2 * pair * FIX, 2 * width), jnp.float32)] + stacked
            if 2 * pair + 2 < heads:
                spare = (heads - 2 * pair - 2) * FIX
                stacked = stacked + [jnp.zeros((spare, 2 * width), jnp.float32)]
            part = jnp.dot(
                mixing,
                jnp.concatenate(stacked).astype(jnp.bfloat16),
                preferred_element_type=jnp.float32,
            )
            part = jnp.concatenate([part[:FIX] + skipped[:, lanes], part[FIX:]])
            whole = slice(start + lanes.start, start + lanes.stop)
            y_part[j, kid, :, lanes] = (
                mixed_ref[q, :, whole] + part + carried[:, lanes].astype(jnp.float32)
            ).astype(jnp.bfloat16)

    copies = []
    for j in range(4):
        for kid in range(kids):
            add(j, kid)
        start = (place_ref[0] ^ j) * (y_ref.shape[2] // 4) + offset * width
        lanes = pl.ds(pl.multiple_of(start, 128), wide)
        copies.append(pltpu.make_async_copy(y_part.at[j], y_ref.at[:, :, lanes], sems.at[j]))
        copies[-1].start()
    for copy in copies:
        copy.wait()


def cast_kernel(parts, tailed, reach, lines, *refs):
    count = len(tailed)
    ins, outs = refs[:-count], refs[-count:]
    states, tails = ins[: parts * count], ins[parts * count :]
    for j, out_ref in enumerate(outs):
        start = 0
        for at in range(parts):
            state = states[parts * j + at][0]
            rows = state.shape[0] * state.shape[1]
            out_ref[start : start + rows] = state.reshape(rows, state.shape[2]).astype(jnp.bfloat16)
            start += rows
            if at == 0 and tailed[j]:
                x_tail = tails[2 * j][0].astype(jnp.float32)
                bc_tail = tails[2 * j + 1][0].astype(jnp.float32)
                pieces = []
                for k in range(reach):
                    pieces += [x_tail[k : k + 1, i * 128 : i * 128 + 128] for i in range(lines - 2)]
                    pieces.append(bc_tail[k])
                spare = tailed[j] - lines * reach
                pieces.append(jnp.zeros((spare, 128), jnp.float32))
                out_ref[start : start + tailed[j]] = jnp.concatenate(pieces).astype(jnp.bfloat16)
                start += tailed[j]


def within_kernel(
    parent_ref,
    x_ref,
    b_ref,
    c_ref,
    dt_ref,
    bias_ref,
    alog_ref,
    skip_ref,
    taps_x_ref,
    taps_bc_ref,
    tail_x_ref,
    tail_bc_ref,
    mixed_ref,
    c_out_ref,
    grow_ref,
    padded,
):
    length = x_ref.shape[1]
    heads = dt_ref.shape[1]
    width = x_ref.shape[2] // heads
    b_conv = conv_silu(padded, tail_bc_ref[0, 0], b_ref[0], taps_bc_ref[0])
    c_conv = conv_silu(padded, tail_bc_ref[0, 1], c_ref[0], taps_bc_ref[1])
    c_out_ref[0] = c_conv
    scores = lax.dot_general(
        c_conv, b_conv, (((1,), (1,)), ((), ())), preferred_element_type=jnp.float32
    )
    raw = dt_ref[0] + bias_ref[...]
    step = jnp.maximum(raw, 0.0) + jnp.log1p(jnp.exp(-jnp.abs(raw)))
    per_token = step * (-jnp.exp(alog_ref[...]))
    row = lax.broadcasted_iota(jnp.int32, (length, length), 0)
    col = lax.broadcasted_iota(jnp.int32, (length, length), 1)
    upper = (row <= col).astype(jnp.float32)
    total = lax.dot_general(
        per_token,
        upper,
        (((1,), (0,)), ((), ())),
        precision=lax.Precision.HIGHEST,
        preferred_element_type=jnp.float32,
    )
    total_t = total.T
    grow_ref[0, 0] = jnp.exp(total_t)
    causal = row >= col
    low = lax.broadcasted_iota(jnp.int32, (length, 2 * width), 1) < width
    for pair in range(heads // 2):
        lanes = slice(pair * 2 * width, (pair + 1) * 2 * width)
        x_conv = conv_silu(
            padded, tail_x_ref[0, :, lanes], x_ref[0, :, lanes], taps_x_ref[:, lanes]
        )
        parts = []
        for head in (2 * pair, 2 * pair + 1):
            gap = total_t[:, head : head + 1] - total[head : head + 1, :]
            factor = jnp.exp(jnp.where(causal, gap, -1e30))
            mixing = (scores * factor * step[head : head + 1, :]).astype(jnp.bfloat16)
            parts.append(jnp.dot(mixing, x_conv, preferred_element_type=jnp.float32))
        mixed_ref[0, :, lanes] = (
            jnp.where(low, parts[0], parts[1]) + skip_ref[:, lanes] * x_conv.astype(jnp.float32)
        )


def carried_kernel(state_ref, c_ref, grow_ref, mixed_ref, y_ref):
    sources, _, part, width, size = state_ref.shape
    length = c_ref.shape[1]
    low = lax.broadcasted_iota(jnp.int32, (length, 2 * width), 1) < width
    c_conv = c_ref[0]
    for source in range(sources):
        state = state_ref[source, 0].reshape(part * width, size)
        term = lax.dot_general(
            c_conv, state, (((1,), (1,)), ((), ())), preferred_element_type=jnp.float32
        )
        for pair in range(part // 2):
            head = source * part + 2 * pair
            grow = jnp.where(
                low, grow_ref[0, 0, :, head : head + 1], grow_ref[0, 0, :, head + 1 : head + 2]
            )
            here = slice(2 * pair * width, (2 * pair + 2) * width)
            lanes = slice(head * width, (head + 2) * width)
            carried = (term[:, here] * grow).astype(jnp.bfloat16).astype(jnp.float32)
            y_ref[0, :, lanes] = (mixed_ref[0, :, lanes] + carried).astype(jnp.bfloat16)


def pick_kernel(parent_ref, state_ref, out_ref):
    out_ref[...] = state_ref[...]


def local_any(
    x_in,
    b_in,
    c_in,
    dt_in,
    dt_bias,
    a_log,
    d_skip,
    conv_x,
    conv_bc,
    par_state,
    tail_x,
    tail_bc,
    counts,
    order,
):
    kids, length, columns = x_in.shape
    heads = dt_in.shape[1]
    width, size = par_state.shape[2:]
    ways = lax.axis_size("batch")
    groups = b_in.shape[2] // size
    per_group = heads // groups
    part = heads // ways
    wide = per_group * width
    reach = tail_x.shape[1]
    parents_all = counts.shape[0]
    kids_all = order.shape[0]

    parent = parent_of(counts, order)
    own = lax.dynamic_slice_in_dim(parent, lax.axis_index("batch") * kids, kids)

    sent = par_state.astype(jnp.bfloat16).reshape(ways, part, width, size)
    shares = lax.all_to_all(sent, "batch", split_axis=0, concat_axis=0, tiled=True)

    tails = jnp.concatenate([tail_x.reshape(-1), tail_bc.reshape(-1)])
    tails = jnp.broadcast_to(tails[None], (ways, tails.shape[0]))
    tails = lax.all_to_all(tails, "batch", split_axis=0, concat_axis=0, tiled=True)
    tails_x = tails[:, : reach * columns].reshape(parents_all, reach, columns)
    tails_bc = tails[:, reach * columns :].reshape(parents_all, 2, reach, groups * size)

    picked = pl.pallas_call(
        pick_kernel,
        grid_spec=pltpu.PrefetchScalarGridSpec(
            num_scalar_prefetch=1,
            grid=(kids_all,),
            in_specs=[pl.BlockSpec((1, part, width, size), lambda i, p: (p[i], 0, 0, 0))],
            out_specs=pl.BlockSpec((1, part, width, size), lambda i, p: (i, 0, 0, 0)),
        ),
        out_shape=jax.ShapeDtypeStruct((kids_all, part, width, size), jnp.bfloat16),
        cost_estimate=pl.CostEstimate(
            flops=0, bytes_accessed=4 * kids_all * part * width * size, transcendentals=0
        ),
        name="pick_states",
    )(parent, shares)
    states = lax.all_to_all(
        picked.reshape(ways, kids, part, width, size), "batch", split_axis=0, concat_axis=0, tiled=True
    )

    skip_row = jnp.repeat(d_skip, width)[None, :]
    mixed, c_conv, grow = pl.pallas_call(
        within_kernel,
        grid_spec=pltpu.PrefetchScalarGridSpec(
            num_scalar_prefetch=1,
            grid=(kids, groups),
            in_specs=[
                pl.BlockSpec((1, length, wide), lambda c, q, p: (c, 0, q)),
                pl.BlockSpec((1, length, size), lambda c, q, p: (c, 0, q)),
                pl.BlockSpec((1, length, size), lambda c, q, p: (c, 0, q)),
                pl.BlockSpec((1, per_group, length), lambda c, q, p: (c, q, 0)),
                pl.BlockSpec((per_group, 1), lambda c, q, p: (q, 0)),
                pl.BlockSpec((per_group, 1), lambda c, q, p: (q, 0)),
                pl.BlockSpec((1, wide), lambda c, q, p: (0, q)),
                pl.BlockSpec((reach + 1, wide), lambda c, q, p: (0, q)),
                pl.BlockSpec((2, reach + 1, size), lambda c, q, p: (0, 0, q)),
                pl.BlockSpec((1, reach, wide), lambda c, q, p: (p[c], 0, q)),
                pl.BlockSpec((1, 2, reach, size), lambda c, q, p: (p[c], 0, 0, q)),
            ],
            out_specs=[
                pl.BlockSpec((1, length, wide), lambda c, q, p: (c, 0, q)),
                pl.BlockSpec((1, length, size), lambda c, q, p: (c, 0, q)),
                pl.BlockSpec((1, 1, length, per_group), lambda c, q, p: (c, q, 0, 0)),
            ],
            scratch_shapes=[pltpu.VMEM((8 + length, size), jnp.float32)],
        ),
        out_shape=[
            jax.ShapeDtypeStruct((kids, length, columns), jnp.float32),
            jax.ShapeDtypeStruct((kids, length, groups * size), jnp.bfloat16),
            jax.ShapeDtypeStruct((kids, groups, length, per_group), jnp.float32),
        ],
        compiler_params=pltpu.CompilerParams(vmem_limit_bytes=4 * VMEM_LIMIT),
        cost_estimate=pl.CostEstimate(
            flops=4 * kids * heads * length * length * width,
            bytes_accessed=6 * kids * length * columns,
            transcendentals=kids * heads * length * length,
        ),
        name="within",
    )(
        own,
        x_in,
        b_in,
        c_in,
        dt_in,
        dt_bias[:, None],
        a_log[:, None],
        skip_row,
        conv_x,
        conv_bc,
        tails_x,
        tails_bc,
    )

    sources = per_group // part
    return pl.pallas_call(
        carried_kernel,
        grid=(kids, groups),
        in_specs=[
            pl.BlockSpec((sources, 1, part, width, size), lambda c, q: (q, c, 0, 0, 0)),
            pl.BlockSpec((1, length, size), lambda c, q: (c, 0, q)),
            pl.BlockSpec((1, 1, length, per_group), lambda c, q: (c, q, 0, 0)),
            pl.BlockSpec((1, length, wide), lambda c, q: (c, 0, q)),
        ],
        out_specs=pl.BlockSpec((1, length, wide), lambda c, q: (c, 0, q)),
        out_shape=jax.ShapeDtypeStruct((kids, length, columns), jnp.bfloat16),
        compiler_params=pltpu.CompilerParams(vmem_limit_bytes=4 * VMEM_LIMIT),
        cost_estimate=pl.CostEstimate(
            flops=2 * kids * length * columns * size,
            bytes_accessed=8 * kids * length * columns,
            transcendentals=0,
        ),
        name="carried",
    )(states, c_conv, grow, mixed)


def local_halves(
    x_in, b_in, c_in, dt_in, dt_bias, a_log, d_skip, conv_x, conv_bc,
    par_state, tail_x, tail_bc, counts, order,
):
    kids, length, columns = x_in.shape
    heads = dt_in.shape[1]
    width, size = par_state.shape[2:]
    groups = b_in.shape[2] // size
    per_group = heads // groups
    wide = per_group * width
    taps = conv_x.shape[0]
    reach = taps - 1
    lines = (wide + 2 * size) // 128
    tail_lines = -(-lines * reach // 16) * 16
    params = pltpu.CompilerParams(vmem_limit_bytes=VMEM_LIMIT)
    anywhere = pl.BlockSpec(memory_space=pl.ANY)
    small = pl.CostEstimate(flops=1, bytes_accessed=1, transcendentals=0)

    stay = lambda x: pltpu.with_memory_space_constraint(x, pltpu.HBM)
    keep_in_vmem = lambda x: pltpu.with_memory_space_constraint(x, pltpu.VMEM)
    x_in, b_in, c_in, dt_in, conv_x, conv_bc = map(stay, (x_in, b_in, c_in, dt_in, conv_x, conv_bc))

    me = lax.axis_index("batch")
    parent = parent_of(counts, order)
    child = (jnp.arange(4 * kids, dtype=jnp.int32) // kids ^ me) * kids
    child = child + jnp.arange(4 * kids, dtype=jnp.int32) % kids
    catalog = jnp.arange(4 * 2 * kids, dtype=jnp.int32)
    owner = jnp.sum(jnp.where(child[:, None] == catalog[None, :], parent[None, :], 0), axis=1)
    slots = owner ^ me
    place = (me % 4).astype(jnp.int32)[None]

    state = stay(par_state.reshape(groups, per_group, width, size))
    x_tails, bc_tails = stay(tail_x), stay(tail_bc.transpose(0, 2, 1, 3))
    offsets = [sum(SPLIT[:k]) for k in range(len(SPLIT))]

    def swap(value, r):
        return lax.ppermute(value, "batch", perm=[(i, i ^ r) for i in range(8)])

    def cast():
        rows = per_group * width + tail_lines
        rows_a = SPLIT[0] * width + tail_lines
        blocks = [(0, SPLIT[0])] + [(at, 4) for at in range(SPLIT[0], per_group, 4)]
        count = len(blocks) + 2

        def kernel(place_ref, *refs):
            ins, outs = refs[: 4 * count], refs[4 * count :]
            quarters = [outs[0], outs[2].at[0], outs[1], outs[2].at[1]]
            for n, out_ref in enumerate(quarters):
                cast_kernel(
                    len(blocks), [tail_lines], reach, lines, *ins[count * n : count * n + count], out_ref
                )
                outs[3 + n // 2][n % 2] = out_ref[:rows_a]

        operands, specs = [], []
        for n in range(4):
            for offset, part in blocks:
                operands.append(state)
                specs.append(
                    pl.BlockSpec(
                        (1, part, width, size),
                        lambda i, p, n=n, at=offset // part: (p[0] ^ n, at, 0, 0),
                    )
                )
            operands += [x_tails, bc_tails]
            specs += [
                pl.BlockSpec((1, reach, wide), lambda i, p, n=n: (0, 0, p[0] ^ n)),
                pl.BlockSpec((1, reach, 2, size), lambda i, p, n=n: (0, 0, 0, p[0] ^ n)),
            ]
        shapes = [(rows, size)] * 2 + [(2, rows, size)] + [(2, rows_a, size)] * 2
        return pl.pallas_call(
            kernel,
            grid_spec=pltpu.PrefetchScalarGridSpec(
                num_scalar_prefetch=1,
                grid=(1,),
                in_specs=specs,
                out_specs=[pl.BlockSpec(memory_space=pltpu.VMEM)] * len(shapes),
            ),
            out_shape=[pltpu.VMEM(shape, jnp.bfloat16) for shape in shapes],
            compiler_params=params,
            cost_estimate=small,
            name="cast_states",
        )(place, *operands)

    def rearrange(scalars, sources, moves, shapes, tokens, name):
        def kernel(scalars_ref, *refs):
            held, outs = refs[: len(sources)], refs[len(sources) :]
            for out, at, scalar, choices in moves:
                for value, (number, take) in enumerate(choices):

                    def copy(out=out, at=at, number=number, take=take):
                        rows = held[number][...] if take is None else held[number][take]
                        if at is None:
                            outs[out][...] = rows
                        else:
                            outs[out][at] = rows

                    if scalar is None:
                        copy()
                    else:
                        pl.when(scalars_ref[scalar] == value)(copy)

        return pl.pallas_call(
            functools.partial(drop_tokens, kernel, 1 + len(sources), len(tokens)),
            grid_spec=pltpu.PrefetchScalarGridSpec(
                num_scalar_prefetch=1,
                grid=(1,),
                in_specs=[pl.BlockSpec(memory_space=pltpu.VMEM)] * len(sources)
                + [anywhere] * len(tokens),
                out_specs=[pl.BlockSpec(memory_space=pltpu.VMEM)] * len(shapes),
            ),
            out_shape=[pltpu.VMEM(shape, jnp.bfloat16) for shape in shapes],
            compiler_params=params,
            cost_estimate=small,
            name=name,
        )(scalars, *map(keep_in_vmem, sources), *tokens)

    def pick(rows, sources, choices, tokens, order=(1, 3, 2)):
        moves = [
            (j, kid, j * kids + kid, choices) for j in range(4) for kid in range(kids)
        ]
        picked = rearrange(
            slots, sources, moves, [(kids, rows, size)] * 4, tokens, "pick_states"
        )
        return [(0, picked[0])] + [(j, swap(picked[j], j)) for j in order]

    def early(c, pieces, piece, before, tokens):
        per = groups // pieces
        at = lambda q: (c, 0, per * piece + q)
        operands = [
            x_in, b_in, c_in, dt_in, dt_bias[:, None], a_log[:, None], skip_row, conv_x, conv_bc
        ]
        keep = len(operands)
        tokens = list(tokens) + [keep_in_vmem(a) for a in before]
        first = keep + len(tokens) - len(before)
        return pl.pallas_call(
            functools.partial(
                drop_tokens, functools.partial(early_kernel, per * piece), keep, len(tokens)
            ),
            grid=(per,),
            in_specs=[
                pl.BlockSpec((1, length, wide), at),
                pl.BlockSpec((1, length, size), at),
                pl.BlockSpec((1, length, size), at),
                pl.BlockSpec((1, per_group, length), lambda q: (c, per * piece + q, 0)),
                pl.BlockSpec((per_group, 1), lambda q: (per * piece + q, 0)),
                pl.BlockSpec((per_group, 1), lambda q: (per * piece + q, 0)),
                pl.BlockSpec((1, wide), lambda q: (0, per * piece + q)),
                pl.BlockSpec((taps, wide), lambda q: (0, per * piece + q)),
                pl.BlockSpec((2, taps, size), lambda q: (0, 0, per * piece + q)),
                *[anywhere] * len(tokens),
            ],
            out_specs=[pl.BlockSpec(memory_space=pltpu.VMEM)] * 6,
            out_shape=[
                pltpu.VMEM((groups, length, wide), jnp.float32),
                pltpu.VMEM((groups, length, size), jnp.bfloat16),
                pltpu.VMEM((groups, per_group, length), jnp.float32),
                pltpu.VMEM((groups, length, per_group * FIX), jnp.float32),
                pltpu.VMEM((groups, FIX, wide + 2 * size), jnp.bfloat16),
                pltpu.VMEM((groups, 8, wide + 2 * size), jnp.float32),
            ],
            input_output_aliases={first + i: i for i in range(len(before))},
            scratch_shapes=[pltpu.VMEM((2, 8 + length, size), jnp.float32)],
            compiler_params=params,
            cost_estimate=small,
            name="early",
        )(*operands, *tokens)

    def late(ks, states, parts, result, tokens):
        offset = offsets[ks[0]]
        chunk = sum(SPLIT[k] for k in ks) * width
        places = [[j for j, _ in chunk_states] for chunk_states in states]
        held = [array for chunk_states in states for _, array in chunk_states]
        operands = [keep_in_vmem(a) for a in (*held[:4], *sum((held[4 * k : 4 * k + 4] for k in ks), []), *parts[0], *parts[1])]
        specs = [pl.BlockSpec(memory_space=pltpu.VMEM)] * len(operands)
        keep = 1 + len(operands)
        operands += tokens
        specs += [anywhere] * len(tokens)
        alias = {}
        if result is not None:
            alias = {1 + len(operands): 0}
            operands.append(result)
            specs.append(anywhere)
        kernel = functools.partial(
            late_kernel, [places[0]] + [places[k] for k in ks], offset, [SPLIT[k] for k in ks], lines, reach, SPLIT[0] * width
        )
        return pl.pallas_call(
            functools.partial(drop_tokens, kernel, keep, 1 + len(operands) - keep),
            grid_spec=pltpu.PrefetchScalarGridSpec(
                num_scalar_prefetch=1,
                grid=(1,),
                in_specs=specs,
                out_specs=anywhere,
                scratch_shapes=[
                    pltpu.VMEM((groups, kids, 8 + FIX, max(chunk, 2 * size)), jnp.float32),
                    pltpu.VMEM((groups, kids, length, chunk), jnp.bfloat16),
                    pltpu.SemaphoreType.DMA((groups,)),
                ],
            ),
            out_shape=jax.ShapeDtypeStruct(x_in.shape, jnp.bfloat16),
            input_output_aliases=alias,
            compiler_params=params,
            cost_estimate=small,
            name="late",
        )(place, *operands)

    skip_row = jnp.repeat(d_skip, width)[None, :]
    rows = [SPLIT[0] * width + tail_lines] + [part * width for part in SPLIT[1:]]
    chunks = [pl.ds(sum(rows[:k]), rows[k]) for k in range(len(SPLIT))]
    own, own_2, own_13, sent_4, sent_6 = cast()
    crossed_a = [swap(sent_4, 4), swap(sent_6, 6)]
    along_y, along_z = swap(own_13, 1), swap(own_2, 2)
    parts = [early(0, 1, 0, [], [own, slots])]
    (turn,) = rearrange(
        place, [along_y], [(0, None, None, [(0, 1)])], [own.shape], [parts[0][1]], "stack_turn"
    )
    inside = [own, along_y, along_z, swap(turn, 2)]

    def inside_rows(k):
        return [(0, chunks[k]), (1, (0, chunks[k])), (2, chunks[k]), (3, chunks[k])]

    def cross(k, tokens):
        moves = [(0, j, None, [choice]) for j, choice in enumerate(inside_rows(k))]
        (sent,) = rearrange(place, inside, moves, [(4, rows[k], size)], tokens, "stack_later")
        return sent, swap(sent, 4)

    def pick_later(k, crossed, tokens):
        choices = inside_rows(k) + [(4, j) for j in range(4)]
        return pick(rows[k], [*inside, crossed], choices, tokens, (3, 2, 1))

    second = early(1, 2, 0, [], [turn])
    moves = [(0, n, None, [(n, 1)]) for n in range(2)]
    (spread,) = rearrange(
        place, crossed_a, moves, [(2, rows[0], size)], [second[1]], "stack_first"
    )
    passed = swap(spread, 1)
    sent_b, crossed_b = cross(1, [spread])
    second = early(1, 2, 1, second, [sent_b])
    parts.append(second)
    choices = inside_rows(0) + [(4, 0), (6, 0), (5, 0), (6, 1)]
    states = [pick(rows[0], [*inside, *crossed_a, passed], choices, [second[1]])]
    sent_c, crossed_c = cross(2, [states[0][0][1], crossed_b])
    states.append(pick_later(1, crossed_b, [sent_c]))
    states.append(pick_later(2, crossed_c, [states[1][0][1]]))
    result = late([0, 1], states, parts, None, [states[2][0][1]])
    return late([2], states, parts, result, [])


def solution(mesh):
    rows, cols = P(("groups", "batch"), None, "head"), P(("groups", "batch"), "head")
    placed = (
        rows, rows, rows, cols, P("head"), P("head"), P("head"), P(None, "head"),
        P(None, None, "head"), cols, rows, P(("groups", "batch"), None, None, "head"),
        P("groups"), P("groups"),
    )
    local = local_halves if mesh.shape["batch"] == 8 else local_any
    return jax.shard_map(local, mesh=mesh, in_specs=placed, out_specs=rows, check_vma=False)
```
